32 devices in a mesh: dp: 8 (over y, x, core), tensor: 4 (over z).
Axes of the slice: x: 2, y: 2, z: 4, core: 2. Of those that a mesh axis runs over, the one named last changes fastest.
Arguments:
- tokens: bfloat16 [4096, 2560], P(('dp', 'tensor')), may hold values from -6 to 6
- norm_gain: bfloat16 [2560], P('dp'), may hold values from 0.5 to 1.5
- x_weight: bfloat16 [2560, 2560], P('dp', 'tensor'), may hold values from -0.125 to 0.125
- y_weight: bfloat16 [2560, 2560], P('dp', 'tensor'), may hold values from -0.125 to 0.125
- conv_weight: float32 [4, 2560], P(None, 'tensor'), may hold values from -3 to 3
- recur_gate_weight: bfloat16 [256, 2560], P('dp', 'tensor'), may hold values from -0.375 to 0.375
- input_gate_weight: bfloat16 [256, 2560], P('dp', 'tensor'), may hold values from -0.375 to 0.375
- decay_param: float32 [2560], P('tensor'), may hold values from 5 to 11
- out_weight: bfloat16 [2560, 2560], P('tensor', 'dp'), may hold values from -0.25 to 0.25
- mlp_gain: bfloat16 [2560], P('dp'), may hold values from 0.5 to 1.5
- gate_weight: bfloat16 [2560, 7680], P('dp', 'tensor'), may hold values from -0.125 to 0.125
- up_weight: bfloat16 [2560, 7680], P('dp', 'tensor'), may hold values from -0.125 to 0.125
- down_weight: bfloat16 [7680, 2560], P('tensor', 'dp'), may hold values from -0.125 to 0.125
- seq_lengths: int32 [3], replicated, may hold values from 1 to 2048, 3968 in all
- token_order: int32 [4096], P(('dp', 'tensor')), may hold values from 0 to 4095, as said below
- cotangent: bfloat16 [4096, 2560], P(('dp', 'tensor')), may hold values from -6 to 6
Outputs:
- output: bfloat16 [4096, 2560], P(('dp', 'tensor'))
- grad_tokens: float32 [4096, 2560], P(('dp', 'tensor'))
- grad_norm_gain: float32 [2560], P('dp')
- grad_x_weight: float32 [2560, 2560], P('dp', 'tensor')
- grad_y_weight: float32 [2560, 2560], P('dp', 'tensor')
- grad_conv_weight: float32 [4, 2560], P(None, 'tensor')
- grad_recur_gate: float32 [256, 2560], P('dp', 'tensor')
- grad_input_gate: float32 [256, 2560], P('dp', 'tensor')
- grad_decay: float32 [2560], P('tensor')
- grad_out_weight: float32 [2560, 2560], P('tensor', 'dp')
- grad_mlp_gain: float32 [2560], P('dp')
- grad_gate_weight: float32 [2560, 7680], P('dp', 'tensor')
- grad_up_weight: float32 [2560, 7680], P('dp', 'tensor')
- grad_down_weight: float32 [7680, 2560], P('tensor', 'dp')
The draws below stay inside these ranges and needn't reach their ends.
Inputs may be any that keep to these rules, and one draw needn't show every extreme that they name: `seq_lengths`: the lengths sum to 3968; the remaining places at the end are padding. The longest is exactly 2048. token_order is a permutation that maps each aligned block of 512 stored rows onto the same block of 512 places.
All inputs are finite; a program needn't handle non-finite values.
Results may differ from the reference program's by a relative error of at most 0.022.
Values may be sent and summed in bfloat16 or wider, within the bound.
A program may use at most 256 MiB of HBM per device.

```python
import math
import jax
import jax.numpy as jnp
import numpy as np
from jax import lax

D = 2560
R = 2560
HEADS = 10
FF = 7680
CONV = 4
TOK_DEV = 128
BLOCK = 256
TOKENS = 4096
GROUP = 512
NSEQ = 3
MAXLEN = 2048


def draw_token_order(key, part):
    key = jax.random.fold_in(key, 5)
    group_keys = jax.random.split(key, TOKENS // GROUP)

    def shuffle(sub_key):
        return jax.random.permutation(sub_key, GROUP).astype(jnp.int32)
    orders = jax.vmap(shuffle)(group_keys)
    offsets = GROUP * jnp.arange(TOKENS // GROUP, dtype=jnp.int32)
    return (orders + offsets[:, None]).reshape(TOKENS).astype(jnp.int32)


def block_scale(stream_key, shape, cuts, smallest, high):
    def one(dim, blocks):
        heights = jax.random.uniform(jax.random.fold_in(jax.random.fold_in(stream_key, 6), dim), (blocks,), jnp.float32, smallest / len(cuts), high / len(cuts))
        return jnp.repeat(jnp.exp(heights), shape[dim] // blocks).reshape((-1,) + (1,) * (len(shape) - dim - 1))

    level = one(*cuts[0])
    for cut in cuts[1:]:
        level = level * one(*cut)
    return level


def profile(amount, total, limit, skew):
    weights = [(1 << 20) // math.isqrt(standing ** skew) + 1 for standing in range(2, amount + 1)]
    rest, counts = total - limit - (amount - 1), [1] * (amount - 1)
    while rest > 0:
        free = [i for i in range(amount - 1) if counts[i] < limit]
        pool, budget = sum([weights[i] for i in free]), rest
        for i in free:
            addition = min(limit - counts[i], max(1, budget * weights[i] // pool), rest)
            counts[i] = counts[i] + addition
            rest = rest - addition
    return np.array([limit] + counts)


def uneven(key, number_of, total, limit, lean):
    if number_of == 2:
        one = jax.random.randint(key, (), max(1, total - limit), min(limit, total - 1) + 1)
        return jnp.stack([one, total - one])
    lengths = jnp.asarray(profile(number_of, total, limit, lean), jnp.int32)
    twos = (number_of - 1) // 2
    donor, receiver = lengths[1:1 + 2 * twos:2], lengths[2:2 + 2 * twos:2]
    slack = jnp.minimum(donor - 1, limit - receiver)
    moved = jax.random.randint(jax.random.fold_in(key, 1), (twos,), 0, 1 << 20) % (slack + 1)
    lengths = lengths.at[1:1 + 2 * twos:2].set(donor - moved).at[2:2 + 2 * twos:2].set(receiver + moved)
    return lengths[jax.random.permutation(jax.random.fold_in(key, 2), number_of)]


def noise(rng, dims, scale, limit, cuts=(), kind=jnp.bfloat16):
    entries = jax.random.normal(rng, dims, jnp.float32) * scale
    if len(cuts) > 0:
        entries = block_scale(rng, dims, cuts, -0.22, 0.18) * entries
    return jnp.clip(entries, min=-limit, max=limit).astype(kind)


def setup_inputs(seed: int = 0) -> dict:
    key_of = jax.random.split(jax.random.key(seed), 17)
    return {
        "tokens": noise(key_of[0], (TOKENS, D), 1.0, 6.0, ((0, 32),)),
        "norm_gain": jnp.clip(1.0 + 0.1 * jax.random.normal(key_of[1], (D,), jnp.float32), 0.5, 1.5).astype(jnp.bfloat16),
        "x_weight": noise(key_of[2], (D, R), D ** -0.5, 0.125, ((0, 8), (1, 4))),
        "y_weight": noise(key_of[3], (D, R), D ** -0.5, 0.125, ((0, 8), (1, 4))),
        "conv_weight": noise(key_of[4], (CONV, R), CONV ** -0.5, 3.0, ((1, 4),), jnp.float32),
        "recur_gate_weight": noise(key_of[5], (BLOCK, R), BLOCK ** -0.5, 0.375, ((0, 8), (1, 4))),
        "input_gate_weight": noise(key_of[6], (BLOCK, R), BLOCK ** -0.5, 0.375, ((0, 8), (1, 4))),
        "decay_param": jnp.clip(5.0 + 6.0 * jax.random.uniform(key_of[7], (R,), jnp.float32) ** block_scale(key_of[7], (R,), ((0, 4),), -0.2, 0.2), 5.0, 11.0),
        "out_weight": noise(key_of[8], (R, D), (R // 4) ** -0.5, 0.25, ((0, 4), (1, 8))),
        "mlp_gain": jnp.clip(1.0 + 0.1 * jax.random.normal(key_of[9], (D,), jnp.float32), 0.5, 1.5).astype(jnp.bfloat16),
        "gate_weight": noise(key_of[10], (D, FF), D ** -0.5, 0.125, ((0, 8), (1, 4))),
        "up_weight": noise(key_of[11], (D, FF), D ** -0.5, 0.125, ((0, 8), (1, 4))),
        "down_weight": noise(key_of[12], (FF, D), (FF // 4) ** -0.5, 0.125, ((0, 4), (1, 8))),
        "seq_lengths": uneven(key_of[13], NSEQ, TOKENS - TOK_DEV, MAXLEN, 1).astype(jnp.int32),
        "token_order": draw_token_order(jax.random.fold_in(key_of[16], 71), 0),
        "cotangent": noise(key_of[15], (TOKENS, D), 1.0, 6.0, ((0, 32),)),
    }


@jax.custom_vjp
def low(v):
    return lax.optimization_barrier(v.astype(jnp.bfloat16)).astype(jnp.float32)

@jax.custom_vjp
def low_back(v):
    return v

def low_keep(v):
    return (low(v), None)

def low_pass(kept, grad):
    return (grad,)

def back_keep(v):
    return (v, None)

def back_low(kept, grad):
    return (low(grad),)
low.defvjp(low_keep, low_pass)
low_back.defvjp(back_keep, back_low)
epsilon = 1e-06
rate_scale = 8.0
highest = lax.Precision.HIGHEST

def matmul(left, right):
    return jnp.dot(left, right, precision=highest, preferred_element_type=jnp.float32)

def rms_scale(values, gain):
    return values * lax.rsqrt(lax.optimization_barrier(jnp.mean(values * values, axis=-1, keepdims=True)) + epsilon) * gain

def segment_of(places, ends):
    return lax.optimization_barrier(jnp.sum((ends[None, :] <= places[:, None]).astype(jnp.int32), axis=1))

def pair_step(early, later):
    return (early[0] * later[0], later[0] * early[1] + later[1])

def reference(tokens, norm_gain, x_weight, y_weight, conv_weight, recur_gate_weight, input_gate_weight, decay_param, out_weight, mlp_gain, gate_weight, up_weight, down_weight, seq_lengths, token_order, cotangent):
    count = tokens.shape[0]
    places = jnp.arange(count, dtype=jnp.int32)
    inverse = jnp.zeros((count,), jnp.int32).at[token_order.astype(jnp.int32)].set(places)
    ends = jnp.cumsum(seq_lengths).astype(jnp.int32)
    segment = segment_of(places, ends)
    starts = (places == 0) | (segment != segment_of(places - 1, ends))
    live = (places < ends[-1]).astype(jnp.float32)
    same = [(segment_of(places - shift, ends) == segment).astype(jnp.float32) for shift in range(CONV)]

    def blockwise(conv_low, weight):
        mixed = jnp.einsum('thj,jhk->thk', conv_low, weight.reshape(BLOCK, HEADS, BLOCK), precision=highest)
        return mixed.reshape(count, R)

    def forward(inputs, gain_one, x_mat, y_mat, kernel, recur_mat, input_mat, decay_vals, out_mat, gain_two, gate_mat, up_mat, down_mat):
        placed_in = inputs[inverse]
        hidden_one = low(rms_scale(placed_in, gain_one))
        x_branch = low_back(low(matmul(hidden_one, x_mat)))
        y_before = low_back(matmul(hidden_one, y_mat))
        padded = jnp.pad(x_branch, ((CONV - 1, 0), (0, 0)))
        conv_out = sum((kernel[shift][None, :] * padded[CONV - 1 - shift:CONV - 1 - shift + count] * same[shift][:, None] for shift in range(CONV)))
        conv_low = low(conv_out).reshape(count, HEADS, BLOCK)
        pre_recur = low_back(blockwise(conv_low, recur_mat))
        pre_input = low_back(blockwise(conv_low, input_mat))
        log_rate = -rate_scale * jax.nn.sigmoid(pre_recur) * jax.nn.softplus(-decay_vals)
        decay_rate = jnp.where(starts[:, None], 0.0, jnp.exp(log_rate))
        scale_in = jnp.where(starts[:, None], 1.0, jnp.sqrt(-jnp.expm1(2.0 * log_rate)))
        driven = conv_out * jax.nn.sigmoid(pre_input) * scale_in
        cum_rate, state = lax.associative_scan(pair_step, (decay_rate, driven), axis=0)
        merged = low(state * jax.nn.gelu(y_before, approximate=True))
        after_mixer = placed_in + low_back(matmul(merged, out_mat))
        hidden_two = low(rms_scale(after_mixer, gain_two))
        gate_pre = low_back(matmul(hidden_two, gate_mat))
        up_pre = low_back(matmul(hidden_two, up_mat))
        product = low(jax.nn.gelu(gate_pre, approximate=True) * up_pre)
        result = (after_mixer + low_back(matmul(product, down_mat))) * live[:, None]
        return result[token_order]
    floats = tuple((value.astype(jnp.float32) for value in (tokens, norm_gain, x_weight, y_weight, conv_weight, recur_gate_weight, input_gate_weight, decay_param, out_weight, mlp_gain, gate_weight, up_weight, down_weight)))
    result, pullback = jax.vjp(forward, *floats)
    grads = pullback(cotangent.astype(jnp.float32))
    return (result.astype(jnp.bfloat16), grads[0], grads[1], grads[2], grads[3], grads[4], grads[5], grads[6], grads[7], grads[8], grads[9], grads[10], grads[11], grads[12])
```

```python
import jax
import jax.numpy as jnp
from jax import lax
from jax.experimental import pallas as pl
from jax.experimental.pallas import tpu as pltpu
from jax.sharding import PartitionSpec as P

epsilon = 1e-06
rate_scale = 8.0


def from_behind(block, axis, distance):
    devices = range(lax.axis_size(axis))
    route = [(i - distance, i) for i in devices if i - distance in devices]
    return lax.ppermute(block, axis, route)


def extended_2(array, sides, width):
    for axis, dim in sides:
        size, length = (lax.axis_size(axis), array.shape[dim])
        up = [(i, (i + 1) % size) for i in range(size - 1)]
        down = [(j, i) for i, j in up]
        last = lax.slice_in_dim(array, length - width, length, axis=dim)
        leading = lax.slice_in_dim(array, 0, width, axis=dim)
        before = lax.ppermute(last, axis, up)
        after = lax.ppermute(leading, axis, down)
        array = jnp.concatenate([before, array, after], axis=dim)
    return array


def entering(value, axis, join, neutral, backward):
    count, mine = (lax.axis_size(axis), lax.axis_index(axis))
    pieces = jax.tree.map(lambda part: lax.all_gather(part, axis), value)
    if backward:
        pieces = jax.tree.map(lambda part: part[::-1], pieces)
        mine = count - 1 - mine
    total = jax.tree.map(
        lambda part, zero: jnp.full_like(part, 0) + jnp.asarray(zero, part.dtype), value, neutral
    )

    def lap(position, total):
        longer = join(total, jax.tree.map(lambda part: part[position], pieces))
        return jax.tree.map(lambda new, old: jnp.where(position < mine, new, old), longer, total)

    return lax.fori_loop(0, count - 1, lap, total)


def rms_scale(values, gain):
    return values * lax.rsqrt(jnp.mean(values * values, axis=-1, keepdims=True) + epsilon) * gain


def norm_back(values, gain, grad):
    inv_root = lax.rsqrt(jnp.mean(values * values, axis=-1, keepdims=True) + epsilon)
    normed = values * inv_root
    upstream = grad * gain
    grad_values = inv_root * (
        upstream - normed * jnp.mean(upstream * normed, axis=-1, keepdims=True)
    )
    return (grad_values, normed)


def segment_of(places, ends):
    return jnp.sum((ends[None, :] <= places[:, None]).astype(jnp.int32), axis=1)


def pair_step(early, later):
    return (early[0] * later[0], later[0] * early[1] + later[1])


def plain_dot(left, right):
    return jnp.dot(left, right, preferred_element_type=jnp.float32)


def times_trans(left, right):
    return lax.dot_general(
        left, right, (((1,), (1,)), ((), ())), preferred_element_type=jnp.float32
    )


def trans_times(left, right):
    return lax.dot_general(
        left, right, (((0,), (0,)), ((), ())), preferred_element_type=jnp.float32
    )


def gelu_tanh(values):
    return jax.nn.gelu(values, approximate=True)


def collect(
    norm_gain,
    mlp_gain,
    x_weight,
    y_weight,
    recur_gate_weight,
    input_gate_weight,
    gate_weight,
    up_weight,
    out_weight,
    down_weight,
):
    return (
        lax.all_gather(norm_gain, "dp", axis=0, tiled=True),
        lax.all_gather(mlp_gain, "dp", axis=0, tiled=True),
        lax.all_gather(x_weight, "dp", axis=0, tiled=True),
        lax.all_gather(y_weight, "dp", axis=0, tiled=True),
        lax.all_gather(recur_gate_weight, "dp", axis=0, tiled=True),
        lax.all_gather(input_gate_weight, "dp", axis=0, tiled=True),
        lax.all_gather(gate_weight, "dp", axis=0, tiled=True),
        lax.all_gather(up_weight, "dp", axis=0, tiled=True),
        lax.all_gather(out_weight, "dp", axis=1, tiled=True),
        lax.all_gather(down_weight, "dp", axis=1, tiled=True),
    )


def row_sums(term_rows, tok_rows):
    return lax.psum_scatter(
        term_rows(jnp.int32(0), lax.axis_size("tensor") * tok_rows).astype(jnp.bfloat16),
        "tensor",
        scatter_dimension=0,
        tiled=True,
    ).astype(jnp.float32)


def spread_rows(values):
    return lax.all_gather(values, "tensor", axis=0, tiled=True)


def local_general(
    tokens,
    norm_gain,
    x_weight,
    y_weight,
    conv_weight,
    recur_gate_weight,
    input_gate_weight,
    decay_param,
    out_weight,
    mlp_gain,
    gate_weight,
    up_weight,
    down_weight,
    seq_lengths,
    token_order,
    cotangent,
):
    n_tensor = lax.axis_size("tensor")
    tensor_index = lax.axis_index("tensor")
    dp_index = lax.axis_index("dp")
    tok_rows = tokens.shape[0]
    row_count = tok_rows * n_tensor
    own_width = conv_weight.shape[1]
    kernel_taps = conv_weight.shape[0]
    edge_rows = kernel_taps - 1
    dp_width = norm_gain.shape[0]
    own_start = tensor_index * tok_rows
    shards = (
        norm_gain,
        mlp_gain,
        x_weight,
        y_weight,
        recur_gate_weight,
        input_gate_weight,
        gate_weight,
        up_weight,
        out_weight,
        down_weight,
    )
    (
        gain_one,
        gain_two,
        x_full,
        y_full,
        recur_full,
        input_full,
        gate_full,
        up_full,
        out_full,
        down_full,
    ) = collect(*shards)
    block_size = recur_full.shape[0]
    first_gain = gain_one.astype(jnp.float32)
    second_gain = gain_two.astype(jnp.float32)
    both_gates = jnp.concatenate([recur_full, input_full], axis=1)
    tok_own = tokens.astype(jnp.float32)
    own_order = token_order - dp_index * row_count
    first_rows = rms_scale(tok_own, first_gain).astype(jnp.bfloat16)
    first_all, cot_all, order_all = (
        lax.all_gather(first_rows, "tensor", axis=0, tiled=True),
        lax.all_gather(cotangent, "tensor", axis=0, tiled=True),
        lax.all_gather(own_order, "tensor", axis=0, tiled=True),
    )
    row_index = jnp.arange(row_count, dtype=jnp.int32)
    inverse = jnp.zeros((row_count,), jnp.int32).at[order_all].set(row_index)
    hidden_place = jnp.take(first_all, inverse, axis=0)
    places = dp_index * row_count + row_index
    ends = jnp.cumsum(seq_lengths)
    segment = segment_of(places, ends)
    starts = (places == 0) | (segment != segment_of(places - 1, ends))
    live = (places < ends[-1]).astype(jnp.float32)
    live_stored = jnp.take(live, order_all, axis=0)
    same = [
        (segment_of(places - shift, ends) == segment).astype(jnp.float32)
        for shift in range(kernel_taps)
    ]
    low_edge = tensor_index * own_width
    own_blocks = (low_edge + jnp.arange(own_width, dtype=jnp.int32)) // block_size
    first_block = low_edge // block_size
    block_count = own_width // block_size + 2

    def block_start(index):
        return (first_block + index) * block_size - low_edge + block_size

    def block_mask(index):
        inside = own_blocks == first_block + index
        return jnp.concatenate([inside, inside])

    def convolve(extended, kernel):
        return sum(
            (
                kernel[shift][None, :]
                * extended[edge_rows - shift : edge_rows - shift + row_count]
                * same[shift][:, None]
                for shift in range(kernel_taps)
            )
        )

    def gates(conv_vals, pre_recur, pre_input, decay_vals):
        log_rate = -rate_scale * jax.nn.sigmoid(pre_recur) * jax.nn.softplus(-decay_vals)
        decay_rate = jnp.where(starts[:, None], 0.0, jnp.exp(log_rate))
        scale_in = jnp.where(starts[:, None], 1.0, jnp.sqrt(-jnp.expm1(2.0 * log_rate)))
        return (decay_rate, conv_vals * jax.nn.sigmoid(pre_input) * scale_in)

    def glu(gate_pre, up_pre):
        return gelu_tanh(gate_pre) * up_pre

    x_branch = plain_dot(hidden_place, x_full).astype(jnp.bfloat16)
    y_before = plain_dot(hidden_place, y_full)
    previous = from_behind(x_branch[row_count - edge_rows :], "dp", 1)
    extended = jnp.concatenate([previous, x_branch], axis=0).astype(jnp.float32)
    conv_out = convolve(extended, conv_weight)
    conv_wide = extended_2(conv_out.astype(jnp.bfloat16), (("tensor", 1),), block_size)
    pre_both = jnp.zeros((row_count, 2 * own_width), jnp.float32)
    for index in range(block_count):
        piece = lax.dynamic_slice_in_dim(conv_wide, block_start(index), block_size, 1)
        pre_both = pre_both + jnp.where(
            block_mask(index)[None, :], plain_dot(piece, both_gates), 0.0
        )
    (decay_rate, driven), gate_pull = jax.vjp(
        gates, conv_out, pre_both[:, :own_width], pre_both[:, own_width:], decay_param
    )
    cum_rate, local_state = lax.associative_scan(pair_step, (decay_rate, driven), axis=0)
    ident = (jnp.ones((own_width,), jnp.float32), jnp.zeros((own_width,), jnp.float32))
    rate_in, state_in = entering((cum_rate[-1], local_state[-1]), "dp", pair_step, ident, False)
    state = local_state + cum_rate * state_in[None, :]
    y_branch = gelu_tanh(y_before)
    merged = (state * y_branch).astype(jnp.bfloat16)
    merged_stored = jnp.take(merged, order_all, axis=0)

    def mixer_rows(begin, number):
        return plain_dot(merged_stored, out_full)

    after_own = tok_own + row_sums(mixer_rows, tok_rows)
    hidden_two = spread_rows(rms_scale(after_own, second_gain).astype(jnp.bfloat16))
    gate_pre = plain_dot(hidden_two, gate_full)
    up_pre = plain_dot(hidden_two, up_full)
    glu_out, glu_pull = jax.vjp(glu, gate_pre, up_pre)
    product = glu_out.astype(jnp.bfloat16)

    def down_rows(begin, number):
        return plain_dot(product, down_full)

    feed_out = row_sums(down_rows, tok_rows)
    live_own = lax.dynamic_slice_in_dim(live_stored, own_start, tok_rows, 0)
    output = ((after_own + feed_out) * live_own[:, None]).astype(jnp.bfloat16)
    grad_out = cot_all.astype(jnp.float32) * live_stored[:, None]
    fresh = lax.optimization_barrier((shards, grad_out))[0]
    (
        gain_one,
        gain_two,
        x_full,
        y_full,
        recur_full,
        input_full,
        gate_full,
        up_full,
        out_full,
        down_full,
    ) = collect(*fresh)
    first_gain = gain_one.astype(jnp.float32)
    second_gain = gain_two.astype(jnp.float32)
    both_gates = jnp.concatenate([recur_full, input_full], axis=1)
    down_in = grad_out.astype(jnp.bfloat16)
    grad_down = trans_times(product, down_in)
    grad_product = times_trans(down_in, down_full)
    grad_gate_pre, grad_up_pre = glu_pull(grad_product)
    grad_gate_pre = grad_gate_pre.astype(jnp.bfloat16)
    grad_up_pre = grad_up_pre.astype(jnp.bfloat16)
    grad_gate = trans_times(hidden_two, grad_gate_pre)
    grad_up = trans_times(hidden_two, grad_up_pre)

    def feed_rows(begin, number):
        return times_trans(grad_gate_pre, gate_full) + times_trans(grad_up_pre, up_full)

    grad_out_own = lax.dynamic_slice_in_dim(grad_out, own_start, tok_rows, 0)
    grad_two_own = row_sums(feed_rows, tok_rows)
    grad_norm_own, normed_two = norm_back(after_own, second_gain, grad_two_own)
    second_part = jnp.sum(grad_two_own * normed_two, axis=0)
    grad_after_own = grad_out_own + grad_norm_own
    mixer_in = spread_rows(grad_after_own.astype(jnp.bfloat16))
    grad_out_mat = trans_times(merged_stored, mixer_in)
    grad_merged = jnp.take(times_trans(mixer_in, out_full), inverse, axis=0)
    grad_state = grad_merged * y_branch
    gelu_pull = jax.vjp(gelu_tanh, y_before)[1]
    grad_y_before = gelu_pull(grad_merged * state)[0].astype(jnp.bfloat16)
    rate_next = jnp.concatenate([decay_rate[1:], jnp.ones((1, own_width), jnp.float32)], axis=0)
    rev_rate, local_lam = lax.associative_scan(
        pair_step, (rate_next, grad_state), reverse=True, axis=0
    )
    head_rate = decay_rate[0] * rev_rate[0]
    head_lam = decay_rate[0] * local_lam[0]
    factor_in, lam_in = entering((head_rate, head_lam), "dp", pair_step, ident, True)
    lam = local_lam + rev_rate * lam_in[None, :]
    state_prev = jnp.concatenate([state_in[None, :], state[:-1]], axis=0)
    grad_conv_local, grad_pre_recur, grad_pre_input, grad_decay_own = gate_pull(
        (lam * state_prev, lam)
    )
    grad_pre = jnp.concatenate([grad_pre_recur, grad_pre_input], axis=1).astype(jnp.bfloat16)
    grad_both = jnp.zeros((block_size, 2 * own_width), jnp.float32)
    grad_wide = jnp.zeros((row_count, own_width + 2 * block_size), jnp.float32)
    for index in range(block_count):
        begin = block_start(index)
        piece = lax.dynamic_slice_in_dim(conv_wide, begin, block_size, 1)
        masked = jnp.where(block_mask(index)[None, :], grad_pre, jnp.zeros((), jnp.bfloat16))
        grad_both = grad_both + trans_times(piece, masked)
        added = lax.dynamic_slice_in_dim(grad_wide, begin, block_size, 1) + times_trans(
            masked, both_gates
        )
        grad_wide = lax.dynamic_update_slice_in_dim(grad_wide, added, begin, 1)
    grad_recur = grad_both[:, :own_width]
    grad_input = grad_both[:, own_width:]
    rims = jnp.concatenate(
        [grad_wide[:, :block_size], grad_wide[:, own_width + block_size :]], axis=1
    )
    arrived = extended_2(rims.astype(jnp.bfloat16), (("tensor", 1),), block_size).astype(rims.dtype)
    from_lower = jnp.pad(arrived[:, :block_size], ((0, 0), (0, own_width - block_size)))
    from_upper = jnp.pad(arrived[:, 3 * block_size :], ((0, 0), (own_width - block_size, 0)))
    grad_conv = (
        grad_conv_local
        + grad_wide[:, block_size : block_size + own_width]
        + from_lower
        + from_upper
    )
    conv_pull = jax.vjp(convolve, extended, conv_weight)[1]
    grad_extended, grad_kernel = conv_pull(grad_conv)
    returned = from_behind(grad_extended[:edge_rows], "dp", -1)
    grad_x_branch = grad_extended[edge_rows:] + jnp.concatenate(
        [jnp.zeros((row_count - edge_rows, own_width), jnp.float32), returned], axis=0
    )
    grad_x_low = grad_x_branch.astype(jnp.bfloat16)
    grad_x_stored = jnp.take(grad_x_low, order_all, axis=0)
    grad_y_stored = jnp.take(grad_y_before, order_all, axis=0)
    grad_x_mat = trans_times(first_all, grad_x_stored)
    grad_y_mat = trans_times(first_all, grad_y_stored)

    def mixer_back_rows(begin, number):
        return times_trans(grad_x_stored, x_full) + times_trans(grad_y_stored, y_full)

    grad_one_own = row_sums(mixer_back_rows, tok_rows)
    grad_norm_one, normed_one = norm_back(tok_own, first_gain, grad_one_own)
    first_part = jnp.sum(grad_one_own * normed_one, axis=0)
    grad_tokens = grad_after_own + grad_norm_one
    chosen = jnp.arange(n_tensor, dtype=jnp.int32) == tensor_index
    kernel_tile = jnp.where(chosen[:, None, None], grad_kernel[None, :, :], 0.0)
    decay_tile = jnp.where(chosen[:, None], grad_decay_own[None, :], 0.0)
    small = lax.psum((first_part, second_part, kernel_tile, decay_tile), ("dp", "tensor"))
    grad_first_gain = lax.dynamic_slice_in_dim(small[0], dp_index * dp_width, dp_width, 0)
    grad_second_gain = lax.dynamic_slice_in_dim(small[1], dp_index * dp_width, dp_width, 0)
    grad_kernel_sum = lax.dynamic_index_in_dim(small[2], tensor_index, 0, keepdims=False)
    grad_decay = lax.dynamic_index_in_dim(small[3], tensor_index, 0, keepdims=False)
    sums = (
        lax.psum_scatter(
            grad_x_mat.astype(jnp.bfloat16), "dp", scatter_dimension=0, tiled=True
        ).astype(jnp.float32),
        lax.psum_scatter(
            grad_y_mat.astype(jnp.bfloat16), "dp", scatter_dimension=0, tiled=True
        ).astype(jnp.float32),
        lax.psum_scatter(
            grad_recur.astype(jnp.bfloat16), "dp", scatter_dimension=0, tiled=True
        ).astype(jnp.float32),
        lax.psum_scatter(
            grad_input.astype(jnp.bfloat16), "dp", scatter_dimension=0, tiled=True
        ).astype(jnp.float32),
        lax.psum_scatter(
            grad_gate.astype(jnp.bfloat16), "dp", scatter_dimension=0, tiled=True
        ).astype(jnp.float32),
        lax.psum_scatter(
            grad_up.astype(jnp.bfloat16), "dp", scatter_dimension=0, tiled=True
        ).astype(jnp.float32),
        lax.psum_scatter(
            grad_out_mat.astype(jnp.bfloat16), "dp", scatter_dimension=1, tiled=True
        ).astype(jnp.float32),
        lax.psum_scatter(
            grad_down.astype(jnp.bfloat16), "dp", scatter_dimension=1, tiled=True
        ).astype(jnp.float32),
    )
    return (
        output,
        grad_tokens,
        grad_first_gain,
        sums[0],
        sums[1],
        grad_kernel_sum,
        sums[2],
        sums[3],
        grad_decay,
        sums[6],
        grad_second_gain,
        sums[4],
        sums[5],
        sums[7],
    )


MESH = pl.DeviceIdType.MESH
VMEM_BYTES = 60 * 2**20


def remote(src, dst, send, recv, device):
    return pltpu.make_async_remote_copy(
        src_ref=src,
        dst_ref=dst,
        send_sem=send,
        recv_sem=recv,
        device_id=device,
        device_id_type=MESH,
    )


class Place:
    def __init__(self, n_dp, n_line):
        self.n_dp, self.n_line = n_dp, n_line
        self.d, self.t = lax.axis_index("dp"), lax.axis_index("tensor")
        self.core = lax.rem(self.d, 2)
        self.x = lax.rem(lax.div(self.d, 2), 2)
        self.y = lax.div(self.d, 4)

    def chip(self, flip_x, flip_y, flip_core=0):
        x = 1 - self.x if flip_x else self.x
        y = 1 - self.y if flip_y else self.y
        core = 1 - self.core if flip_core else self.core
        return y * 4 + x * 2 + core

    def at(self, flip_x=0, flip_y=0, flip_core=0):
        return (self.chip(flip_x, flip_y, flip_core), self.t)

    def up(self):
        return (self.d, lax.rem(self.t + 1, self.n_line))

    def down(self):
        return (self.d, lax.rem(self.t + self.n_line - 1, self.n_line))

    def meet(self, everyone=False):
        barrier = pltpu.get_barrier_semaphore()

        def greet(device):
            pl.semaphore_signal(barrier, inc=1, device_id=device, device_id_type=MESH)

        if everyone:
            for i in range(1, self.n_dp):
                greet((lax.rem(self.d + i, self.n_dp), self.t))
            for i in range(1, self.n_line):
                greet((self.d, lax.rem(self.t + i, self.n_line)))
            pl.semaphore_wait(barrier, self.n_dp + self.n_line - 2)
            return
        for flips in ((1, 0), (0, 1), (0, 0, 1)):
            greet(self.at(*flips))
        below, above = self.t > 0, self.t < self.n_line - 1

        @pl.when(below)
        def _():
            greet(self.down())

        @pl.when(above)
        def _():
            greet(self.up())

        pl.semaphore_wait(barrier, 3 + below.astype(jnp.int32) + above.astype(jnp.int32))


class GatherPlane:
    def __init__(self, place, src, dst, send, recv, local):
        self.p, self.src, self.dst = place, src, dst
        self.rows = src.shape[0]
        self.send, self.recv, self.local = send, recv, local

    def block(self, fx, fy, fc=0, part=None):
        first = self.p.chip(fx, fy, fc) * self.rows
        size = self.rows
        if part is not None:
            size = self.rows // 2
            first = first + part * size
        return self.dst.at[pl.ds(pl.multiple_of(first, 16), size)]

    def copy(self, i, src, dst, device):
        return remote(src, dst, self.send.at[i], self.recv.at[i], device)

    def mine(self):
        return pltpu.make_async_copy(self.src, self.block(0, 0), self.local)

    def outgoing(self, i):
        at, block = self.p.at, self.block
        if i == 0:
            return self.copy(0, self.src, block(0, 0), at(1, 0))
        if i == 1:
            return self.copy(1, self.src, block(0, 0), at(0, 1))
        if i == 2:
            return self.copy(2, self.src, block(0, 0), at(0, 0, 1))
        if i == 3:
            return self.copy(3, block(1, 0, 0, 0), block(1, 0, 0, 0), at(0, 1))
        if i == 4:
            return self.copy(4, block(0, 1, 0, 1), block(0, 1, 0, 1), at(1, 0))
        spot = ((1, 0), (0, 1), (1, 1, 0, 0), (1, 1, 0, 1))[i - 5]
        return self.copy(i, block(*spot), block(*spot), at(0, 0, 1))

    def arrive(self, i):
        spot = (
            (1, 0),
            (0, 1),
            (0, 0, 1),
            (1, 1, 0, 0),
            (1, 1, 0, 1),
            (1, 0, 1),
            (0, 1, 1),
            (1, 1, 1, 0),
            (1, 1, 1, 1),
        )[i]
        here = self.block(*spot)
        self.copy(i, here, here, self.p.at(0, 0, 1)).wait_recv()

    def begin(self):
        self.mine().start()
        for i in (0, 1, 2):
            self.outgoing(i).start()

    def forward(self):
        self.arrive(0)
        self.outgoing(3).start()
        self.arrive(1)
        self.outgoing(4).start()
        self.outgoing(5).start()
        self.outgoing(6).start()

    def share(self):
        self.arrive(3)
        self.outgoing(7).start()
        self.arrive(4)
        self.outgoing(8).start()

    def finish(self):
        for i in (2, 5, 6, 7, 8):
            self.arrive(i)
        for i in range(9):
            self.outgoing(i).wait_send()
        self.mine().wait()


class GatherLine:
    def __init__(self, place, dst, rows, begin, span, send, recv):
        self.p, self.dst, self.rows = place, dst, rows
        self.begin, self.span = begin, span
        self.send, self.recv = send, recv
        self.last = place.n_line - 1

    def block(self, owner):
        first = owner * self.rows + self.begin
        return self.dst.at[pl.ds(pl.multiple_of(first, 8), self.span)]

    def copy(self, way, k, owner, source=None):
        to = self.p.up() if way == 0 else self.p.down()
        block = self.block(owner)
        return remote(
            block if source is None else source,
            block,
            self.send.at[way, k],
            self.recv.at[way, k],
            to,
        )

    def step(self, k, source=None):
        t, last = self.p.t, self.last
        if k > 0:
            self.arrive(k - 1)

        @pl.when((t < last) & (t >= k))
        def _():
            self.copy(0, k, t - k, source).start()

        @pl.when((t > 0) & (t + k <= last))
        def _():
            self.copy(1, k, t + k, source).start()

    def arrive(self, k):
        t, last = self.p.t, self.last

        @pl.when(t >= k + 1)
        def _():
            self.copy(0, k, t - 1 - k).wait_recv()

        @pl.when(t + k + 1 <= last)
        def _():
            self.copy(1, k, t + 1 + k).wait_recv()

    def finish(self):
        t, last = self.p.t, self.last
        self.arrive(last - 1)
        for k in range(last):

            @pl.when((t < last) & (t >= k))
            def _():
                self.copy(0, k, t - k).wait_send()

            @pl.when((t > 0) & (t + k <= last))
            def _():
                self.copy(1, k, t + k).wait_send()


class ReduceLine:
    def __init__(self, place, terms, rows, begin, span, stage, inbox, send, recv):
        self.p, self.terms, self.rows = place, terms, rows
        self.begin, self.span = begin, span
        self.stage, self.inbox = stage, inbox
        self.send, self.recv = send, recv
        self.last = place.n_line - 1

    def own(self, owner):
        first = owner * self.rows + self.begin
        return self.terms.at[pl.ds(pl.multiple_of(first, 16), self.span)]

    def copy(self, way, j, source):
        to = self.p.up() if way == 0 else self.p.down()
        return remote(
            source, self.inbox.at[way, j], self.send.at[way, j], self.recv.at[way, j], to
        )

    def step(self, j):
        t, last = self.p.t, self.last
        for way in (0, 1):
            owner = last - j if way == 0 else j
            first = (t == 0) if way == 0 else (t == last)
            passing = (t > 0) & (t < owner) if way == 0 else (t < last) & (t > owner)
            term = self.own(owner)

            @pl.when(first)
            def _():
                self.copy(way, j, term).start()

            @pl.when(passing)
            def _():
                self.copy(way, j, term).wait_recv()
                self.stage[way, j] = (
                    term[...].astype(jnp.float32) + self.inbox[way, j].astype(jnp.float32)
                ).astype(jnp.bfloat16)
                self.copy(way, j, self.stage.at[way, j]).start()

    def total(self, result):
        t, last = self.p.t, self.last
        result[...] = self.own(t)[...].astype(jnp.float32)

        @pl.when(t > 0)
        def _():
            j = last - t
            self.copy(0, j, self.stage.at[0, 0]).wait_recv()
            result[...] += self.inbox[0, j].astype(jnp.float32)

        @pl.when(t < last)
        def _():
            self.copy(1, t, self.stage.at[0, 0]).wait_recv()
            result[...] += self.inbox[1, t].astype(jnp.float32)

    def finish(self):
        t, last = self.p.t, self.last
        for j in range(last):

            @pl.when(t < last - j)
            def _():
                self.copy(0, j, self.stage.at[0, j]).wait_send()

            @pl.when(t > j)
            def _():
                self.copy(1, j, self.stage.at[1, j]).wait_send()


def add_rows(into, other, result=None):
    result = into if result is None else result

    def tile(i, carry):
        rows = pl.ds(pl.multiple_of(i * 16, 16), 16)
        result[rows] = (
            into[rows].astype(jnp.float32) + other[rows].astype(jnp.float32)
        ).astype(result.dtype)
        return carry

    lax.fori_loop(0, into.shape[0] // 16, tile, None)


class ReducePlane:
    chips = ((0, 0), (1, 0), (0, 1), (1, 1))

    def __init__(self, place, terms, scratch):
        self.p, self.terms = place, terms
        self.held, self.near, self.along, self.last, self.send, self.recv, self.local = scratch
        self.rows = self.held.shape[1]
        self.half = self.rows // 2

    @staticmethod
    def scratch(rows, width):
        return [
            pltpu.VMEM((4, rows, width), jnp.bfloat16),
            pltpu.VMEM((4, rows, width), jnp.bfloat16),
            pltpu.VMEM((4, rows // 2, width), jnp.bfloat16),
            pltpu.VMEM((2, rows // 2, width), jnp.bfloat16),
            pltpu.SemaphoreType.DMA((10,)),
            pltpu.SemaphoreType.DMA((10,)),
            pltpu.SemaphoreType.DMA((4,)),
        ]

    def block(self, k, other):
        first = self.p.chip(*self.chips[k], other) * self.rows
        return self.terms.at[pl.ds(pl.multiple_of(first, 16), self.rows)]

    def half_of(self, k, part):
        return self.held.at[k, pl.ds(part * self.half, self.half)]

    def load(self, k):
        return pltpu.make_async_copy(self.block(k, 0), self.held.at[k], self.local.at[k])

    def copy(self, i):
        at = self.p.at
        if i < 4:
            src, dst, to = self.block(i, 1), self.near.at[i], at(0, 0, 1)
        elif i < 8:
            src, to = (
                (self.half_of(1, 0), at(1, 0)),
                (self.half_of(3, 0), at(1, 0)),
                (self.half_of(2, 1), at(0, 1)),
                (self.half_of(3, 1), at(0, 1)),
            )[i - 4]
            dst = self.along.at[i - 4]
        else:
            src, to = ((self.half_of(2, 0), at(0, 1)), (self.half_of(1, 1), at(1, 0)))[i - 8]
            dst = self.last.at[i - 8]
        return remote(src, dst, self.send.at[i], self.recv.at[i], to)

    def begin(self):
        for k in (3, 1, 2, 0):
            self.copy(k).start()
            self.load(k).start()

    def cores(self):
        for k in (3, 1, 2, 0):
            self.load(k).wait()
            self.copy(k).wait_recv()
            add_rows(self.held.at[k], self.near.at[k])
            if k == 3:
                self.copy(5).start()
                self.copy(7).start()
            elif k == 1:
                self.copy(4).start()
            elif k == 2:
                self.copy(6).start()

    def turn(self):
        self.copy(5).wait_recv()
        add_rows(self.half_of(2, 0), self.along.at[1])
        self.copy(8).start()
        self.copy(7).wait_recv()
        add_rows(self.half_of(1, 1), self.along.at[3])
        self.copy(9).start()
        self.copy(4).wait_recv()
        add_rows(self.half_of(0, 0), self.along.at[0])
        self.copy(6).wait_recv()
        add_rows(self.half_of(0, 1), self.along.at[2])

    def finish(self, result):
        for part in (0, 1):
            self.copy(8 + part).wait_recv()
            rows = pl.ds(part * self.half, self.half)
            add_rows(self.half_of(0, part), self.last.at[part], result.at[rows])
        for i in range(10):
            self.copy(i).wait_send()


def dma_sems(*dims):
    return pltpu.SemaphoreType.DMA(dims)


def in_vmem():
    return pl.BlockSpec(memory_space=pltpu.VMEM)


def in_any():
    return pl.BlockSpec(memory_space=pl.ANY)


def comm_params(number):
    return pltpu.CompilerParams(
        collective_id=number, has_side_effects=True, vmem_limit_bytes=VMEM_BYTES
    )


def shaped(dims, kind):
    return jax.ShapeDtypeStruct(dims, kind)


def first_gather(n_dp, n_line, mats, minor, rows_in, order):
    def kernel(a, b, c, e, a_out, b_out, c_out, e_out, ps, pr, pl_sem, ls, lr, ll):
        place = Place(n_dp, n_line)
        place.meet()
        planes = [
            GatherPlane(place, a, a_out, ps.at[0], pr.at[0], pl_sem.at[0]),
            GatherPlane(place, b, b_out, ps.at[1], pr.at[1], pl_sem.at[1]),
        ]
        lines, copies = [], []
        for i, (src, dst) in enumerate(((c, c_out), (e, e_out))):
            rows = src.shape[0]
            lines.append(GatherLine(place, dst, rows, 0, rows, ls.at[i], lr.at[i]))
            own = dst.at[pl.ds(pl.multiple_of(place.t * rows, 8), rows)]
            copies.append(pltpu.make_async_copy(src, own, ll.at[i]))
        for copy in copies:
            copy.start()
        lines[0].step(0, c)
        lines[1].step(0, e)
        planes[0].begin()
        planes[1].begin()
        lines[0].step(1)
        lines[1].step(1)
        planes[0].forward()
        planes[1].forward()
        lines[0].step(2)
        lines[1].step(2)
        planes[0].share()
        planes[1].share()
        for part in lines + planes:
            part.finish()
        for copy in copies:
            copy.wait()

    return pl.pallas_call(
        kernel,
        out_shape=(
            shaped((n_dp * mats.shape[0], mats.shape[1]), mats.dtype),
            shaped((n_dp * minor.shape[0], minor.shape[1]), minor.dtype),
            shaped((n_line * rows_in.shape[0], rows_in.shape[1]), rows_in.dtype),
            shaped((n_line * order.shape[0], order.shape[1]), order.dtype),
        ),
        in_specs=[in_any()] * 4,
        out_specs=[in_any()] * 4,
        scratch_shapes=[
            dma_sems(2, 9),
            dma_sems(2, 9),
            dma_sems(2),
            dma_sems(2, 2, n_line - 1),
            dma_sems(2, 2, n_line - 1),
            dma_sems(2),
        ],
        compiler_params=comm_params(1),
        name="first_gather",
    )(mats, minor, rows_in, order)


CHUNKS = 4


def line_scratch(n_line, span, width):
    hops = n_line - 1
    return [
        pltpu.VMEM((CHUNKS, 2, hops, span, width), jnp.bfloat16),
        pltpu.VMEM((CHUNKS, 2, hops, span, width), jnp.bfloat16),
        dma_sems(CHUNKS, 2, hops),
        dma_sems(CHUNKS, 2, hops),
        dma_sems(CHUNKS, 2, hops),
        dma_sems(CHUNKS, 2, hops),
        pltpu.VMEM((span, width), jnp.float32),
    ]


def sum_rows_and_spread(place, terms, scratch, finish_rows, spread, between):
    stage, inbox, rs, rr, gs, gr, total = scratch
    span = total.shape[0]
    rows = span * CHUNKS
    hops = place.n_line - 1
    sums = [
        ReduceLine(place, terms, rows, c * span, span, stage.at[c], inbox.at[c], rs.at[c], rr.at[c])
        for c in range(CHUNKS)
    ]
    gathers = []
    if spread is not None:
        gathers = [
            GatherLine(place, spread, rows, c * span, span, gs.at[c], gr.at[c])
            for c in range(CHUNKS)
        ]
    for c in range(CHUNKS + 1):
        for j in range(hops):
            if c < CHUNKS:
                sums[c].step(j)
            if c > 0 and gathers:
                gathers[c - 1].step(j)
        if c < CHUNKS:
            sums[c].total(total)
            finish_rows(c, pl.ds(c * span, span), total)
        if c < len(between):
            between[c]()
    for part in gathers + sums:
        part.finish()


def middle_gather(n_dp, n_line, terms, tokens, gain, mats):
    rows, width = tokens.shape
    count = len(mats)

    def kernel(*refs):
        s, tok, gain_ref = refs[:3]
        srcs = refs[3 : 3 + count]
        after, hidden = refs[3 + count : 5 + count]
        dsts = refs[5 + count : 5 + 2 * count]
        ps, pr, pl_sem = refs[5 + 2 * count : 8 + 2 * count]
        scratch = refs[8 + 2 * count :]
        place = Place(n_dp, n_line)
        place.meet()
        planes = [
            GatherPlane(place, a, b, ps.at[i], pr.at[i], pl_sem.at[i])
            for i, (a, b) in enumerate(zip(srcs, dsts))
        ]
        for part in planes:
            part.begin()

        def norm(c, here, total):
            values = tok[here].astype(jnp.float32) + total[...]
            after[here] = values
            low = rms_scale(values, gain_ref[...]).astype(jnp.bfloat16)
            first = pl.multiple_of(place.t * rows, 16) + c * total.shape[0]
            hidden[pl.ds(pl.multiple_of(first, 16), total.shape[0])] = low

        sum_rows_and_spread(place, s, scratch, norm, hidden, [])
        for part in planes:
            part.forward()
        for part in planes:
            part.share()
        for part in planes:
            part.finish()

    return pl.pallas_call(
        kernel,
        out_shape=(
            shaped((rows, width), jnp.float32),
            shaped((n_line * rows, width), jnp.bfloat16),
        )
        + tuple(shaped((n_dp * m.shape[0], m.shape[1]), m.dtype) for m in mats),
        in_specs=[in_vmem()] * 3 + [in_any()] * count,
        out_specs=[in_vmem()] * 2 + [in_any()] * count,
        scratch_shapes=[dma_sems(count, 9), dma_sems(count, 9), dma_sems(count)]
        + line_scratch(n_line, rows // CHUNKS, width),
        compiler_params=comm_params(2),
        name="middle_gather",
    )(terms, tokens, gain, *mats)


def middle_sums(n_dp, n_line, terms, after, gain, grad_in, mats):
    rows, width = after.shape
    count = len(mats)
    block = mats[0].shape[0] // n_dp
    per = len(ReducePlane.scratch(16, 128))

    def kernel(*refs):
        s, after_ref, gain_ref, g_ref = refs[:4]
        srcs = refs[4 : 4 + count]
        grad_after, gain_sum, spread = refs[4 + count : 7 + count]
        results = refs[7 + count : 7 + 2 * count]
        rest = refs[7 + 2 * count :]
        scratch = rest[count * per :]
        place = Place(n_dp, n_line)
        place.meet()
        planes = [
            ReducePlane(place, srcs[i], rest[i * per : (i + 1) * per]) for i in range(count)
        ]
        for part in planes:
            part.begin()
        gain_sum[...] = jnp.zeros_like(gain_sum)

        def norm(c, here, total):
            grad = total[...]
            grad_rows, normed = norm_back(after_ref[here], gain_ref[...], grad)
            gain_sum[...] += jnp.sum(grad * normed, axis=0, keepdims=True)
            both = g_ref[here].astype(jnp.float32) + grad_rows
            grad_after[here] = both
            first = pl.multiple_of(place.t * rows, 16) + c * total.shape[0]
            spread[pl.ds(pl.multiple_of(first, 16), total.shape[0])] = both.astype(jnp.bfloat16)

        between = [planes[0].cores, planes[1].cores, planes[0].turn]
        sum_rows_and_spread(place, s, scratch, norm, spread, between)
        planes[1].turn()
        for part, result in zip(planes, results):
            part.finish(result)

    return pl.pallas_call(
        kernel,
        out_shape=(
            shaped((rows, width), jnp.float32),
            shaped((1, width), jnp.float32),
            shaped((n_line * rows, width), jnp.bfloat16),
        )
        + tuple(shaped((block, m.shape[1]), jnp.bfloat16) for m in mats),
        in_specs=[in_vmem()] * 4 + [in_any()] * count,
        out_specs=[in_vmem()] * (3 + count),
        scratch_shapes=sum([ReducePlane.scratch(block, m.shape[1]) for m in mats], [])
        + line_scratch(n_line, rows // CHUNKS, width),
        compiler_params=comm_params(3),
        name="middle_sums",
    )(terms, after, gain, grad_in, *mats)


class Exchange:
    def __init__(self, place, axis, src, slots, send, recv, local):
        self.p, self.src, self.slots = place, src, slots
        self.over_dp = axis == "dp"
        self.size = place.n_dp if self.over_dp else place.n_line
        self.me = place.d if self.over_dp else place.t
        self.send, self.recv, self.local = send, recv, local

    def copy(self, i):
        to = lax.rem(self.me + i, self.size)
        device = (to, self.p.t) if self.over_dp else (self.p.d, to)
        return remote(
            self.src, self.slots.at[self.me], self.send.at[i - 1], self.recv.at[i - 1], device
        )

    def mine(self):
        return pltpu.make_async_copy(self.src, self.slots.at[self.me], self.local)

    def begin(self):
        for i in range(1, self.size):
            self.copy(i).start()
        self.mine().start()

    def finish(self):
        self.mine().wait()
        for i in range(1, self.size):
            self.copy(i).wait()
        total = self.slots[0]
        for i in range(1, self.size):
            total = total + self.slots[i]
        return total


def last_sums(n_dp, n_line, terms, tokens, gain, grad_after, small, mats):
    rows, width = tokens.shape
    count = len(mats)
    per = len(ReducePlane.scratch(16, 128))

    def kernel(*refs):
        s, tok, gain_ref, g_ref, small_ref = refs[:5]
        srcs = refs[5 : 5 + count]
        grad_tok, small_out, first_out = refs[5 + count : 8 + count]
        results = refs[8 + count : 8 + 2 * count]
        rest = refs[8 + 2 * count :]
        own_first, row_sum = rest[count * per : count * per + 2]
        slots_a, slots_b, slots_c, slots_d = rest[count * per + 2 : count * per + 6]
        xs, xr, xl = rest[count * per + 6 : count * per + 9]
        scratch = rest[count * per + 9 :]
        place = Place(n_dp, n_line)
        place.meet(True)
        planes = [
            ReducePlane(place, srcs[i], rest[i * per : (i + 1) * per]) for i in range(count)
        ]
        for part in planes:
            part.begin()
        early = Exchange(place, "dp", small_ref, slots_a, xs.at[0], xr.at[0], xl.at[0])
        early.begin()
        own_first[...] = jnp.zeros_like(own_first)

        def norm(c, here, total):
            grad = total[...]
            grad_rows, normed = norm_back(tok[here].astype(jnp.float32), gain_ref[...], grad)
            own_first[...] += jnp.sum(grad * normed, axis=0, keepdims=True)
            grad_tok[here] = g_ref[here] + grad_rows

        def cores():
            for part in planes:
                part.cores()

        def turn():
            for part in planes:
                part.turn()

        sum_rows_and_spread(place, s, scratch, norm, None, [cores, turn])
        first = Exchange(place, "dp", own_first, slots_b, xs.at[1], xr.at[1], xl.at[1])
        first.begin()
        small_out[...] = early.finish()
        row_sum[0:1] = small_out[0:1]
        row_sum[1:2] = first.finish()
        both = Exchange(place, "tensor", row_sum, slots_c, xs.at[2], xr.at[2], xl.at[2])
        both.begin()
        for part, result in zip(planes, results):
            part.finish(result)
        first_out[...] = both.finish()

    return pl.pallas_call(
        kernel,
        out_shape=(
            shaped((rows, width), jnp.float32),
            shaped(small.shape, jnp.float32),
            shaped((2, width), jnp.float32),
        )
        + tuple(shaped((m.shape[0] // n_dp, m.shape[1]), jnp.bfloat16) for m in mats),
        in_specs=[in_vmem()] * 5 + [in_any()] * count,
        out_specs=[in_vmem()] * (3 + count),
        scratch_shapes=sum([ReducePlane.scratch(m.shape[0] // n_dp, m.shape[1]) for m in mats], [])
        + [
            pltpu.VMEM((1, width), jnp.float32),
            pltpu.VMEM((2, width), jnp.float32),
            pltpu.VMEM((n_dp,) + small.shape, jnp.float32),
            pltpu.VMEM((n_dp, 1, width), jnp.float32),
            pltpu.VMEM((n_line, 2, width), jnp.float32),
            pltpu.VMEM((1, width), jnp.float32),
            dma_sems(3, n_dp),
            dma_sems(3, n_dp),
            dma_sems(3),
        ]
        + line_scratch(n_line, rows // CHUNKS, width),
        compiler_params=comm_params(4),
        name="last_sums",
    )(terms, tokens, gain, grad_after, small, *mats)


def matches(mesh):
    return mesh.shape["dp"] == 8 and mesh.shape["tensor"] == 4


def local_blocks(
    tokens,
    norm_gain,
    x_weight,
    y_weight,
    conv_weight,
    recur_gate_weight,
    input_gate_weight,
    decay_param,
    out_weight,
    mlp_gain,
    gate_weight,
    up_weight,
    down_weight,
    seq_lengths,
    token_order,
    cotangent,
):
    n_dp, n_tensor = lax.axis_size("dp"), lax.axis_size("tensor")
    tensor_index = lax.axis_index("tensor")
    dp_index = lax.axis_index("dp")
    tok_rows, width = tokens.shape
    row_count = tok_rows * n_tensor
    own_width = conv_weight.shape[1]
    kernel_taps = conv_weight.shape[0]
    edge_rows = kernel_taps - 1
    dp_width = norm_gain.shape[0]
    gate_rows = recur_gate_weight.shape[0]
    own_start = tensor_index * tok_rows

    mats = jnp.concatenate([x_weight, y_weight, out_weight.T], axis=1)
    gains = jnp.concatenate([norm_gain, mlp_gain])
    spare = gate_rows * 128 - gains.shape[0]
    gains = jnp.pad(gains, (0, spare)).reshape(gate_rows, 128)
    minor = jnp.concatenate([recur_gate_weight, input_gate_weight, gains], axis=1)
    own_order = (token_order - dp_index * row_count).astype(jnp.int32)
    order_rows = jnp.broadcast_to(own_order[None, :], (8, tok_rows))
    mats_full, minor_full, tok_all, order_full = first_gather(
        n_dp, n_tensor, mats, minor, tokens, order_rows
    )
    down_full = lax.all_gather(down_weight.T, "dp", axis=0, tiled=True)
    cot_all = lax.all_gather(
        lax.optimization_barrier((cotangent, order_full))[0], "tensor", axis=0, tiled=True
    )
    order_all = order_full.reshape(n_tensor, 8, tok_rows)[:, 0].reshape(row_count)
    both_gates = minor_full[:, : 2 * own_width]
    gain_rows = minor_full[:, 2 * own_width :].reshape(n_dp, -1)
    first_gain = gain_rows[:, :dp_width].reshape(1, width).astype(jnp.float32)
    second_gain = gain_rows[:, dp_width : 2 * dp_width].reshape(1, width).astype(jnp.float32)
    block_size = both_gates.shape[0]
    x_full, y_full, out_full = (
        mats_full[:, :own_width],
        mats_full[:, own_width : 2 * own_width],
        mats_full[:, 2 * own_width :],
    )

    first_all = rms_scale(tok_all.astype(jnp.float32), first_gain).astype(jnp.bfloat16)
    row_index = jnp.arange(row_count, dtype=jnp.int32)
    to_place = (row_index[:, None] == order_all[None, :]).astype(jnp.bfloat16)

    def placed(stored):
        return plain_dot(to_place, stored).astype(jnp.bfloat16)

    def stored(rows):
        return trans_times(to_place, rows).astype(jnp.bfloat16)

    hidden_place = placed(first_all)
    places = dp_index * row_count + row_index
    ends = jnp.cumsum(seq_lengths)
    segment = segment_of(places, ends)
    starts = (places == 0) | (segment != segment_of(places - 1, ends))
    live_stored = (order_all + dp_index * row_count < ends[-1]).astype(jnp.float32)
    live_own = (token_order < ends[-1]).astype(jnp.float32)
    same = [
        (segment_of(places - shift, ends) == segment).astype(jnp.float32)
        for shift in range(kernel_taps)
    ]
    low_edge = tensor_index * own_width
    own_blocks = (low_edge + jnp.arange(own_width, dtype=jnp.int32)) // block_size
    first_block = low_edge // block_size
    block_count = own_width // block_size + 2

    def block_start(index):
        return (first_block + index) * block_size - low_edge + block_size

    def block_mask(index):
        inside = own_blocks == first_block + index
        return jnp.concatenate([inside, inside])

    def convolve(extended, kernel):
        return sum(
            (
                kernel[shift][None, :]
                * extended[edge_rows - shift : edge_rows - shift + row_count]
                * same[shift][:, None]
                for shift in range(kernel_taps)
            )
        )

    def gates(conv_vals, pre_recur, pre_input, decay_vals):
        log_rate = -rate_scale * jax.nn.sigmoid(pre_recur) * jax.nn.softplus(-decay_vals)
        decay_rate = jnp.where(starts[:, None], 0.0, jnp.exp(log_rate))
        scale_in = jnp.where(starts[:, None], 1.0, jnp.sqrt(-jnp.expm1(2.0 * log_rate)))
        return (decay_rate, conv_vals * jax.nn.sigmoid(pre_input) * scale_in)

    def glu(gate_pre, up_pre):
        return gelu_tanh(gate_pre) * up_pre

    x_branch = plain_dot(hidden_place, x_full).astype(jnp.bfloat16)
    y_before = plain_dot(hidden_place, y_full)
    previous = from_behind(x_branch[row_count - edge_rows :], "dp", 1)
    extended = jnp.concatenate([previous, x_branch], axis=0).astype(jnp.float32)
    conv_out = convolve(extended, conv_weight)
    conv_wide = extended_2(conv_out.astype(jnp.bfloat16), (("tensor", 1),), block_size)
    pre_both = jnp.zeros((row_count, 2 * own_width), jnp.float32)
    for index in range(block_count):
        piece = lax.dynamic_slice_in_dim(conv_wide, block_start(index), block_size, 1)
        pre_both = pre_both + jnp.where(
            block_mask(index)[None, :], plain_dot(piece, both_gates), 0.0
        )
    (decay_rate, driven), gate_pull = jax.vjp(
        gates, conv_out, pre_both[:, :own_width], pre_both[:, own_width:], decay_param
    )
    cum_rate, local_state = lax.associative_scan(pair_step, (decay_rate, driven), axis=0)
    ident = (jnp.ones((own_width,), jnp.float32), jnp.zeros((own_width,), jnp.float32))
    rate_in, state_in = entering((cum_rate[-1], local_state[-1]), "dp", pair_step, ident, False)
    state = local_state + cum_rate * state_in[None, :]
    y_branch = gelu_tanh(y_before)
    merged = (state * y_branch).astype(jnp.bfloat16)
    merged_stored = stored(merged)

    mixer_terms = times_trans(merged_stored, out_full).astype(jnp.bfloat16)
    after_own, hidden_two, gate_full, up_full = middle_gather(
        n_dp, n_tensor, mixer_terms, tokens, second_gain, (gate_weight, up_weight)
    )
    gate_pre = plain_dot(hidden_two, gate_full)
    up_pre = plain_dot(hidden_two, up_full)
    glu_out, glu_pull = jax.vjp(glu, gate_pre, up_pre)
    product = glu_out.astype(jnp.bfloat16)
    feed_out = lax.psum_scatter(
        times_trans(product, down_full).astype(jnp.bfloat16),
        "tensor",
        scatter_dimension=0,
        tiled=True,
    ).astype(jnp.float32)
    output = ((after_own + feed_out) * live_own[:, None]).astype(jnp.bfloat16)

    down_in = (cot_all.astype(jnp.float32) * live_stored[:, None]).astype(jnp.bfloat16)
    grad_in_own = (cotangent.astype(jnp.float32) * live_own[:, None]).astype(jnp.bfloat16)
    grad_down = trans_times(down_in, product).astype(jnp.bfloat16)
    grad_product = plain_dot(down_in, down_full)
    grad_gate_pre, grad_up_pre = glu_pull(grad_product)
    grad_gate_pre = grad_gate_pre.astype(jnp.bfloat16)
    grad_up_pre = grad_up_pre.astype(jnp.bfloat16)
    grad_gate = trans_times(hidden_two, grad_gate_pre).astype(jnp.bfloat16)
    grad_up = trans_times(hidden_two, grad_up_pre).astype(jnp.bfloat16)
    feed_terms = (
        times_trans(grad_gate_pre, gate_full) + times_trans(grad_up_pre, up_full)
    ).astype(jnp.bfloat16)
    down_sum = lax.psum_scatter(grad_down, "dp", scatter_dimension=0, tiled=True)
    grad_after_own, second_part, mixer_in, gate_sum, up_sum = middle_sums(
        n_dp, n_tensor, feed_terms, after_own, second_gain, grad_in_own, (grad_gate, grad_up)
    )

    grad_out_mat = trans_times(mixer_in, merged_stored).astype(jnp.bfloat16)
    out_sum = lax.psum_scatter(grad_out_mat, "dp", scatter_dimension=0, tiled=True)
    grad_merged = plain_dot(placed(mixer_in), out_full)
    grad_state = grad_merged * y_branch
    gelu_pull = jax.vjp(gelu_tanh, y_before)[1]
    grad_y_before = gelu_pull(grad_merged * state)[0].astype(jnp.bfloat16)
    rate_next = jnp.concatenate([decay_rate[1:], jnp.ones((1, own_width), jnp.float32)], axis=0)
    rev_rate, local_lam = lax.associative_scan(
        pair_step, (rate_next, grad_state), reverse=True, axis=0
    )
    head_rate = decay_rate[0] * rev_rate[0]
    head_lam = decay_rate[0] * local_lam[0]
    factor_in, lam_in = entering((head_rate, head_lam), "dp", pair_step, ident, True)
    lam = local_lam + rev_rate * lam_in[None, :]
    state_prev = jnp.concatenate([state_in[None, :], state[:-1]], axis=0)
    grad_conv_local, grad_pre_recur, grad_pre_input, grad_decay_own = gate_pull(
        (lam * state_prev, lam)
    )
    grad_pre = jnp.concatenate([grad_pre_recur, grad_pre_input], axis=1).astype(jnp.bfloat16)
    grad_both = jnp.zeros((block_size, 2 * own_width), jnp.float32)
    grad_wide = jnp.zeros((row_count, own_width + 2 * block_size), jnp.float32)
    for index in range(block_count):
        begin = block_start(index)
        piece = lax.dynamic_slice_in_dim(conv_wide, begin, block_size, 1)
        masked = jnp.where(block_mask(index)[None, :], grad_pre, jnp.zeros((), jnp.bfloat16))
        grad_both = grad_both + trans_times(piece, masked)
        added = lax.dynamic_slice_in_dim(grad_wide, begin, block_size, 1) + times_trans(
            masked, both_gates
        )
        grad_wide = lax.dynamic_update_slice_in_dim(grad_wide, added, begin, 1)
    rims = jnp.concatenate(
        [grad_wide[:, :block_size], grad_wide[:, own_width + block_size :]], axis=1
    )
    arrived = extended_2(rims.astype(jnp.bfloat16), (("tensor", 1),), block_size).astype(rims.dtype)
    from_lower = jnp.pad(arrived[:, :block_size], ((0, 0), (0, own_width - block_size)))
    from_upper = jnp.pad(arrived[:, 3 * block_size :], ((0, 0), (own_width - block_size, 0)))
    grad_conv = (
        grad_conv_local
        + grad_wide[:, block_size : block_size + own_width]
        + from_lower
        + from_upper
    )
    conv_pull = jax.vjp(convolve, extended, conv_weight)[1]
    grad_extended, grad_kernel = conv_pull(grad_conv)
    returned = from_behind(grad_extended[:edge_rows], "dp", -1)
    grad_x_branch = grad_extended[edge_rows:] + jnp.concatenate(
        [jnp.zeros((row_count - edge_rows, own_width), jnp.float32), returned], axis=0
    )
    grad_xy = stored(
        jnp.concatenate([grad_x_branch.astype(jnp.bfloat16), grad_y_before], axis=1)
    )
    grad_xy_mat = trans_times(first_all, grad_xy).astype(jnp.bfloat16)
    one_terms = times_trans(grad_xy, mats_full[:, : 2 * own_width]).astype(jnp.bfloat16)
    small = jnp.concatenate(
        [
            second_part,
            grad_kernel.reshape(1, -1),
            jnp.pad(grad_decay_own, (0, width - own_width)).reshape(1, width),
            jnp.zeros((1, width), jnp.float32),
        ],
        axis=0,
    )
    grad_tokens, small_sum, gain_sums, xy_sum, gates_sum = last_sums(
        n_dp,
        n_tensor,
        one_terms,
        tokens,
        first_gain,
        grad_after_own,
        small,
        (grad_xy_mat, grad_both.astype(jnp.bfloat16)),
    )
    xy_sum, gates_sum = xy_sum.astype(jnp.float32), gates_sum.astype(jnp.float32)
    own_gains = lax.dynamic_slice_in_dim(gain_sums, dp_index * dp_width, dp_width, 1)
    return (
        output,
        grad_tokens,
        own_gains[1],
        xy_sum[:, :own_width],
        xy_sum[:, own_width:],
        small_sum[1].reshape(kernel_taps, own_width),
        gates_sum[:, :own_width],
        gates_sum[:, own_width:],
        small_sum[2, :own_width],
        out_sum.astype(jnp.float32).T,
        own_gains[0],
        gate_sum.astype(jnp.float32),
        up_sum.astype(jnp.float32),
        down_sum.astype(jnp.float32).T,
    )


def solution(mesh):
    in_specs = (
        P(("dp", "tensor"), None),
        P("dp"),
        P("dp", "tensor"),
        P("dp", "tensor"),
        P(None, "tensor"),
        P("dp", "tensor"),
        P("dp", "tensor"),
        P("tensor"),
        P("tensor", "dp"),
        P("dp"),
        P("dp", "tensor"),
        P("dp", "tensor"),
        P("tensor", "dp"),
        P(),
        P(("dp", "tensor")),
        P(("dp", "tensor"), None),
    )
    out_specs = (
        P(("dp", "tensor"), None),
        P(("dp", "tensor"), None),
        P("dp"),
        P("dp", "tensor"),
        P("dp", "tensor"),
        P(None, "tensor"),
        P("dp", "tensor"),
        P("dp", "tensor"),
        P("tensor"),
        P("tensor", "dp"),
        P("dp"),
        P("dp", "tensor"),
        P("dp", "tensor"),
        P("tensor", "dp"),
    )
    fits = matches(mesh)
    local = local_blocks if fits else local_general
    return jax.shard_map(local, mesh=mesh, in_specs=in_specs, out_specs=out_specs, check_vma=False)
```

```python
import jax
import jax.numpy as jnp
from jax import lax
from jax.experimental import pallas as pl
from jax.experimental.pallas import tpu as pltpu
from jax.sharding import PartitionSpec as P

epsilon = 1e-06
rate_scale = 8.0


def from_behind(block, axis, distance):
    devices = range(lax.axis_size(axis))
    route = [(i - distance, i) for i in devices if i - distance in devices]
    return lax.ppermute(block, axis, route)


def extended_2(array, sides, width):
    for axis, dim in sides:
        size, length = (lax.axis_size(axis), array.shape[dim])
        up = [(i, (i + 1) % size) for i in range(size - 1)]
        down = [(j, i) for i, j in up]
        last = lax.slice_in_dim(array, length - width, length, axis=dim)
        leading = lax.slice_in_dim(array, 0, width, axis=dim)
        before = lax.ppermute(last, axis, up)
        after = lax.ppermute(leading, axis, down)
        array = jnp.concatenate([before, array, after], axis=dim)
    return array


def entering(value, axis, join, neutral, backward):
    count, mine = (lax.axis_size(axis), lax.axis_index(axis))
    pieces = jax.tree.map(lambda part: lax.all_gather(part, axis), value)
    if backward:
        pieces = jax.tree.map(lambda part: part[::-1], pieces)
        mine = count - 1 - mine
    total = jax.tree.map(
        lambda part, zero: jnp.full_like(part, 0) + jnp.asarray(zero, part.dtype), value, neutral
    )

    def lap(position, total):
        longer = join(total, jax.tree.map(lambda part: part[position], pieces))
        return jax.tree.map(lambda new, old: jnp.where(position < mine, new, old), longer, total)

    return lax.fori_loop(0, count - 1, lap, total)


def rms_scale(values, gain):
    return values * lax.rsqrt(jnp.mean(values * values, axis=-1, keepdims=True) + epsilon) * gain


def norm_back(values, gain, grad):
    inv_root = lax.rsqrt(jnp.mean(values * values, axis=-1, keepdims=True) + epsilon)
    normed = values * inv_root
    upstream = grad * gain
    grad_values = inv_root * (
        upstream - normed * jnp.mean(upstream * normed, axis=-1, keepdims=True)
    )
    return (grad_values, normed)


def segment_of(places, ends):
    return jnp.sum((ends[None, :] <= places[:, None]).astype(jnp.int32), axis=1)


def pair_step(early, later):
    return (early[0] * later[0], later[0] * early[1] + later[1])


def plain_dot(left, right):
    return jnp.dot(left, right, preferred_element_type=jnp.float32)


def times_trans(left, right):
    return lax.dot_general(
        left, right, (((1,), (1,)), ((), ())), preferred_element_type=jnp.float32
    )


def trans_times(left, right):
    return lax.dot_general(
        left, right, (((0,), (0,)), ((), ())), preferred_element_type=jnp.float32
    )


def gelu_tanh(values):
    return jax.nn.gelu(values, approximate=True)


def collect(
    norm_gain,
    mlp_gain,
    x_weight,
    y_weight,
    recur_gate_weight,
    input_gate_weight,
    gate_weight,
    up_weight,
    out_weight,
    down_weight,
):
    return (
        lax.all_gather(norm_gain, "dp", axis=0, tiled=True),
        lax.all_gather(mlp_gain, "dp", axis=0, tiled=True),
        lax.all_gather(x_weight, "dp", axis=0, tiled=True),
        lax.all_gather(y_weight, "dp", axis=0, tiled=True),
        lax.all_gather(recur_gate_weight, "dp", axis=0, tiled=True),
        lax.all_gather(input_gate_weight, "dp", axis=0, tiled=True),
        lax.all_gather(gate_weight, "dp", axis=0, tiled=True),
        lax.all_gather(up_weight, "dp", axis=0, tiled=True),
        lax.all_gather(out_weight, "dp", axis=1, tiled=True),
        lax.all_gather(down_weight, "dp", axis=1, tiled=True),
    )


def row_sums(term_rows, tok_rows):
    return lax.psum_scatter(
        term_rows(jnp.int32(0), lax.axis_size("tensor") * tok_rows).astype(jnp.bfloat16),
        "tensor",
        scatter_dimension=0,
        tiled=True,
    ).astype(jnp.float32)


def spread_rows(values):
    return lax.all_gather(values, "tensor", axis=0, tiled=True)


def local_general(
    tokens,
    norm_gain,
    x_weight,
    y_weight,
    conv_weight,
    recur_gate_weight,
    input_gate_weight,
    decay_param,
    out_weight,
    mlp_gain,
    gate_weight,
    up_weight,
    down_weight,
    seq_lengths,
    token_order,
    cotangent,
):
    n_tensor = lax.axis_size("tensor")
    tensor_index = lax.axis_index("tensor")
    dp_index = lax.axis_index("dp")
    tok_rows = tokens.shape[0]
    row_count = tok_rows * n_tensor
    own_width = conv_weight.shape[1]
    kernel_taps = conv_weight.shape[0]
    edge_rows = kernel_taps - 1
    dp_width = norm_gain.shape[0]
    own_start = tensor_index * tok_rows
    shards = (
        norm_gain,
        mlp_gain,
        x_weight,
        y_weight,
        recur_gate_weight,
        input_gate_weight,
        gate_weight,
        up_weight,
        out_weight,
        down_weight,
    )
    (
        gain_one,
        gain_two,
        x_full,
        y_full,
        recur_full,
        input_full,
        gate_full,
        up_full,
        out_full,
        down_full,
    ) = collect(*shards)
    block_size = recur_full.shape[0]
    first_gain = gain_one.astype(jnp.float32)
    second_gain = gain_two.astype(jnp.float32)
    both_gates = jnp.concatenate([recur_full, input_full], axis=1)
    tok_own = tokens.astype(jnp.float32)
    own_order = token_order - dp_index * row_count
    first_rows = rms_scale(tok_own, first_gain).astype(jnp.bfloat16)
    first_all, cot_all, order_all = (
        lax.all_gather(first_rows, "tensor", axis=0, tiled=True),
        lax.all_gather(cotangent, "tensor", axis=0, tiled=True),
        lax.all_gather(own_order, "tensor", axis=0, tiled=True),
    )
    row_index = jnp.arange(row_count, dtype=jnp.int32)
    inverse = jnp.zeros((row_count,), jnp.int32).at[order_all].set(row_index)
    hidden_place = jnp.take(first_all, inverse, axis=0)
    places = dp_index * row_count + row_index
    ends = jnp.cumsum(seq_lengths)
    segment = segment_of(places, ends)
    starts = (places == 0) | (segment != segment_of(places - 1, ends))
    live = (places < ends[-1]).astype(jnp.float32)
    live_stored = jnp.take(live, order_all, axis=0)
    same = [
        (segment_of(places - shift, ends) == segment).astype(jnp.float32)
        for shift in range(kernel_taps)
    ]
    low_edge = tensor_index * own_width
    own_blocks = (low_edge + jnp.arange(own_width, dtype=jnp.int32)) // block_size
    first_block = low_edge // block_size
    block_count = own_width // block_size + 2

    def block_start(index):
        return (first_block + index) * block_size - low_edge + block_size

    def block_mask(index):
        inside = own_blocks == first_block + index
        return jnp.concatenate([inside, inside])

    def convolve(extended, kernel):
        return sum(
            (
                kernel[shift][None, :]
                * extended[edge_rows - shift : edge_rows - shift + row_count]
                * same[shift][:, None]
                for shift in range(kernel_taps)
            )
        )

    def gates(conv_vals, pre_recur, pre_input, decay_vals):
        log_rate = -rate_scale * jax.nn.sigmoid(pre_recur) * jax.nn.softplus(-decay_vals)
        decay_rate = jnp.where(starts[:, None], 0.0, jnp.exp(log_rate))
        scale_in = jnp.where(starts[:, None], 1.0, jnp.sqrt(-jnp.expm1(2.0 * log_rate)))
        return (decay_rate, conv_vals * jax.nn.sigmoid(pre_input) * scale_in)

    def glu(gate_pre, up_pre):
        return gelu_tanh(gate_pre) * up_pre

    x_branch = plain_dot(hidden_place, x_full).astype(jnp.bfloat16)
    y_before = plain_dot(hidden_place, y_full)
    previous = from_behind(x_branch[row_count - edge_rows :], "dp", 1)
    extended = jnp.concatenate([previous, x_branch], axis=0).astype(jnp.float32)
    conv_out = convolve(extended, conv_weight)
    conv_wide = extended_2(conv_out.astype(jnp.bfloat16), (("tensor", 1),), block_size)
    pre_both = jnp.zeros((row_count, 2 * own_width), jnp.float32)
    for index in range(block_count):
        piece = lax.dynamic_slice_in_dim(conv_wide, block_start(index), block_size, 1)
        pre_both = pre_both + jnp.where(
            block_mask(index)[None, :], plain_dot(piece, both_gates), 0.0
        )
    (decay_rate, driven), gate_pull = jax.vjp(
        gates, conv_out, pre_both[:, :own_width], pre_both[:, own_width:], decay_param
    )
    cum_rate, local_state = lax.associative_scan(pair_step, (decay_rate, driven), axis=0)
    ident = (jnp.ones((own_width,), jnp.float32), jnp.zeros((own_width,), jnp.float32))
    rate_in, state_in = entering((cum_rate[-1], local_state[-1]), "dp", pair_step, ident, False)
    state = local_state + cum_rate * state_in[None, :]
    y_branch = gelu_tanh(y_before)
    merged = (state * y_branch).astype(jnp.bfloat16)
    merged_stored = jnp.take(merged, order_all, axis=0)

    def mixer_rows(begin, number):
        return plain_dot(merged_stored, out_full)

    after_own = tok_own + row_sums(mixer_rows, tok_rows)
    hidden_two = spread_rows(rms_scale(after_own, second_gain).astype(jnp.bfloat16))
    gate_pre = plain_dot(hidden_two, gate_full)
    up_pre = plain_dot(hidden_two, up_full)
    glu_out, glu_pull = jax.vjp(glu, gate_pre, up_pre)
    product = glu_out.astype(jnp.bfloat16)

    def down_rows(begin, number):
        return plain_dot(product, down_full)

    feed_out = row_sums(down_rows, tok_rows)
    live_own = lax.dynamic_slice_in_dim(live_stored, own_start, tok_rows, 0)
    output = ((after_own + feed_out) * live_own[:, None]).astype(jnp.bfloat16)
    grad_out = cot_all.astype(jnp.float32) * live_stored[:, None]
    fresh = lax.optimization_barrier((shards, grad_out))[0]
    (
        gain_one,
        gain_two,
        x_full,
        y_full,
        recur_full,
        input_full,
        gate_full,
        up_full,
        out_full,
        down_full,
    ) = collect(*fresh)
    first_gain = gain_one.astype(jnp.float32)
    second_gain = gain_two.astype(jnp.float32)
    both_gates = jnp.concatenate([recur_full, input_full], axis=1)
    down_in = grad_out.astype(jnp.bfloat16)
    grad_down = trans_times(product, down_in)
    grad_product = times_trans(down_in, down_full)
    grad_gate_pre, grad_up_pre = glu_pull(grad_product)
    grad_gate_pre = grad_gate_pre.astype(jnp.bfloat16)
    grad_up_pre = grad_up_pre.astype(jnp.bfloat16)
    grad_gate = trans_times(hidden_two, grad_gate_pre)
    grad_up = trans_times(hidden_two, grad_up_pre)

    def feed_rows(begin, number):
        return times_trans(grad_gate_pre, gate_full) + times_trans(grad_up_pre, up_full)

    grad_out_own = lax.dynamic_slice_in_dim(grad_out, own_start, tok_rows, 0)
    grad_two_own = row_sums(feed_rows, tok_rows)
    grad_norm_own, normed_two = norm_back(after_own, second_gain, grad_two_own)
    second_part = jnp.sum(grad_two_own * normed_two, axis=0)
    grad_after_own = grad_out_own + grad_norm_own
    mixer_in = spread_rows(grad_after_own.astype(jnp.bfloat16))
    grad_out_mat = trans_times(merged_stored, mixer_in)
    grad_merged = jnp.take(times_trans(mixer_in, out_full), inverse, axis=0)
    grad_state = grad_merged * y_branch
    gelu_pull = jax.vjp(gelu_tanh, y_before)[1]
    grad_y_before = gelu_pull(grad_merged * state)[0].astype(jnp.bfloat16)
    rate_next = jnp.concatenate([decay_rate[1:], jnp.ones((1, own_width), jnp.float32)], axis=0)
    rev_rate, local_lam = lax.associative_scan(
        pair_step, (rate_next, grad_state), reverse=True, axis=0
    )
    head_rate = decay_rate[0] * rev_rate[0]
    head_lam = decay_rate[0] * local_lam[0]
    factor_in, lam_in = entering((head_rate, head_lam), "dp", pair_step, ident, True)
    lam = local_lam + rev_rate * lam_in[None, :]
    state_prev = jnp.concatenate([state_in[None, :], state[:-1]], axis=0)
    grad_conv_local, grad_pre_recur, grad_pre_input, grad_decay_own = gate_pull(
        (lam * state_prev, lam)
    )
    grad_pre = jnp.concatenate([grad_pre_recur, grad_pre_input], axis=1).astype(jnp.bfloat16)
    grad_both = jnp.zeros((block_size, 2 * own_width), jnp.float32)
    grad_wide = jnp.zeros((row_count, own_width + 2 * block_size), jnp.float32)
    for index in range(block_count):
        begin = block_start(index)
        piece = lax.dynamic_slice_in_dim(conv_wide, begin, block_size, 1)
        masked = jnp.where(block_mask(index)[None, :], grad_pre, jnp.zeros((), jnp.bfloat16))
        grad_both = grad_both + trans_times(piece, masked)
        added = lax.dynamic_slice_in_dim(grad_wide, begin, block_size, 1) + times_trans(
            masked, both_gates
        )
        grad_wide = lax.dynamic_update_slice_in_dim(grad_wide, added, begin, 1)
    grad_recur = grad_both[:, :own_width]
    grad_input = grad_both[:, own_width:]
    rims = jnp.concatenate(
        [grad_wide[:, :block_size], grad_wide[:, own_width + block_size :]], axis=1
    )
    arrived = extended_2(rims.astype(jnp.bfloat16), (("tensor", 1),), block_size).astype(rims.dtype)
    from_lower = jnp.pad(arrived[:, :block_size], ((0, 0), (0, own_width - block_size)))
    from_upper = jnp.pad(arrived[:, 3 * block_size :], ((0, 0), (own_width - block_size, 0)))
    grad_conv = (
        grad_conv_local
        + grad_wide[:, block_size : block_size + own_width]
        + from_lower
        + from_upper
    )
    conv_pull = jax.vjp(convolve, extended, conv_weight)[1]
    grad_extended, grad_kernel = conv_pull(grad_conv)
    returned = from_behind(grad_extended[:edge_rows], "dp", -1)
    grad_x_branch = grad_extended[edge_rows:] + jnp.concatenate(
        [jnp.zeros((row_count - edge_rows, own_width), jnp.float32), returned], axis=0
    )
    grad_x_low = grad_x_branch.astype(jnp.bfloat16)
    grad_x_stored = jnp.take(grad_x_low, order_all, axis=0)
    grad_y_stored = jnp.take(grad_y_before, order_all, axis=0)
    grad_x_mat = trans_times(first_all, grad_x_stored)
    grad_y_mat = trans_times(first_all, grad_y_stored)

    def mixer_back_rows(begin, number):
        return times_trans(grad_x_stored, x_full) + times_trans(grad_y_stored, y_full)

    grad_one_own = row_sums(mixer_back_rows, tok_rows)
    grad_norm_one, normed_one = norm_back(tok_own, first_gain, grad_one_own)
    first_part = jnp.sum(grad_one_own * normed_one, axis=0)
    grad_tokens = grad_after_own + grad_norm_one
    chosen = jnp.arange(n_tensor, dtype=jnp.int32) == tensor_index
    kernel_tile = jnp.where(chosen[:, None, None], grad_kernel[None, :, :], 0.0)
    decay_tile = jnp.where(chosen[:, None], grad_decay_own[None, :], 0.0)
    small = lax.psum((first_part, second_part, kernel_tile, decay_tile), ("dp", "tensor"))
    grad_first_gain = lax.dynamic_slice_in_dim(small[0], dp_index * dp_width, dp_width, 0)
    grad_second_gain = lax.dynamic_slice_in_dim(small[1], dp_index * dp_width, dp_width, 0)
    grad_kernel_sum = lax.dynamic_index_in_dim(small[2], tensor_index, 0, keepdims=False)
    grad_decay = lax.dynamic_index_in_dim(small[3], tensor_index, 0, keepdims=False)
    sums = (
        lax.psum_scatter(
            grad_x_mat.astype(jnp.bfloat16), "dp", scatter_dimension=0, tiled=True
        ).astype(jnp.float32),
        lax.psum_scatter(
            grad_y_mat.astype(jnp.bfloat16), "dp", scatter_dimension=0, tiled=True
        ).astype(jnp.float32),
        lax.psum_scatter(
            grad_recur.astype(jnp.bfloat16), "dp", scatter_dimension=0, tiled=True
        ).astype(jnp.float32),
        lax.psum_scatter(
            grad_input.astype(jnp.bfloat16), "dp", scatter_dimension=0, tiled=True
        ).astype(jnp.float32),
        lax.psum_scatter(
            grad_gate.astype(jnp.bfloat16), "dp", scatter_dimension=0, tiled=True
        ).astype(jnp.float32),
        lax.psum_scatter(
            grad_up.astype(jnp.bfloat16), "dp", scatter_dimension=0, tiled=True
        ).astype(jnp.float32),
        lax.psum_scatter(
            grad_out_mat.astype(jnp.bfloat16), "dp", scatter_dimension=1, tiled=True
        ).astype(jnp.float32),
        lax.psum_scatter(
            grad_down.astype(jnp.bfloat16), "dp", scatter_dimension=1, tiled=True
        ).astype(jnp.float32),
    )
    return (
        output,
        grad_tokens,
        grad_first_gain,
        sums[0],
        sums[1],
        grad_kernel_sum,
        sums[2],
        sums[3],
        grad_decay,
        sums[6],
        grad_second_gain,
        sums[4],
        sums[5],
        sums[7],
    )


MESH = pl.DeviceIdType.MESH
VMEM_BYTES = 60 * 2**20


def remote(src, dst, send, recv, device):
    return pltpu.make_async_remote_copy(
        src_ref=src,
        dst_ref=dst,
        send_sem=send,
        recv_sem=recv,
        device_id=device,
        device_id_type=MESH,
    )


class Place:
    def __init__(self, n_dp, n_line):
        self.n_dp, self.n_line = n_dp, n_line
        self.d, self.t = lax.axis_index("dp"), lax.axis_index("tensor")
        self.core = lax.rem(self.d, 2)
        self.x = lax.rem(lax.div(self.d, 2), 2)
        self.y = lax.div(self.d, 4)

    def chip(self, flip_x, flip_y, flip_core=0):
        x = 1 - self.x if flip_x else self.x
        y = 1 - self.y if flip_y else self.y
        core = 1 - self.core if flip_core else self.core
        return y * 4 + x * 2 + core

    def at(self, flip_x=0, flip_y=0, flip_core=0):
        return (self.chip(flip_x, flip_y, flip_core), self.t)

    def up(self):
        return (self.d, lax.rem(self.t + 1, self.n_line))

    def down(self):
        return (self.d, lax.rem(self.t + self.n_line - 1, self.n_line))

    def meet(self, everyone=False):
        barrier = pltpu.get_barrier_semaphore()

        def greet(device):
            pl.semaphore_signal(barrier, inc=1, device_id=device, device_id_type=MESH)

        if everyone:
            for i in range(1, self.n_dp):
                greet((lax.rem(self.d + i, self.n_dp), self.t))
            for i in range(1, self.n_line):
                greet((self.d, lax.rem(self.t + i, self.n_line)))
            pl.semaphore_wait(barrier, self.n_dp + self.n_line - 2)
            return
        for flips in ((1, 0), (0, 1), (0, 0, 1)):
            greet(self.at(*flips))
        below, above = self.t > 0, self.t < self.n_line - 1

        @pl.when(below)
        def _():
            greet(self.down())

        @pl.when(above)
        def _():
            greet(self.up())

        pl.semaphore_wait(barrier, 3 + below.astype(jnp.int32) + above.astype(jnp.int32))


class GatherPlane:
    def __init__(self, place, src, dst, send, recv, local):
        self.p, self.src, self.dst = place, src, dst
        self.rows = src.shape[0]
        self.send, self.recv, self.local = send, recv, local

    def block(self, fx, fy, fc=0, part=None):
        first = self.p.chip(fx, fy, fc) * self.rows
        size = self.rows
        if part is not None:
            size = self.rows // 2
            first = first + part * size
        return self.dst.at[pl.ds(pl.multiple_of(first, 16), size)]

    def copy(self, i, src, dst, device):
        return remote(src, dst, self.send.at[i], self.recv.at[i], device)

    def mine(self):
        return pltpu.make_async_copy(self.src, self.block(0, 0), self.local)

    def outgoing(self, i):
        at, block = self.p.at, self.block
        if i == 0:
            return self.copy(0, self.src, block(0, 0), at(1, 0))
        if i == 1:
            return self.copy(1, self.src, block(0, 0), at(0, 1))
        if i == 2:
            return self.copy(2, self.src, block(0, 0), at(0, 0, 1))
        if i == 3:
            return self.copy(3, block(1, 0, 0, 0), block(1, 0, 0, 0), at(0, 1))
        if i == 4:
            return self.copy(4, block(0, 1, 0, 1), block(0, 1, 0, 1), at(1, 0))
        spot = ((1, 0), (0, 1), (1, 1, 0, 0), (1, 1, 0, 1))[i - 5]
        return self.copy(i, block(*spot), block(*spot), at(0, 0, 1))

    def arrive(self, i):
        spot = (
            (1, 0),
            (0, 1),
            (0, 0, 1),
            (1, 1, 0, 0),
            (1, 1, 0, 1),
            (1, 0, 1),
            (0, 1, 1),
            (1, 1, 1, 0),
            (1, 1, 1, 1),
        )[i]
        here = self.block(*spot)
        self.copy(i, here, here, self.p.at(0, 0, 1)).wait_recv()

    def begin(self):
        self.mine().start()
        for i in (0, 1, 2):
            self.outgoing(i).start()

    def forward(self):
        self.arrive(0)
        self.outgoing(3).start()
        self.arrive(1)
        self.outgoing(4).start()
        self.outgoing(5).start()
        self.outgoing(6).start()

    def share(self):
        self.arrive(3)
        self.outgoing(7).start()
        self.arrive(4)
        self.outgoing(8).start()

    def finish(self):
        for i in (2, 5, 6, 7, 8):
            self.arrive(i)
        for i in range(9):
            self.outgoing(i).wait_send()
        self.mine().wait()


class GatherLine:
    def __init__(self, place, dst, rows, begin, span, send, recv):
        self.p, self.dst, self.rows = place, dst, rows
        self.begin, self.span = begin, span
        self.send, self.recv = send, recv
        self.last = place.n_line - 1

    def block(self, owner):
        first = owner * self.rows + self.begin
        return self.dst.at[pl.ds(pl.multiple_of(first, 8), self.span)]

    def copy(self, way, k, owner, source=None):
        to = self.p.up() if way == 0 else self.p.down()
        block = self.block(owner)
        return remote(
            block if source is None else source,
            block,
            self.send.at[way, k],
            self.recv.at[way, k],
            to,
        )

    def step(self, k, source=None):
        t, last = self.p.t, self.last
        if k > 0:
            self.arrive(k - 1)

        @pl.when((t < last) & (t >= k))
        def _():
            self.copy(0, k, t - k, source).start()

        @pl.when((t > 0) & (t + k <= last))
        def _():
            self.copy(1, k, t + k, source).start()

    def arrive(self, k):
        t, last = self.p.t, self.last

        @pl.when(t >= k + 1)
        def _():
            self.copy(0, k, t - 1 - k).wait_recv()

        @pl.when(t + k + 1 <= last)
        def _():
            self.copy(1, k, t + 1 + k).wait_recv()

    def finish(self):
        t, last = self.p.t, self.last
        self.arrive(last - 1)
        for k in range(last):

            @pl.when((t < last) & (t >= k))
            def _():
                self.copy(0, k, t - k).wait_send()

            @pl.when((t > 0) & (t + k <= last))
            def _():
                self.copy(1, k, t + k).wait_send()


class ReduceLine:
    def __init__(self, place, terms, rows, begin, span, stage, inbox, send, recv):
        self.p, self.terms, self.rows = place, terms, rows
        self.begin, self.span = begin, span
        self.stage, self.inbox = stage, inbox
        self.send, self.recv = send, recv
        self.last = place.n_line - 1

    def own(self, owner):
        first = owner * self.rows + self.begin
        return self.terms.at[pl.ds(pl.multiple_of(first, 16), self.span)]

    def copy(self, way, j, source):
        to = self.p.up() if way == 0 else self.p.down()
        return remote(
            source, self.inbox.at[way, j], self.send.at[way, j], self.recv.at[way, j], to
        )

    def ends(self):
        t, last = self.p.t, self.last

        @pl.when(t == 0)
        def _():
            for j in range(last):
                self.copy(0, j, self.own(last - j)).start()

        @pl.when(t == last)
        def _():
            for j in range(last):
                self.copy(1, j, self.own(j)).start()

    def sent(self):
        t, last = self.p.t, self.last

        @pl.when(t == 0)
        def _():
            for j in range(last):
                self.copy(0, j, self.own(last - j)).wait_send()

        @pl.when(t == last)
        def _():
            for j in range(last):
                self.copy(1, j, self.own(j)).wait_send()

    def hand_on(self, way, j):
        term = self.own(self.last - j if way == 0 else j)
        self.copy(way, j, term).wait_recv()
        self.stage[way, j] = (
            term[...].astype(jnp.float32) + self.inbox[way, j].astype(jnp.float32)
        ).astype(jnp.bfloat16)
        self.copy(way, j, self.stage.at[way, j]).start()

    def hop(self, k):
        t, last = self.p.t, self.last

        @pl.when(t == k + 1)
        def _():
            for j in range(last - 1 - k):
                self.hand_on(0, j)

        @pl.when(t == last - 1 - k)
        def _():
            for j in range(last - 1 - k):
                self.hand_on(1, j)

    def total(self, result):
        t, last = self.p.t, self.last
        result[...] = self.own(t)[...].astype(jnp.float32)

        @pl.when(t > 0)
        def _():
            j = last - t
            self.copy(0, j, self.stage.at[0, 0]).wait_recv()
            result[...] += self.inbox[0, j].astype(jnp.float32)

        @pl.when(t < last)
        def _():
            self.copy(1, t, self.stage.at[0, 0]).wait_recv()
            result[...] += self.inbox[1, t].astype(jnp.float32)

    def finish(self):
        t, last = self.p.t, self.last
        for j in range(last - 1):

            @pl.when((t > 0) & (t < last - j))
            def _():
                self.copy(0, j, self.stage.at[0, j]).wait_send()

            @pl.when((t < last) & (t > j))
            def _():
                self.copy(1, j, self.stage.at[1, j]).wait_send()


def add_rows(into, other, result=None):
    result = into if result is None else result

    def tile(i, carry):
        rows = pl.ds(pl.multiple_of(i * 16, 16), 16)
        result[rows] = (
            into[rows].astype(jnp.float32) + other[rows].astype(jnp.float32)
        ).astype(result.dtype)
        return carry

    lax.fori_loop(0, into.shape[0] // 16, tile, None)


class ReducePlane:
    chips = ((0, 0), (1, 0), (0, 1), (1, 1))

    def __init__(self, place, terms, scratch):
        self.p, self.terms = place, terms
        self.held, self.near, self.along, self.last, self.send, self.recv, self.local = scratch
        self.rows = self.held.shape[1]
        self.half = self.rows // 2

    @staticmethod
    def scratch(rows, width):
        return [
            pltpu.VMEM((4, rows, width), jnp.bfloat16),
            pltpu.VMEM((4, rows, width), jnp.bfloat16),
            pltpu.VMEM((4, rows // 2, width), jnp.bfloat16),
            pltpu.VMEM((2, rows // 2, width), jnp.bfloat16),
            pltpu.SemaphoreType.DMA((10,)),
            pltpu.SemaphoreType.DMA((10,)),
            pltpu.SemaphoreType.DMA((4,)),
        ]

    def block(self, k, other):
        first = self.p.chip(*self.chips[k], other) * self.rows
        return self.terms.at[pl.ds(pl.multiple_of(first, 16), self.rows)]

    def half_of(self, k, part):
        return self.held.at[k, pl.ds(part * self.half, self.half)]

    def load(self, k):
        return pltpu.make_async_copy(self.block(k, 0), self.held.at[k], self.local.at[k])

    def copy(self, i):
        at = self.p.at
        if i < 4:
            src, dst, to = self.block(i, 1), self.near.at[i], at(0, 0, 1)
        elif i < 8:
            src, to = (
                (self.half_of(1, 0), at(1, 0)),
                (self.half_of(3, 0), at(1, 0)),
                (self.half_of(2, 1), at(0, 1)),
                (self.half_of(3, 1), at(0, 1)),
            )[i - 4]
            dst = self.along.at[i - 4]
        else:
            src, to = ((self.half_of(2, 0), at(0, 1)), (self.half_of(1, 1), at(1, 0)))[i - 8]
            dst = self.last.at[i - 8]
        return remote(src, dst, self.send.at[i], self.recv.at[i], to)

    def begin(self):
        for k in (3, 1, 2, 0):
            self.copy(k).start()
            self.load(k).start()

    def cores(self):
        for k in (3, 1, 2, 0):
            self.load(k).wait()
            self.copy(k).wait_recv()
            add_rows(self.held.at[k], self.near.at[k])
            if k == 3:
                self.copy(5).start()
                self.copy(7).start()
            elif k == 1:
                self.copy(4).start()
            elif k == 2:
                self.copy(6).start()

    def turn(self):
        self.copy(5).wait_recv()
        add_rows(self.half_of(2, 0), self.along.at[1])
        self.copy(8).start()
        self.copy(7).wait_recv()
        add_rows(self.half_of(1, 1), self.along.at[3])
        self.copy(9).start()
        self.copy(4).wait_recv()
        add_rows(self.half_of(0, 0), self.along.at[0])
        self.copy(6).wait_recv()
        add_rows(self.half_of(0, 1), self.along.at[2])

    def finish(self, result):
        for part in (0, 1):
            self.copy(8 + part).wait_recv()
            rows = pl.ds(part * self.half, self.half)
            add_rows(self.half_of(0, part), self.last.at[part], result.at[rows])
        for i in range(10):
            self.copy(i).wait_send()


def dma_sems(*dims):
    return pltpu.SemaphoreType.DMA(dims)


def in_vmem():
    return pl.BlockSpec(memory_space=pltpu.VMEM)


def in_any():
    return pl.BlockSpec(memory_space=pl.ANY)


def comm_params(number):
    return pltpu.CompilerParams(
        collective_id=number, has_side_effects=True, vmem_limit_bytes=VMEM_BYTES
    )


def shaped(dims, kind):
    return jax.ShapeDtypeStruct(dims, kind)


def first_gather(n_dp, n_line, mats, minor, rows_in, order):
    def kernel(a, b, c, e, a_out, b_out, c_out, e_out, ps, pr, pl_sem, ls, lr, ll):
        place = Place(n_dp, n_line)
        place.meet()
        planes = [
            GatherPlane(place, a, a_out, ps.at[0], pr.at[0], pl_sem.at[0]),
            GatherPlane(place, b, b_out, ps.at[1], pr.at[1], pl_sem.at[1]),
        ]
        lines, copies = [], []
        for i, (src, dst) in enumerate(((c, c_out), (e, e_out))):
            rows = src.shape[0]
            lines.append(GatherLine(place, dst, rows, 0, rows, ls.at[i], lr.at[i]))
            own = dst.at[pl.ds(pl.multiple_of(place.t * rows, 8), rows)]
            copies.append(pltpu.make_async_copy(src, own, ll.at[i]))
        for copy in copies:
            copy.start()
        lines[0].step(0, c)
        lines[1].step(0, e)
        planes[0].begin()
        planes[1].begin()
        lines[0].step(1)
        lines[1].step(1)
        planes[0].forward()
        planes[1].forward()
        lines[0].step(2)
        lines[1].step(2)
        planes[0].share()
        planes[1].share()
        for part in lines + planes:
            part.finish()
        for copy in copies:
            copy.wait()

    return pl.pallas_call(
        kernel,
        out_shape=(
            shaped((n_dp * mats.shape[0], mats.shape[1]), mats.dtype),
            shaped((n_dp * minor.shape[0], minor.shape[1]), minor.dtype),
            shaped((n_line * rows_in.shape[0], rows_in.shape[1]), rows_in.dtype),
            shaped((n_line * order.shape[0], order.shape[1]), order.dtype),
        ),
        in_specs=[in_any()] * 4,
        out_specs=[in_any()] * 4,
        scratch_shapes=[
            dma_sems(2, 9),
            dma_sems(2, 9),
            dma_sems(2),
            dma_sems(2, 2, n_line - 1),
            dma_sems(2, 2, n_line - 1),
            dma_sems(2),
        ],
        compiler_params=comm_params(1),
        name="first_gather",
    )(mats, minor, rows_in, order)


CHUNKS = 8


def line_scratch(n_line, span, width):
    hops = n_line - 1
    return [
        pltpu.VMEM((CHUNKS, 2, hops, span, width), jnp.bfloat16),
        pltpu.VMEM((CHUNKS, 2, hops, span, width), jnp.bfloat16),
        dma_sems(CHUNKS, 2, hops),
        dma_sems(CHUNKS, 2, hops),
        dma_sems(CHUNKS, 2, hops),
        dma_sems(CHUNKS, 2, hops),
        pltpu.VMEM((span, width), jnp.float32),
    ]


def sum_rows_and_spread(place, terms, scratch, finish_rows, spread, between):
    stage, inbox, rs, rr, gs, gr, total = scratch
    span = total.shape[0]
    count = stage.shape[0]
    rows = span * count
    hops = place.n_line - 1
    sums = [
        ReduceLine(place, terms, rows, c * span, span, stage.at[c], inbox.at[c], rs.at[c], rr.at[c])
        for c in range(count)
    ]
    gathers = []
    if spread is not None:
        gathers = [
            GatherLine(place, spread, rows, c * span, span, gs.at[c], gr.at[c])
            for c in range(count)
        ]
    sums[0].ends()

    def total_of(c):
        sums[c].total(total)
        finish_rows(c, pl.ds(c * span, span), total)
        if gathers:
            gathers[c].step(0)

    stages = [lambda c, k=k: sums[c].hop(k) for k in range(hops - 1)] + [total_of]
    lags = [LAGS[min(k, len(LAGS) - 1)] for k in range(hops)]
    if gathers:
        stages += [lambda c, k=k: gathers[c].step(k) for k in range(1, hops)]
        lags += [lags[-1] + LAG_STEP * k for k in range(1, hops)]
    for i in range(count + lags[-1]):
        if i < count:
            sums[i].sent()
        if i + 1 < count:
            sums[i + 1].ends()
        for work, lag in zip(stages, lags):
            if 0 <= i - lag < count:
                work(i - lag)
        if i in between:
            between[i]()
    for part in gathers + sums:
        part.finish()


LAGS = (0, 1, 1)
LAG_STEP = 1


def middle_gather(n_dp, n_line, terms, tokens, gain, mats):
    rows, width = tokens.shape
    count = len(mats)

    def kernel(*refs):
        s, tok, gain_ref = refs[:3]
        srcs = refs[3 : 3 + count]
        after, hidden = refs[3 + count : 5 + count]
        dsts = refs[5 + count : 5 + 2 * count]
        ps, pr, pl_sem = refs[5 + 2 * count : 8 + 2 * count]
        scratch = refs[8 + 2 * count :]
        place = Place(n_dp, n_line)
        place.meet()
        planes = [
            GatherPlane(place, a, b, ps.at[i], pr.at[i], pl_sem.at[i])
            for i, (a, b) in enumerate(zip(srcs, dsts))
        ]
        planes[0].begin()

        def norm(c, here, total):
            values = tok[here].astype(jnp.float32) + total[...]
            after[here] = values
            low = rms_scale(values, gain_ref[...]).astype(jnp.bfloat16)
            first = pl.multiple_of(place.t * rows, 16) + c * total.shape[0]
            hidden[pl.ds(pl.multiple_of(first, 16), total.shape[0])] = low

        between = {4: planes[1].begin, 5: planes[0].forward}
        sum_rows_and_spread(place, s, scratch, norm, hidden, between)
        planes[1].forward()
        planes[0].share()
        planes[1].share()
        for part in planes:
            part.finish()

    return pl.pallas_call(
        kernel,
        out_shape=(
            shaped((rows, width), jnp.float32),
            shaped((n_line * rows, width), jnp.bfloat16),
        )
        + tuple(shaped((n_dp * m.shape[0], m.shape[1]), m.dtype) for m in mats),
        in_specs=[in_vmem()] * 3 + [in_any()] * count,
        out_specs=[in_vmem()] * 2 + [in_any()] * count,
        scratch_shapes=[dma_sems(count, 9), dma_sems(count, 9), dma_sems(count)]
        + line_scratch(n_line, rows // CHUNKS, width),
        compiler_params=comm_params(2),
        name="middle_gather",
    )(terms, tokens, gain, *mats)


def middle_sums(n_dp, n_line, terms, after, gain, grad_in, mats):
    rows, width = after.shape
    count = len(mats)
    block = mats[0].shape[0] // n_dp
    per = len(ReducePlane.scratch(16, 128))

    def kernel(*refs):
        s, after_ref, gain_ref, g_ref = refs[:4]
        srcs = refs[4 : 4 + count]
        grad_after, gain_sum, spread = refs[4 + count : 7 + count]
        results = refs[7 + count : 7 + 2 * count]
        rest = refs[7 + 2 * count :]
        scratch = rest[count * per :]
        place = Place(n_dp, n_line)
        place.meet()
        planes = [
            ReducePlane(place, srcs[i], rest[i * per : (i + 1) * per]) for i in range(count)
        ]
        for part in planes:
            part.begin()
        gain_sum[...] = jnp.zeros_like(gain_sum)

        def norm(c, here, total):
            grad = total[...]
            grad_rows, normed = norm_back(after_ref[here], gain_ref[...], grad)
            gain_sum[...] += jnp.sum(grad * normed, axis=0, keepdims=True)
            both = g_ref[here].astype(jnp.float32) + grad_rows
            grad_after[here] = both
            first = pl.multiple_of(place.t * rows, 16) + c * total.shape[0]
            spread[pl.ds(pl.multiple_of(first, 16), total.shape[0])] = both.astype(jnp.bfloat16)

        between = {0: planes[0].cores, 3: planes[1].cores, 5: planes[0].turn}
        sum_rows_and_spread(place, s, scratch, norm, spread, between)
        planes[1].turn()
        for part, result in zip(planes, results):
            part.finish(result)

    return pl.pallas_call(
        kernel,
        out_shape=(
            shaped((rows, width), jnp.float32),
            shaped((1, width), jnp.float32),
            shaped((n_line * rows, width), jnp.bfloat16),
        )
        + tuple(shaped((block, m.shape[1]), jnp.bfloat16) for m in mats),
        in_specs=[in_vmem()] * 4 + [in_any()] * count,
        out_specs=[in_vmem()] * (3 + count),
        scratch_shapes=sum([ReducePlane.scratch(block, m.shape[1]) for m in mats], [])
        + line_scratch(n_line, rows // CHUNKS, width),
        compiler_params=comm_params(3),
        name="middle_sums",
    )(terms, after, gain, grad_in, *mats)


class Exchange:
    def __init__(self, place, axis, src, slots, send, recv, local):
        self.p, self.src, self.slots = place, src, slots
        self.over_dp = axis == "dp"
        self.size = place.n_dp if self.over_dp else place.n_line
        self.me = place.d if self.over_dp else place.t
        self.send, self.recv, self.local = send, recv, local

    def copy(self, i):
        to = lax.rem(self.me + i, self.size)
        device = (to, self.p.t) if self.over_dp else (self.p.d, to)
        return remote(
            self.src, self.slots.at[self.me], self.send.at[i - 1], self.recv.at[i - 1], device
        )

    def mine(self):
        return pltpu.make_async_copy(self.src, self.slots.at[self.me], self.local)

    def begin(self):
        for i in range(1, self.size):
            self.copy(i).start()
        self.mine().start()

    def wait(self):
        self.mine().wait()
        for i in range(1, self.size):
            self.copy(i).wait()

    def finish(self):
        self.wait()
        total = self.slots[0]
        for i in range(1, self.size):
            total = total + self.slots[i]
        return total


def last_sums(n_dp, n_line, terms, tokens, gain, grad_after, small, mats):
    rows, width = tokens.shape
    count = len(mats)
    per = len(ReducePlane.scratch(16, 128))

    def kernel(*refs):
        s, tok, gain_ref, g_ref, small_ref = refs[:5]
        srcs = refs[5 : 5 + count]
        grad_tok, small_out, first_out = refs[5 + count : 8 + count]
        results = refs[8 + count : 8 + 2 * count]
        rest = refs[8 + 2 * count :]
        own_first, row_sum = rest[count * per : count * per + 2]
        slots_a, slots_b, slots_c, slots_d = rest[count * per + 2 : count * per + 6]
        xs, xr, xl = rest[count * per + 6 : count * per + 9]
        scratch = rest[count * per + 9 :]
        place = Place(n_dp, n_line)
        place.meet(True)
        planes = [
            ReducePlane(place, srcs[i], rest[i * per : (i + 1) * per]) for i in range(count)
        ]
        for part in planes:
            part.begin()
        early = Exchange(place, "dp", small_ref, slots_a, xs.at[0], xr.at[0], xl.at[0])
        early.begin()
        own_first[...] = jnp.zeros_like(own_first)

        def norm(c, here, total):
            grad = total[...]
            grad_rows, normed = norm_back(tok[here].astype(jnp.float32), gain_ref[...], grad)
            own_first[...] += jnp.sum(grad * normed, axis=0, keepdims=True)
            grad_tok[here] = g_ref[here] + grad_rows

        def cores():
            for part in planes:
                part.cores()

        def turn():
            for part in planes:
                part.turn()

        sum_rows_and_spread(place, s, scratch, norm, None, {0: cores, 5: turn})
        first = Exchange(place, "dp", own_first, slots_b, xs.at[1], xr.at[1], xl.at[1])
        first.begin()
        small_out[...] = early.finish()
        row_sum[0:1] = small_out[0:1]
        row_sum[1:2] = first.finish()
        both = Exchange(place, "tensor", row_sum, slots_c, xs.at[2], xr.at[2], xl.at[2])
        both.begin()
        for part, result in zip(planes, results):
            part.finish(result)
        first_out[...] = both.finish()

    return pl.pallas_call(
        kernel,
        out_shape=(
            shaped((rows, width), jnp.float32),
            shaped(small.shape, jnp.float32),
            shaped((2, width), jnp.float32),
        )
        + tuple(shaped((m.shape[0] // n_dp, m.shape[1]), jnp.bfloat16) for m in mats),
        in_specs=[in_vmem()] * 5 + [in_any()] * count,
        out_specs=[in_vmem()] * (3 + count),
        scratch_shapes=sum([ReducePlane.scratch(m.shape[0] // n_dp, m.shape[1]) for m in mats], [])
        + [
            pltpu.VMEM((1, width), jnp.float32),
            pltpu.VMEM((2, width), jnp.float32),
            pltpu.VMEM((n_dp,) + small.shape, jnp.float32),
            pltpu.VMEM((n_dp, 1, width), jnp.float32),
            pltpu.VMEM((n_line, 2, width), jnp.float32),
            pltpu.VMEM((1, width), jnp.float32),
            dma_sems(3, n_dp),
            dma_sems(3, n_dp),
            dma_sems(3),
        ]
        + line_scratch(n_line, rows // CHUNKS, width),
        compiler_params=comm_params(4),
        name="last_sums",
    )(terms, tokens, gain, grad_after, small, *mats)


def loop(count, body, unroll=1):
    def step(i, carry):
        body(i)
        return carry

    lax.fori_loop(0, count, step, None, unroll=unroll)


def tile_rows(i, size, ahead=0):
    return pl.ds(pl.multiple_of(i * size + ahead, 8), size)


def moved_up(values, distance, count):
    size = values.shape[0]
    return pltpu.roll(values, (size - distance) % size, 0)[:count]


def take_lanes(ref, here):
    return jnp.concatenate([ref[c, here] for c in range(ref.shape[0])], axis=1)


def put_lanes(ref, here, values):
    for c in range(ref.shape[0]):
        ref[c, here] = values[:, c * LANES : (c + 1) * LANES]


def gelu_parts(values):
    inner = GELU_C * (values + 0.044715 * (values * values * values))
    tanh = jnp.tanh(inner)
    half = 0.5 * (1.0 + tanh)
    slope = half + 0.5 * values * (1.0 - tanh * tanh) * GELU_C * (
        1.0 + 3.0 * 0.044715 * (values * values)
    )
    return values * half, slope


GELU_C = 0.7978845608028654
RIM = 128
LANES = 128
TILE = 16


def one_minus_exp(values, exponential):
    series = jnp.ones_like(values)
    for term in range(9, 1, -1):
        series = 1.0 + values * (1.0 / term) * series
    return jnp.where(values > -0.35, -values * series, 1.0 - exponential)


def rate_and_scale(pre_recur, soft, start):
    sr = jax.nn.sigmoid(pre_recur)
    log_rate = -rate_scale * sr * soft
    decay = jnp.exp(log_rate)
    rate = jnp.where(start, 0.0, decay)
    scale = jnp.where(start, 1.0, jnp.sqrt(one_minus_exp(2.0 * log_rate, decay * decay)))
    return sr, rate, scale


class RimSwap:
    def __init__(self, place, own):
        self.odd = lax.rem(place.t, 2)
        self.partner = (place.d, place.t + 1 - 2 * self.odd)
        self.first = pl.multiple_of(RIM - RIM * self.odd, RIM)
        self.edge = pl.ds(pl.multiple_of((1 - self.odd) * own + self.odd * RIM, RIM), RIM)
        self.over_there = pl.ds(pl.multiple_of(self.odd * (own + RIM), RIM), RIM)
        self.beyond = pl.ds(pl.multiple_of((1 - self.odd) * (own + RIM), RIM), RIM)

    def block(self, index, size):
        return pl.ds(pl.multiple_of(self.first + index * size, RIM), size)


def recur_forward(
    n_dp, n_line, tok_all, cot, to_place, to_stored, mats, out_full, gain, gates, taps, soft, flags
):
    rows, width = tok_all.shape
    count, own = taps.shape
    size = gates.shape[0]
    wide = own + 2 * RIM
    blocks = (wide - RIM) // size
    chunk = rows // 8
    cot_rows = cot.shape[0]
    parts = 2

    def kernel(*refs):
        (tok, cot_ref, plc, sto, w, wo, gain_ref, gw, cw, sp, fl) = refs[:11]
        (hp, xext, y, conv_low, conv, pre_r, pre_i, rate, state, merged_st, terms, cot_all) = refs[
            11:23
        ]
        (h, xf, local, cum, merged, agg, slots, hs, hr, es, er, el, gs, gr, gl) = refs[23:]
        place = Place(n_dp, n_line)
        place.meet(True)
        swap = RimSwap(place, own)
        own_cot = cot_all.at[pl.ds(pl.multiple_of(place.t * cot_rows, 16), cot_rows)]
        keep = pltpu.make_async_copy(cot_ref, own_cot, gl)
        keep.start()
        span = cot_rows // parts
        lines = [
            GatherLine(place, cot_all, cot_rows, c * span, span, gs.at[c], gr.at[c])
            for c in range(parts)
        ]
        for c, line in enumerate(lines):
            line.step(0, cot_ref.at[pl.ds(c * span, span)])

        def norm(i):
            here = tile_rows(i, TILE)
            h[here] = rms_scale(tok[here].astype(jnp.float32), gain_ref[...]).astype(jnp.bfloat16)

        loop(rows // TILE, norm)

        def project(i):
            here = tile_rows(i, 128)
            hp[here] = plain_dot(plc[here], h[...]).astype(jnp.bfloat16)
            xext[tile_rows(i, 128, 16)] = plain_dot(hp[here], w[:, :own]).astype(jnp.bfloat16)

        loop(rows // 128, project)
        edge = remote(
            xext.at[pl.ds(rows, 16)],
            xext.at[pl.ds(0, 16)],
            hs.at[0],
            hr.at[0],
            (lax.rem(place.d + 1, n_dp), place.t),
        )
        edge.start()

        def project_y(i):
            here = tile_rows(i, 128)
            y[here] = plain_dot(hp[here], w[:, own : 2 * own])

        loop(rows // 128, project_y)
        for line in lines:
            line.step(1)
        edge.wait()
        top = xext[pl.ds(0, 16)]
        xext[pl.ds(0, 16)] = jnp.where(place.d > 0, top, jnp.zeros_like(top))

        def widen(i):
            xf[tile_rows(i, TILE)] = xext[tile_rows(i, TILE)].astype(jnp.float32)

        loop(rows // TILE + 1, widen)

        def convolve(i):
            here = tile_rows(i, TILE)
            near = xf[pl.ds(pl.multiple_of(i * TILE + 8, 8), TILE + 8)]
            same = fl[tile_rows(i, TILE, 8)]
            total = cw[0:1] * near[8:]
            for k in range(1, count):
                total += cw[k : k + 1] * moved_up(near, 8 - k, TILE) * same[:, k : k + 1]
            conv[here] = total
            conv_low[here, RIM : RIM + own] = total.astype(jnp.bfloat16)

        loop(rows // TILE, convolve)
        rim = remote(
            conv_low.at[:, swap.edge],
            conv_low.at[:, swap.over_there],
            hs.at[1],
            hr.at[1],
            swap.partner,
        )
        rim.start()
        for i in range(blocks):
            index = lax.rem(i + swap.odd, blocks)
            cols = swap.block(index, size)
            other = pl.ds(pl.multiple_of(wide + swap.first + index * size, RIM), size)
            if i == blocks - 1:
                rim.wait()
            pre_r[:, cols] = plain_dot(conv_low[:, cols], gw[:, cols])
            pre_i[:, cols] = plain_dot(conv_low[:, cols], gw[:, other])

        def drive(i):
            here = tile_rows(i, TILE)
            start = fl[tile_rows(i, TILE, 8)][:, 0:1] > 0.0
            own_cols = pl.ds(RIM, own)
            _, decay, scale = rate_and_scale(pre_r[here, own_cols], sp[...], start)
            put_lanes(rate, here, decay)
            put_lanes(local, here, conv[here] * jax.nn.sigmoid(pre_i[here, own_cols]) * scale)

        loop(rows // TILE, drive)
        groups = own // LANES

        def scan(i, carry):
            here = pl.ds(i, 8, chunk)
            result = []
            for c in range(groups):
                product, total = carry[c]
                r = rate[c, here]
                product = product * r
                total = total * r + local[c, here]
                cum[c, here] = product
                local[c, here] = total
                result.append((product, total))
            return tuple(result)

        blank = (jnp.ones((8, LANES), jnp.float32), jnp.zeros((8, LANES), jnp.float32))
        lax.fori_loop(0, chunk, scan, (blank,) * groups)
        product, total = jnp.ones((1, own), jnp.float32), jnp.zeros((1, own), jnp.float32)
        for j in range(8):
            last = pl.ds(j * chunk + chunk - 1, 1)
            total = take_lanes(local, last) + take_lanes(cum, last) * total
            product = product * take_lanes(cum, last)
        agg[0:1] = product
        agg[1:2] = total
        swap_all = Exchange(place, "dp", agg, slots, es, er, el)
        swap_all.begin()
        swap_all.wait()
        entry = jnp.zeros((1, own), jnp.float32)
        for q in range(n_dp):
            longer = slots[q, 1:2] + slots[q, 0:1] * entry
            entry = jnp.where(q < place.d, longer, entry)
        state[pl.ds(0, 8)] = jnp.broadcast_to(entry, (8, own))
        for j in range(8):

            def settle(i, entry=entry):
                here = tile_rows(i, TILE, j * chunk)
                values = take_lanes(local, here) + take_lanes(cum, here) * entry
                state[tile_rows(i, TILE, j * chunk + 8)] = values
                merged[here] = (values * gelu_parts(y[here])[0]).astype(jnp.bfloat16)

            loop(chunk // TILE, settle)
            last = pl.ds(j * chunk + chunk - 1, 1)
            entry = take_lanes(local, last) + take_lanes(cum, last) * entry
        for line in lines:
            line.step(2)
        merged_st[...] = plain_dot(sto[...], merged[...]).astype(jnp.bfloat16)

        def mix(i):
            some = tile_rows(i, 512)
            terms[:, pl.ds(pl.multiple_of(i * 512, 512), 512)] = times_trans(
                merged_st[...], wo[some, :]
            ).astype(jnp.bfloat16)

        loop(width // 512, mix)
        for line in lines:
            line.finish()
        keep.wait()

    low, full = jnp.bfloat16, jnp.float32
    return pl.pallas_call(
        kernel,
        out_shape=(
            shaped((rows, width), low),
            shaped((rows + 16, own), low),
            shaped((rows, own), full),
            shaped((rows, wide), low),
            shaped((rows, own), full),
            shaped((rows, wide), full),
            shaped((rows, wide), full),
            shaped((own // LANES, rows, LANES), full),
            shaped((rows + 8, own), full),
            shaped((rows, own), low),
            shaped((rows, width), low),
            shaped((n_line * cot_rows, width), low),
        ),
        in_specs=[in_vmem(), in_any()] + [in_vmem()] * 9,
        out_specs=[in_vmem()] * 11 + [in_any()],
        scratch_shapes=[
            pltpu.VMEM((rows, width), low),
            pltpu.VMEM((rows + 16, own), full),
            pltpu.VMEM((own // LANES, rows, LANES), full),
            pltpu.VMEM((own // LANES, rows, LANES), full),
            pltpu.VMEM((rows, own), low),
            pltpu.VMEM((2, own), full),
            pltpu.VMEM((n_dp, 2, own), full),
            dma_sems(2),
            dma_sems(2),
            dma_sems(n_dp),
            dma_sems(n_dp),
            pltpu.SemaphoreType.DMA,
            dma_sems(parts, 2, n_line - 1),
            dma_sems(parts, 2, n_line - 1),
            pltpu.SemaphoreType.DMA,
        ],
        compiler_params=comm_params(5),
        name="recur_forward",
    )(tok_all, cot, to_place, to_stored, mats, out_full, gain, gates, taps, soft, flags)


def recur_backward(
    n_dp, n_line, mixer_in, to_place, out_full, gates, taps, soft, slope, flags, kept
):
    rows, width = mixer_in.shape
    count, own = taps.shape
    size = gates.shape[0]
    wide = own + 2 * RIM
    blocks = (wide - RIM) // size
    chunk = rows // 8

    def kernel(*refs):
        (mix, plc, wo, gw, cw, sp, sg, fl) = refs[:8]
        (xext, y, conv_low, conv, pre_r, pre_i, rate, state) = refs[8:16]
        (gxy, gate_grads, tap_grads, decay_grad) = refs[16:20]
        (mp, gm, lam, reach, gp_r, gp_i, grad, spread, rim_out, rim_in, ret_out, ret_in) = refs[
            20:32
        ]
        (tap_sums, decay_sums, ends, agg, slots, hs, hr, es, er, el) = refs[32:]
        place = Place(n_dp, n_line)
        place.meet(True)
        swap = RimSwap(place, own)
        own_cols = pl.ds(RIM, own)

        def project(i):
            here = tile_rows(i, 128)
            mp[here] = plain_dot(plc[here], mix[...]).astype(jnp.bfloat16)
            gm[here] = plain_dot(mp[here], wo[...])

        loop(rows // 128, project)

        def split(i):
            here = tile_rows(i, TILE)
            branch, slope_y = gelu_parts(y[here])
            grads = gm[here]
            put_lanes(lam, here, grads * branch)
            values = state[tile_rows(i, TILE, 8)]
            gxy[here, own:] = (grads * values * slope_y).astype(jnp.bfloat16)

        loop(rows // TILE, split)
        groups = own // LANES

        def scan(i, carry):
            here = pl.ds(chunk - 1 - i, 8, chunk)
            result = []
            for c in range(groups):
                product, message = carry[c]
                r = rate[c, here]
                value = lam[c, here] + message
                lam[c, here] = value
                reach[c, here] = product
                result.append((product * r, value * r))
            return tuple(result)

        blank = (jnp.ones((8, LANES), jnp.float32), jnp.zeros((8, LANES), jnp.float32))
        done = lax.fori_loop(0, chunk, scan, (blank,) * groups)
        for c in range(groups):
            lanes = pl.ds(c * LANES, LANES)
            ends[0, :, lanes] = done[c][0]
            ends[1, :, lanes] = done[c][1]
        product, message = jnp.ones((1, own), jnp.float32), jnp.zeros((1, own), jnp.float32)
        for j in reversed(range(8)):
            message = ends[1, j : j + 1] + ends[0, j : j + 1] * message
            product = product * ends[0, j : j + 1]
        agg[0:1] = product
        agg[1:2] = message
        swap_all = Exchange(place, "dp", agg, slots, es, er, el)
        swap_all.begin()
        swap_all.wait()
        entry = jnp.zeros((1, own), jnp.float32)
        for q in reversed(range(n_dp)):
            longer = slots[q, 1:2] + slots[q, 0:1] * entry
            entry = jnp.where(q > place.d, longer, entry)
        for ref in (tap_sums, decay_sums):
            ref[...] = jnp.zeros_like(ref)
        for ref in (gp_r, gp_i):
            ref[:, 0:RIM] = jnp.zeros((rows, RIM), jnp.bfloat16)
            ref[:, RIM + own :] = jnp.zeros((rows, RIM), jnp.bfloat16)
        grad[pl.ds(0, 8)] = jnp.zeros((8, own), jnp.float32)
        grad[pl.ds(rows + 8, 8)] = jnp.zeros((8, own), jnp.float32)
        for j in reversed(range(8)):

            def back(i, entry=entry):
                here = tile_rows(i, TILE, j * chunk)
                flag = fl[tile_rows(i, TILE, j * chunk + 8)]
                start = flag[:, 0:1] > 0.0
                values = take_lanes(lam, here) + take_lanes(reach, here) * entry
                before = moved_up(
                    state[pl.ds(pl.multiple_of(j * chunk + i * TILE, 8), TILE + 8)], 7, TILE
                )
                sr, decay, scale = rate_and_scale(pre_r[here, own_cols], sp[...], start)
                si = jax.nn.sigmoid(pre_i[here, own_cols])
                block = conv[here]
                driven = values * si
                log_grad = values * before * decay - block * driven * (decay * decay) / scale
                log_grad = jnp.where(start, 0.0, log_grad)
                inner = sr * log_grad
                gp_r[here, own_cols] = (
                    -rate_scale * sp[...] * inner * (1.0 - sr)
                ).astype(jnp.bfloat16)
                gp_i[here, own_cols] = (driven * block * (1.0 - si) * scale).astype(jnp.bfloat16)
                grad[tile_rows(i, TILE, j * chunk + 8)] = driven * scale
                decay_sums[...] += inner[:8] + inner[8:]

            loop(chunk // TILE, back)
            entry = ends[1, j : j + 1] + ends[0, j : j + 1] * entry
        decay_grad[...] = rate_scale * sg[...] * jnp.sum(decay_sums[...], axis=0, keepdims=True)

        for i in range(blocks):
            index = lax.rem(i + 2 - 2 * swap.odd, blocks)
            cols = swap.block(index, size)
            other = pl.ds(pl.multiple_of(wide + swap.first + index * size, RIM), size)
            spread[:, cols] = times_trans(gp_r[:, cols], gw[:, cols]) + times_trans(
                gp_i[:, cols], gw[:, other]
            )
            if i == 0:
                rim_out[...] = spread[:, swap.beyond].astype(jnp.bfloat16)
                rim = remote(rim_out, rim_in, hs.at[0], hr.at[0], swap.partner)
                rim.start()
        rim.wait()
        shared = pl.ds(pl.multiple_of((1 - swap.odd) * (own - RIM), RIM), RIM)

        def join(i):
            here = tile_rows(i, TILE)
            there = tile_rows(i, TILE, 8)
            grad[there] += spread[here, own_cols]
            grad[there, shared] += rim_in[here].astype(jnp.float32)

        loop(rows // TILE, join)

        near = grad[pl.ds(0, 16)]
        back_rows = jnp.zeros((8, own), jnp.float32)
        for k in range(1, count):
            masked = near * fl[pl.ds(0, 16)][:, k : k + 1]
            back_rows += cw[k : k + 1] * moved_up(masked, k, 8)
        ret_out[...] = back_rows
        ret = remote(
            ret_out,
            ret_in,
            hs.at[1],
            hr.at[1],
            (lax.rem(place.d + n_dp - 1, n_dp), place.t),
        )
        ret.start()
        for i in range(blocks):
            cols = swap.block(i, size)
            spread[0:size, cols] = trans_times(conv_low[:, cols], gp_r[:, cols])
            spread[size : 2 * size, cols] = trans_times(conv_low[:, cols], gp_i[:, cols])
        gate_grads[:, 0:own] = spread[0:size, own_cols].astype(jnp.bfloat16)
        gate_grads[:, own:] = spread[size : 2 * size, own_cols].astype(jnp.bfloat16)

        def taps_back(i, added=None):
            here = tile_rows(i, TILE)
            start = pl.ds(pl.multiple_of(i * TILE + 8, 8), TILE + 8)
            after = grad[start]
            flag = fl[start]
            behind = xext[pl.ds(pl.multiple_of(i * TILE, 16), 2 * TILE)].astype(jnp.float32)
            total = cw[0:1] * after[:TILE]
            for k in range(count):
                if k > 0:
                    masked = after * flag[:, k : k + 1]
                    total += cw[k : k + 1] * moved_up(masked, k, TILE)
                    mine = masked[:TILE]
                else:
                    mine = after[:TILE]
                term = mine * moved_up(behind, 16 - k, TILE)
                tap_sums[k] += term[:8] + term[8:]
            if added is not None:
                total = total + jnp.concatenate([jnp.zeros((8, own), jnp.float32), added], axis=0)
            gxy[here, 0:own] = total.astype(jnp.bfloat16)

        loop(rows // TILE - 1, taps_back)
        ret.wait()
        taps_back(rows // TILE - 1, jnp.where(place.d < n_dp - 1, ret_in[...], 0.0))
        tap_grads[...] = jnp.zeros_like(tap_grads)
        for k in range(count):
            tap_grads[k : k + 1] = jnp.sum(tap_sums[k], axis=0, keepdims=True)

    low, full = jnp.bfloat16, jnp.float32
    return pl.pallas_call(
        kernel,
        out_shape=(
            shaped((rows, 2 * own), low),
            shaped((size, 2 * own), low),
            shaped((8, own), full),
            shaped((1, own), full),
        ),
        in_specs=[in_vmem()] * 16,
        out_specs=[in_vmem()] * 4,
        scratch_shapes=[
            pltpu.VMEM((rows, width), low),
            pltpu.VMEM((rows, own), full),
            pltpu.VMEM((own // LANES, rows, LANES), full),
            pltpu.VMEM((own // LANES, rows, LANES), full),
            pltpu.VMEM((rows, wide), low),
            pltpu.VMEM((rows, wide), low),
            pltpu.VMEM((rows + 16, own), full),
            pltpu.VMEM((rows, wide), full),
            pltpu.VMEM((rows, RIM), low),
            pltpu.VMEM((rows, RIM), low),
            pltpu.VMEM((8, own), full),
            pltpu.VMEM((8, own), full),
            pltpu.VMEM((count, 8, own), full),
            pltpu.VMEM((8, own), full),
            pltpu.VMEM((2, 8, own), full),
            pltpu.VMEM((2, own), full),
            pltpu.VMEM((n_dp, 2, own), full),
            dma_sems(2),
            dma_sems(2),
            dma_sems(n_dp),
            dma_sems(n_dp),
            pltpu.SemaphoreType.DMA,
        ],
        compiler_params=comm_params(6),
        name="recur_backward",
    )(mixer_in, to_place, out_full, gates, taps, soft, slope, flags, *kept)


def matches(mesh):
    return mesh.shape["dp"] == 8 and mesh.shape["tensor"] == 4


def local_blocks(
    tokens,
    norm_gain,
    x_weight,
    y_weight,
    conv_weight,
    recur_gate_weight,
    input_gate_weight,
    decay_param,
    out_weight,
    mlp_gain,
    gate_weight,
    up_weight,
    down_weight,
    seq_lengths,
    token_order,
    cotangent,
):
    n_dp, n_tensor = lax.axis_size("dp"), lax.axis_size("tensor")
    tensor_index = lax.axis_index("tensor")
    dp_index = lax.axis_index("dp")
    tok_rows, width = tokens.shape
    row_count = tok_rows * n_tensor
    own_width = conv_weight.shape[1]
    kernel_taps = conv_weight.shape[0]
    edge_rows = kernel_taps - 1
    dp_width = norm_gain.shape[0]
    gate_rows = recur_gate_weight.shape[0]
    own_start = tensor_index * tok_rows

    mats = jnp.concatenate([x_weight, y_weight], axis=1)
    out_full = lax.all_gather(out_weight.T, "dp", axis=0, tiled=True)
    gains = jnp.concatenate([norm_gain, mlp_gain])
    spare = gate_rows * 128 - gains.shape[0]
    gains = jnp.pad(gains, (0, spare)).reshape(gate_rows, 128)
    minor = jnp.concatenate([recur_gate_weight, input_gate_weight, gains], axis=1)
    own_order = (token_order - dp_index * row_count).astype(jnp.int32)
    order_rows = jnp.broadcast_to(own_order[None, :], (8, tok_rows))
    xy_full, minor_full, tok_all, order_full = first_gather(
        n_dp, n_tensor, mats, minor, tokens, order_rows
    )
    down_full = lax.all_gather(
        lax.optimization_barrier((down_weight.T, out_full))[0], "dp", axis=0, tiled=True
    )
    order_all = order_full.reshape(n_tensor, 8, tok_rows)[:, 0].reshape(row_count)
    both_gates = minor_full[:, : 2 * own_width]
    gain_rows = minor_full[:, 2 * own_width :].reshape(n_dp, -1)
    first_gain = gain_rows[:, :dp_width].reshape(1, width).astype(jnp.float32)
    second_gain = gain_rows[:, dp_width : 2 * dp_width].reshape(1, width).astype(jnp.float32)
    block_size = both_gates.shape[0]
    row_index = jnp.arange(row_count, dtype=jnp.int32)
    hits = row_index[:, None] == order_all[None, :]
    to_place = hits.astype(jnp.bfloat16)
    to_stored = (order_all[:, None] == row_index[None, :]).astype(jnp.bfloat16)
    places = dp_index * row_count + jnp.arange(-8, row_count + 8, dtype=jnp.int32)
    inside = (jnp.arange(row_count + 16) >= 8) & (jnp.arange(row_count + 16) < row_count + 8)
    ends = jnp.cumsum(seq_lengths)
    segment = segment_of(places, ends)
    starts = (places == 0) | (segment != segment_of(places - 1, ends))
    columns = [starts] + [
        segment_of(places - shift, ends) == segment for shift in range(1, kernel_taps)
    ]
    columns += [jnp.zeros_like(starts)] * (8 - len(columns))
    flags = (jnp.stack(columns, axis=1) & inside[:, None]).astype(jnp.float32)
    live_stored = (order_all + dp_index * row_count < ends[-1]).astype(jnp.float32)
    live_own = (token_order < ends[-1]).astype(jnp.float32)
    soft = jax.nn.softplus(-decay_param).reshape(1, own_width)
    slope = jax.nn.sigmoid(-decay_param).reshape(1, own_width)
    zero_rim = jnp.zeros((block_size, RIM), jnp.bfloat16)
    gates_wide = jnp.concatenate(
        [
            zero_rim,
            both_gates[:, :own_width],
            zero_rim,
            zero_rim,
            both_gates[:, own_width:],
            zero_rim,
        ],
        axis=1,
    )
    def glu(gate_pre, up_pre):
        return gelu_tanh(gate_pre) * up_pre

    hidden_place, *kept, merged_stored, mixer_terms, cot_all = recur_forward(
        n_dp,
        n_tensor,
        tok_all,
        cotangent,
        to_place,
        to_stored,
        xy_full,
        out_full,
        first_gain,
        gates_wide,
        conv_weight,
        soft,
        flags,
    )
    after_own, hidden_two, gate_full, up_full = middle_gather(
        n_dp, n_tensor, mixer_terms, tokens, second_gain, (gate_weight, up_weight)
    )
    gate_pre = plain_dot(hidden_two, gate_full)
    up_pre = plain_dot(hidden_two, up_full)
    glu_out, glu_pull = jax.vjp(glu, gate_pre, up_pre)
    product = glu_out.astype(jnp.bfloat16)
    feed_out = lax.psum_scatter(
        times_trans(product, down_full).astype(jnp.bfloat16),
        "tensor",
        scatter_dimension=0,
        tiled=True,
    ).astype(jnp.float32)
    output = ((after_own + feed_out) * live_own[:, None]).astype(jnp.bfloat16)

    down_in = (cot_all.astype(jnp.float32) * live_stored[:, None]).astype(jnp.bfloat16)
    grad_in_own = (cotangent.astype(jnp.float32) * live_own[:, None]).astype(jnp.bfloat16)
    grad_down = trans_times(down_in, product).astype(jnp.bfloat16)
    grad_product = plain_dot(down_in, down_full)
    grad_gate_pre, grad_up_pre = glu_pull(grad_product)
    grad_gate_pre = grad_gate_pre.astype(jnp.bfloat16)
    grad_up_pre = grad_up_pre.astype(jnp.bfloat16)
    grad_gate = trans_times(hidden_two, grad_gate_pre).astype(jnp.bfloat16)
    grad_up = trans_times(hidden_two, grad_up_pre).astype(jnp.bfloat16)
    feed_terms = (
        times_trans(grad_gate_pre, gate_full) + times_trans(grad_up_pre, up_full)
    ).astype(jnp.bfloat16)
    down_sum = lax.psum_scatter(grad_down, "dp", scatter_dimension=0, tiled=True)
    grad_after_own, second_part, mixer_in, gate_sum, up_sum = middle_sums(
        n_dp, n_tensor, feed_terms, after_own, second_gain, grad_in_own, (grad_gate, grad_up)
    )

    grad_out_mat = trans_times(mixer_in, merged_stored).astype(jnp.bfloat16)
    out_sum = lax.psum_scatter(grad_out_mat, "dp", scatter_dimension=0, tiled=True)
    grad_xy, gate_grads, tap_grads, decay_grad = recur_backward(
        n_dp,
        n_tensor,
        mixer_in,
        to_place,
        out_full,
        gates_wide,
        conv_weight,
        soft,
        slope,
        flags,
        kept,
    )
    grad_xy_mat = trans_times(hidden_place, grad_xy).astype(jnp.bfloat16)
    grad_xy_stored = plain_dot(to_stored, grad_xy).astype(jnp.bfloat16)
    one_terms = times_trans(grad_xy_stored, xy_full).astype(jnp.bfloat16)
    small = jnp.concatenate(
        [
            second_part,
            tap_grads[:kernel_taps].reshape(1, -1),
            jnp.pad(decay_grad, ((0, 0), (0, width - own_width))),
            jnp.zeros((1, width), jnp.float32),
        ],
        axis=0,
    )
    grad_tokens, small_sum, gain_sums, xy_sum, gates_sum = last_sums(
        n_dp,
        n_tensor,
        one_terms,
        tokens,
        first_gain,
        grad_after_own,
        small,
        (grad_xy_mat, gate_grads),
    )
    xy_sum, gates_sum = xy_sum.astype(jnp.float32), gates_sum.astype(jnp.float32)
    own_gains = lax.dynamic_slice_in_dim(gain_sums, dp_index * dp_width, dp_width, 1)
    return (
        output,
        grad_tokens,
        own_gains[1],
        xy_sum[:, :own_width],
        xy_sum[:, own_width:],
        small_sum[1].reshape(kernel_taps, own_width),
        gates_sum[:, :own_width],
        gates_sum[:, own_width:],
        small_sum[2, :own_width],
        out_sum.astype(jnp.float32).T,
        own_gains[0],
        gate_sum.astype(jnp.float32),
        up_sum.astype(jnp.float32),
        down_sum.astype(jnp.float32).T,
    )


def solution(mesh):
    in_specs = (
        P(("dp", "tensor"), None),
        P("dp"),
        P("dp", "tensor"),
        P("dp", "tensor"),
        P(None, "tensor"),
        P("dp", "tensor"),
        P("dp", "tensor"),
        P("tensor"),
        P("tensor", "dp"),
        P("dp"),
        P("dp", "tensor"),
        P("dp", "tensor"),
        P("tensor", "dp"),
        P(),
        P(("dp", "tensor")),
        P(("dp", "tensor"), None),
    )
    out_specs = (
        P(("dp", "tensor"), None),
        P(("dp", "tensor"), None),
        P("dp"),
        P("dp", "tensor"),
        P("dp", "tensor"),
        P(None, "tensor"),
        P("dp", "tensor"),
        P("dp", "tensor"),
        P("tensor"),
        P("tensor", "dp"),
        P("dp"),
        P("dp", "tensor"),
        P("dp", "tensor"),
        P("tensor", "dp"),
    )
    fits = matches(mesh)
    local = local_blocks if fits else local_general
    return jax.shard_map(local, mesh=mesh, in_specs=in_specs, out_specs=out_specs, check_vma=False)
```

```python
import jax
import jax.numpy as jnp
from jax import lax
from jax.experimental import pallas as pl
from jax.experimental.pallas import tpu as pltpu
from jax.sharding import PartitionSpec as P

epsilon = 1e-06
rate_scale = 8.0


def from_behind(block, axis, distance):
    devices = range(lax.axis_size(axis))
    route = [(i - distance, i) for i in devices if i - distance in devices]
    return lax.ppermute(block, axis, route)


def extended_2(array, sides, width):
    for axis, dim in sides:
        size, length = (lax.axis_size(axis), array.shape[dim])
        up = [(i, (i + 1) % size) for i in range(size - 1)]
        down = [(j, i) for i, j in up]
        last = lax.slice_in_dim(array, length - width, length, axis=dim)
        leading = lax.slice_in_dim(array, 0, width, axis=dim)
        before = lax.ppermute(last, axis, up)
        after = lax.ppermute(leading, axis, down)
        array = jnp.concatenate([before, array, after], axis=dim)
    return array


def entering(value, axis, join, neutral, backward):
    count, mine = (lax.axis_size(axis), lax.axis_index(axis))
    pieces = jax.tree.map(lambda part: lax.all_gather(part, axis), value)
    if backward:
        pieces = jax.tree.map(lambda part: part[::-1], pieces)
        mine = count - 1 - mine
    total = jax.tree.map(
        lambda part, zero: jnp.full_like(part, 0) + jnp.asarray(zero, part.dtype), value, neutral
    )

    def lap(position, total):
        longer = join(total, jax.tree.map(lambda part: part[position], pieces))
        return jax.tree.map(lambda new, old: jnp.where(position < mine, new, old), longer, total)

    return lax.fori_loop(0, count - 1, lap, total)


def rms_scale(values, gain):
    return values * lax.rsqrt(jnp.mean(values * values, axis=-1, keepdims=True) + epsilon) * gain


def norm_back(values, gain, grad):
    inv_root = lax.rsqrt(jnp.mean(values * values, axis=-1, keepdims=True) + epsilon)
    normed = values * inv_root
    upstream = grad * gain
    grad_values = inv_root * (
        upstream - normed * jnp.mean(upstream * normed, axis=-1, keepdims=True)
    )
    return (grad_values, normed)


def segment_of(places, ends):
    return jnp.sum((ends[None, :] <= places[:, None]).astype(jnp.int32), axis=1)


def pair_step(early, later):
    return (early[0] * later[0], later[0] * early[1] + later[1])


def plain_dot(left, right):
    return jnp.dot(left, right, preferred_element_type=jnp.float32)


def times_trans(left, right):
    return lax.dot_general(
        left, right, (((1,), (1,)), ((), ())), preferred_element_type=jnp.float32
    )


def trans_times(left, right):
    return lax.dot_general(
        left, right, (((0,), (0,)), ((), ())), preferred_element_type=jnp.float32
    )


def gelu_tanh(values):
    return jax.nn.gelu(values, approximate=True)


def collect(
    norm_gain,
    mlp_gain,
    x_weight,
    y_weight,
    recur_gate_weight,
    input_gate_weight,
    gate_weight,
    up_weight,
    out_weight,
    down_weight,
):
    return (
        lax.all_gather(norm_gain, "dp", axis=0, tiled=True),
        lax.all_gather(mlp_gain, "dp", axis=0, tiled=True),
        lax.all_gather(x_weight, "dp", axis=0, tiled=True),
        lax.all_gather(y_weight, "dp", axis=0, tiled=True),
        lax.all_gather(recur_gate_weight, "dp", axis=0, tiled=True),
        lax.all_gather(input_gate_weight, "dp", axis=0, tiled=True),
        lax.all_gather(gate_weight, "dp", axis=0, tiled=True),
        lax.all_gather(up_weight, "dp", axis=0, tiled=True),
        lax.all_gather(out_weight, "dp", axis=1, tiled=True),
        lax.all_gather(down_weight, "dp", axis=1, tiled=True),
    )


def row_sums(term_rows, tok_rows):
    return lax.psum_scatter(
        term_rows(jnp.int32(0), lax.axis_size("tensor") * tok_rows).astype(jnp.bfloat16),
        "tensor",
        scatter_dimension=0,
        tiled=True,
    ).astype(jnp.float32)


def spread_rows(values):
    return lax.all_gather(values, "tensor", axis=0, tiled=True)


def local_general(
    tokens,
    norm_gain,
    x_weight,
    y_weight,
    conv_weight,
    recur_gate_weight,
    input_gate_weight,
    decay_param,
    out_weight,
    mlp_gain,
    gate_weight,
    up_weight,
    down_weight,
    seq_lengths,
    token_order,
    cotangent,
):
    n_tensor = lax.axis_size("tensor")
    tensor_index = lax.axis_index("tensor")
    dp_index = lax.axis_index("dp")
    tok_rows = tokens.shape[0]
    row_count = tok_rows * n_tensor
    own_width = conv_weight.shape[1]
    kernel_taps = conv_weight.shape[0]
    edge_rows = kernel_taps - 1
    dp_width = norm_gain.shape[0]
    own_start = tensor_index * tok_rows
    shards = (
        norm_gain,
        mlp_gain,
        x_weight,
        y_weight,
        recur_gate_weight,
        input_gate_weight,
        gate_weight,
        up_weight,
        out_weight,
        down_weight,
    )
    (
        gain_one,
        gain_two,
        x_full,
        y_full,
        recur_full,
        input_full,
        gate_full,
        up_full,
        out_full,
        down_full,
    ) = collect(*shards)
    block_size = recur_full.shape[0]
    first_gain = gain_one.astype(jnp.float32)
    second_gain = gain_two.astype(jnp.float32)
    both_gates = jnp.concatenate([recur_full, input_full], axis=1)
    tok_own = tokens.astype(jnp.float32)
    own_order = token_order - dp_index * row_count
    first_rows = rms_scale(tok_own, first_gain).astype(jnp.bfloat16)
    first_all, cot_all, order_all = (
        lax.all_gather(first_rows, "tensor", axis=0, tiled=True),
        lax.all_gather(cotangent, "tensor", axis=0, tiled=True),
        lax.all_gather(own_order, "tensor", axis=0, tiled=True),
    )
    row_index = jnp.arange(row_count, dtype=jnp.int32)
    inverse = jnp.zeros((row_count,), jnp.int32).at[order_all].set(row_index)
    hidden_place = jnp.take(first_all, inverse, axis=0)
    places = dp_index * row_count + row_index
    ends = jnp.cumsum(seq_lengths)
    segment = segment_of(places, ends)
    starts = (places == 0) | (segment != segment_of(places - 1, ends))
    live = (places < ends[-1]).astype(jnp.float32)
    live_stored = jnp.take(live, order_all, axis=0)
    same = [
        (segment_of(places - shift, ends) == segment).astype(jnp.float32)
        for shift in range(kernel_taps)
    ]
    low_edge = tensor_index * own_width
    own_blocks = (low_edge + jnp.arange(own_width, dtype=jnp.int32)) // block_size
    first_block = low_edge // block_size
    block_count = own_width // block_size + 2

    def block_start(index):
        return (first_block + index) * block_size - low_edge + block_size

    def block_mask(index):
        inside = own_blocks == first_block + index
        return jnp.concatenate([inside, inside])

    def convolve(extended, kernel):
        return sum(
            (
                kernel[shift][None, :]
                * extended[edge_rows - shift : edge_rows - shift + row_count]
                * same[shift][:, None]
                for shift in range(kernel_taps)
            )
        )

    def gates(conv_vals, pre_recur, pre_input, decay_vals):
        log_rate = -rate_scale * jax.nn.sigmoid(pre_recur) * jax.nn.softplus(-decay_vals)
        decay_rate = jnp.where(starts[:, None], 0.0, jnp.exp(log_rate))
        scale_in = jnp.where(starts[:, None], 1.0, jnp.sqrt(-jnp.expm1(2.0 * log_rate)))
        return (decay_rate, conv_vals * jax.nn.sigmoid(pre_input) * scale_in)

    def glu(gate_pre, up_pre):
        return gelu_tanh(gate_pre) * up_pre

    x_branch = plain_dot(hidden_place, x_full).astype(jnp.bfloat16)
    y_before = plain_dot(hidden_place, y_full)
    previous = from_behind(x_branch[row_count - edge_rows :], "dp", 1)
    extended = jnp.concatenate([previous, x_branch], axis=0).astype(jnp.float32)
    conv_out = convolve(extended, conv_weight)
    conv_wide = extended_2(conv_out.astype(jnp.bfloat16), (("tensor", 1),), block_size)
    pre_both = jnp.zeros((row_count, 2 * own_width), jnp.float32)
    for index in range(block_count):
        piece = lax.dynamic_slice_in_dim(conv_wide, block_start(index), block_size, 1)
        pre_both = pre_both + jnp.where(
            block_mask(index)[None, :], plain_dot(piece, both_gates), 0.0
        )
    (decay_rate, driven), gate_pull = jax.vjp(
        gates, conv_out, pre_both[:, :own_width], pre_both[:, own_width:], decay_param
    )
    cum_rate, local_state = lax.associative_scan(pair_step, (decay_rate, driven), axis=0)
    ident = (jnp.ones((own_width,), jnp.float32), jnp.zeros((own_width,), jnp.float32))
    rate_in, state_in = entering((cum_rate[-1], local_state[-1]), "dp", pair_step, ident, False)
    state = local_state + cum_rate * state_in[None, :]
    y_branch = gelu_tanh(y_before)
    merged = (state * y_branch).astype(jnp.bfloat16)
    merged_stored = jnp.take(merged, order_all, axis=0)

    def mixer_rows(begin, number):
        return plain_dot(merged_stored, out_full)

    after_own = tok_own + row_sums(mixer_rows, tok_rows)
    hidden_two = spread_rows(rms_scale(after_own, second_gain).astype(jnp.bfloat16))
    gate_pre = plain_dot(hidden_two, gate_full)
    up_pre = plain_dot(hidden_two, up_full)
    glu_out, glu_pull = jax.vjp(glu, gate_pre, up_pre)
    product = glu_out.astype(jnp.bfloat16)

    def down_rows(begin, number):
        return plain_dot(product, down_full)

    feed_out = row_sums(down_rows, tok_rows)
    live_own = lax.dynamic_slice_in_dim(live_stored, own_start, tok_rows, 0)
    output = ((after_own + feed_out) * live_own[:, None]).astype(jnp.bfloat16)
    grad_out = cot_all.astype(jnp.float32) * live_stored[:, None]
    fresh = lax.optimization_barrier((shards, grad_out))[0]
    (
        gain_one,
        gain_two,
        x_full,
        y_full,
        recur_full,
        input_full,
        gate_full,
        up_full,
        out_full,
        down_full,
    ) = collect(*fresh)
    first_gain = gain_one.astype(jnp.float32)
    second_gain = gain_two.astype(jnp.float32)
    both_gates = jnp.concatenate([recur_full, input_full], axis=1)
    down_in = grad_out.astype(jnp.bfloat16)
    grad_down = trans_times(product, down_in)
    grad_product = times_trans(down_in, down_full)
    grad_gate_pre, grad_up_pre = glu_pull(grad_product)
    grad_gate_pre = grad_gate_pre.astype(jnp.bfloat16)
    grad_up_pre = grad_up_pre.astype(jnp.bfloat16)
    grad_gate = trans_times(hidden_two, grad_gate_pre)
    grad_up = trans_times(hidden_two, grad_up_pre)

    def feed_rows(begin, number):
        return times_trans(grad_gate_pre, gate_full) + times_trans(grad_up_pre, up_full)

    grad_out_own = lax.dynamic_slice_in_dim(grad_out, own_start, tok_rows, 0)
    grad_two_own = row_sums(feed_rows, tok_rows)
    grad_norm_own, normed_two = norm_back(after_own, second_gain, grad_two_own)
    second_part = jnp.sum(grad_two_own * normed_two, axis=0)
    grad_after_own = grad_out_own + grad_norm_own
    mixer_in = spread_rows(grad_after_own.astype(jnp.bfloat16))
    grad_out_mat = trans_times(merged_stored, mixer_in)
    grad_merged = jnp.take(times_trans(mixer_in, out_full), inverse, axis=0)
    grad_state = grad_merged * y_branch
    gelu_pull = jax.vjp(gelu_tanh, y_before)[1]
    grad_y_before = gelu_pull(grad_merged * state)[0].astype(jnp.bfloat16)
    rate_next = jnp.concatenate([decay_rate[1:], jnp.ones((1, own_width), jnp.float32)], axis=0)
    rev_rate, local_lam = lax.associative_scan(
        pair_step, (rate_next, grad_state), reverse=True, axis=0
    )
    head_rate = decay_rate[0] * rev_rate[0]
    head_lam = decay_rate[0] * local_lam[0]
    factor_in, lam_in = entering((head_rate, head_lam), "dp", pair_step, ident, True)
    lam = local_lam + rev_rate * lam_in[None, :]
    state_prev = jnp.concatenate([state_in[None, :], state[:-1]], axis=0)
    grad_conv_local, grad_pre_recur, grad_pre_input, grad_decay_own = gate_pull(
        (lam * state_prev, lam)
    )
    grad_pre = jnp.concatenate([grad_pre_recur, grad_pre_input], axis=1).astype(jnp.bfloat16)
    grad_both = jnp.zeros((block_size, 2 * own_width), jnp.float32)
    grad_wide = jnp.zeros((row_count, own_width + 2 * block_size), jnp.float32)
    for index in range(block_count):
        begin = block_start(index)
        piece = lax.dynamic_slice_in_dim(conv_wide, begin, block_size, 1)
        masked = jnp.where(block_mask(index)[None, :], grad_pre, jnp.zeros((), jnp.bfloat16))
        grad_both = grad_both + trans_times(piece, masked)
        added = lax.dynamic_slice_in_dim(grad_wide, begin, block_size, 1) + times_trans(
            masked, both_gates
        )
        grad_wide = lax.dynamic_update_slice_in_dim(grad_wide, added, begin, 1)
    grad_recur = grad_both[:, :own_width]
    grad_input = grad_both[:, own_width:]
    rims = jnp.concatenate(
        [grad_wide[:, :block_size], grad_wide[:, own_width + block_size :]], axis=1
    )
    arrived = extended_2(rims.astype(jnp.bfloat16), (("tensor", 1),), block_size).astype(rims.dtype)
    from_lower = jnp.pad(arrived[:, :block_size], ((0, 0), (0, own_width - block_size)))
    from_upper = jnp.pad(arrived[:, 3 * block_size :], ((0, 0), (own_width - block_size, 0)))
    grad_conv = (
        grad_conv_local
        + grad_wide[:, block_size : block_size + own_width]
        + from_lower
        + from_upper
    )
    conv_pull = jax.vjp(convolve, extended, conv_weight)[1]
    grad_extended, grad_kernel = conv_pull(grad_conv)
    returned = from_behind(grad_extended[:edge_rows], "dp", -1)
    grad_x_branch = grad_extended[edge_rows:] + jnp.concatenate(
        [jnp.zeros((row_count - edge_rows, own_width), jnp.float32), returned], axis=0
    )
    grad_x_low = grad_x_branch.astype(jnp.bfloat16)
    grad_x_stored = jnp.take(grad_x_low, order_all, axis=0)
    grad_y_stored = jnp.take(grad_y_before, order_all, axis=0)
    grad_x_mat = trans_times(first_all, grad_x_stored)
    grad_y_mat = trans_times(first_all, grad_y_stored)

    def mixer_back_rows(begin, number):
        return times_trans(grad_x_stored, x_full) + times_trans(grad_y_stored, y_full)

    grad_one_own = row_sums(mixer_back_rows, tok_rows)
    grad_norm_one, normed_one = norm_back(tok_own, first_gain, grad_one_own)
    first_part = jnp.sum(grad_one_own * normed_one, axis=0)
    grad_tokens = grad_after_own + grad_norm_one
    chosen = jnp.arange(n_tensor, dtype=jnp.int32) == tensor_index
    kernel_tile = jnp.where(chosen[:, None, None], grad_kernel[None, :, :], 0.0)
    decay_tile = jnp.where(chosen[:, None], grad_decay_own[None, :], 0.0)
    small = lax.psum((first_part, second_part, kernel_tile, decay_tile), ("dp", "tensor"))
    grad_first_gain = lax.dynamic_slice_in_dim(small[0], dp_index * dp_width, dp_width, 0)
    grad_second_gain = lax.dynamic_slice_in_dim(small[1], dp_index * dp_width, dp_width, 0)
    grad_kernel_sum = lax.dynamic_index_in_dim(small[2], tensor_index, 0, keepdims=False)
    grad_decay = lax.dynamic_index_in_dim(small[3], tensor_index, 0, keepdims=False)
    sums = (
        lax.psum_scatter(
            grad_x_mat.astype(jnp.bfloat16), "dp", scatter_dimension=0, tiled=True
        ).astype(jnp.float32),
        lax.psum_scatter(
            grad_y_mat.astype(jnp.bfloat16), "dp", scatter_dimension=0, tiled=True
        ).astype(jnp.float32),
        lax.psum_scatter(
            grad_recur.astype(jnp.bfloat16), "dp", scatter_dimension=0, tiled=True
        ).astype(jnp.float32),
        lax.psum_scatter(
            grad_input.astype(jnp.bfloat16), "dp", scatter_dimension=0, tiled=True
        ).astype(jnp.float32),
        lax.psum_scatter(
            grad_gate.astype(jnp.bfloat16), "dp", scatter_dimension=0, tiled=True
        ).astype(jnp.float32),
        lax.psum_scatter(
            grad_up.astype(jnp.bfloat16), "dp", scatter_dimension=0, tiled=True
        ).astype(jnp.float32),
        lax.psum_scatter(
            grad_out_mat.astype(jnp.bfloat16), "dp", scatter_dimension=1, tiled=True
        ).astype(jnp.float32),
        lax.psum_scatter(
            grad_down.astype(jnp.bfloat16), "dp", scatter_dimension=1, tiled=True
        ).astype(jnp.float32),
    )
    return (
        output,
        grad_tokens,
        grad_first_gain,
        sums[0],
        sums[1],
        grad_kernel_sum,
        sums[2],
        sums[3],
        grad_decay,
        sums[6],
        grad_second_gain,
        sums[4],
        sums[5],
        sums[7],
    )


MESH = pl.DeviceIdType.MESH
VMEM_BYTES = 60 * 2**20


def remote(src, dst, send, recv, device):
    return pltpu.make_async_remote_copy(
        src_ref=src,
        dst_ref=dst,
        send_sem=send,
        recv_sem=recv,
        device_id=device,
        device_id_type=MESH,
    )


class Place:
    def __init__(self, n_dp, n_line):
        self.n_dp, self.n_line = n_dp, n_line
        self.d, self.t = lax.axis_index("dp"), lax.axis_index("tensor")
        self.core = lax.rem(self.d, 2)
        self.x = lax.rem(lax.div(self.d, 2), 2)
        self.y = lax.div(self.d, 4)

    def chip(self, flip_x, flip_y, flip_core=0):
        x = 1 - self.x if flip_x else self.x
        y = 1 - self.y if flip_y else self.y
        core = 1 - self.core if flip_core else self.core
        return y * 4 + x * 2 + core

    def at(self, flip_x=0, flip_y=0, flip_core=0):
        return (self.chip(flip_x, flip_y, flip_core), self.t)

    def up(self):
        return (self.d, lax.rem(self.t + 1, self.n_line))

    def down(self):
        return (self.d, lax.rem(self.t + self.n_line - 1, self.n_line))

    def meet(self, everyone=False):
        barrier = pltpu.get_barrier_semaphore()

        def greet(device):
            pl.semaphore_signal(barrier, inc=1, device_id=device, device_id_type=MESH)

        if everyone:
            for i in range(1, self.n_dp):
                greet((lax.rem(self.d + i, self.n_dp), self.t))
            for i in range(1, self.n_line):
                greet((self.d, lax.rem(self.t + i, self.n_line)))
            pl.semaphore_wait(barrier, self.n_dp + self.n_line - 2)
            return
        for flips in ((1, 0), (0, 1), (0, 0, 1)):
            greet(self.at(*flips))
        below, above = self.t > 0, self.t < self.n_line - 1

        @pl.when(below)
        def _():
            greet(self.down())

        @pl.when(above)
        def _():
            greet(self.up())

        pl.semaphore_wait(barrier, 3 + below.astype(jnp.int32) + above.astype(jnp.int32))


class GatherPlane:
    def __init__(self, place, src, dst, send, recv, local):
        self.p, self.src, self.dst = place, src, dst
        self.rows = src.shape[0]
        self.send, self.recv, self.local = send, recv, local

    def block(self, fx, fy, fc=0, part=None):
        first = self.p.chip(fx, fy, fc) * self.rows
        size = self.rows
        if part is not None:
            size = self.rows // 2
            first = first + part * size
        return self.dst.at[pl.ds(pl.multiple_of(first, 16), size)]

    def copy(self, i, src, dst, device):
        return remote(src, dst, self.send.at[i], self.recv.at[i], device)

    def mine(self):
        return pltpu.make_async_copy(self.src, self.block(0, 0), self.local)

    def outgoing(self, i):
        at, block = self.p.at, self.block
        if i == 0:
            return self.copy(0, self.src, block(0, 0), at(1, 0))
        if i == 1:
            return self.copy(1, self.src, block(0, 0), at(0, 1))
        if i == 2:
            return self.copy(2, self.src, block(0, 0), at(0, 0, 1))
        if i == 3:
            return self.copy(3, block(1, 0, 0, 0), block(1, 0, 0, 0), at(0, 1))
        if i == 4:
            return self.copy(4, block(0, 1, 0, 1), block(0, 1, 0, 1), at(1, 0))
        spot = ((1, 0), (0, 1), (1, 1, 0, 0), (1, 1, 0, 1))[i - 5]
        return self.copy(i, block(*spot), block(*spot), at(0, 0, 1))

    def arrive(self, i):
        spot = (
            (1, 0),
            (0, 1),
            (0, 0, 1),
            (1, 1, 0, 0),
            (1, 1, 0, 1),
            (1, 0, 1),
            (0, 1, 1),
            (1, 1, 1, 0),
            (1, 1, 1, 1),
        )[i]
        here = self.block(*spot)
        self.copy(i, here, here, self.p.at(0, 0, 1)).wait_recv()

    def begin(self):
        self.mine().start()
        for i in (0, 1, 2):
            self.outgoing(i).start()

    def forward(self):
        self.arrive(0)
        self.outgoing(3).start()
        self.arrive(1)
        self.outgoing(4).start()
        self.outgoing(5).start()
        self.outgoing(6).start()

    def share(self):
        self.arrive(3)
        self.outgoing(7).start()
        self.arrive(4)
        self.outgoing(8).start()

    def finish(self):
        for i in (2, 5, 6, 7, 8):
            self.arrive(i)
        for i in range(9):
            self.outgoing(i).wait_send()
        self.mine().wait()


class GatherLine:
    def __init__(self, place, dst, rows, begin, span, send, recv):
        self.p, self.dst, self.rows = place, dst, rows
        self.begin, self.span = begin, span
        self.send, self.recv = send, recv
        self.last = place.n_line - 1

    def block(self, owner):
        first = owner * self.rows + self.begin
        return self.dst.at[pl.ds(pl.multiple_of(first, 8), self.span)]

    def copy(self, way, k, owner, source=None):
        to = self.p.up() if way == 0 else self.p.down()
        block = self.block(owner)
        return remote(
            block if source is None else source,
            block,
            self.send.at[way, k],
            self.recv.at[way, k],
            to,
        )

    def step(self, k, source=None):
        t, last = self.p.t, self.last
        if k > 0:
            self.arrive(k - 1)

        @pl.when((t < last) & (t >= k))
        def _():
            self.copy(0, k, t - k, source).start()

        @pl.when((t > 0) & (t + k <= last))
        def _():
            self.copy(1, k, t + k, source).start()

    def arrive(self, k):
        t, last = self.p.t, self.last

        @pl.when(t >= k + 1)
        def _():
            self.copy(0, k, t - 1 - k).wait_recv()

        @pl.when(t + k + 1 <= last)
        def _():
            self.copy(1, k, t + 1 + k).wait_recv()

    def finish(self):
        t, last = self.p.t, self.last
        self.arrive(last - 1)
        for k in range(last):

            @pl.when((t < last) & (t >= k))
            def _():
                self.copy(0, k, t - k).wait_send()

            @pl.when((t > 0) & (t + k <= last))
            def _():
                self.copy(1, k, t + k).wait_send()


class ReduceLine:
    def __init__(self, place, terms, rows, begin, span, stage, inbox, send, recv):
        self.p, self.terms, self.rows = place, terms, rows
        self.begin, self.span = begin, span
        self.stage, self.inbox = stage, inbox
        self.send, self.recv = send, recv
        self.last = place.n_line - 1

    def own(self, owner):
        first = owner * self.rows + self.begin
        return self.terms.at[pl.ds(pl.multiple_of(first, 16), self.span)]

    def copy(self, way, j, source):
        to = self.p.up() if way == 0 else self.p.down()
        return remote(
            source, self.inbox.at[way, j], self.send.at[way, j], self.recv.at[way, j], to
        )

    def ends(self):
        t, last = self.p.t, self.last

        @pl.when(t == 0)
        def _():
            for j in range(last):
                self.copy(0, j, self.own(last - j)).start()

        @pl.when(t == last)
        def _():
            for j in range(last):
                self.copy(1, j, self.own(j)).start()

    def sent(self):
        t, last = self.p.t, self.last

        @pl.when(t == 0)
        def _():
            for j in range(last):
                self.copy(0, j, self.own(last - j)).wait_send()

        @pl.when(t == last)
        def _():
            for j in range(last):
                self.copy(1, j, self.own(j)).wait_send()

    def hand_on(self, way, j):
        term = self.own(self.last - j if way == 0 else j)
        self.copy(way, j, term).wait_recv()
        self.stage[way, j] = (
            term[...].astype(jnp.float32) + self.inbox[way, j].astype(jnp.float32)
        ).astype(jnp.bfloat16)
        self.copy(way, j, self.stage.at[way, j]).start()

    def hop(self, k):
        t, last = self.p.t, self.last

        @pl.when(t == k + 1)
        def _():
            for j in range(last - 1 - k):
                self.hand_on(0, j)

        @pl.when(t == last - 1 - k)
        def _():
            for j in range(last - 1 - k):
                self.hand_on(1, j)

    def total(self, result):
        t, last = self.p.t, self.last
        result[...] = self.own(t)[...].astype(jnp.float32)

        @pl.when(t > 0)
        def _():
            j = last - t
            self.copy(0, j, self.stage.at[0, 0]).wait_recv()
            result[...] += self.inbox[0, j].astype(jnp.float32)

        @pl.when(t < last)
        def _():
            self.copy(1, t, self.stage.at[0, 0]).wait_recv()
            result[...] += self.inbox[1, t].astype(jnp.float32)

    def finish(self):
        t, last = self.p.t, self.last
        for j in range(last - 1):

            @pl.when((t > 0) & (t < last - j))
            def _():
                self.copy(0, j, self.stage.at[0, j]).wait_send()

            @pl.when((t < last) & (t > j))
            def _():
                self.copy(1, j, self.stage.at[1, j]).wait_send()


def add_rows(into, other, result=None):
    result = into if result is None else result

    def tile(i, carry):
        rows = pl.ds(pl.multiple_of(i * 16, 16), 16)
        result[rows] = (
            into[rows].astype(jnp.float32) + other[rows].astype(jnp.float32)
        ).astype(result.dtype)
        return carry

    lax.fori_loop(0, into.shape[0] // 16, tile, None)


class ReducePlane:
    chips = ((0, 0), (1, 0), (0, 1), (1, 1))

    def __init__(self, place, terms, scratch):
        self.p, self.terms = place, terms
        self.held, self.near, self.along, self.last, self.send, self.recv, self.local = scratch
        self.rows = self.held.shape[1]
        self.half = self.rows // 2

    @staticmethod
    def scratch(rows, width):
        return [
            pltpu.VMEM((4, rows, width), jnp.bfloat16),
            pltpu.VMEM((4, rows, width), jnp.bfloat16),
            pltpu.VMEM((4, rows // 2, width), jnp.bfloat16),
            pltpu.VMEM((2, rows // 2, width), jnp.bfloat16),
            pltpu.SemaphoreType.DMA((10,)),
            pltpu.SemaphoreType.DMA((10,)),
            pltpu.SemaphoreType.DMA((4,)),
        ]

    def block(self, k, other):
        first = self.p.chip(*self.chips[k], other) * self.rows
        return self.terms.at[pl.ds(pl.multiple_of(first, 16), self.rows)]

    def half_of(self, k, part):
        return self.held.at[k, pl.ds(part * self.half, self.half)]

    def load(self, k):
        return pltpu.make_async_copy(self.block(k, 0), self.held.at[k], self.local.at[k])

    def copy(self, i):
        at = self.p.at
        if i < 4:
            src, dst, to = self.block(i, 1), self.near.at[i], at(0, 0, 1)
        elif i < 8:
            src, to = (
                (self.half_of(1, 0), at(1, 0)),
                (self.half_of(3, 0), at(1, 0)),
                (self.half_of(2, 1), at(0, 1)),
                (self.half_of(3, 1), at(0, 1)),
            )[i - 4]
            dst = self.along.at[i - 4]
        else:
            src, to = ((self.half_of(2, 0), at(0, 1)), (self.half_of(1, 1), at(1, 0)))[i - 8]
            dst = self.last.at[i - 8]
        return remote(src, dst, self.send.at[i], self.recv.at[i], to)

    def begin(self):
        for k in (3, 1, 2, 0):
            self.copy(k).start()
            self.load(k).start()

    def cores(self):
        for k in (3, 1, 2, 0):
            self.load(k).wait()
            self.copy(k).wait_recv()
            add_rows(self.held.at[k], self.near.at[k])
            if k == 3:
                self.copy(5).start()
                self.copy(7).start()
            elif k == 1:
                self.copy(4).start()
            elif k == 2:
                self.copy(6).start()

    def turn(self):
        self.copy(5).wait_recv()
        add_rows(self.half_of(2, 0), self.along.at[1])
        self.copy(8).start()
        self.copy(7).wait_recv()
        add_rows(self.half_of(1, 1), self.along.at[3])
        self.copy(9).start()
        self.copy(4).wait_recv()
        add_rows(self.half_of(0, 0), self.along.at[0])
        self.copy(6).wait_recv()
        add_rows(self.half_of(0, 1), self.along.at[2])

    def finish(self, result):
        for part in (0, 1):
            self.copy(8 + part).wait_recv()
            rows = pl.ds(part * self.half, self.half)
            add_rows(self.half_of(0, part), self.last.at[part], result.at[rows])
        for i in range(10):
            self.copy(i).wait_send()


def dma_sems(*dims):
    return pltpu.SemaphoreType.DMA(dims)


def in_vmem():
    return pl.BlockSpec(memory_space=pltpu.VMEM)


def in_any():
    return pl.BlockSpec(memory_space=pl.ANY)


def comm_params(number):
    return pltpu.CompilerParams(
        collective_id=number, has_side_effects=True, vmem_limit_bytes=VMEM_BYTES
    )


def shaped(dims, kind):
    return jax.ShapeDtypeStruct(dims, kind)


def first_gather(n_dp, n_line, mats, rows_in, order):
    count = len(mats)
    parts = 2

    def kernel(*refs):
        srcs, (c, e) = refs[:count], refs[count : count + 2]
        dsts, (c_out, e_out) = refs[count + 2 : 2 * count + 2], refs[2 * count + 2 : 2 * count + 4]
        ps, pr, pl_sem, ls, lr, ll = refs[2 * count + 4 :]
        place = Place(n_dp, n_line)
        place.meet()
        planes = [
            GatherPlane(place, a, b, ps.at[i], pr.at[i], pl_sem.at[i])
            for i, (a, b) in enumerate(zip(srcs, dsts))
        ]
        rows = c.shape[0]
        span = rows // parts
        lines = [
            GatherLine(place, c_out, rows, i * span, span, ls.at[i], lr.at[i])
            for i in range(parts)
        ]
        lines.append(
            GatherLine(place, e_out, e.shape[0], 0, e.shape[0], ls.at[parts], lr.at[parts])
        )
        for i in range(parts):
            lines[i].step(0, c.at[pl.ds(i * span, span)])
        lines[parts].step(0, e)
        early, late = planes[: count // 2], planes[count // 2 :]
        for part in early:
            part.begin()
        copies = []
        for i, (src, dst) in enumerate(((c, c_out), (e, e_out))):
            own = dst.at[pl.ds(pl.multiple_of(place.t * src.shape[0], 8), src.shape[0])]
            copies.append(pltpu.make_async_copy(src, own, ll.at[i]))
            copies[i].start()
        for line in lines:
            line.step(1)
        for part in late:
            part.begin()
        for part in early:
            part.forward()
        for line in lines:
            line.step(2)
        for part in early:
            part.share()
        for part in late:
            part.forward()
        for part in late:
            part.share()
        for part in lines + planes:
            part.finish()
        for copy in copies:
            copy.wait()

    return pl.pallas_call(
        kernel,
        out_shape=tuple(shaped((n_dp * m.shape[0], m.shape[1]), m.dtype) for m in mats)
        + (
            shaped((n_line * rows_in.shape[0], rows_in.shape[1]), rows_in.dtype),
            shaped((n_line * order.shape[0], order.shape[1]), order.dtype),
        ),
        in_specs=[in_any()] * (count + 2),
        out_specs=[in_any()] * (count + 2),
        scratch_shapes=[
            dma_sems(count, 9),
            dma_sems(count, 9),
            dma_sems(count),
            dma_sems(parts + 1, 2, n_line - 1),
            dma_sems(parts + 1, 2, n_line - 1),
            dma_sems(2),
        ],
        compiler_params=comm_params(1),
        name="first_gather",
    )(*mats, rows_in, order)


CHUNKS = 8


def line_scratch(n_line, span, width):
    hops = n_line - 1
    return [
        pltpu.VMEM((CHUNKS, 2, hops, span, width), jnp.bfloat16),
        pltpu.VMEM((CHUNKS, 2, hops, span, width), jnp.bfloat16),
        dma_sems(CHUNKS, 2, hops),
        dma_sems(CHUNKS, 2, hops),
        dma_sems(CHUNKS, 2, hops),
        dma_sems(CHUNKS, 2, hops),
        pltpu.VMEM((span, width), jnp.float32),
    ]


def sum_rows_and_spread(place, terms, scratch, finish_rows, spread, between):
    stage, inbox, rs, rr, gs, gr, total = scratch
    span = total.shape[0]
    count = stage.shape[0]
    rows = span * count
    hops = place.n_line - 1
    sums = [
        ReduceLine(place, terms, rows, c * span, span, stage.at[c], inbox.at[c], rs.at[c], rr.at[c])
        for c in range(count)
    ]
    gathers = []
    if spread is not None:
        gathers = [
            GatherLine(place, spread, rows, c * span, span, gs.at[c], gr.at[c])
            for c in range(count)
        ]
    sums[0].ends()

    def total_of(c):
        sums[c].total(total)
        finish_rows(c, pl.ds(c * span, span), total)
        if gathers:
            gathers[c].step(0)

    stages = [lambda c, k=k: sums[c].hop(k) for k in range(hops - 1)] + [total_of]
    lags = [LAGS[min(k, len(LAGS) - 1)] for k in range(hops)]
    if gathers:
        stages += [lambda c, k=k: gathers[c].step(k) for k in range(1, hops)]
        lags += [lags[-1] + LAG_STEP * k for k in range(1, hops)]
    for i in range(count + lags[-1]):
        if i < count:
            sums[i].sent()
        if i + 1 < count:
            sums[i + 1].ends()
        for work, lag in zip(stages, lags):
            if 0 <= i - lag < count:
                work(i - lag)
        if i in between:
            between[i]()
    for part in gathers + sums:
        part.finish()


LAGS = (0, 1, 1)
LAG_STEP = 1


def middle_gather(n_dp, n_line, terms, tokens, gain, mats):
    rows, width = tokens.shape
    count = len(mats)

    def kernel(*refs):
        s, tok, gain_ref = refs[:3]
        srcs = refs[3 : 3 + count]
        after, hidden = refs[3 + count : 5 + count]
        dsts = refs[5 + count : 5 + 2 * count]
        ps, pr, pl_sem = refs[5 + 2 * count : 8 + 2 * count]
        scratch = refs[8 + 2 * count :]
        place = Place(n_dp, n_line)
        place.meet()
        planes = [
            GatherPlane(place, a, b, ps.at[i], pr.at[i], pl_sem.at[i])
            for i, (a, b) in enumerate(zip(srcs, dsts))
        ]
        planes[0].begin()

        def norm(c, here, total):
            values = tok[here].astype(jnp.float32) + total[...]
            after[here] = values
            low = rms_scale(values, gain_ref[...]).astype(jnp.bfloat16)
            first = pl.multiple_of(place.t * rows, 16) + c * total.shape[0]
            hidden[pl.ds(pl.multiple_of(first, 16), total.shape[0])] = low

        between = {4: planes[1].begin, 5: planes[0].forward}
        sum_rows_and_spread(place, s, scratch, norm, hidden, between)
        planes[1].forward()
        planes[0].share()
        planes[1].share()
        for part in planes:
            part.finish()

    return pl.pallas_call(
        kernel,
        out_shape=(
            shaped((rows, width), jnp.float32),
            shaped((n_line * rows, width), jnp.bfloat16),
        )
        + tuple(shaped((n_dp * m.shape[0], m.shape[1]), m.dtype) for m in mats),
        in_specs=[in_vmem()] * 3 + [in_any()] * count,
        out_specs=[in_vmem()] * 2 + [in_any()] * count,
        scratch_shapes=[dma_sems(count, 9), dma_sems(count, 9), dma_sems(count)]
        + line_scratch(n_line, rows // CHUNKS, width),
        compiler_params=comm_params(2),
        name="middle_gather",
    )(terms, tokens, gain, *mats)


def middle_sums(n_dp, n_line, terms, after, gain, grad_in, mats):
    rows, width = after.shape
    count = len(mats)
    block = mats[0].shape[0] // n_dp
    per = len(ReducePlane.scratch(16, 128))

    def kernel(*refs):
        s, after_ref, gain_ref, g_ref = refs[:4]
        srcs = refs[4 : 4 + count]
        grad_after, gain_sum, spread = refs[4 + count : 7 + count]
        results = refs[7 + count : 7 + 2 * count]
        rest = refs[7 + 2 * count :]
        scratch = rest[count * per :]
        place = Place(n_dp, n_line)
        place.meet()
        planes = [
            ReducePlane(place, srcs[i], rest[i * per : (i + 1) * per]) for i in range(count)
        ]
        for part in planes:
            part.begin()
        gain_sum[...] = jnp.zeros_like(gain_sum)

        def norm(c, here, total):
            grad = total[...]
            grad_rows, normed = norm_back(after_ref[here], gain_ref[...], grad)
            gain_sum[...] += jnp.sum(grad * normed, axis=0, keepdims=True)
            both = g_ref[here].astype(jnp.float32) + grad_rows
            grad_after[here] = both
            first = pl.multiple_of(place.t * rows, 16) + c * total.shape[0]
            spread[pl.ds(pl.multiple_of(first, 16), total.shape[0])] = both.astype(jnp.bfloat16)

        between = {0: planes[0].cores, 3: planes[1].cores, 5: planes[0].turn}
        sum_rows_and_spread(place, s, scratch, norm, spread, between)
        planes[1].turn()
        for part, result in zip(planes, results):
            part.finish(result)

    return pl.pallas_call(
        kernel,
        out_shape=(
            shaped((rows, width), jnp.float32),
            shaped((1, width), jnp.float32),
            shaped((n_line * rows, width), jnp.bfloat16),
        )
        + tuple(shaped((block, m.shape[1]), jnp.bfloat16) for m in mats),
        in_specs=[in_vmem()] * 4 + [in_any()] * count,
        out_specs=[in_vmem()] * (3 + count),
        scratch_shapes=sum([ReducePlane.scratch(block, m.shape[1]) for m in mats], [])
        + line_scratch(n_line, rows // CHUNKS, width),
        compiler_params=comm_params(3),
        name="middle_sums",
    )(terms, after, gain, grad_in, *mats)


class Exchange:
    def __init__(self, place, axis, src, slots, send, recv, local):
        self.p, self.src, self.slots = place, src, slots
        self.over_dp = axis == "dp"
        self.size = place.n_dp if self.over_dp else place.n_line
        self.me = place.d if self.over_dp else place.t
        self.send, self.recv, self.local = send, recv, local

    def copy(self, i):
        to = lax.rem(self.me + i, self.size)
        device = (to, self.p.t) if self.over_dp else (self.p.d, to)
        return remote(
            self.src, self.slots.at[self.me], self.send.at[i - 1], self.recv.at[i - 1], device
        )

    def mine(self):
        return pltpu.make_async_copy(self.src, self.slots.at[self.me], self.local)

    def begin(self):
        for i in range(1, self.size):
            self.copy(i).start()
        self.mine().start()

    def wait(self):
        self.mine().wait()
        for i in range(1, self.size):
            self.copy(i).wait()

    def finish(self):
        self.wait()
        total = self.slots[0]
        for i in range(1, self.size):
            total = total + self.slots[i]
        return total


def last_sums(n_dp, n_line, terms, tokens, gain, grad_after, small, mats):
    rows, width = tokens.shape
    count = len(mats)
    per = len(ReducePlane.scratch(16, 128))

    def kernel(*refs):
        s, tok, gain_ref, g_ref, small_ref = refs[:5]
        srcs = refs[5 : 5 + count]
        grad_tok, small_out, first_out = refs[5 + count : 8 + count]
        results = refs[8 + count : 8 + 2 * count]
        rest = refs[8 + 2 * count :]
        own_first, row_sum = rest[count * per : count * per + 2]
        slots_a, slots_b, slots_c, slots_d = rest[count * per + 2 : count * per + 6]
        xs, xr, xl = rest[count * per + 6 : count * per + 9]
        scratch = rest[count * per + 9 :]
        place = Place(n_dp, n_line)
        place.meet(True)
        planes = [
            ReducePlane(place, srcs[i], rest[i * per : (i + 1) * per]) for i in range(count)
        ]
        for part in planes:
            part.begin()
        early = Exchange(place, "dp", small_ref, slots_a, xs.at[0], xr.at[0], xl.at[0])
        early.begin()
        own_first[...] = jnp.zeros_like(own_first)

        def norm(c, here, total):
            grad = total[...]
            grad_rows, normed = norm_back(tok[here].astype(jnp.float32), gain_ref[...], grad)
            own_first[...] += jnp.sum(grad * normed, axis=0, keepdims=True)
            grad_tok[here] = g_ref[here] + grad_rows

        def cores():
            for part in planes:
                part.cores()

        def turn():
            for part in planes:
                part.turn()

        sum_rows_and_spread(place, s, scratch, norm, None, {0: cores, 5: turn})
        first = Exchange(place, "dp", own_first, slots_b, xs.at[1], xr.at[1], xl.at[1])
        first.begin()
        small_out[...] = early.finish()
        row_sum[0:1] = small_out[0:1]
        row_sum[1:2] = first.finish()
        both = Exchange(place, "tensor", row_sum, slots_c, xs.at[2], xr.at[2], xl.at[2])
        both.begin()
        for part, result in zip(planes, results):
            part.finish(result)
        first_out[...] = both.finish()

    return pl.pallas_call(
        kernel,
        out_shape=(
            shaped((rows, width), jnp.float32),
            shaped(small.shape, jnp.float32),
            shaped((2, width), jnp.float32),
        )
        + tuple(shaped((m.shape[0] // n_dp, m.shape[1]), jnp.bfloat16) for m in mats),
        in_specs=[in_vmem()] * 5 + [in_any()] * count,
        out_specs=[in_vmem()] * (3 + count),
        scratch_shapes=sum([ReducePlane.scratch(m.shape[0] // n_dp, m.shape[1]) for m in mats], [])
        + [
            pltpu.VMEM((1, width), jnp.float32),
            pltpu.VMEM((2, width), jnp.float32),
            pltpu.VMEM((n_dp,) + small.shape, jnp.float32),
            pltpu.VMEM((n_dp, 1, width), jnp.float32),
            pltpu.VMEM((n_line, 2, width), jnp.float32),
            pltpu.VMEM((1, width), jnp.float32),
            dma_sems(3, n_dp),
            dma_sems(3, n_dp),
            dma_sems(3),
        ]
        + line_scratch(n_line, rows // CHUNKS, width),
        compiler_params=comm_params(4),
        name="last_sums",
    )(terms, tokens, gain, grad_after, small, *mats)


def loop(count, body, unroll=1):
    def step(i, carry):
        body(i)
        return carry

    lax.fori_loop(0, count, step, None, unroll=unroll)


def tile_rows(i, size, ahead=0):
    return pl.ds(pl.multiple_of(i * size + ahead, 8), size)


def moved_up(values, distance, count):
    size = values.shape[0]
    return pltpu.roll(values, (size - distance) % size, 0)[:count]


def take_lanes(ref, here):
    return jnp.concatenate([ref[c, here] for c in range(ref.shape[0])], axis=1)


def put_lanes(ref, here, values):
    for c in range(ref.shape[0]):
        ref[c, here] = values[:, c * LANES : (c + 1) * LANES]


def gelu_parts(values):
    inner = GELU_C * (values + 0.044715 * (values * values * values))
    tanh = jnp.tanh(inner)
    half = 0.5 * (1.0 + tanh)
    slope = half + 0.5 * values * (1.0 - tanh * tanh) * GELU_C * (
        1.0 + 3.0 * 0.044715 * (values * values)
    )
    return values * half, slope


GELU_C = 0.7978845608028654
RIM = 128
LANES = 128
TILE = 16


def one_minus_exp(values, exponential):
    series = jnp.ones_like(values)
    for term in range(9, 1, -1):
        series = 1.0 + values * (1.0 / term) * series
    return jnp.where(values > -0.35, -values * series, 1.0 - exponential)


def rate_and_scale(pre_recur, soft, start):
    sr = jax.nn.sigmoid(pre_recur)
    log_rate = -rate_scale * sr * soft
    decay = jnp.exp(log_rate)
    rate = jnp.where(start, 0.0, decay)
    scale = jnp.where(start, 1.0, jnp.sqrt(one_minus_exp(2.0 * log_rate, decay * decay)))
    return sr, rate, scale


class RimSwap:
    def __init__(self, place, own):
        self.odd = lax.rem(place.t, 2)
        self.partner = (place.d, place.t + 1 - 2 * self.odd)
        self.first = pl.multiple_of(RIM - RIM * self.odd, RIM)
        self.edge = pl.ds(pl.multiple_of((1 - self.odd) * own + self.odd * RIM, RIM), RIM)
        self.over_there = pl.ds(pl.multiple_of(self.odd * (own + RIM), RIM), RIM)
        self.beyond = pl.ds(pl.multiple_of((1 - self.odd) * (own + RIM), RIM), RIM)

    def block(self, index, size):
        return pl.ds(pl.multiple_of(self.first + index * size, RIM), size)


def recur_forward(
    n_dp,
    n_line,
    tok_all,
    cot,
    to_place,
    to_stored,
    x_full,
    y_full,
    out_full,
    gain,
    gates,
    taps,
    soft,
    flags,
):
    rows, width = tok_all.shape
    count, own = taps.shape
    size = gates.shape[0]
    wide = own + 2 * RIM
    blocks = (wide - RIM) // size
    chunk = rows // 8
    cot_rows = cot.shape[0]
    parts = 1

    def kernel(*refs):
        (tok, cot_ref, plc, sto, wx, wy, wo, gain_ref, gw, cw, sp, fl) = refs[:12]
        (hp, xext, y, conv_low, conv, pre_r, pre_i, rate, state, merged_st, terms, cot_all) = refs[
            12:24
        ]
        (h, xf, local, cum, merged, agg, slots, hs, hr, es, er, el, gs, gr, gl) = refs[24:]
        place = Place(n_dp, n_line)
        place.meet(True)
        swap = RimSwap(place, own)
        own_cot = cot_all.at[pl.ds(pl.multiple_of(place.t * cot_rows, 16), cot_rows)]
        keep = pltpu.make_async_copy(cot_ref, own_cot, gl)
        keep.start()
        span = cot_rows // parts
        lines = [
            GatherLine(place, cot_all, cot_rows, c * span, span, gs.at[c], gr.at[c])
            for c in range(parts)
        ]
        for c, line in enumerate(lines):
            line.step(0, cot_ref.at[pl.ds(c * span, span)])

        def norm(i):
            here = tile_rows(i, TILE)
            h[here] = rms_scale(tok[here].astype(jnp.float32), gain_ref[...]).astype(jnp.bfloat16)

        loop(rows // TILE, norm)

        def project(i):
            here = tile_rows(i, 128)
            hp[here] = plain_dot(plc[here], h[...]).astype(jnp.bfloat16)
            xext[tile_rows(i, 128, 16)] = plain_dot(hp[here], wx[...]).astype(jnp.bfloat16)

        loop(rows // 128, project)
        edge = remote(
            xext.at[pl.ds(rows, 16)],
            xext.at[pl.ds(0, 16)],
            hs.at[0],
            hr.at[0],
            (lax.rem(place.d + 1, n_dp), place.t),
        )
        edge.start()
        for line in lines:
            line.step(1)

        def project_y(i):
            here = tile_rows(i, 128)
            y[here] = plain_dot(hp[here], wy[...])

        loop(rows // 128, project_y)
        edge.wait()
        top = xext[pl.ds(0, 16)]
        xext[pl.ds(0, 16)] = jnp.where(place.d > 0, top, jnp.zeros_like(top))

        def widen(i):
            xf[tile_rows(i, TILE)] = xext[tile_rows(i, TILE)].astype(jnp.float32)

        loop(rows // TILE + 1, widen)

        def convolve(i):
            here = tile_rows(i, TILE)
            near = xf[pl.ds(pl.multiple_of(i * TILE + 8, 8), TILE + 8)]
            same = fl[tile_rows(i, TILE, 8)]
            total = cw[0:1] * near[8:]
            for k in range(1, count):
                total += cw[k : k + 1] * moved_up(near, 8 - k, TILE) * same[:, k : k + 1]
            conv[here] = total
            conv_low[here, RIM : RIM + own] = total.astype(jnp.bfloat16)

        loop(rows // TILE, convolve)
        rim = remote(
            conv_low.at[:, swap.edge],
            conv_low.at[:, swap.over_there],
            hs.at[1],
            hr.at[1],
            swap.partner,
        )
        rim.start()
        for i in range(blocks):
            index = lax.rem(i + swap.odd, blocks)
            cols = swap.block(index, size)
            other = pl.ds(pl.multiple_of(wide + swap.first + index * size, RIM), size)
            if i == blocks - 1:
                rim.wait()
            pre_r[:, cols] = plain_dot(conv_low[:, cols], gw[:, cols])
            pre_i[:, cols] = plain_dot(conv_low[:, cols], gw[:, other])

        def drive(i):
            here = tile_rows(i, TILE)
            start = fl[tile_rows(i, TILE, 8)][:, 0:1] > 0.0
            own_cols = pl.ds(RIM, own)
            _, decay, scale = rate_and_scale(pre_r[here, own_cols], sp[...], start)
            put_lanes(rate, here, decay)
            put_lanes(local, here, conv[here] * jax.nn.sigmoid(pre_i[here, own_cols]) * scale)

        loop(rows // TILE, drive)
        for line in lines:
            line.step(2)
        groups = own // LANES

        def scan(i, carry):
            here = pl.ds(i, 8, chunk)
            result = []
            for c in range(groups):
                product, total = carry[c]
                r = rate[c, here]
                product = product * r
                total = total * r + local[c, here]
                cum[c, here] = product
                local[c, here] = total
                result.append((product, total))
            return tuple(result)

        blank = (jnp.ones((8, LANES), jnp.float32), jnp.zeros((8, LANES), jnp.float32))
        lax.fori_loop(0, chunk, scan, (blank,) * groups)
        product, total = jnp.ones((1, own), jnp.float32), jnp.zeros((1, own), jnp.float32)
        for j in range(8):
            last = pl.ds(j * chunk + chunk - 1, 1)
            total = take_lanes(local, last) + take_lanes(cum, last) * total
            product = product * take_lanes(cum, last)
        agg[0:1] = product
        agg[1:2] = total
        swap_all = Exchange(place, "dp", agg, slots, es, er, el)
        swap_all.begin()
        swap_all.wait()
        entry = jnp.zeros((1, own), jnp.float32)
        for q in range(n_dp):
            longer = slots[q, 1:2] + slots[q, 0:1] * entry
            entry = jnp.where(q < place.d, longer, entry)
        state[pl.ds(0, 8)] = jnp.broadcast_to(entry, (8, own))
        for j in range(8):

            def settle(i, entry=entry):
                here = tile_rows(i, TILE, j * chunk)
                values = take_lanes(local, here) + take_lanes(cum, here) * entry
                state[tile_rows(i, TILE, j * chunk + 8)] = values
                merged[here] = (values * gelu_parts(y[here])[0]).astype(jnp.bfloat16)

            loop(chunk // TILE, settle)
            last = pl.ds(j * chunk + chunk - 1, 1)
            entry = take_lanes(local, last) + take_lanes(cum, last) * entry
        merged_st[...] = plain_dot(sto[...], merged[...]).astype(jnp.bfloat16)

        def mix(i):
            some = tile_rows(i, 512)
            terms[:, pl.ds(pl.multiple_of(i * 512, 512), 512)] = times_trans(
                merged_st[...], wo[some, :]
            ).astype(jnp.bfloat16)

        loop(width // 512, mix)
        for line in lines:
            line.finish()
        keep.wait()

    low, full = jnp.bfloat16, jnp.float32
    return pl.pallas_call(
        kernel,
        out_shape=(
            shaped((rows, width), low),
            shaped((rows + 16, own), low),
            shaped((rows, own), full),
            shaped((rows, wide), low),
            shaped((rows, own), full),
            shaped((rows, wide), full),
            shaped((rows, wide), full),
            shaped((own // LANES, rows, LANES), full),
            shaped((rows + 8, own), full),
            shaped((rows, own), low),
            shaped((rows, width), low),
            shaped((n_line * cot_rows, width), low),
        ),
        in_specs=[in_vmem(), in_any()] + [in_vmem()] * 10,
        out_specs=[in_vmem()] * 11 + [in_any()],
        scratch_shapes=[
            pltpu.VMEM((rows, width), low),
            pltpu.VMEM((rows + 16, own), full),
            pltpu.VMEM((own // LANES, rows, LANES), full),
            pltpu.VMEM((own // LANES, rows, LANES), full),
            pltpu.VMEM((rows, own), low),
            pltpu.VMEM((2, own), full),
            pltpu.VMEM((n_dp, 2, own), full),
            dma_sems(2),
            dma_sems(2),
            dma_sems(n_dp),
            dma_sems(n_dp),
            pltpu.SemaphoreType.DMA,
            dma_sems(parts, 2, n_line - 1),
            dma_sems(parts, 2, n_line - 1),
            pltpu.SemaphoreType.DMA,
        ],
        compiler_params=comm_params(5),
        name="recur_forward",
    )(
        tok_all,
        cot,
        to_place,
        to_stored,
        x_full,
        y_full,
        out_full,
        gain,
        gates,
        taps,
        soft,
        flags,
    )


def recur_backward(
    n_dp,
    n_line,
    mixer_in,
    to_place,
    to_stored,
    x_full,
    y_full,
    out_full,
    gates,
    taps,
    soft,
    slope,
    flags,
    kept,
):
    rows, width = mixer_in.shape
    count, own = taps.shape
    size = gates.shape[0]
    wide = own + 2 * RIM
    blocks = (wide - RIM) // size
    chunk = rows // 8

    def kernel(*refs):
        (mix, plc, sto, wx, wy, wo, gw, cw, sp, sg, fl) = refs[:11]
        (xext, y, conv_low, conv, pre_r, pre_i, rate, state) = refs[11:19]
        (gxy, gate_grads, tap_grads, decay_grad, terms) = refs[19:24]
        (mp, gm, lam, reach, gp_r, gp_i, grad, spread, rim_out, rim_in, ret_out, ret_in) = refs[
            24:36
        ]
        (tap_sums, decay_sums, ends, agg, slots, hs, hr, es, er, el) = refs[36:]
        place = Place(n_dp, n_line)
        place.meet(True)
        swap = RimSwap(place, own)
        own_cols = pl.ds(RIM, own)

        def project(i):
            here = tile_rows(i, 128)
            mp[here] = plain_dot(plc[here], mix[...]).astype(jnp.bfloat16)
            gm[here] = plain_dot(mp[here], wo[...])

        loop(rows // 128, project)

        def split(i):
            here = tile_rows(i, TILE)
            branch, slope_y = gelu_parts(y[here])
            grads = gm[here]
            put_lanes(lam, here, grads * branch)
            values = state[tile_rows(i, TILE, 8)]
            gxy[here, own:] = (grads * values * slope_y).astype(jnp.bfloat16)

        loop(rows // TILE, split)
        groups = own // LANES

        def scan(i, carry):
            here = pl.ds(chunk - 1 - i, 8, chunk)
            result = []
            for c in range(groups):
                product, message = carry[c]
                r = rate[c, here]
                value = lam[c, here] + message
                lam[c, here] = value
                reach[c, here] = product
                result.append((product * r, value * r))
            return tuple(result)

        blank = (jnp.ones((8, LANES), jnp.float32), jnp.zeros((8, LANES), jnp.float32))
        done = lax.fori_loop(0, chunk, scan, (blank,) * groups)
        for c in range(groups):
            lanes = pl.ds(c * LANES, LANES)
            ends[0, :, lanes] = done[c][0]
            ends[1, :, lanes] = done[c][1]
        product, message = jnp.ones((1, own), jnp.float32), jnp.zeros((1, own), jnp.float32)
        for j in reversed(range(8)):
            message = ends[1, j : j + 1] + ends[0, j : j + 1] * message
            product = product * ends[0, j : j + 1]
        agg[0:1] = product
        agg[1:2] = message
        swap_all = Exchange(place, "dp", agg, slots, es, er, el)
        swap_all.begin()
        swap_all.wait()
        entry = jnp.zeros((1, own), jnp.float32)
        for q in reversed(range(n_dp)):
            longer = slots[q, 1:2] + slots[q, 0:1] * entry
            entry = jnp.where(q > place.d, longer, entry)
        for ref in (tap_sums, decay_sums):
            ref[...] = jnp.zeros_like(ref)
        for ref in (gp_r, gp_i):
            ref[:, 0:RIM] = jnp.zeros((rows, RIM), jnp.bfloat16)
            ref[:, RIM + own :] = jnp.zeros((rows, RIM), jnp.bfloat16)
        grad[pl.ds(0, 8)] = jnp.zeros((8, own), jnp.float32)
        grad[pl.ds(rows + 8, 8)] = jnp.zeros((8, own), jnp.float32)
        for j in reversed(range(8)):

            def back(i, entry=entry):
                here = tile_rows(i, TILE, j * chunk)
                flag = fl[tile_rows(i, TILE, j * chunk + 8)]
                start = flag[:, 0:1] > 0.0
                values = take_lanes(lam, here) + take_lanes(reach, here) * entry
                before = moved_up(
                    state[pl.ds(pl.multiple_of(j * chunk + i * TILE, 8), TILE + 8)], 7, TILE
                )
                sr, decay, scale = rate_and_scale(pre_r[here, own_cols], sp[...], start)
                si = jax.nn.sigmoid(pre_i[here, own_cols])
                block = conv[here]
                driven = values * si
                log_grad = values * before * decay - block * driven * (decay * decay) / scale
                log_grad = jnp.where(start, 0.0, log_grad)
                inner = sr * log_grad
                gp_r[here, own_cols] = (
                    -rate_scale * sp[...] * inner * (1.0 - sr)
                ).astype(jnp.bfloat16)
                gp_i[here, own_cols] = (driven * block * (1.0 - si) * scale).astype(jnp.bfloat16)
                grad[tile_rows(i, TILE, j * chunk + 8)] = driven * scale
                decay_sums[...] += inner[:8] + inner[8:]

            loop(chunk // TILE, back)
            entry = ends[1, j : j + 1] + ends[0, j : j + 1] * entry
        decay_grad[...] = rate_scale * sg[...] * jnp.sum(decay_sums[...], axis=0, keepdims=True)

        for i in range(blocks):
            index = lax.rem(i + 2 - 2 * swap.odd, blocks)
            cols = swap.block(index, size)
            other = pl.ds(pl.multiple_of(wide + swap.first + index * size, RIM), size)
            spread[:, cols] = times_trans(gp_r[:, cols], gw[:, cols]) + times_trans(
                gp_i[:, cols], gw[:, other]
            )
            if i == 0:
                rim_out[...] = spread[:, swap.beyond].astype(jnp.bfloat16)
                rim = remote(rim_out, rim_in, hs.at[0], hr.at[0], swap.partner)
                rim.start()
        rim.wait()
        shared = pl.ds(pl.multiple_of((1 - swap.odd) * (own - RIM), RIM), RIM)

        def join(i):
            here = tile_rows(i, TILE)
            there = tile_rows(i, TILE, 8)
            grad[there] += spread[here, own_cols]
            grad[there, shared] += rim_in[here].astype(jnp.float32)

        loop(rows // TILE, join)

        near = grad[pl.ds(0, 16)]
        back_rows = jnp.zeros((8, own), jnp.float32)
        for k in range(1, count):
            masked = near * fl[pl.ds(0, 16)][:, k : k + 1]
            back_rows += cw[k : k + 1] * moved_up(masked, k, 8)
        ret_out[...] = back_rows
        ret = remote(
            ret_out,
            ret_in,
            hs.at[1],
            hr.at[1],
            (lax.rem(place.d + n_dp - 1, n_dp), place.t),
        )
        ret.start()
        for i in range(blocks):
            cols = swap.block(i, size)
            spread[0:size, cols] = trans_times(conv_low[:, cols], gp_r[:, cols])
            spread[size : 2 * size, cols] = trans_times(conv_low[:, cols], gp_i[:, cols])
        gate_grads[:, 0:own] = spread[0:size, own_cols].astype(jnp.bfloat16)
        gate_grads[:, own:] = spread[size : 2 * size, own_cols].astype(jnp.bfloat16)

        def taps_back(i, added=None):
            here = tile_rows(i, TILE)
            start = pl.ds(pl.multiple_of(i * TILE + 8, 8), TILE + 8)
            after = grad[start]
            flag = fl[start]
            behind = xext[pl.ds(pl.multiple_of(i * TILE, 16), 2 * TILE)].astype(jnp.float32)
            total = cw[0:1] * after[:TILE]
            for k in range(count):
                if k > 0:
                    masked = after * flag[:, k : k + 1]
                    total += cw[k : k + 1] * moved_up(masked, k, TILE)
                    mine = masked[:TILE]
                else:
                    mine = after[:TILE]
                term = mine * moved_up(behind, 16 - k, TILE)
                tap_sums[k] += term[:8] + term[8:]
            if added is not None:
                total = total + jnp.concatenate([jnp.zeros((8, own), jnp.float32), added], axis=0)
            gxy[here, 0:own] = total.astype(jnp.bfloat16)

        loop(rows // TILE - 1, taps_back)
        ret.wait()
        taps_back(rows // TILE - 1, jnp.where(place.d < n_dp - 1, ret_in[...], 0.0))
        tap_grads[...] = jnp.zeros_like(tap_grads)
        for k in range(count):
            tap_grads[k : k + 1] = jnp.sum(tap_sums[k], axis=0, keepdims=True)

        def restore(i):
            here = tile_rows(i, 128)
            mp[here, 0 : 2 * own] = plain_dot(sto[here], gxy[...]).astype(jnp.bfloat16)

        loop(rows // 128, restore)

        def spread_back(i):
            some = tile_rows(i, 512)
            terms[:, pl.ds(pl.multiple_of(i * 512, 512), 512)] = (
                times_trans(mp[:, 0:own], wx[some]) + times_trans(mp[:, own : 2 * own], wy[some])
            ).astype(jnp.bfloat16)

        loop(width // 512, spread_back)

    low, full = jnp.bfloat16, jnp.float32
    return pl.pallas_call(
        kernel,
        out_shape=(
            shaped((rows, 2 * own), low),
            shaped((size, 2 * own), low),
            shaped((8, own), full),
            shaped((1, own), full),
            shaped((rows, width), low),
        ),
        in_specs=[in_vmem()] * 19,
        out_specs=[in_vmem()] * 5,
        scratch_shapes=[
            pltpu.VMEM((rows, width), low),
            pltpu.VMEM((rows, own), full),
            pltpu.VMEM((own // LANES, rows, LANES), full),
            pltpu.VMEM((own // LANES, rows, LANES), full),
            pltpu.VMEM((rows, wide), low),
            pltpu.VMEM((rows, wide), low),
            pltpu.VMEM((rows + 16, own), full),
            pltpu.VMEM((rows, wide), full),
            pltpu.VMEM((rows, RIM), low),
            pltpu.VMEM((rows, RIM), low),
            pltpu.VMEM((8, own), full),
            pltpu.VMEM((8, own), full),
            pltpu.VMEM((count, 8, own), full),
            pltpu.VMEM((8, own), full),
            pltpu.VMEM((2, 8, own), full),
            pltpu.VMEM((2, own), full),
            pltpu.VMEM((n_dp, 2, own), full),
            dma_sems(2),
            dma_sems(2),
            dma_sems(n_dp),
            dma_sems(n_dp),
            pltpu.SemaphoreType.DMA,
        ],
        compiler_params=comm_params(6),
        name="recur_backward",
    )(
        mixer_in,
        to_place,
        to_stored,
        x_full,
        y_full,
        out_full,
        gates,
        taps,
        soft,
        slope,
        flags,
        *kept,
    )


def matches(mesh):
    return mesh.shape["dp"] == 8 and mesh.shape["tensor"] == 4


def local_blocks(
    tokens,
    norm_gain,
    x_weight,
    y_weight,
    conv_weight,
    recur_gate_weight,
    input_gate_weight,
    decay_param,
    out_weight,
    mlp_gain,
    gate_weight,
    up_weight,
    down_weight,
    seq_lengths,
    token_order,
    cotangent,
):
    n_dp, n_tensor = lax.axis_size("dp"), lax.axis_size("tensor")
    tensor_index = lax.axis_index("tensor")
    dp_index = lax.axis_index("dp")
    tok_rows, width = tokens.shape
    row_count = tok_rows * n_tensor
    own_width = conv_weight.shape[1]
    kernel_taps = conv_weight.shape[0]
    edge_rows = kernel_taps - 1
    dp_width = norm_gain.shape[0]
    gate_rows = recur_gate_weight.shape[0]
    own_start = tensor_index * tok_rows

    gains = jnp.concatenate([norm_gain, mlp_gain])
    spare = gate_rows * 128 - gains.shape[0]
    gains = jnp.pad(gains, (0, spare)).reshape(gate_rows, 128)
    minor = jnp.concatenate([recur_gate_weight, input_gate_weight, gains], axis=1)
    own_order = (token_order - dp_index * row_count).astype(jnp.int32)
    order_rows = jnp.broadcast_to(own_order[None, :], (8, tok_rows))
    x_full, y_full, out_full, minor_full, tok_all, order_full = first_gather(
        n_dp, n_tensor, (x_weight, y_weight, out_weight.T, minor), tokens, order_rows
    )
    down_full = lax.all_gather(
        lax.optimization_barrier((down_weight.T, tok_all))[0], "dp", axis=0, tiled=True
    )
    order_all = order_full.reshape(n_tensor, 8, tok_rows)[:, 0].reshape(row_count)
    both_gates = minor_full[:, : 2 * own_width]
    gain_rows = minor_full[:, 2 * own_width :].reshape(n_dp, -1)
    first_gain = gain_rows[:, :dp_width].reshape(1, width).astype(jnp.float32)
    second_gain = gain_rows[:, dp_width : 2 * dp_width].reshape(1, width).astype(jnp.float32)
    block_size = both_gates.shape[0]
    row_index = jnp.arange(row_count, dtype=jnp.int32)
    hits = row_index[:, None] == order_all[None, :]
    to_place = hits.astype(jnp.bfloat16)
    to_stored = (order_all[:, None] == row_index[None, :]).astype(jnp.bfloat16)
    places = dp_index * row_count + jnp.arange(-8, row_count + 8, dtype=jnp.int32)
    inside = (jnp.arange(row_count + 16) >= 8) & (jnp.arange(row_count + 16) < row_count + 8)
    ends = jnp.cumsum(seq_lengths)
    segment = segment_of(places, ends)
    starts = (places == 0) | (segment != segment_of(places - 1, ends))
    columns = [starts] + [
        segment_of(places - shift, ends) == segment for shift in range(1, kernel_taps)
    ]
    columns += [jnp.zeros_like(starts)] * (8 - len(columns))
    flags = (jnp.stack(columns, axis=1) & inside[:, None]).astype(jnp.float32)
    live_stored = (order_all + dp_index * row_count < ends[-1]).astype(jnp.float32)
    live_own = (token_order < ends[-1]).astype(jnp.float32)
    soft = jax.nn.softplus(-decay_param).reshape(1, own_width)
    slope = jax.nn.sigmoid(-decay_param).reshape(1, own_width)
    zero_rim = jnp.zeros((block_size, RIM), jnp.bfloat16)
    gates_wide = jnp.concatenate(
        [
            zero_rim,
            both_gates[:, :own_width],
            zero_rim,
            zero_rim,
            both_gates[:, own_width:],
            zero_rim,
        ],
        axis=1,
    )
    def glu(gate_pre, up_pre):
        return gelu_tanh(gate_pre) * up_pre

    hidden_place, *kept, merged_stored, mixer_terms, cot_all = recur_forward(
        n_dp,
        n_tensor,
        tok_all,
        cotangent,
        to_place,
        to_stored,
        x_full,
        y_full,
        out_full,
        first_gain,
        gates_wide,
        conv_weight,
        soft,
        flags,
    )
    after_own, hidden_two, gate_full, up_full = middle_gather(
        n_dp, n_tensor, mixer_terms, tokens, second_gain, (gate_weight, up_weight)
    )
    gate_pre = plain_dot(hidden_two, gate_full)
    up_pre = plain_dot(hidden_two, up_full)
    glu_out, glu_pull = jax.vjp(glu, gate_pre, up_pre)
    product = glu_out.astype(jnp.bfloat16)
    down_in = (cot_all.astype(jnp.float32) * live_stored[:, None]).astype(jnp.bfloat16)
    grad_in_own = (cotangent.astype(jnp.float32) * live_own[:, None]).astype(jnp.bfloat16)
    grad_down = trans_times(down_in, product).astype(jnp.bfloat16)
    down_sum = lax.psum_scatter(grad_down, "dp", scatter_dimension=0, tiled=True)
    down_in, _ = lax.optimization_barrier((down_in, grad_down))
    grad_product = plain_dot(down_in, down_full)
    grad_gate_pre, grad_up_pre = glu_pull(grad_product)
    grad_gate_pre = grad_gate_pre.astype(jnp.bfloat16)
    grad_up_pre = grad_up_pre.astype(jnp.bfloat16)
    grad_gate = trans_times(hidden_two, grad_gate_pre).astype(jnp.bfloat16)
    grad_up = trans_times(hidden_two, grad_up_pre).astype(jnp.bfloat16)
    back_terms = (
        times_trans(grad_gate_pre, gate_full) + times_trans(grad_up_pre, up_full)
    ).astype(jnp.bfloat16)
    feed_terms = times_trans(product, down_full).astype(jnp.bfloat16)
    grad_after_own, second_part, mixer_in, gate_sum, up_sum = middle_sums(
        n_dp, n_tensor, back_terms, after_own, second_gain, grad_in_own, (grad_gate, grad_up)
    )
    feed_out = lax.psum_scatter(
        lax.optimization_barrier((feed_terms, mixer_in))[0],
        "tensor",
        scatter_dimension=0,
        tiled=True,
    ).astype(jnp.float32)
    output = ((after_own + feed_out) * live_own[:, None]).astype(jnp.bfloat16)

    grad_xy, gate_grads, tap_grads, decay_grad, one_terms = recur_backward(
        n_dp,
        n_tensor,
        mixer_in,
        to_place,
        to_stored,
        x_full,
        y_full,
        out_full,
        gates_wide,
        conv_weight,
        soft,
        slope,
        flags,
        kept,
    )
    grad_out_mat = trans_times(mixer_in, merged_stored).astype(jnp.bfloat16)
    grad_xy_mat = trans_times(hidden_place, grad_xy).astype(jnp.bfloat16)
    small = jnp.concatenate(
        [
            second_part,
            tap_grads[:kernel_taps].reshape(1, -1),
            jnp.pad(decay_grad, ((0, 0), (0, width - own_width))),
            jnp.zeros((1, width), jnp.float32),
        ],
        axis=0,
    )
    grad_tokens, small_sum, gain_sums, xy_sum, out_sum, gates_sum = last_sums(
        n_dp,
        n_tensor,
        one_terms,
        tokens,
        first_gain,
        grad_after_own,
        small,
        (grad_xy_mat, grad_out_mat, gate_grads),
    )
    xy_sum, gates_sum = xy_sum.astype(jnp.float32), gates_sum.astype(jnp.float32)
    own_gains = lax.dynamic_slice_in_dim(gain_sums, dp_index * dp_width, dp_width, 1)
    return (
        output,
        grad_tokens,
        own_gains[1],
        xy_sum[:, :own_width],
        xy_sum[:, own_width:],
        small_sum[1].reshape(kernel_taps, own_width),
        gates_sum[:, :own_width],
        gates_sum[:, own_width:],
        small_sum[2, :own_width],
        out_sum.astype(jnp.float32).T,
        own_gains[0],
        gate_sum.astype(jnp.float32),
        up_sum.astype(jnp.float32),
        down_sum.astype(jnp.float32).T,
    )


def solution(mesh):
    in_specs = (
        P(("dp", "tensor"), None),
        P("dp"),
        P("dp", "tensor"),
        P("dp", "tensor"),
        P(None, "tensor"),
        P("dp", "tensor"),
        P("dp", "tensor"),
        P("tensor"),
        P("tensor", "dp"),
        P("dp"),
        P("dp", "tensor"),
        P("dp", "tensor"),
        P("tensor", "dp"),
        P(),
        P(("dp", "tensor")),
        P(("dp", "tensor"), None),
    )
    out_specs = (
        P(("dp", "tensor"), None),
        P(("dp", "tensor"), None),
        P("dp"),
        P("dp", "tensor"),
        P("dp", "tensor"),
        P(None, "tensor"),
        P("dp", "tensor"),
        P("dp", "tensor"),
        P("tensor"),
        P("tensor", "dp"),
        P("dp"),
        P("dp", "tensor"),
        P("dp", "tensor"),
        P("tensor", "dp"),
    )
    fits = matches(mesh)
    local = local_blocks if fits else local_general
    return jax.shard_map(local, mesh=mesh, in_specs=in_specs, out_specs=out_specs, check_vma=False)
```

```python
import jax
import jax.numpy as jnp
from jax import lax
from jax.experimental import pallas as pl
from jax.experimental.pallas import tpu as pltpu
from jax.sharding import PartitionSpec as P

epsilon = 1e-06
rate_scale = 8.0


def from_behind(block, axis, distance):
    devices = range(lax.axis_size(axis))
    route = [(i - distance, i) for i in devices if i - distance in devices]
    return lax.ppermute(block, axis, route)


def extended_2(array, sides, width):
    for axis, dim in sides:
        size, length = (lax.axis_size(axis), array.shape[dim])
        up = [(i, (i + 1) % size) for i in range(size - 1)]
        down = [(j, i) for i, j in up]
        last = lax.slice_in_dim(array, length - width, length, axis=dim)
        leading = lax.slice_in_dim(array, 0, width, axis=dim)
        before = lax.ppermute(last, axis, up)
        after = lax.ppermute(leading, axis, down)
        array = jnp.concatenate([before, array, after], axis=dim)
    return array


def entering(value, axis, join, neutral, backward):
    count, mine = (lax.axis_size(axis), lax.axis_index(axis))
    pieces = jax.tree.map(lambda part: lax.all_gather(part, axis), value)
    if backward:
        pieces = jax.tree.map(lambda part: part[::-1], pieces)
        mine = count - 1 - mine
    total = jax.tree.map(
        lambda part, zero: jnp.full_like(part, 0) + jnp.asarray(zero, part.dtype), value, neutral
    )

    def lap(position, total):
        longer = join(total, jax.tree.map(lambda part: part[position], pieces))
        return jax.tree.map(lambda new, old: jnp.where(position < mine, new, old), longer, total)

    return lax.fori_loop(0, count - 1, lap, total)


def rms_scale(values, gain):
    return values * lax.rsqrt(jnp.mean(values * values, axis=-1, keepdims=True) + epsilon) * gain


def norm_back(values, gain, grad):
    inv_root = lax.rsqrt(jnp.mean(values * values, axis=-1, keepdims=True) + epsilon)
    normed = values * inv_root
    upstream = grad * gain
    grad_values = inv_root * (
        upstream - normed * jnp.mean(upstream * normed, axis=-1, keepdims=True)
    )
    return (grad_values, normed)


def segment_of(places, ends):
    return jnp.sum((ends[None, :] <= places[:, None]).astype(jnp.int32), axis=1)


def pair_step(early, later):
    return (early[0] * later[0], later[0] * early[1] + later[1])


def plain_dot(left, right):
    return jnp.dot(left, right, preferred_element_type=jnp.float32)


def times_trans(left, right):
    return lax.dot_general(
        left, right, (((1,), (1,)), ((), ())), preferred_element_type=jnp.float32
    )


def trans_times(left, right):
    return lax.dot_general(
        left, right, (((0,), (0,)), ((), ())), preferred_element_type=jnp.float32
    )


def gelu_tanh(values):
    return jax.nn.gelu(values, approximate=True)


def collect(
    norm_gain,
    mlp_gain,
    x_weight,
    y_weight,
    recur_gate_weight,
    input_gate_weight,
    gate_weight,
    up_weight,
    out_weight,
    down_weight,
):
    return (
        lax.all_gather(norm_gain, "dp", axis=0, tiled=True),
        lax.all_gather(mlp_gain, "dp", axis=0, tiled=True),
        lax.all_gather(x_weight, "dp", axis=0, tiled=True),
        lax.all_gather(y_weight, "dp", axis=0, tiled=True),
        lax.all_gather(recur_gate_weight, "dp", axis=0, tiled=True),
        lax.all_gather(input_gate_weight, "dp", axis=0, tiled=True),
        lax.all_gather(gate_weight, "dp", axis=0, tiled=True),
        lax.all_gather(up_weight, "dp", axis=0, tiled=True),
        lax.all_gather(out_weight, "dp", axis=1, tiled=True),
        lax.all_gather(down_weight, "dp", axis=1, tiled=True),
    )


def row_sums(term_rows, tok_rows):
    return lax.psum_scatter(
        term_rows(jnp.int32(0), lax.axis_size("tensor") * tok_rows).astype(jnp.bfloat16),
        "tensor",
        scatter_dimension=0,
        tiled=True,
    ).astype(jnp.float32)


def spread_rows(values):
    return lax.all_gather(values, "tensor", axis=0, tiled=True)


def local_general(
    tokens,
    norm_gain,
    x_weight,
    y_weight,
    conv_weight,
    recur_gate_weight,
    input_gate_weight,
    decay_param,
    out_weight,
    mlp_gain,
    gate_weight,
    up_weight,
    down_weight,
    seq_lengths,
    token_order,
    cotangent,
):
    n_tensor = lax.axis_size("tensor")
    tensor_index = lax.axis_index("tensor")
    dp_index = lax.axis_index("dp")
    tok_rows = tokens.shape[0]
    row_count = tok_rows * n_tensor
    own_width = conv_weight.shape[1]
    kernel_taps = conv_weight.shape[0]
    edge_rows = kernel_taps - 1
    dp_width = norm_gain.shape[0]
    own_start = tensor_index * tok_rows
    shards = (
        norm_gain,
        mlp_gain,
        x_weight,
        y_weight,
        recur_gate_weight,
        input_gate_weight,
        gate_weight,
        up_weight,
        out_weight,
        down_weight,
    )
    (
        gain_one,
        gain_two,
        x_full,
        y_full,
        recur_full,
        input_full,
        gate_full,
        up_full,
        out_full,
        down_full,
    ) = collect(*shards)
    block_size = recur_full.shape[0]
    first_gain = gain_one.astype(jnp.float32)
    second_gain = gain_two.astype(jnp.float32)
    both_gates = jnp.concatenate([recur_full, input_full], axis=1)
    tok_own = tokens.astype(jnp.float32)
    own_order = token_order - dp_index * row_count
    first_rows = rms_scale(tok_own, first_gain).astype(jnp.bfloat16)
    first_all, cot_all, order_all = (
        lax.all_gather(first_rows, "tensor", axis=0, tiled=True),
        lax.all_gather(cotangent, "tensor", axis=0, tiled=True),
        lax.all_gather(own_order, "tensor", axis=0, tiled=True),
    )
    row_index = jnp.arange(row_count, dtype=jnp.int32)
    inverse = jnp.zeros((row_count,), jnp.int32).at[order_all].set(row_index)
    hidden_place = jnp.take(first_all, inverse, axis=0)
    places = dp_index * row_count + row_index
    ends = jnp.cumsum(seq_lengths)
    segment = segment_of(places, ends)
    starts = (places == 0) | (segment != segment_of(places - 1, ends))
    live = (places < ends[-1]).astype(jnp.float32)
    live_stored = jnp.take(live, order_all, axis=0)
    same = [
        (segment_of(places - shift, ends) == segment).astype(jnp.float32)
        for shift in range(kernel_taps)
    ]
    low_edge = tensor_index * own_width
    own_blocks = (low_edge + jnp.arange(own_width, dtype=jnp.int32)) // block_size
    first_block = low_edge // block_size
    block_count = own_width // block_size + 2

    def block_start(index):
        return (first_block + index) * block_size - low_edge + block_size

    def block_mask(index):
        inside = own_blocks == first_block + index
        return jnp.concatenate([inside, inside])

    def convolve(extended, kernel):
        return sum(
            (
                kernel[shift][None, :]
                * extended[edge_rows - shift : edge_rows - shift + row_count]
                * same[shift][:, None]
                for shift in range(kernel_taps)
            )
        )

    def gates(conv_vals, pre_recur, pre_input, decay_vals):
        log_rate = -rate_scale * jax.nn.sigmoid(pre_recur) * jax.nn.softplus(-decay_vals)
        decay_rate = jnp.where(starts[:, None], 0.0, jnp.exp(log_rate))
        scale_in = jnp.where(starts[:, None], 1.0, jnp.sqrt(-jnp.expm1(2.0 * log_rate)))
        return (decay_rate, conv_vals * jax.nn.sigmoid(pre_input) * scale_in)

    def glu(gate_pre, up_pre):
        return gelu_tanh(gate_pre) * up_pre

    x_branch = plain_dot(hidden_place, x_full).astype(jnp.bfloat16)
    y_before = plain_dot(hidden_place, y_full)
    previous = from_behind(x_branch[row_count - edge_rows :], "dp", 1)
    extended = jnp.concatenate([previous, x_branch], axis=0).astype(jnp.float32)
    conv_out = convolve(extended, conv_weight)
    conv_wide = extended_2(conv_out.astype(jnp.bfloat16), (("tensor", 1),), block_size)
    pre_both = jnp.zeros((row_count, 2 * own_width), jnp.float32)
    for index in range(block_count):
        piece = lax.dynamic_slice_in_dim(conv_wide, block_start(index), block_size, 1)
        pre_both = pre_both + jnp.where(
            block_mask(index)[None, :], plain_dot(piece, both_gates), 0.0
        )
    (decay_rate, driven), gate_pull = jax.vjp(
        gates, conv_out, pre_both[:, :own_width], pre_both[:, own_width:], decay_param
    )
    cum_rate, local_state = lax.associative_scan(pair_step, (decay_rate, driven), axis=0)
    ident = (jnp.ones((own_width,), jnp.float32), jnp.zeros((own_width,), jnp.float32))
    rate_in, state_in = entering((cum_rate[-1], local_state[-1]), "dp", pair_step, ident, False)
    state = local_state + cum_rate * state_in[None, :]
    y_branch = gelu_tanh(y_before)
    merged = (state * y_branch).astype(jnp.bfloat16)
    merged_stored = jnp.take(merged, order_all, axis=0)

    def mixer_rows(begin, number):
        return plain_dot(merged_stored, out_full)

    after_own = tok_own + row_sums(mixer_rows, tok_rows)
    hidden_two = spread_rows(rms_scale(after_own, second_gain).astype(jnp.bfloat16))
    gate_pre = plain_dot(hidden_two, gate_full)
    up_pre = plain_dot(hidden_two, up_full)
    glu_out, glu_pull = jax.vjp(glu, gate_pre, up_pre)
    product = glu_out.astype(jnp.bfloat16)

    def down_rows(begin, number):
        return plain_dot(product, down_full)

    feed_out = row_sums(down_rows, tok_rows)
    live_own = lax.dynamic_slice_in_dim(live_stored, own_start, tok_rows, 0)
    output = ((after_own + feed_out) * live_own[:, None]).astype(jnp.bfloat16)
    grad_out = cot_all.astype(jnp.float32) * live_stored[:, None]
    fresh = lax.optimization_barrier((shards, grad_out))[0]
    (
        gain_one,
        gain_two,
        x_full,
        y_full,
        recur_full,
        input_full,
        gate_full,
        up_full,
        out_full,
        down_full,
    ) = collect(*fresh)
    first_gain = gain_one.astype(jnp.float32)
    second_gain = gain_two.astype(jnp.float32)
    both_gates = jnp.concatenate([recur_full, input_full], axis=1)
    down_in = grad_out.astype(jnp.bfloat16)
    grad_down = trans_times(product, down_in)
    grad_product = times_trans(down_in, down_full)
    grad_gate_pre, grad_up_pre = glu_pull(grad_product)
    grad_gate_pre = grad_gate_pre.astype(jnp.bfloat16)
    grad_up_pre = grad_up_pre.astype(jnp.bfloat16)
    grad_gate = trans_times(hidden_two, grad_gate_pre)
    grad_up = trans_times(hidden_two, grad_up_pre)

    def feed_rows(begin, number):
        return times_trans(grad_gate_pre, gate_full) + times_trans(grad_up_pre, up_full)

    grad_out_own = lax.dynamic_slice_in_dim(grad_out, own_start, tok_rows, 0)
    grad_two_own = row_sums(feed_rows, tok_rows)
    grad_norm_own, normed_two = norm_back(after_own, second_gain, grad_two_own)
    second_part = jnp.sum(grad_two_own * normed_two, axis=0)
    grad_after_own = grad_out_own + grad_norm_own
    mixer_in = spread_rows(grad_after_own.astype(jnp.bfloat16))
    grad_out_mat = trans_times(merged_stored, mixer_in)
    grad_merged = jnp.take(times_trans(mixer_in, out_full), inverse, axis=0)
    grad_state = grad_merged * y_branch
    gelu_pull = jax.vjp(gelu_tanh, y_before)[1]
    grad_y_before = gelu_pull(grad_merged * state)[0].astype(jnp.bfloat16)
    rate_next = jnp.concatenate([decay_rate[1:], jnp.ones((1, own_width), jnp.float32)], axis=0)
    rev_rate, local_lam = lax.associative_scan(
        pair_step, (rate_next, grad_state), reverse=True, axis=0
    )
    head_rate = decay_rate[0] * rev_rate[0]
    head_lam = decay_rate[0] * local_lam[0]
    factor_in, lam_in = entering((head_rate, head_lam), "dp", pair_step, ident, True)
    lam = local_lam + rev_rate * lam_in[None, :]
    state_prev = jnp.concatenate([state_in[None, :], state[:-1]], axis=0)
    grad_conv_local, grad_pre_recur, grad_pre_input, grad_decay_own = gate_pull(
        (lam * state_prev, lam)
    )
    grad_pre = jnp.concatenate([grad_pre_recur, grad_pre_input], axis=1).astype(jnp.bfloat16)
    grad_both = jnp.zeros((block_size, 2 * own_width), jnp.float32)
    grad_wide = jnp.zeros((row_count, own_width + 2 * block_size), jnp.float32)
    for index in range(block_count):
        begin = block_start(index)
        piece = lax.dynamic_slice_in_dim(conv_wide, begin, block_size, 1)
        masked = jnp.where(block_mask(index)[None, :], grad_pre, jnp.zeros((), jnp.bfloat16))
        grad_both = grad_both + trans_times(piece, masked)
        added = lax.dynamic_slice_in_dim(grad_wide, begin, block_size, 1) + times_trans(
            masked, both_gates
        )
        grad_wide = lax.dynamic_update_slice_in_dim(grad_wide, added, begin, 1)
    grad_recur = grad_both[:, :own_width]
    grad_input = grad_both[:, own_width:]
    rims = jnp.concatenate(
        [grad_wide[:, :block_size], grad_wide[:, own_width + block_size :]], axis=1
    )
    arrived = extended_2(rims.astype(jnp.bfloat16), (("tensor", 1),), block_size).astype(rims.dtype)
    from_lower = jnp.pad(arrived[:, :block_size], ((0, 0), (0, own_width - block_size)))
    from_upper = jnp.pad(arrived[:, 3 * block_size :], ((0, 0), (own_width - block_size, 0)))
    grad_conv = (
        grad_conv_local
        + grad_wide[:, block_size : block_size + own_width]
        + from_lower
        + from_upper
    )
    conv_pull = jax.vjp(convolve, extended, conv_weight)[1]
    grad_extended, grad_kernel = conv_pull(grad_conv)
    returned = from_behind(grad_extended[:edge_rows], "dp", -1)
    grad_x_branch = grad_extended[edge_rows:] + jnp.concatenate(
        [jnp.zeros((row_count - edge_rows, own_width), jnp.float32), returned], axis=0
    )
    grad_x_low = grad_x_branch.astype(jnp.bfloat16)
    grad_x_stored = jnp.take(grad_x_low, order_all, axis=0)
    grad_y_stored = jnp.take(grad_y_before, order_all, axis=0)
    grad_x_mat = trans_times(first_all, grad_x_stored)
    grad_y_mat = trans_times(first_all, grad_y_stored)

    def mixer_back_rows(begin, number):
        return times_trans(grad_x_stored, x_full) + times_trans(grad_y_stored, y_full)

    grad_one_own = row_sums(mixer_back_rows, tok_rows)
    grad_norm_one, normed_one = norm_back(tok_own, first_gain, grad_one_own)
    first_part = jnp.sum(grad_one_own * normed_one, axis=0)
    grad_tokens = grad_after_own + grad_norm_one
    chosen = jnp.arange(n_tensor, dtype=jnp.int32) == tensor_index
    kernel_tile = jnp.where(chosen[:, None, None], grad_kernel[None, :, :], 0.0)
    decay_tile = jnp.where(chosen[:, None], grad_decay_own[None, :], 0.0)
    small = lax.psum((first_part, second_part, kernel_tile, decay_tile), ("dp", "tensor"))
    grad_first_gain = lax.dynamic_slice_in_dim(small[0], dp_index * dp_width, dp_width, 0)
    grad_second_gain = lax.dynamic_slice_in_dim(small[1], dp_index * dp_width, dp_width, 0)
    grad_kernel_sum = lax.dynamic_index_in_dim(small[2], tensor_index, 0, keepdims=False)
    grad_decay = lax.dynamic_index_in_dim(small[3], tensor_index, 0, keepdims=False)
    sums = (
        lax.psum_scatter(
            grad_x_mat.astype(jnp.bfloat16), "dp", scatter_dimension=0, tiled=True
        ).astype(jnp.float32),
        lax.psum_scatter(
            grad_y_mat.astype(jnp.bfloat16), "dp", scatter_dimension=0, tiled=True
        ).astype(jnp.float32),
        lax.psum_scatter(
            grad_recur.astype(jnp.bfloat16), "dp", scatter_dimension=0, tiled=True
        ).astype(jnp.float32),
        lax.psum_scatter(
            grad_input.astype(jnp.bfloat16), "dp", scatter_dimension=0, tiled=True
        ).astype(jnp.float32),
        lax.psum_scatter(
            grad_gate.astype(jnp.bfloat16), "dp", scatter_dimension=0, tiled=True
        ).astype(jnp.float32),
        lax.psum_scatter(
            grad_up.astype(jnp.bfloat16), "dp", scatter_dimension=0, tiled=True
        ).astype(jnp.float32),
        lax.psum_scatter(
            grad_out_mat.astype(jnp.bfloat16), "dp", scatter_dimension=1, tiled=True
        ).astype(jnp.float32),
        lax.psum_scatter(
            grad_down.astype(jnp.bfloat16), "dp", scatter_dimension=1, tiled=True
        ).astype(jnp.float32),
    )
    return (
        output,
        grad_tokens,
        grad_first_gain,
        sums[0],
        sums[1],
        grad_kernel_sum,
        sums[2],
        sums[3],
        grad_decay,
        sums[6],
        grad_second_gain,
        sums[4],
        sums[5],
        sums[7],
    )


MESH = pl.DeviceIdType.MESH
VMEM_BYTES = 60 * 2**20


def remote(src, dst, send, recv, device):
    return pltpu.make_async_remote_copy(
        src_ref=src,
        dst_ref=dst,
        send_sem=send,
        recv_sem=recv,
        device_id=device,
        device_id_type=MESH,
    )


class Place:
    def __init__(self, n_dp, n_line):
        self.n_dp, self.n_line = n_dp, n_line
        self.d, self.t = lax.axis_index("dp"), lax.axis_index("tensor")
        self.core = lax.rem(self.d, 2)
        self.x = lax.rem(lax.div(self.d, 2), 2)
        self.y = lax.div(self.d, 4)

    def chip(self, flip_x, flip_y, flip_core=0):
        x = 1 - self.x if flip_x else self.x
        y = 1 - self.y if flip_y else self.y
        core = 1 - self.core if flip_core else self.core
        return y * 4 + x * 2 + core

    def at(self, flip_x=0, flip_y=0, flip_core=0):
        return (self.chip(flip_x, flip_y, flip_core), self.t)

    def up(self):
        return (self.d, lax.rem(self.t + 1, self.n_line))

    def down(self):
        return (self.d, lax.rem(self.t + self.n_line - 1, self.n_line))

    def meet(self, everyone=False):
        barrier = pltpu.get_barrier_semaphore()

        def greet(device):
            pl.semaphore_signal(barrier, inc=1, device_id=device, device_id_type=MESH)

        if everyone:
            for i in range(1, self.n_dp):
                greet((lax.rem(self.d + i, self.n_dp), self.t))
            for i in range(1, self.n_line):
                greet((self.d, lax.rem(self.t + i, self.n_line)))
            pl.semaphore_wait(barrier, self.n_dp + self.n_line - 2)
            return
        for flips in ((1, 0), (0, 1), (0, 0, 1)):
            greet(self.at(*flips))
        below, above = self.t > 0, self.t < self.n_line - 1

        @pl.when(below)
        def _():
            greet(self.down())

        @pl.when(above)
        def _():
            greet(self.up())

        pl.semaphore_wait(barrier, 3 + below.astype(jnp.int32) + above.astype(jnp.int32))


class GatherPlane:
    def __init__(self, place, src, dst, send, recv, local):
        self.p, self.src, self.dst = place, src, dst
        self.rows = src.shape[0]
        self.send, self.recv, self.local = send, recv, local

    def block(self, fx, fy, fc=0, part=None):
        first = self.p.chip(fx, fy, fc) * self.rows
        size = self.rows
        if part is not None:
            size = self.rows // 2
            first = first + part * size
        return self.dst.at[pl.ds(pl.multiple_of(first, 16), size)]

    def copy(self, i, src, dst, device):
        return remote(src, dst, self.send.at[i], self.recv.at[i], device)

    def mine(self):
        return pltpu.make_async_copy(self.src, self.block(0, 0), self.local)

    def outgoing(self, i):
        at, block = self.p.at, self.block
        if i == 0:
            return self.copy(0, self.src, block(0, 0), at(1, 0))
        if i == 1:
            return self.copy(1, self.src, block(0, 0), at(0, 1))
        if i == 2:
            return self.copy(2, self.src, block(0, 0), at(0, 0, 1))
        if i == 3:
            return self.copy(3, block(1, 0, 0, 0), block(1, 0, 0, 0), at(0, 1))
        if i == 4:
            return self.copy(4, block(0, 1, 0, 1), block(0, 1, 0, 1), at(1, 0))
        spot = ((1, 0), (0, 1), (1, 1, 0, 0), (1, 1, 0, 1))[i - 5]
        return self.copy(i, block(*spot), block(*spot), at(0, 0, 1))

    def arrive(self, i):
        spot = (
            (1, 0),
            (0, 1),
            (0, 0, 1),
            (1, 1, 0, 0),
            (1, 1, 0, 1),
            (1, 0, 1),
            (0, 1, 1),
            (1, 1, 1, 0),
            (1, 1, 1, 1),
        )[i]
        here = self.block(*spot)
        self.copy(i, here, here, self.p.at(0, 0, 1)).wait_recv()

    def begin(self):
        self.mine().start()
        for i in (0, 1, 2):
            self.outgoing(i).start()

    def forward(self):
        self.arrive(0)
        self.outgoing(3).start()
        self.arrive(1)
        self.outgoing(4).start()
        self.outgoing(5).start()
        self.outgoing(6).start()

    def share(self):
        self.arrive(3)
        self.outgoing(7).start()
        self.arrive(4)
        self.outgoing(8).start()

    def finish(self):
        for i in (2, 5, 6, 7, 8):
            self.arrive(i)
        for i in range(9):
            self.outgoing(i).wait_send()
        self.mine().wait()


class GatherLine:
    def __init__(self, place, dst, rows, begin, span, send, recv):
        self.p, self.dst, self.rows = place, dst, rows
        self.begin, self.span = begin, span
        self.send, self.recv = send, recv
        self.last = place.n_line - 1

    def block(self, owner):
        first = owner * self.rows + self.begin
        return self.dst.at[pl.ds(pl.multiple_of(first, 8), self.span)]

    def copy(self, way, k, owner, source=None):
        to = self.p.up() if way == 0 else self.p.down()
        block = self.block(owner)
        return remote(
            block if source is None else source,
            block,
            self.send.at[way, k],
            self.recv.at[way, k],
            to,
        )

    def step(self, k, source=None):
        t, last = self.p.t, self.last
        if k > 0:
            self.arrive(k - 1)

        @pl.when((t < last) & (t >= k))
        def _():
            self.copy(0, k, t - k, source).start()

        @pl.when((t > 0) & (t + k <= last))
        def _():
            self.copy(1, k, t + k, source).start()

    def arrive(self, k):
        t, last = self.p.t, self.last

        @pl.when(t >= k + 1)
        def _():
            self.copy(0, k, t - 1 - k).wait_recv()

        @pl.when(t + k + 1 <= last)
        def _():
            self.copy(1, k, t + 1 + k).wait_recv()

    def finish(self):
        t, last = self.p.t, self.last
        self.arrive(last - 1)
        for k in range(last):

            @pl.when((t < last) & (t >= k))
            def _():
                self.copy(0, k, t - k).wait_send()

            @pl.when((t > 0) & (t + k <= last))
            def _():
                self.copy(1, k, t + k).wait_send()


class ReduceLine:
    def __init__(self, place, terms, rows, begin, span, stage, inbox, send, recv):
        self.p, self.terms, self.rows = place, terms, rows
        self.begin, self.span = begin, span
        self.stage, self.inbox = stage, inbox
        self.send, self.recv = send, recv
        self.last = place.n_line - 1

    def own(self, owner):
        first = owner * self.rows + self.begin
        return self.terms.at[pl.ds(pl.multiple_of(first, 16), self.span)]

    def copy(self, way, j, source):
        to = self.p.up() if way == 0 else self.p.down()
        return remote(
            source, self.inbox.at[way, j], self.send.at[way, j], self.recv.at[way, j], to
        )

    def ends(self):
        t, last = self.p.t, self.last

        @pl.when(t == 0)
        def _():
            for j in range(last):
                self.copy(0, j, self.own(last - j)).start()

        @pl.when(t == last)
        def _():
            for j in range(last):
                self.copy(1, j, self.own(j)).start()

    def sent(self):
        t, last = self.p.t, self.last

        @pl.when(t == 0)
        def _():
            for j in range(last):
                self.copy(0, j, self.own(last - j)).wait_send()

        @pl.when(t == last)
        def _():
            for j in range(last):
                self.copy(1, j, self.own(j)).wait_send()

    def hand_on(self, way, j):
        term = self.own(self.last - j if way == 0 else j)
        self.copy(way, j, term).wait_recv()
        self.stage[way, j] = (
            term[...].astype(jnp.float32) + self.inbox[way, j].astype(jnp.float32)
        ).astype(jnp.bfloat16)
        self.copy(way, j, self.stage.at[way, j]).start()

    def hop(self, k):
        t, last = self.p.t, self.last

        @pl.when(t == k + 1)
        def _():
            for j in range(last - 1 - k):
                self.hand_on(0, j)

        @pl.when(t == last - 1 - k)
        def _():
            for j in range(last - 1 - k):
                self.hand_on(1, j)

    def total(self, result):
        t, last = self.p.t, self.last
        result[...] = self.own(t)[...].astype(jnp.float32)

        @pl.when(t > 0)
        def _():
            j = last - t
            self.copy(0, j, self.stage.at[0, 0]).wait_recv()
            result[...] += self.inbox[0, j].astype(jnp.float32)

        @pl.when(t < last)
        def _():
            self.copy(1, t, self.stage.at[0, 0]).wait_recv()
            result[...] += self.inbox[1, t].astype(jnp.float32)

    def finish(self):
        t, last = self.p.t, self.last
        for j in range(last - 1):

            @pl.when((t > 0) & (t < last - j))
            def _():
                self.copy(0, j, self.stage.at[0, j]).wait_send()

            @pl.when((t < last) & (t > j))
            def _():
                self.copy(1, j, self.stage.at[1, j]).wait_send()


def add_rows(into, other, result=None):
    result = into if result is None else result

    def tile(i, carry):
        rows = pl.ds(pl.multiple_of(i * 16, 16), 16)
        result[rows] = (
            into[rows].astype(jnp.float32) + other[rows].astype(jnp.float32)
        ).astype(result.dtype)
        return carry

    lax.fori_loop(0, into.shape[0] // 16, tile, None)


class ReducePlane:
    chips = ((0, 0), (1, 0), (0, 1), (1, 1))

    def __init__(self, place, terms, scratch):
        self.p, self.terms = place, terms
        self.held, self.near, self.along, self.last, self.send, self.recv, self.local = scratch
        self.rows = self.held.shape[1]
        self.half = self.rows // 2

    @staticmethod
    def scratch(rows, width):
        return [
            pltpu.VMEM((4, rows, width), jnp.bfloat16),
            pltpu.VMEM((4, rows, width), jnp.bfloat16),
            pltpu.VMEM((4, rows // 2, width), jnp.bfloat16),
            pltpu.VMEM((2, rows // 2, width), jnp.bfloat16),
            pltpu.SemaphoreType.DMA((10,)),
            pltpu.SemaphoreType.DMA((10,)),
            pltpu.SemaphoreType.DMA((4,)),
        ]

    def block(self, k, other):
        first = self.p.chip(*self.chips[k], other) * self.rows
        return self.terms.at[pl.ds(pl.multiple_of(first, 16), self.rows)]

    def half_of(self, k, part):
        return self.held.at[k, pl.ds(part * self.half, self.half)]

    def load(self, k):
        return pltpu.make_async_copy(self.block(k, 0), self.held.at[k], self.local.at[k])

    def copy(self, i):
        at = self.p.at
        if i < 4:
            src, dst, to = self.block(i, 1), self.near.at[i], at(0, 0, 1)
        elif i < 8:
            src, to = (
                (self.half_of(1, 0), at(1, 0)),
                (self.half_of(3, 0), at(1, 0)),
                (self.half_of(2, 1), at(0, 1)),
                (self.half_of(3, 1), at(0, 1)),
            )[i - 4]
            dst = self.along.at[i - 4]
        else:
            src, to = ((self.half_of(2, 0), at(0, 1)), (self.half_of(1, 1), at(1, 0)))[i - 8]
            dst = self.last.at[i - 8]
        return remote(src, dst, self.send.at[i], self.recv.at[i], to)

    def begin(self):
        for k in (3, 1, 2, 0):
            self.copy(k).start()
            self.load(k).start()

    def cores(self):
        for k in (3, 1, 2, 0):
            self.load(k).wait()
            self.copy(k).wait_recv()
            add_rows(self.held.at[k], self.near.at[k])
            if k == 3:
                self.copy(5).start()
                self.copy(7).start()
            elif k == 1:
                self.copy(4).start()
            elif k == 2:
                self.copy(6).start()

    def turn(self):
        self.copy(5).wait_recv()
        add_rows(self.half_of(2, 0), self.along.at[1])
        self.copy(8).start()
        self.copy(7).wait_recv()
        add_rows(self.half_of(1, 1), self.along.at[3])
        self.copy(9).start()
        self.copy(4).wait_recv()
        add_rows(self.half_of(0, 0), self.along.at[0])
        self.copy(6).wait_recv()
        add_rows(self.half_of(0, 1), self.along.at[2])

    def finish(self, result):
        for part in (0, 1):
            self.copy(8 + part).wait_recv()
            rows = pl.ds(part * self.half, self.half)
            add_rows(self.half_of(0, part), self.last.at[part], result.at[rows])
        for i in range(10):
            self.copy(i).wait_send()


def dma_sems(*dims):
    return pltpu.SemaphoreType.DMA(dims)


def in_vmem():
    return pl.BlockSpec(memory_space=pltpu.VMEM)


def in_any():
    return pl.BlockSpec(memory_space=pl.ANY)


def comm_params(number):
    return pltpu.CompilerParams(
        collective_id=number, has_side_effects=True, vmem_limit_bytes=VMEM_BYTES
    )


def shaped(dims, kind):
    return jax.ShapeDtypeStruct(dims, kind)


def first_gather(n_dp, n_line, mats, rows_in, order):
    count = len(mats)
    parts = 2

    def kernel(*refs):
        srcs, (c, e) = refs[:count], refs[count : count + 2]
        dsts, (c_out, e_out) = refs[count + 2 : 2 * count + 2], refs[2 * count + 2 : 2 * count + 4]
        ps, pr, pl_sem, ls, lr, ll = refs[2 * count + 4 :]
        place = Place(n_dp, n_line)
        place.meet()
        planes = [
            GatherPlane(place, a, b, ps.at[i], pr.at[i], pl_sem.at[i])
            for i, (a, b) in enumerate(zip(srcs, dsts))
        ]
        rows = c.shape[0]
        span = rows // parts
        lines = [
            GatherLine(place, c_out, rows, i * span, span, ls.at[i], lr.at[i])
            for i in range(parts)
        ]
        lines.append(
            GatherLine(place, e_out, e.shape[0], 0, e.shape[0], ls.at[parts], lr.at[parts])
        )
        for i in range(parts):
            lines[i].step(0, c.at[pl.ds(i * span, span)])
        lines[parts].step(0, e)
        early, late = planes[: count // 2], planes[count // 2 :]
        for part in early:
            part.begin()
        copies = []
        for i, (src, dst) in enumerate(((c, c_out), (e, e_out))):
            own = dst.at[pl.ds(pl.multiple_of(place.t * src.shape[0], 8), src.shape[0])]
            copies.append(pltpu.make_async_copy(src, own, ll.at[i]))
            copies[i].start()
        for line in lines:
            line.step(1)
        for part in late:
            part.begin()
        for part in early:
            part.forward()
        for line in lines:
            line.step(2)
        for part in early:
            part.share()
        for part in late:
            part.forward()
        for part in late:
            part.share()
        for part in lines + planes:
            part.finish()
        for copy in copies:
            copy.wait()

    return pl.pallas_call(
        kernel,
        out_shape=tuple(shaped((n_dp * m.shape[0], m.shape[1]), m.dtype) for m in mats)
        + (
            shaped((n_line * rows_in.shape[0], rows_in.shape[1]), rows_in.dtype),
            shaped((n_line * order.shape[0], order.shape[1]), order.dtype),
        ),
        in_specs=[in_any()] * (count + 2),
        out_specs=[in_any()] * (count + 2),
        scratch_shapes=[
            dma_sems(count, 9),
            dma_sems(count, 9),
            dma_sems(count),
            dma_sems(parts + 1, 2, n_line - 1),
            dma_sems(parts + 1, 2, n_line - 1),
            dma_sems(2),
        ],
        compiler_params=comm_params(1),
        name="first_gather",
    )(*mats, rows_in, order)


CHUNKS = 8


def line_scratch(n_line, span, width):
    hops = n_line - 1
    return [
        pltpu.VMEM((CHUNKS, 2, hops, span, width), jnp.bfloat16),
        pltpu.VMEM((CHUNKS, 2, hops, span, width), jnp.bfloat16),
        dma_sems(CHUNKS, 2, hops),
        dma_sems(CHUNKS, 2, hops),
        dma_sems(CHUNKS, 2, hops),
        dma_sems(CHUNKS, 2, hops),
        pltpu.VMEM((span, width), jnp.float32),
    ]


def sum_rows_and_spread(place, terms, scratch, finish_rows, spread, between):
    stage, inbox, rs, rr, gs, gr, total = scratch
    span = total.shape[0]
    count = stage.shape[0]
    rows = span * count
    hops = place.n_line - 1
    sums = [
        ReduceLine(place, terms, rows, c * span, span, stage.at[c], inbox.at[c], rs.at[c], rr.at[c])
        for c in range(count)
    ]
    gathers = []
    if spread is not None:
        gathers = [
            GatherLine(place, spread, rows, c * span, span, gs.at[c], gr.at[c])
            for c in range(count)
        ]
    sums[0].ends()

    def total_of(c):
        sums[c].total(total)
        finish_rows(c, pl.ds(c * span, span), total)
        if gathers:
            gathers[c].step(0)

    stages = [lambda c, k=k: sums[c].hop(k) for k in range(hops - 1)] + [total_of]
    lags = [LAGS[min(k, len(LAGS) - 1)] for k in range(hops)]
    if gathers:
        stages += [lambda c, k=k: gathers[c].step(k) for k in range(1, hops)]
        lags += [lags[-1] + LAG_STEP * k for k in range(1, hops)]
    for i in range(count + lags[-1]):
        if i < count:
            sums[i].sent()
        if i + 1 < count:
            sums[i + 1].ends()
        for work, lag in zip(stages, lags):
            if 0 <= i - lag < count:
                work(i - lag)
        if i in between:
            between[i]()
    for part in gathers + sums:
        part.finish()


LAGS = (0, 1, 1)
LAG_STEP = 1


def middle_gather(n_dp, n_line, terms, tokens, gain, mats):
    rows, width = tokens.shape
    count = len(mats)

    def kernel(*refs):
        s, tok, gain_ref = refs[:3]
        srcs = refs[3 : 3 + count]
        after, hidden = refs[3 + count : 5 + count]
        dsts = refs[5 + count : 5 + 2 * count]
        ps, pr, pl_sem = refs[5 + 2 * count : 8 + 2 * count]
        scratch = refs[8 + 2 * count :]
        place = Place(n_dp, n_line)
        place.meet()
        planes = [
            GatherPlane(place, a, b, ps.at[i], pr.at[i], pl_sem.at[i])
            for i, (a, b) in enumerate(zip(srcs, dsts))
        ]
        planes[0].begin()

        def norm(c, here, total):
            values = tok[here].astype(jnp.float32) + total[...]
            after[here] = values
            low = rms_scale(values, gain_ref[...]).astype(jnp.bfloat16)
            first = pl.multiple_of(place.t * rows, 16) + c * total.shape[0]
            hidden[pl.ds(pl.multiple_of(first, 16), total.shape[0])] = low

        between = {5: planes[0].forward, 8: planes[0].share}
        sum_rows_and_spread(place, s, scratch, norm, hidden, between)
        for part in planes:
            part.finish()

    return pl.pallas_call(
        kernel,
        out_shape=(
            shaped((rows, width), jnp.float32),
            shaped((n_line * rows, width), jnp.bfloat16),
        )
        + tuple(shaped((n_dp * m.shape[0], m.shape[1]), m.dtype) for m in mats),
        in_specs=[in_vmem()] * 3 + [in_any()] * count,
        out_specs=[in_vmem()] * 2 + [in_any()] * count,
        scratch_shapes=[dma_sems(count, 9), dma_sems(count, 9), dma_sems(count)]
        + line_scratch(n_line, rows // CHUNKS, width),
        compiler_params=comm_params(2),
        name="middle_gather",
    )(terms, tokens, gain, *mats)


def middle_sums(n_dp, n_line, terms, after, gain, grad_in, mats):
    rows, width = after.shape
    count = len(mats)
    block = mats[0].shape[0] // n_dp
    per = len(ReducePlane.scratch(16, 128))

    def kernel(*refs):
        s, after_ref, gain_ref, g_ref = refs[:4]
        srcs = refs[4 : 4 + count]
        grad_after, gain_sum, spread = refs[4 + count : 7 + count]
        results = refs[7 + count : 7 + 2 * count]
        rest = refs[7 + 2 * count :]
        scratch = rest[count * per :]
        place = Place(n_dp, n_line)
        place.meet()
        planes = [
            ReducePlane(place, srcs[i], rest[i * per : (i + 1) * per]) for i in range(count)
        ]
        for part in planes:
            part.begin()
        gain_sum[...] = jnp.zeros_like(gain_sum)

        def norm(c, here, total):
            grad = total[...]
            grad_rows, normed = norm_back(after_ref[here], gain_ref[...], grad)
            gain_sum[...] += jnp.sum(grad * normed, axis=0, keepdims=True)
            both = g_ref[here].astype(jnp.float32) + grad_rows
            grad_after[here] = both
            first = pl.multiple_of(place.t * rows, 16) + c * total.shape[0]
            spread[pl.ds(pl.multiple_of(first, 16), total.shape[0])] = both.astype(jnp.bfloat16)

        between = {1: planes[0].cores, 7: planes[0].turn}
        sum_rows_and_spread(place, s, scratch, norm, spread, between)
        for part, result in zip(planes, results):
            part.finish(result)

    return pl.pallas_call(
        kernel,
        out_shape=(
            shaped((rows, width), jnp.float32),
            shaped((1, width), jnp.float32),
            shaped((n_line * rows, width), jnp.bfloat16),
        )
        + tuple(shaped((block, m.shape[1]), jnp.bfloat16) for m in mats),
        in_specs=[in_vmem()] * 4 + [in_any()] * count,
        out_specs=[in_vmem()] * (3 + count),
        scratch_shapes=sum([ReducePlane.scratch(block, m.shape[1]) for m in mats], [])
        + line_scratch(n_line, rows // CHUNKS, width),
        compiler_params=comm_params(3),
        name="middle_sums",
    )(terms, after, gain, grad_in, *mats)


class Exchange:
    def __init__(self, place, axis, src, slots, send, recv, local):
        self.p, self.src, self.slots = place, src, slots
        self.over_dp = axis == "dp"
        self.size = place.n_dp if self.over_dp else place.n_line
        self.me = place.d if self.over_dp else place.t
        self.send, self.recv, self.local = send, recv, local

    def copy(self, i):
        to = lax.rem(self.me + i, self.size)
        device = (to, self.p.t) if self.over_dp else (self.p.d, to)
        return remote(
            self.src, self.slots.at[self.me], self.send.at[i - 1], self.recv.at[i - 1], device
        )

    def mine(self):
        return pltpu.make_async_copy(self.src, self.slots.at[self.me], self.local)

    def begin(self):
        for i in range(1, self.size):
            self.copy(i).start()
        self.mine().start()

    def wait(self):
        self.mine().wait()
        for i in range(1, self.size):
            self.copy(i).wait()

    def finish(self):
        self.wait()
        total = self.slots[0]
        for i in range(1, self.size):
            total = total + self.slots[i]
        return total


def last_sums(n_dp, n_line, terms, tokens, gain, grad_after, small, mats):
    rows, width = tokens.shape
    count = len(mats)
    per = len(ReducePlane.scratch(16, 128))

    def kernel(*refs):
        s, tok, gain_ref, g_ref, small_ref = refs[:5]
        srcs = refs[5 : 5 + count]
        grad_tok, small_out, first_out = refs[5 + count : 8 + count]
        results = refs[8 + count : 8 + 2 * count]
        rest = refs[8 + 2 * count :]
        own_first, row_sum = rest[count * per : count * per + 2]
        slots_a, slots_b, slots_c, slots_d = rest[count * per + 2 : count * per + 6]
        xs, xr, xl = rest[count * per + 6 : count * per + 9]
        scratch = rest[count * per + 9 :]
        place = Place(n_dp, n_line)
        place.meet(True)
        planes = [
            ReducePlane(place, srcs[i], rest[i * per : (i + 1) * per]) for i in range(count)
        ]
        for part in planes:
            part.begin()
        early = Exchange(place, "dp", small_ref, slots_a, xs.at[0], xr.at[0], xl.at[0])
        early.begin()
        own_first[...] = jnp.zeros_like(own_first)

        def norm(c, here, total):
            grad = total[...]
            grad_rows, normed = norm_back(tok[here].astype(jnp.float32), gain_ref[...], grad)
            own_first[...] += jnp.sum(grad * normed, axis=0, keepdims=True)
            grad_tok[here] = g_ref[here] + grad_rows

        def cores():
            for part in planes:
                part.cores()

        def turn():
            for part in planes:
                part.turn()

        sum_rows_and_spread(place, s, scratch, norm, None, {0: cores, 5: turn})
        first = Exchange(place, "dp", own_first, slots_b, xs.at[1], xr.at[1], xl.at[1])
        first.begin()
        small_out[...] = early.finish()
        row_sum[0:1] = small_out[0:1]
        row_sum[1:2] = first.finish()
        both = Exchange(place, "tensor", row_sum, slots_c, xs.at[2], xr.at[2], xl.at[2])
        both.begin()
        for part, result in zip(planes, results):
            part.finish(result)
        first_out[...] = both.finish()

    return pl.pallas_call(
        kernel,
        out_shape=(
            shaped((rows, width), jnp.float32),
            shaped(small.shape, jnp.float32),
            shaped((2, width), jnp.float32),
        )
        + tuple(shaped((m.shape[0] // n_dp, m.shape[1]), jnp.bfloat16) for m in mats),
        in_specs=[in_vmem()] * 5 + [in_any()] * count,
        out_specs=[in_vmem()] * (3 + count),
        scratch_shapes=sum([ReducePlane.scratch(m.shape[0] // n_dp, m.shape[1]) for m in mats], [])
        + [
            pltpu.VMEM((1, width), jnp.float32),
            pltpu.VMEM((2, width), jnp.float32),
            pltpu.VMEM((n_dp,) + small.shape, jnp.float32),
            pltpu.VMEM((n_dp, 1, width), jnp.float32),
            pltpu.VMEM((n_line, 2, width), jnp.float32),
            pltpu.VMEM((1, width), jnp.float32),
            dma_sems(3, n_dp),
            dma_sems(3, n_dp),
            dma_sems(3),
        ]
        + line_scratch(n_line, rows // CHUNKS, width),
        compiler_params=comm_params(4),
        name="last_sums",
    )(terms, tokens, gain, grad_after, small, *mats)


def loop(count, body, unroll=1):
    def step(i, carry):
        body(i)
        return carry

    lax.fori_loop(0, count, step, None, unroll=unroll)


def tile_rows(i, size, ahead=0):
    return pl.ds(pl.multiple_of(i * size + ahead, 8), size)


def moved_up(values, distance, count):
    size = values.shape[0]
    return pltpu.roll(values, (size - distance) % size, 0)[:count]


def take_lanes(ref, here):
    return jnp.concatenate([ref[c, here] for c in range(ref.shape[0])], axis=1)


def put_lanes(ref, here, values):
    for c in range(ref.shape[0]):
        ref[c, here] = values[:, c * LANES : (c + 1) * LANES]


def gelu_parts(values):
    inner = GELU_C * (values + 0.044715 * (values * values * values))
    tanh = jnp.tanh(inner)
    half = 0.5 * (1.0 + tanh)
    slope = half + 0.5 * values * (1.0 - tanh * tanh) * GELU_C * (
        1.0 + 3.0 * 0.044715 * (values * values)
    )
    return values * half, slope


GELU_C = 0.7978845608028654
RIM = 128
LANES = 128
TILE = 16


def one_minus_exp(values, exponential):
    series = jnp.ones_like(values)
    for term in range(9, 1, -1):
        series = 1.0 + values * (1.0 / term) * series
    return jnp.where(values > -0.35, -values * series, 1.0 - exponential)


def rate_and_scale(pre_recur, soft, start):
    sr = jax.nn.sigmoid(pre_recur)
    log_rate = -rate_scale * sr * soft
    decay = jnp.exp(log_rate)
    rate = jnp.where(start, 0.0, decay)
    scale = jnp.where(start, 1.0, jnp.sqrt(one_minus_exp(2.0 * log_rate, decay * decay)))
    return sr, rate, scale


class RimSwap:
    def __init__(self, place, own):
        self.odd = lax.rem(place.t, 2)
        self.partner = (place.d, place.t + 1 - 2 * self.odd)
        self.first = pl.multiple_of(RIM - RIM * self.odd, RIM)
        self.edge = pl.ds(pl.multiple_of((1 - self.odd) * own + self.odd * RIM, RIM), RIM)
        self.over_there = pl.ds(pl.multiple_of(self.odd * (own + RIM), RIM), RIM)
        self.beyond = pl.ds(pl.multiple_of((1 - self.odd) * (own + RIM), RIM), RIM)

    def block(self, index, size):
        return pl.ds(pl.multiple_of(self.first + index * size, RIM), size)


def recur_forward(
    n_dp,
    n_line,
    tok_all,
    cot,
    to_place,
    to_stored,
    x_full,
    y_full,
    out_full,
    gain,
    gates,
    taps,
    soft,
    flags,
):
    rows, width = tok_all.shape
    count, own = taps.shape
    size = gates.shape[0]
    wide = own + 2 * RIM
    blocks = (wide - RIM) // size
    chunk = rows // 8
    cot_rows = cot.shape[0]
    parts = 1

    def kernel(*refs):
        (tok, cot_ref, plc, sto, wx, wy, wo, gain_ref, gw, cw, sp, fl) = refs[:12]
        (hp, xext, y, conv_low, conv, pre_r, pre_i, rate, state, merged_st, terms, cot_all) = refs[
            12:24
        ]
        (h, xf, local, cum, merged, agg, slots, hs, hr, es, er, el, gs, gr, gl) = refs[24:]
        place = Place(n_dp, n_line)
        place.meet(True)
        swap = RimSwap(place, own)
        own_cot = cot_all.at[pl.ds(pl.multiple_of(place.t * cot_rows, 16), cot_rows)]
        keep = pltpu.make_async_copy(cot_ref, own_cot, gl)
        keep.start()
        span = cot_rows // parts
        lines = [
            GatherLine(place, cot_all, cot_rows, c * span, span, gs.at[c], gr.at[c])
            for c in range(parts)
        ]
        for c, line in enumerate(lines):
            line.step(0, cot_ref.at[pl.ds(c * span, span)])

        def norm(i):
            here = tile_rows(i, TILE)
            h[here] = rms_scale(tok[here].astype(jnp.float32), gain_ref[...]).astype(jnp.bfloat16)

        loop(rows // TILE, norm)

        def project(i):
            here = tile_rows(i, 128)
            hp[here] = plain_dot(plc[here], h[...]).astype(jnp.bfloat16)
            xext[tile_rows(i, 128, 16)] = plain_dot(hp[here], wx[...]).astype(jnp.bfloat16)

        loop(rows // 128, project)
        edge = remote(
            xext.at[pl.ds(rows, 16)],
            xext.at[pl.ds(0, 16)],
            hs.at[0],
            hr.at[0],
            (lax.rem(place.d + 1, n_dp), place.t),
        )
        edge.start()
        for line in lines:
            line.step(1)

        def project_y(i):
            here = tile_rows(i, 128)
            y[here] = plain_dot(hp[here], wy[...])

        loop(rows // 128, project_y)
        edge.wait()
        top = xext[pl.ds(0, 16)]
        xext[pl.ds(0, 16)] = jnp.where(place.d > 0, top, jnp.zeros_like(top))

        def widen(i):
            xf[tile_rows(i, TILE)] = xext[tile_rows(i, TILE)].astype(jnp.float32)

        loop(rows // TILE + 1, widen)

        def convolve(i):
            here = tile_rows(i, TILE)
            near = xf[pl.ds(pl.multiple_of(i * TILE + 8, 8), TILE + 8)]
            same = fl[tile_rows(i, TILE, 8)]
            total = cw[0:1] * near[8:]
            for k in range(1, count):
                total += cw[k : k + 1] * moved_up(near, 8 - k, TILE) * same[:, k : k + 1]
            conv[here] = total
            conv_low[here, RIM : RIM + own] = total.astype(jnp.bfloat16)

        loop(rows // TILE, convolve)
        rim = remote(
            conv_low.at[:, swap.edge],
            conv_low.at[:, swap.over_there],
            hs.at[1],
            hr.at[1],
            swap.partner,
        )
        rim.start()
        for i in range(blocks):
            index = lax.rem(i + swap.odd, blocks)
            cols = swap.block(index, size)
            other = pl.ds(pl.multiple_of(wide + swap.first + index * size, RIM), size)
            if i == blocks - 1:
                rim.wait()
            pre_r[:, cols] = plain_dot(conv_low[:, cols], gw[:, cols])
            pre_i[:, cols] = plain_dot(conv_low[:, cols], gw[:, other])

        def drive(i):
            here = tile_rows(i, TILE)
            start = fl[tile_rows(i, TILE, 8)][:, 0:1] > 0.0
            own_cols = pl.ds(RIM, own)
            _, decay, scale = rate_and_scale(pre_r[here, own_cols], sp[...], start)
            put_lanes(rate, here, decay)
            put_lanes(local, here, conv[here] * jax.nn.sigmoid(pre_i[here, own_cols]) * scale)

        loop(rows // TILE, drive)
        for line in lines:
            line.step(2)
        groups = own // LANES

        def scan(i, carry):
            here = pl.ds(i, 8, chunk)
            result = []
            for c in range(groups):
                product, total = carry[c]
                r = rate[c, here]
                product = product * r
                total = total * r + local[c, here]
                cum[c, here] = product
                local[c, here] = total
                result.append((product, total))
            return tuple(result)

        blank = (jnp.ones((8, LANES), jnp.float32), jnp.zeros((8, LANES), jnp.float32))
        lax.fori_loop(0, chunk, scan, (blank,) * groups)
        product, total = jnp.ones((1, own), jnp.float32), jnp.zeros((1, own), jnp.float32)
        for j in range(8):
            last = pl.ds(j * chunk + chunk - 1, 1)
            total = take_lanes(local, last) + take_lanes(cum, last) * total
            product = product * take_lanes(cum, last)
        agg[0:1] = product
        agg[1:2] = total
        swap_all = Exchange(place, "dp", agg, slots, es, er, el)
        swap_all.begin()
        swap_all.wait()
        entry = jnp.zeros((1, own), jnp.float32)
        for q in range(n_dp):
            longer = slots[q, 1:2] + slots[q, 0:1] * entry
            entry = jnp.where(q < place.d, longer, entry)
        state[pl.ds(0, 8)] = jnp.broadcast_to(entry, (8, own))
        for j in range(8):

            def settle(i, entry=entry):
                here = tile_rows(i, TILE, j * chunk)
                values = take_lanes(local, here) + take_lanes(cum, here) * entry
                state[tile_rows(i, TILE, j * chunk + 8)] = values
                merged[here] = (values * gelu_parts(y[here])[0]).astype(jnp.bfloat16)

            loop(chunk // TILE, settle)
            last = pl.ds(j * chunk + chunk - 1, 1)
            entry = take_lanes(local, last) + take_lanes(cum, last) * entry
        merged_st[...] = plain_dot(sto[...], merged[...]).astype(jnp.bfloat16)

        def mix(i):
            some = tile_rows(i, 512)
            terms[:, pl.ds(pl.multiple_of(i * 512, 512), 512)] = times_trans(
                merged_st[...], wo[some, :]
            ).astype(jnp.bfloat16)

        loop(width // 512, mix)
        for line in lines:
            line.finish()
        keep.wait()

    low, full = jnp.bfloat16, jnp.float32
    return pl.pallas_call(
        kernel,
        out_shape=(
            shaped((rows, width), low),
            shaped((rows + 16, own), low),
            shaped((rows, own), full),
            shaped((rows, wide), low),
            shaped((rows, own), full),
            shaped((rows, wide), full),
            shaped((rows, wide), full),
            shaped((own // LANES, rows, LANES), full),
            shaped((rows + 8, own), full),
            shaped((rows, own), low),
            shaped((rows, width), low),
            shaped((n_line * cot_rows, width), low),
        ),
        in_specs=[in_vmem(), in_any()] + [in_vmem()] * 10,
        out_specs=[in_vmem()] * 11 + [in_any()],
        scratch_shapes=[
            pltpu.VMEM((rows, width), low),
            pltpu.VMEM((rows + 16, own), full),
            pltpu.VMEM((own // LANES, rows, LANES), full),
            pltpu.VMEM((own // LANES, rows, LANES), full),
            pltpu.VMEM((rows, own), low),
            pltpu.VMEM((2, own), full),
            pltpu.VMEM((n_dp, 2, own), full),
            dma_sems(2),
            dma_sems(2),
            dma_sems(n_dp),
            dma_sems(n_dp),
            pltpu.SemaphoreType.DMA,
            dma_sems(parts, 2, n_line - 1),
            dma_sems(parts, 2, n_line - 1),
            pltpu.SemaphoreType.DMA,
        ],
        compiler_params=comm_params(5),
        name="recur_forward",
    )(
        tok_all,
        cot,
        to_place,
        to_stored,
        x_full,
        y_full,
        out_full,
        gain,
        gates,
        taps,
        soft,
        flags,
    )


def recur_backward(
    n_dp,
    n_line,
    mixer_in,
    to_place,
    to_stored,
    x_full,
    y_full,
    out_full,
    gates,
    taps,
    soft,
    slope,
    flags,
    kept,
):
    rows, width = mixer_in.shape
    count, own = taps.shape
    size = gates.shape[0]
    wide = own + 2 * RIM
    blocks = (wide - RIM) // size
    chunk = rows // 8

    def kernel(*refs):
        (mix, plc, sto, wx, wy, wo, gw, cw, sp, sg, fl) = refs[:11]
        (xext, y, conv_low, conv, pre_r, pre_i, rate, state) = refs[11:19]
        (gxy, gate_grads, tap_grads, decay_grad, terms) = refs[19:24]
        (mp, gm, lam, reach, gp_r, gp_i, grad, spread, rim_out, rim_in, ret_out, ret_in) = refs[
            24:36
        ]
        (tap_sums, decay_sums, ends, agg, slots, hs, hr, es, er, el) = refs[36:]
        place = Place(n_dp, n_line)
        place.meet(True)
        swap = RimSwap(place, own)
        own_cols = pl.ds(RIM, own)

        def project(i):
            here = tile_rows(i, 128)
            mp[here] = plain_dot(plc[here], mix[...]).astype(jnp.bfloat16)
            gm[here] = plain_dot(mp[here], wo[...])

        loop(rows // 128, project)

        def split(i):
            here = tile_rows(i, TILE)
            branch, slope_y = gelu_parts(y[here])
            grads = gm[here]
            put_lanes(lam, here, grads * branch)
            values = state[tile_rows(i, TILE, 8)]
            gxy[here, own:] = (grads * values * slope_y).astype(jnp.bfloat16)

        loop(rows // TILE, split)
        groups = own // LANES

        def scan(i, carry):
            here = pl.ds(chunk - 1 - i, 8, chunk)
            result = []
            for c in range(groups):
                product, message = carry[c]
                r = rate[c, here]
                value = lam[c, here] + message
                lam[c, here] = value
                reach[c, here] = product
                result.append((product * r, value * r))
            return tuple(result)

        blank = (jnp.ones((8, LANES), jnp.float32), jnp.zeros((8, LANES), jnp.float32))
        done = lax.fori_loop(0, chunk, scan, (blank,) * groups)
        for c in range(groups):
            lanes = pl.ds(c * LANES, LANES)
            ends[0, :, lanes] = done[c][0]
            ends[1, :, lanes] = done[c][1]
        product, message = jnp.ones((1, own), jnp.float32), jnp.zeros((1, own), jnp.float32)
        for j in reversed(range(8)):
            message = ends[1, j : j + 1] + ends[0, j : j + 1] * message
            product = product * ends[0, j : j + 1]
        agg[0:1] = product
        agg[1:2] = message
        swap_all = Exchange(place, "dp", agg, slots, es, er, el)
        swap_all.begin()
        swap_all.wait()
        entry = jnp.zeros((1, own), jnp.float32)
        for q in reversed(range(n_dp)):
            longer = slots[q, 1:2] + slots[q, 0:1] * entry
            entry = jnp.where(q > place.d, longer, entry)
        for ref in (tap_sums, decay_sums):
            ref[...] = jnp.zeros_like(ref)
        for ref in (gp_r, gp_i):
            ref[:, 0:RIM] = jnp.zeros((rows, RIM), jnp.bfloat16)
            ref[:, RIM + own :] = jnp.zeros((rows, RIM), jnp.bfloat16)
        grad[pl.ds(0, 8)] = jnp.zeros((8, own), jnp.float32)
        grad[pl.ds(rows + 8, 8)] = jnp.zeros((8, own), jnp.float32)
        for j in reversed(range(8)):

            def back(i, entry=entry):
                here = tile_rows(i, TILE, j * chunk)
                flag = fl[tile_rows(i, TILE, j * chunk + 8)]
                start = flag[:, 0:1] > 0.0
                values = take_lanes(lam, here) + take_lanes(reach, here) * entry
                before = moved_up(
                    state[pl.ds(pl.multiple_of(j * chunk + i * TILE, 8), TILE + 8)], 7, TILE
                )
                sr, decay, scale = rate_and_scale(pre_r[here, own_cols], sp[...], start)
                si = jax.nn.sigmoid(pre_i[here, own_cols])
                block = conv[here]
                driven = values * si
                log_grad = values * before * decay - block * driven * (decay * decay) / scale
                log_grad = jnp.where(start, 0.0, log_grad)
                inner = sr * log_grad
                gp_r[here, own_cols] = (
                    -rate_scale * sp[...] * inner * (1.0 - sr)
                ).astype(jnp.bfloat16)
                gp_i[here, own_cols] = (driven * block * (1.0 - si) * scale).astype(jnp.bfloat16)
                grad[tile_rows(i, TILE, j * chunk + 8)] = driven * scale
                decay_sums[...] += inner[:8] + inner[8:]

            loop(chunk // TILE, back)
            entry = ends[1, j : j + 1] + ends[0, j : j + 1] * entry
        decay_grad[...] = rate_scale * sg[...] * jnp.sum(decay_sums[...], axis=0, keepdims=True)

        for i in range(blocks):
            index = lax.rem(i + 2 - 2 * swap.odd, blocks)
            cols = swap.block(index, size)
            other = pl.ds(pl.multiple_of(wide + swap.first + index * size, RIM), size)
            spread[:, cols] = times_trans(gp_r[:, cols], gw[:, cols]) + times_trans(
                gp_i[:, cols], gw[:, other]
            )
            if i == 0:
                rim_out[...] = spread[:, swap.beyond].astype(jnp.bfloat16)
                rim = remote(rim_out, rim_in, hs.at[0], hr.at[0], swap.partner)
                rim.start()
        rim.wait()
        shared = pl.ds(pl.multiple_of((1 - swap.odd) * (own - RIM), RIM), RIM)

        def join(i):
            here = tile_rows(i, TILE)
            there = tile_rows(i, TILE, 8)
            grad[there] += spread[here, own_cols]
            grad[there, shared] += rim_in[here].astype(jnp.float32)

        loop(rows // TILE, join)

        near = grad[pl.ds(0, 16)]
        back_rows = jnp.zeros((8, own), jnp.float32)
        for k in range(1, count):
            masked = near * fl[pl.ds(0, 16)][:, k : k + 1]
            back_rows += cw[k : k + 1] * moved_up(masked, k, 8)
        ret_out[...] = back_rows
        ret = remote(
            ret_out,
            ret_in,
            hs.at[1],
            hr.at[1],
            (lax.rem(place.d + n_dp - 1, n_dp), place.t),
        )
        ret.start()
        for i in range(blocks):
            cols = swap.block(i, size)
            spread[0:size, cols] = trans_times(conv_low[:, cols], gp_r[:, cols])
            spread[size : 2 * size, cols] = trans_times(conv_low[:, cols], gp_i[:, cols])
        gate_grads[:, 0:own] = spread[0:size, own_cols].astype(jnp.bfloat16)
        gate_grads[:, own:] = spread[size : 2 * size, own_cols].astype(jnp.bfloat16)

        def taps_back(i, added=None):
            here = tile_rows(i, TILE)
            start = pl.ds(pl.multiple_of(i * TILE + 8, 8), TILE + 8)
            after = grad[start]
            flag = fl[start]
            behind = xext[pl.ds(pl.multiple_of(i * TILE, 16), 2 * TILE)].astype(jnp.float32)
            total = cw[0:1] * after[:TILE]
            for k in range(count):
                if k > 0:
                    masked = after * flag[:, k : k + 1]
                    total += cw[k : k + 1] * moved_up(masked, k, TILE)
                    mine = masked[:TILE]
                else:
                    mine = after[:TILE]
                term = mine * moved_up(behind, 16 - k, TILE)
                tap_sums[k] += term[:8] + term[8:]
            if added is not None:
                total = total + jnp.concatenate([jnp.zeros((8, own), jnp.float32), added], axis=0)
            gxy[here, 0:own] = total.astype(jnp.bfloat16)

        loop(rows // TILE - 1, taps_back)
        ret.wait()
        taps_back(rows // TILE - 1, jnp.where(place.d < n_dp - 1, ret_in[...], 0.0))
        tap_grads[...] = jnp.zeros_like(tap_grads)
        for k in range(count):
            tap_grads[k : k + 1] = jnp.sum(tap_sums[k], axis=0, keepdims=True)

        def restore(i):
            here = tile_rows(i, 128)
            mp[here, 0 : 2 * own] = plain_dot(sto[here], gxy[...]).astype(jnp.bfloat16)

        loop(rows // 128, restore)

        def spread_back(i):
            some = tile_rows(i, 512)
            terms[:, pl.ds(pl.multiple_of(i * 512, 512), 512)] = (
                times_trans(mp[:, 0:own], wx[some]) + times_trans(mp[:, own : 2 * own], wy[some])
            ).astype(jnp.bfloat16)

        loop(width // 512, spread_back)

    low, full = jnp.bfloat16, jnp.float32
    return pl.pallas_call(
        kernel,
        out_shape=(
            shaped((rows, 2 * own), low),
            shaped((size, 2 * own), low),
            shaped((8, own), full),
            shaped((1, own), full),
            shaped((rows, width), low),
        ),
        in_specs=[in_vmem()] * 19,
        out_specs=[in_vmem()] * 5,
        scratch_shapes=[
            pltpu.VMEM((rows, width), low),
            pltpu.VMEM((rows, own), full),
            pltpu.VMEM((own // LANES, rows, LANES), full),
            pltpu.VMEM((own // LANES, rows, LANES), full),
            pltpu.VMEM((rows, wide), low),
            pltpu.VMEM((rows, wide), low),
            pltpu.VMEM((rows + 16, own), full),
            pltpu.VMEM((rows, wide), full),
            pltpu.VMEM((rows, RIM), low),
            pltpu.VMEM((rows, RIM), low),
            pltpu.VMEM((8, own), full),
            pltpu.VMEM((8, own), full),
            pltpu.VMEM((count, 8, own), full),
            pltpu.VMEM((8, own), full),
            pltpu.VMEM((2, 8, own), full),
            pltpu.VMEM((2, own), full),
            pltpu.VMEM((n_dp, 2, own), full),
            dma_sems(2),
            dma_sems(2),
            dma_sems(n_dp),
            dma_sems(n_dp),
            pltpu.SemaphoreType.DMA,
        ],
        compiler_params=comm_params(6),
        name="recur_backward",
    )(
        mixer_in,
        to_place,
        to_stored,
        x_full,
        y_full,
        out_full,
        gates,
        taps,
        soft,
        slope,
        flags,
        *kept,
    )


def matches(mesh):
    return mesh.shape["dp"] == 8 and mesh.shape["tensor"] == 4


def local_blocks(
    tokens,
    norm_gain,
    x_weight,
    y_weight,
    conv_weight,
    recur_gate_weight,
    input_gate_weight,
    decay_param,
    out_weight,
    mlp_gain,
    gate_weight,
    up_weight,
    down_weight,
    seq_lengths,
    token_order,
    cotangent,
):
    n_dp, n_tensor = lax.axis_size("dp"), lax.axis_size("tensor")
    tensor_index = lax.axis_index("tensor")
    dp_index = lax.axis_index("dp")
    tok_rows, width = tokens.shape
    row_count = tok_rows * n_tensor
    own_width = conv_weight.shape[1]
    kernel_taps = conv_weight.shape[0]
    edge_rows = kernel_taps - 1
    dp_width = norm_gain.shape[0]
    gate_rows = recur_gate_weight.shape[0]
    own_start = tensor_index * tok_rows

    gains = jnp.concatenate([norm_gain, mlp_gain])
    spare = gate_rows * 128 - gains.shape[0]
    gains = jnp.pad(gains, (0, spare)).reshape(gate_rows, 128)
    minor = jnp.concatenate([recur_gate_weight, input_gate_weight, gains], axis=1)
    own_order = (token_order - dp_index * row_count).astype(jnp.int32)
    order_rows = jnp.broadcast_to(own_order[None, :], (8, tok_rows))
    x_full, y_full, out_full, minor_full, tok_all, order_full = first_gather(
        n_dp, n_tensor, (x_weight, y_weight, out_weight.T, minor), tokens, order_rows
    )
    late_up, late_down, _ = lax.optimization_barrier((up_weight, down_weight.T, tok_all))
    up_full = lax.all_gather(late_up, "dp", axis=0, tiled=True)
    down_full = lax.all_gather(late_down, "dp", axis=0, tiled=True)
    order_all = order_full.reshape(n_tensor, 8, tok_rows)[:, 0].reshape(row_count)
    both_gates = minor_full[:, : 2 * own_width]
    gain_rows = minor_full[:, 2 * own_width :].reshape(n_dp, -1)
    first_gain = gain_rows[:, :dp_width].reshape(1, width).astype(jnp.float32)
    second_gain = gain_rows[:, dp_width : 2 * dp_width].reshape(1, width).astype(jnp.float32)
    block_size = both_gates.shape[0]
    row_index = jnp.arange(row_count, dtype=jnp.int32)
    hits = row_index[:, None] == order_all[None, :]
    to_place = hits.astype(jnp.bfloat16)
    to_stored = (order_all[:, None] == row_index[None, :]).astype(jnp.bfloat16)
    places = dp_index * row_count + jnp.arange(-8, row_count + 8, dtype=jnp.int32)
    inside = (jnp.arange(row_count + 16) >= 8) & (jnp.arange(row_count + 16) < row_count + 8)
    ends = jnp.cumsum(seq_lengths)
    segment = segment_of(places, ends)
    starts = (places == 0) | (segment != segment_of(places - 1, ends))
    columns = [starts] + [
        segment_of(places - shift, ends) == segment for shift in range(1, kernel_taps)
    ]
    columns += [jnp.zeros_like(starts)] * (8 - len(columns))
    flags = (jnp.stack(columns, axis=1) & inside[:, None]).astype(jnp.float32)
    live_stored = (order_all + dp_index * row_count < ends[-1]).astype(jnp.float32)
    live_own = (token_order < ends[-1]).astype(jnp.float32)
    soft = jax.nn.softplus(-decay_param).reshape(1, own_width)
    slope = jax.nn.sigmoid(-decay_param).reshape(1, own_width)
    zero_rim = jnp.zeros((block_size, RIM), jnp.bfloat16)
    gates_wide = jnp.concatenate(
        [
            zero_rim,
            both_gates[:, :own_width],
            zero_rim,
            zero_rim,
            both_gates[:, own_width:],
            zero_rim,
        ],
        axis=1,
    )
    def glu(gate_pre, up_pre):
        return gelu_tanh(gate_pre) * up_pre

    hidden_place, *kept, merged_stored, mixer_terms, cot_all = recur_forward(
        n_dp,
        n_tensor,
        tok_all,
        cotangent,
        to_place,
        to_stored,
        x_full,
        y_full,
        out_full,
        first_gain,
        gates_wide,
        conv_weight,
        soft,
        flags,
    )
    after_own, hidden_two, gate_full = middle_gather(
        n_dp, n_tensor, mixer_terms, tokens, second_gain, (gate_weight,)
    )
    gate_pre = plain_dot(hidden_two, gate_full)
    up_pre = plain_dot(hidden_two, up_full)
    glu_out, glu_pull = jax.vjp(glu, gate_pre, up_pre)
    product = glu_out.astype(jnp.bfloat16)
    down_in = (cot_all.astype(jnp.float32) * live_stored[:, None]).astype(jnp.bfloat16)
    grad_in_own = (cotangent.astype(jnp.float32) * live_own[:, None]).astype(jnp.bfloat16)
    grad_down = trans_times(down_in, product).astype(jnp.bfloat16)
    down_sum = lax.psum_scatter(grad_down, "dp", scatter_dimension=0, tiled=True)
    down_in, _ = lax.optimization_barrier((down_in, grad_down))
    grad_product = plain_dot(down_in, down_full)
    grad_gate_pre, grad_up_pre = glu_pull(grad_product)
    grad_gate_pre = grad_gate_pre.astype(jnp.bfloat16)
    grad_up_pre = grad_up_pre.astype(jnp.bfloat16)
    grad_gate = trans_times(hidden_two, grad_gate_pre).astype(jnp.bfloat16)
    grad_up = trans_times(hidden_two, grad_up_pre).astype(jnp.bfloat16)
    back_terms = (
        times_trans(grad_gate_pre, gate_full) + times_trans(grad_up_pre, up_full)
    ).astype(jnp.bfloat16)
    feed_terms = times_trans(product, down_full).astype(jnp.bfloat16)
    up_sum = lax.psum_scatter(grad_up, "dp", scatter_dimension=0, tiled=True)
    grad_after_own, second_part, mixer_in, gate_sum = middle_sums(
        n_dp, n_tensor, back_terms, after_own, second_gain, grad_in_own, (grad_gate,)
    )
    feed_out = lax.psum_scatter(
        lax.optimization_barrier((feed_terms, mixer_in))[0],
        "tensor",
        scatter_dimension=0,
        tiled=True,
    ).astype(jnp.float32)
    output = ((after_own + feed_out) * live_own[:, None]).astype(jnp.bfloat16)

    grad_xy, gate_grads, tap_grads, decay_grad, one_terms = recur_backward(
        n_dp,
        n_tensor,
        mixer_in,
        to_place,
        to_stored,
        x_full,
        y_full,
        out_full,
        gates_wide,
        conv_weight,
        soft,
        slope,
        flags,
        kept,
    )
    grad_out_mat = trans_times(mixer_in, merged_stored).astype(jnp.bfloat16)
    grad_xy_mat = trans_times(hidden_place, grad_xy).astype(jnp.bfloat16)
    small = jnp.concatenate(
        [
            second_part,
            tap_grads[:kernel_taps].reshape(1, -1),
            jnp.pad(decay_grad, ((0, 0), (0, width - own_width))),
            jnp.zeros((1, width), jnp.float32),
        ],
        axis=0,
    )
    grad_tokens, small_sum, gain_sums, xy_sum, out_sum, gates_sum = last_sums(
        n_dp,
        n_tensor,
        one_terms,
        tokens,
        first_gain,
        grad_after_own,
        small,
        (grad_xy_mat, grad_out_mat, gate_grads),
    )
    xy_sum, gates_sum = xy_sum.astype(jnp.float32), gates_sum.astype(jnp.float32)
    own_gains = lax.dynamic_slice_in_dim(gain_sums, dp_index * dp_width, dp_width, 1)
    return (
        output,
        grad_tokens,
        own_gains[1],
        xy_sum[:, :own_width],
        xy_sum[:, own_width:],
        small_sum[1].reshape(kernel_taps, own_width),
        gates_sum[:, :own_width],
        gates_sum[:, own_width:],
        small_sum[2, :own_width],
        out_sum.astype(jnp.float32).T,
        own_gains[0],
        gate_sum.astype(jnp.float32),
        up_sum.astype(jnp.float32),
        down_sum.astype(jnp.float32).T,
    )


def solution(mesh):
    in_specs = (
        P(("dp", "tensor"), None),
        P("dp"),
        P("dp", "tensor"),
        P("dp", "tensor"),
        P(None, "tensor"),
        P("dp", "tensor"),
        P("dp", "tensor"),
        P("tensor"),
        P("tensor", "dp"),
        P("dp"),
        P("dp", "tensor"),
        P("dp", "tensor"),
        P("tensor", "dp"),
        P(),
        P(("dp", "tensor")),
        P(("dp", "tensor"), None),
    )
    out_specs = (
        P(("dp", "tensor"), None),
        P(("dp", "tensor"), None),
        P("dp"),
        P("dp", "tensor"),
        P("dp", "tensor"),
        P(None, "tensor"),
        P("dp", "tensor"),
        P("dp", "tensor"),
        P("tensor"),
        P("tensor", "dp"),
        P("dp"),
        P("dp", "tensor"),
        P("dp", "tensor"),
        P("tensor", "dp"),
    )
    fits = matches(mesh)
    local = local_blocks if fits else local_general
    return jax.shard_map(local, mesh=mesh, in_specs=in_specs, out_specs=out_specs, check_vma=False)
```

```python
import jax
import jax.numpy as jnp
from jax import lax
from jax.experimental import pallas as pl
from jax.experimental.pallas import tpu as pltpu
from jax.sharding import PartitionSpec as P

epsilon = 1e-06
rate_scale = 8.0


def from_behind(block, axis, distance):
    devices = range(lax.axis_size(axis))
    route = [(i - distance, i) for i in devices if i - distance in devices]
    return lax.ppermute(block, axis, route)


def extended_2(array, sides, width):
    for axis, dim in sides:
        size, length = (lax.axis_size(axis), array.shape[dim])
        up = [(i, (i + 1) % size) for i in range(size - 1)]
        down = [(j, i) for i, j in up]
        last = lax.slice_in_dim(array, length - width, length, axis=dim)
        leading = lax.slice_in_dim(array, 0, width, axis=dim)
        before = lax.ppermute(last, axis, up)
        after = lax.ppermute(leading, axis, down)
        array = jnp.concatenate([before, array, after], axis=dim)
    return array


def entering(value, axis, join, neutral, backward):
    count, mine = (lax.axis_size(axis), lax.axis_index(axis))
    pieces = jax.tree.map(lambda part: lax.all_gather(part, axis), value)
    if backward:
        pieces = jax.tree.map(lambda part: part[::-1], pieces)
        mine = count - 1 - mine
    total = jax.tree.map(
        lambda part, zero: jnp.full_like(part, 0) + jnp.asarray(zero, part.dtype), value, neutral
    )

    def lap(position, total):
        longer = join(total, jax.tree.map(lambda part: part[position], pieces))
        return jax.tree.map(lambda new, old: jnp.where(position < mine, new, old), longer, total)

    return lax.fori_loop(0, count - 1, lap, total)


def rms_scale(values, gain):
    return values * lax.rsqrt(jnp.mean(values * values, axis=-1, keepdims=True) + epsilon) * gain


def norm_back(values, gain, grad):
    inv_root = lax.rsqrt(jnp.mean(values * values, axis=-1, keepdims=True) + epsilon)
    normed = values * inv_root
    upstream = grad * gain
    grad_values = inv_root * (
        upstream - normed * jnp.mean(upstream * normed, axis=-1, keepdims=True)
    )
    return (grad_values, normed)


def segment_of(places, ends):
    return jnp.sum((ends[None, :] <= places[:, None]).astype(jnp.int32), axis=1)


def pair_step(early, later):
    return (early[0] * later[0], later[0] * early[1] + later[1])


def plain_dot(left, right):
    return jnp.dot(left, right, preferred_element_type=jnp.float32)


def times_trans(left, right):
    return lax.dot_general(
        left, right, (((1,), (1,)), ((), ())), preferred_element_type=jnp.float32
    )


def trans_times(left, right):
    return lax.dot_general(
        left, right, (((0,), (0,)), ((), ())), preferred_element_type=jnp.float32
    )


def gelu_tanh(values):
    return jax.nn.gelu(values, approximate=True)


def collect(
    norm_gain,
    mlp_gain,
    x_weight,
    y_weight,
    recur_gate_weight,
    input_gate_weight,
    gate_weight,
    up_weight,
    out_weight,
    down_weight,
):
    return (
        lax.all_gather(norm_gain, "dp", axis=0, tiled=True),
        lax.all_gather(mlp_gain, "dp", axis=0, tiled=True),
        lax.all_gather(x_weight, "dp", axis=0, tiled=True),
        lax.all_gather(y_weight, "dp", axis=0, tiled=True),
        lax.all_gather(recur_gate_weight, "dp", axis=0, tiled=True),
        lax.all_gather(input_gate_weight, "dp", axis=0, tiled=True),
        lax.all_gather(gate_weight, "dp", axis=0, tiled=True),
        lax.all_gather(up_weight, "dp", axis=0, tiled=True),
        lax.all_gather(out_weight, "dp", axis=1, tiled=True),
        lax.all_gather(down_weight, "dp", axis=1, tiled=True),
    )


def row_sums(term_rows, tok_rows):
    return lax.psum_scatter(
        term_rows(jnp.int32(0), lax.axis_size("tensor") * tok_rows).astype(jnp.bfloat16),
        "tensor",
        scatter_dimension=0,
        tiled=True,
    ).astype(jnp.float32)


def spread_rows(values):
    return lax.all_gather(values, "tensor", axis=0, tiled=True)


def local_general(
    tokens,
    norm_gain,
    x_weight,
    y_weight,
    conv_weight,
    recur_gate_weight,
    input_gate_weight,
    decay_param,
    out_weight,
    mlp_gain,
    gate_weight,
    up_weight,
    down_weight,
    seq_lengths,
    token_order,
    cotangent,
):
    n_tensor = lax.axis_size("tensor")
    tensor_index = lax.axis_index("tensor")
    dp_index = lax.axis_index("dp")
    tok_rows = tokens.shape[0]
    row_count = tok_rows * n_tensor
    own_width = conv_weight.shape[1]
    kernel_taps = conv_weight.shape[0]
    edge_rows = kernel_taps - 1
    dp_width = norm_gain.shape[0]
    own_start = tensor_index * tok_rows
    shards = (
        norm_gain,
        mlp_gain,
        x_weight,
        y_weight,
        recur_gate_weight,
        input_gate_weight,
        gate_weight,
        up_weight,
        out_weight,
        down_weight,
    )
    (
        gain_one,
        gain_two,
        x_full,
        y_full,
        recur_full,
        input_full,
        gate_full,
        up_full,
        out_full,
        down_full,
    ) = collect(*shards)
    block_size = recur_full.shape[0]
    first_gain = gain_one.astype(jnp.float32)
    second_gain = gain_two.astype(jnp.float32)
    both_gates = jnp.concatenate([recur_full, input_full], axis=1)
    tok_own = tokens.astype(jnp.float32)
    own_order = token_order - dp_index * row_count
    first_rows = rms_scale(tok_own, first_gain).astype(jnp.bfloat16)
    first_all, cot_all, order_all = (
        lax.all_gather(first_rows, "tensor", axis=0, tiled=True),
        lax.all_gather(cotangent, "tensor", axis=0, tiled=True),
        lax.all_gather(own_order, "tensor", axis=0, tiled=True),
    )
    row_index = jnp.arange(row_count, dtype=jnp.int32)
    inverse = jnp.zeros((row_count,), jnp.int32).at[order_all].set(row_index)
    hidden_place = jnp.take(first_all, inverse, axis=0)
    places = dp_index * row_count + row_index
    ends = jnp.cumsum(seq_lengths)
    segment = segment_of(places, ends)
    starts = (places == 0) | (segment != segment_of(places - 1, ends))
    live = (places < ends[-1]).astype(jnp.float32)
    live_stored = jnp.take(live, order_all, axis=0)
    same = [
        (segment_of(places - shift, ends) == segment).astype(jnp.float32)
        for shift in range(kernel_taps)
    ]
    low_edge = tensor_index * own_width
    own_blocks = (low_edge + jnp.arange(own_width, dtype=jnp.int32)) // block_size
    first_block = low_edge // block_size
    block_count = own_width // block_size + 2

    def block_start(index):
        return (first_block + index) * block_size - low_edge + block_size

    def block_mask(index):
        inside = own_blocks == first_block + index
        return jnp.concatenate([inside, inside])

    def convolve(extended, kernel):
        return sum(
            (
                kernel[shift][None, :]
                * extended[edge_rows - shift : edge_rows - shift + row_count]
                * same[shift][:, None]
                for shift in range(kernel_taps)
            )
        )

    def gates(conv_vals, pre_recur, pre_input, decay_vals):
        log_rate = -rate_scale * jax.nn.sigmoid(pre_recur) * jax.nn.softplus(-decay_vals)
        decay_rate = jnp.where(starts[:, None], 0.0, jnp.exp(log_rate))
        scale_in = jnp.where(starts[:, None], 1.0, jnp.sqrt(-jnp.expm1(2.0 * log_rate)))
        return (decay_rate, conv_vals * jax.nn.sigmoid(pre_input) * scale_in)

    def glu(gate_pre, up_pre):
        return gelu_tanh(gate_pre) * up_pre

    x_branch = plain_dot(hidden_place, x_full).astype(jnp.bfloat16)
    y_before = plain_dot(hidden_place, y_full)
    previous = from_behind(x_branch[row_count - edge_rows :], "dp", 1)
    extended = jnp.concatenate([previous, x_branch], axis=0).astype(jnp.float32)
    conv_out = convolve(extended, conv_weight)
    conv_wide = extended_2(conv_out.astype(jnp.bfloat16), (("tensor", 1),), block_size)
    pre_both = jnp.zeros((row_count, 2 * own_width), jnp.float32)
    for index in range(block_count):
        piece = lax.dynamic_slice_in_dim(conv_wide, block_start(index), block_size, 1)
        pre_both = pre_both + jnp.where(
            block_mask(index)[None, :], plain_dot(piece, both_gates), 0.0
        )
    (decay_rate, driven), gate_pull = jax.vjp(
        gates, conv_out, pre_both[:, :own_width], pre_both[:, own_width:], decay_param
    )
    cum_rate, local_state = lax.associative_scan(pair_step, (decay_rate, driven), axis=0)
    ident = (jnp.ones((own_width,), jnp.float32), jnp.zeros((own_width,), jnp.float32))
    rate_in, state_in = entering((cum_rate[-1], local_state[-1]), "dp", pair_step, ident, False)
    state = local_state + cum_rate * state_in[None, :]
    y_branch = gelu_tanh(y_before)
    merged = (state * y_branch).astype(jnp.bfloat16)
    merged_stored = jnp.take(merged, order_all, axis=0)

    def mixer_rows(begin, number):
        return plain_dot(merged_stored, out_full)

    after_own = tok_own + row_sums(mixer_rows, tok_rows)
    hidden_two = spread_rows(rms_scale(after_own, second_gain).astype(jnp.bfloat16))
    gate_pre = plain_dot(hidden_two, gate_full)
    up_pre = plain_dot(hidden_two, up_full)
    glu_out, glu_pull = jax.vjp(glu, gate_pre, up_pre)
    product = glu_out.astype(jnp.bfloat16)

    def down_rows(begin, number):
        return plain_dot(product, down_full)

    feed_out = row_sums(down_rows, tok_rows)
    live_own = lax.dynamic_slice_in_dim(live_stored, own_start, tok_rows, 0)
    output = ((after_own + feed_out) * live_own[:, None]).astype(jnp.bfloat16)
    grad_out = cot_all.astype(jnp.float32) * live_stored[:, None]
    fresh = lax.optimization_barrier((shards, grad_out))[0]
    (
        gain_one,
        gain_two,
        x_full,
        y_full,
        recur_full,
        input_full,
        gate_full,
        up_full,
        out_full,
        down_full,
    ) = collect(*fresh)
    first_gain = gain_one.astype(jnp.float32)
    second_gain = gain_two.astype(jnp.float32)
    both_gates = jnp.concatenate([recur_full, input_full], axis=1)
    down_in = grad_out.astype(jnp.bfloat16)
    grad_down = trans_times(product, down_in)
    grad_product = times_trans(down_in, down_full)
    grad_gate_pre, grad_up_pre = glu_pull(grad_product)
    grad_gate_pre = grad_gate_pre.astype(jnp.bfloat16)
    grad_up_pre = grad_up_pre.astype(jnp.bfloat16)
    grad_gate = trans_times(hidden_two, grad_gate_pre)
    grad_up = trans_times(hidden_two, grad_up_pre)

    def feed_rows(begin, number):
        return times_trans(grad_gate_pre, gate_full) + times_trans(grad_up_pre, up_full)

    grad_out_own = lax.dynamic_slice_in_dim(grad_out, own_start, tok_rows, 0)
    grad_two_own = row_sums(feed_rows, tok_rows)
    grad_norm_own, normed_two = norm_back(after_own, second_gain, grad_two_own)
    second_part = jnp.sum(grad_two_own * normed_two, axis=0)
    grad_after_own = grad_out_own + grad_norm_own
    mixer_in = spread_rows(grad_after_own.astype(jnp.bfloat16))
    grad_out_mat = trans_times(merged_stored, mixer_in)
    grad_merged = jnp.take(times_trans(mixer_in, out_full), inverse, axis=0)
    grad_state = grad_merged * y_branch
    gelu_pull = jax.vjp(gelu_tanh, y_before)[1]
    grad_y_before = gelu_pull(grad_merged * state)[0].astype(jnp.bfloat16)
    rate_next = jnp.concatenate([decay_rate[1:], jnp.ones((1, own_width), jnp.float32)], axis=0)
    rev_rate, local_lam = lax.associative_scan(
        pair_step, (rate_next, grad_state), reverse=True, axis=0
    )
    head_rate = decay_rate[0] * rev_rate[0]
    head_lam = decay_rate[0] * local_lam[0]
    factor_in, lam_in = entering((head_rate, head_lam), "dp", pair_step, ident, True)
    lam = local_lam + rev_rate * lam_in[None, :]
    state_prev = jnp.concatenate([state_in[None, :], state[:-1]], axis=0)
    grad_conv_local, grad_pre_recur, grad_pre_input, grad_decay_own = gate_pull(
        (lam * state_prev, lam)
    )
    grad_pre = jnp.concatenate([grad_pre_recur, grad_pre_input], axis=1).astype(jnp.bfloat16)
    grad_both = jnp.zeros((block_size, 2 * own_width), jnp.float32)
    grad_wide = jnp.zeros((row_count, own_width + 2 * block_size), jnp.float32)
    for index in range(block_count):
        begin = block_start(index)
        piece = lax.dynamic_slice_in_dim(conv_wide, begin, block_size, 1)
        masked = jnp.where(block_mask(index)[None, :], grad_pre, jnp.zeros((), jnp.bfloat16))
        grad_both = grad_both + trans_times(piece, masked)
        added = lax.dynamic_slice_in_dim(grad_wide, begin, block_size, 1) + times_trans(
            masked, both_gates
        )
        grad_wide = lax.dynamic_update_slice_in_dim(grad_wide, added, begin, 1)
    grad_recur = grad_both[:, :own_width]
    grad_input = grad_both[:, own_width:]
    rims = jnp.concatenate(
        [grad_wide[:, :block_size], grad_wide[:, own_width + block_size :]], axis=1
    )
    arrived = extended_2(rims.astype(jnp.bfloat16), (("tensor", 1),), block_size).astype(rims.dtype)
    from_lower = jnp.pad(arrived[:, :block_size], ((0, 0), (0, own_width - block_size)))
    from_upper = jnp.pad(arrived[:, 3 * block_size :], ((0, 0), (own_width - block_size, 0)))
    grad_conv = (
        grad_conv_local
        + grad_wide[:, block_size : block_size + own_width]
        + from_lower
        + from_upper
    )
    conv_pull = jax.vjp(convolve, extended, conv_weight)[1]
    grad_extended, grad_kernel = conv_pull(grad_conv)
    returned = from_behind(grad_extended[:edge_rows], "dp", -1)
    grad_x_branch = grad_extended[edge_rows:] + jnp.concatenate(
        [jnp.zeros((row_count - edge_rows, own_width), jnp.float32), returned], axis=0
    )
    grad_x_low = grad_x_branch.astype(jnp.bfloat16)
    grad_x_stored = jnp.take(grad_x_low, order_all, axis=0)
    grad_y_stored = jnp.take(grad_y_before, order_all, axis=0)
    grad_x_mat = trans_times(first_all, grad_x_stored)
    grad_y_mat = trans_times(first_all, grad_y_stored)

    def mixer_back_rows(begin, number):
        return times_trans(grad_x_stored, x_full) + times_trans(grad_y_stored, y_full)

    grad_one_own = row_sums(mixer_back_rows, tok_rows)
    grad_norm_one, normed_one = norm_back(tok_own, first_gain, grad_one_own)
    first_part = jnp.sum(grad_one_own * normed_one, axis=0)
    grad_tokens = grad_after_own + grad_norm_one
    chosen = jnp.arange(n_tensor, dtype=jnp.int32) == tensor_index
    kernel_tile = jnp.where(chosen[:, None, None], grad_kernel[None, :, :], 0.0)
    decay_tile = jnp.where(chosen[:, None], grad_decay_own[None, :], 0.0)
    small = lax.psum((first_part, second_part, kernel_tile, decay_tile), ("dp", "tensor"))
    grad_first_gain = lax.dynamic_slice_in_dim(small[0], dp_index * dp_width, dp_width, 0)
    grad_second_gain = lax.dynamic_slice_in_dim(small[1], dp_index * dp_width, dp_width, 0)
    grad_kernel_sum = lax.dynamic_index_in_dim(small[2], tensor_index, 0, keepdims=False)
    grad_decay = lax.dynamic_index_in_dim(small[3], tensor_index, 0, keepdims=False)
    sums = (
        lax.psum_scatter(
            grad_x_mat.astype(jnp.bfloat16), "dp", scatter_dimension=0, tiled=True
        ).astype(jnp.float32),
        lax.psum_scatter(
            grad_y_mat.astype(jnp.bfloat16), "dp", scatter_dimension=0, tiled=True
        ).astype(jnp.float32),
        lax.psum_scatter(
            grad_recur.astype(jnp.bfloat16), "dp", scatter_dimension=0, tiled=True
        ).astype(jnp.float32),
        lax.psum_scatter(
            grad_input.astype(jnp.bfloat16), "dp", scatter_dimension=0, tiled=True
        ).astype(jnp.float32),
        lax.psum_scatter(
            grad_gate.astype(jnp.bfloat16), "dp", scatter_dimension=0, tiled=True
        ).astype(jnp.float32),
        lax.psum_scatter(
            grad_up.astype(jnp.bfloat16), "dp", scatter_dimension=0, tiled=True
        ).astype(jnp.float32),
        lax.psum_scatter(
            grad_out_mat.astype(jnp.bfloat16), "dp", scatter_dimension=1, tiled=True
        ).astype(jnp.float32),
        lax.psum_scatter(
            grad_down.astype(jnp.bfloat16), "dp", scatter_dimension=1, tiled=True
        ).astype(jnp.float32),
    )
    return (
        output,
        grad_tokens,
        grad_first_gain,
        sums[0],
        sums[1],
        grad_kernel_sum,
        sums[2],
        sums[3],
        grad_decay,
        sums[6],
        grad_second_gain,
        sums[4],
        sums[5],
        sums[7],
    )


MESH = pl.DeviceIdType.MESH
VMEM_BYTES = 60 * 2**20


def remote(src, dst, send, recv, device):
    return pltpu.make_async_remote_copy(
        src_ref=src,
        dst_ref=dst,
        send_sem=send,
        recv_sem=recv,
        device_id=device,
        device_id_type=MESH,
    )


class Place:
    def __init__(self, n_dp, n_line):
        self.n_dp, self.n_line = n_dp, n_line
        self.d, self.t = lax.axis_index("dp"), lax.axis_index("tensor")
        self.core = lax.rem(self.d, 2)
        self.x = lax.rem(lax.div(self.d, 2), 2)
        self.y = lax.div(self.d, 4)

    def chip(self, flip_x, flip_y, flip_core=0):
        x = 1 - self.x if flip_x else self.x
        y = 1 - self.y if flip_y else self.y
        core = 1 - self.core if flip_core else self.core
        return y * 4 + x * 2 + core

    def at(self, flip_x=0, flip_y=0, flip_core=0):
        return (self.chip(flip_x, flip_y, flip_core), self.t)

    def up(self):
        return (self.d, lax.rem(self.t + 1, self.n_line))

    def down(self):
        return (self.d, lax.rem(self.t + self.n_line - 1, self.n_line))

    def meet(self, everyone=False):
        barrier = pltpu.get_barrier_semaphore()

        def greet(device):
            pl.semaphore_signal(barrier, inc=1, device_id=device, device_id_type=MESH)

        if everyone:
            for i in range(1, self.n_dp):
                greet((lax.rem(self.d + i, self.n_dp), self.t))
            for i in range(1, self.n_line):
                greet((self.d, lax.rem(self.t + i, self.n_line)))
            pl.semaphore_wait(barrier, self.n_dp + self.n_line - 2)
            return
        for flips in ((1, 0), (0, 1), (0, 0, 1)):
            greet(self.at(*flips))
        below, above = self.t > 0, self.t < self.n_line - 1

        @pl.when(below)
        def _():
            greet(self.down())

        @pl.when(above)
        def _():
            greet(self.up())

        pl.semaphore_wait(barrier, 3 + below.astype(jnp.int32) + above.astype(jnp.int32))


class GatherPlane:
    def __init__(self, place, src, dst, send, recv, local):
        self.p, self.src, self.dst = place, src, dst
        self.rows = src.shape[0]
        self.send, self.recv, self.local = send, recv, local

    def block(self, fx, fy, fc=0, part=None):
        first = self.p.chip(fx, fy, fc) * self.rows
        size = self.rows
        if part is not None:
            size = self.rows // 2
            first = first + part * size
        return self.dst.at[pl.ds(pl.multiple_of(first, 16), size)]

    def copy(self, i, src, dst, device):
        return remote(src, dst, self.send.at[i], self.recv.at[i], device)

    def mine(self):
        return pltpu.make_async_copy(self.src, self.block(0, 0), self.local)

    def outgoing(self, i):
        at, block = self.p.at, self.block
        if i == 0:
            return self.copy(0, self.src, block(0, 0), at(1, 0))
        if i == 1:
            return self.copy(1, self.src, block(0, 0), at(0, 1))
        if i == 2:
            return self.copy(2, self.src, block(0, 0), at(0, 0, 1))
        if i == 3:
            return self.copy(3, block(1, 0, 0, 0), block(1, 0, 0, 0), at(0, 1))
        if i == 4:
            return self.copy(4, block(0, 1, 0, 1), block(0, 1, 0, 1), at(1, 0))
        spot = ((1, 0), (0, 1), (1, 1, 0, 0), (1, 1, 0, 1))[i - 5]
        return self.copy(i, block(*spot), block(*spot), at(0, 0, 1))

    def arrive(self, i):
        spot = (
            (1, 0),
            (0, 1),
            (0, 0, 1),
            (1, 1, 0, 0),
            (1, 1, 0, 1),
            (1, 0, 1),
            (0, 1, 1),
            (1, 1, 1, 0),
            (1, 1, 1, 1),
        )[i]
        here = self.block(*spot)
        self.copy(i, here, here, self.p.at(0, 0, 1)).wait_recv()

    def begin(self):
        self.mine().start()
        for i in (0, 1, 2):
            self.outgoing(i).start()

    def forward(self):
        self.arrive(0)
        self.outgoing(3).start()
        self.arrive(1)
        self.outgoing(4).start()
        self.outgoing(5).start()
        self.outgoing(6).start()

    def share(self):
        self.arrive(3)
        self.outgoing(7).start()
        self.arrive(4)
        self.outgoing(8).start()

    def finish(self):
        for i in (2, 5, 6, 7, 8):
            self.arrive(i)
        for i in range(9):
            self.outgoing(i).wait_send()
        self.mine().wait()


class GatherLine:
    def __init__(self, place, dst, rows, begin, span, send, recv):
        self.p, self.dst, self.rows = place, dst, rows
        self.begin, self.span = begin, span
        self.send, self.recv = send, recv
        self.last = place.n_line - 1

    def block(self, owner):
        first = owner * self.rows + self.begin
        return self.dst.at[pl.ds(pl.multiple_of(first, 8), self.span)]

    def copy(self, way, k, owner, source=None):
        to = self.p.up() if way == 0 else self.p.down()
        block = self.block(owner)
        return remote(
            block if source is None else source,
            block,
            self.send.at[way, k],
            self.recv.at[way, k],
            to,
        )

    def step(self, k, source=None):
        t, last = self.p.t, self.last
        if k > 0:
            self.arrive(k - 1)

        @pl.when((t < last) & (t >= k))
        def _():
            self.copy(0, k, t - k, source).start()

        @pl.when((t > 0) & (t + k <= last))
        def _():
            self.copy(1, k, t + k, source).start()

    def arrive(self, k):
        t, last = self.p.t, self.last

        @pl.when(t >= k + 1)
        def _():
            self.copy(0, k, t - 1 - k).wait_recv()

        @pl.when(t + k + 1 <= last)
        def _():
            self.copy(1, k, t + 1 + k).wait_recv()

    def finish(self):
        t, last = self.p.t, self.last
        self.arrive(last - 1)
        for k in range(last):

            @pl.when((t < last) & (t >= k))
            def _():
                self.copy(0, k, t - k).wait_send()

            @pl.when((t > 0) & (t + k <= last))
            def _():
                self.copy(1, k, t + k).wait_send()


class ReduceLine:
    def __init__(self, place, terms, rows, begin, span, stage, inbox, send, recv):
        self.p, self.terms, self.rows = place, terms, rows
        self.begin, self.span = begin, span
        self.stage, self.inbox = stage, inbox
        self.send, self.recv = send, recv
        self.last = place.n_line - 1

    def own(self, owner):
        first = owner * self.rows + self.begin
        return self.terms.at[pl.ds(pl.multiple_of(first, 16), self.span)]

    def copy(self, way, j, source):
        to = self.p.up() if way == 0 else self.p.down()
        return remote(
            source, self.inbox.at[way, j], self.send.at[way, j], self.recv.at[way, j], to
        )

    def ends(self):
        t, last = self.p.t, self.last

        @pl.when(t == 0)
        def _():
            for j in range(last):
                self.copy(0, j, self.own(last - j)).start()

        @pl.when(t == last)
        def _():
            for j in range(last):
                self.copy(1, j, self.own(j)).start()

    def sent(self):
        t, last = self.p.t, self.last

        @pl.when(t == 0)
        def _():
            for j in range(last):
                self.copy(0, j, self.own(last - j)).wait_send()

        @pl.when(t == last)
        def _():
            for j in range(last):
                self.copy(1, j, self.own(j)).wait_send()

    def hand_on(self, way, j):
        term = self.own(self.last - j if way == 0 else j)
        self.copy(way, j, term).wait_recv()
        self.stage[way, j] = (
            term[...].astype(jnp.float32) + self.inbox[way, j].astype(jnp.float32)
        ).astype(jnp.bfloat16)
        self.copy(way, j, self.stage.at[way, j]).start()

    def hop(self, k):
        t, last = self.p.t, self.last

        @pl.when(t == k + 1)
        def _():
            for j in range(last - 1 - k):
                self.hand_on(0, j)

        @pl.when(t == last - 1 - k)
        def _():
            for j in range(last - 1 - k):
                self.hand_on(1, j)

    def total(self, result):
        t, last = self.p.t, self.last
        result[...] = self.own(t)[...].astype(jnp.float32)

        @pl.when(t > 0)
        def _():
            j = last - t
            self.copy(0, j, self.stage.at[0, 0]).wait_recv()
            result[...] += self.inbox[0, j].astype(jnp.float32)

        @pl.when(t < last)
        def _():
            self.copy(1, t, self.stage.at[0, 0]).wait_recv()
            result[...] += self.inbox[1, t].astype(jnp.float32)

    def finish(self):
        t, last = self.p.t, self.last
        for j in range(last - 1):

            @pl.when((t > 0) & (t < last - j))
            def _():
                self.copy(0, j, self.stage.at[0, j]).wait_send()

            @pl.when((t < last) & (t > j))
            def _():
                self.copy(1, j, self.stage.at[1, j]).wait_send()


def add_rows(into, other, result=None):
    result = into if result is None else result

    def tile(i, carry):
        rows = pl.ds(pl.multiple_of(i * 16, 16), 16)
        result[rows] = (
            into[rows].astype(jnp.float32) + other[rows].astype(jnp.float32)
        ).astype(result.dtype)
        return carry

    lax.fori_loop(0, into.shape[0] // 16, tile, None)


class ReducePlane:
    chips = ((0, 0), (1, 0), (0, 1), (1, 1))

    def __init__(self, place, terms, scratch):
        self.p, self.terms = place, terms
        self.held, self.near, self.along, self.last, self.send, self.recv, self.local = scratch
        self.rows = self.held.shape[1]
        self.half = self.rows // 2

    @staticmethod
    def scratch(rows, width):
        return [
            pltpu.VMEM((4, rows, width), jnp.bfloat16),
            pltpu.VMEM((4, rows, width), jnp.bfloat16),
            pltpu.VMEM((4, rows // 2, width), jnp.bfloat16),
            pltpu.VMEM((2, rows // 2, width), jnp.bfloat16),
            pltpu.SemaphoreType.DMA((10,)),
            pltpu.SemaphoreType.DMA((10,)),
            pltpu.SemaphoreType.DMA((4,)),
        ]

    def block(self, k, other):
        first = self.p.chip(*self.chips[k], other) * self.rows
        return self.terms.at[pl.ds(pl.multiple_of(first, 16), self.rows)]

    def half_of(self, k, part):
        return self.held.at[k, pl.ds(part * self.half, self.half)]

    def load(self, k):
        return pltpu.make_async_copy(self.block(k, 0), self.held.at[k], self.local.at[k])

    def copy(self, i):
        at = self.p.at
        if i < 4:
            src, dst, to = self.block(i, 1), self.near.at[i], at(0, 0, 1)
        elif i < 8:
            src, to = (
                (self.half_of(1, 0), at(1, 0)),
                (self.half_of(3, 0), at(1, 0)),
                (self.half_of(2, 1), at(0, 1)),
                (self.half_of(3, 1), at(0, 1)),
            )[i - 4]
            dst = self.along.at[i - 4]
        else:
            src, to = ((self.half_of(2, 0), at(0, 1)), (self.half_of(1, 1), at(1, 0)))[i - 8]
            dst = self.last.at[i - 8]
        return remote(src, dst, self.send.at[i], self.recv.at[i], to)

    def begin(self):
        for k in (3, 1, 2, 0):
            self.copy(k).start()
            self.load(k).start()

    def cores(self):
        for k in (3, 1, 2, 0):
            self.load(k).wait()
            self.copy(k).wait_recv()
            add_rows(self.held.at[k], self.near.at[k])
            if k == 3:
                self.copy(5).start()
                self.copy(7).start()
            elif k == 1:
                self.copy(4).start()
            elif k == 2:
                self.copy(6).start()

    def turn(self):
        self.copy(5).wait_recv()
        add_rows(self.half_of(2, 0), self.along.at[1])
        self.copy(8).start()
        self.copy(7).wait_recv()
        add_rows(self.half_of(1, 1), self.along.at[3])
        self.copy(9).start()
        self.copy(4).wait_recv()
        add_rows(self.half_of(0, 0), self.along.at[0])
        self.copy(6).wait_recv()
        add_rows(self.half_of(0, 1), self.along.at[2])

    def finish(self, result):
        for part in (0, 1):
            self.copy(8 + part).wait_recv()
            rows = pl.ds(part * self.half, self.half)
            add_rows(self.half_of(0, part), self.last.at[part], result.at[rows])
        for i in range(10):
            self.copy(i).wait_send()


def dma_sems(*dims):
    return pltpu.SemaphoreType.DMA(dims)


def in_vmem():
    return pl.BlockSpec(memory_space=pltpu.VMEM)


def in_any():
    return pl.BlockSpec(memory_space=pl.ANY)


def comm_params(number):
    return pltpu.CompilerParams(
        collective_id=number, has_side_effects=True, vmem_limit_bytes=VMEM_BYTES
    )


def shaped(dims, kind):
    return jax.ShapeDtypeStruct(dims, kind)


def first_gather(n_dp, n_line, mats, rows_in, order):
    count = len(mats)
    parts = 2

    def kernel(*refs):
        srcs, (c, e) = refs[:count], refs[count : count + 2]
        dsts, (c_out, e_out) = refs[count + 2 : 2 * count + 2], refs[2 * count + 2 : 2 * count + 4]
        ps, pr, pl_sem, ls, lr, ll = refs[2 * count + 4 :]
        place = Place(n_dp, n_line)
        place.meet()
        planes = [
            GatherPlane(place, a, b, ps.at[i], pr.at[i], pl_sem.at[i])
            for i, (a, b) in enumerate(zip(srcs, dsts))
        ]
        rows = c.shape[0]
        span = rows // parts
        lines = [
            GatherLine(place, c_out, rows, i * span, span, ls.at[i], lr.at[i])
            for i in range(parts)
        ]
        lines.append(
            GatherLine(place, e_out, e.shape[0], 0, e.shape[0], ls.at[parts], lr.at[parts])
        )
        for i in range(parts):
            lines[i].step(0, c.at[pl.ds(i * span, span)])
        lines[parts].step(0, e)
        early, late = planes[: count // 2], planes[count // 2 :]
        for part in early:
            part.begin()
        copies = []
        for i, (src, dst) in enumerate(((c, c_out), (e, e_out))):
            own = dst.at[pl.ds(pl.multiple_of(place.t * src.shape[0], 8), src.shape[0])]
            copies.append(pltpu.make_async_copy(src, own, ll.at[i]))
            copies[i].start()
        for line in lines:
            line.step(1)
        for part in late:
            part.begin()
        for part in early:
            part.forward()
        for line in lines:
            line.step(2)
        for part in early:
            part.share()
        for part in late:
            part.forward()
        for part in late:
            part.share()
        for part in lines + planes:
            part.finish()
        for copy in copies:
            copy.wait()

    return pl.pallas_call(
        kernel,
        out_shape=tuple(shaped((n_dp * m.shape[0], m.shape[1]), m.dtype) for m in mats)
        + (
            shaped((n_line * rows_in.shape[0], rows_in.shape[1]), rows_in.dtype),
            shaped((n_line * order.shape[0], order.shape[1]), order.dtype),
        ),
        in_specs=[in_any()] * (count + 2),
        out_specs=[in_any()] * (count + 2),
        scratch_shapes=[
            dma_sems(count, 9),
            dma_sems(count, 9),
            dma_sems(count),
            dma_sems(parts + 1, 2, n_line - 1),
            dma_sems(parts + 1, 2, n_line - 1),
            dma_sems(2),
        ],
        compiler_params=comm_params(1),
        name="first_gather",
    )(*mats, rows_in, order)


CHUNKS = 8


def line_scratch(n_line, span, width):
    hops = n_line - 1
    return [
        pltpu.VMEM((CHUNKS, 2, hops, span, width), jnp.bfloat16),
        pltpu.VMEM((CHUNKS, 2, hops, span, width), jnp.bfloat16),
        dma_sems(CHUNKS, 2, hops),
        dma_sems(CHUNKS, 2, hops),
        dma_sems(CHUNKS, 2, hops),
        dma_sems(CHUNKS, 2, hops),
        pltpu.VMEM((span, width), jnp.float32),
    ]


def sum_rows_and_spread(place, terms, scratch, finish_rows, spread, between):
    stage, inbox, rs, rr, gs, gr, total = scratch
    span = total.shape[0]
    count = stage.shape[0]
    rows = span * count
    hops = place.n_line - 1
    sums = [
        ReduceLine(place, terms, rows, c * span, span, stage.at[c], inbox.at[c], rs.at[c], rr.at[c])
        for c in range(count)
    ]
    gathers = []
    if spread is not None:
        gathers = [
            GatherLine(place, spread, rows, c * span, span, gs.at[c], gr.at[c])
            for c in range(count)
        ]
    sums[0].ends()

    def total_of(c):
        sums[c].total(total)
        finish_rows(c, pl.ds(c * span, span), total)
        if gathers:
            gathers[c].step(0)

    stages = [lambda c, k=k: sums[c].hop(k) for k in range(hops - 1)] + [total_of]
    lags = [LAGS[min(k, len(LAGS) - 1)] for k in range(hops)]
    if gathers:
        stages += [lambda c, k=k: gathers[c].step(k) for k in range(1, hops)]
        lags += [lags[-1] + LAG_STEP * k for k in range(1, hops)]
    for i in range(count + lags[-1]):
        if i < count:
            sums[i].sent()
        if i + 1 < count:
            sums[i + 1].ends()
        for work, lag in zip(stages, lags):
            if 0 <= i - lag < count:
                work(i - lag)
        if i in between:
            between[i]()
    for part in gathers + sums:
        part.finish()


LAGS = (0, 1, 1)
LAG_STEP = 1


def middle_gather(n_dp, n_line, terms, tokens, gain, mats):
    rows, width = tokens.shape
    count = len(mats)

    def kernel(*refs):
        s, tok, gain_ref = refs[:3]
        srcs = refs[3 : 3 + count]
        after, hidden = refs[3 + count : 5 + count]
        dsts = refs[5 + count : 5 + 2 * count]
        ps, pr, pl_sem = refs[5 + 2 * count : 8 + 2 * count]
        scratch = refs[8 + 2 * count :]
        place = Place(n_dp, n_line)
        place.meet()
        planes = [
            GatherPlane(place, a, b, ps.at[i], pr.at[i], pl_sem.at[i])
            for i, (a, b) in enumerate(zip(srcs, dsts))
        ]
        planes[0].begin()

        def norm(c, here, total):
            values = tok[here].astype(jnp.float32) + total[...]
            after[here] = values
            low = rms_scale(values, gain_ref[...]).astype(jnp.bfloat16)
            first = pl.multiple_of(place.t * rows, 16) + c * total.shape[0]
            hidden[pl.ds(pl.multiple_of(first, 16), total.shape[0])] = low

        between = {4: planes[1].begin, 5: planes[0].forward}
        sum_rows_and_spread(place, s, scratch, norm, hidden, between)
        planes[1].forward()
        planes[0].share()
        planes[1].share()
        for part in planes:
            part.finish()

    return pl.pallas_call(
        kernel,
        out_shape=(
            shaped((rows, width), jnp.float32),
            shaped((n_line * rows, width), jnp.bfloat16),
        )
        + tuple(shaped((n_dp * m.shape[0], m.shape[1]), m.dtype) for m in mats),
        in_specs=[in_vmem()] * 3 + [in_any()] * count,
        out_specs=[in_vmem()] * 2 + [in_any()] * count,
        scratch_shapes=[dma_sems(count, 9), dma_sems(count, 9), dma_sems(count)]
        + line_scratch(n_line, rows // CHUNKS, width),
        compiler_params=comm_params(2),
        name="middle_gather",
    )(terms, tokens, gain, *mats)


def middle_sums(n_dp, n_line, terms, after, gain, grad_in, mat, hidden, grad_up, product, down):
    rows, width = after.shape
    block = mat.shape[0] // n_dp
    wide = grad_up.shape[1]
    spread_rows = n_line * rows

    def kernel(*refs):
        s, after_ref, gain_ref, g_ref, src = refs[:5]
        hid_far, gu_far, pr_far, dw_far = refs[5:9]
        grad_after, gain_sum, spread, result, up_far, feed_far = refs[9:15]
        hid, gu, pr, dw, up_out, feed, sems = refs[15:22]
        rest = refs[22:]
        fetch = Fetch(
            [
                (hid_far, hid),
                (gu_far, gu),
                (pr_far, pr),
                (dw_far, dw),
                (feed, feed_far),
                (up_out.at[0], up_far.at[pl.ds(0, width // 2)]),
                (up_out.at[1], up_far.at[pl.ds(width // 2, width // 2)]),
            ],
            sems,
        )
        fetch.start(0, 1, 2, 3)
        place = Place(n_dp, n_line)
        place.meet()
        plane = ReducePlane(place, src, rest[:7])
        scratch = rest[7:]
        plane.begin()
        gain_sum[...] = jnp.zeros_like(gain_sum)

        def norm(c, here, total):
            grad = total[...]
            grad_rows, normed = norm_back(after_ref[here], gain_ref[...], grad)
            gain_sum[...] += jnp.sum(grad * normed, axis=0, keepdims=True)
            both = g_ref[here].astype(jnp.float32) + grad_rows
            grad_after[here] = both
            first = pl.multiple_of(place.t * rows, 16) + c * total.shape[0]
            spread[pl.ds(pl.multiple_of(first, 16), total.shape[0])] = both.astype(jnp.bfloat16)

        def feed_part(i):
            cols = pl.ds(i * (width // 4), width // 4)
            feed[:, cols] = times_trans(pr[...], dw[cols]).astype(jnp.bfloat16)

        def up_part(i):
            cols = pl.ds(i * (width // 4), width // 4)
            here = pl.ds((i % 2) * (width // 4), width // 4)
            up_out[i // 2, here] = trans_times(hid[:, cols], gu[...]).astype(jnp.bfloat16)

        def early():
            plane.cores()
            fetch.wait(0, 1)

        def two():
            up_part(0)

        def three():
            up_part(1)
            fetch.start(5)

        def four():
            up_part(2)

        def five():
            up_part(3)
            fetch.start(6)
            fetch.wait(2, 3)

        def six():
            feed_part(0)

        def seven():
            plane.turn()
            feed_part(1)

        def eight():
            feed_part(2)

        def nine():
            feed_part(3)
            fetch.start(4)

        steps = {1: early, 2: two, 3: three, 4: four, 5: five, 6: six, 7: seven, 8: eight, 9: nine}
        sum_rows_and_spread(place, s, scratch, norm, spread, steps)
        plane.finish(result)
        fetch.wait(4, 5, 6)

    low, full = jnp.bfloat16, jnp.float32
    near, far = in_vmem(), in_any()
    return pl.pallas_call(
        kernel,
        out_shape=(
            shaped((rows, width), full),
            shaped((1, width), full),
            shaped((spread_rows, width), low),
            shaped((block, mat.shape[1]), low),
            shaped((width, wide), low),
            shaped((spread_rows, width), low),
        ),
        in_specs=[near] * 4 + [far] * 5,
        out_specs=[near] * 4 + [far] * 2,
        scratch_shapes=[vmem_like(m) for m in (hidden, grad_up, product, down)]
        + [
            pltpu.VMEM((2, width // 2, wide), low),
            pltpu.VMEM((spread_rows, width), low),
            dma_sems(7),
        ]
        + ReducePlane.scratch(block, mat.shape[1])
        + line_scratch(n_line, rows // CHUNKS, width),
        compiler_params=comm_params(3),
        name="middle_sums",
    )(terms, after, gain, grad_in, mat, hidden, grad_up, product, down)


class Exchange:
    def __init__(self, place, axis, src, slots, send, recv, local):
        self.p, self.src, self.slots = place, src, slots
        self.over_dp = axis == "dp"
        self.size = place.n_dp if self.over_dp else place.n_line
        self.me = place.d if self.over_dp else place.t
        self.send, self.recv, self.local = send, recv, local

    def copy(self, i):
        to = lax.rem(self.me + i, self.size)
        device = (to, self.p.t) if self.over_dp else (self.p.d, to)
        return remote(
            self.src, self.slots.at[self.me], self.send.at[i - 1], self.recv.at[i - 1], device
        )

    def mine(self):
        return pltpu.make_async_copy(self.src, self.slots.at[self.me], self.local)

    def begin(self):
        for i in range(1, self.size):
            self.copy(i).start()
        self.mine().start()

    def wait(self):
        self.mine().wait()
        for i in range(1, self.size):
            self.copy(i).wait()

    def finish(self):
        self.wait()
        total = self.slots[0]
        for i in range(1, self.size):
            total = total + self.slots[i]
        return total


def last_sums(n_dp, n_line, terms, tokens, gain, grad_after, small, mats):
    rows, width = tokens.shape
    count = len(mats)
    per = len(ReducePlane.scratch(16, 128))

    def kernel(*refs):
        s, tok, gain_ref, g_ref, small_ref = refs[:5]
        srcs = refs[5 : 5 + count]
        grad_tok, small_out, first_out = refs[5 + count : 8 + count]
        results = refs[8 + count : 8 + 2 * count]
        rest = refs[8 + 2 * count :]
        own_first, row_sum = rest[count * per : count * per + 2]
        slots_a, slots_b, slots_c, slots_d = rest[count * per + 2 : count * per + 6]
        xs, xr, xl = rest[count * per + 6 : count * per + 9]
        scratch = rest[count * per + 9 :]
        place = Place(n_dp, n_line)
        place.meet(True)
        planes = [
            ReducePlane(place, srcs[i], rest[i * per : (i + 1) * per]) for i in range(count)
        ]
        for part in planes:
            part.begin()
        early = Exchange(place, "dp", small_ref, slots_a, xs.at[0], xr.at[0], xl.at[0])
        early.begin()
        own_first[...] = jnp.zeros_like(own_first)

        def norm(c, here, total):
            grad = total[...]
            grad_rows, normed = norm_back(tok[here].astype(jnp.float32), gain_ref[...], grad)
            own_first[...] += jnp.sum(grad * normed, axis=0, keepdims=True)
            grad_tok[here] = g_ref[here] + grad_rows

        def cores():
            for part in planes:
                part.cores()

        def turn():
            for part in planes:
                part.turn()

        sum_rows_and_spread(place, s, scratch, norm, None, {0: cores, 5: turn})
        first = Exchange(place, "dp", own_first, slots_b, xs.at[1], xr.at[1], xl.at[1])
        first.begin()
        small_out[...] = early.finish()
        row_sum[0:1] = small_out[0:1]
        row_sum[1:2] = first.finish()
        both = Exchange(place, "tensor", row_sum, slots_c, xs.at[2], xr.at[2], xl.at[2])
        both.begin()
        for part, result in zip(planes, results):
            part.finish(result)
        first_out[...] = both.finish()

    return pl.pallas_call(
        kernel,
        out_shape=(
            shaped((rows, width), jnp.float32),
            shaped(small.shape, jnp.float32),
            shaped((2, width), jnp.float32),
        )
        + tuple(shaped((m.shape[0] // n_dp, m.shape[1]), jnp.bfloat16) for m in mats),
        in_specs=[in_vmem()] * 5 + [in_any()] * count,
        out_specs=[in_vmem()] * (3 + count),
        scratch_shapes=sum([ReducePlane.scratch(m.shape[0] // n_dp, m.shape[1]) for m in mats], [])
        + [
            pltpu.VMEM((1, width), jnp.float32),
            pltpu.VMEM((2, width), jnp.float32),
            pltpu.VMEM((n_dp,) + small.shape, jnp.float32),
            pltpu.VMEM((n_dp, 1, width), jnp.float32),
            pltpu.VMEM((n_line, 2, width), jnp.float32),
            pltpu.VMEM((1, width), jnp.float32),
            dma_sems(3, n_dp),
            dma_sems(3, n_dp),
            dma_sems(3),
        ]
        + line_scratch(n_line, rows // CHUNKS, width),
        compiler_params=comm_params(4),
        name="last_sums",
    )(terms, tokens, gain, grad_after, small, *mats)


def loop(count, body, unroll=1):
    def step(i, carry):
        body(i)
        return carry

    lax.fori_loop(0, count, step, None, unroll=unroll)


def tile_rows(i, size, ahead=0):
    return pl.ds(pl.multiple_of(i * size + ahead, 8), size)


def moved_up(values, distance, count):
    size = values.shape[0]
    return pltpu.roll(values, (size - distance) % size, 0)[:count]


def take_lanes(ref, here):
    return jnp.concatenate([ref[c, here] for c in range(ref.shape[0])], axis=1)


def put_lanes(ref, here, values):
    for c in range(ref.shape[0]):
        ref[c, here] = values[:, c * LANES : (c + 1) * LANES]


def gelu_parts(values):
    inner = GELU_C * (values + 0.044715 * (values * values * values))
    tanh = jnp.tanh(inner)
    half = 0.5 * (1.0 + tanh)
    slope = half + 0.5 * values * (1.0 - tanh * tanh) * GELU_C * (
        1.0 + 3.0 * 0.044715 * (values * values)
    )
    return values * half, slope


GELU_C = 0.7978845608028654
RIM = 128
LANES = 128
TILE = 16


def one_minus_exp(values, exponential):
    series = jnp.ones_like(values)
    for term in range(9, 1, -1):
        series = 1.0 + values * (1.0 / term) * series
    return jnp.where(values > -0.35, -values * series, 1.0 - exponential)


def rate_and_scale(pre_recur, soft, start):
    sr = jax.nn.sigmoid(pre_recur)
    log_rate = -rate_scale * sr * soft
    decay = jnp.exp(log_rate)
    rate = jnp.where(start, 0.0, decay)
    scale = jnp.where(start, 1.0, jnp.sqrt(one_minus_exp(2.0 * log_rate, decay * decay)))
    return sr, rate, scale


class RimSwap:
    def __init__(self, place, own):
        self.odd = lax.rem(place.t, 2)
        self.partner = (place.d, place.t + 1 - 2 * self.odd)
        self.first = pl.multiple_of(RIM - RIM * self.odd, RIM)
        self.edge = pl.ds(pl.multiple_of((1 - self.odd) * own + self.odd * RIM, RIM), RIM)
        self.over_there = pl.ds(pl.multiple_of(self.odd * (own + RIM), RIM), RIM)
        self.beyond = pl.ds(pl.multiple_of((1 - self.odd) * (own + RIM), RIM), RIM)

    def block(self, index, size):
        return pl.ds(pl.multiple_of(self.first + index * size, RIM), size)


class Fetch:
    def __init__(self, pairs, sems):
        self.copies = [
            pltpu.make_async_copy(src, dst, sems.at[i]) for i, (src, dst) in enumerate(pairs)
        ]

    def start(self, *which):
        for i in which:
            self.copies[i].start()

    def wait(self, *which):
        for i in which:
            self.copies[i].wait()


def vmem_like(array):
    return pltpu.VMEM(array.shape, array.dtype)


def recur_forward(
    n_dp,
    n_line,
    tok_all,
    cot,
    to_place,
    to_stored,
    x_full,
    y_full,
    out_full,
    gain,
    gates,
    taps,
    soft,
    flags,
):
    rows, width = tok_all.shape
    count, own = taps.shape
    size = gates.shape[0]
    wide = own + 2 * RIM
    blocks = (wide - RIM) // size
    chunk = rows // 8
    cot_rows = cot.shape[0]
    parts = 1

    def kernel(*refs):
        (tok_far, cot_ref, plc, sto, wx_far, wy_far, wo_far, gain_ref, gw, cw, sp, fl) = refs[:12]
        far, cot_all = refs[12:23], refs[23]
        tok, wx, wy, wo = refs[24:28]
        results = refs[28:39]
        hp, xext, y, conv_low, conv, pre_r, pre_i, rate, state, merged_st, terms = results
        (h, xf, local, cum, merged, agg, slots, hs, hr, es, er, el, gs, gr, gl) = refs[39:54]
        in_sems, out_sems = refs[54:]
        fetch = Fetch(((tok_far, tok), (wx_far, wx), (wy_far, wy), (wo_far, wo)), in_sems)
        store = Fetch(zip(results, far), out_sems)
        fetch.start(0, 1, 2, 3)
        place = Place(n_dp, n_line)
        place.meet(True)
        swap = RimSwap(place, own)
        own_cot = cot_all.at[pl.ds(pl.multiple_of(place.t * cot_rows, 16), cot_rows)]
        keep = pltpu.make_async_copy(cot_ref, own_cot, gl)
        keep.start()
        span = cot_rows // parts
        lines = [
            GatherLine(place, cot_all, cot_rows, c * span, span, gs.at[c], gr.at[c])
            for c in range(parts)
        ]
        for c, line in enumerate(lines):
            line.step(0, cot_ref.at[pl.ds(c * span, span)])

        def norm(i):
            here = tile_rows(i, TILE)
            h[here] = rms_scale(tok[here].astype(jnp.float32), gain_ref[...]).astype(jnp.bfloat16)

        fetch.wait(0)
        loop(rows // TILE, norm)
        fetch.wait(1)

        def project(i):
            here = tile_rows(i, 128)
            hp[here] = plain_dot(plc[here], h[...]).astype(jnp.bfloat16)
            xext[tile_rows(i, 128, 16)] = plain_dot(hp[here], wx[...]).astype(jnp.bfloat16)

        loop(rows // 128, project)
        store.start(0)
        edge = remote(
            xext.at[pl.ds(rows, 16)],
            xext.at[pl.ds(0, 16)],
            hs.at[0],
            hr.at[0],
            (lax.rem(place.d + 1, n_dp), place.t),
        )
        edge.start()
        for line in lines:
            line.step(1)

        def project_y(i):
            here = tile_rows(i, 128)
            y[here] = plain_dot(hp[here], wy[...])

        fetch.wait(2)
        loop(rows // 128, project_y)
        store.start(2)
        edge.wait()
        top = xext[pl.ds(0, 16)]
        xext[pl.ds(0, 16)] = jnp.where(place.d > 0, top, jnp.zeros_like(top))
        store.start(1)

        def widen(i):
            xf[tile_rows(i, TILE)] = xext[tile_rows(i, TILE)].astype(jnp.float32)

        loop(rows // TILE + 1, widen)

        def convolve(i):
            here = tile_rows(i, TILE)
            near = xf[pl.ds(pl.multiple_of(i * TILE + 8, 8), TILE + 8)]
            same = fl[tile_rows(i, TILE, 8)]
            total = cw[0:1] * near[8:]
            for k in range(1, count):
                total += cw[k : k + 1] * moved_up(near, 8 - k, TILE) * same[:, k : k + 1]
            conv[here] = total
            conv_low[here, RIM : RIM + own] = total.astype(jnp.bfloat16)

        loop(rows // TILE, convolve)
        store.start(4)
        rim = remote(
            conv_low.at[:, swap.edge],
            conv_low.at[:, swap.over_there],
            hs.at[1],
            hr.at[1],
            swap.partner,
        )
        rim.start()
        for i in range(blocks):
            index = lax.rem(i + swap.odd, blocks)
            cols = swap.block(index, size)
            other = pl.ds(pl.multiple_of(wide + swap.first + index * size, RIM), size)
            if i == blocks - 1:
                rim.wait()
            pre_r[:, cols] = plain_dot(conv_low[:, cols], gw[:, cols])
            pre_i[:, cols] = plain_dot(conv_low[:, cols], gw[:, other])

        store.start(3, 5, 6)

        def drive(i):
            here = tile_rows(i, TILE)
            start = fl[tile_rows(i, TILE, 8)][:, 0:1] > 0.0
            own_cols = pl.ds(RIM, own)
            _, decay, scale = rate_and_scale(pre_r[here, own_cols], sp[...], start)
            put_lanes(rate, here, decay)
            put_lanes(local, here, conv[here] * jax.nn.sigmoid(pre_i[here, own_cols]) * scale)

        loop(rows // TILE, drive)
        store.start(7)
        for line in lines:
            line.step(2)
        groups = own // LANES

        def scan(i, carry):
            here = pl.ds(i, 8, chunk)
            result = []
            for c in range(groups):
                product, total = carry[c]
                r = rate[c, here]
                product = product * r
                total = total * r + local[c, here]
                cum[c, here] = product
                local[c, here] = total
                result.append((product, total))
            return tuple(result)

        blank = (jnp.ones((8, LANES), jnp.float32), jnp.zeros((8, LANES), jnp.float32))
        lax.fori_loop(0, chunk, scan, (blank,) * groups)
        product, total = jnp.ones((1, own), jnp.float32), jnp.zeros((1, own), jnp.float32)
        for j in range(8):
            last = pl.ds(j * chunk + chunk - 1, 1)
            total = take_lanes(local, last) + take_lanes(cum, last) * total
            product = product * take_lanes(cum, last)
        agg[0:1] = product
        agg[1:2] = total
        swap_all = Exchange(place, "dp", agg, slots, es, er, el)
        swap_all.begin()
        swap_all.wait()
        entry = jnp.zeros((1, own), jnp.float32)
        for q in range(n_dp):
            longer = slots[q, 1:2] + slots[q, 0:1] * entry
            entry = jnp.where(q < place.d, longer, entry)
        state[pl.ds(0, 8)] = jnp.broadcast_to(entry, (8, own))
        for j in range(8):

            def settle(i, entry=entry):
                here = tile_rows(i, TILE, j * chunk)
                values = take_lanes(local, here) + take_lanes(cum, here) * entry
                state[tile_rows(i, TILE, j * chunk + 8)] = values
                merged[here] = (values * gelu_parts(y[here])[0]).astype(jnp.bfloat16)

            loop(chunk // TILE, settle)
            last = pl.ds(j * chunk + chunk - 1, 1)
            entry = take_lanes(local, last) + take_lanes(cum, last) * entry
        store.start(8)
        merged_st[...] = plain_dot(sto[...], merged[...]).astype(jnp.bfloat16)

        store.start(9)
        fetch.wait(3)

        def mix(i):
            some = tile_rows(i, 512)
            terms[:, pl.ds(pl.multiple_of(i * 512, 512), 512)] = times_trans(
                merged_st[...], wo[some, :]
            ).astype(jnp.bfloat16)

        loop(width // 512, mix)
        for line in lines:
            line.finish()
        keep.wait()
        store.start(10)
        store.wait(*range(11))

    low, full = jnp.bfloat16, jnp.float32
    results = (
        shaped((rows, width), low),
        shaped((rows + 16, own), low),
        shaped((rows, own), full),
        shaped((rows, wide), low),
        shaped((rows, own), full),
        shaped((rows, wide), full),
        shaped((rows, wide), full),
        shaped((own // LANES, rows, LANES), full),
        shaped((rows + 8, own), full),
        shaped((rows, own), low),
        shaped((rows, width), low),
    )
    near, far = in_vmem(), in_any()
    return pl.pallas_call(
        kernel,
        out_shape=results + (shaped((n_line * cot_rows, width), low),),
        in_specs=[far, far, near, near, far, far, far] + [near] * 5,
        out_specs=[far] * 12,
        scratch_shapes=[vmem_like(m) for m in (tok_all, x_full, y_full, out_full) + results]
        + [
            pltpu.VMEM((rows, width), low),
            pltpu.VMEM((rows + 16, own), full),
            pltpu.VMEM((own // LANES, rows, LANES), full),
            pltpu.VMEM((own // LANES, rows, LANES), full),
            pltpu.VMEM((rows, own), low),
            pltpu.VMEM((2, own), full),
            pltpu.VMEM((n_dp, 2, own), full),
            dma_sems(2),
            dma_sems(2),
            dma_sems(n_dp),
            dma_sems(n_dp),
            pltpu.SemaphoreType.DMA,
            dma_sems(parts, 2, n_line - 1),
            dma_sems(parts, 2, n_line - 1),
            pltpu.SemaphoreType.DMA,
            dma_sems(4),
            dma_sems(11),
        ],
        compiler_params=comm_params(5),
        name="recur_forward",
    )(
        tok_all,
        cot,
        to_place,
        to_stored,
        x_full,
        y_full,
        out_full,
        gain,
        gates,
        taps,
        soft,
        flags,
    )


def recur_backward(
    n_dp,
    n_line,
    mixer_in,
    to_place,
    to_stored,
    x_full,
    y_full,
    out_full,
    gates,
    taps,
    soft,
    slope,
    flags,
    kept,
    weight_terms,
):
    rows, width = mixer_in.shape
    count, own = taps.shape
    size = gates.shape[0]
    wide = own + 2 * RIM
    blocks = (wide - RIM) // size
    chunk = rows // 8

    def kernel(*refs):
        (mix_far, plc, sto, wx_far, wy_far, wo_far, gw, cw, sp, sg, fl) = refs[:11]
        kept_far, weights = refs[11:19], refs[19]
        (gxy_far, gate_grads, tap_grads, decay_grad, terms_far, weight_sum) = refs[20:26]
        mix, wx, wy, wo = refs[26:30]
        (xext, y, conv_low, conv, pre_r, pre_i, rate, state) = refs[30:38]
        (gxy, mp, gm, lam, reach, gp_r, gp_i, grad, spread, rim_out, rim_in) = refs[38:49]
        (ret_out, ret_in, tap_sums, decay_sums, ends, agg, slots) = refs[49:56]
        (hs, hr, es, er, el, in_sems, out_sems) = refs[56:63]
        terms = mix
        fetch = Fetch(
            [
                (mix_far, mix),
                (wo_far, wo),
                (kept_far[1], y),
                (kept_far[7], state),
                (kept_far[6], rate),
                (kept_far[4], pre_r),
                (kept_far[5], pre_i),
                (kept_far[3], conv),
                (kept_far[2], conv_low),
                (kept_far[0], xext),
                (wx_far, wx),
                (wy_far, wy),
            ],
            in_sems,
        )
        fetch.start(*range(12))
        store = Fetch(((gxy, gxy_far), (terms, terms_far)), out_sems)
        place = Place(n_dp, n_line)
        place.meet(True)
        plane = ReducePlane(place, weights, refs[63:])
        plane.begin()
        swap = RimSwap(place, own)
        own_cols = pl.ds(RIM, own)

        def project(i):
            here = tile_rows(i, 128)
            mp[here] = plain_dot(plc[here], mix[...]).astype(jnp.bfloat16)
            gm[here] = plain_dot(mp[here], wo[...])

        fetch.wait(0, 1)
        loop(rows // 128, project)

        def split(i):
            here = tile_rows(i, TILE)
            branch, slope_y = gelu_parts(y[here])
            grads = gm[here]
            put_lanes(lam, here, grads * branch)
            values = state[tile_rows(i, TILE, 8)]
            gxy[here, own:] = (grads * values * slope_y).astype(jnp.bfloat16)

        fetch.wait(2, 3)
        loop(rows // TILE, split)
        plane.cores()
        fetch.wait(4)
        groups = own // LANES

        def scan(i, carry):
            here = pl.ds(chunk - 1 - i, 8, chunk)
            result = []
            for c in range(groups):
                product, message = carry[c]
                r = rate[c, here]
                value = lam[c, here] + message
                lam[c, here] = value
                reach[c, here] = product
                result.append((product * r, value * r))
            return tuple(result)

        blank = (jnp.ones((8, LANES), jnp.float32), jnp.zeros((8, LANES), jnp.float32))
        done = lax.fori_loop(0, chunk, scan, (blank,) * groups)
        for c in range(groups):
            lanes = pl.ds(c * LANES, LANES)
            ends[0, :, lanes] = done[c][0]
            ends[1, :, lanes] = done[c][1]
        product, message = jnp.ones((1, own), jnp.float32), jnp.zeros((1, own), jnp.float32)
        for j in reversed(range(8)):
            message = ends[1, j : j + 1] + ends[0, j : j + 1] * message
            product = product * ends[0, j : j + 1]
        agg[0:1] = product
        agg[1:2] = message
        swap_all = Exchange(place, "dp", agg, slots, es, er, el)
        swap_all.begin()
        swap_all.wait()
        entry = jnp.zeros((1, own), jnp.float32)
        for q in reversed(range(n_dp)):
            longer = slots[q, 1:2] + slots[q, 0:1] * entry
            entry = jnp.where(q > place.d, longer, entry)
        fetch.wait(5, 6, 7)
        for ref in (tap_sums, decay_sums):
            ref[...] = jnp.zeros_like(ref)
        for ref in (gp_r, gp_i):
            ref[:, 0:RIM] = jnp.zeros((rows, RIM), jnp.bfloat16)
            ref[:, RIM + own :] = jnp.zeros((rows, RIM), jnp.bfloat16)
        grad[pl.ds(0, 8)] = jnp.zeros((8, own), jnp.float32)
        grad[pl.ds(rows + 8, 8)] = jnp.zeros((8, own), jnp.float32)
        for j in reversed(range(8)):

            def back(i, entry=entry):
                here = tile_rows(i, TILE, j * chunk)
                flag = fl[tile_rows(i, TILE, j * chunk + 8)]
                start = flag[:, 0:1] > 0.0
                values = take_lanes(lam, here) + take_lanes(reach, here) * entry
                before = moved_up(
                    state[pl.ds(pl.multiple_of(j * chunk + i * TILE, 8), TILE + 8)], 7, TILE
                )
                sr, decay, scale = rate_and_scale(pre_r[here, own_cols], sp[...], start)
                si = jax.nn.sigmoid(pre_i[here, own_cols])
                block = conv[here]
                driven = values * si
                log_grad = values * before * decay - block * driven * (decay * decay) / scale
                log_grad = jnp.where(start, 0.0, log_grad)
                inner = sr * log_grad
                gp_r[here, own_cols] = (
                    -rate_scale * sp[...] * inner * (1.0 - sr)
                ).astype(jnp.bfloat16)
                gp_i[here, own_cols] = (driven * block * (1.0 - si) * scale).astype(jnp.bfloat16)
                grad[tile_rows(i, TILE, j * chunk + 8)] = driven * scale
                decay_sums[...] += inner[:8] + inner[8:]

            loop(chunk // TILE, back)
            entry = ends[1, j : j + 1] + ends[0, j : j + 1] * entry
        decay_grad[...] = rate_scale * sg[...] * jnp.sum(decay_sums[...], axis=0, keepdims=True)

        for i in range(blocks):
            index = lax.rem(i + 2 - 2 * swap.odd, blocks)
            cols = swap.block(index, size)
            other = pl.ds(pl.multiple_of(wide + swap.first + index * size, RIM), size)
            spread[:, cols] = times_trans(gp_r[:, cols], gw[:, cols]) + times_trans(
                gp_i[:, cols], gw[:, other]
            )
            if i == 0:
                rim_out[...] = spread[:, swap.beyond].astype(jnp.bfloat16)
                rim = remote(rim_out, rim_in, hs.at[0], hr.at[0], swap.partner)
                rim.start()
        rim.wait()
        shared = pl.ds(pl.multiple_of((1 - swap.odd) * (own - RIM), RIM), RIM)

        def join(i):
            here = tile_rows(i, TILE)
            there = tile_rows(i, TILE, 8)
            grad[there] += spread[here, own_cols]
            grad[there, shared] += rim_in[here].astype(jnp.float32)

        loop(rows // TILE, join)

        near = grad[pl.ds(0, 16)]
        back_rows = jnp.zeros((8, own), jnp.float32)
        for k in range(1, count):
            masked = near * fl[pl.ds(0, 16)][:, k : k + 1]
            back_rows += cw[k : k + 1] * moved_up(masked, k, 8)
        ret_out[...] = back_rows
        ret = remote(
            ret_out,
            ret_in,
            hs.at[1],
            hr.at[1],
            (lax.rem(place.d + n_dp - 1, n_dp), place.t),
        )
        ret.start()
        fetch.wait(8)
        for i in range(blocks):
            cols = swap.block(i, size)
            spread[0:size, cols] = trans_times(conv_low[:, cols], gp_r[:, cols])
            spread[size : 2 * size, cols] = trans_times(conv_low[:, cols], gp_i[:, cols])
        gate_grads[:, 0:own] = spread[0:size, own_cols].astype(jnp.bfloat16)
        gate_grads[:, own:] = spread[size : 2 * size, own_cols].astype(jnp.bfloat16)

        def taps_back(i, added=None):
            here = tile_rows(i, TILE)
            start = pl.ds(pl.multiple_of(i * TILE + 8, 8), TILE + 8)
            after = grad[start]
            flag = fl[start]
            behind = xext[pl.ds(pl.multiple_of(i * TILE, 16), 2 * TILE)].astype(jnp.float32)
            total = cw[0:1] * after[:TILE]
            for k in range(count):
                if k > 0:
                    masked = after * flag[:, k : k + 1]
                    total += cw[k : k + 1] * moved_up(masked, k, TILE)
                    mine = masked[:TILE]
                else:
                    mine = after[:TILE]
                term = mine * moved_up(behind, 16 - k, TILE)
                tap_sums[k] += term[:8] + term[8:]
            if added is not None:
                total = total + jnp.concatenate([jnp.zeros((8, own), jnp.float32), added], axis=0)
            gxy[here, 0:own] = total.astype(jnp.bfloat16)

        fetch.wait(9)
        loop(rows // TILE - 1, taps_back)
        ret.wait()
        taps_back(rows // TILE - 1, jnp.where(place.d < n_dp - 1, ret_in[...], 0.0))
        tap_grads[...] = jnp.zeros_like(tap_grads)
        for k in range(count):
            tap_grads[k : k + 1] = jnp.sum(tap_sums[k], axis=0, keepdims=True)

        store.start(0)
        plane.turn()

        def restore(i):
            here = tile_rows(i, 128)
            mp[here, 0 : 2 * own] = plain_dot(sto[here], gxy[...]).astype(jnp.bfloat16)

        loop(rows // 128, restore)

        def spread_back(i):
            some = tile_rows(i, 512)
            terms[:, pl.ds(pl.multiple_of(i * 512, 512), 512)] = (
                times_trans(mp[:, 0:own], wx[some]) + times_trans(mp[:, own : 2 * own], wy[some])
            ).astype(jnp.bfloat16)

        fetch.wait(10, 11)
        loop(width // 512, spread_back)
        store.start(1)
        plane.finish(weight_sum)
        store.wait(0, 1)

    low, full = jnp.bfloat16, jnp.float32
    block = weight_terms.shape[0] // n_dp
    near, far = in_vmem(), in_any()
    return pl.pallas_call(
        kernel,
        out_shape=(
            shaped((rows, 2 * own), low),
            shaped((size, 2 * own), low),
            shaped((8, own), full),
            shaped((1, own), full),
            shaped((rows, width), low),
            shaped((block, weight_terms.shape[1]), low),
        ),
        in_specs=[far, near, near, far, far, far] + [near] * 5 + [far] * 9,
        out_specs=[far, near, near, near, far, near],
        scratch_shapes=[vmem_like(m) for m in (mixer_in, x_full, y_full, out_full, *kept)]
        + [
            pltpu.VMEM((rows, 2 * own), low),
            pltpu.VMEM((rows, width), low),
            pltpu.VMEM((rows, own), full),
            pltpu.VMEM((own // LANES, rows, LANES), full),
            pltpu.VMEM((own // LANES, rows, LANES), full),
            pltpu.VMEM((rows, wide), low),
            pltpu.VMEM((rows, wide), low),
            pltpu.VMEM((rows + 16, own), full),
            pltpu.VMEM((rows, wide), full),
            pltpu.VMEM((rows, RIM), low),
            pltpu.VMEM((rows, RIM), low),
            pltpu.VMEM((8, own), full),
            pltpu.VMEM((8, own), full),
            pltpu.VMEM((count, 8, own), full),
            pltpu.VMEM((8, own), full),
            pltpu.VMEM((2, 8, own), full),
            pltpu.VMEM((2, own), full),
            pltpu.VMEM((n_dp, 2, own), full),
            dma_sems(2),
            dma_sems(2),
            dma_sems(n_dp),
            dma_sems(n_dp),
            pltpu.SemaphoreType.DMA,
            dma_sems(12),
            dma_sems(2),
        ]
        + ReducePlane.scratch(block, weight_terms.shape[1]),
        compiler_params=comm_params(6),
        name="recur_backward",
    )(
        mixer_in,
        to_place,
        to_stored,
        x_full,
        y_full,
        out_full,
        gates,
        taps,
        soft,
        slope,
        flags,
        *kept,
        weight_terms,
    )


def matches(mesh):
    return mesh.shape["dp"] == 8 and mesh.shape["tensor"] == 4


def local_blocks(
    tokens,
    norm_gain,
    x_weight,
    y_weight,
    conv_weight,
    recur_gate_weight,
    input_gate_weight,
    decay_param,
    out_weight,
    mlp_gain,
    gate_weight,
    up_weight,
    down_weight,
    seq_lengths,
    token_order,
    cotangent,
):
    n_dp, n_tensor = lax.axis_size("dp"), lax.axis_size("tensor")
    tensor_index = lax.axis_index("tensor")
    dp_index = lax.axis_index("dp")
    tok_rows, width = tokens.shape
    row_count = tok_rows * n_tensor
    own_width = conv_weight.shape[1]
    kernel_taps = conv_weight.shape[0]
    edge_rows = kernel_taps - 1
    dp_width = norm_gain.shape[0]
    gate_rows = recur_gate_weight.shape[0]
    own_start = tensor_index * tok_rows

    gains = jnp.concatenate([norm_gain, mlp_gain])
    spare = gate_rows * 128 - gains.shape[0]
    gains = jnp.pad(gains, (0, spare)).reshape(gate_rows, 128)
    minor = jnp.concatenate([recur_gate_weight, input_gate_weight, gains], axis=1)
    own_order = (token_order - dp_index * row_count).astype(jnp.int32)
    order_rows = jnp.broadcast_to(own_order[None, :], (8, tok_rows))
    x_full, y_full, out_full, minor_full, tok_all, order_full = first_gather(
        n_dp, n_tensor, (x_weight, y_weight, out_weight.T, minor), tokens, order_rows
    )
    down_full = lax.all_gather(
        lax.optimization_barrier((down_weight.T, tok_all))[0], "dp", axis=0, tiled=True
    )
    order_all = order_full.reshape(n_tensor, 8, tok_rows)[:, 0].reshape(row_count)
    both_gates = minor_full[:, : 2 * own_width]
    gain_rows = minor_full[:, 2 * own_width :].reshape(n_dp, -1)
    first_gain = gain_rows[:, :dp_width].reshape(1, width).astype(jnp.float32)
    second_gain = gain_rows[:, dp_width : 2 * dp_width].reshape(1, width).astype(jnp.float32)
    block_size = both_gates.shape[0]
    row_index = jnp.arange(row_count, dtype=jnp.int32)
    hits = row_index[:, None] == order_all[None, :]
    to_place = hits.astype(jnp.bfloat16)
    to_stored = (order_all[:, None] == row_index[None, :]).astype(jnp.bfloat16)
    places = dp_index * row_count + jnp.arange(-8, row_count + 8, dtype=jnp.int32)
    inside = (jnp.arange(row_count + 16) >= 8) & (jnp.arange(row_count + 16) < row_count + 8)
    ends = jnp.cumsum(seq_lengths)
    segment = segment_of(places, ends)
    starts = (places == 0) | (segment != segment_of(places - 1, ends))
    columns = [starts] + [
        segment_of(places - shift, ends) == segment for shift in range(1, kernel_taps)
    ]
    columns += [jnp.zeros_like(starts)] * (8 - len(columns))
    flags = (jnp.stack(columns, axis=1) & inside[:, None]).astype(jnp.float32)
    live_own = (token_order < ends[-1]).astype(jnp.float32)
    grad_in_own = (cotangent.astype(jnp.float32) * live_own[:, None]).astype(jnp.bfloat16)
    soft = jax.nn.softplus(-decay_param).reshape(1, own_width)
    slope = jax.nn.sigmoid(-decay_param).reshape(1, own_width)
    zero_rim = jnp.zeros((block_size, RIM), jnp.bfloat16)
    gates_wide = jnp.concatenate(
        [
            zero_rim,
            both_gates[:, :own_width],
            zero_rim,
            zero_rim,
            both_gates[:, own_width:],
            zero_rim,
        ],
        axis=1,
    )
    def glu(gate_pre, up_pre):
        return gelu_tanh(gate_pre) * up_pre

    hidden_place, *kept, merged_stored, mixer_terms, down_in = recur_forward(
        n_dp,
        n_tensor,
        tok_all,
        grad_in_own,
        to_place,
        to_stored,
        x_full,
        y_full,
        out_full,
        first_gain,
        gates_wide,
        conv_weight,
        soft,
        flags,
    )
    after_own, hidden_two, gate_full, up_full = middle_gather(
        n_dp, n_tensor, mixer_terms, tokens, second_gain, (gate_weight, up_weight)
    )
    gate_pre = plain_dot(hidden_two, gate_full)
    up_pre = plain_dot(hidden_two, up_full)
    glu_out, glu_pull = jax.vjp(glu, gate_pre, up_pre)
    product = glu_out.astype(jnp.bfloat16)
    grad_down = trans_times(down_in, product).astype(jnp.bfloat16)
    down_sum = lax.psum_scatter(grad_down, "dp", scatter_dimension=0, tiled=True)
    down_in, _ = lax.optimization_barrier((down_in, grad_down))
    grad_product = plain_dot(down_in, down_full)
    grad_gate_pre, grad_up_pre = glu_pull(grad_product)
    grad_gate_pre = grad_gate_pre.astype(jnp.bfloat16)
    grad_up_pre = grad_up_pre.astype(jnp.bfloat16)
    grad_gate = trans_times(hidden_two, grad_gate_pre).astype(jnp.bfloat16)
    back_terms = (
        times_trans(grad_gate_pre, gate_full) + times_trans(grad_up_pre, up_full)
    ).astype(jnp.bfloat16)
    grad_after_own, second_part, mixer_in, gate_sum, grad_up, feed_terms = middle_sums(
        n_dp,
        n_tensor,
        back_terms,
        after_own,
        second_gain,
        grad_in_own,
        grad_gate,
        hidden_two,
        grad_up_pre,
        product,
        down_full,
    )
    feed_out = lax.psum_scatter(
        feed_terms,
        "tensor",
        scatter_dimension=0,
        tiled=True,
    ).astype(jnp.float32)
    output = ((after_own + feed_out) * live_own[:, None]).astype(jnp.bfloat16)

    grad_xy, gate_grads, tap_grads, decay_grad, one_terms, up_sum = recur_backward(
        n_dp,
        n_tensor,
        mixer_in,
        to_place,
        to_stored,
        x_full,
        y_full,
        out_full,
        gates_wide,
        conv_weight,
        soft,
        slope,
        flags,
        kept,
        grad_up,
    )
    grad_out_mat = trans_times(mixer_in, merged_stored).astype(jnp.bfloat16)
    grad_xy_mat = trans_times(hidden_place, grad_xy).astype(jnp.bfloat16)
    small = jnp.concatenate(
        [
            second_part,
            tap_grads[:kernel_taps].reshape(1, -1),
            jnp.pad(decay_grad, ((0, 0), (0, width - own_width))),
            jnp.zeros((1, width), jnp.float32),
        ],
        axis=0,
    )
    grad_tokens, small_sum, gain_sums, xy_sum, out_sum, gates_sum = last_sums(
        n_dp,
        n_tensor,
        one_terms,
        tokens,
        first_gain,
        grad_after_own,
        small,
        (grad_xy_mat, grad_out_mat, gate_grads),
    )
    xy_sum, gates_sum = xy_sum.astype(jnp.float32), gates_sum.astype(jnp.float32)
    own_gains = lax.dynamic_slice_in_dim(gain_sums, dp_index * dp_width, dp_width, 1)
    return (
        output,
        grad_tokens,
        own_gains[1],
        xy_sum[:, :own_width],
        xy_sum[:, own_width:],
        small_sum[1].reshape(kernel_taps, own_width),
        gates_sum[:, :own_width],
        gates_sum[:, own_width:],
        small_sum[2, :own_width],
        out_sum.astype(jnp.float32).T,
        own_gains[0],
        gate_sum.astype(jnp.float32),
        up_sum.astype(jnp.float32),
        down_sum.astype(jnp.float32).T,
    )


def solution(mesh):
    in_specs = (
        P(("dp", "tensor"), None),
        P("dp"),
        P("dp", "tensor"),
        P("dp", "tensor"),
        P(None, "tensor"),
        P("dp", "tensor"),
        P("dp", "tensor"),
        P("tensor"),
        P("tensor", "dp"),
        P("dp"),
        P("dp", "tensor"),
        P("dp", "tensor"),
        P("tensor", "dp"),
        P(),
        P(("dp", "tensor")),
        P(("dp", "tensor"), None),
    )
    out_specs = (
        P(("dp", "tensor"), None),
        P(("dp", "tensor"), None),
        P("dp"),
        P("dp", "tensor"),
        P("dp", "tensor"),
        P(None, "tensor"),
        P("dp", "tensor"),
        P("dp", "tensor"),
        P("tensor"),
        P("tensor", "dp"),
        P("dp"),
        P("dp", "tensor"),
        P("dp", "tensor"),
        P("tensor", "dp"),
    )
    fits = matches(mesh)
    local = local_blocks if fits else local_general
    return jax.shard_map(local, mesh=mesh, in_specs=in_specs, out_specs=out_specs, check_vma=False)
```

```python
import jax
import jax.numpy as jnp
from jax import lax
from jax.experimental import pallas as pl
from jax.experimental.pallas import tpu as pltpu
from jax.sharding import PartitionSpec as P

epsilon = 1e-06
rate_scale = 8.0


def from_behind(block, axis, distance):
    devices = range(lax.axis_size(axis))
    route = [(i - distance, i) for i in devices if i - distance in devices]
    return lax.ppermute(block, axis, route)


def extended_2(array, sides, width):
    for axis, dim in sides:
        size, length = (lax.axis_size(axis), array.shape[dim])
        up = [(i, (i + 1) % size) for i in range(size - 1)]
        down = [(j, i) for i, j in up]
        last = lax.slice_in_dim(array, length - width, length, axis=dim)
        leading = lax.slice_in_dim(array, 0, width, axis=dim)
        before = lax.ppermute(last, axis, up)
        after = lax.ppermute(leading, axis, down)
        array = jnp.concatenate([before, array, after], axis=dim)
    return array


def entering(value, axis, join, neutral, backward):
    count, mine = (lax.axis_size(axis), lax.axis_index(axis))
    pieces = jax.tree.map(lambda part: lax.all_gather(part, axis), value)
    if backward:
        pieces = jax.tree.map(lambda part: part[::-1], pieces)
        mine = count - 1 - mine
    total = jax.tree.map(
        lambda part, zero: jnp.full_like(part, 0) + jnp.asarray(zero, part.dtype), value, neutral
    )

    def lap(position, total):
        longer = join(total, jax.tree.map(lambda part: part[position], pieces))
        return jax.tree.map(lambda new, old: jnp.where(position < mine, new, old), longer, total)

    return lax.fori_loop(0, count - 1, lap, total)


def rms_scale(values, gain):
    return values * lax.rsqrt(jnp.mean(values * values, axis=-1, keepdims=True) + epsilon) * gain


def norm_back(values, gain, grad):
    inv_root = lax.rsqrt(jnp.mean(values * values, axis=-1, keepdims=True) + epsilon)
    normed = values * inv_root
    upstream = grad * gain
    grad_values = inv_root * (
        upstream - normed * jnp.mean(upstream * normed, axis=-1, keepdims=True)
    )
    return (grad_values, normed)


def segment_of(places, ends):
    return jnp.sum((ends[None, :] <= places[:, None]).astype(jnp.int32), axis=1)


def pair_step(early, later):
    return (early[0] * later[0], later[0] * early[1] + later[1])


def plain_dot(left, right):
    return jnp.dot(left, right, preferred_element_type=jnp.float32)


def times_trans(left, right):
    return lax.dot_general(
        left, right, (((1,), (1,)), ((), ())), preferred_element_type=jnp.float32
    )


def trans_times(left, right):
    return lax.dot_general(
        left, right, (((0,), (0,)), ((), ())), preferred_element_type=jnp.float32
    )


def gelu_tanh(values):
    return jax.nn.gelu(values, approximate=True)


def collect(
    norm_gain,
    mlp_gain,
    x_weight,
    y_weight,
    recur_gate_weight,
    input_gate_weight,
    gate_weight,
    up_weight,
    out_weight,
    down_weight,
):
    return (
        lax.all_gather(norm_gain, "dp", axis=0, tiled=True),
        lax.all_gather(mlp_gain, "dp", axis=0, tiled=True),
        lax.all_gather(x_weight, "dp", axis=0, tiled=True),
        lax.all_gather(y_weight, "dp", axis=0, tiled=True),
        lax.all_gather(recur_gate_weight, "dp", axis=0, tiled=True),
        lax.all_gather(input_gate_weight, "dp", axis=0, tiled=True),
        lax.all_gather(gate_weight, "dp", axis=0, tiled=True),
        lax.all_gather(up_weight, "dp", axis=0, tiled=True),
        lax.all_gather(out_weight, "dp", axis=1, tiled=True),
        lax.all_gather(down_weight, "dp", axis=1, tiled=True),
    )


def row_sums(term_rows, tok_rows):
    return lax.psum_scatter(
        term_rows(jnp.int32(0), lax.axis_size("tensor") * tok_rows).astype(jnp.bfloat16),
        "tensor",
        scatter_dimension=0,
        tiled=True,
    ).astype(jnp.float32)


def spread_rows(values):
    return lax.all_gather(values, "tensor", axis=0, tiled=True)


def local_general(
    tokens,
    norm_gain,
    x_weight,
    y_weight,
    conv_weight,
    recur_gate_weight,
    input_gate_weight,
    decay_param,
    out_weight,
    mlp_gain,
    gate_weight,
    up_weight,
    down_weight,
    seq_lengths,
    token_order,
    cotangent,
):
    n_tensor = lax.axis_size("tensor")
    tensor_index = lax.axis_index("tensor")
    dp_index = lax.axis_index("dp")
    tok_rows = tokens.shape[0]
    row_count = tok_rows * n_tensor
    own_width = conv_weight.shape[1]
    kernel_taps = conv_weight.shape[0]
    edge_rows = kernel_taps - 1
    dp_width = norm_gain.shape[0]
    own_start = tensor_index * tok_rows
    shards = (
        norm_gain,
        mlp_gain,
        x_weight,
        y_weight,
        recur_gate_weight,
        input_gate_weight,
        gate_weight,
        up_weight,
        out_weight,
        down_weight,
    )
    (
        gain_one,
        gain_two,
        x_full,
        y_full,
        recur_full,
        input_full,
        gate_full,
        up_full,
        out_full,
        down_full,
    ) = collect(*shards)
    block_size = recur_full.shape[0]
    first_gain = gain_one.astype(jnp.float32)
    second_gain = gain_two.astype(jnp.float32)
    both_gates = jnp.concatenate([recur_full, input_full], axis=1)
    tok_own = tokens.astype(jnp.float32)
    own_order = token_order - dp_index * row_count
    first_rows = rms_scale(tok_own, first_gain).astype(jnp.bfloat16)
    first_all, cot_all, order_all = (
        lax.all_gather(first_rows, "tensor", axis=0, tiled=True),
        lax.all_gather(cotangent, "tensor", axis=0, tiled=True),
        lax.all_gather(own_order, "tensor", axis=0, tiled=True),
    )
    row_index = jnp.arange(row_count, dtype=jnp.int32)
    inverse = jnp.zeros((row_count,), jnp.int32).at[order_all].set(row_index)
    hidden_place = jnp.take(first_all, inverse, axis=0)
    places = dp_index * row_count + row_index
    ends = jnp.cumsum(seq_lengths)
    segment = segment_of(places, ends)
    starts = (places == 0) | (segment != segment_of(places - 1, ends))
    live = (places < ends[-1]).astype(jnp.float32)
    live_stored = jnp.take(live, order_all, axis=0)
    same = [
        (segment_of(places - shift, ends) == segment).astype(jnp.float32)
        for shift in range(kernel_taps)
    ]
    low_edge = tensor_index * own_width
    own_blocks = (low_edge + jnp.arange(own_width, dtype=jnp.int32)) // block_size
    first_block = low_edge // block_size
    block_count = own_width // block_size + 2

    def block_start(index):
        return (first_block + index) * block_size - low_edge + block_size

    def block_mask(index):
        inside = own_blocks == first_block + index
        return jnp.concatenate([inside, inside])

    def convolve(extended, kernel):
        return sum(
            (
                kernel[shift][None, :]
                * extended[edge_rows - shift : edge_rows - shift + row_count]
                * same[shift][:, None]
                for shift in range(kernel_taps)
            )
        )

    def gates(conv_vals, pre_recur, pre_input, decay_vals):
        log_rate = -rate_scale * jax.nn.sigmoid(pre_recur) * jax.nn.softplus(-decay_vals)
        decay_rate = jnp.where(starts[:, None], 0.0, jnp.exp(log_rate))
        scale_in = jnp.where(starts[:, None], 1.0, jnp.sqrt(-jnp.expm1(2.0 * log_rate)))
        return (decay_rate, conv_vals * jax.nn.sigmoid(pre_input) * scale_in)

    def glu(gate_pre, up_pre):
        return gelu_tanh(gate_pre) * up_pre

    x_branch = plain_dot(hidden_place, x_full).astype(jnp.bfloat16)
    y_before = plain_dot(hidden_place, y_full)
    previous = from_behind(x_branch[row_count - edge_rows :], "dp", 1)
    extended = jnp.concatenate([previous, x_branch], axis=0).astype(jnp.float32)
    conv_out = convolve(extended, conv_weight)
    conv_wide = extended_2(conv_out.astype(jnp.bfloat16), (("tensor", 1),), block_size)
    pre_both = jnp.zeros((row_count, 2 * own_width), jnp.float32)
    for index in range(block_count):
        piece = lax.dynamic_slice_in_dim(conv_wide, block_start(index), block_size, 1)
        pre_both = pre_both + jnp.where(
            block_mask(index)[None, :], plain_dot(piece, both_gates), 0.0
        )
    (decay_rate, driven), gate_pull = jax.vjp(
        gates, conv_out, pre_both[:, :own_width], pre_both[:, own_width:], decay_param
    )
    cum_rate, local_state = lax.associative_scan(pair_step, (decay_rate, driven), axis=0)
    ident = (jnp.ones((own_width,), jnp.float32), jnp.zeros((own_width,), jnp.float32))
    rate_in, state_in = entering((cum_rate[-1], local_state[-1]), "dp", pair_step, ident, False)
    state = local_state + cum_rate * state_in[None, :]
    y_branch = gelu_tanh(y_before)
    merged = (state * y_branch).astype(jnp.bfloat16)
    merged_stored = jnp.take(merged, order_all, axis=0)

    def mixer_rows(begin, number):
        return plain_dot(merged_stored, out_full)

    after_own = tok_own + row_sums(mixer_rows, tok_rows)
    hidden_two = spread_rows(rms_scale(after_own, second_gain).astype(jnp.bfloat16))
    gate_pre = plain_dot(hidden_two, gate_full)
    up_pre = plain_dot(hidden_two, up_full)
    glu_out, glu_pull = jax.vjp(glu, gate_pre, up_pre)
    product = glu_out.astype(jnp.bfloat16)

    def down_rows(begin, number):
        return plain_dot(product, down_full)

    feed_out = row_sums(down_rows, tok_rows)
    live_own = lax.dynamic_slice_in_dim(live_stored, own_start, tok_rows, 0)
    output = ((after_own + feed_out) * live_own[:, None]).astype(jnp.bfloat16)
    grad_out = cot_all.astype(jnp.float32) * live_stored[:, None]
    fresh = lax.optimization_barrier((shards, grad_out))[0]
    (
        gain_one,
        gain_two,
        x_full,
        y_full,
        recur_full,
        input_full,
        gate_full,
        up_full,
        out_full,
        down_full,
    ) = collect(*fresh)
    first_gain = gain_one.astype(jnp.float32)
    second_gain = gain_two.astype(jnp.float32)
    both_gates = jnp.concatenate([recur_full, input_full], axis=1)
    down_in = grad_out.astype(jnp.bfloat16)
    grad_down = trans_times(product, down_in)
    grad_product = times_trans(down_in, down_full)
    grad_gate_pre, grad_up_pre = glu_pull(grad_product)
    grad_gate_pre = grad_gate_pre.astype(jnp.bfloat16)
    grad_up_pre = grad_up_pre.astype(jnp.bfloat16)
    grad_gate = trans_times(hidden_two, grad_gate_pre)
    grad_up = trans_times(hidden_two, grad_up_pre)

    def feed_rows(begin, number):
        return times_trans(grad_gate_pre, gate_full) + times_trans(grad_up_pre, up_full)

    grad_out_own = lax.dynamic_slice_in_dim(grad_out, own_start, tok_rows, 0)
    grad_two_own = row_sums(feed_rows, tok_rows)
    grad_norm_own, normed_two = norm_back(after_own, second_gain, grad_two_own)
    second_part = jnp.sum(grad_two_own * normed_two, axis=0)
    grad_after_own = grad_out_own + grad_norm_own
    mixer_in = spread_rows(grad_after_own.astype(jnp.bfloat16))
    grad_out_mat = trans_times(merged_stored, mixer_in)
    grad_merged = jnp.take(times_trans(mixer_in, out_full), inverse, axis=0)
    grad_state = grad_merged * y_branch
    gelu_pull = jax.vjp(gelu_tanh, y_before)[1]
    grad_y_before = gelu_pull(grad_merged * state)[0].astype(jnp.bfloat16)
    rate_next = jnp.concatenate([decay_rate[1:], jnp.ones((1, own_width), jnp.float32)], axis=0)
    rev_rate, local_lam = lax.associative_scan(
        pair_step, (rate_next, grad_state), reverse=True, axis=0
    )
    head_rate = decay_rate[0] * rev_rate[0]
    head_lam = decay_rate[0] * local_lam[0]
    factor_in, lam_in = entering((head_rate, head_lam), "dp", pair_step, ident, True)
    lam = local_lam + rev_rate * lam_in[None, :]
    state_prev = jnp.concatenate([state_in[None, :], state[:-1]], axis=0)
    grad_conv_local, grad_pre_recur, grad_pre_input, grad_decay_own = gate_pull(
        (lam * state_prev, lam)
    )
    grad_pre = jnp.concatenate([grad_pre_recur, grad_pre_input], axis=1).astype(jnp.bfloat16)
    grad_both = jnp.zeros((block_size, 2 * own_width), jnp.float32)
    grad_wide = jnp.zeros((row_count, own_width + 2 * block_size), jnp.float32)
    for index in range(block_count):
        begin = block_start(index)
        piece = lax.dynamic_slice_in_dim(conv_wide, begin, block_size, 1)
        masked = jnp.where(block_mask(index)[None, :], grad_pre, jnp.zeros((), jnp.bfloat16))
        grad_both = grad_both + trans_times(piece, masked)
        added = lax.dynamic_slice_in_dim(grad_wide, begin, block_size, 1) + times_trans(
            masked, both_gates
        )
        grad_wide = lax.dynamic_update_slice_in_dim(grad_wide, added, begin, 1)
    grad_recur = grad_both[:, :own_width]
    grad_input = grad_both[:, own_width:]
    rims = jnp.concatenate(
        [grad_wide[:, :block_size], grad_wide[:, own_width + block_size :]], axis=1
    )
    arrived = extended_2(rims.astype(jnp.bfloat16), (("tensor", 1),), block_size).astype(rims.dtype)
    from_lower = jnp.pad(arrived[:, :block_size], ((0, 0), (0, own_width - block_size)))
    from_upper = jnp.pad(arrived[:, 3 * block_size :], ((0, 0), (own_width - block_size, 0)))
    grad_conv = (
        grad_conv_local
        + grad_wide[:, block_size : block_size + own_width]
        + from_lower
        + from_upper
    )
    conv_pull = jax.vjp(convolve, extended, conv_weight)[1]
    grad_extended, grad_kernel = conv_pull(grad_conv)
    returned = from_behind(grad_extended[:edge_rows], "dp", -1)
    grad_x_branch = grad_extended[edge_rows:] + jnp.concatenate(
        [jnp.zeros((row_count - edge_rows, own_width), jnp.float32), returned], axis=0
    )
    grad_x_low = grad_x_branch.astype(jnp.bfloat16)
    grad_x_stored = jnp.take(grad_x_low, order_all, axis=0)
    grad_y_stored = jnp.take(grad_y_before, order_all, axis=0)
    grad_x_mat = trans_times(first_all, grad_x_stored)
    grad_y_mat = trans_times(first_all, grad_y_stored)

    def mixer_back_rows(begin, number):
        return times_trans(grad_x_stored, x_full) + times_trans(grad_y_stored, y_full)

    grad_one_own = row_sums(mixer_back_rows, tok_rows)
    grad_norm_one, normed_one = norm_back(tok_own, first_gain, grad_one_own)
    first_part = jnp.sum(grad_one_own * normed_one, axis=0)
    grad_tokens = grad_after_own + grad_norm_one
    chosen = jnp.arange(n_tensor, dtype=jnp.int32) == tensor_index
    kernel_tile = jnp.where(chosen[:, None, None], grad_kernel[None, :, :], 0.0)
    decay_tile = jnp.where(chosen[:, None], grad_decay_own[None, :], 0.0)
    small = lax.psum((first_part, second_part, kernel_tile, decay_tile), ("dp", "tensor"))
    grad_first_gain = lax.dynamic_slice_in_dim(small[0], dp_index * dp_width, dp_width, 0)
    grad_second_gain = lax.dynamic_slice_in_dim(small[1], dp_index * dp_width, dp_width, 0)
    grad_kernel_sum = lax.dynamic_index_in_dim(small[2], tensor_index, 0, keepdims=False)
    grad_decay = lax.dynamic_index_in_dim(small[3], tensor_index, 0, keepdims=False)
    sums = (
        lax.psum_scatter(
            grad_x_mat.astype(jnp.bfloat16), "dp", scatter_dimension=0, tiled=True
        ).astype(jnp.float32),
        lax.psum_scatter(
            grad_y_mat.astype(jnp.bfloat16), "dp", scatter_dimension=0, tiled=True
        ).astype(jnp.float32),
        lax.psum_scatter(
            grad_recur.astype(jnp.bfloat16), "dp", scatter_dimension=0, tiled=True
        ).astype(jnp.float32),
        lax.psum_scatter(
            grad_input.astype(jnp.bfloat16), "dp", scatter_dimension=0, tiled=True
        ).astype(jnp.float32),
        lax.psum_scatter(
            grad_gate.astype(jnp.bfloat16), "dp", scatter_dimension=0, tiled=True
        ).astype(jnp.float32),
        lax.psum_scatter(
            grad_up.astype(jnp.bfloat16), "dp", scatter_dimension=0, tiled=True
        ).astype(jnp.float32),
        lax.psum_scatter(
            grad_out_mat.astype(jnp.bfloat16), "dp", scatter_dimension=1, tiled=True
        ).astype(jnp.float32),
        lax.psum_scatter(
            grad_down.astype(jnp.bfloat16), "dp", scatter_dimension=1, tiled=True
        ).astype(jnp.float32),
    )
    return (
        output,
        grad_tokens,
        grad_first_gain,
        sums[0],
        sums[1],
        grad_kernel_sum,
        sums[2],
        sums[3],
        grad_decay,
        sums[6],
        grad_second_gain,
        sums[4],
        sums[5],
        sums[7],
    )


MESH = pl.DeviceIdType.MESH
VMEM_BYTES = 60 * 2**20


def remote(src, dst, send, recv, device):
    return pltpu.make_async_remote_copy(
        src_ref=src,
        dst_ref=dst,
        send_sem=send,
        recv_sem=recv,
        device_id=device,
        device_id_type=MESH,
    )


class Place:
    def __init__(self, n_dp, n_line):
        self.n_dp, self.n_line = n_dp, n_line
        self.d, self.t = lax.axis_index("dp"), lax.axis_index("tensor")
        self.core = lax.rem(self.d, 2)
        self.x = lax.rem(lax.div(self.d, 2), 2)
        self.y = lax.div(self.d, 4)

    def chip(self, flip_x, flip_y, flip_core=0):
        x = 1 - self.x if flip_x else self.x
        y = 1 - self.y if flip_y else self.y
        core = 1 - self.core if flip_core else self.core
        return y * 4 + x * 2 + core

    def at(self, flip_x=0, flip_y=0, flip_core=0):
        return (self.chip(flip_x, flip_y, flip_core), self.t)

    def up(self):
        return (self.d, lax.rem(self.t + 1, self.n_line))

    def down(self):
        return (self.d, lax.rem(self.t + self.n_line - 1, self.n_line))

    def meet(self, everyone=False):
        barrier = pltpu.get_barrier_semaphore()

        def greet(device):
            pl.semaphore_signal(barrier, inc=1, device_id=device, device_id_type=MESH)

        if everyone:
            for i in range(1, self.n_dp):
                greet((lax.rem(self.d + i, self.n_dp), self.t))
            for i in range(1, self.n_line):
                greet((self.d, lax.rem(self.t + i, self.n_line)))
            pl.semaphore_wait(barrier, self.n_dp + self.n_line - 2)
            return
        for flips in ((1, 0), (0, 1), (0, 0, 1)):
            greet(self.at(*flips))
        below, above = self.t > 0, self.t < self.n_line - 1

        @pl.when(below)
        def _():
            greet(self.down())

        @pl.when(above)
        def _():
            greet(self.up())

        pl.semaphore_wait(barrier, 3 + below.astype(jnp.int32) + above.astype(jnp.int32))


class Fetch:
    def __init__(self, pairs, sems):
        self.copies = [
            pltpu.make_async_copy(src, dst, sems.at[i]) for i, (src, dst) in enumerate(pairs)
        ]

    def start(self, *which):
        for i in which:
            self.copies[i].start()

    def wait(self, *which):
        for i in which:
            self.copies[i].wait()


def vmem_like(array):
    return pltpu.VMEM(array.shape, array.dtype)


class Kept:
    def __init__(self, src, dst, held, sems):
        self.there = pltpu.make_async_copy(src, held, sems.at[0])
        self.back = pltpu.make_async_copy(held, dst, sems.at[1])

    def begin(self):
        self.there.start()

    def turn(self):
        self.there.wait()
        self.back.start()

    def finish(self):
        self.back.wait()


class GatherPlane:
    def __init__(self, place, src, dst, send, recv, local, held):
        self.p, self.src, self.dst = place, src, dst
        self.rows = src.shape[0]
        self.send, self.recv = send, recv
        self.keep = Kept(src, self.block(0, 0), held, local)

    def block(self, fx, fy, fc=0, part=None):
        first = self.p.chip(fx, fy, fc) * self.rows
        size = self.rows
        if part is not None:
            size = self.rows // 2
            first = first + part * size
        return self.dst.at[pl.ds(pl.multiple_of(first, 16), size)]

    def copy(self, i, src, dst, device):
        return remote(src, dst, self.send.at[i], self.recv.at[i], device)

    def outgoing(self, i):
        at, block = self.p.at, self.block
        if i == 0:
            return self.copy(0, self.src, block(0, 0), at(1, 0))
        if i == 1:
            return self.copy(1, self.src, block(0, 0), at(0, 1))
        if i == 2:
            return self.copy(2, self.src, block(0, 0), at(0, 0, 1))
        if i == 3:
            return self.copy(3, block(1, 0, 0, 0), block(1, 0, 0, 0), at(0, 1))
        if i == 4:
            return self.copy(4, block(0, 1, 0, 1), block(0, 1, 0, 1), at(1, 0))
        spot = ((1, 0), (0, 1), (1, 1, 0, 0), (1, 1, 0, 1))[i - 5]
        return self.copy(i, block(*spot), block(*spot), at(0, 0, 1))

    def arrive(self, i):
        spot = (
            (1, 0),
            (0, 1),
            (0, 0, 1),
            (1, 1, 0, 0),
            (1, 1, 0, 1),
            (1, 0, 1),
            (0, 1, 1),
            (1, 1, 1, 0),
            (1, 1, 1, 1),
        )[i]
        here = self.block(*spot)
        self.copy(i, here, here, self.p.at(0, 0, 1)).wait_recv()

    def begin(self):
        for i in (0, 1, 2):
            self.outgoing(i).start()
        self.keep.begin()

    def forward(self):
        self.keep.turn()
        self.arrive(0)
        self.outgoing(3).start()
        self.arrive(1)
        self.outgoing(4).start()
        self.outgoing(5).start()
        self.outgoing(6).start()

    def share(self):
        self.arrive(3)
        self.outgoing(7).start()
        self.arrive(4)
        self.outgoing(8).start()

    def finish(self):
        for i in (2, 5, 6, 7, 8):
            self.arrive(i)
        for i in range(9):
            self.outgoing(i).wait_send()
        self.keep.finish()


class GatherLine:
    def __init__(self, place, dst, rows, begin, span, send, recv):
        self.p, self.dst, self.rows = place, dst, rows
        self.begin, self.span = begin, span
        self.send, self.recv = send, recv
        self.last = place.n_line - 1

    def block(self, owner):
        first = owner * self.rows + self.begin
        return self.dst.at[pl.ds(pl.multiple_of(first, 8), self.span)]

    def copy(self, way, k, owner, source=None):
        to = self.p.up() if way == 0 else self.p.down()
        block = self.block(owner)
        return remote(
            block if source is None else source,
            block,
            self.send.at[way, k],
            self.recv.at[way, k],
            to,
        )

    def step(self, k, source=None):
        t, last = self.p.t, self.last
        if k > 0:
            self.arrive(k - 1)

        @pl.when((t < last) & (t >= k))
        def _():
            self.copy(0, k, t - k, source).start()

        @pl.when((t > 0) & (t + k <= last))
        def _():
            self.copy(1, k, t + k, source).start()

    def arrive(self, k):
        t, last = self.p.t, self.last

        @pl.when(t >= k + 1)
        def _():
            self.copy(0, k, t - 1 - k).wait_recv()

        @pl.when(t + k + 1 <= last)
        def _():
            self.copy(1, k, t + 1 + k).wait_recv()

    def finish(self):
        t, last = self.p.t, self.last
        self.arrive(last - 1)
        for k in range(last):

            @pl.when((t < last) & (t >= k))
            def _():
                self.copy(0, k, t - k).wait_send()

            @pl.when((t > 0) & (t + k <= last))
            def _():
                self.copy(1, k, t + k).wait_send()


class ReduceLine:
    def __init__(self, place, terms, rows, begin, span, stage, inbox, send, recv):
        self.p, self.terms, self.rows = place, terms, rows
        self.begin, self.span = begin, span
        self.stage, self.inbox = stage, inbox
        self.send, self.recv = send, recv
        self.last = place.n_line - 1

    def own(self, owner):
        first = owner * self.rows + self.begin
        return self.terms.at[pl.ds(pl.multiple_of(first, 16), self.span)]

    def copy(self, way, j, source):
        to = self.p.up() if way == 0 else self.p.down()
        return remote(
            source, self.inbox.at[way, j], self.send.at[way, j], self.recv.at[way, j], to
        )

    def ends(self):
        t, last = self.p.t, self.last

        @pl.when(t == 0)
        def _():
            for j in range(last):
                self.copy(0, j, self.own(last - j)).start()

        @pl.when(t == last)
        def _():
            for j in range(last):
                self.copy(1, j, self.own(j)).start()

    def sent(self):
        t, last = self.p.t, self.last

        @pl.when(t == 0)
        def _():
            for j in range(last):
                self.copy(0, j, self.own(last - j)).wait_send()

        @pl.when(t == last)
        def _():
            for j in range(last):
                self.copy(1, j, self.own(j)).wait_send()

    def hand_on(self, way, j):
        term = self.own(self.last - j if way == 0 else j)
        self.copy(way, j, term).wait_recv()
        self.stage[way, j] = term[...] + self.inbox[way, j]
        self.copy(way, j, self.stage.at[way, j]).start()

    def hop(self, k):
        t, last = self.p.t, self.last

        @pl.when(t == k + 1)
        def _():
            for j in range(last - 1 - k):
                self.hand_on(0, j)

        @pl.when(t == last - 1 - k)
        def _():
            for j in range(last - 1 - k):
                self.hand_on(1, j)

    def total(self, result):
        t, last = self.p.t, self.last
        result[...] = self.own(t)[...].astype(jnp.float32)

        @pl.when(t > 0)
        def _():
            j = last - t
            self.copy(0, j, self.stage.at[0, 0]).wait_recv()
            result[...] += self.inbox[0, j].astype(jnp.float32)

        @pl.when(t < last)
        def _():
            self.copy(1, t, self.stage.at[0, 0]).wait_recv()
            result[...] += self.inbox[1, t].astype(jnp.float32)

    def finish(self):
        t, last = self.p.t, self.last
        for j in range(last - 1):

            @pl.when((t > 0) & (t < last - j))
            def _():
                self.copy(0, j, self.stage.at[0, j]).wait_send()

            @pl.when((t < last) & (t > j))
            def _():
                self.copy(1, j, self.stage.at[1, j]).wait_send()


def add_rows(into, other, result=None):
    result = into if result is None else result

    def tile(i, carry):
        rows = pl.ds(pl.multiple_of(i * 16, 16), 16)
        result[rows] = into[rows] + other[rows]
        return carry

    lax.fori_loop(0, into.shape[0] // 16, tile, None)


class ReducePlane:
    chips = ((0, 0), (1, 0), (0, 1), (1, 1))

    def __init__(self, place, terms, scratch):
        self.p, self.terms = place, terms
        self.held, self.near, self.along, self.last, self.send, self.recv, self.local = scratch
        self.rows = self.held.shape[1]
        self.half = self.rows // 2

    @staticmethod
    def scratch(rows, width):
        return [
            pltpu.VMEM((4, rows, width), jnp.bfloat16),
            pltpu.VMEM((4, rows, width), jnp.bfloat16),
            pltpu.VMEM((4, rows // 2, width), jnp.bfloat16),
            pltpu.VMEM((2, rows // 2, width), jnp.bfloat16),
            pltpu.SemaphoreType.DMA((10,)),
            pltpu.SemaphoreType.DMA((10,)),
            pltpu.SemaphoreType.DMA((4,)),
        ]

    def block(self, k, other):
        first = self.p.chip(*self.chips[k], other) * self.rows
        return self.terms.at[pl.ds(pl.multiple_of(first, 16), self.rows)]

    def half_of(self, k, part):
        return self.held.at[k, pl.ds(part * self.half, self.half)]

    def load(self, k):
        return pltpu.make_async_copy(self.block(k, 0), self.held.at[k], self.local.at[k])

    def copy(self, i):
        at = self.p.at
        if i < 4:
            src, dst, to = self.block(i, 1), self.near.at[i], at(0, 0, 1)
        elif i < 8:
            src, to = (
                (self.half_of(1, 0), at(1, 0)),
                (self.half_of(3, 0), at(1, 0)),
                (self.half_of(2, 1), at(0, 1)),
                (self.half_of(3, 1), at(0, 1)),
            )[i - 4]
            dst = self.along.at[i - 4]
        else:
            src, to = ((self.half_of(2, 0), at(0, 1)), (self.half_of(1, 1), at(1, 0)))[i - 8]
            dst = self.last.at[i - 8]
        return remote(src, dst, self.send.at[i], self.recv.at[i], to)

    def begin(self):
        for k in (3, 1, 2, 0):
            self.copy(k).start()
            self.load(k).start()

    def cores(self):
        for k in (3, 1, 2, 0):
            self.load(k).wait()
            self.copy(k).wait_recv()
            add_rows(self.held.at[k], self.near.at[k])
            if k == 3:
                self.copy(5).start()
                self.copy(7).start()
            elif k == 1:
                self.copy(4).start()
            elif k == 2:
                self.copy(6).start()

    def turn(self):
        self.copy(5).wait_recv()
        add_rows(self.half_of(2, 0), self.along.at[1])
        self.copy(8).start()
        self.copy(7).wait_recv()
        add_rows(self.half_of(1, 1), self.along.at[3])
        self.copy(9).start()
        self.copy(4).wait_recv()
        add_rows(self.half_of(0, 0), self.along.at[0])
        self.copy(6).wait_recv()
        add_rows(self.half_of(0, 1), self.along.at[2])

    def finish(self, result):
        for part in (0, 1):
            self.copy(8 + part).wait_recv()
            rows = pl.ds(part * self.half, self.half)
            add_rows(self.half_of(0, part), self.last.at[part], result.at[rows])
        for i in range(10):
            self.copy(i).wait_send()


def dma_sems(*dims):
    return pltpu.SemaphoreType.DMA(dims)


def in_vmem():
    return pl.BlockSpec(memory_space=pltpu.VMEM)


def in_any():
    return pl.BlockSpec(memory_space=pl.ANY)


def comm_params(number):
    return pltpu.CompilerParams(
        collective_id=number, has_side_effects=True, vmem_limit_bytes=VMEM_BYTES
    )


def shaped(dims, kind):
    return jax.ShapeDtypeStruct(dims, kind)


def first_gather(n_dp, n_line, mats, rows_in, order):
    count = len(mats)
    parts = 2

    def kernel(*refs):
        srcs, (c, e) = refs[:count], refs[count : count + 2]
        dsts, (c_out, e_out) = refs[count + 2 : 2 * count + 2], refs[2 * count + 2 : 2 * count + 4]
        ps, pr, pl_sem, ls, lr, ll = refs[2 * count + 4 : 2 * count + 10]
        held = refs[2 * count + 10 :]
        place = Place(n_dp, n_line)
        place.meet()
        planes = [
            GatherPlane(place, a, b, ps.at[i], pr.at[i], pl_sem.at[i], held[i])
            for i, (a, b) in enumerate(zip(srcs, dsts))
        ]
        rows = c.shape[0]
        span = rows // parts
        lines = [
            GatherLine(place, c_out, rows, i * span, span, ls.at[i], lr.at[i])
            for i in range(parts)
        ]
        lines.append(
            GatherLine(place, e_out, e.shape[0], 0, e.shape[0], ls.at[parts], lr.at[parts])
        )
        for i in range(parts):
            lines[i].step(0, c.at[pl.ds(i * span, span)])
        lines[parts].step(0, e)
        early, late = planes[: count // 2], planes[count // 2 :]
        for part in early:
            part.begin()
        copies = []
        for i, (src, dst) in enumerate(((c, c_out), (e, e_out))):
            own = dst.at[pl.ds(pl.multiple_of(place.t * src.shape[0], 8), src.shape[0])]
            copies.append(Kept(src, own, held[count + i], ll.at[i]))
            copies[i].begin()
        for line in lines:
            line.step(1)
        for part in late:
            part.begin()
        for part in early:
            part.forward()
        for copy in copies:
            copy.turn()
        for line in lines:
            line.step(2)
        for part in early:
            part.share()
        for part in late:
            part.forward()
        for part in late:
            part.share()
        for part in lines + planes:
            part.finish()
        for copy in copies:
            copy.finish()

    return pl.pallas_call(
        kernel,
        out_shape=tuple(shaped((n_dp * m.shape[0], m.shape[1]), m.dtype) for m in mats)
        + (
            shaped((n_line * rows_in.shape[0], rows_in.shape[1]), rows_in.dtype),
            shaped((n_line * order.shape[0], order.shape[1]), order.dtype),
        ),
        in_specs=[in_any()] * (count + 2),
        out_specs=[in_any()] * (count + 2),
        scratch_shapes=[
            dma_sems(count, 9),
            dma_sems(count, 9),
            dma_sems(count, 2),
            dma_sems(parts + 1, 2, n_line - 1),
            dma_sems(parts + 1, 2, n_line - 1),
            dma_sems(2, 2),
        ]
        + [vmem_like(m) for m in (*mats, rows_in, order)],
        compiler_params=comm_params(1),
        name="first_gather",
    )(*mats, rows_in, order)


CHUNKS = 8
LAST_CHUNKS = 4


def line_scratch(n_line, span, width, chunks):
    hops = n_line - 1
    return [
        pltpu.VMEM((chunks, 2, hops, span, width), jnp.bfloat16),
        pltpu.VMEM((chunks, 2, hops, span, width), jnp.bfloat16),
        dma_sems(chunks, 2, hops),
        dma_sems(chunks, 2, hops),
        dma_sems(chunks, 2, hops),
        dma_sems(chunks, 2, hops),
        pltpu.VMEM((span, width), jnp.float32),
    ]


def sum_rows_and_spread(place, terms, scratch, finish_rows, spread, between):
    stage, inbox, rs, rr, gs, gr, total = scratch
    span = total.shape[0]
    count = stage.shape[0]
    rows = span * count
    hops = place.n_line - 1
    sums = [
        ReduceLine(place, terms, rows, c * span, span, stage.at[c], inbox.at[c], rs.at[c], rr.at[c])
        for c in range(count)
    ]
    gathers = []
    if spread is not None:
        gathers = [
            GatherLine(place, spread, rows, c * span, span, gs.at[c], gr.at[c])
            for c in range(count)
        ]
    sums[0].ends()

    def total_of(c):
        sums[c].total(total)
        finish_rows(c, pl.ds(c * span, span), total)
        if gathers:
            gathers[c].step(0)

    stages = [lambda c, k=k: sums[c].hop(k) for k in range(hops - 1)] + [total_of]
    lags = [LAGS[min(k, len(LAGS) - 1)] for k in range(hops)]
    if gathers:
        stages += [lambda c, k=k: gathers[c].step(k) for k in range(1, hops)]
        lags += [lags[-1] + LAG_STEP * k for k in range(1, hops)]
    for i in range(count + lags[-1]):
        if i < count:
            sums[i].sent()
        if i + 1 < count:
            sums[i + 1].ends()
        for work, lag in zip(stages, lags):
            if 0 <= i - lag < count:
                work(i - lag)
        if i in between:
            between[i]()
    for part in gathers + sums:
        part.finish()


LAGS = (0, 1, 1)
LAG_STEP = 1


def middle_gather(n_dp, n_line, terms, tokens, gain, mats):
    rows, width = tokens.shape
    count = len(mats)

    def kernel(*refs):
        s, tok, gain_ref = refs[:3]
        srcs = refs[3 : 3 + count]
        after, hidden = refs[3 + count : 5 + count]
        dsts = refs[5 + count : 5 + 2 * count]
        ps, pr, pl_sem = refs[5 + 2 * count : 8 + 2 * count]
        held = refs[8 + 2 * count : 8 + 3 * count]
        scratch = refs[8 + 3 * count :]
        place = Place(n_dp, n_line)
        place.meet()
        planes = [
            GatherPlane(place, a, b, ps.at[i], pr.at[i], pl_sem.at[i], held[i])
            for i, (a, b) in enumerate(zip(srcs, dsts))
        ]
        planes[0].begin()

        def norm(c, here, total):
            values = tok[here].astype(jnp.float32) + total[...]
            after[here] = values
            low = rms_scale(values, gain_ref[...]).astype(jnp.bfloat16)
            first = pl.multiple_of(place.t * rows, 16) + c * total.shape[0]
            hidden[pl.ds(pl.multiple_of(first, 16), total.shape[0])] = low

        between = {6: planes[0].forward, 9: planes[0].share}
        sum_rows_and_spread(place, s, scratch, norm, hidden, between)
        for part in planes:
            part.finish()

    return pl.pallas_call(
        kernel,
        out_shape=(
            shaped((rows, width), jnp.float32),
            shaped((n_line * rows, width), jnp.bfloat16),
        )
        + tuple(shaped((n_dp * m.shape[0], m.shape[1]), m.dtype) for m in mats),
        in_specs=[in_vmem()] * 3 + [in_any()] * count,
        out_specs=[in_vmem()] * 2 + [in_any()] * count,
        scratch_shapes=[dma_sems(count, 9), dma_sems(count, 9), dma_sems(count, 2)]
        + [vmem_like(m) for m in mats]
        + line_scratch(n_line, rows // CHUNKS, width, CHUNKS),
        compiler_params=comm_params(2),
        name="middle_gather",
    )(terms, tokens, gain, *mats)


def middle_sums(n_dp, n_line, terms, after, gain, grad_in, mat, hidden, grad_up, product, down):
    rows, width = after.shape
    block = mat.shape[0] // n_dp
    wide = grad_up.shape[1]
    spread_rows = n_line * rows

    def kernel(*refs):
        s, after_ref, gain_ref, g_ref, src = refs[:5]
        hid_far, gu_far, pr_far, dw_far = refs[5:9]
        grad_after, gain_sum, spread, result, up_far, feed_far = refs[9:15]
        hid, gu, pr, dw, up_out, feed, sems = refs[15:22]
        rest = refs[22:]
        fetch = Fetch(
            [
                (hid_far, hid),
                (gu_far, gu),
                (pr_far, pr),
                (dw_far, dw),
                (feed, feed_far),
                (up_out.at[0], up_far.at[pl.ds(0, width // 2)]),
                (up_out.at[1], up_far.at[pl.ds(width // 2, width // 2)]),
            ],
            sems,
        )
        fetch.start(0, 1, 2, 3)
        place = Place(n_dp, n_line)
        place.meet()
        plane = ReducePlane(place, src, rest[:7])
        scratch = rest[7:]
        plane.begin()
        gain_sum[...] = jnp.zeros_like(gain_sum)

        def norm(c, here, total):
            grad = total[...]
            grad_rows, normed = norm_back(after_ref[here], gain_ref[...], grad)
            gain_sum[...] += jnp.sum(grad * normed, axis=0, keepdims=True)
            both = g_ref[here].astype(jnp.float32) + grad_rows
            grad_after[here] = both
            first = pl.multiple_of(place.t * rows, 16) + c * total.shape[0]
            spread[pl.ds(pl.multiple_of(first, 16), total.shape[0])] = both.astype(jnp.bfloat16)

        def feed_part(i):
            cols = pl.ds(i * (width // 4), width // 4)
            feed[:, cols] = times_trans(pr[...], dw[cols]).astype(jnp.bfloat16)

        def up_part(i):
            cols = pl.ds(i * (width // 4), width // 4)
            here = pl.ds((i % 2) * (width // 4), width // 4)
            up_out[i // 2, here] = trans_times(hid[:, cols], gu[...]).astype(jnp.bfloat16)

        def early():
            plane.cores()
            fetch.wait(0, 1)

        def two():
            up_part(0)

        def three():
            up_part(1)
            fetch.start(5)

        def four():
            up_part(2)

        def five():
            up_part(3)
            fetch.start(6)
            fetch.wait(2, 3)

        def six():
            feed_part(0)

        def seven():
            plane.turn()
            feed_part(1)

        def eight():
            feed_part(2)

        def nine():
            feed_part(3)
            fetch.start(4)

        steps = {1: early, 2: two, 3: three, 4: four, 5: five, 6: six, 7: seven, 8: eight, 9: nine}
        sum_rows_and_spread(place, s, scratch, norm, spread, steps)
        plane.finish(result)
        fetch.wait(4, 5, 6)

    low, full = jnp.bfloat16, jnp.float32
    near, far = in_vmem(), in_any()
    return pl.pallas_call(
        kernel,
        out_shape=(
            shaped((rows, width), full),
            shaped((1, width), full),
            shaped((spread_rows, width), low),
            shaped((block, mat.shape[1]), low),
            shaped((width, wide), low),
            shaped((spread_rows, width), low),
        ),
        in_specs=[near] * 4 + [far] * 5,
        out_specs=[near] * 4 + [far] * 2,
        scratch_shapes=[vmem_like(m) for m in (hidden, grad_up, product, down)]
        + [
            pltpu.VMEM((2, width // 2, wide), low),
            pltpu.VMEM((spread_rows, width), low),
            dma_sems(7),
        ]
        + ReducePlane.scratch(block, mat.shape[1])
        + line_scratch(n_line, rows // CHUNKS, width, CHUNKS),
        compiler_params=comm_params(3),
        name="middle_sums",
    )(terms, after, gain, grad_in, mat, hidden, grad_up, product, down)


class Exchange:
    def __init__(self, place, axis, src, slots, send, recv, local):
        self.p, self.src, self.slots = place, src, slots
        self.over_dp = axis == "dp"
        self.size = place.n_dp if self.over_dp else place.n_line
        self.me = place.d if self.over_dp else place.t
        self.send, self.recv, self.local = send, recv, local

    def copy(self, i):
        to = lax.rem(self.me + i, self.size)
        device = (to, self.p.t) if self.over_dp else (self.p.d, to)
        return remote(
            self.src, self.slots.at[self.me], self.send.at[i - 1], self.recv.at[i - 1], device
        )

    def mine(self):
        return pltpu.make_async_copy(self.src, self.slots.at[self.me], self.local)

    def begin(self):
        for i in range(1, self.size):
            self.copy(i).start()
        self.mine().start()

    def wait(self):
        self.mine().wait()
        for i in range(1, self.size):
            self.copy(i).wait()

    def finish(self):
        self.wait()
        total = self.slots[0]
        for i in range(1, self.size):
            total = total + self.slots[i]
        return total


def last_sums(n_dp, n_line, terms, tokens, gain, grad_after, small, mats):
    rows, width = tokens.shape
    count = len(mats)
    per = len(ReducePlane.scratch(16, 128))

    def kernel(*refs):
        s, tok, gain_ref, g_ref, small_ref = refs[:5]
        srcs = refs[5 : 5 + count]
        grad_tok, small_out, first_out = refs[5 + count : 8 + count]
        results = refs[8 + count : 8 + 2 * count]
        rest = refs[8 + 2 * count :]
        own_first, row_sum = rest[count * per : count * per + 2]
        slots_a, slots_b, slots_c, slots_d = rest[count * per + 2 : count * per + 6]
        xs, xr, xl = rest[count * per + 6 : count * per + 9]
        scratch = rest[count * per + 9 :]
        place = Place(n_dp, n_line)
        place.meet(True)
        planes = [
            ReducePlane(place, srcs[i], rest[i * per : (i + 1) * per]) for i in range(count)
        ]
        for part in planes:
            part.begin()
        early = Exchange(place, "dp", small_ref, slots_a, xs.at[0], xr.at[0], xl.at[0])
        early.begin()
        own_first[...] = jnp.zeros_like(own_first)

        def norm(c, here, total):
            grad = total[...]
            grad_rows, normed = norm_back(tok[here].astype(jnp.float32), gain_ref[...], grad)
            own_first[...] += jnp.sum(grad * normed, axis=0, keepdims=True)
            grad_tok[here] = g_ref[here] + grad_rows

        def cores():
            for part in planes:
                part.cores()

        def turn():
            for part in planes:
                part.turn()

        sum_rows_and_spread(place, s, scratch, norm, None, {1: cores, 3: turn})
        first = Exchange(place, "dp", own_first, slots_b, xs.at[1], xr.at[1], xl.at[1])
        first.begin()
        small_out[...] = early.finish()
        row_sum[0:1] = small_out[0:1]
        row_sum[1:2] = first.finish()
        both = Exchange(place, "tensor", row_sum, slots_c, xs.at[2], xr.at[2], xl.at[2])
        both.begin()
        for part, result in zip(planes, results):
            part.finish(result)
        first_out[...] = both.finish()

    return pl.pallas_call(
        kernel,
        out_shape=(
            shaped((rows, width), jnp.float32),
            shaped(small.shape, jnp.float32),
            shaped((2, width), jnp.float32),
        )
        + tuple(shaped((m.shape[0] // n_dp, m.shape[1]), jnp.bfloat16) for m in mats),
        in_specs=[in_vmem()] * 5 + [in_any()] * count,
        out_specs=[in_vmem()] * (3 + count),
        scratch_shapes=sum([ReducePlane.scratch(m.shape[0] // n_dp, m.shape[1]) for m in mats], [])
        + [
            pltpu.VMEM((1, width), jnp.float32),
            pltpu.VMEM((2, width), jnp.float32),
            pltpu.VMEM((n_dp,) + small.shape, jnp.float32),
            pltpu.VMEM((n_dp, 1, width), jnp.float32),
            pltpu.VMEM((n_line, 2, width), jnp.float32),
            pltpu.VMEM((1, width), jnp.float32),
            dma_sems(3, n_dp),
            dma_sems(3, n_dp),
            dma_sems(3),
        ]
        + line_scratch(n_line, rows // LAST_CHUNKS, width, LAST_CHUNKS),
        compiler_params=comm_params(4),
        name="last_sums",
    )(terms, tokens, gain, grad_after, small, *mats)


def loop(count, body, unroll=1):
    def step(i, carry):
        body(i)
        return carry

    lax.fori_loop(0, count, step, None, unroll=unroll)


def tile_rows(i, size, ahead=0):
    return pl.ds(pl.multiple_of(i * size + ahead, 8), size)


def moved_up(values, distance, count):
    size = values.shape[0]
    return pltpu.roll(values, (size - distance) % size, 0)[:count]


def take_lanes(ref, here):
    return jnp.concatenate([ref[c, here] for c in range(ref.shape[0])], axis=1)


def put_lanes(ref, here, values):
    for c in range(ref.shape[0]):
        ref[c, here] = values[:, c * LANES : (c + 1) * LANES]


def gelu_parts(values):
    inner = GELU_C * (values + 0.044715 * (values * values * values))
    tanh = jnp.tanh(inner)
    half = 0.5 * (1.0 + tanh)
    slope = half + 0.5 * values * (1.0 - tanh * tanh) * GELU_C * (
        1.0 + 3.0 * 0.044715 * (values * values)
    )
    return values * half, slope


GELU_C = 0.7978845608028654
RIM = 128
LANES = 128
TILE = 16


def one_minus_exp(values, exponential):
    series = jnp.ones_like(values)
    for term in range(9, 1, -1):
        series = 1.0 + values * (1.0 / term) * series
    return jnp.where(values > -0.35, -values * series, 1.0 - exponential)


def rate_and_scale(pre_recur, soft, start):
    sr = jax.nn.sigmoid(pre_recur)
    log_rate = -rate_scale * sr * soft
    decay = jnp.exp(log_rate)
    rate = jnp.where(start, 0.0, decay)
    scale = jnp.where(start, 1.0, jnp.sqrt(one_minus_exp(2.0 * log_rate, decay * decay)))
    return sr, rate, scale


class RimSwap:
    def __init__(self, place, own):
        self.odd = lax.rem(place.t, 2)
        self.partner = (place.d, place.t + 1 - 2 * self.odd)
        self.first = pl.multiple_of(RIM - RIM * self.odd, RIM)
        self.edge = pl.ds(pl.multiple_of((1 - self.odd) * own + self.odd * RIM, RIM), RIM)
        self.over_there = pl.ds(pl.multiple_of(self.odd * (own + RIM), RIM), RIM)
        self.beyond = pl.ds(pl.multiple_of((1 - self.odd) * (own + RIM), RIM), RIM)

    def block(self, index, size):
        return pl.ds(pl.multiple_of(self.first + index * size, RIM), size)


def recur_forward(
    n_dp,
    n_line,
    tok_all,
    cot,
    to_place,
    to_stored,
    x_full,
    y_full,
    out_full,
    gain,
    gates,
    taps,
    soft,
    flags,
):
    rows, width = tok_all.shape
    count, own = taps.shape
    size = gates.shape[0]
    wide = own + 2 * RIM
    blocks = (wide - RIM) // size
    chunk = rows // 8
    cot_rows = cot.shape[0]
    parts = 1

    def kernel(*refs):
        (tok_far, cot_ref, plc, sto, wx_far, wy_far, wo_far, gain_ref, gw, cw, sp, fl) = refs[:12]
        far, cot_all = refs[12:23], refs[23]
        tok, wx, wy, wo = refs[24:28]
        results = refs[28:39]
        hp, xext, y, conv_low, conv, pre_r, pre_i, rate, state, merged_st, terms = results
        (h, xf, local, cum, merged, agg, slots, hs, hr, es, er, el, gs, gr, gl) = refs[39:54]
        in_sems, out_sems, cot_held = refs[54:]
        fetch = Fetch(((tok_far, tok), (wx_far, wx), (wy_far, wy), (wo_far, wo)), in_sems)
        store = Fetch(zip(results, far), out_sems)
        fetch.start(0, 1, 2, 3)
        place = Place(n_dp, n_line)
        place.meet(True)
        swap = RimSwap(place, own)
        own_cot = cot_all.at[pl.ds(pl.multiple_of(place.t * cot_rows, 16), cot_rows)]
        keep = Kept(cot_ref, own_cot, cot_held, gl)
        keep.begin()
        span = cot_rows // parts
        lines = [
            GatherLine(place, cot_all, cot_rows, c * span, span, gs.at[c], gr.at[c])
            for c in range(parts)
        ]
        for c, line in enumerate(lines):
            line.step(0, cot_ref.at[pl.ds(c * span, span)])

        def norm(i):
            here = tile_rows(i, TILE)
            h[here] = rms_scale(tok[here].astype(jnp.float32), gain_ref[...]).astype(jnp.bfloat16)

        fetch.wait(0)
        loop(rows // TILE, norm)
        fetch.wait(1)

        def project(i):
            here = tile_rows(i, 128)
            hp[here] = plain_dot(plc[here], h[...]).astype(jnp.bfloat16)
            xext[tile_rows(i, 128, 16)] = plain_dot(hp[here], wx[...]).astype(jnp.bfloat16)

        loop(rows // 128, project)
        store.start(0)
        edge = remote(
            xext.at[pl.ds(rows, 16)],
            xext.at[pl.ds(0, 16)],
            hs.at[0],
            hr.at[0],
            (lax.rem(place.d + 1, n_dp), place.t),
        )
        edge.start()
        keep.turn()
        for line in lines:
            line.step(1)

        def project_y(i):
            here = tile_rows(i, 128)
            y[here] = plain_dot(hp[here], wy[...])

        fetch.wait(2)
        loop(rows // 128, project_y)
        store.start(2)
        edge.wait()
        top = xext[pl.ds(0, 16)]
        xext[pl.ds(0, 16)] = jnp.where(place.d > 0, top, jnp.zeros_like(top))
        store.start(1)

        def widen(i):
            xf[tile_rows(i, TILE)] = xext[tile_rows(i, TILE)].astype(jnp.float32)

        loop(rows // TILE + 1, widen)

        def convolve(i):
            here = tile_rows(i, TILE)
            near = xf[pl.ds(pl.multiple_of(i * TILE + 8, 8), TILE + 8)]
            same = fl[tile_rows(i, TILE, 8)]
            total = cw[0:1] * near[8:]
            for k in range(1, count):
                total += cw[k : k + 1] * moved_up(near, 8 - k, TILE) * same[:, k : k + 1]
            conv[here] = total
            conv_low[here, RIM : RIM + own] = total.astype(jnp.bfloat16)

        loop(rows // TILE, convolve)
        store.start(4)
        rim = remote(
            conv_low.at[:, swap.edge],
            conv_low.at[:, swap.over_there],
            hs.at[1],
            hr.at[1],
            swap.partner,
        )
        rim.start()
        for i in range(blocks):
            index = lax.rem(i + swap.odd, blocks)
            cols = swap.block(index, size)
            other = pl.ds(pl.multiple_of(wide + swap.first + index * size, RIM), size)
            if i == blocks - 1:
                rim.wait()
            pre_r[:, cols] = plain_dot(conv_low[:, cols], gw[:, cols])
            pre_i[:, cols] = plain_dot(conv_low[:, cols], gw[:, other])

        store.start(3, 5, 6)

        def drive(i):
            here = tile_rows(i, TILE)
            start = fl[tile_rows(i, TILE, 8)][:, 0:1] > 0.0
            own_cols = pl.ds(RIM, own)
            _, decay, scale = rate_and_scale(pre_r[here, own_cols], sp[...], start)
            put_lanes(rate, here, decay)
            put_lanes(local, here, conv[here] * jax.nn.sigmoid(pre_i[here, own_cols]) * scale)

        loop(rows // TILE, drive)
        store.start(7)
        for line in lines:
            line.step(2)
        groups = own // LANES

        def scan(i, carry):
            here = pl.ds(i, 8, chunk)
            result = []
            for c in range(groups):
                product, total = carry[c]
                r = rate[c, here]
                product = product * r
                total = total * r + local[c, here]
                cum[c, here] = product
                local[c, here] = total
                result.append((product, total))
            return tuple(result)

        blank = (jnp.ones((8, LANES), jnp.float32), jnp.zeros((8, LANES), jnp.float32))
        lax.fori_loop(0, chunk, scan, (blank,) * groups)
        product, total = jnp.ones((1, own), jnp.float32), jnp.zeros((1, own), jnp.float32)
        for j in range(8):
            last = pl.ds(j * chunk + chunk - 1, 1)
            total = take_lanes(local, last) + take_lanes(cum, last) * total
            product = product * take_lanes(cum, last)
        agg[0:1] = product
        agg[1:2] = total
        swap_all = Exchange(place, "dp", agg, slots, es, er, el)
        swap_all.begin()
        swap_all.wait()
        entry = jnp.zeros((1, own), jnp.float32)
        for q in range(n_dp):
            longer = slots[q, 1:2] + slots[q, 0:1] * entry
            entry = jnp.where(q < place.d, longer, entry)
        state[pl.ds(0, 8)] = jnp.broadcast_to(entry, (8, own))
        for j in range(8):

            def settle(i, entry=entry):
                here = tile_rows(i, TILE, j * chunk)
                values = take_lanes(local, here) + take_lanes(cum, here) * entry
                state[tile_rows(i, TILE, j * chunk + 8)] = values
                merged[here] = (values * gelu_parts(y[here])[0]).astype(jnp.bfloat16)

            loop(chunk // TILE, settle)
            last = pl.ds(j * chunk + chunk - 1, 1)
            entry = take_lanes(local, last) + take_lanes(cum, last) * entry
        store.start(8)
        merged_st[...] = plain_dot(sto[...], merged[...]).astype(jnp.bfloat16)

        store.start(9)
        fetch.wait(3)

        def mix(i):
            some = tile_rows(i, 512)
            terms[:, pl.ds(pl.multiple_of(i * 512, 512), 512)] = times_trans(
                merged_st[...], wo[some, :]
            ).astype(jnp.bfloat16)

        loop(width // 512, mix)
        for line in lines:
            line.finish()
        keep.finish()
        store.start(10)
        store.wait(*range(11))

    low, full = jnp.bfloat16, jnp.float32
    results = (
        shaped((rows, width), low),
        shaped((rows + 16, own), low),
        shaped((rows, own), full),
        shaped((rows, wide), low),
        shaped((rows, own), full),
        shaped((rows, wide), full),
        shaped((rows, wide), full),
        shaped((own // LANES, rows, LANES), full),
        shaped((rows + 8, own), full),
        shaped((rows, own), low),
        shaped((rows, width), low),
    )
    near, far = in_vmem(), in_any()
    return pl.pallas_call(
        kernel,
        out_shape=results + (shaped((n_line * cot_rows, width), low),),
        in_specs=[far, far, near, near, far, far, far] + [near] * 5,
        out_specs=[far] * 12,
        scratch_shapes=[vmem_like(m) for m in (tok_all, x_full, y_full, out_full) + results]
        + [
            pltpu.VMEM((rows, width), low),
            pltpu.VMEM((rows + 16, own), full),
            pltpu.VMEM((own // LANES, rows, LANES), full),
            pltpu.VMEM((own // LANES, rows, LANES), full),
            pltpu.VMEM((rows, own), low),
            pltpu.VMEM((2, own), full),
            pltpu.VMEM((n_dp, 2, own), full),
            dma_sems(2),
            dma_sems(2),
            dma_sems(n_dp),
            dma_sems(n_dp),
            pltpu.SemaphoreType.DMA,
            dma_sems(parts, 2, n_line - 1),
            dma_sems(parts, 2, n_line - 1),
            dma_sems(2),
            dma_sems(4),
            dma_sems(11),
            vmem_like(cot),
        ],
        compiler_params=comm_params(5),
        name="recur_forward",
    )(
        tok_all,
        cot,
        to_place,
        to_stored,
        x_full,
        y_full,
        out_full,
        gain,
        gates,
        taps,
        soft,
        flags,
    )


def recur_backward(
    n_dp,
    n_line,
    mixer_in,
    to_place,
    to_stored,
    x_full,
    y_full,
    out_full,
    gates,
    taps,
    soft,
    slope,
    flags,
    kept,
    weight_terms,
):
    rows, width = mixer_in.shape
    count, own = taps.shape
    size = gates.shape[0]
    wide = own + 2 * RIM
    blocks = (wide - RIM) // size
    chunk = rows // 8

    def kernel(*refs):
        (mix_far, plc, sto, wx_far, wy_far, wo_far, gw, cw, sp, sg, fl) = refs[:11]
        kept_far, weights = refs[11:19], refs[19]
        (gxy_far, gate_grads, tap_grads, decay_grad, terms_far, weight_sum) = refs[20:26]
        mix, wx, wy, wo = refs[26:30]
        (xext, y, conv_low, conv, pre_r, pre_i, rate, state) = refs[30:38]
        (gxy, mp, gm, lam, reach, gp_r, gp_i, grad, spread, rim_out, rim_in) = refs[38:49]
        (ret_out, ret_in, tap_sums, decay_sums, ends, agg, slots) = refs[49:56]
        (hs, hr, es, er, el, in_sems, out_sems) = refs[56:63]
        terms = mix
        fetch = Fetch(
            [
                (mix_far, mix),
                (wo_far, wo),
                (kept_far[1], y),
                (kept_far[7], state),
                (kept_far[6], rate),
                (kept_far[4], pre_r),
                (kept_far[5], pre_i),
                (kept_far[3], conv),
                (kept_far[2], conv_low),
                (kept_far[0], xext),
                (wx_far, wx),
                (wy_far, wy),
            ],
            in_sems,
        )
        fetch.start(*range(12))
        store = Fetch(((gxy, gxy_far), (terms, terms_far)), out_sems)
        place = Place(n_dp, n_line)
        place.meet(True)
        plane = ReducePlane(place, weights, refs[63:])
        plane.begin()
        swap = RimSwap(place, own)
        own_cols = pl.ds(RIM, own)

        def project(i):
            here = tile_rows(i, 128)
            mp[here] = plain_dot(plc[here], mix[...]).astype(jnp.bfloat16)
            gm[here] = plain_dot(mp[here], wo[...])

        fetch.wait(0, 1)
        loop(rows // 128, project)

        def split(i):
            here = tile_rows(i, TILE)
            branch, slope_y = gelu_parts(y[here])
            grads = gm[here]
            put_lanes(lam, here, grads * branch)
            values = state[tile_rows(i, TILE, 8)]
            gxy[here, own:] = (grads * values * slope_y).astype(jnp.bfloat16)

        fetch.wait(2, 3)
        loop(rows // TILE, split)
        fetch.wait(4)
        groups = own // LANES

        def scan(i, carry):
            here = pl.ds(chunk - 1 - i, 8, chunk)
            result = []
            for c in range(groups):
                product, message = carry[c]
                r = rate[c, here]
                value = lam[c, here] + message
                lam[c, here] = value
                reach[c, here] = product
                result.append((product * r, value * r))
            return tuple(result)

        blank = (jnp.ones((8, LANES), jnp.float32), jnp.zeros((8, LANES), jnp.float32))
        done = lax.fori_loop(0, chunk, scan, (blank,) * groups)
        for c in range(groups):
            lanes = pl.ds(c * LANES, LANES)
            ends[0, :, lanes] = done[c][0]
            ends[1, :, lanes] = done[c][1]
        product, message = jnp.ones((1, own), jnp.float32), jnp.zeros((1, own), jnp.float32)
        for j in reversed(range(8)):
            message = ends[1, j : j + 1] + ends[0, j : j + 1] * message
            product = product * ends[0, j : j + 1]
        agg[0:1] = product
        agg[1:2] = message
        swap_all = Exchange(place, "dp", agg, slots, es, er, el)
        swap_all.begin()
        plane.cores()
        swap_all.wait()
        entry = jnp.zeros((1, own), jnp.float32)
        for q in reversed(range(n_dp)):
            longer = slots[q, 1:2] + slots[q, 0:1] * entry
            entry = jnp.where(q > place.d, longer, entry)
        fetch.wait(5, 6, 7)
        for ref in (tap_sums, decay_sums):
            ref[...] = jnp.zeros_like(ref)
        for ref in (gp_r, gp_i):
            ref[:, 0:RIM] = jnp.zeros((rows, RIM), jnp.bfloat16)
            ref[:, RIM + own :] = jnp.zeros((rows, RIM), jnp.bfloat16)
        grad[pl.ds(0, 8)] = jnp.zeros((8, own), jnp.float32)
        grad[pl.ds(rows + 8, 8)] = jnp.zeros((8, own), jnp.float32)
        for j in reversed(range(8)):

            def back(i, entry=entry):
                here = tile_rows(i, TILE, j * chunk)
                flag = fl[tile_rows(i, TILE, j * chunk + 8)]
                start = flag[:, 0:1] > 0.0
                values = take_lanes(lam, here) + take_lanes(reach, here) * entry
                before = moved_up(
                    state[pl.ds(pl.multiple_of(j * chunk + i * TILE, 8), TILE + 8)], 7, TILE
                )
                sr, decay, scale = rate_and_scale(pre_r[here, own_cols], sp[...], start)
                si = jax.nn.sigmoid(pre_i[here, own_cols])
                block = conv[here]
                driven = values * si
                log_grad = values * before * decay - block * driven * (decay * decay) / scale
                log_grad = jnp.where(start, 0.0, log_grad)
                inner = sr * log_grad
                gp_r[here, own_cols] = (
                    -rate_scale * sp[...] * inner * (1.0 - sr)
                ).astype(jnp.bfloat16)
                gp_i[here, own_cols] = (driven * block * (1.0 - si) * scale).astype(jnp.bfloat16)
                grad[tile_rows(i, TILE, j * chunk + 8)] = driven * scale
                decay_sums[...] += inner[:8] + inner[8:]

            loop(chunk // TILE, back)
            entry = ends[1, j : j + 1] + ends[0, j : j + 1] * entry
        decay_grad[...] = rate_scale * sg[...] * jnp.sum(decay_sums[...], axis=0, keepdims=True)

        for i in range(blocks):
            index = lax.rem(i + 2 - 2 * swap.odd, blocks)
            cols = swap.block(index, size)
            other = pl.ds(pl.multiple_of(wide + swap.first + index * size, RIM), size)
            spread[:, cols] = times_trans(gp_r[:, cols], gw[:, cols]) + times_trans(
                gp_i[:, cols], gw[:, other]
            )
            if i == 0:
                rim_out[...] = spread[:, swap.beyond].astype(jnp.bfloat16)
                rim = remote(rim_out, rim_in, hs.at[0], hr.at[0], swap.partner)
                rim.start()
        rim.wait()
        shared = pl.ds(pl.multiple_of((1 - swap.odd) * (own - RIM), RIM), RIM)

        def join(i):
            here = tile_rows(i, TILE)
            there = tile_rows(i, TILE, 8)
            grad[there] += spread[here, own_cols]
            grad[there, shared] += rim_in[here].astype(jnp.float32)

        loop(rows // TILE, join)

        near = grad[pl.ds(0, 16)]
        back_rows = jnp.zeros((8, own), jnp.float32)
        for k in range(1, count):
            masked = near * fl[pl.ds(0, 16)][:, k : k + 1]
            back_rows += cw[k : k + 1] * moved_up(masked, k, 8)
        ret_out[...] = back_rows
        ret = remote(
            ret_out,
            ret_in,
            hs.at[1],
            hr.at[1],
            (lax.rem(place.d + n_dp - 1, n_dp), place.t),
        )
        ret.start()
        fetch.wait(8)
        for i in range(blocks):
            cols = swap.block(i, size)
            spread[0:size, cols] = trans_times(conv_low[:, cols], gp_r[:, cols])
            spread[size : 2 * size, cols] = trans_times(conv_low[:, cols], gp_i[:, cols])
        gate_grads[:, 0:own] = spread[0:size, own_cols].astype(jnp.bfloat16)
        gate_grads[:, own:] = spread[size : 2 * size, own_cols].astype(jnp.bfloat16)

        def taps_back(i, added=None):
            here = tile_rows(i, TILE)
            start = pl.ds(pl.multiple_of(i * TILE + 8, 8), TILE + 8)
            after = grad[start]
            flag = fl[start]
            behind = xext[pl.ds(pl.multiple_of(i * TILE, 16), 2 * TILE)].astype(jnp.float32)
            total = cw[0:1] * after[:TILE]
            for k in range(count):
                if k > 0:
                    masked = after * flag[:, k : k + 1]
                    total += cw[k : k + 1] * moved_up(masked, k, TILE)
                    mine = masked[:TILE]
                else:
                    mine = after[:TILE]
                term = mine * moved_up(behind, 16 - k, TILE)
                tap_sums[k] += term[:8] + term[8:]
            if added is not None:
                total = total + jnp.concatenate([jnp.zeros((8, own), jnp.float32), added], axis=0)
            gxy[here, 0:own] = total.astype(jnp.bfloat16)

        fetch.wait(9)
        loop(rows // TILE - 1, taps_back)
        ret.wait()
        taps_back(rows // TILE - 1, jnp.where(place.d < n_dp - 1, ret_in[...], 0.0))
        tap_grads[...] = jnp.zeros_like(tap_grads)
        for k in range(count):
            tap_grads[k : k + 1] = jnp.sum(tap_sums[k], axis=0, keepdims=True)

        store.start(0)
        plane.turn()

        def restore(i):
            here = tile_rows(i, 128)
            mp[here, 0 : 2 * own] = plain_dot(sto[here], gxy[...]).astype(jnp.bfloat16)

        loop(rows // 128, restore)

        def spread_back(i):
            some = tile_rows(i, 512)
            terms[:, pl.ds(pl.multiple_of(i * 512, 512), 512)] = (
                times_trans(mp[:, 0:own], wx[some]) + times_trans(mp[:, own : 2 * own], wy[some])
            ).astype(jnp.bfloat16)

        fetch.wait(10, 11)
        loop(width // 512, spread_back)
        store.start(1)
        plane.finish(weight_sum)
        store.wait(0, 1)

    low, full = jnp.bfloat16, jnp.float32
    block = weight_terms.shape[0] // n_dp
    near, far = in_vmem(), in_any()
    return pl.pallas_call(
        kernel,
        out_shape=(
            shaped((rows, 2 * own), low),
            shaped((size, 2 * own), low),
            shaped((8, own), full),
            shaped((1, own), full),
            shaped((rows, width), low),
            shaped((block, weight_terms.shape[1]), low),
        ),
        in_specs=[far, near, near, far, far, far] + [near] * 5 + [far] * 9,
        out_specs=[far, near, near, near, far, near],
        scratch_shapes=[vmem_like(m) for m in (mixer_in, x_full, y_full, out_full, *kept)]
        + [
            pltpu.VMEM((rows, 2 * own), low),
            pltpu.VMEM((rows, width), low),
            pltpu.VMEM((rows, own), full),
            pltpu.VMEM((own // LANES, rows, LANES), full),
            pltpu.VMEM((own // LANES, rows, LANES), full),
            pltpu.VMEM((rows, wide), low),
            pltpu.VMEM((rows, wide), low),
            pltpu.VMEM((rows + 16, own), full),
            pltpu.VMEM((rows, wide), full),
            pltpu.VMEM((rows, RIM), low),
            pltpu.VMEM((rows, RIM), low),
            pltpu.VMEM((8, own), full),
            pltpu.VMEM((8, own), full),
            pltpu.VMEM((count, 8, own), full),
            pltpu.VMEM((8, own), full),
            pltpu.VMEM((2, 8, own), full),
            pltpu.VMEM((2, own), full),
            pltpu.VMEM((n_dp, 2, own), full),
            dma_sems(2),
            dma_sems(2),
            dma_sems(n_dp),
            dma_sems(n_dp),
            pltpu.SemaphoreType.DMA,
            dma_sems(12),
            dma_sems(2),
        ]
        + ReducePlane.scratch(block, weight_terms.shape[1]),
        compiler_params=comm_params(6),
        name="recur_backward",
    )(
        mixer_in,
        to_place,
        to_stored,
        x_full,
        y_full,
        out_full,
        gates,
        taps,
        soft,
        slope,
        flags,
        *kept,
        weight_terms,
    )


def matches(mesh):
    return mesh.shape["dp"] == 8 and mesh.shape["tensor"] == 4


def local_blocks(
    tokens,
    norm_gain,
    x_weight,
    y_weight,
    conv_weight,
    recur_gate_weight,
    input_gate_weight,
    decay_param,
    out_weight,
    mlp_gain,
    gate_weight,
    up_weight,
    down_weight,
    seq_lengths,
    token_order,
    cotangent,
):
    n_dp, n_tensor = lax.axis_size("dp"), lax.axis_size("tensor")
    tensor_index = lax.axis_index("tensor")
    dp_index = lax.axis_index("dp")
    tok_rows, width = tokens.shape
    row_count = tok_rows * n_tensor
    own_width = conv_weight.shape[1]
    kernel_taps = conv_weight.shape[0]
    edge_rows = kernel_taps - 1
    dp_width = norm_gain.shape[0]
    gate_rows = recur_gate_weight.shape[0]
    own_start = tensor_index * tok_rows

    gains = jnp.concatenate([norm_gain, mlp_gain])
    spare = gate_rows * 128 - gains.shape[0]
    gains = jnp.pad(gains, (0, spare)).reshape(gate_rows, 128)
    minor = jnp.concatenate([recur_gate_weight, input_gate_weight, gains], axis=1)
    own_order = (token_order - dp_index * row_count).astype(jnp.int32)
    order_rows = jnp.broadcast_to(own_order[None, :], (8, tok_rows))
    x_full, y_full, out_full, minor_full, tok_all, order_full = first_gather(
        n_dp, n_tensor, (x_weight, y_weight, out_weight.T, minor), tokens, order_rows
    )
    late_up, late_down, _ = lax.optimization_barrier((up_weight, down_weight.T, tok_all))
    up_full = lax.all_gather(late_up, "dp", axis=0, tiled=True)
    down_full = lax.all_gather(late_down, "dp", axis=0, tiled=True)
    order_all = order_full.reshape(n_tensor, 8, tok_rows)[:, 0].reshape(row_count)
    both_gates = minor_full[:, : 2 * own_width]
    gain_rows = minor_full[:, 2 * own_width :].reshape(n_dp, -1)
    first_gain = gain_rows[:, :dp_width].reshape(1, width).astype(jnp.float32)
    second_gain = gain_rows[:, dp_width : 2 * dp_width].reshape(1, width).astype(jnp.float32)
    block_size = both_gates.shape[0]
    row_index = jnp.arange(row_count, dtype=jnp.int32)
    hits = row_index[:, None] == order_all[None, :]
    to_place = hits.astype(jnp.bfloat16)
    to_stored = (order_all[:, None] == row_index[None, :]).astype(jnp.bfloat16)
    places = dp_index * row_count + jnp.arange(-8, row_count + 8, dtype=jnp.int32)
    inside = (jnp.arange(row_count + 16) >= 8) & (jnp.arange(row_count + 16) < row_count + 8)
    ends = jnp.cumsum(seq_lengths)
    segment = segment_of(places, ends)
    starts = (places == 0) | (segment != segment_of(places - 1, ends))
    columns = [starts] + [
        segment_of(places - shift, ends) == segment for shift in range(1, kernel_taps)
    ]
    columns += [jnp.zeros_like(starts)] * (8 - len(columns))
    flags = (jnp.stack(columns, axis=1) & inside[:, None]).astype(jnp.float32)
    live_own = (token_order < ends[-1]).astype(jnp.float32)
    grad_in_own = (cotangent.astype(jnp.float32) * live_own[:, None]).astype(jnp.bfloat16)
    soft = jax.nn.softplus(-decay_param).reshape(1, own_width)
    slope = jax.nn.sigmoid(-decay_param).reshape(1, own_width)
    zero_rim = jnp.zeros((block_size, RIM), jnp.bfloat16)
    gates_wide = jnp.concatenate(
        [
            zero_rim,
            both_gates[:, :own_width],
            zero_rim,
            zero_rim,
            both_gates[:, own_width:],
            zero_rim,
        ],
        axis=1,
    )
    def glu(gate_pre, up_pre):
        return gelu_tanh(gate_pre) * up_pre

    hidden_place, *kept, merged_stored, mixer_terms, down_in = recur_forward(
        n_dp,
        n_tensor,
        tok_all,
        grad_in_own,
        to_place,
        to_stored,
        x_full,
        y_full,
        out_full,
        first_gain,
        gates_wide,
        conv_weight,
        soft,
        flags,
    )
    after_own, hidden_two, gate_full = middle_gather(
        n_dp, n_tensor, mixer_terms, tokens, second_gain, (gate_weight,)
    )
    gate_pre = plain_dot(hidden_two, gate_full)
    up_pre = plain_dot(hidden_two, up_full)
    glu_out, glu_pull = jax.vjp(glu, gate_pre, up_pre)
    product = glu_out.astype(jnp.bfloat16)
    grad_down = trans_times(down_in, product).astype(jnp.bfloat16)
    down_sum = lax.psum_scatter(grad_down, "dp", scatter_dimension=0, tiled=True)
    down_in, _ = lax.optimization_barrier((down_in, grad_down))
    grad_product = plain_dot(down_in, down_full)
    grad_gate_pre, grad_up_pre = glu_pull(grad_product)
    grad_gate_pre = grad_gate_pre.astype(jnp.bfloat16)
    grad_up_pre = grad_up_pre.astype(jnp.bfloat16)
    grad_gate = trans_times(hidden_two, grad_gate_pre).astype(jnp.bfloat16)
    back_terms = (
        times_trans(grad_gate_pre, gate_full) + times_trans(grad_up_pre, up_full)
    ).astype(jnp.bfloat16)
    grad_after_own, second_part, mixer_in, gate_sum, grad_up, feed_terms = middle_sums(
        n_dp,
        n_tensor,
        back_terms,
        after_own,
        second_gain,
        grad_in_own,
        grad_gate,
        hidden_two,
        grad_up_pre,
        product,
        down_full,
    )
    feed_out = lax.psum_scatter(
        feed_terms,
        "tensor",
        scatter_dimension=0,
        tiled=True,
    ).astype(jnp.float32)
    output = ((after_own + feed_out) * live_own[:, None]).astype(jnp.bfloat16)

    grad_xy, gate_grads, tap_grads, decay_grad, one_terms, up_sum = recur_backward(
        n_dp,
        n_tensor,
        mixer_in,
        to_place,
        to_stored,
        x_full,
        y_full,
        out_full,
        gates_wide,
        conv_weight,
        soft,
        slope,
        flags,
        kept,
        grad_up,
    )
    grad_out_mat = trans_times(mixer_in, merged_stored).astype(jnp.bfloat16)
    grad_xy_mat = trans_times(hidden_place, grad_xy).astype(jnp.bfloat16)
    small = jnp.concatenate(
        [
            second_part,
            tap_grads[:kernel_taps].reshape(1, -1),
            jnp.pad(decay_grad, ((0, 0), (0, width - own_width))),
            jnp.zeros((1, width), jnp.float32),
        ],
        axis=0,
    )
    grad_tokens, small_sum, gain_sums, xy_sum, out_sum, gates_sum = last_sums(
        n_dp,
        n_tensor,
        one_terms,
        tokens,
        first_gain,
        grad_after_own,
        small,
        (grad_xy_mat, grad_out_mat, gate_grads),
    )
    xy_sum, gates_sum = xy_sum.astype(jnp.float32), gates_sum.astype(jnp.float32)
    own_gains = lax.dynamic_slice_in_dim(gain_sums, dp_index * dp_width, dp_width, 1)
    return (
        output,
        grad_tokens,
        own_gains[1],
        xy_sum[:, :own_width],
        xy_sum[:, own_width:],
        small_sum[1].reshape(kernel_taps, own_width),
        gates_sum[:, :own_width],
        gates_sum[:, own_width:],
        small_sum[2, :own_width],
        out_sum.astype(jnp.float32).T,
        own_gains[0],
        gate_sum.astype(jnp.float32),
        up_sum.astype(jnp.float32),
        down_sum.astype(jnp.float32).T,
    )


def solution(mesh):
    in_specs = (
        P(("dp", "tensor"), None),
        P("dp"),
        P("dp", "tensor"),
        P("dp", "tensor"),
        P(None, "tensor"),
        P("dp", "tensor"),
        P("dp", "tensor"),
        P("tensor"),
        P("tensor", "dp"),
        P("dp"),
        P("dp", "tensor"),
        P("dp", "tensor"),
        P("tensor", "dp"),
        P(),
        P(("dp", "tensor")),
        P(("dp", "tensor"), None),
    )
    out_specs = (
        P(("dp", "tensor"), None),
        P(("dp", "tensor"), None),
        P("dp"),
        P("dp", "tensor"),
        P("dp", "tensor"),
        P(None, "tensor"),
        P("dp", "tensor"),
        P("dp", "tensor"),
        P("tensor"),
        P("tensor", "dp"),
        P("dp"),
        P("dp", "tensor"),
        P("dp", "tensor"),
        P("tensor", "dp"),
    )
    fits = matches(mesh)
    local = local_blocks if fits else local_general
    return jax.shard_map(local, mesh=mesh, in_specs=in_specs, out_specs=out_specs, check_vma=False)
```

```python
import jax
import jax.numpy as jnp
from jax import lax
from jax.experimental import pallas as pl
from jax.experimental.pallas import tpu as pltpu
from jax.sharding import PartitionSpec as P

epsilon = 1e-06
rate_scale = 8.0


def from_behind(block, axis, distance):
    devices = range(lax.axis_size(axis))
    route = [(i - distance, i) for i in devices if i - distance in devices]
    return lax.ppermute(block, axis, route)


def extended_2(array, sides, width):
    for axis, dim in sides:
        size, length = (lax.axis_size(axis), array.shape[dim])
        up = [(i, (i + 1) % size) for i in range(size - 1)]
        down = [(j, i) for i, j in up]
        last = lax.slice_in_dim(array, length - width, length, axis=dim)
        leading = lax.slice_in_dim(array, 0, width, axis=dim)
        before = lax.ppermute(last, axis, up)
        after = lax.ppermute(leading, axis, down)
        array = jnp.concatenate([before, array, after], axis=dim)
    return array


def entering(value, axis, join, neutral, backward):
    count, mine = (lax.axis_size(axis), lax.axis_index(axis))
    pieces = jax.tree.map(lambda part: lax.all_gather(part, axis), value)
    if backward:
        pieces = jax.tree.map(lambda part: part[::-1], pieces)
        mine = count - 1 - mine
    total = jax.tree.map(
        lambda part, zero: jnp.full_like(part, 0) + jnp.asarray(zero, part.dtype), value, neutral
    )

    def lap(position, total):
        longer = join(total, jax.tree.map(lambda part: part[position], pieces))
        return jax.tree.map(lambda new, old: jnp.where(position < mine, new, old), longer, total)

    return lax.fori_loop(0, count - 1, lap, total)


def rms_scale(values, gain):
    return values * lax.rsqrt(jnp.mean(values * values, axis=-1, keepdims=True) + epsilon) * gain


def norm_back(values, gain, grad):
    inv_root = lax.rsqrt(jnp.mean(values * values, axis=-1, keepdims=True) + epsilon)
    normed = values * inv_root
    upstream = grad * gain
    grad_values = inv_root * (
        upstream - normed * jnp.mean(upstream * normed, axis=-1, keepdims=True)
    )
    return (grad_values, normed)


def segment_of(places, ends):
    return jnp.sum((ends[None, :] <= places[:, None]).astype(jnp.int32), axis=1)


def pair_step(early, later):
    return (early[0] * later[0], later[0] * early[1] + later[1])


def plain_dot(left, right):
    return jnp.dot(left, right, preferred_element_type=jnp.float32)


def times_trans(left, right):
    return lax.dot_general(
        left, right, (((1,), (1,)), ((), ())), preferred_element_type=jnp.float32
    )


def trans_times(left, right):
    return lax.dot_general(
        left, right, (((0,), (0,)), ((), ())), preferred_element_type=jnp.float32
    )


def gelu_tanh(values):
    return jax.nn.gelu(values, approximate=True)


def collect(
    norm_gain,
    mlp_gain,
    x_weight,
    y_weight,
    recur_gate_weight,
    input_gate_weight,
    gate_weight,
    up_weight,
    out_weight,
    down_weight,
):
    return (
        lax.all_gather(norm_gain, "dp", axis=0, tiled=True),
        lax.all_gather(mlp_gain, "dp", axis=0, tiled=True),
        lax.all_gather(x_weight, "dp", axis=0, tiled=True),
        lax.all_gather(y_weight, "dp", axis=0, tiled=True),
        lax.all_gather(recur_gate_weight, "dp", axis=0, tiled=True),
        lax.all_gather(input_gate_weight, "dp", axis=0, tiled=True),
        lax.all_gather(gate_weight, "dp", axis=0, tiled=True),
        lax.all_gather(up_weight, "dp", axis=0, tiled=True),
        lax.all_gather(out_weight, "dp", axis=1, tiled=True),
        lax.all_gather(down_weight, "dp", axis=1, tiled=True),
    )


def row_sums(term_rows, tok_rows):
    return lax.psum_scatter(
        term_rows(jnp.int32(0), lax.axis_size("tensor") * tok_rows).astype(jnp.bfloat16),
        "tensor",
        scatter_dimension=0,
        tiled=True,
    ).astype(jnp.float32)


def spread_rows(values):
    return lax.all_gather(values, "tensor", axis=0, tiled=True)


def local_general(
    tokens,
    norm_gain,
    x_weight,
    y_weight,
    conv_weight,
    recur_gate_weight,
    input_gate_weight,
    decay_param,
    out_weight,
    mlp_gain,
    gate_weight,
    up_weight,
    down_weight,
    seq_lengths,
    token_order,
    cotangent,
):
    n_tensor = lax.axis_size("tensor")
    tensor_index = lax.axis_index("tensor")
    dp_index = lax.axis_index("dp")
    tok_rows = tokens.shape[0]
    row_count = tok_rows * n_tensor
    own_width = conv_weight.shape[1]
    kernel_taps = conv_weight.shape[0]
    edge_rows = kernel_taps - 1
    dp_width = norm_gain.shape[0]
    own_start = tensor_index * tok_rows
    shards = (
        norm_gain,
        mlp_gain,
        x_weight,
        y_weight,
        recur_gate_weight,
        input_gate_weight,
        gate_weight,
        up_weight,
        out_weight,
        down_weight,
    )
    (
        gain_one,
        gain_two,
        x_full,
        y_full,
        recur_full,
        input_full,
        gate_full,
        up_full,
        out_full,
        down_full,
    ) = collect(*shards)
    block_size = recur_full.shape[0]
    first_gain = gain_one.astype(jnp.float32)
    second_gain = gain_two.astype(jnp.float32)
    both_gates = jnp.concatenate([recur_full, input_full], axis=1)
    tok_own = tokens.astype(jnp.float32)
    own_order = token_order - dp_index * row_count
    first_rows = rms_scale(tok_own, first_gain).astype(jnp.bfloat16)
    first_all, cot_all, order_all = (
        lax.all_gather(first_rows, "tensor", axis=0, tiled=True),
        lax.all_gather(cotangent, "tensor", axis=0, tiled=True),
        lax.all_gather(own_order, "tensor", axis=0, tiled=True),
    )
    row_index = jnp.arange(row_count, dtype=jnp.int32)
    inverse = jnp.zeros((row_count,), jnp.int32).at[order_all].set(row_index)
    hidden_place = jnp.take(first_all, inverse, axis=0)
    places = dp_index * row_count + row_index
    ends = jnp.cumsum(seq_lengths)
    segment = segment_of(places, ends)
    starts = (places == 0) | (segment != segment_of(places - 1, ends))
    live = (places < ends[-1]).astype(jnp.float32)
    live_stored = jnp.take(live, order_all, axis=0)
    same = [
        (segment_of(places - shift, ends) == segment).astype(jnp.float32)
        for shift in range(kernel_taps)
    ]
    low_edge = tensor_index * own_width
    own_blocks = (low_edge + jnp.arange(own_width, dtype=jnp.int32)) // block_size
    first_block = low_edge // block_size
    block_count = own_width // block_size + 2

    def block_start(index):
        return (first_block + index) * block_size - low_edge + block_size

    def block_mask(index):
        inside = own_blocks == first_block + index
        return jnp.concatenate([inside, inside])

    def convolve(extended, kernel):
        return sum(
            (
                kernel[shift][None, :]
                * extended[edge_rows - shift : edge_rows - shift + row_count]
                * same[shift][:, None]
                for shift in range(kernel_taps)
            )
        )

    def gates(conv_vals, pre_recur, pre_input, decay_vals):
        log_rate = -rate_scale * jax.nn.sigmoid(pre_recur) * jax.nn.softplus(-decay_vals)
        decay_rate = jnp.where(starts[:, None], 0.0, jnp.exp(log_rate))
        scale_in = jnp.where(starts[:, None], 1.0, jnp.sqrt(-jnp.expm1(2.0 * log_rate)))
        return (decay_rate, conv_vals * jax.nn.sigmoid(pre_input) * scale_in)

    def glu(gate_pre, up_pre):
        return gelu_tanh(gate_pre) * up_pre

    x_branch = plain_dot(hidden_place, x_full).astype(jnp.bfloat16)
    y_before = plain_dot(hidden_place, y_full)
    previous = from_behind(x_branch[row_count - edge_rows :], "dp", 1)
    extended = jnp.concatenate([previous, x_branch], axis=0).astype(jnp.float32)
    conv_out = convolve(extended, conv_weight)
    conv_wide = extended_2(conv_out.astype(jnp.bfloat16), (("tensor", 1),), block_size)
    pre_both = jnp.zeros((row_count, 2 * own_width), jnp.float32)
    for index in range(block_count):
        piece = lax.dynamic_slice_in_dim(conv_wide, block_start(index), block_size, 1)
        pre_both = pre_both + jnp.where(
            block_mask(index)[None, :], plain_dot(piece, both_gates), 0.0
        )
    (decay_rate, driven), gate_pull = jax.vjp(
        gates, conv_out, pre_both[:, :own_width], pre_both[:, own_width:], decay_param
    )
    cum_rate, local_state = lax.associative_scan(pair_step, (decay_rate, driven), axis=0)
    ident = (jnp.ones((own_width,), jnp.float32), jnp.zeros((own_width,), jnp.float32))
    rate_in, state_in = entering((cum_rate[-1], local_state[-1]), "dp", pair_step, ident, False)
    state = local_state + cum_rate * state_in[None, :]
    y_branch = gelu_tanh(y_before)
    merged = (state * y_branch).astype(jnp.bfloat16)
    merged_stored = jnp.take(merged, order_all, axis=0)

    def mixer_rows(begin, number):
        return plain_dot(merged_stored, out_full)

    after_own = tok_own + row_sums(mixer_rows, tok_rows)
    hidden_two = spread_rows(rms_scale(after_own, second_gain).astype(jnp.bfloat16))
    gate_pre = plain_dot(hidden_two, gate_full)
    up_pre = plain_dot(hidden_two, up_full)
    glu_out, glu_pull = jax.vjp(glu, gate_pre, up_pre)
    product = glu_out.astype(jnp.bfloat16)

    def down_rows(begin, number):
        return plain_dot(product, down_full)

    feed_out = row_sums(down_rows, tok_rows)
    live_own = lax.dynamic_slice_in_dim(live_stored, own_start, tok_rows, 0)
    output = ((after_own + feed_out) * live_own[:, None]).astype(jnp.bfloat16)
    grad_out = cot_all.astype(jnp.float32) * live_stored[:, None]
    fresh = lax.optimization_barrier((shards, grad_out))[0]
    (
        gain_one,
        gain_two,
        x_full,
        y_full,
        recur_full,
        input_full,
        gate_full,
        up_full,
        out_full,
        down_full,
    ) = collect(*fresh)
    first_gain = gain_one.astype(jnp.float32)
    second_gain = gain_two.astype(jnp.float32)
    both_gates = jnp.concatenate([recur_full, input_full], axis=1)
    down_in = grad_out.astype(jnp.bfloat16)
    grad_down = trans_times(product, down_in)
    grad_product = times_trans(down_in, down_full)
    grad_gate_pre, grad_up_pre = glu_pull(grad_product)
    grad_gate_pre = grad_gate_pre.astype(jnp.bfloat16)
    grad_up_pre = grad_up_pre.astype(jnp.bfloat16)
    grad_gate = trans_times(hidden_two, grad_gate_pre)
    grad_up = trans_times(hidden_two, grad_up_pre)

    def feed_rows(begin, number):
        return times_trans(grad_gate_pre, gate_full) + times_trans(grad_up_pre, up_full)

    grad_out_own = lax.dynamic_slice_in_dim(grad_out, own_start, tok_rows, 0)
    grad_two_own = row_sums(feed_rows, tok_rows)
    grad_norm_own, normed_two = norm_back(after_own, second_gain, grad_two_own)
    second_part = jnp.sum(grad_two_own * normed_two, axis=0)
    grad_after_own = grad_out_own + grad_norm_own
    mixer_in = spread_rows(grad_after_own.astype(jnp.bfloat16))
    grad_out_mat = trans_times(merged_stored, mixer_in)
    grad_merged = jnp.take(times_trans(mixer_in, out_full), inverse, axis=0)
    grad_state = grad_merged * y_branch
    gelu_pull = jax.vjp(gelu_tanh, y_before)[1]
    grad_y_before = gelu_pull(grad_merged * state)[0].astype(jnp.bfloat16)
    rate_next = jnp.concatenate([decay_rate[1:], jnp.ones((1, own_width), jnp.float32)], axis=0)
    rev_rate, local_lam = lax.associative_scan(
        pair_step, (rate_next, grad_state), reverse=True, axis=0
    )
    head_rate = decay_rate[0] * rev_rate[0]
    head_lam = decay_rate[0] * local_lam[0]
    factor_in, lam_in = entering((head_rate, head_lam), "dp", pair_step, ident, True)
    lam = local_lam + rev_rate * lam_in[None, :]
    state_prev = jnp.concatenate([state_in[None, :], state[:-1]], axis=0)
    grad_conv_local, grad_pre_recur, grad_pre_input, grad_decay_own = gate_pull(
        (lam * state_prev, lam)
    )
    grad_pre = jnp.concatenate([grad_pre_recur, grad_pre_input], axis=1).astype(jnp.bfloat16)
    grad_both = jnp.zeros((block_size, 2 * own_width), jnp.float32)
    grad_wide = jnp.zeros((row_count, own_width + 2 * block_size), jnp.float32)
    for index in range(block_count):
        begin = block_start(index)
        piece = lax.dynamic_slice_in_dim(conv_wide, begin, block_size, 1)
        masked = jnp.where(block_mask(index)[None, :], grad_pre, jnp.zeros((), jnp.bfloat16))
        grad_both = grad_both + trans_times(piece, masked)
        added = lax.dynamic_slice_in_dim(grad_wide, begin, block_size, 1) + times_trans(
            masked, both_gates
        )
        grad_wide = lax.dynamic_update_slice_in_dim(grad_wide, added, begin, 1)
    grad_recur = grad_both[:, :own_width]
    grad_input = grad_both[:, own_width:]
    rims = jnp.concatenate(
        [grad_wide[:, :block_size], grad_wide[:, own_width + block_size :]], axis=1
    )
    arrived = extended_2(rims.astype(jnp.bfloat16), (("tensor", 1),), block_size).astype(rims.dtype)
    from_lower = jnp.pad(arrived[:, :block_size], ((0, 0), (0, own_width - block_size)))
    from_upper = jnp.pad(arrived[:, 3 * block_size :], ((0, 0), (own_width - block_size, 0)))
    grad_conv = (
        grad_conv_local
        + grad_wide[:, block_size : block_size + own_width]
        + from_lower
        + from_upper
    )
    conv_pull = jax.vjp(convolve, extended, conv_weight)[1]
    grad_extended, grad_kernel = conv_pull(grad_conv)
    returned = from_behind(grad_extended[:edge_rows], "dp", -1)
    grad_x_branch = grad_extended[edge_rows:] + jnp.concatenate(
        [jnp.zeros((row_count - edge_rows, own_width), jnp.float32), returned], axis=0
    )
    grad_x_low = grad_x_branch.astype(jnp.bfloat16)
    grad_x_stored = jnp.take(grad_x_low, order_all, axis=0)
    grad_y_stored = jnp.take(grad_y_before, order_all, axis=0)
    grad_x_mat = trans_times(first_all, grad_x_stored)
    grad_y_mat = trans_times(first_all, grad_y_stored)

    def mixer_back_rows(begin, number):
        return times_trans(grad_x_stored, x_full) + times_trans(grad_y_stored, y_full)

    grad_one_own = row_sums(mixer_back_rows, tok_rows)
    grad_norm_one, normed_one = norm_back(tok_own, first_gain, grad_one_own)
    first_part = jnp.sum(grad_one_own * normed_one, axis=0)
    grad_tokens = grad_after_own + grad_norm_one
    chosen = jnp.arange(n_tensor, dtype=jnp.int32) == tensor_index
    kernel_tile = jnp.where(chosen[:, None, None], grad_kernel[None, :, :], 0.0)
    decay_tile = jnp.where(chosen[:, None], grad_decay_own[None, :], 0.0)
    small = lax.psum((first_part, second_part, kernel_tile, decay_tile), ("dp", "tensor"))
    grad_first_gain = lax.dynamic_slice_in_dim(small[0], dp_index * dp_width, dp_width, 0)
    grad_second_gain = lax.dynamic_slice_in_dim(small[1], dp_index * dp_width, dp_width, 0)
    grad_kernel_sum = lax.dynamic_index_in_dim(small[2], tensor_index, 0, keepdims=False)
    grad_decay = lax.dynamic_index_in_dim(small[3], tensor_index, 0, keepdims=False)
    sums = (
        lax.psum_scatter(
            grad_x_mat.astype(jnp.bfloat16), "dp", scatter_dimension=0, tiled=True
        ).astype(jnp.float32),
        lax.psum_scatter(
            grad_y_mat.astype(jnp.bfloat16), "dp", scatter_dimension=0, tiled=True
        ).astype(jnp.float32),
        lax.psum_scatter(
            grad_recur.astype(jnp.bfloat16), "dp", scatter_dimension=0, tiled=True
        ).astype(jnp.float32),
        lax.psum_scatter(
            grad_input.astype(jnp.bfloat16), "dp", scatter_dimension=0, tiled=True
        ).astype(jnp.float32),
        lax.psum_scatter(
            grad_gate.astype(jnp.bfloat16), "dp", scatter_dimension=0, tiled=True
        ).astype(jnp.float32),
        lax.psum_scatter(
            grad_up.astype(jnp.bfloat16), "dp", scatter_dimension=0, tiled=True
        ).astype(jnp.float32),
        lax.psum_scatter(
            grad_out_mat.astype(jnp.bfloat16), "dp", scatter_dimension=1, tiled=True
        ).astype(jnp.float32),
        lax.psum_scatter(
            grad_down.astype(jnp.bfloat16), "dp", scatter_dimension=1, tiled=True
        ).astype(jnp.float32),
    )
    return (
        output,
        grad_tokens,
        grad_first_gain,
        sums[0],
        sums[1],
        grad_kernel_sum,
        sums[2],
        sums[3],
        grad_decay,
        sums[6],
        grad_second_gain,
        sums[4],
        sums[5],
        sums[7],
    )


MESH = pl.DeviceIdType.MESH
VMEM_BYTES = 60 * 2**20


def remote(src, dst, send, recv, device):
    return pltpu.make_async_remote_copy(
        src_ref=src,
        dst_ref=dst,
        send_sem=send,
        recv_sem=recv,
        device_id=device,
        device_id_type=MESH,
    )


class Place:
    def __init__(self, n_dp, n_line):
        self.n_dp, self.n_line = n_dp, n_line
        self.d, self.t = lax.axis_index("dp"), lax.axis_index("tensor")
        self.core = lax.rem(self.d, 2)
        self.x = lax.rem(lax.div(self.d, 2), 2)
        self.y = lax.div(self.d, 4)

    def chip(self, flip_x, flip_y, flip_core=0):
        x = 1 - self.x if flip_x else self.x
        y = 1 - self.y if flip_y else self.y
        core = 1 - self.core if flip_core else self.core
        return y * 4 + x * 2 + core

    def at(self, flip_x=0, flip_y=0, flip_core=0):
        return (self.chip(flip_x, flip_y, flip_core), self.t)

    def up(self):
        return (self.d, lax.rem(self.t + 1, self.n_line))

    def down(self):
        return (self.d, lax.rem(self.t + self.n_line - 1, self.n_line))

    def meet(self, everyone=False):
        barrier = pltpu.get_barrier_semaphore()

        def greet(device):
            pl.semaphore_signal(barrier, inc=1, device_id=device, device_id_type=MESH)

        if everyone:
            for i in range(1, self.n_dp):
                greet((lax.rem(self.d + i, self.n_dp), self.t))
            for i in range(1, self.n_line):
                greet((self.d, lax.rem(self.t + i, self.n_line)))
            pl.semaphore_wait(barrier, self.n_dp + self.n_line - 2)
            return
        for flips in ((1, 0), (0, 1), (0, 0, 1)):
            greet(self.at(*flips))
        below, above = self.t > 0, self.t < self.n_line - 1

        @pl.when(below)
        def _():
            greet(self.down())

        @pl.when(above)
        def _():
            greet(self.up())

        pl.semaphore_wait(barrier, 3 + below.astype(jnp.int32) + above.astype(jnp.int32))


class Fetch:
    def __init__(self, pairs, sems):
        self.copies = [
            pltpu.make_async_copy(src, dst, sems.at[i]) for i, (src, dst) in enumerate(pairs)
        ]

    def start(self, *which):
        for i in which:
            self.copies[i].start()

    def wait(self, *which):
        for i in which:
            self.copies[i].wait()


def vmem_like(array):
    return pltpu.VMEM(array.shape, array.dtype)


class Kept:
    def __init__(self, src, dst, held, sems):
        self.there = pltpu.make_async_copy(src, held, sems.at[0])
        self.back = pltpu.make_async_copy(held, dst, sems.at[1])

    def begin(self):
        self.there.start()

    def turn(self):
        self.there.wait()
        self.back.start()

    def finish(self):
        self.back.wait()


class GatherPlane:
    def __init__(self, place, src, dst, send, recv, local, held):
        self.p, self.src, self.dst = place, src, dst
        self.rows = src.shape[0]
        self.send, self.recv = send, recv
        self.keep = Kept(src, self.block(0, 0), held, local)

    def block(self, fx, fy, fc=0, part=None):
        first = self.p.chip(fx, fy, fc) * self.rows
        size = self.rows
        if part is not None:
            size = self.rows // 2
            first = first + part * size
        return self.dst.at[pl.ds(pl.multiple_of(first, 16), size)]

    def copy(self, i, src, dst, device):
        return remote(src, dst, self.send.at[i], self.recv.at[i], device)

    def outgoing(self, i):
        at, block = self.p.at, self.block
        if i == 0:
            return self.copy(0, self.src, block(0, 0), at(1, 0))
        if i == 1:
            return self.copy(1, self.src, block(0, 0), at(0, 1))
        if i == 2:
            return self.copy(2, self.src, block(0, 0), at(0, 0, 1))
        if i == 3:
            return self.copy(3, block(1, 0, 0, 0), block(1, 0, 0, 0), at(0, 1))
        if i == 4:
            return self.copy(4, block(0, 1, 0, 1), block(0, 1, 0, 1), at(1, 0))
        spot = ((1, 0), (0, 1), (1, 1, 0, 0), (1, 1, 0, 1))[i - 5]
        return self.copy(i, block(*spot), block(*spot), at(0, 0, 1))

    def arrive(self, i):
        spot = (
            (1, 0),
            (0, 1),
            (0, 0, 1),
            (1, 1, 0, 0),
            (1, 1, 0, 1),
            (1, 0, 1),
            (0, 1, 1),
            (1, 1, 1, 0),
            (1, 1, 1, 1),
        )[i]
        here = self.block(*spot)
        self.copy(i, here, here, self.p.at(0, 0, 1)).wait_recv()

    def begin(self):
        for i in (0, 1, 2):
            self.outgoing(i).start()
        self.keep.begin()

    def forward(self):
        self.keep.turn()
        self.arrive(0)
        self.outgoing(3).start()
        self.arrive(1)
        self.outgoing(4).start()
        self.outgoing(5).start()
        self.outgoing(6).start()

    def share(self):
        self.arrive(3)
        self.outgoing(7).start()
        self.arrive(4)
        self.outgoing(8).start()

    def finish(self):
        for i in (2, 5, 6, 7, 8):
            self.arrive(i)
        for i in range(9):
            self.outgoing(i).wait_send()
        self.keep.finish()


class GatherLine:
    def __init__(self, place, dst, rows, begin, span, send, recv):
        self.p, self.dst, self.rows = place, dst, rows
        self.begin, self.span = begin, span
        self.send, self.recv = send, recv
        self.last = place.n_line - 1

    def block(self, owner):
        first = owner * self.rows + self.begin
        return self.dst.at[pl.ds(pl.multiple_of(first, 8), self.span)]

    def copy(self, way, k, owner, source=None):
        to = self.p.up() if way == 0 else self.p.down()
        block = self.block(owner)
        return remote(
            block if source is None else source,
            block,
            self.send.at[way, k],
            self.recv.at[way, k],
            to,
        )

    def step(self, k, source=None):
        t, last = self.p.t, self.last
        if k > 0:
            self.arrive(k - 1)

        @pl.when((t < last) & (t >= k))
        def _():
            self.copy(0, k, t - k, source).start()

        @pl.when((t > 0) & (t + k <= last))
        def _():
            self.copy(1, k, t + k, source).start()

    def arrive(self, k):
        t, last = self.p.t, self.last

        @pl.when(t >= k + 1)
        def _():
            self.copy(0, k, t - 1 - k).wait_recv()

        @pl.when(t + k + 1 <= last)
        def _():
            self.copy(1, k, t + 1 + k).wait_recv()

    def finish(self):
        t, last = self.p.t, self.last
        self.arrive(last - 1)
        for k in range(last):

            @pl.when((t < last) & (t >= k))
            def _():
                self.copy(0, k, t - k).wait_send()

            @pl.when((t > 0) & (t + k <= last))
            def _():
                self.copy(1, k, t + k).wait_send()


class ReduceLine:
    def __init__(self, place, terms, rows, begin, span, inbox, send, recv):
        self.p, self.terms, self.rows = place, terms, rows
        self.begin, self.span = begin, span
        self.inbox = inbox
        self.send, self.recv = send, recv
        self.last = place.n_line - 1

    def own(self, owner):
        first = owner * self.rows + self.begin
        return self.terms.at[pl.ds(pl.multiple_of(first, 16), self.span)]

    def copy(self, way, j, source):
        to = self.p.up() if way == 0 else self.p.down()
        return remote(
            source, self.inbox.at[way, j], self.send.at[way, j], self.recv.at[way, j], to
        )

    def ends(self):
        t, last = self.p.t, self.last

        @pl.when(t == 0)
        def _():
            for j in range(last):
                self.copy(0, j, self.own(last - j)).start()

        @pl.when(t == last)
        def _():
            for j in range(last):
                self.copy(1, j, self.own(j)).start()

    def sent(self):
        t, last = self.p.t, self.last

        @pl.when(t == 0)
        def _():
            for j in range(last):
                self.copy(0, j, self.own(last - j)).wait_send()

        @pl.when(t == last)
        def _():
            for j in range(last):
                self.copy(1, j, self.own(j)).wait_send()

    def hand_on(self, way, j):
        term = self.own(self.last - j if way == 0 else j)
        self.copy(way, j, term).wait_recv()
        self.inbox[way, j] = term[...] + self.inbox[way, j]
        self.copy(way, j, self.inbox.at[way, j]).start()

    def hop(self, k):
        t, last = self.p.t, self.last

        @pl.when(t == k + 1)
        def _():
            for j in range(last - 1 - k):
                self.hand_on(0, j)

        @pl.when(t == last - 1 - k)
        def _():
            for j in range(last - 1 - k):
                self.hand_on(1, j)

    def total(self, result):
        t, last = self.p.t, self.last
        result[...] = self.own(t)[...].astype(jnp.float32)

        @pl.when(t > 0)
        def _():
            j = last - t
            self.copy(0, j, self.inbox.at[0, 0]).wait_recv()
            result[...] += self.inbox[0, j].astype(jnp.float32)

        @pl.when(t < last)
        def _():
            self.copy(1, t, self.inbox.at[0, 0]).wait_recv()
            result[...] += self.inbox[1, t].astype(jnp.float32)

    def finish(self):
        t, last = self.p.t, self.last
        for j in range(last - 1):

            @pl.when((t > 0) & (t < last - j))
            def _():
                self.copy(0, j, self.inbox.at[0, j]).wait_send()

            @pl.when((t < last) & (t > j))
            def _():
                self.copy(1, j, self.inbox.at[1, j]).wait_send()


def add_rows(into, other, result=None):
    result = into if result is None else result

    def tile(i, carry):
        rows = pl.ds(pl.multiple_of(i * 16, 16), 16)
        result[rows] = into[rows] + other[rows]
        return carry

    lax.fori_loop(0, into.shape[0] // 16, tile, None)


class ReducePlane:
    chips = ((0, 0), (1, 0), (0, 1), (1, 1))

    def __init__(self, place, terms, scratch):
        self.p, self.terms = place, terms
        self.held, self.near, self.along, self.last, self.send, self.recv, self.local = scratch
        self.rows = self.held.shape[1]
        self.half = self.rows // 2

    @staticmethod
    def scratch(rows, width):
        return [
            pltpu.VMEM((4, rows, width), jnp.bfloat16),
            pltpu.VMEM((4, rows, width), jnp.bfloat16),
            pltpu.VMEM((4, rows // 2, width), jnp.bfloat16),
            pltpu.VMEM((2, rows // 2, width), jnp.bfloat16),
            pltpu.SemaphoreType.DMA((10,)),
            pltpu.SemaphoreType.DMA((10,)),
            pltpu.SemaphoreType.DMA((4,)),
        ]

    def block(self, k, other):
        first = self.p.chip(*self.chips[k], other) * self.rows
        return self.terms.at[pl.ds(pl.multiple_of(first, 16), self.rows)]

    def half_of(self, k, part):
        return self.held.at[k, pl.ds(part * self.half, self.half)]

    def load(self, k):
        return pltpu.make_async_copy(self.block(k, 0), self.held.at[k], self.local.at[k])

    def copy(self, i):
        at = self.p.at
        if i < 4:
            src, dst, to = self.block(i, 1), self.near.at[i], at(0, 0, 1)
        elif i < 8:
            src, to = (
                (self.half_of(1, 0), at(1, 0)),
                (self.half_of(3, 0), at(1, 0)),
                (self.half_of(2, 1), at(0, 1)),
                (self.half_of(3, 1), at(0, 1)),
            )[i - 4]
            dst = self.along.at[i - 4]
        else:
            src, to = ((self.half_of(2, 0), at(0, 1)), (self.half_of(1, 1), at(1, 0)))[i - 8]
            dst = self.last.at[i - 8]
        return remote(src, dst, self.send.at[i], self.recv.at[i], to)

    def begin(self):
        for k in (3, 1, 2, 0):
            self.copy(k).start()
            self.load(k).start()

    def cores(self):
        for k in (3, 1, 2, 0):
            self.load(k).wait()
            self.copy(k).wait_recv()
            add_rows(self.held.at[k], self.near.at[k])
            if k == 3:
                self.copy(5).start()
                self.copy(7).start()
            elif k == 1:
                self.copy(4).start()
            elif k == 2:
                self.copy(6).start()

    def turn(self):
        self.copy(5).wait_recv()
        add_rows(self.half_of(2, 0), self.along.at[1])
        self.copy(8).start()
        self.copy(7).wait_recv()
        add_rows(self.half_of(1, 1), self.along.at[3])
        self.copy(9).start()
        self.copy(4).wait_recv()
        add_rows(self.half_of(0, 0), self.along.at[0])
        self.copy(6).wait_recv()
        add_rows(self.half_of(0, 1), self.along.at[2])

    def finish(self, result):
        for part in (0, 1):
            self.copy(8 + part).wait_recv()
            rows = pl.ds(part * self.half, self.half)
            add_rows(self.half_of(0, part), self.last.at[part], result.at[rows])
        for i in range(10):
            self.copy(i).wait_send()


def dma_sems(*dims):
    return pltpu.SemaphoreType.DMA(dims)


def in_vmem():
    return pl.BlockSpec(memory_space=pltpu.VMEM)


def in_any():
    return pl.BlockSpec(memory_space=pl.ANY)


def comm_params(number):
    return pltpu.CompilerParams(
        collective_id=number, has_side_effects=True, vmem_limit_bytes=VMEM_BYTES
    )


def shaped(dims, kind):
    return jax.ShapeDtypeStruct(dims, kind)


def first_gather(n_dp, n_line, mats, rows_in, order):
    count = len(mats)
    parts = 2

    def kernel(*refs):
        srcs, (c, e) = refs[:count], refs[count : count + 2]
        dsts, (c_out, e_out) = refs[count + 2 : 2 * count + 2], refs[2 * count + 2 : 2 * count + 4]
        ps, pr, pl_sem, ls, lr, ll = refs[2 * count + 4 : 2 * count + 10]
        held = refs[2 * count + 10 :]
        place = Place(n_dp, n_line)
        place.meet()
        planes = [
            GatherPlane(place, a, b, ps.at[i], pr.at[i], pl_sem.at[i], held[i])
            for i, (a, b) in enumerate(zip(srcs, dsts))
        ]
        rows = c.shape[0]
        span = rows // parts
        lines = [
            GatherLine(place, c_out, rows, i * span, span, ls.at[i], lr.at[i])
            for i in range(parts)
        ]
        lines.append(
            GatherLine(place, e_out, e.shape[0], 0, e.shape[0], ls.at[parts], lr.at[parts])
        )
        for i in range(parts):
            lines[i].step(0, c.at[pl.ds(i * span, span)])
        lines[parts].step(0, e)
        early, late = planes[: count // 2], planes[count // 2 :]
        for part in early:
            part.begin()
        copies = []
        for i, (src, dst) in enumerate(((c, c_out), (e, e_out))):
            own = dst.at[pl.ds(pl.multiple_of(place.t * src.shape[0], 8), src.shape[0])]
            copies.append(Kept(src, own, held[count + i], ll.at[i]))
            copies[i].begin()
        for line in lines:
            line.step(1)
        for part in late:
            part.begin()
        for part in early:
            part.forward()
        for copy in copies:
            copy.turn()
        for line in lines:
            line.step(2)
        for part in early:
            part.share()
        for part in late:
            part.forward()
        for part in late:
            part.share()
        for part in lines + planes:
            part.finish()
        for copy in copies:
            copy.finish()

    return pl.pallas_call(
        kernel,
        out_shape=tuple(shaped((n_dp * m.shape[0], m.shape[1]), m.dtype) for m in mats)
        + (
            shaped((n_line * rows_in.shape[0], rows_in.shape[1]), rows_in.dtype),
            shaped((n_line * order.shape[0], order.shape[1]), order.dtype),
        ),
        in_specs=[in_any()] * (count + 2),
        out_specs=[in_any()] * (count + 2),
        scratch_shapes=[
            dma_sems(count, 9),
            dma_sems(count, 9),
            dma_sems(count, 2),
            dma_sems(parts + 1, 2, n_line - 1),
            dma_sems(parts + 1, 2, n_line - 1),
            dma_sems(2, 2),
        ]
        + [vmem_like(m) for m in (*mats, rows_in, order)],
        compiler_params=comm_params(1),
        name="first_gather",
    )(*mats, rows_in, order)


CHUNKS = 8
LAST_CHUNKS = 4


def line_scratch(n_line, span, width, chunks):
    hops = n_line - 1
    return [
        pltpu.VMEM((chunks, 2, hops, span, width), jnp.bfloat16),
        dma_sems(chunks, 2, hops),
        dma_sems(chunks, 2, hops),
        dma_sems(chunks, 2, hops),
        dma_sems(chunks, 2, hops),
        pltpu.VMEM((span, width), jnp.float32),
    ]


def sum_rows_and_spread(place, terms, scratch, finish_rows, spread, between):
    inbox, rs, rr, gs, gr, total = scratch
    span = total.shape[0]
    count = inbox.shape[0]
    rows = span * count
    hops = place.n_line - 1
    sums = [
        ReduceLine(place, terms, rows, c * span, span, inbox.at[c], rs.at[c], rr.at[c])
        for c in range(count)
    ]
    gathers = []
    if spread is not None:
        gathers = [
            GatherLine(place, spread, rows, c * span, span, gs.at[c], gr.at[c])
            for c in range(count)
        ]
    sums[0].ends()

    def total_of(c):
        sums[c].total(total)
        finish_rows(c, pl.ds(c * span, span), total)
        if gathers:
            gathers[c].step(0)

    stages = [lambda c, k=k: sums[c].hop(k) for k in range(hops - 1)] + [total_of]
    lags = [LAGS[min(k, len(LAGS) - 1)] for k in range(hops)]
    if gathers:
        stages += [lambda c, k=k: gathers[c].step(k) for k in range(1, hops)]
        lags += [lags[-1] + LAG_STEP * k for k in range(1, hops)]
    for i in range(count + lags[-1]):
        if i < count:
            sums[i].sent()
        if i + 1 < count:
            sums[i + 1].ends()
        for work, lag in zip(stages, lags):
            if 0 <= i - lag < count:
                work(i - lag)
        if i in between:
            between[i]()
    for part in gathers + sums:
        part.finish()


LAGS = (0, 1, 1)
LAG_STEP = 1


def middle_gather(n_dp, n_line, terms, tokens, gain, mats):
    rows, width = tokens.shape
    count = len(mats)

    def kernel(*refs):
        s, tok, gain_ref = refs[:3]
        srcs = refs[3 : 3 + count]
        after, hidden = refs[3 + count : 5 + count]
        dsts = refs[5 + count : 5 + 2 * count]
        ps, pr, pl_sem = refs[5 + 2 * count : 8 + 2 * count]
        held = refs[8 + 2 * count : 8 + 3 * count]
        scratch = refs[8 + 3 * count :]
        place = Place(n_dp, n_line)
        place.meet()
        planes = [
            GatherPlane(place, a, b, ps.at[i], pr.at[i], pl_sem.at[i], held[i])
            for i, (a, b) in enumerate(zip(srcs, dsts))
        ]
        planes[0].begin()

        def norm(c, here, total):
            values = tok[here].astype(jnp.float32) + total[...]
            after[here] = values
            low = rms_scale(values, gain_ref[...]).astype(jnp.bfloat16)
            first = pl.multiple_of(place.t * rows, 16) + c * total.shape[0]
            hidden[pl.ds(pl.multiple_of(first, 16), total.shape[0])] = low

        between = {6: planes[0].forward, 9: planes[0].share}
        sum_rows_and_spread(place, s, scratch, norm, hidden, between)
        for part in planes:
            part.finish()

    return pl.pallas_call(
        kernel,
        out_shape=(
            shaped((rows, width), jnp.float32),
            shaped((n_line * rows, width), jnp.bfloat16),
        )
        + tuple(shaped((n_dp * m.shape[0], m.shape[1]), m.dtype) for m in mats),
        in_specs=[in_vmem()] * 3 + [in_any()] * count,
        out_specs=[in_vmem()] * 2 + [in_any()] * count,
        scratch_shapes=[dma_sems(count, 9), dma_sems(count, 9), dma_sems(count, 2)]
        + [vmem_like(m) for m in mats]
        + line_scratch(n_line, rows // CHUNKS, width, CHUNKS),
        compiler_params=comm_params(2),
        name="middle_gather",
    )(terms, tokens, gain, *mats)


def middle_sums(n_dp, n_line, terms, after, gain, grad_in, mat, hidden, grad_up, product, down):
    rows, width = after.shape
    block = mat.shape[0] // n_dp
    wide = grad_up.shape[1]
    spread_rows = n_line * rows

    def kernel(*refs):
        s, after_ref, gain_ref, g_ref, src = refs[:5]
        hid_far, gu_far, pr_far, dw_far = refs[5:9]
        grad_after, gain_sum, spread, result, up_far, feed_far = refs[9:15]
        hid, gu, pr, dw, up_out, feed, sems = refs[15:22]
        rest = refs[22:]
        fetch = Fetch(
            [
                (hid_far, hid),
                (gu_far, gu),
                (pr_far, pr),
                (dw_far, dw),
                (feed, feed_far),
                (up_out.at[0], up_far.at[pl.ds(0, width // 2)]),
                (up_out.at[1], up_far.at[pl.ds(width // 2, width // 2)]),
            ],
            sems,
        )
        fetch.start(0, 1, 2, 3)
        place = Place(n_dp, n_line)
        place.meet()
        plane = ReducePlane(place, src, rest[:7])
        scratch = rest[7:]
        plane.begin()
        gain_sum[...] = jnp.zeros_like(gain_sum)

        def norm(c, here, total):
            grad = total[...]
            grad_rows, normed = norm_back(after_ref[here], gain_ref[...], grad)
            gain_sum[...] += jnp.sum(grad * normed, axis=0, keepdims=True)
            both = g_ref[here].astype(jnp.float32) + grad_rows
            grad_after[here] = both
            first = pl.multiple_of(place.t * rows, 16) + c * total.shape[0]
            spread[pl.ds(pl.multiple_of(first, 16), total.shape[0])] = both.astype(jnp.bfloat16)

        def feed_part(i):
            cols = pl.ds(i * (width // 4), width // 4)
            feed[:, cols] = times_trans(pr[...], dw[cols]).astype(jnp.bfloat16)

        def up_part(i):
            cols = pl.ds(i * (width // 4), width // 4)
            here = pl.ds((i % 2) * (width // 4), width // 4)
            up_out[i // 2, here] = trans_times(hid[:, cols], gu[...]).astype(jnp.bfloat16)

        def early():
            plane.cores()
            fetch.wait(0, 1)

        def two():
            up_part(0)

        def three():
            up_part(1)
            fetch.start(5)

        def four():
            up_part(2)

        def five():
            up_part(3)
            fetch.start(6)
            fetch.wait(2, 3)

        def six():
            feed_part(0)

        def seven():
            plane.turn()
            feed_part(1)

        def eight():
            feed_part(2)

        def nine():
            feed_part(3)
            fetch.start(4)

        steps = {1: early, 2: two, 3: three, 4: four, 5: five, 6: six, 7: seven, 8: eight, 9: nine}
        sum_rows_and_spread(place, s, scratch, norm, spread, steps)
        plane.finish(result)
        fetch.wait(4, 5, 6)

    low, full = jnp.bfloat16, jnp.float32
    near, far = in_vmem(), in_any()
    return pl.pallas_call(
        kernel,
        out_shape=(
            shaped((rows, width), full),
            shaped((1, width), full),
            shaped((spread_rows, width), low),
            shaped((block, mat.shape[1]), low),
            shaped((width, wide), low),
            shaped((spread_rows, width), low),
        ),
        in_specs=[near] * 4 + [far] * 5,
        out_specs=[near] * 4 + [far] * 2,
        scratch_shapes=[vmem_like(m) for m in (hidden, grad_up, product, down)]
        + [
            pltpu.VMEM((2, width // 2, wide), low),
            pltpu.VMEM((spread_rows, width), low),
            dma_sems(7),
        ]
        + ReducePlane.scratch(block, mat.shape[1])
        + line_scratch(n_line, rows // CHUNKS, width, CHUNKS),
        compiler_params=comm_params(3),
        name="middle_sums",
    )(terms, after, gain, grad_in, mat, hidden, grad_up, product, down)


class Exchange:
    def __init__(self, place, axis, src, slots, send, recv, local):
        self.p, self.src, self.slots = place, src, slots
        self.over_dp = axis == "dp"
        self.size = place.n_dp if self.over_dp else place.n_line
        self.me = place.d if self.over_dp else place.t
        self.send, self.recv, self.local = send, recv, local

    def copy(self, i):
        to = lax.rem(self.me + i, self.size)
        device = (to, self.p.t) if self.over_dp else (self.p.d, to)
        return remote(
            self.src, self.slots.at[self.me], self.send.at[i - 1], self.recv.at[i - 1], device
        )

    def mine(self):
        return pltpu.make_async_copy(self.src, self.slots.at[self.me], self.local)

    def begin(self):
        for i in range(1, self.size):
            self.copy(i).start()
        self.mine().start()

    def wait(self):
        self.mine().wait()
        for i in range(1, self.size):
            self.copy(i).wait()

    def finish(self):
        self.wait()
        total = self.slots[0]
        for i in range(1, self.size):
            total = total + self.slots[i]
        return total


def last_sums(n_dp, n_line, terms, tokens, gain, grad_after, small, mats):
    rows, width = tokens.shape
    count = len(mats)
    per = len(ReducePlane.scratch(16, 128))

    def kernel(*refs):
        s, tok, gain_ref, g_ref, small_ref = refs[:5]
        srcs = refs[5 : 5 + count]
        grad_tok, small_out, first_out = refs[5 + count : 8 + count]
        results = refs[8 + count : 8 + 2 * count]
        rest = refs[8 + 2 * count :]
        own_first, row_sum = rest[count * per : count * per + 2]
        slots_a, slots_b, slots_c, slots_d = rest[count * per + 2 : count * per + 6]
        xs, xr, xl = rest[count * per + 6 : count * per + 9]
        scratch = rest[count * per + 9 :]
        place = Place(n_dp, n_line)
        place.meet(True)
        planes = [
            ReducePlane(place, srcs[i], rest[i * per : (i + 1) * per]) for i in range(count)
        ]
        for part in planes:
            part.begin()
        early = Exchange(place, "dp", small_ref, slots_a, xs.at[0], xr.at[0], xl.at[0])
        early.begin()
        own_first[...] = jnp.zeros_like(own_first)

        def norm(c, here, total):
            grad = total[...]
            grad_rows, normed = norm_back(tok[here].astype(jnp.float32), gain_ref[...], grad)
            own_first[...] += jnp.sum(grad * normed, axis=0, keepdims=True)
            grad_tok[here] = g_ref[here] + grad_rows

        def cores():
            for part in planes:
                part.cores()

        def turn():
            for part in planes:
                part.turn()

        sum_rows_and_spread(place, s, scratch, norm, None, {1: cores, 3: turn})
        first = Exchange(place, "dp", own_first, slots_b, xs.at[1], xr.at[1], xl.at[1])
        first.begin()
        small_out[...] = early.finish()
        row_sum[0:1] = small_out[0:1]
        row_sum[1:2] = first.finish()
        both = Exchange(place, "tensor", row_sum, slots_c, xs.at[2], xr.at[2], xl.at[2])
        both.begin()
        for part, result in zip(planes, results):
            part.finish(result)
        first_out[...] = both.finish()

    return pl.pallas_call(
        kernel,
        out_shape=(
            shaped((rows, width), jnp.float32),
            shaped(small.shape, jnp.float32),
            shaped((2, width), jnp.float32),
        )
        + tuple(shaped((m.shape[0] // n_dp, m.shape[1]), jnp.bfloat16) for m in mats),
        in_specs=[in_vmem()] * 5 + [in_any()] * count,
        out_specs=[in_vmem()] * (3 + count),
        scratch_shapes=sum([ReducePlane.scratch(m.shape[0] // n_dp, m.shape[1]) for m in mats], [])
        + [
            pltpu.VMEM((1, width), jnp.float32),
            pltpu.VMEM((2, width), jnp.float32),
            pltpu.VMEM((n_dp,) + small.shape, jnp.float32),
            pltpu.VMEM((n_dp, 1, width), jnp.float32),
            pltpu.VMEM((n_line, 2, width), jnp.float32),
            pltpu.VMEM((1, width), jnp.float32),
            dma_sems(3, n_dp),
            dma_sems(3, n_dp),
            dma_sems(3),
        ]
        + line_scratch(n_line, rows // LAST_CHUNKS, width, LAST_CHUNKS),
        compiler_params=comm_params(4),
        name="last_sums",
    )(terms, tokens, gain, grad_after, small, *mats)


def loop(count, body, unroll=1):
    def step(i, carry):
        body(i)
        return carry

    lax.fori_loop(0, count, step, None, unroll=unroll)


def tile_rows(i, size, ahead=0):
    return pl.ds(pl.multiple_of(i * size + ahead, 8), size)


def moved_up(values, distance, count):
    size = values.shape[0]
    return pltpu.roll(values, (size - distance) % size, 0)[:count]


def take_lanes(ref, here):
    return jnp.concatenate([ref[c, here] for c in range(ref.shape[0])], axis=1)


def put_lanes(ref, here, values):
    for c in range(ref.shape[0]):
        ref[c, here] = values[:, c * LANES : (c + 1) * LANES]


def gelu_parts(values):
    inner = GELU_C * (values + 0.044715 * (values * values * values))
    tanh = jnp.tanh(inner)
    half = 0.5 * (1.0 + tanh)
    slope = half + 0.5 * values * (1.0 - tanh * tanh) * GELU_C * (
        1.0 + 3.0 * 0.044715 * (values * values)
    )
    return values * half, slope


GELU_C = 0.7978845608028654
RIM = 128
LANES = 128
TILE = 16


def one_minus_exp(values, exponential):
    series = jnp.ones_like(values)
    for term in range(9, 1, -1):
        series = 1.0 + values * (1.0 / term) * series
    return jnp.where(values > -0.35, -values * series, 1.0 - exponential)


def rate_and_scale(pre_recur, soft, start):
    sr = jax.nn.sigmoid(pre_recur)
    log_rate = -rate_scale * sr * soft
    decay = jnp.exp(log_rate)
    rate = jnp.where(start, 0.0, decay)
    scale = jnp.where(start, 1.0, jnp.sqrt(one_minus_exp(2.0 * log_rate, decay * decay)))
    return sr, rate, scale


class RimSwap:
    def __init__(self, place, own):
        self.odd = lax.rem(place.t, 2)
        self.partner = (place.d, place.t + 1 - 2 * self.odd)
        self.first = pl.multiple_of(RIM - RIM * self.odd, RIM)
        self.edge = pl.ds(pl.multiple_of((1 - self.odd) * own + self.odd * RIM, RIM), RIM)
        self.over_there = pl.ds(pl.multiple_of(self.odd * (own + RIM), RIM), RIM)
        self.beyond = pl.ds(pl.multiple_of((1 - self.odd) * (own + RIM), RIM), RIM)

    def block(self, index, size):
        return pl.ds(pl.multiple_of(self.first + index * size, RIM), size)


def recur_forward(
    n_dp,
    n_line,
    tok_all,
    cot,
    to_place,
    to_stored,
    x_full,
    y_full,
    out_full,
    gain,
    gates,
    taps,
    soft,
    flags,
):
    rows, width = tok_all.shape
    count, own = taps.shape
    size = gates.shape[0]
    wide = own + 2 * RIM
    blocks = (wide - RIM) // size
    chunk = rows // 8
    cot_rows = cot.shape[0]
    parts = 1

    def kernel(*refs):
        (tok_far, cot_ref, plc, sto, wx_far, wy_far, wo_far, gain_ref, gw, cw, sp, fl) = refs[:12]
        far, cot_all = refs[12:23], refs[23]
        tok, wx, wy, wo = refs[24:28]
        results = refs[28:39]
        hp, xext, y, conv_low, conv, pre_r, pre_i, rate, state, merged_st, terms = results
        (h, xf, local, cum, merged, agg, slots, hs, hr, es, er, el, gs, gr, gl) = refs[39:54]
        in_sems, out_sems, cot_held = refs[54:]
        fetch = Fetch(((tok_far, tok), (wx_far, wx), (wy_far, wy), (wo_far, wo)), in_sems)
        store = Fetch(zip(results, far), out_sems)
        fetch.start(0, 1, 2, 3)
        place = Place(n_dp, n_line)
        place.meet(True)
        swap = RimSwap(place, own)
        own_cot = cot_all.at[pl.ds(pl.multiple_of(place.t * cot_rows, 16), cot_rows)]
        keep = Kept(cot_ref, own_cot, cot_held, gl)
        keep.begin()
        span = cot_rows // parts
        lines = [
            GatherLine(place, cot_all, cot_rows, c * span, span, gs.at[c], gr.at[c])
            for c in range(parts)
        ]
        for c, line in enumerate(lines):
            line.step(0, cot_ref.at[pl.ds(c * span, span)])

        def norm(i):
            here = tile_rows(i, TILE)
            h[here] = rms_scale(tok[here].astype(jnp.float32), gain_ref[...]).astype(jnp.bfloat16)

        fetch.wait(0)
        loop(rows // TILE, norm)
        fetch.wait(1)

        def project(i):
            here = tile_rows(i, 128)
            hp[here] = plain_dot(plc[here], h[...]).astype(jnp.bfloat16)
            xext[tile_rows(i, 128, 16)] = plain_dot(hp[here], wx[...]).astype(jnp.bfloat16)

        loop(rows // 128, project)
        store.start(0)
        edge = remote(
            xext.at[pl.ds(rows, 16)],
            xext.at[pl.ds(0, 16)],
            hs.at[0],
            hr.at[0],
            (lax.rem(place.d + 1, n_dp), place.t),
        )
        edge.start()
        keep.turn()
        for line in lines:
            line.step(1)

        def project_y(i):
            here = tile_rows(i, 128)
            y[here] = plain_dot(hp[here], wy[...])

        fetch.wait(2)
        loop(rows // 128, project_y)
        store.start(2)
        edge.wait()
        top = xext[pl.ds(0, 16)]
        xext[pl.ds(0, 16)] = jnp.where(place.d > 0, top, jnp.zeros_like(top))
        store.start(1)

        def widen(i):
            xf[tile_rows(i, TILE)] = xext[tile_rows(i, TILE)].astype(jnp.float32)

        loop(rows // TILE + 1, widen)

        def convolve(i):
            here = tile_rows(i, TILE)
            near = xf[pl.ds(pl.multiple_of(i * TILE + 8, 8), TILE + 8)]
            same = fl[tile_rows(i, TILE, 8)]
            total = cw[0:1] * near[8:]
            for k in range(1, count):
                total += cw[k : k + 1] * moved_up(near, 8 - k, TILE) * same[:, k : k + 1]
            conv[here] = total
            conv_low[here, RIM : RIM + own] = total.astype(jnp.bfloat16)

        loop(rows // TILE, convolve)
        store.start(4)
        rim = remote(
            conv_low.at[:, swap.edge],
            conv_low.at[:, swap.over_there],
            hs.at[1],
            hr.at[1],
            swap.partner,
        )
        rim.start()
        for i in range(blocks):
            index = lax.rem(i + swap.odd, blocks)
            cols = swap.block(index, size)
            other = pl.ds(pl.multiple_of(wide + swap.first + index * size, RIM), size)
            if i == blocks - 1:
                rim.wait()
            pre_r[:, cols] = plain_dot(conv_low[:, cols], gw[:, cols])
            pre_i[:, cols] = plain_dot(conv_low[:, cols], gw[:, other])

        store.start(3, 5, 6)

        def drive(i):
            here = tile_rows(i, TILE)
            start = fl[tile_rows(i, TILE, 8)][:, 0:1] > 0.0
            own_cols = pl.ds(RIM, own)
            _, decay, scale = rate_and_scale(pre_r[here, own_cols], sp[...], start)
            put_lanes(rate, here, decay)
            put_lanes(local, here, conv[here] * jax.nn.sigmoid(pre_i[here, own_cols]) * scale)

        loop(rows // TILE, drive)
        store.start(7)
        for line in lines:
            line.step(2)
        groups = own // LANES

        def scan(i, carry):
            here = pl.ds(i, 8, chunk)
            result = []
            for c in range(groups):
                product, total = carry[c]
                r = rate[c, here]
                product = product * r
                total = total * r + local[c, here]
                cum[c, here] = product
                local[c, here] = total
                result.append((product, total))
            return tuple(result)

        blank = (jnp.ones((8, LANES), jnp.float32), jnp.zeros((8, LANES), jnp.float32))
        lax.fori_loop(0, chunk, scan, (blank,) * groups)
        product, total = jnp.ones((1, own), jnp.float32), jnp.zeros((1, own), jnp.float32)
        for j in range(8):
            last = pl.ds(j * chunk + chunk - 1, 1)
            total = take_lanes(local, last) + take_lanes(cum, last) * total
            product = product * take_lanes(cum, last)
        agg[0:1] = product
        agg[1:2] = total
        swap_all = Exchange(place, "dp", agg, slots, es, er, el)
        swap_all.begin()
        swap_all.wait()
        entry = jnp.zeros((1, own), jnp.float32)
        for q in range(n_dp):
            longer = slots[q, 1:2] + slots[q, 0:1] * entry
            entry = jnp.where(q < place.d, longer, entry)
        state[pl.ds(0, 8)] = jnp.broadcast_to(entry, (8, own))
        for j in range(8):

            def settle(i, entry=entry):
                here = tile_rows(i, TILE, j * chunk)
                values = take_lanes(local, here) + take_lanes(cum, here) * entry
                state[tile_rows(i, TILE, j * chunk + 8)] = values
                merged[here] = (values * gelu_parts(y[here])[0]).astype(jnp.bfloat16)

            loop(chunk // TILE, settle)
            last = pl.ds(j * chunk + chunk - 1, 1)
            entry = take_lanes(local, last) + take_lanes(cum, last) * entry
        store.start(8)
        merged_st[...] = plain_dot(sto[...], merged[...]).astype(jnp.bfloat16)

        store.start(9)
        fetch.wait(3)

        def mix(i):
            some = tile_rows(i, 512)
            terms[:, pl.ds(pl.multiple_of(i * 512, 512), 512)] = times_trans(
                merged_st[...], wo[some, :]
            ).astype(jnp.bfloat16)

        loop(width // 512, mix)
        for line in lines:
            line.finish()
        keep.finish()
        store.start(10)
        store.wait(*range(11))

    low, full = jnp.bfloat16, jnp.float32
    results = (
        shaped((rows, width), low),
        shaped((rows + 16, own), low),
        shaped((rows, own), full),
        shaped((rows, wide), low),
        shaped((rows, own), full),
        shaped((rows, wide), full),
        shaped((rows, wide), full),
        shaped((own // LANES, rows, LANES), full),
        shaped((rows + 8, own), full),
        shaped((rows, own), low),
        shaped((rows, width), low),
    )
    near, far = in_vmem(), in_any()
    return pl.pallas_call(
        kernel,
        out_shape=results + (shaped((n_line * cot_rows, width), low),),
        in_specs=[far, far, near, near, far, far, far] + [near] * 5,
        out_specs=[far] * 12,
        scratch_shapes=[vmem_like(m) for m in (tok_all, x_full, y_full, out_full) + results]
        + [
            pltpu.VMEM((rows, width), low),
            pltpu.VMEM((rows + 16, own), full),
            pltpu.VMEM((own // LANES, rows, LANES), full),
            pltpu.VMEM((own // LANES, rows, LANES), full),
            pltpu.VMEM((rows, own), low),
            pltpu.VMEM((2, own), full),
            pltpu.VMEM((n_dp, 2, own), full),
            dma_sems(2),
            dma_sems(2),
            dma_sems(n_dp),
            dma_sems(n_dp),
            pltpu.SemaphoreType.DMA,
            dma_sems(parts, 2, n_line - 1),
            dma_sems(parts, 2, n_line - 1),
            dma_sems(2),
            dma_sems(4),
            dma_sems(11),
            vmem_like(cot),
        ],
        compiler_params=comm_params(5),
        name="recur_forward",
    )(
        tok_all,
        cot,
        to_place,
        to_stored,
        x_full,
        y_full,
        out_full,
        gain,
        gates,
        taps,
        soft,
        flags,
    )


def recur_backward(
    n_dp,
    n_line,
    mixer_in,
    to_place,
    to_stored,
    x_full,
    y_full,
    out_full,
    gates,
    taps,
    soft,
    slope,
    flags,
    kept,
    weight_terms,
    row_terms,
):
    rows, width = mixer_in.shape
    count, own = taps.shape
    size = gates.shape[0]
    wide = own + 2 * RIM
    blocks = (wide - RIM) // size
    chunk = rows // 8
    own_rows = rows // n_line
    parts = 4
    span = own_rows // parts

    def kernel(*refs):
        (mix_far, plc, sto, wx_far, wy_far, wo_far, gw, cw, sp, sg, fl) = refs[:11]
        kept_far, weights, feed_far = refs[11:19], refs[19], refs[20]
        (gxy_far, gate_grads, tap_grads, decay_grad, terms_far, weight_sum, row_sum) = refs[21:28]
        mix, wy, wo, feed = refs[28:32]
        (xext, y, conv_low, conv, pre_r, pre_i, rate, state) = refs[32:40]
        (gxy, mp, gm, lam, reach, gp_r, gp_i, grad, spread, rim_out, rim_in) = refs[40:51]
        (ret_out, ret_in, tap_sums, decay_sums, ends, agg, slots) = refs[51:58]
        (hs, hr, es, er, el, in_sems, out_sems, inbox, ls, lr, total) = refs[58:69]
        terms, wx = mix, wo
        fetch = Fetch(
            [
                (mix_far, mix),
                (wo_far, wo),
                (kept_far[1], y),
                (kept_far[7], state),
                (kept_far[6], rate),
                (kept_far[4], pre_r),
                (kept_far[5], pre_i),
                (kept_far[3], conv),
                (kept_far[2], conv_low),
                (kept_far[0], xext),
                (wx_far, wx),
                (wy_far, wy),
                (feed_far, feed),
            ],
            in_sems,
        )
        fetch.start(12, *range(10), 11)
        store = Fetch(((gxy, gxy_far), (terms, terms_far)), out_sems)
        place = Place(n_dp, n_line)
        place.meet(True)
        plane = ReducePlane(place, weights, refs[69:])
        plane.begin()
        lines = [
            ReduceLine(place, feed, own_rows, c * span, span, inbox.at[c], ls.at[c], lr.at[c])
            for c in range(parts)
        ]
        early, late = lines[: parts // 2], lines[parts // 2 :]

        def add_up(c):
            lines[c].total(total)
            row_sum[pl.ds(c * span, span)] = total[...].astype(jnp.bfloat16)

        fetch.wait(12)
        for line in early:
            line.ends()
        swap = RimSwap(place, own)
        own_cols = pl.ds(RIM, own)

        def project(i):
            here = tile_rows(i, 128)
            mp[here] = plain_dot(plc[here], mix[...]).astype(jnp.bfloat16)
            gm[here] = plain_dot(mp[here], wo[...])

        fetch.wait(0, 1)
        loop(rows // 128, project)
        fetch.start(10)

        def split(i):
            here = tile_rows(i, TILE)
            branch, slope_y = gelu_parts(y[here])
            grads = gm[here]
            put_lanes(lam, here, grads * branch)
            values = state[tile_rows(i, TILE, 8)]
            gxy[here, own:] = (grads * values * slope_y).astype(jnp.bfloat16)

        fetch.wait(2, 3)
        loop(rows // TILE, split)
        fetch.wait(4)
        groups = own // LANES

        def scan(i, carry):
            here = pl.ds(chunk - 1 - i, 8, chunk)
            result = []
            for c in range(groups):
                product, message = carry[c]
                r = rate[c, here]
                value = lam[c, here] + message
                lam[c, here] = value
                reach[c, here] = product
                result.append((product * r, value * r))
            return tuple(result)

        blank = (jnp.ones((8, LANES), jnp.float32), jnp.zeros((8, LANES), jnp.float32))
        done = lax.fori_loop(0, chunk, scan, (blank,) * groups)
        for c in range(groups):
            lanes = pl.ds(c * LANES, LANES)
            ends[0, :, lanes] = done[c][0]
            ends[1, :, lanes] = done[c][1]
        product, message = jnp.ones((1, own), jnp.float32), jnp.zeros((1, own), jnp.float32)
        for j in reversed(range(8)):
            message = ends[1, j : j + 1] + ends[0, j : j + 1] * message
            product = product * ends[0, j : j + 1]
        agg[0:1] = product
        agg[1:2] = message
        swap_all = Exchange(place, "dp", agg, slots, es, er, el)
        swap_all.begin()
        plane.cores()
        swap_all.wait()
        for line in early:
            line.sent()
        for line in late:
            line.ends()
        for line in early:
            line.hop(0)
        entry = jnp.zeros((1, own), jnp.float32)
        for q in reversed(range(n_dp)):
            longer = slots[q, 1:2] + slots[q, 0:1] * entry
            entry = jnp.where(q > place.d, longer, entry)
        fetch.wait(5, 6, 7)
        for ref in (tap_sums, decay_sums):
            ref[...] = jnp.zeros_like(ref)
        for ref in (gp_r, gp_i):
            ref[:, 0:RIM] = jnp.zeros((rows, RIM), jnp.bfloat16)
            ref[:, RIM + own :] = jnp.zeros((rows, RIM), jnp.bfloat16)
        grad[pl.ds(0, 8)] = jnp.zeros((8, own), jnp.float32)
        grad[pl.ds(rows + 8, 8)] = jnp.zeros((8, own), jnp.float32)
        for j in reversed(range(8)):

            def back(i, entry=entry):
                here = tile_rows(i, TILE, j * chunk)
                flag = fl[tile_rows(i, TILE, j * chunk + 8)]
                start = flag[:, 0:1] > 0.0
                values = take_lanes(lam, here) + take_lanes(reach, here) * entry
                before = moved_up(
                    state[pl.ds(pl.multiple_of(j * chunk + i * TILE, 8), TILE + 8)], 7, TILE
                )
                sr, decay, scale = rate_and_scale(pre_r[here, own_cols], sp[...], start)
                si = jax.nn.sigmoid(pre_i[here, own_cols])
                block = conv[here]
                driven = values * si
                log_grad = values * before * decay - block * driven * (decay * decay) / scale
                log_grad = jnp.where(start, 0.0, log_grad)
                inner = sr * log_grad
                gp_r[here, own_cols] = (
                    -rate_scale * sp[...] * inner * (1.0 - sr)
                ).astype(jnp.bfloat16)
                gp_i[here, own_cols] = (driven * block * (1.0 - si) * scale).astype(jnp.bfloat16)
                grad[tile_rows(i, TILE, j * chunk + 8)] = driven * scale
                decay_sums[...] += inner[:8] + inner[8:]

            loop(chunk // TILE, back)
            entry = ends[1, j : j + 1] + ends[0, j : j + 1] * entry
        for line in early:
            line.hop(1)
        decay_grad[...] = rate_scale * sg[...] * jnp.sum(decay_sums[...], axis=0, keepdims=True)

        for i in range(blocks):
            index = lax.rem(i + 2 - 2 * swap.odd, blocks)
            cols = swap.block(index, size)
            other = pl.ds(pl.multiple_of(wide + swap.first + index * size, RIM), size)
            spread[:, cols] = times_trans(gp_r[:, cols], gw[:, cols]) + times_trans(
                gp_i[:, cols], gw[:, other]
            )
            if i == 0:
                rim_out[...] = spread[:, swap.beyond].astype(jnp.bfloat16)
                rim = remote(rim_out, rim_in, hs.at[0], hr.at[0], swap.partner)
                rim.start()
        rim.wait()
        shared = pl.ds(pl.multiple_of((1 - swap.odd) * (own - RIM), RIM), RIM)

        def join(i):
            here = tile_rows(i, TILE)
            there = tile_rows(i, TILE, 8)
            grad[there] += spread[here, own_cols]
            grad[there, shared] += rim_in[here].astype(jnp.float32)

        loop(rows // TILE, join)

        near = grad[pl.ds(0, 16)]
        back_rows = jnp.zeros((8, own), jnp.float32)
        for k in range(1, count):
            masked = near * fl[pl.ds(0, 16)][:, k : k + 1]
            back_rows += cw[k : k + 1] * moved_up(masked, k, 8)
        ret_out[...] = back_rows
        ret = remote(
            ret_out,
            ret_in,
            hs.at[1],
            hr.at[1],
            (lax.rem(place.d + n_dp - 1, n_dp), place.t),
        )
        ret.start()
        fetch.wait(8)
        for i in range(blocks):
            cols = swap.block(i, size)
            spread[0:size, cols] = trans_times(conv_low[:, cols], gp_r[:, cols])
            spread[size : 2 * size, cols] = trans_times(conv_low[:, cols], gp_i[:, cols])
        gate_grads[:, 0:own] = spread[0:size, own_cols].astype(jnp.bfloat16)
        gate_grads[:, own:] = spread[size : 2 * size, own_cols].astype(jnp.bfloat16)

        def taps_back(i, added=None):
            here = tile_rows(i, TILE)
            start = pl.ds(pl.multiple_of(i * TILE + 8, 8), TILE + 8)
            after = grad[start]
            flag = fl[start]
            behind = xext[pl.ds(pl.multiple_of(i * TILE, 16), 2 * TILE)].astype(jnp.float32)
            total = cw[0:1] * after[:TILE]
            for k in range(count):
                if k > 0:
                    masked = after * flag[:, k : k + 1]
                    total += cw[k : k + 1] * moved_up(masked, k, TILE)
                    mine = masked[:TILE]
                else:
                    mine = after[:TILE]
                term = mine * moved_up(behind, 16 - k, TILE)
                tap_sums[k] += term[:8] + term[8:]
            if added is not None:
                total = total + jnp.concatenate([jnp.zeros((8, own), jnp.float32), added], axis=0)
            gxy[here, 0:own] = total.astype(jnp.bfloat16)

        fetch.wait(9)
        loop(rows // TILE - 1, taps_back)
        ret.wait()
        taps_back(rows // TILE - 1, jnp.where(place.d < n_dp - 1, ret_in[...], 0.0))
        tap_grads[...] = jnp.zeros_like(tap_grads)
        for k in range(count):
            tap_grads[k : k + 1] = jnp.sum(tap_sums[k], axis=0, keepdims=True)

        store.start(0)
        plane.turn()
        for c in range(parts // 2):
            add_up(c)
        for line in late:
            line.sent()
        for line in late:
            line.hop(0)

        def restore(i):
            here = tile_rows(i, 128)
            mp[here, 0 : 2 * own] = plain_dot(sto[here], gxy[...]).astype(jnp.bfloat16)

        loop(rows // 128, restore)

        def spread_back(i):
            some = tile_rows(i, 512)
            terms[:, pl.ds(pl.multiple_of(i * 512, 512), 512)] = (
                times_trans(mp[:, 0:own], wx[some]) + times_trans(mp[:, own : 2 * own], wy[some])
            ).astype(jnp.bfloat16)

        fetch.wait(10, 11)
        loop(width // 512, spread_back)
        store.start(1)
        for line in late:
            line.hop(1)
        plane.finish(weight_sum)
        for c in range(parts // 2, parts):
            add_up(c)
        for line in lines:
            line.finish()
        store.wait(0, 1)

    low, full = jnp.bfloat16, jnp.float32
    block = weight_terms.shape[0] // n_dp
    near, far = in_vmem(), in_any()
    return pl.pallas_call(
        kernel,
        out_shape=(
            shaped((rows, 2 * own), low),
            shaped((size, 2 * own), low),
            shaped((8, own), full),
            shaped((1, own), full),
            shaped((rows, width), low),
            shaped((block, weight_terms.shape[1]), low),
            shaped((own_rows, width), low),
        ),
        in_specs=[far, near, near, far, far, far] + [near] * 5 + [far] * 10,
        out_specs=[far, near, near, near, far, near, near],
        scratch_shapes=[vmem_like(m) for m in (mixer_in, y_full, out_full, row_terms, *kept)]
        + [
            pltpu.VMEM((rows, 2 * own), low),
            pltpu.VMEM((rows, width), low),
            pltpu.VMEM((rows, own), full),
            pltpu.VMEM((own // LANES, rows, LANES), full),
            pltpu.VMEM((own // LANES, rows, LANES), full),
            pltpu.VMEM((rows, wide), low),
            pltpu.VMEM((rows, wide), low),
            pltpu.VMEM((rows + 16, own), full),
            pltpu.VMEM((rows, wide), full),
            pltpu.VMEM((rows, RIM), low),
            pltpu.VMEM((rows, RIM), low),
            pltpu.VMEM((8, own), full),
            pltpu.VMEM((8, own), full),
            pltpu.VMEM((count, 8, own), full),
            pltpu.VMEM((8, own), full),
            pltpu.VMEM((2, 8, own), full),
            pltpu.VMEM((2, own), full),
            pltpu.VMEM((n_dp, 2, own), full),
            dma_sems(2),
            dma_sems(2),
            dma_sems(n_dp),
            dma_sems(n_dp),
            pltpu.SemaphoreType.DMA,
            dma_sems(13),
            dma_sems(2),
            pltpu.VMEM((parts, 2, n_line - 1, span, width), low),
            dma_sems(parts, 2, n_line - 1),
            dma_sems(parts, 2, n_line - 1),
            pltpu.VMEM((span, width), full),
        ]
        + ReducePlane.scratch(block, weight_terms.shape[1]),
        compiler_params=comm_params(6),
        name="recur_backward",
    )(
        mixer_in,
        to_place,
        to_stored,
        x_full,
        y_full,
        out_full,
        gates,
        taps,
        soft,
        slope,
        flags,
        *kept,
        weight_terms,
        row_terms,
    )


def matches(mesh):
    return mesh.shape["dp"] == 8 and mesh.shape["tensor"] == 4


def local_blocks(
    tokens,
    norm_gain,
    x_weight,
    y_weight,
    conv_weight,
    recur_gate_weight,
    input_gate_weight,
    decay_param,
    out_weight,
    mlp_gain,
    gate_weight,
    up_weight,
    down_weight,
    seq_lengths,
    token_order,
    cotangent,
):
    n_dp, n_tensor = lax.axis_size("dp"), lax.axis_size("tensor")
    tensor_index = lax.axis_index("tensor")
    dp_index = lax.axis_index("dp")
    tok_rows, width = tokens.shape
    row_count = tok_rows * n_tensor
    own_width = conv_weight.shape[1]
    kernel_taps = conv_weight.shape[0]
    edge_rows = kernel_taps - 1
    dp_width = norm_gain.shape[0]
    gate_rows = recur_gate_weight.shape[0]
    own_start = tensor_index * tok_rows

    gains = jnp.concatenate([norm_gain, mlp_gain])
    spare = gate_rows * 128 - gains.shape[0]
    gains = jnp.pad(gains, (0, spare)).reshape(gate_rows, 128)
    minor = jnp.concatenate([recur_gate_weight, input_gate_weight, gains], axis=1)
    own_order = (token_order - dp_index * row_count).astype(jnp.int32)
    order_rows = jnp.broadcast_to(own_order[None, :], (8, tok_rows))
    x_full, y_full, out_full, minor_full, tok_all, order_full = first_gather(
        n_dp, n_tensor, (x_weight, y_weight, out_weight.T, minor), tokens, order_rows
    )
    late_up, late_down, _ = lax.optimization_barrier((up_weight, down_weight.T, tok_all))
    up_full = lax.all_gather(late_up, "dp", axis=0, tiled=True)
    down_full = lax.all_gather(late_down, "dp", axis=0, tiled=True)
    order_all = order_full.reshape(n_tensor, 8, tok_rows)[:, 0].reshape(row_count)
    both_gates = minor_full[:, : 2 * own_width]
    gain_rows = minor_full[:, 2 * own_width :].reshape(n_dp, -1)
    first_gain = gain_rows[:, :dp_width].reshape(1, width).astype(jnp.float32)
    second_gain = gain_rows[:, dp_width : 2 * dp_width].reshape(1, width).astype(jnp.float32)
    block_size = both_gates.shape[0]
    row_index = jnp.arange(row_count, dtype=jnp.int32)
    hits = row_index[:, None] == order_all[None, :]
    to_place = hits.astype(jnp.bfloat16)
    to_stored = (order_all[:, None] == row_index[None, :]).astype(jnp.bfloat16)
    places = dp_index * row_count + jnp.arange(-8, row_count + 8, dtype=jnp.int32)
    inside = (jnp.arange(row_count + 16) >= 8) & (jnp.arange(row_count + 16) < row_count + 8)
    ends = jnp.cumsum(seq_lengths)
    segment = segment_of(places, ends)
    starts = (places == 0) | (segment != segment_of(places - 1, ends))
    columns = [starts] + [
        segment_of(places - shift, ends) == segment for shift in range(1, kernel_taps)
    ]
    columns += [jnp.zeros_like(starts)] * (8 - len(columns))
    flags = (jnp.stack(columns, axis=1) & inside[:, None]).astype(jnp.float32)
    live_own = (token_order < ends[-1]).astype(jnp.float32)
    grad_in_own = (cotangent.astype(jnp.float32) * live_own[:, None]).astype(jnp.bfloat16)
    soft = jax.nn.softplus(-decay_param).reshape(1, own_width)
    slope = jax.nn.sigmoid(-decay_param).reshape(1, own_width)
    zero_rim = jnp.zeros((block_size, RIM), jnp.bfloat16)
    gates_wide = jnp.concatenate(
        [
            zero_rim,
            both_gates[:, :own_width],
            zero_rim,
            zero_rim,
            both_gates[:, own_width:],
            zero_rim,
        ],
        axis=1,
    )
    def glu(gate_pre, up_pre):
        return gelu_tanh(gate_pre) * up_pre

    hidden_place, *kept, merged_stored, mixer_terms, down_in = recur_forward(
        n_dp,
        n_tensor,
        tok_all,
        grad_in_own,
        to_place,
        to_stored,
        x_full,
        y_full,
        out_full,
        first_gain,
        gates_wide,
        conv_weight,
        soft,
        flags,
    )
    after_own, hidden_two, gate_full = middle_gather(
        n_dp, n_tensor, mixer_terms, tokens, second_gain, (gate_weight,)
    )
    gate_pre = plain_dot(hidden_two, gate_full)
    up_pre = plain_dot(hidden_two, up_full)
    glu_out, glu_pull = jax.vjp(glu, gate_pre, up_pre)
    product = glu_out.astype(jnp.bfloat16)
    grad_down = trans_times(down_in, product).astype(jnp.bfloat16)
    down_sum = lax.psum_scatter(grad_down, "dp", scatter_dimension=0, tiled=True)
    down_in, _ = lax.optimization_barrier((down_in, grad_down))
    grad_product = plain_dot(down_in, down_full)
    grad_gate_pre, grad_up_pre = glu_pull(grad_product)
    grad_gate_pre = grad_gate_pre.astype(jnp.bfloat16)
    grad_up_pre = grad_up_pre.astype(jnp.bfloat16)
    grad_gate = trans_times(hidden_two, grad_gate_pre).astype(jnp.bfloat16)
    back_terms = (
        times_trans(grad_gate_pre, gate_full) + times_trans(grad_up_pre, up_full)
    ).astype(jnp.bfloat16)
    grad_after_own, second_part, mixer_in, gate_sum, grad_up, feed_terms = middle_sums(
        n_dp,
        n_tensor,
        back_terms,
        after_own,
        second_gain,
        grad_in_own,
        grad_gate,
        hidden_two,
        grad_up_pre,
        product,
        down_full,
    )
    grad_xy, gate_grads, tap_grads, decay_grad, one_terms, up_sum, feed_out = recur_backward(
        n_dp,
        n_tensor,
        mixer_in,
        to_place,
        to_stored,
        x_full,
        y_full,
        out_full,
        gates_wide,
        conv_weight,
        soft,
        slope,
        flags,
        kept,
        grad_up,
        feed_terms,
    )
    output = (after_own + feed_out.astype(jnp.float32)) * live_own[:, None]
    output = output.astype(jnp.bfloat16)
    grad_out_mat = trans_times(mixer_in, merged_stored).astype(jnp.bfloat16)
    grad_xy_mat = trans_times(hidden_place, grad_xy).astype(jnp.bfloat16)
    small = jnp.concatenate(
        [
            second_part,
            tap_grads[:kernel_taps].reshape(1, -1),
            jnp.pad(decay_grad, ((0, 0), (0, width - own_width))),
            jnp.zeros((1, width), jnp.float32),
        ],
        axis=0,
    )
    grad_tokens, small_sum, gain_sums, xy_sum, out_sum, gates_sum = last_sums(
        n_dp,
        n_tensor,
        one_terms,
        tokens,
        first_gain,
        grad_after_own,
        small,
        (grad_xy_mat, grad_out_mat, gate_grads),
    )
    xy_sum, gates_sum = xy_sum.astype(jnp.float32), gates_sum.astype(jnp.float32)
    own_gains = lax.dynamic_slice_in_dim(gain_sums, dp_index * dp_width, dp_width, 1)
    return (
        output,
        grad_tokens,
        own_gains[1],
        xy_sum[:, :own_width],
        xy_sum[:, own_width:],
        small_sum[1].reshape(kernel_taps, own_width),
        gates_sum[:, :own_width],
        gates_sum[:, own_width:],
        small_sum[2, :own_width],
        out_sum.astype(jnp.float32).T,
        own_gains[0],
        gate_sum.astype(jnp.float32),
        up_sum.astype(jnp.float32),
        down_sum.astype(jnp.float32).T,
    )


def solution(mesh):
    in_specs = (
        P(("dp", "tensor"), None),
        P("dp"),
        P("dp", "tensor"),
        P("dp", "tensor"),
        P(None, "tensor"),
        P("dp", "tensor"),
        P("dp", "tensor"),
        P("tensor"),
        P("tensor", "dp"),
        P("dp"),
        P("dp", "tensor"),
        P("dp", "tensor"),
        P("tensor", "dp"),
        P(),
        P(("dp", "tensor")),
        P(("dp", "tensor"), None),
    )
    out_specs = (
        P(("dp", "tensor"), None),
        P(("dp", "tensor"), None),
        P("dp"),
        P("dp", "tensor"),
        P("dp", "tensor"),
        P(None, "tensor"),
        P("dp", "tensor"),
        P("dp", "tensor"),
        P("tensor"),
        P("tensor", "dp"),
        P("dp"),
        P("dp", "tensor"),
        P("dp", "tensor"),
        P("tensor", "dp"),
    )
    fits = matches(mesh)
    local = local_blocks if fits else local_general
    return jax.shard_map(local, mesh=mesh, in_specs=in_specs, out_specs=out_specs, check_vma=False)
```

```python
import jax
import jax.numpy as jnp
from jax import lax
from jax.experimental import pallas as pl
from jax.experimental.pallas import tpu as pltpu
from jax.sharding import PartitionSpec as P

epsilon = 1e-06
rate_scale = 8.0


def from_behind(block, axis, distance):
    devices = range(lax.axis_size(axis))
    route = [(i - distance, i) for i in devices if i - distance in devices]
    return lax.ppermute(block, axis, route)


def extended_2(array, sides, width):
    for axis, dim in sides:
        size, length = (lax.axis_size(axis), array.shape[dim])
        up = [(i, (i + 1) % size) for i in range(size - 1)]
        down = [(j, i) for i, j in up]
        last = lax.slice_in_dim(array, length - width, length, axis=dim)
        leading = lax.slice_in_dim(array, 0, width, axis=dim)
        before = lax.ppermute(last, axis, up)
        after = lax.ppermute(leading, axis, down)
        array = jnp.concatenate([before, array, after], axis=dim)
    return array


def entering(value, axis, join, neutral, backward):
    count, mine = (lax.axis_size(axis), lax.axis_index(axis))
    pieces = jax.tree.map(lambda part: lax.all_gather(part, axis), value)
    if backward:
        pieces = jax.tree.map(lambda part: part[::-1], pieces)
        mine = count - 1 - mine
    total = jax.tree.map(
        lambda part, zero: jnp.full_like(part, 0) + jnp.asarray(zero, part.dtype), value, neutral
    )

    def lap(position, total):
        longer = join(total, jax.tree.map(lambda part: part[position], pieces))
        return jax.tree.map(lambda new, old: jnp.where(position < mine, new, old), longer, total)

    return lax.fori_loop(0, count - 1, lap, total)


def rms_scale(values, gain):
    return values * lax.rsqrt(jnp.mean(values * values, axis=-1, keepdims=True) + epsilon) * gain


def norm_back(values, gain, grad):
    inv_root = lax.rsqrt(jnp.mean(values * values, axis=-1, keepdims=True) + epsilon)
    normed = values * inv_root
    upstream = grad * gain
    grad_values = inv_root * (
        upstream - normed * jnp.mean(upstream * normed, axis=-1, keepdims=True)
    )
    return (grad_values, normed)


def segment_of(places, ends):
    return jnp.sum((ends[None, :] <= places[:, None]).astype(jnp.int32), axis=1)


def pair_step(early, later):
    return (early[0] * later[0], later[0] * early[1] + later[1])


def plain_dot(left, right):
    return jnp.dot(left, right, preferred_element_type=jnp.float32)


def times_trans(left, right):
    return lax.dot_general(
        left, right, (((1,), (1,)), ((), ())), preferred_element_type=jnp.float32
    )


def trans_times(left, right):
    return lax.dot_general(
        left, right, (((0,), (0,)), ((), ())), preferred_element_type=jnp.float32
    )


def gelu_tanh(values):
    return jax.nn.gelu(values, approximate=True)


def collect(
    norm_gain,
    mlp_gain,
    x_weight,
    y_weight,
    recur_gate_weight,
    input_gate_weight,
    gate_weight,
    up_weight,
    out_weight,
    down_weight,
):
    return (
        lax.all_gather(norm_gain, "dp", axis=0, tiled=True),
        lax.all_gather(mlp_gain, "dp", axis=0, tiled=True),
        lax.all_gather(x_weight, "dp", axis=0, tiled=True),
        lax.all_gather(y_weight, "dp", axis=0, tiled=True),
        lax.all_gather(recur_gate_weight, "dp", axis=0, tiled=True),
        lax.all_gather(input_gate_weight, "dp", axis=0, tiled=True),
        lax.all_gather(gate_weight, "dp", axis=0, tiled=True),
        lax.all_gather(up_weight, "dp", axis=0, tiled=True),
        lax.all_gather(out_weight, "dp", axis=1, tiled=True),
        lax.all_gather(down_weight, "dp", axis=1, tiled=True),
    )


def row_sums(term_rows, tok_rows):
    return lax.psum_scatter(
        term_rows(jnp.int32(0), lax.axis_size("tensor") * tok_rows).astype(jnp.bfloat16),
        "tensor",
        scatter_dimension=0,
        tiled=True,
    ).astype(jnp.float32)


def spread_rows(values):
    return lax.all_gather(values, "tensor", axis=0, tiled=True)


def local_general(
    tokens,
    norm_gain,
    x_weight,
    y_weight,
    conv_weight,
    recur_gate_weight,
    input_gate_weight,
    decay_param,
    out_weight,
    mlp_gain,
    gate_weight,
    up_weight,
    down_weight,
    seq_lengths,
    token_order,
    cotangent,
):
    n_tensor = lax.axis_size("tensor")
    tensor_index = lax.axis_index("tensor")
    dp_index = lax.axis_index("dp")
    tok_rows = tokens.shape[0]
    row_count = tok_rows * n_tensor
    own_width = conv_weight.shape[1]
    kernel_taps = conv_weight.shape[0]
    edge_rows = kernel_taps - 1
    dp_width = norm_gain.shape[0]
    own_start = tensor_index * tok_rows
    shards = (
        norm_gain,
        mlp_gain,
        x_weight,
        y_weight,
        recur_gate_weight,
        input_gate_weight,
        gate_weight,
        up_weight,
        out_weight,
        down_weight,
    )
    (
        gain_one,
        gain_two,
        x_full,
        y_full,
        recur_full,
        input_full,
        gate_full,
        up_full,
        out_full,
        down_full,
    ) = collect(*shards)
    block_size = recur_full.shape[0]
    first_gain = gain_one.astype(jnp.float32)
    second_gain = gain_two.astype(jnp.float32)
    both_gates = jnp.concatenate([recur_full, input_full], axis=1)
    tok_own = tokens.astype(jnp.float32)
    own_order = token_order - dp_index * row_count
    first_rows = rms_scale(tok_own, first_gain).astype(jnp.bfloat16)
    first_all, cot_all, order_all = (
        lax.all_gather(first_rows, "tensor", axis=0, tiled=True),
        lax.all_gather(cotangent, "tensor", axis=0, tiled=True),
        lax.all_gather(own_order, "tensor", axis=0, tiled=True),
    )
    row_index = jnp.arange(row_count, dtype=jnp.int32)
    inverse = jnp.zeros((row_count,), jnp.int32).at[order_all].set(row_index)
    hidden_place = jnp.take(first_all, inverse, axis=0)
    places = dp_index * row_count + row_index
    ends = jnp.cumsum(seq_lengths)
    segment = segment_of(places, ends)
    starts = (places == 0) | (segment != segment_of(places - 1, ends))
    live = (places < ends[-1]).astype(jnp.float32)
    live_stored = jnp.take(live, order_all, axis=0)
    same = [
        (segment_of(places - shift, ends) == segment).astype(jnp.float32)
        for shift in range(kernel_taps)
    ]
    low_edge = tensor_index * own_width
    own_blocks = (low_edge + jnp.arange(own_width, dtype=jnp.int32)) // block_size
    first_block = low_edge // block_size
    block_count = own_width // block_size + 2

    def block_start(index):
        return (first_block + index) * block_size - low_edge + block_size

    def block_mask(index):
        inside = own_blocks == first_block + index
        return jnp.concatenate([inside, inside])

    def convolve(extended, kernel):
        return sum(
            (
                kernel[shift][None, :]
                * extended[edge_rows - shift : edge_rows - shift + row_count]
                * same[shift][:, None]
                for shift in range(kernel_taps)
            )
        )

    def gates(conv_vals, pre_recur, pre_input, decay_vals):
        log_rate = -rate_scale * jax.nn.sigmoid(pre_recur) * jax.nn.softplus(-decay_vals)
        decay_rate = jnp.where(starts[:, None], 0.0, jnp.exp(log_rate))
        scale_in = jnp.where(starts[:, None], 1.0, jnp.sqrt(-jnp.expm1(2.0 * log_rate)))
        return (decay_rate, conv_vals * jax.nn.sigmoid(pre_input) * scale_in)

    def glu(gate_pre, up_pre):
        return gelu_tanh(gate_pre) * up_pre

    x_branch = plain_dot(hidden_place, x_full).astype(jnp.bfloat16)
    y_before = plain_dot(hidden_place, y_full)
    previous = from_behind(x_branch[row_count - edge_rows :], "dp", 1)
    extended = jnp.concatenate([previous, x_branch], axis=0).astype(jnp.float32)
    conv_out = convolve(extended, conv_weight)
    conv_wide = extended_2(conv_out.astype(jnp.bfloat16), (("tensor", 1),), block_size)
    pre_both = jnp.zeros((row_count, 2 * own_width), jnp.float32)
    for index in range(block_count):
        piece = lax.dynamic_slice_in_dim(conv_wide, block_start(index), block_size, 1)
        pre_both = pre_both + jnp.where(
            block_mask(index)[None, :], plain_dot(piece, both_gates), 0.0
        )
    (decay_rate, driven), gate_pull = jax.vjp(
        gates, conv_out, pre_both[:, :own_width], pre_both[:, own_width:], decay_param
    )
    cum_rate, local_state = lax.associative_scan(pair_step, (decay_rate, driven), axis=0)
    ident = (jnp.ones((own_width,), jnp.float32), jnp.zeros((own_width,), jnp.float32))
    rate_in, state_in = entering((cum_rate[-1], local_state[-1]), "dp", pair_step, ident, False)
    state = local_state + cum_rate * state_in[None, :]
    y_branch = gelu_tanh(y_before)
    merged = (state * y_branch).astype(jnp.bfloat16)
    merged_stored = jnp.take(merged, order_all, axis=0)

    def mixer_rows(begin, number):
        return plain_dot(merged_stored, out_full)

    after_own = tok_own + row_sums(mixer_rows, tok_rows)
    hidden_two = spread_rows(rms_scale(after_own, second_gain).astype(jnp.bfloat16))
    gate_pre = plain_dot(hidden_two, gate_full)
    up_pre = plain_dot(hidden_two, up_full)
    glu_out, glu_pull = jax.vjp(glu, gate_pre, up_pre)
    product = glu_out.astype(jnp.bfloat16)

    def down_rows(begin, number):
        return plain_dot(product, down_full)

    feed_out = row_sums(down_rows, tok_rows)
    live_own = lax.dynamic_slice_in_dim(live_stored, own_start, tok_rows, 0)
    output = ((after_own + feed_out) * live_own[:, None]).astype(jnp.bfloat16)
    grad_out = cot_all.astype(jnp.float32) * live_stored[:, None]
    fresh = lax.optimization_barrier((shards, grad_out))[0]
    (
        gain_one,
        gain_two,
        x_full,
        y_full,
        recur_full,
        input_full,
        gate_full,
        up_full,
        out_full,
        down_full,
    ) = collect(*fresh)
    first_gain = gain_one.astype(jnp.float32)
    second_gain = gain_two.astype(jnp.float32)
    both_gates = jnp.concatenate([recur_full, input_full], axis=1)
    down_in = grad_out.astype(jnp.bfloat16)
    grad_down = trans_times(product, down_in)
    grad_product = times_trans(down_in, down_full)
    grad_gate_pre, grad_up_pre = glu_pull(grad_product)
    grad_gate_pre = grad_gate_pre.astype(jnp.bfloat16)
    grad_up_pre = grad_up_pre.astype(jnp.bfloat16)
    grad_gate = trans_times(hidden_two, grad_gate_pre)
    grad_up = trans_times(hidden_two, grad_up_pre)

    def feed_rows(begin, number):
        return times_trans(grad_gate_pre, gate_full) + times_trans(grad_up_pre, up_full)

    grad_out_own = lax.dynamic_slice_in_dim(grad_out, own_start, tok_rows, 0)
    grad_two_own = row_sums(feed_rows, tok_rows)
    grad_norm_own, normed_two = norm_back(after_own, second_gain, grad_two_own)
    second_part = jnp.sum(grad_two_own * normed_two, axis=0)
    grad_after_own = grad_out_own + grad_norm_own
    mixer_in = spread_rows(grad_after_own.astype(jnp.bfloat16))
    grad_out_mat = trans_times(merged_stored, mixer_in)
    grad_merged = jnp.take(times_trans(mixer_in, out_full), inverse, axis=0)
    grad_state = grad_merged * y_branch
    gelu_pull = jax.vjp(gelu_tanh, y_before)[1]
    grad_y_before = gelu_pull(grad_merged * state)[0].astype(jnp.bfloat16)
    rate_next = jnp.concatenate([decay_rate[1:], jnp.ones((1, own_width), jnp.float32)], axis=0)
    rev_rate, local_lam = lax.associative_scan(
        pair_step, (rate_next, grad_state), reverse=True, axis=0
    )
    head_rate = decay_rate[0] * rev_rate[0]
    head_lam = decay_rate[0] * local_lam[0]
    factor_in, lam_in = entering((head_rate, head_lam), "dp", pair_step, ident, True)
    lam = local_lam + rev_rate * lam_in[None, :]
    state_prev = jnp.concatenate([state_in[None, :], state[:-1]], axis=0)
    grad_conv_local, grad_pre_recur, grad_pre_input, grad_decay_own = gate_pull(
        (lam * state_prev, lam)
    )
    grad_pre = jnp.concatenate([grad_pre_recur, grad_pre_input], axis=1).astype(jnp.bfloat16)
    grad_both = jnp.zeros((block_size, 2 * own_width), jnp.float32)
    grad_wide = jnp.zeros((row_count, own_width + 2 * block_size), jnp.float32)
    for index in range(block_count):
        begin = block_start(index)
        piece = lax.dynamic_slice_in_dim(conv_wide, begin, block_size, 1)
        masked = jnp.where(block_mask(index)[None, :], grad_pre, jnp.zeros((), jnp.bfloat16))
        grad_both = grad_both + trans_times(piece, masked)
        added = lax.dynamic_slice_in_dim(grad_wide, begin, block_size, 1) + times_trans(
            masked, both_gates
        )
        grad_wide = lax.dynamic_update_slice_in_dim(grad_wide, added, begin, 1)
    grad_recur = grad_both[:, :own_width]
    grad_input = grad_both[:, own_width:]
    rims = jnp.concatenate(
        [grad_wide[:, :block_size], grad_wide[:, own_width + block_size :]], axis=1
    )
    arrived = extended_2(rims.astype(jnp.bfloat16), (("tensor", 1),), block_size).astype(rims.dtype)
    from_lower = jnp.pad(arrived[:, :block_size], ((0, 0), (0, own_width - block_size)))
    from_upper = jnp.pad(arrived[:, 3 * block_size :], ((0, 0), (own_width - block_size, 0)))
    grad_conv = (
        grad_conv_local
        + grad_wide[:, block_size : block_size + own_width]
        + from_lower
        + from_upper
    )
    conv_pull = jax.vjp(convolve, extended, conv_weight)[1]
    grad_extended, grad_kernel = conv_pull(grad_conv)
    returned = from_behind(grad_extended[:edge_rows], "dp", -1)
    grad_x_branch = grad_extended[edge_rows:] + jnp.concatenate(
        [jnp.zeros((row_count - edge_rows, own_width), jnp.float32), returned], axis=0
    )
    grad_x_low = grad_x_branch.astype(jnp.bfloat16)
    grad_x_stored = jnp.take(grad_x_low, order_all, axis=0)
    grad_y_stored = jnp.take(grad_y_before, order_all, axis=0)
    grad_x_mat = trans_times(first_all, grad_x_stored)
    grad_y_mat = trans_times(first_all, grad_y_stored)

    def mixer_back_rows(begin, number):
        return times_trans(grad_x_stored, x_full) + times_trans(grad_y_stored, y_full)

    grad_one_own = row_sums(mixer_back_rows, tok_rows)
    grad_norm_one, normed_one = norm_back(tok_own, first_gain, grad_one_own)
    first_part = jnp.sum(grad_one_own * normed_one, axis=0)
    grad_tokens = grad_after_own + grad_norm_one
    chosen = jnp.arange(n_tensor, dtype=jnp.int32) == tensor_index
    kernel_tile = jnp.where(chosen[:, None, None], grad_kernel[None, :, :], 0.0)
    decay_tile = jnp.where(chosen[:, None], grad_decay_own[None, :], 0.0)
    small = lax.psum((first_part, second_part, kernel_tile, decay_tile), ("dp", "tensor"))
    grad_first_gain = lax.dynamic_slice_in_dim(small[0], dp_index * dp_width, dp_width, 0)
    grad_second_gain = lax.dynamic_slice_in_dim(small[1], dp_index * dp_width, dp_width, 0)
    grad_kernel_sum = lax.dynamic_index_in_dim(small[2], tensor_index, 0, keepdims=False)
    grad_decay = lax.dynamic_index_in_dim(small[3], tensor_index, 0, keepdims=False)
    sums = (
        lax.psum_scatter(
            grad_x_mat.astype(jnp.bfloat16), "dp", scatter_dimension=0, tiled=True
        ).astype(jnp.float32),
        lax.psum_scatter(
            grad_y_mat.astype(jnp.bfloat16), "dp", scatter_dimension=0, tiled=True
        ).astype(jnp.float32),
        lax.psum_scatter(
            grad_recur.astype(jnp.bfloat16), "dp", scatter_dimension=0, tiled=True
        ).astype(jnp.float32),
        lax.psum_scatter(
            grad_input.astype(jnp.bfloat16), "dp", scatter_dimension=0, tiled=True
        ).astype(jnp.float32),
        lax.psum_scatter(
            grad_gate.astype(jnp.bfloat16), "dp", scatter_dimension=0, tiled=True
        ).astype(jnp.float32),
        lax.psum_scatter(
            grad_up.astype(jnp.bfloat16), "dp", scatter_dimension=0, tiled=True
        ).astype(jnp.float32),
        lax.psum_scatter(
            grad_out_mat.astype(jnp.bfloat16), "dp", scatter_dimension=1, tiled=True
        ).astype(jnp.float32),
        lax.psum_scatter(
            grad_down.astype(jnp.bfloat16), "dp", scatter_dimension=1, tiled=True
        ).astype(jnp.float32),
    )
    return (
        output,
        grad_tokens,
        grad_first_gain,
        sums[0],
        sums[1],
        grad_kernel_sum,
        sums[2],
        sums[3],
        grad_decay,
        sums[6],
        grad_second_gain,
        sums[4],
        sums[5],
        sums[7],
    )


MESH = pl.DeviceIdType.MESH
VMEM_BYTES = 60 * 2**20


def remote(src, dst, send, recv, device):
    return pltpu.make_async_remote_copy(
        src_ref=src,
        dst_ref=dst,
        send_sem=send,
        recv_sem=recv,
        device_id=device,
        device_id_type=MESH,
    )


class Place:
    def __init__(self, n_dp, n_line):
        self.n_dp, self.n_line = n_dp, n_line
        self.d, self.t = lax.axis_index("dp"), lax.axis_index("tensor")
        self.core = lax.rem(self.d, 2)
        self.x = lax.rem(lax.div(self.d, 2), 2)
        self.y = lax.div(self.d, 4)

    def chip(self, flip_x, flip_y, flip_core=0):
        x = 1 - self.x if flip_x else self.x
        y = 1 - self.y if flip_y else self.y
        core = 1 - self.core if flip_core else self.core
        return y * 4 + x * 2 + core

    def at(self, flip_x=0, flip_y=0, flip_core=0):
        return (self.chip(flip_x, flip_y, flip_core), self.t)

    def up(self):
        return (self.d, lax.rem(self.t + 1, self.n_line))

    def down(self):
        return (self.d, lax.rem(self.t + self.n_line - 1, self.n_line))

    def meet(self, everyone=False):
        barrier = pltpu.get_barrier_semaphore()

        def greet(device):
            pl.semaphore_signal(barrier, inc=1, device_id=device, device_id_type=MESH)

        if everyone:
            for i in range(1, self.n_dp):
                greet((lax.rem(self.d + i, self.n_dp), self.t))
            for i in range(1, self.n_line):
                greet((self.d, lax.rem(self.t + i, self.n_line)))
            pl.semaphore_wait(barrier, self.n_dp + self.n_line - 2)
            return
        for flips in ((1, 0), (0, 1), (0, 0, 1)):
            greet(self.at(*flips))
        below, above = self.t > 0, self.t < self.n_line - 1

        @pl.when(below)
        def _():
            greet(self.down())

        @pl.when(above)
        def _():
            greet(self.up())

        pl.semaphore_wait(barrier, 3 + below.astype(jnp.int32) + above.astype(jnp.int32))


class Fetch:
    def __init__(self, pairs, sems):
        self.copies = [
            pltpu.make_async_copy(src, dst, sems.at[i]) for i, (src, dst) in enumerate(pairs)
        ]

    def start(self, *which):
        for i in which:
            self.copies[i].start()

    def wait(self, *which):
        for i in which:
            self.copies[i].wait()


def vmem_like(array):
    return pltpu.VMEM(array.shape, array.dtype)


class Kept:
    def __init__(self, src, dst, held, sems):
        self.there = pltpu.make_async_copy(src, held, sems.at[0])
        self.back = pltpu.make_async_copy(held, dst, sems.at[1])

    def begin(self):
        self.there.start()

    def turn(self):
        self.there.wait()
        self.back.start()

    def finish(self):
        self.back.wait()


class GatherPlane:
    def __init__(self, place, src, dst, send, recv, local, held):
        self.p, self.src, self.dst = place, src, dst
        self.rows = src.shape[0]
        self.send, self.recv = send, recv
        self.keep = Kept(src, self.block(0, 0), held, local)

    def block(self, fx, fy, fc=0, part=None):
        first = self.p.chip(fx, fy, fc) * self.rows
        size = self.rows
        if part is not None:
            size = self.rows // 2
            first = first + part * size
        return self.dst.at[pl.ds(pl.multiple_of(first, 16), size)]

    def copy(self, i, src, dst, device):
        return remote(src, dst, self.send.at[i], self.recv.at[i], device)

    def outgoing(self, i):
        at, block = self.p.at, self.block
        if i == 0:
            return self.copy(0, self.src, block(0, 0), at(1, 0))
        if i == 1:
            return self.copy(1, self.src, block(0, 0), at(0, 1))
        if i == 2:
            return self.copy(2, self.src, block(0, 0), at(0, 0, 1))
        if i == 3:
            return self.copy(3, block(1, 0, 0, 0), block(1, 0, 0, 0), at(0, 1))
        if i == 4:
            return self.copy(4, block(0, 1, 0, 1), block(0, 1, 0, 1), at(1, 0))
        spot = ((1, 0), (0, 1), (1, 1, 0, 0), (1, 1, 0, 1))[i - 5]
        return self.copy(i, block(*spot), block(*spot), at(0, 0, 1))

    def arrive(self, i):
        spot = (
            (1, 0),
            (0, 1),
            (0, 0, 1),
            (1, 1, 0, 0),
            (1, 1, 0, 1),
            (1, 0, 1),
            (0, 1, 1),
            (1, 1, 1, 0),
            (1, 1, 1, 1),
        )[i]
        here = self.block(*spot)
        self.copy(i, here, here, self.p.at(0, 0, 1)).wait_recv()

    def begin(self):
        for i in (0, 1, 2):
            self.outgoing(i).start()
        self.keep.begin()

    def forward(self):
        self.keep.turn()
        self.arrive(0)
        self.outgoing(3).start()
        self.arrive(1)
        self.outgoing(4).start()
        self.outgoing(5).start()
        self.outgoing(6).start()

    def share(self):
        self.arrive(3)
        self.outgoing(7).start()
        self.arrive(4)
        self.outgoing(8).start()

    def finish(self):
        for i in (2, 5, 6, 7, 8):
            self.arrive(i)
        for i in range(9):
            self.outgoing(i).wait_send()
        self.keep.finish()


class GatherLine:
    def __init__(self, place, dst, rows, begin, span, send, recv):
        self.p, self.dst, self.rows = place, dst, rows
        self.begin, self.span = begin, span
        self.send, self.recv = send, recv
        self.last = place.n_line - 1

    def block(self, owner):
        first = owner * self.rows + self.begin
        return self.dst.at[pl.ds(pl.multiple_of(first, 8), self.span)]

    def copy(self, way, k, owner, source=None):
        to = self.p.up() if way == 0 else self.p.down()
        block = self.block(owner)
        return remote(
            block if source is None else source,
            block,
            self.send.at[way, k],
            self.recv.at[way, k],
            to,
        )

    def step(self, k, source=None):
        t, last = self.p.t, self.last
        if k > 0:
            self.arrive(k - 1)

        @pl.when((t < last) & (t >= k))
        def _():
            self.copy(0, k, t - k, source).start()

        @pl.when((t > 0) & (t + k <= last))
        def _():
            self.copy(1, k, t + k, source).start()

    def arrive(self, k):
        t, last = self.p.t, self.last

        @pl.when(t >= k + 1)
        def _():
            self.copy(0, k, t - 1 - k).wait_recv()

        @pl.when(t + k + 1 <= last)
        def _():
            self.copy(1, k, t + 1 + k).wait_recv()

    def finish(self):
        t, last = self.p.t, self.last
        self.arrive(last - 1)
        for k in range(last):

            @pl.when((t < last) & (t >= k))
            def _():
                self.copy(0, k, t - k).wait_send()

            @pl.when((t > 0) & (t + k <= last))
            def _():
                self.copy(1, k, t + k).wait_send()


class ReduceLine:
    def __init__(self, place, terms, rows, begin, span, inbox, send, recv):
        self.p, self.terms, self.rows = place, terms, rows
        self.begin, self.span = begin, span
        self.inbox = inbox
        self.send, self.recv = send, recv
        self.last = place.n_line - 1

    def own(self, owner):
        first = owner * self.rows + self.begin
        return self.terms.at[pl.ds(pl.multiple_of(first, 16), self.span)]

    def copy(self, way, j, source):
        to = self.p.up() if way == 0 else self.p.down()
        return remote(
            source, self.inbox.at[way, j], self.send.at[way, j], self.recv.at[way, j], to
        )

    def ends(self):
        t, last = self.p.t, self.last

        @pl.when(t == 0)
        def _():
            for j in range(last):
                self.copy(0, j, self.own(last - j)).start()

        @pl.when(t == last)
        def _():
            for j in range(last):
                self.copy(1, j, self.own(j)).start()

    def sent(self):
        t, last = self.p.t, self.last

        @pl.when(t == 0)
        def _():
            for j in range(last):
                self.copy(0, j, self.own(last - j)).wait_send()

        @pl.when(t == last)
        def _():
            for j in range(last):
                self.copy(1, j, self.own(j)).wait_send()

    def hand_on(self, way, j):
        term = self.own(self.last - j if way == 0 else j)
        self.copy(way, j, term).wait_recv()
        self.inbox[way, j] = term[...] + self.inbox[way, j]
        self.copy(way, j, self.inbox.at[way, j]).start()

    def hop(self, k):
        t, last = self.p.t, self.last

        @pl.when(t == k + 1)
        def _():
            for j in range(last - 1 - k):
                self.hand_on(0, j)

        @pl.when(t == last - 1 - k)
        def _():
            for j in range(last - 1 - k):
                self.hand_on(1, j)

    def total(self, result):
        t, last = self.p.t, self.last
        result[...] = self.own(t)[...].astype(jnp.float32)

        @pl.when(t > 0)
        def _():
            j = last - t
            self.copy(0, j, self.inbox.at[0, 0]).wait_recv()
            result[...] += self.inbox[0, j].astype(jnp.float32)

        @pl.when(t < last)
        def _():
            self.copy(1, t, self.inbox.at[0, 0]).wait_recv()
            result[...] += self.inbox[1, t].astype(jnp.float32)

    def finish(self):
        t, last = self.p.t, self.last
        for j in range(last - 1):

            @pl.when((t > 0) & (t < last - j))
            def _():
                self.copy(0, j, self.inbox.at[0, j]).wait_send()

            @pl.when((t < last) & (t > j))
            def _():
                self.copy(1, j, self.inbox.at[1, j]).wait_send()


def add_rows(into, other, result=None):
    result = into if result is None else result

    def tile(i, carry):
        rows = pl.ds(pl.multiple_of(i * 16, 16), 16)
        result[rows] = into[rows] + other[rows]
        return carry

    lax.fori_loop(0, into.shape[0] // 16, tile, None)


class ReducePlane:
    chips = ((0, 0), (1, 0), (0, 1), (1, 1))

    def __init__(self, place, terms, scratch):
        self.p, self.terms = place, terms
        self.held, self.near, self.along, self.last, self.send, self.recv, self.local = scratch
        self.rows = self.held.shape[1]
        self.half = self.rows // 2

    @staticmethod
    def scratch(rows, width):
        return [
            pltpu.VMEM((4, rows, width), jnp.bfloat16),
            pltpu.VMEM((4, rows, width), jnp.bfloat16),
            pltpu.VMEM((4, rows // 2, width), jnp.bfloat16),
            pltpu.VMEM((2, rows // 2, width), jnp.bfloat16),
            pltpu.SemaphoreType.DMA((10,)),
            pltpu.SemaphoreType.DMA((10,)),
            pltpu.SemaphoreType.DMA((4,)),
        ]

    def block(self, k, other):
        first = self.p.chip(*self.chips[k], other) * self.rows
        return self.terms.at[pl.ds(pl.multiple_of(first, 16), self.rows)]

    def half_of(self, k, part):
        return self.held.at[k, pl.ds(part * self.half, self.half)]

    def load(self, k):
        return pltpu.make_async_copy(self.block(k, 0), self.held.at[k], self.local.at[k])

    def copy(self, i):
        at = self.p.at
        if i < 4:
            src, dst, to = self.block(i, 1), self.near.at[i], at(0, 0, 1)
        elif i < 8:
            src, to = (
                (self.half_of(1, 0), at(1, 0)),
                (self.half_of(3, 0), at(1, 0)),
                (self.half_of(2, 1), at(0, 1)),
                (self.half_of(3, 1), at(0, 1)),
            )[i - 4]
            dst = self.along.at[i - 4]
        else:
            src, to = ((self.half_of(2, 0), at(0, 1)), (self.half_of(1, 1), at(1, 0)))[i - 8]
            dst = self.last.at[i - 8]
        return remote(src, dst, self.send.at[i], self.recv.at[i], to)

    def begin(self):
        for k in (3, 1, 2, 0):
            self.copy(k).start()
            self.load(k).start()

    def cores(self):
        for k in (3, 1, 2, 0):
            self.load(k).wait()
            self.copy(k).wait_recv()
            add_rows(self.held.at[k], self.near.at[k])
            if k == 3:
                self.copy(5).start()
                self.copy(7).start()
            elif k == 1:
                self.copy(4).start()
            elif k == 2:
                self.copy(6).start()

    def turn(self):
        self.copy(5).wait_recv()
        add_rows(self.half_of(2, 0), self.along.at[1])
        self.copy(8).start()
        self.copy(7).wait_recv()
        add_rows(self.half_of(1, 1), self.along.at[3])
        self.copy(9).start()
        self.copy(4).wait_recv()
        add_rows(self.half_of(0, 0), self.along.at[0])
        self.copy(6).wait_recv()
        add_rows(self.half_of(0, 1), self.along.at[2])

    def finish(self, result):
        for part in (0, 1):
            self.copy(8 + part).wait_recv()
            rows = pl.ds(part * self.half, self.half)
            add_rows(self.half_of(0, part), self.last.at[part], result.at[rows])
        for i in range(10):
            self.copy(i).wait_send()


def dma_sems(*dims):
    return pltpu.SemaphoreType.DMA(dims)


def in_vmem():
    return pl.BlockSpec(memory_space=pltpu.VMEM)


def in_any():
    return pl.BlockSpec(memory_space=pl.ANY)


def comm_params(number):
    return pltpu.CompilerParams(
        collective_id=number, has_side_effects=True, vmem_limit_bytes=VMEM_BYTES
    )


def shaped(dims, kind):
    return jax.ShapeDtypeStruct(dims, kind)


def first_gather(n_dp, n_line, mats, rows_in, order):
    count = len(mats)
    parts = 2

    def kernel(*refs):
        srcs, (c, e) = refs[:count], refs[count : count + 2]
        dsts, (c_out, e_out) = refs[count + 2 : 2 * count + 2], refs[2 * count + 2 : 2 * count + 4]
        ps, pr, pl_sem, ls, lr, ll = refs[2 * count + 4 : 2 * count + 10]
        held = refs[2 * count + 10 :]
        place = Place(n_dp, n_line)
        place.meet()
        planes = [
            GatherPlane(place, a, b, ps.at[i], pr.at[i], pl_sem.at[i], held[i])
            for i, (a, b) in enumerate(zip(srcs, dsts))
        ]
        rows = c.shape[0]
        span = rows // parts
        lines = [
            GatherLine(place, c_out, rows, i * span, span, ls.at[i], lr.at[i])
            for i in range(parts)
        ]
        lines.append(
            GatherLine(place, e_out, e.shape[0], 0, e.shape[0], ls.at[parts], lr.at[parts])
        )
        for i in range(parts):
            lines[i].step(0, c.at[pl.ds(i * span, span)])
        lines[parts].step(0, e)
        early, late = planes[: count // 2], planes[count // 2 :]
        for part in early:
            part.begin()
        copies = []
        for i, (src, dst) in enumerate(((c, c_out), (e, e_out))):
            own = dst.at[pl.ds(pl.multiple_of(place.t * src.shape[0], 8), src.shape[0])]
            copies.append(Kept(src, own, held[count + i], ll.at[i]))
            copies[i].begin()
        for line in lines:
            line.step(1)
        for part in late:
            part.begin()
        for part in early:
            part.forward()
        for copy in copies:
            copy.turn()
        for line in lines:
            line.step(2)
        for part in early:
            part.share()
        for part in late:
            part.forward()
        for part in late:
            part.share()
        for part in lines + planes:
            part.finish()
        for copy in copies:
            copy.finish()

    return pl.pallas_call(
        kernel,
        out_shape=tuple(shaped((n_dp * m.shape[0], m.shape[1]), m.dtype) for m in mats)
        + (
            shaped((n_line * rows_in.shape[0], rows_in.shape[1]), rows_in.dtype),
            shaped((n_line * order.shape[0], order.shape[1]), order.dtype),
        ),
        in_specs=[in_any()] * (count + 2),
        out_specs=[in_any()] * (count + 2),
        scratch_shapes=[
            dma_sems(count, 9),
            dma_sems(count, 9),
            dma_sems(count, 2),
            dma_sems(parts + 1, 2, n_line - 1),
            dma_sems(parts + 1, 2, n_line - 1),
            dma_sems(2, 2),
        ]
        + [vmem_like(m) for m in (*mats, rows_in, order)],
        compiler_params=comm_params(1),
        name="first_gather",
    )(*mats, rows_in, order)


CHUNKS = 8
LAST_CHUNKS = 8


def line_scratch(n_line, span, width, chunks):
    hops = n_line - 1
    return [
        pltpu.VMEM((chunks, 2, hops, span, width), jnp.bfloat16),
        dma_sems(chunks, 2, hops),
        dma_sems(chunks, 2, hops),
        dma_sems(chunks, 2, hops),
        dma_sems(chunks, 2, hops),
        pltpu.VMEM((span, width), jnp.float32),
    ]


def sum_rows_and_spread(place, terms, scratch, finish_rows, spread, between):
    inbox, rs, rr, gs, gr, total = scratch
    span = total.shape[0]
    count = inbox.shape[0]
    rows = span * count
    hops = place.n_line - 1
    sums = [
        ReduceLine(place, terms, rows, c * span, span, inbox.at[c], rs.at[c], rr.at[c])
        for c in range(count)
    ]
    gathers = []
    if spread is not None:
        gathers = [
            GatherLine(place, spread, rows, c * span, span, gs.at[c], gr.at[c])
            for c in range(count)
        ]
    sums[0].ends()

    def total_of(c):
        sums[c].total(total)
        finish_rows(c, pl.ds(c * span, span), total)
        if gathers:
            gathers[c].step(0)

    stages = [lambda c, k=k: sums[c].hop(k) for k in range(hops - 1)] + [total_of]
    lags = [LAGS[min(k, len(LAGS) - 1)] for k in range(hops)]
    if gathers:
        stages += [lambda c, k=k: gathers[c].step(k) for k in range(1, hops)]
        lags += [lags[-1] + LAG_STEP * k for k in range(1, hops)]
    for i in range(count + lags[-1]):
        if i < count:
            sums[i].sent()
        if i + 1 < count:
            sums[i + 1].ends()
        for work, lag in zip(stages, lags):
            if 0 <= i - lag < count:
                work(i - lag)
        if i in between:
            between[i]()
    for part in gathers + sums:
        part.finish()


LAGS = (0, 1, 1)
LAG_STEP = 1


def middle_gather(n_dp, n_line, terms, tokens, gain, mats):
    rows, width = tokens.shape
    count = len(mats)

    def kernel(*refs):
        s, tok, gain_ref = refs[:3]
        srcs = refs[3 : 3 + count]
        after, hidden = refs[3 + count : 5 + count]
        dsts = refs[5 + count : 5 + 2 * count]
        ps, pr, pl_sem = refs[5 + 2 * count : 8 + 2 * count]
        held = refs[8 + 2 * count : 8 + 3 * count]
        scratch = refs[8 + 3 * count :]
        place = Place(n_dp, n_line)
        place.meet()
        planes = [
            GatherPlane(place, a, b, ps.at[i], pr.at[i], pl_sem.at[i], held[i])
            for i, (a, b) in enumerate(zip(srcs, dsts))
        ]
        planes[0].begin()

        def norm(c, here, total):
            values = tok[here].astype(jnp.float32) + total[...]
            after[here] = values
            low = rms_scale(values, gain_ref[...]).astype(jnp.bfloat16)
            first = pl.multiple_of(place.t * rows, 16) + c * total.shape[0]
            hidden[pl.ds(pl.multiple_of(first, 16), total.shape[0])] = low

        between = {6: planes[0].forward, 9: planes[0].share}
        sum_rows_and_spread(place, s, scratch, norm, hidden, between)
        for part in planes:
            part.finish()

    return pl.pallas_call(
        kernel,
        out_shape=(
            shaped((rows, width), jnp.float32),
            shaped((n_line * rows, width), jnp.bfloat16),
        )
        + tuple(shaped((n_dp * m.shape[0], m.shape[1]), m.dtype) for m in mats),
        in_specs=[in_vmem()] * 3 + [in_any()] * count,
        out_specs=[in_vmem()] * 2 + [in_any()] * count,
        scratch_shapes=[dma_sems(count, 9), dma_sems(count, 9), dma_sems(count, 2)]
        + [vmem_like(m) for m in mats]
        + line_scratch(n_line, rows // CHUNKS, width, CHUNKS),
        compiler_params=comm_params(2),
        name="middle_gather",
    )(terms, tokens, gain, *mats)


def middle_sums(n_dp, n_line, terms, after, gain, grad_in, mat, hidden, grad_up, product, down):
    rows, width = after.shape
    block = mat.shape[0] // n_dp
    wide = grad_up.shape[1]
    spread_rows = n_line * rows

    def kernel(*refs):
        s, after_ref, gain_ref, g_ref, src = refs[:5]
        hid_far, gu_far, pr_far, dw_far = refs[5:9]
        grad_after, gain_sum, spread, result, up_far, feed_far = refs[9:15]
        hid, gu, pr, dw, up_out, feed, sems = refs[15:22]
        rest = refs[22:]
        fetch = Fetch(
            [
                (hid_far, hid),
                (gu_far, gu),
                (pr_far, pr),
                (dw_far, dw),
                (feed, feed_far),
                (up_out.at[0], up_far.at[pl.ds(0, width // 2)]),
                (up_out.at[1], up_far.at[pl.ds(width // 2, width // 2)]),
            ],
            sems,
        )
        fetch.start(0, 1, 2, 3)
        place = Place(n_dp, n_line)
        place.meet()
        plane = ReducePlane(place, src, rest[:7])
        scratch = rest[7:]
        plane.begin()
        gain_sum[...] = jnp.zeros_like(gain_sum)

        def norm(c, here, total):
            grad = total[...]
            grad_rows, normed = norm_back(after_ref[here], gain_ref[...], grad)
            gain_sum[...] += jnp.sum(grad * normed, axis=0, keepdims=True)
            both = g_ref[here].astype(jnp.float32) + grad_rows
            grad_after[here] = both
            first = pl.multiple_of(place.t * rows, 16) + c * total.shape[0]
            spread[pl.ds(pl.multiple_of(first, 16), total.shape[0])] = both.astype(jnp.bfloat16)

        def feed_part(i):
            cols = pl.ds(i * (width // 4), width // 4)
            feed[:, cols] = times_trans(pr[...], dw[cols]).astype(jnp.bfloat16)

        def up_part(i):
            cols = pl.ds(i * (width // 4), width // 4)
            here = pl.ds((i % 2) * (width // 4), width // 4)
            up_out[i // 2, here] = trans_times(hid[:, cols], gu[...]).astype(jnp.bfloat16)

        def early():
            plane.cores()
            fetch.wait(0, 1)

        def two():
            up_part(0)

        def three():
            up_part(1)
            fetch.start(5)

        def four():
            up_part(2)

        def five():
            up_part(3)
            fetch.start(6)
            fetch.wait(2, 3)

        def six():
            feed_part(0)

        def seven():
            plane.turn()
            feed_part(1)

        def eight():
            feed_part(2)

        def nine():
            feed_part(3)
            fetch.start(4)

        steps = {1: early, 2: two, 3: three, 4: four, 5: five, 6: six, 7: seven, 8: eight, 9: nine}
        sum_rows_and_spread(place, s, scratch, norm, spread, steps)
        plane.finish(result)
        fetch.wait(4, 5, 6)

    low, full = jnp.bfloat16, jnp.float32
    near, far = in_vmem(), in_any()
    return pl.pallas_call(
        kernel,
        out_shape=(
            shaped((rows, width), full),
            shaped((1, width), full),
            shaped((spread_rows, width), low),
            shaped((block, mat.shape[1]), low),
            shaped((width, wide), low),
            shaped((spread_rows, width), low),
        ),
        in_specs=[near] * 4 + [far] * 5,
        out_specs=[near] * 4 + [far] * 2,
        scratch_shapes=[vmem_like(m) for m in (hidden, grad_up, product, down)]
        + [
            pltpu.VMEM((2, width // 2, wide), low),
            pltpu.VMEM((spread_rows, width), low),
            dma_sems(7),
        ]
        + ReducePlane.scratch(block, mat.shape[1])
        + line_scratch(n_line, rows // CHUNKS, width, CHUNKS),
        compiler_params=comm_params(3),
        name="middle_sums",
    )(terms, after, gain, grad_in, mat, hidden, grad_up, product, down)


class Exchange:
    def __init__(self, place, axis, src, slots, send, recv, local):
        self.p, self.src, self.slots = place, src, slots
        self.over_dp = axis == "dp"
        self.size = place.n_dp if self.over_dp else place.n_line
        self.me = place.d if self.over_dp else place.t
        self.send, self.recv, self.local = send, recv, local

    def copy(self, i):
        to = lax.rem(self.me + i, self.size)
        device = (to, self.p.t) if self.over_dp else (self.p.d, to)
        return remote(
            self.src, self.slots.at[self.me], self.send.at[i - 1], self.recv.at[i - 1], device
        )

    def mine(self):
        return pltpu.make_async_copy(self.src, self.slots.at[self.me], self.local)

    def begin(self):
        for i in range(1, self.size):
            self.copy(i).start()
        self.mine().start()

    def wait(self):
        self.mine().wait()
        for i in range(1, self.size):
            self.copy(i).wait()

    def finish(self):
        self.wait()
        total = self.slots[0]
        for i in range(1, self.size):
            total = total + self.slots[i]
        return total


def last_sums(n_dp, n_line, terms, tokens, gain, grad_after, small, mats):
    rows, width = tokens.shape
    count = len(mats)
    per = len(ReducePlane.scratch(16, 128))

    def kernel(*refs):
        s, tok, gain_ref, g_ref, small_ref = refs[:5]
        srcs = refs[5 : 5 + count]
        grad_tok, small_out, first_out = refs[5 + count : 8 + count]
        results = refs[8 + count : 8 + 2 * count]
        rest = refs[8 + 2 * count :]
        own_first, row_sum = rest[count * per : count * per + 2]
        slots_a, slots_b, slots_c, slots_d = rest[count * per + 2 : count * per + 6]
        xs, xr, xl = rest[count * per + 6 : count * per + 9]
        scratch = rest[count * per + 9 :]
        place = Place(n_dp, n_line)
        place.meet(True)
        planes = [
            ReducePlane(place, srcs[i], rest[i * per : (i + 1) * per]) for i in range(count)
        ]
        for part in planes:
            part.begin()
        early = Exchange(place, "dp", small_ref, slots_a, xs.at[0], xr.at[0], xl.at[0])
        early.begin()
        own_first[...] = jnp.zeros_like(own_first)

        def norm(c, here, total):
            grad = total[...]
            grad_rows, normed = norm_back(tok[here].astype(jnp.float32), gain_ref[...], grad)
            own_first[...] += jnp.sum(grad * normed, axis=0, keepdims=True)
            grad_tok[here] = g_ref[here] + grad_rows

        def cores():
            for part in planes:
                part.cores()

        def turn():
            for part in planes:
                part.turn()

        sum_rows_and_spread(place, s, scratch, norm, None, {0: cores, 5: turn})
        first = Exchange(place, "dp", own_first, slots_b, xs.at[1], xr.at[1], xl.at[1])
        first.begin()
        small_out[...] = early.finish()
        row_sum[0:1] = small_out[0:1]
        row_sum[1:2] = first.finish()
        both = Exchange(place, "tensor", row_sum, slots_c, xs.at[2], xr.at[2], xl.at[2])
        both.begin()
        for part, result in zip(planes, results):
            part.finish(result)
        first_out[...] = both.finish()

    return pl.pallas_call(
        kernel,
        out_shape=(
            shaped((rows, width), jnp.float32),
            shaped(small.shape, jnp.float32),
            shaped((2, width), jnp.float32),
        )
        + tuple(shaped((m.shape[0] // n_dp, m.shape[1]), jnp.bfloat16) for m in mats),
        in_specs=[in_vmem()] * 5 + [in_any()] * count,
        out_specs=[in_vmem()] * (3 + count),
        scratch_shapes=sum([ReducePlane.scratch(m.shape[0] // n_dp, m.shape[1]) for m in mats], [])
        + [
            pltpu.VMEM((1, width), jnp.float32),
            pltpu.VMEM((2, width), jnp.float32),
            pltpu.VMEM((n_dp,) + small.shape, jnp.float32),
            pltpu.VMEM((n_dp, 1, width), jnp.float32),
            pltpu.VMEM((n_line, 2, width), jnp.float32),
            pltpu.VMEM((1, width), jnp.float32),
            dma_sems(3, n_dp),
            dma_sems(3, n_dp),
            dma_sems(3),
        ]
        + line_scratch(n_line, rows // LAST_CHUNKS, width, LAST_CHUNKS),
        compiler_params=comm_params(4),
        name="last_sums",
    )(terms, tokens, gain, grad_after, small, *mats)


def loop(count, body, unroll=1):
    def step(i, carry):
        body(i)
        return carry

    lax.fori_loop(0, count, step, None, unroll=unroll)


def tile_rows(i, size, ahead=0):
    return pl.ds(pl.multiple_of(i * size + ahead, 8), size)


def moved_up(values, distance, count):
    size = values.shape[0]
    return pltpu.roll(values, (size - distance) % size, 0)[:count]


def take_lanes(ref, here):
    return jnp.concatenate([ref[c, here] for c in range(ref.shape[0])], axis=1)


def put_lanes(ref, here, values):
    for c in range(ref.shape[0]):
        ref[c, here] = values[:, c * LANES : (c + 1) * LANES]


def gelu_parts(values):
    inner = GELU_C * (values + 0.044715 * (values * values * values))
    tanh = jnp.tanh(inner)
    half = 0.5 * (1.0 + tanh)
    slope = half + 0.5 * values * (1.0 - tanh * tanh) * GELU_C * (
        1.0 + 3.0 * 0.044715 * (values * values)
    )
    return values * half, slope


GELU_C = 0.7978845608028654
RIM = 128
LANES = 128
TILE = 16


def one_minus_exp(values, exponential):
    series = jnp.ones_like(values)
    for term in range(9, 1, -1):
        series = 1.0 + values * (1.0 / term) * series
    return jnp.where(values > -0.35, -values * series, 1.0 - exponential)


def rate_and_scale(pre_recur, soft, start):
    sr = jax.nn.sigmoid(pre_recur)
    log_rate = -rate_scale * sr * soft
    decay = jnp.exp(log_rate)
    rate = jnp.where(start, 0.0, decay)
    scale = jnp.where(start, 1.0, jnp.sqrt(one_minus_exp(2.0 * log_rate, decay * decay)))
    return sr, rate, scale


class RimSwap:
    def __init__(self, place, own):
        self.odd = lax.rem(place.t, 2)
        self.partner = (place.d, place.t + 1 - 2 * self.odd)
        self.first = pl.multiple_of(RIM - RIM * self.odd, RIM)
        self.edge = pl.ds(pl.multiple_of((1 - self.odd) * own + self.odd * RIM, RIM), RIM)
        self.over_there = pl.ds(pl.multiple_of(self.odd * (own + RIM), RIM), RIM)
        self.beyond = pl.ds(pl.multiple_of((1 - self.odd) * (own + RIM), RIM), RIM)

    def block(self, index, size):
        return pl.ds(pl.multiple_of(self.first + index * size, RIM), size)


LATE_SHARE = 4


def recur_forward(
    n_dp,
    n_line,
    tok_all,
    cot,
    to_place,
    to_stored,
    x_full,
    y_full,
    out_full,
    gain,
    gates,
    taps,
    soft,
    flags,
):
    rows, width = tok_all.shape
    count, own = taps.shape
    size = gates.shape[0]
    wide = own + 2 * RIM
    blocks = (wide - RIM) // size
    chunk = rows // 8
    cot_rows = cot.shape[0] - cot.shape[0] // LATE_SHARE
    parts = 1

    def kernel(*refs):
        (tok_far, cot_ref, plc, sto, wx_far, wy_far, wo_far, gain_ref, gw, cw, sp, fl) = refs[:12]
        far, cot_all = refs[12:23], refs[23]
        tok, wx, wy, wo = refs[24:28]
        results = refs[28:39]
        hp, xext, y, conv_low, conv, pre_r, pre_i, rate, state, merged_st, terms = results
        (h, xf, local, cum, merged, agg, slots, hs, hr, es, er, el, gs, gr, gl) = refs[39:54]
        in_sems, out_sems, cot_held = refs[54:]
        fetch = Fetch(((tok_far, tok), (wx_far, wx), (wy_far, wy), (wo_far, wo)), in_sems)
        store = Fetch(zip(results, far), out_sems)
        fetch.start(0, 1, 2, 3)
        place = Place(n_dp, n_line)
        place.meet(True)
        swap = RimSwap(place, own)
        own_cot = cot_all.at[pl.ds(pl.multiple_of(place.t * cot_rows, 16), cot_rows)]
        cot_ref = cot_ref.at[pl.ds(0, cot_rows)]
        keep = Kept(cot_ref, own_cot, cot_held, gl)
        keep.begin()
        span = cot_rows // parts
        lines = [
            GatherLine(place, cot_all, cot_rows, c * span, span, gs.at[c], gr.at[c])
            for c in range(parts)
        ]
        for c, line in enumerate(lines):
            line.step(0, cot_ref.at[pl.ds(c * span, span)])

        def norm(i):
            here = tile_rows(i, TILE)
            h[here] = rms_scale(tok[here].astype(jnp.float32), gain_ref[...]).astype(jnp.bfloat16)

        fetch.wait(0)
        loop(rows // TILE, norm)
        fetch.wait(1)

        def project(i):
            here = tile_rows(i, 128)
            hp[here] = plain_dot(plc[here], h[...]).astype(jnp.bfloat16)
            xext[tile_rows(i, 128, 16)] = plain_dot(hp[here], wx[...]).astype(jnp.bfloat16)

        loop(rows // 128, project)
        store.start(0)
        edge = remote(
            xext.at[pl.ds(rows, 16)],
            xext.at[pl.ds(0, 16)],
            hs.at[0],
            hr.at[0],
            (lax.rem(place.d + 1, n_dp), place.t),
        )
        edge.start()
        keep.turn()
        for line in lines:
            line.step(1)

        def project_y(i):
            here = tile_rows(i, 128)
            y[here] = plain_dot(hp[here], wy[...])

        fetch.wait(2)
        loop(rows // 128, project_y)
        store.start(2)
        edge.wait()
        top = xext[pl.ds(0, 16)]
        xext[pl.ds(0, 16)] = jnp.where(place.d > 0, top, jnp.zeros_like(top))
        store.start(1)

        def widen(i):
            xf[tile_rows(i, TILE)] = xext[tile_rows(i, TILE)].astype(jnp.float32)

        loop(rows // TILE + 1, widen)

        def convolve(i):
            here = tile_rows(i, TILE)
            near = xf[pl.ds(pl.multiple_of(i * TILE + 8, 8), TILE + 8)]
            same = fl[tile_rows(i, TILE, 8)]
            total = cw[0:1] * near[8:]
            for k in range(1, count):
                total += cw[k : k + 1] * moved_up(near, 8 - k, TILE) * same[:, k : k + 1]
            conv[here] = total
            conv_low[here, RIM : RIM + own] = total.astype(jnp.bfloat16)

        loop(rows // TILE, convolve)
        store.start(4)
        rim = remote(
            conv_low.at[:, swap.edge],
            conv_low.at[:, swap.over_there],
            hs.at[1],
            hr.at[1],
            swap.partner,
        )
        rim.start()
        for i in range(blocks):
            index = lax.rem(i + swap.odd, blocks)
            cols = swap.block(index, size)
            other = pl.ds(pl.multiple_of(wide + swap.first + index * size, RIM), size)
            if i == blocks - 1:
                rim.wait()
            pre_r[:, cols] = plain_dot(conv_low[:, cols], gw[:, cols])
            pre_i[:, cols] = plain_dot(conv_low[:, cols], gw[:, other])

        store.start(3, 5, 6)

        def drive(i):
            here = tile_rows(i, TILE)
            start = fl[tile_rows(i, TILE, 8)][:, 0:1] > 0.0
            own_cols = pl.ds(RIM, own)
            _, decay, scale = rate_and_scale(pre_r[here, own_cols], sp[...], start)
            put_lanes(rate, here, decay)
            put_lanes(local, here, conv[here] * jax.nn.sigmoid(pre_i[here, own_cols]) * scale)

        loop(rows // TILE, drive)
        store.start(7)
        for line in lines:
            line.step(2)
        groups = own // LANES

        def scan(i, carry):
            here = pl.ds(i, 8, chunk)
            result = []
            for c in range(groups):
                product, total = carry[c]
                r = rate[c, here]
                product = product * r
                total = total * r + local[c, here]
                cum[c, here] = product
                local[c, here] = total
                result.append((product, total))
            return tuple(result)

        blank = (jnp.ones((8, LANES), jnp.float32), jnp.zeros((8, LANES), jnp.float32))
        lax.fori_loop(0, chunk, scan, (blank,) * groups)
        product, total = jnp.ones((1, own), jnp.float32), jnp.zeros((1, own), jnp.float32)
        for j in range(8):
            last = pl.ds(j * chunk + chunk - 1, 1)
            total = take_lanes(local, last) + take_lanes(cum, last) * total
            product = product * take_lanes(cum, last)
        agg[0:1] = product
        agg[1:2] = total
        swap_all = Exchange(place, "dp", agg, slots, es, er, el)
        swap_all.begin()
        swap_all.wait()
        entry = jnp.zeros((1, own), jnp.float32)
        for q in range(n_dp):
            longer = slots[q, 1:2] + slots[q, 0:1] * entry
            entry = jnp.where(q < place.d, longer, entry)
        state[pl.ds(0, 8)] = jnp.broadcast_to(entry, (8, own))
        for j in range(8):

            def settle(i, entry=entry):
                here = tile_rows(i, TILE, j * chunk)
                values = take_lanes(local, here) + take_lanes(cum, here) * entry
                state[tile_rows(i, TILE, j * chunk + 8)] = values
                merged[here] = (values * gelu_parts(y[here])[0]).astype(jnp.bfloat16)

            loop(chunk // TILE, settle)
            last = pl.ds(j * chunk + chunk - 1, 1)
            entry = take_lanes(local, last) + take_lanes(cum, last) * entry
        store.start(8)
        merged_st[...] = plain_dot(sto[...], merged[...]).astype(jnp.bfloat16)

        store.start(9)
        fetch.wait(3)

        def mix(i):
            some = tile_rows(i, 512)
            terms[:, pl.ds(pl.multiple_of(i * 512, 512), 512)] = times_trans(
                merged_st[...], wo[some, :]
            ).astype(jnp.bfloat16)

        loop(width // 512, mix)
        for line in lines:
            line.finish()
        keep.finish()
        store.start(10)
        store.wait(*range(11))

    low, full = jnp.bfloat16, jnp.float32
    results = (
        shaped((rows, width), low),
        shaped((rows + 16, own), low),
        shaped((rows, own), full),
        shaped((rows, wide), low),
        shaped((rows, own), full),
        shaped((rows, wide), full),
        shaped((rows, wide), full),
        shaped((own // LANES, rows, LANES), full),
        shaped((rows + 8, own), full),
        shaped((rows, own), low),
        shaped((rows, width), low),
    )
    near, far = in_vmem(), in_any()
    return pl.pallas_call(
        kernel,
        out_shape=results + (shaped((n_line * cot_rows, width), low),),
        in_specs=[far, far, near, near, far, far, far] + [near] * 5,
        out_specs=[far] * 12,
        scratch_shapes=[vmem_like(m) for m in (tok_all, x_full, y_full, out_full) + results]
        + [
            pltpu.VMEM((rows, width), low),
            pltpu.VMEM((rows + 16, own), full),
            pltpu.VMEM((own // LANES, rows, LANES), full),
            pltpu.VMEM((own // LANES, rows, LANES), full),
            pltpu.VMEM((rows, own), low),
            pltpu.VMEM((2, own), full),
            pltpu.VMEM((n_dp, 2, own), full),
            dma_sems(2),
            dma_sems(2),
            dma_sems(n_dp),
            dma_sems(n_dp),
            pltpu.SemaphoreType.DMA,
            dma_sems(parts, 2, n_line - 1),
            dma_sems(parts, 2, n_line - 1),
            dma_sems(2),
            dma_sems(4),
            dma_sems(11),
            pltpu.VMEM((cot_rows, width), low),
        ],
        compiler_params=comm_params(5),
        name="recur_forward",
    )(
        tok_all,
        cot,
        to_place,
        to_stored,
        x_full,
        y_full,
        out_full,
        gain,
        gates,
        taps,
        soft,
        flags,
    )


def recur_backward(
    n_dp,
    n_line,
    mixer_in,
    to_place,
    to_stored,
    x_full,
    y_full,
    out_full,
    gates,
    taps,
    soft,
    slope,
    flags,
    kept,
    weight_terms,
    row_terms,
):
    rows, width = mixer_in.shape
    count, own = taps.shape
    size = gates.shape[0]
    wide = own + 2 * RIM
    blocks = (wide - RIM) // size
    chunk = rows // 8
    own_rows = rows // n_line
    parts = 4
    span = own_rows // parts

    def kernel(*refs):
        (mix_far, plc, sto, wx_far, wy_far, wo_far, gw, cw, sp, sg, fl) = refs[:11]
        kept_far, weights, feed_far = refs[11:19], refs[19], refs[20]
        (gxy_far, gate_grads, tap_grads, decay_grad, terms_far, weight_sum, row_sum) = refs[21:28]
        mix, wy, wo, feed = refs[28:32]
        (xext, y, conv_low, conv, pre_r, pre_i, rate, state) = refs[32:40]
        (gxy, mp, gm, lam, reach, gp_r, gp_i, grad, spread, rim_out, rim_in) = refs[40:51]
        (ret_out, ret_in, tap_sums, decay_sums, ends, agg, slots) = refs[51:58]
        (hs, hr, es, er, el, in_sems, out_sems, inbox, ls, lr, total) = refs[58:69]
        terms, wx = mix, wo
        fetch = Fetch(
            [
                (mix_far, mix),
                (wo_far, wo),
                (kept_far[1], y),
                (kept_far[7], state),
                (kept_far[6], rate),
                (kept_far[4], pre_r),
                (kept_far[5], pre_i),
                (kept_far[3], conv),
                (kept_far[2], conv_low),
                (kept_far[0], xext),
                (wx_far, wx),
                (wy_far, wy),
                (feed_far, feed),
            ],
            in_sems,
        )
        fetch.start(12, *range(10), 11)
        store = Fetch(((gxy, gxy_far), (terms, terms_far)), out_sems)
        place = Place(n_dp, n_line)
        place.meet(True)
        plane = ReducePlane(place, weights, refs[69:])
        plane.begin()
        lines = [
            ReduceLine(place, feed, own_rows, c * span, span, inbox.at[c], ls.at[c], lr.at[c])
            for c in range(parts)
        ]

        def send(c):
            if c > 0:
                lines[c - 1].sent()
            if c < parts:
                lines[c].ends()

        def add_up(c):
            lines[c].total(total)
            row_sum[pl.ds(c * span, span)] = total[...].astype(jnp.bfloat16)

        fetch.wait(12)
        send(0)
        swap = RimSwap(place, own)
        own_cols = pl.ds(RIM, own)

        def project(i):
            here = tile_rows(i, 128)
            mp[here] = plain_dot(plc[here], mix[...]).astype(jnp.bfloat16)
            gm[here] = plain_dot(mp[here], wo[...])

        fetch.wait(0, 1)
        loop(rows // 128, project)
        fetch.start(10)

        def split(i):
            here = tile_rows(i, TILE)
            branch, slope_y = gelu_parts(y[here])
            grads = gm[here]
            put_lanes(lam, here, grads * branch)
            values = state[tile_rows(i, TILE, 8)]
            gxy[here, own:] = (grads * values * slope_y).astype(jnp.bfloat16)

        fetch.wait(2, 3)
        loop(rows // TILE, split)
        send(1)
        lines[0].hop(0)
        fetch.wait(4)
        groups = own // LANES

        def scan(i, carry):
            here = pl.ds(chunk - 1 - i, 8, chunk)
            result = []
            for c in range(groups):
                product, message = carry[c]
                r = rate[c, here]
                value = lam[c, here] + message
                lam[c, here] = value
                reach[c, here] = product
                result.append((product * r, value * r))
            return tuple(result)

        blank = (jnp.ones((8, LANES), jnp.float32), jnp.zeros((8, LANES), jnp.float32))
        done = lax.fori_loop(0, chunk, scan, (blank,) * groups)
        for c in range(groups):
            lanes = pl.ds(c * LANES, LANES)
            ends[0, :, lanes] = done[c][0]
            ends[1, :, lanes] = done[c][1]
        product, message = jnp.ones((1, own), jnp.float32), jnp.zeros((1, own), jnp.float32)
        for j in reversed(range(8)):
            message = ends[1, j : j + 1] + ends[0, j : j + 1] * message
            product = product * ends[0, j : j + 1]
        agg[0:1] = product
        agg[1:2] = message
        swap_all = Exchange(place, "dp", agg, slots, es, er, el)
        swap_all.begin()
        plane.cores()
        swap_all.wait()
        lines[0].hop(1)
        entry = jnp.zeros((1, own), jnp.float32)
        for q in reversed(range(n_dp)):
            longer = slots[q, 1:2] + slots[q, 0:1] * entry
            entry = jnp.where(q > place.d, longer, entry)
        fetch.wait(5, 6, 7)
        for ref in (tap_sums, decay_sums):
            ref[...] = jnp.zeros_like(ref)
        for ref in (gp_r, gp_i):
            ref[:, 0:RIM] = jnp.zeros((rows, RIM), jnp.bfloat16)
            ref[:, RIM + own :] = jnp.zeros((rows, RIM), jnp.bfloat16)
        grad[pl.ds(0, 8)] = jnp.zeros((8, own), jnp.float32)
        grad[pl.ds(rows + 8, 8)] = jnp.zeros((8, own), jnp.float32)
        for j in reversed(range(8)):

            def back(i, entry=entry):
                here = tile_rows(i, TILE, j * chunk)
                flag = fl[tile_rows(i, TILE, j * chunk + 8)]
                start = flag[:, 0:1] > 0.0
                values = take_lanes(lam, here) + take_lanes(reach, here) * entry
                before = moved_up(
                    state[pl.ds(pl.multiple_of(j * chunk + i * TILE, 8), TILE + 8)], 7, TILE
                )
                sr, decay, scale = rate_and_scale(pre_r[here, own_cols], sp[...], start)
                si = jax.nn.sigmoid(pre_i[here, own_cols])
                block = conv[here]
                driven = values * si
                log_grad = values * before * decay - block * driven * (decay * decay) / scale
                log_grad = jnp.where(start, 0.0, log_grad)
                inner = sr * log_grad
                gp_r[here, own_cols] = (
                    -rate_scale * sp[...] * inner * (1.0 - sr)
                ).astype(jnp.bfloat16)
                gp_i[here, own_cols] = (driven * block * (1.0 - si) * scale).astype(jnp.bfloat16)
                grad[tile_rows(i, TILE, j * chunk + 8)] = driven * scale
                decay_sums[...] += inner[:8] + inner[8:]

            loop(chunk // TILE, back)
            if j == 4:
                send(2)
                lines[1].hop(0)
            entry = ends[1, j : j + 1] + ends[0, j : j + 1] * entry
        lines[1].hop(1)
        add_up(0)
        decay_grad[...] = rate_scale * sg[...] * jnp.sum(decay_sums[...], axis=0, keepdims=True)

        for i in range(blocks):
            index = lax.rem(i + 2 - 2 * swap.odd, blocks)
            cols = swap.block(index, size)
            other = pl.ds(pl.multiple_of(wide + swap.first + index * size, RIM), size)
            spread[:, cols] = times_trans(gp_r[:, cols], gw[:, cols]) + times_trans(
                gp_i[:, cols], gw[:, other]
            )
            if i == 0:
                rim_out[...] = spread[:, swap.beyond].astype(jnp.bfloat16)
                rim = remote(rim_out, rim_in, hs.at[0], hr.at[0], swap.partner)
                rim.start()
        send(3)
        lines[2].hop(0)
        rim.wait()
        shared = pl.ds(pl.multiple_of((1 - swap.odd) * (own - RIM), RIM), RIM)

        def join(i):
            here = tile_rows(i, TILE)
            there = tile_rows(i, TILE, 8)
            grad[there] += spread[here, own_cols]
            grad[there, shared] += rim_in[here].astype(jnp.float32)

        loop(rows // TILE, join)

        near = grad[pl.ds(0, 16)]
        back_rows = jnp.zeros((8, own), jnp.float32)
        for k in range(1, count):
            masked = near * fl[pl.ds(0, 16)][:, k : k + 1]
            back_rows += cw[k : k + 1] * moved_up(masked, k, 8)
        ret_out[...] = back_rows
        ret = remote(
            ret_out,
            ret_in,
            hs.at[1],
            hr.at[1],
            (lax.rem(place.d + n_dp - 1, n_dp), place.t),
        )
        ret.start()
        fetch.wait(8)
        for i in range(blocks):
            cols = swap.block(i, size)
            spread[0:size, cols] = trans_times(conv_low[:, cols], gp_r[:, cols])
            spread[size : 2 * size, cols] = trans_times(conv_low[:, cols], gp_i[:, cols])
        gate_grads[:, 0:own] = spread[0:size, own_cols].astype(jnp.bfloat16)
        gate_grads[:, own:] = spread[size : 2 * size, own_cols].astype(jnp.bfloat16)

        def taps_back(i, added=None):
            here = tile_rows(i, TILE)
            start = pl.ds(pl.multiple_of(i * TILE + 8, 8), TILE + 8)
            after = grad[start]
            flag = fl[start]
            behind = xext[pl.ds(pl.multiple_of(i * TILE, 16), 2 * TILE)].astype(jnp.float32)
            total = cw[0:1] * after[:TILE]
            for k in range(count):
                if k > 0:
                    masked = after * flag[:, k : k + 1]
                    total += cw[k : k + 1] * moved_up(masked, k, TILE)
                    mine = masked[:TILE]
                else:
                    mine = after[:TILE]
                term = mine * moved_up(behind, 16 - k, TILE)
                tap_sums[k] += term[:8] + term[8:]
            if added is not None:
                total = total + jnp.concatenate([jnp.zeros((8, own), jnp.float32), added], axis=0)
            gxy[here, 0:own] = total.astype(jnp.bfloat16)

        fetch.wait(9)
        loop(rows // TILE - 1, taps_back)
        lines[2].hop(1)
        add_up(1)
        ret.wait()
        taps_back(rows // TILE - 1, jnp.where(place.d < n_dp - 1, ret_in[...], 0.0))
        tap_grads[...] = jnp.zeros_like(tap_grads)
        for k in range(count):
            tap_grads[k : k + 1] = jnp.sum(tap_sums[k], axis=0, keepdims=True)

        store.start(0)
        plane.turn()
        send(4)
        lines[3].hop(0)

        def restore(i):
            here = tile_rows(i, 128)
            mp[here, 0 : 2 * own] = plain_dot(sto[here], gxy[...]).astype(jnp.bfloat16)

        loop(rows // 128, restore)

        def spread_back(i):
            some = tile_rows(i, 512)
            terms[:, pl.ds(pl.multiple_of(i * 512, 512), 512)] = (
                times_trans(mp[:, 0:own], wx[some]) + times_trans(mp[:, own : 2 * own], wy[some])
            ).astype(jnp.bfloat16)

        fetch.wait(10, 11)
        loop(width // 512, spread_back)
        store.start(1)
        lines[3].hop(1)
        add_up(2)
        plane.finish(weight_sum)
        add_up(3)
        for line in lines:
            line.finish()
        store.wait(0, 1)

    low, full = jnp.bfloat16, jnp.float32
    block = weight_terms.shape[0] // n_dp
    near, far = in_vmem(), in_any()
    return pl.pallas_call(
        kernel,
        out_shape=(
            shaped((rows, 2 * own), low),
            shaped((size, 2 * own), low),
            shaped((8, own), full),
            shaped((1, own), full),
            shaped((rows, width), low),
            shaped((block, weight_terms.shape[1]), low),
            shaped((own_rows, width), low),
        ),
        in_specs=[far, near, near, far, far, far] + [near] * 5 + [far] * 10,
        out_specs=[far, near, near, near, far, near, near],
        scratch_shapes=[vmem_like(m) for m in (mixer_in, y_full, out_full, row_terms, *kept)]
        + [
            pltpu.VMEM((rows, 2 * own), low),
            pltpu.VMEM((rows, width), low),
            pltpu.VMEM((rows, own), full),
            pltpu.VMEM((own // LANES, rows, LANES), full),
            pltpu.VMEM((own // LANES, rows, LANES), full),
            pltpu.VMEM((rows, wide), low),
            pltpu.VMEM((rows, wide), low),
            pltpu.VMEM((rows + 16, own), full),
            pltpu.VMEM((rows, wide), full),
            pltpu.VMEM((rows, RIM), low),
            pltpu.VMEM((rows, RIM), low),
            pltpu.VMEM((8, own), full),
            pltpu.VMEM((8, own), full),
            pltpu.VMEM((count, 8, own), full),
            pltpu.VMEM((8, own), full),
            pltpu.VMEM((2, 8, own), full),
            pltpu.VMEM((2, own), full),
            pltpu.VMEM((n_dp, 2, own), full),
            dma_sems(2),
            dma_sems(2),
            dma_sems(n_dp),
            dma_sems(n_dp),
            pltpu.SemaphoreType.DMA,
            dma_sems(13),
            dma_sems(2),
            pltpu.VMEM((parts, 2, n_line - 1, span, width), low),
            dma_sems(parts, 2, n_line - 1),
            dma_sems(parts, 2, n_line - 1),
            pltpu.VMEM((span, width), full),
        ]
        + ReducePlane.scratch(block, weight_terms.shape[1]),
        compiler_params=comm_params(6),
        name="recur_backward",
    )(
        mixer_in,
        to_place,
        to_stored,
        x_full,
        y_full,
        out_full,
        gates,
        taps,
        soft,
        slope,
        flags,
        *kept,
        weight_terms,
        row_terms,
    )


def column_parts(width, size=768):
    return [(c, min(size, width - c)) for c in range(0, width, size)]


def feed_forward(n_dp, n_line, hidden, gate, up, down, grads, grad_own):
    rows, width = hidden.shape
    units = gate.shape[1]
    own_rows = grad_own.shape[0]
    ready = grads.shape[0] // n_line
    late = own_rows - ready
    part = width // 4

    def kernel(*refs):
        hid_far, wg_far, wu_far, wd_far, grads_far, own_far = refs[:6]
        product_far, gup_far, back_far, gdown_far, ggate_far = refs[6:11]
        hid, wg, wu, wd, grad, slope, branch, product, ggate, gup, stage, back = refs[11:23]
        in_sems, out_sems, stage_sems, ls, lr = refs[23:]
        place = Place(n_dp, n_line)
        pairs = [(hid_far, hid), (wg_far, wg), (wu_far, wu), (wd_far, wd)]
        pairs += [
            (grads_far.at[pl.ds(q * ready, ready)], grad.at[pl.ds(q * own_rows, ready)])
            for q in range(n_line)
        ]
        mine = pl.ds(pl.multiple_of(place.t * own_rows + ready, 16), late)
        pairs.append((own_far.at[pl.ds(ready, late)], grad.at[mine]))
        fetch = Fetch(pairs, in_sems)
        fetch.start(*range(len(pairs)))
        store = Fetch(((product, product_far), (gup, gup_far), (back, back_far)), out_sems)
        place.meet()
        line = GatherLine(place, grad, own_rows, ready, late, ls, lr)
        line.step(0, own_far.at[pl.ds(ready, late)])
        columns = column_parts(units)
        fetch.wait(0, 1)
        for c, size in columns:
            cols = pl.ds(c, size)

            def gates(i, cols=cols):
                here = tile_rows(i, 256)
                branch[here, cols] = plain_dot(hid[here], wg[:, cols])

            loop(rows // 256, gates)
        line.step(1)
        fetch.wait(2)
        for c, size in columns:
            cols = pl.ds(c, size)

            def ups(i, cols=cols):
                here = tile_rows(i, 256)
                value = plain_dot(hid[here], wu[:, cols])
                active, bend = gelu_parts(branch[here, cols])
                product[here, cols] = (active * value).astype(jnp.bfloat16)
                branch[here, cols] = active
                slope[here, cols] = bend * value

            loop(rows // 256, ups)
        store.start(0)
        line.step(2)
        fetch.wait(*range(4, len(pairs)))
        line.finish()

        def weight_rows(left, right, far, first):
            for i in range(4):
                some = pl.ds(i * part, part)
                copy = pltpu.make_async_copy(
                    stage.at[i % 2], far.at[some], stage_sems.at[first + i]
                )
                if i >= 2:
                    pltpu.make_async_copy(
                        stage.at[i % 2],
                        far.at[pl.ds((i - 2) * part, part)],
                        stage_sems.at[first + i - 2],
                    ).wait()
                stage[i % 2] = trans_times(left[:, some], right[...]).astype(jnp.bfloat16)
                copy.start()
            for i in (2, 3):
                pltpu.make_async_copy(
                    stage.at[i % 2], far.at[pl.ds(i * part, part)], stage_sems.at[first + i]
                ).wait()

        weight_rows(grad, product, gdown_far, 0)
        fetch.wait(3)
        for c, size in columns:
            cols = pl.ds(c, size)

            def backs(i, cols=cols):
                here = tile_rows(i, 256)
                value = plain_dot(grad[here], wd[:, cols])
                ggate[here, cols] = (value * slope[here, cols]).astype(jnp.bfloat16)
                gup[here, cols] = (value * branch[here, cols]).astype(jnp.bfloat16)

            loop(rows // 256, backs)
        store.start(1)
        for i in range(4):
            some = pl.ds(i * part, part)
            back[:, some] = (
                times_trans(ggate[...], wg[some]) + times_trans(gup[...], wu[some])
            ).astype(jnp.bfloat16)
        store.start(2)
        weight_rows(hid, ggate, ggate_far, 4)
        store.wait(0, 1, 2)

    low, full = jnp.bfloat16, jnp.float32
    return pl.pallas_call(
        kernel,
        out_shape=(
            shaped((rows, units), low),
            shaped((rows, units), low),
            shaped((rows, width), low),
            shaped((width, units), low),
            shaped((width, units), low),
        ),
        in_specs=[in_any()] * 6,
        out_specs=[in_any()] * 5,
        scratch_shapes=[vmem_like(m) for m in (hidden, gate, up, down)]
        + [
            pltpu.VMEM((n_line * own_rows, width), low),
            pltpu.VMEM((rows, units), full),
            pltpu.VMEM((rows, units), full),
            pltpu.VMEM((rows, units), low),
            pltpu.VMEM((rows, units), low),
            pltpu.VMEM((rows, units), low),
            pltpu.VMEM((2, part, units), low),
            pltpu.VMEM((rows, width), low),
            dma_sems(5 + n_line),
            dma_sems(3),
            dma_sems(8),
            dma_sems(2, n_line - 1),
            dma_sems(2, n_line - 1),
        ],
        compiler_params=comm_params(7),
        name="feed_forward",
    )(hidden, gate, up, down, grads, grad_own)


def matches(mesh):
    return mesh.shape["dp"] == 8 and mesh.shape["tensor"] == 4


def local_blocks(
    tokens,
    norm_gain,
    x_weight,
    y_weight,
    conv_weight,
    recur_gate_weight,
    input_gate_weight,
    decay_param,
    out_weight,
    mlp_gain,
    gate_weight,
    up_weight,
    down_weight,
    seq_lengths,
    token_order,
    cotangent,
):
    n_dp, n_tensor = lax.axis_size("dp"), lax.axis_size("tensor")
    tensor_index = lax.axis_index("tensor")
    dp_index = lax.axis_index("dp")
    tok_rows, width = tokens.shape
    row_count = tok_rows * n_tensor
    own_width = conv_weight.shape[1]
    kernel_taps = conv_weight.shape[0]
    edge_rows = kernel_taps - 1
    dp_width = norm_gain.shape[0]
    gate_rows = recur_gate_weight.shape[0]
    own_start = tensor_index * tok_rows

    gains = jnp.concatenate([norm_gain, mlp_gain])
    spare = gate_rows * 128 - gains.shape[0]
    gains = jnp.pad(gains, (0, spare)).reshape(gate_rows, 128)
    minor = jnp.concatenate([recur_gate_weight, input_gate_weight, gains], axis=1)
    own_order = (token_order - dp_index * row_count).astype(jnp.int32)
    order_rows = jnp.broadcast_to(own_order[None, :], (8, tok_rows))
    x_full, y_full, out_full, minor_full, tok_all, order_full = first_gather(
        n_dp, n_tensor, (x_weight, y_weight, out_weight.T, minor), tokens, order_rows
    )
    late_up, late_down, _ = lax.optimization_barrier((up_weight, down_weight.T, tok_all))
    up_full = lax.all_gather(late_up, "dp", axis=0, tiled=True)
    down_full = lax.all_gather(late_down, "dp", axis=0, tiled=True)
    order_all = order_full.reshape(n_tensor, 8, tok_rows)[:, 0].reshape(row_count)
    both_gates = minor_full[:, : 2 * own_width]
    gain_rows = minor_full[:, 2 * own_width :].reshape(n_dp, -1)
    first_gain = gain_rows[:, :dp_width].reshape(1, width).astype(jnp.float32)
    second_gain = gain_rows[:, dp_width : 2 * dp_width].reshape(1, width).astype(jnp.float32)
    block_size = both_gates.shape[0]
    row_index = jnp.arange(row_count, dtype=jnp.int32)
    hits = row_index[:, None] == order_all[None, :]
    to_place = hits.astype(jnp.bfloat16)
    to_stored = (order_all[:, None] == row_index[None, :]).astype(jnp.bfloat16)
    places = dp_index * row_count + jnp.arange(-8, row_count + 8, dtype=jnp.int32)
    inside = (jnp.arange(row_count + 16) >= 8) & (jnp.arange(row_count + 16) < row_count + 8)
    ends = jnp.cumsum(seq_lengths)
    segment = segment_of(places, ends)
    starts = (places == 0) | (segment != segment_of(places - 1, ends))
    columns = [starts] + [
        segment_of(places - shift, ends) == segment for shift in range(1, kernel_taps)
    ]
    columns += [jnp.zeros_like(starts)] * (8 - len(columns))
    flags = (jnp.stack(columns, axis=1) & inside[:, None]).astype(jnp.float32)
    live_own = (token_order < ends[-1]).astype(jnp.float32)
    grad_in_own = (cotangent.astype(jnp.float32) * live_own[:, None]).astype(jnp.bfloat16)
    soft = jax.nn.softplus(-decay_param).reshape(1, own_width)
    slope = jax.nn.sigmoid(-decay_param).reshape(1, own_width)
    zero_rim = jnp.zeros((block_size, RIM), jnp.bfloat16)
    gates_wide = jnp.concatenate(
        [
            zero_rim,
            both_gates[:, :own_width],
            zero_rim,
            zero_rim,
            both_gates[:, own_width:],
            zero_rim,
        ],
        axis=1,
    )
    hidden_place, *kept, merged_stored, mixer_terms, grad_rows = recur_forward(
        n_dp,
        n_tensor,
        tok_all,
        grad_in_own,
        to_place,
        to_stored,
        x_full,
        y_full,
        out_full,
        first_gain,
        gates_wide,
        conv_weight,
        soft,
        flags,
    )
    after_own, hidden_two, gate_full = middle_gather(
        n_dp, n_tensor, mixer_terms, tokens, second_gain, (gate_weight,)
    )
    product, grad_up_pre, back_terms, grad_down, grad_gate = feed_forward(
        n_dp,
        n_tensor,
        hidden_two,
        gate_full,
        up_full,
        down_full,
        grad_rows,
        grad_in_own,
    )
    down_sum = lax.psum_scatter(grad_down, "dp", scatter_dimension=0, tiled=True)
    grad_after_own, second_part, mixer_in, gate_sum, grad_up, feed_terms = middle_sums(
        n_dp,
        n_tensor,
        back_terms,
        after_own,
        second_gain,
        grad_in_own,
        grad_gate,
        hidden_two,
        grad_up_pre,
        product,
        down_full,
    )
    grad_xy, gate_grads, tap_grads, decay_grad, one_terms, up_sum, feed_out = recur_backward(
        n_dp,
        n_tensor,
        mixer_in,
        to_place,
        to_stored,
        x_full,
        y_full,
        out_full,
        gates_wide,
        conv_weight,
        soft,
        slope,
        flags,
        kept,
        grad_up,
        feed_terms,
    )
    output = (after_own + feed_out.astype(jnp.float32)) * live_own[:, None]
    output = output.astype(jnp.bfloat16)
    grad_out_mat = trans_times(mixer_in, merged_stored).astype(jnp.bfloat16)
    grad_xy_mat = trans_times(hidden_place, grad_xy).astype(jnp.bfloat16)
    small = jnp.concatenate(
        [
            second_part,
            tap_grads[:kernel_taps].reshape(1, -1),
            jnp.pad(decay_grad, ((0, 0), (0, width - own_width))),
            jnp.zeros((1, width), jnp.float32),
        ],
        axis=0,
    )
    grad_tokens, small_sum, gain_sums, xy_sum, out_sum, gates_sum = last_sums(
        n_dp,
        n_tensor,
        one_terms,
        tokens,
        first_gain,
        grad_after_own,
        small,
        (grad_xy_mat, grad_out_mat, gate_grads),
    )
    xy_sum, gates_sum = xy_sum.astype(jnp.float32), gates_sum.astype(jnp.float32)
    own_gains = lax.dynamic_slice_in_dim(gain_sums, dp_index * dp_width, dp_width, 1)
    return (
        output,
        grad_tokens,
        own_gains[1],
        xy_sum[:, :own_width],
        xy_sum[:, own_width:],
        small_sum[1].reshape(kernel_taps, own_width),
        gates_sum[:, :own_width],
        gates_sum[:, own_width:],
        small_sum[2, :own_width],
        out_sum.astype(jnp.float32).T,
        own_gains[0],
        gate_sum.astype(jnp.float32),
        up_sum.astype(jnp.float32),
        down_sum.astype(jnp.float32).T,
    )


def solution(mesh):
    in_specs = (
        P(("dp", "tensor"), None),
        P("dp"),
        P("dp", "tensor"),
        P("dp", "tensor"),
        P(None, "tensor"),
        P("dp", "tensor"),
        P("dp", "tensor"),
        P("tensor"),
        P("tensor", "dp"),
        P("dp"),
        P("dp", "tensor"),
        P("dp", "tensor"),
        P("tensor", "dp"),
        P(),
        P(("dp", "tensor")),
        P(("dp", "tensor"), None),
    )
    out_specs = (
        P(("dp", "tensor"), None),
        P(("dp", "tensor"), None),
        P("dp"),
        P("dp", "tensor"),
        P("dp", "tensor"),
        P(None, "tensor"),
        P("dp", "tensor"),
        P("dp", "tensor"),
        P("tensor"),
        P("tensor", "dp"),
        P("dp"),
        P("dp", "tensor"),
        P("dp", "tensor"),
        P("tensor", "dp"),
    )
    fits = matches(mesh)
    local = local_blocks if fits else local_general
    return jax.shard_map(local, mesh=mesh, in_specs=in_specs, out_specs=out_specs, check_vma=False)
```

```python
import jax
import jax.numpy as jnp
from jax import lax
from jax.experimental import pallas as pl
from jax.experimental.pallas import tpu as pltpu
from jax.sharding import PartitionSpec as P

epsilon = 1e-06
rate_scale = 8.0


def from_behind(block, axis, distance):
    devices = range(lax.axis_size(axis))
    route = [(i - distance, i) for i in devices if i - distance in devices]
    return lax.ppermute(block, axis, route)


def extended_2(array, sides, width):
    for axis, dim in sides:
        size, length = (lax.axis_size(axis), array.shape[dim])
        up = [(i, (i + 1) % size) for i in range(size - 1)]
        down = [(j, i) for i, j in up]
        last = lax.slice_in_dim(array, length - width, length, axis=dim)
        leading = lax.slice_in_dim(array, 0, width, axis=dim)
        before = lax.ppermute(last, axis, up)
        after = lax.ppermute(leading, axis, down)
        array = jnp.concatenate([before, array, after], axis=dim)
    return array


def entering(value, axis, join, neutral, backward):
    count, mine = (lax.axis_size(axis), lax.axis_index(axis))
    pieces = jax.tree.map(lambda part: lax.all_gather(part, axis), value)
    if backward:
        pieces = jax.tree.map(lambda part: part[::-1], pieces)
        mine = count - 1 - mine
    total = jax.tree.map(
        lambda part, zero: jnp.full_like(part, 0) + jnp.asarray(zero, part.dtype), value, neutral
    )

    def lap(position, total):
        longer = join(total, jax.tree.map(lambda part: part[position], pieces))
        return jax.tree.map(lambda new, old: jnp.where(position < mine, new, old), longer, total)

    return lax.fori_loop(0, count - 1, lap, total)


def rms_scale(values, gain):
    return values * lax.rsqrt(jnp.mean(values * values, axis=-1, keepdims=True) + epsilon) * gain


def norm_back(values, gain, grad):
    inv_root = lax.rsqrt(jnp.mean(values * values, axis=-1, keepdims=True) + epsilon)
    normed = values * inv_root
    upstream = grad * gain
    grad_values = inv_root * (
        upstream - normed * jnp.mean(upstream * normed, axis=-1, keepdims=True)
    )
    return (grad_values, normed)


def segment_of(places, ends):
    return jnp.sum((ends[None, :] <= places[:, None]).astype(jnp.int32), axis=1)


def pair_step(early, later):
    return (early[0] * later[0], later[0] * early[1] + later[1])


def plain_dot(left, right):
    return jnp.dot(left, right, preferred_element_type=jnp.float32)


def times_trans(left, right):
    return lax.dot_general(
        left, right, (((1,), (1,)), ((), ())), preferred_element_type=jnp.float32
    )


def trans_times(left, right):
    return lax.dot_general(
        left, right, (((0,), (0,)), ((), ())), preferred_element_type=jnp.float32
    )


def gelu_tanh(values):
    return jax.nn.gelu(values, approximate=True)


def collect(
    norm_gain,
    mlp_gain,
    x_weight,
    y_weight,
    recur_gate_weight,
    input_gate_weight,
    gate_weight,
    up_weight,
    out_weight,
    down_weight,
):
    return (
        lax.all_gather(norm_gain, "dp", axis=0, tiled=True),
        lax.all_gather(mlp_gain, "dp", axis=0, tiled=True),
        lax.all_gather(x_weight, "dp", axis=0, tiled=True),
        lax.all_gather(y_weight, "dp", axis=0, tiled=True),
        lax.all_gather(recur_gate_weight, "dp", axis=0, tiled=True),
        lax.all_gather(input_gate_weight, "dp", axis=0, tiled=True),
        lax.all_gather(gate_weight, "dp", axis=0, tiled=True),
        lax.all_gather(up_weight, "dp", axis=0, tiled=True),
        lax.all_gather(out_weight, "dp", axis=1, tiled=True),
        lax.all_gather(down_weight, "dp", axis=1, tiled=True),
    )


def row_sums(term_rows, tok_rows):
    return lax.psum_scatter(
        term_rows(jnp.int32(0), lax.axis_size("tensor") * tok_rows).astype(jnp.bfloat16),
        "tensor",
        scatter_dimension=0,
        tiled=True,
    ).astype(jnp.float32)


def spread_rows(values):
    return lax.all_gather(values, "tensor", axis=0, tiled=True)


def local_general(
    tokens,
    norm_gain,
    x_weight,
    y_weight,
    conv_weight,
    recur_gate_weight,
    input_gate_weight,
    decay_param,
    out_weight,
    mlp_gain,
    gate_weight,
    up_weight,
    down_weight,
    seq_lengths,
    token_order,
    cotangent,
):
    n_tensor = lax.axis_size("tensor")
    tensor_index = lax.axis_index("tensor")
    dp_index = lax.axis_index("dp")
    tok_rows = tokens.shape[0]
    row_count = tok_rows * n_tensor
    own_width = conv_weight.shape[1]
    kernel_taps = conv_weight.shape[0]
    edge_rows = kernel_taps - 1
    dp_width = norm_gain.shape[0]
    own_start = tensor_index * tok_rows
    shards = (
        norm_gain,
        mlp_gain,
        x_weight,
        y_weight,
        recur_gate_weight,
        input_gate_weight,
        gate_weight,
        up_weight,
        out_weight,
        down_weight,
    )
    (
        gain_one,
        gain_two,
        x_full,
        y_full,
        recur_full,
        input_full,
        gate_full,
        up_full,
        out_full,
        down_full,
    ) = collect(*shards)
    block_size = recur_full.shape[0]
    first_gain = gain_one.astype(jnp.float32)
    second_gain = gain_two.astype(jnp.float32)
    both_gates = jnp.concatenate([recur_full, input_full], axis=1)
    tok_own = tokens.astype(jnp.float32)
    own_order = token_order - dp_index * row_count
    first_rows = rms_scale(tok_own, first_gain).astype(jnp.bfloat16)
    first_all, cot_all, order_all = (
        lax.all_gather(first_rows, "tensor", axis=0, tiled=True),
        lax.all_gather(cotangent, "tensor", axis=0, tiled=True),
        lax.all_gather(own_order, "tensor", axis=0, tiled=True),
    )
    row_index = jnp.arange(row_count, dtype=jnp.int32)
    inverse = jnp.zeros((row_count,), jnp.int32).at[order_all].set(row_index)
    hidden_place = jnp.take(first_all, inverse, axis=0)
    places = dp_index * row_count + row_index
    ends = jnp.cumsum(seq_lengths)
    segment = segment_of(places, ends)
    starts = (places == 0) | (segment != segment_of(places - 1, ends))
    live = (places < ends[-1]).astype(jnp.float32)
    live_stored = jnp.take(live, order_all, axis=0)
    same = [
        (segment_of(places - shift, ends) == segment).astype(jnp.float32)
        for shift in range(kernel_taps)
    ]
    low_edge = tensor_index * own_width
    own_blocks = (low_edge + jnp.arange(own_width, dtype=jnp.int32)) // block_size
    first_block = low_edge // block_size
    block_count = own_width // block_size + 2

    def block_start(index):
        return (first_block + index) * block_size - low_edge + block_size

    def block_mask(index):
        inside = own_blocks == first_block + index
        return jnp.concatenate([inside, inside])

    def convolve(extended, kernel):
        return sum(
            (
                kernel[shift][None, :]
                * extended[edge_rows - shift : edge_rows - shift + row_count]
                * same[shift][:, None]
                for shift in range(kernel_taps)
            )
        )

    def gates(conv_vals, pre_recur, pre_input, decay_vals):
        log_rate = -rate_scale * jax.nn.sigmoid(pre_recur) * jax.nn.softplus(-decay_vals)
        decay_rate = jnp.where(starts[:, None], 0.0, jnp.exp(log_rate))
        scale_in = jnp.where(starts[:, None], 1.0, jnp.sqrt(-jnp.expm1(2.0 * log_rate)))
        return (decay_rate, conv_vals * jax.nn.sigmoid(pre_input) * scale_in)

    def glu(gate_pre, up_pre):
        return gelu_tanh(gate_pre) * up_pre

    x_branch = plain_dot(hidden_place, x_full).astype(jnp.bfloat16)
    y_before = plain_dot(hidden_place, y_full)
    previous = from_behind(x_branch[row_count - edge_rows :], "dp", 1)
    extended = jnp.concatenate([previous, x_branch], axis=0).astype(jnp.float32)
    conv_out = convolve(extended, conv_weight)
    conv_wide = extended_2(conv_out.astype(jnp.bfloat16), (("tensor", 1),), block_size)
    pre_both = jnp.zeros((row_count, 2 * own_width), jnp.float32)
    for index in range(block_count):
        piece = lax.dynamic_slice_in_dim(conv_wide, block_start(index), block_size, 1)
        pre_both = pre_both + jnp.where(
            block_mask(index)[None, :], plain_dot(piece, both_gates), 0.0
        )
    (decay_rate, driven), gate_pull = jax.vjp(
        gates, conv_out, pre_both[:, :own_width], pre_both[:, own_width:], decay_param
    )
    cum_rate, local_state = lax.associative_scan(pair_step, (decay_rate, driven), axis=0)
    ident = (jnp.ones((own_width,), jnp.float32), jnp.zeros((own_width,), jnp.float32))
    rate_in, state_in = entering((cum_rate[-1], local_state[-1]), "dp", pair_step, ident, False)
    state = local_state + cum_rate * state_in[None, :]
    y_branch = gelu_tanh(y_before)
    merged = (state * y_branch).astype(jnp.bfloat16)
    merged_stored = jnp.take(merged, order_all, axis=0)

    def mixer_rows(begin, number):
        return plain_dot(merged_stored, out_full)

    after_own = tok_own + row_sums(mixer_rows, tok_rows)
    hidden_two = spread_rows(rms_scale(after_own, second_gain).astype(jnp.bfloat16))
    gate_pre = plain_dot(hidden_two, gate_full)
    up_pre = plain_dot(hidden_two, up_full)
    glu_out, glu_pull = jax.vjp(glu, gate_pre, up_pre)
    product = glu_out.astype(jnp.bfloat16)

    def down_rows(begin, number):
        return plain_dot(product, down_full)

    feed_out = row_sums(down_rows, tok_rows)
    live_own = lax.dynamic_slice_in_dim(live_stored, own_start, tok_rows, 0)
    output = ((after_own + feed_out) * live_own[:, None]).astype(jnp.bfloat16)
    grad_out = cot_all.astype(jnp.float32) * live_stored[:, None]
    fresh = lax.optimization_barrier((shards, grad_out))[0]
    (
        gain_one,
        gain_two,
        x_full,
        y_full,
        recur_full,
        input_full,
        gate_full,
        up_full,
        out_full,
        down_full,
    ) = collect(*fresh)
    first_gain = gain_one.astype(jnp.float32)
    second_gain = gain_two.astype(jnp.float32)
    both_gates = jnp.concatenate([recur_full, input_full], axis=1)
    down_in = grad_out.astype(jnp.bfloat16)
    grad_down = trans_times(product, down_in)
    grad_product = times_trans(down_in, down_full)
    grad_gate_pre, grad_up_pre = glu_pull(grad_product)
    grad_gate_pre = grad_gate_pre.astype(jnp.bfloat16)
    grad_up_pre = grad_up_pre.astype(jnp.bfloat16)
    grad_gate = trans_times(hidden_two, grad_gate_pre)
    grad_up = trans_times(hidden_two, grad_up_pre)

    def feed_rows(begin, number):
        return times_trans(grad_gate_pre, gate_full) + times_trans(grad_up_pre, up_full)

    grad_out_own = lax.dynamic_slice_in_dim(grad_out, own_start, tok_rows, 0)
    grad_two_own = row_sums(feed_rows, tok_rows)
    grad_norm_own, normed_two = norm_back(after_own, second_gain, grad_two_own)
    second_part = jnp.sum(grad_two_own * normed_two, axis=0)
    grad_after_own = grad_out_own + grad_norm_own
    mixer_in = spread_rows(grad_after_own.astype(jnp.bfloat16))
    grad_out_mat = trans_times(merged_stored, mixer_in)
    grad_merged = jnp.take(times_trans(mixer_in, out_full), inverse, axis=0)
    grad_state = grad_merged * y_branch
    gelu_pull = jax.vjp(gelu_tanh, y_before)[1]
    grad_y_before = gelu_pull(grad_merged * state)[0].astype(jnp.bfloat16)
    rate_next = jnp.concatenate([decay_rate[1:], jnp.ones((1, own_width), jnp.float32)], axis=0)
    rev_rate, local_lam = lax.associative_scan(
        pair_step, (rate_next, grad_state), reverse=True, axis=0
    )
    head_rate = decay_rate[0] * rev_rate[0]
    head_lam = decay_rate[0] * local_lam[0]
    factor_in, lam_in = entering((head_rate, head_lam), "dp", pair_step, ident, True)
    lam = local_lam + rev_rate * lam_in[None, :]
    state_prev = jnp.concatenate([state_in[None, :], state[:-1]], axis=0)
    grad_conv_local, grad_pre_recur, grad_pre_input, grad_decay_own = gate_pull(
        (lam * state_prev, lam)
    )
    grad_pre = jnp.concatenate([grad_pre_recur, grad_pre_input], axis=1).astype(jnp.bfloat16)
    grad_both = jnp.zeros((block_size, 2 * own_width), jnp.float32)
    grad_wide = jnp.zeros((row_count, own_width + 2 * block_size), jnp.float32)
    for index in range(block_count):
        begin = block_start(index)
        piece = lax.dynamic_slice_in_dim(conv_wide, begin, block_size, 1)
        masked = jnp.where(block_mask(index)[None, :], grad_pre, jnp.zeros((), jnp.bfloat16))
        grad_both = grad_both + trans_times(piece, masked)
        added = lax.dynamic_slice_in_dim(grad_wide, begin, block_size, 1) + times_trans(
            masked, both_gates
        )
        grad_wide = lax.dynamic_update_slice_in_dim(grad_wide, added, begin, 1)
    grad_recur = grad_both[:, :own_width]
    grad_input = grad_both[:, own_width:]
    rims = jnp.concatenate(
        [grad_wide[:, :block_size], grad_wide[:, own_width + block_size :]], axis=1
    )
    arrived = extended_2(rims.astype(jnp.bfloat16), (("tensor", 1),), block_size).astype(rims.dtype)
    from_lower = jnp.pad(arrived[:, :block_size], ((0, 0), (0, own_width - block_size)))
    from_upper = jnp.pad(arrived[:, 3 * block_size :], ((0, 0), (own_width - block_size, 0)))
    grad_conv = (
        grad_conv_local
        + grad_wide[:, block_size : block_size + own_width]
        + from_lower
        + from_upper
    )
    conv_pull = jax.vjp(convolve, extended, conv_weight)[1]
    grad_extended, grad_kernel = conv_pull(grad_conv)
    returned = from_behind(grad_extended[:edge_rows], "dp", -1)
    grad_x_branch = grad_extended[edge_rows:] + jnp.concatenate(
        [jnp.zeros((row_count - edge_rows, own_width), jnp.float32), returned], axis=0
    )
    grad_x_low = grad_x_branch.astype(jnp.bfloat16)
    grad_x_stored = jnp.take(grad_x_low, order_all, axis=0)
    grad_y_stored = jnp.take(grad_y_before, order_all, axis=0)
    grad_x_mat = trans_times(first_all, grad_x_stored)
    grad_y_mat = trans_times(first_all, grad_y_stored)

    def mixer_back_rows(begin, number):
        return times_trans(grad_x_stored, x_full) + times_trans(grad_y_stored, y_full)

    grad_one_own = row_sums(mixer_back_rows, tok_rows)
    grad_norm_one, normed_one = norm_back(tok_own, first_gain, grad_one_own)
    first_part = jnp.sum(grad_one_own * normed_one, axis=0)
    grad_tokens = grad_after_own + grad_norm_one
    chosen = jnp.arange(n_tensor, dtype=jnp.int32) == tensor_index
    kernel_tile = jnp.where(chosen[:, None, None], grad_kernel[None, :, :], 0.0)
    decay_tile = jnp.where(chosen[:, None], grad_decay_own[None, :], 0.0)
    small = lax.psum((first_part, second_part, kernel_tile, decay_tile), ("dp", "tensor"))
    grad_first_gain = lax.dynamic_slice_in_dim(small[0], dp_index * dp_width, dp_width, 0)
    grad_second_gain = lax.dynamic_slice_in_dim(small[1], dp_index * dp_width, dp_width, 0)
    grad_kernel_sum = lax.dynamic_index_in_dim(small[2], tensor_index, 0, keepdims=False)
    grad_decay = lax.dynamic_index_in_dim(small[3], tensor_index, 0, keepdims=False)
    sums = (
        lax.psum_scatter(
            grad_x_mat.astype(jnp.bfloat16), "dp", scatter_dimension=0, tiled=True
        ).astype(jnp.float32),
        lax.psum_scatter(
            grad_y_mat.astype(jnp.bfloat16), "dp", scatter_dimension=0, tiled=True
        ).astype(jnp.float32),
        lax.psum_scatter(
            grad_recur.astype(jnp.bfloat16), "dp", scatter_dimension=0, tiled=True
        ).astype(jnp.float32),
        lax.psum_scatter(
            grad_input.astype(jnp.bfloat16), "dp", scatter_dimension=0, tiled=True
        ).astype(jnp.float32),
        lax.psum_scatter(
            grad_gate.astype(jnp.bfloat16), "dp", scatter_dimension=0, tiled=True
        ).astype(jnp.float32),
        lax.psum_scatter(
            grad_up.astype(jnp.bfloat16), "dp", scatter_dimension=0, tiled=True
        ).astype(jnp.float32),
        lax.psum_scatter(
            grad_out_mat.astype(jnp.bfloat16), "dp", scatter_dimension=1, tiled=True
        ).astype(jnp.float32),
        lax.psum_scatter(
            grad_down.astype(jnp.bfloat16), "dp", scatter_dimension=1, tiled=True
        ).astype(jnp.float32),
    )
    return (
        output,
        grad_tokens,
        grad_first_gain,
        sums[0],
        sums[1],
        grad_kernel_sum,
        sums[2],
        sums[3],
        grad_decay,
        sums[6],
        grad_second_gain,
        sums[4],
        sums[5],
        sums[7],
    )


MESH = pl.DeviceIdType.MESH
VMEM_BYTES = 60 * 2**20


def remote(src, dst, send, recv, device):
    return pltpu.make_async_remote_copy(
        src_ref=src,
        dst_ref=dst,
        send_sem=send,
        recv_sem=recv,
        device_id=device,
        device_id_type=MESH,
    )


class Place:
    def __init__(self, n_dp, n_line):
        self.n_dp, self.n_line = n_dp, n_line
        self.d, self.t = lax.axis_index("dp"), lax.axis_index("tensor")
        self.core = lax.rem(self.d, 2)
        self.x = lax.rem(lax.div(self.d, 2), 2)
        self.y = lax.div(self.d, 4)

    def chip(self, flip_x, flip_y, flip_core=0):
        x = 1 - self.x if flip_x else self.x
        y = 1 - self.y if flip_y else self.y
        core = 1 - self.core if flip_core else self.core
        return y * 4 + x * 2 + core

    def at(self, flip_x=0, flip_y=0, flip_core=0):
        return (self.chip(flip_x, flip_y, flip_core), self.t)

    def up(self):
        return (self.d, lax.rem(self.t + 1, self.n_line))

    def down(self):
        return (self.d, lax.rem(self.t + self.n_line - 1, self.n_line))

    def meet(self, everyone=False):
        barrier = pltpu.get_barrier_semaphore()

        def greet(device):
            pl.semaphore_signal(barrier, inc=1, device_id=device, device_id_type=MESH)

        if everyone:
            for i in range(1, self.n_dp):
                greet((lax.rem(self.d + i, self.n_dp), self.t))
            for i in range(1, self.n_line):
                greet((self.d, lax.rem(self.t + i, self.n_line)))
            pl.semaphore_wait(barrier, self.n_dp + self.n_line - 2)
            return
        for flips in ((1, 0), (0, 1), (0, 0, 1)):
            greet(self.at(*flips))
        below, above = self.t > 0, self.t < self.n_line - 1

        @pl.when(below)
        def _():
            greet(self.down())

        @pl.when(above)
        def _():
            greet(self.up())

        pl.semaphore_wait(barrier, 3 + below.astype(jnp.int32) + above.astype(jnp.int32))


class Fetch:
    def __init__(self, pairs, sems):
        self.copies = [
            pltpu.make_async_copy(src, dst, sems.at[i]) for i, (src, dst) in enumerate(pairs)
        ]

    def start(self, *which):
        for i in which:
            self.copies[i].start()

    def wait(self, *which):
        for i in which:
            self.copies[i].wait()


def vmem_like(array):
    return pltpu.VMEM(array.shape, array.dtype)


class Kept:
    def __init__(self, src, dst, held, sems):
        self.there = pltpu.make_async_copy(src, held, sems.at[0])
        self.back = pltpu.make_async_copy(held, dst, sems.at[1])

    def begin(self):
        self.there.start()

    def turn(self):
        self.there.wait()
        self.back.start()

    def finish(self):
        self.back.wait()


class GatherPlane:
    def __init__(self, place, src, dst, send, recv, local, held):
        self.p, self.src, self.dst = place, src, dst
        self.rows = src.shape[0]
        self.send, self.recv = send, recv
        self.keep = Kept(src, self.block(0, 0), held, local)

    def block(self, fx, fy, fc=0, part=None):
        first = self.p.chip(fx, fy, fc) * self.rows
        size = self.rows
        if part is not None:
            size = self.rows // 2
            first = first + part * size
        return self.dst.at[pl.ds(pl.multiple_of(first, 16), size)]

    def copy(self, i, src, dst, device):
        return remote(src, dst, self.send.at[i], self.recv.at[i], device)

    def outgoing(self, i):
        at, block = self.p.at, self.block
        if i == 0:
            return self.copy(0, self.src, block(0, 0), at(1, 0))
        if i == 1:
            return self.copy(1, self.src, block(0, 0), at(0, 1))
        if i == 2:
            return self.copy(2, self.src, block(0, 0), at(0, 0, 1))
        if i == 3:
            return self.copy(3, block(1, 0, 0, 0), block(1, 0, 0, 0), at(0, 1))
        if i == 4:
            return self.copy(4, block(0, 1, 0, 1), block(0, 1, 0, 1), at(1, 0))
        spot = ((1, 0), (0, 1), (1, 1, 0, 0), (1, 1, 0, 1))[i - 5]
        return self.copy(i, block(*spot), block(*spot), at(0, 0, 1))

    def arrive(self, i):
        spot = (
            (1, 0),
            (0, 1),
            (0, 0, 1),
            (1, 1, 0, 0),
            (1, 1, 0, 1),
            (1, 0, 1),
            (0, 1, 1),
            (1, 1, 1, 0),
            (1, 1, 1, 1),
        )[i]
        here = self.block(*spot)
        self.copy(i, here, here, self.p.at(0, 0, 1)).wait_recv()

    def begin(self):
        for i in (0, 1, 2):
            self.outgoing(i).start()
        self.keep.begin()

    def forward(self):
        self.keep.turn()
        self.arrive(0)
        self.outgoing(3).start()
        self.arrive(1)
        self.outgoing(4).start()
        self.outgoing(5).start()
        self.outgoing(6).start()

    def share(self):
        self.arrive(3)
        self.outgoing(7).start()
        self.arrive(4)
        self.outgoing(8).start()

    def finish(self):
        for i in (2, 5, 6, 7, 8):
            self.arrive(i)
        for i in range(9):
            self.outgoing(i).wait_send()
        self.keep.finish()


class GatherLine:
    def __init__(self, place, dst, rows, begin, span, send, recv):
        self.p, self.dst, self.rows = place, dst, rows
        self.begin, self.span = begin, span
        self.send, self.recv = send, recv
        self.last = place.n_line - 1

    def block(self, owner):
        first = owner * self.rows + self.begin
        return self.dst.at[pl.ds(pl.multiple_of(first, 8), self.span)]

    def copy(self, way, k, owner, source=None):
        to = self.p.up() if way == 0 else self.p.down()
        block = self.block(owner)
        return remote(
            block if source is None else source,
            block,
            self.send.at[way, k],
            self.recv.at[way, k],
            to,
        )

    def step(self, k, source=None):
        t, last = self.p.t, self.last
        if k > 0:
            self.arrive(k - 1)

        @pl.when((t < last) & (t >= k))
        def _():
            self.copy(0, k, t - k, source).start()

        @pl.when((t > 0) & (t + k <= last))
        def _():
            self.copy(1, k, t + k, source).start()

    def arrive(self, k):
        t, last = self.p.t, self.last

        @pl.when(t >= k + 1)
        def _():
            self.copy(0, k, t - 1 - k).wait_recv()

        @pl.when(t + k + 1 <= last)
        def _():
            self.copy(1, k, t + 1 + k).wait_recv()

    def finish(self):
        t, last = self.p.t, self.last
        self.arrive(last - 1)
        for k in range(last):

            @pl.when((t < last) & (t >= k))
            def _():
                self.copy(0, k, t - k).wait_send()

            @pl.when((t > 0) & (t + k <= last))
            def _():
                self.copy(1, k, t + k).wait_send()


class ReduceLine:
    def __init__(self, place, terms, rows, begin, span, inbox, send, recv):
        self.p, self.terms, self.rows = place, terms, rows
        self.begin, self.span = begin, span
        self.inbox = inbox
        self.send, self.recv = send, recv
        self.last = place.n_line - 1

    def own(self, owner):
        first = owner * self.rows + self.begin
        return self.terms.at[pl.ds(pl.multiple_of(first, 16), self.span)]

    def copy(self, way, j, source):
        to = self.p.up() if way == 0 else self.p.down()
        return remote(
            source, self.inbox.at[way, j], self.send.at[way, j], self.recv.at[way, j], to
        )

    def ends(self):
        t, last = self.p.t, self.last

        @pl.when(t == 0)
        def _():
            for j in range(last):
                self.copy(0, j, self.own(last - j)).start()

        @pl.when(t == last)
        def _():
            for j in range(last):
                self.copy(1, j, self.own(j)).start()

    def sent(self):
        t, last = self.p.t, self.last

        @pl.when(t == 0)
        def _():
            for j in range(last):
                self.copy(0, j, self.own(last - j)).wait_send()

        @pl.when(t == last)
        def _():
            for j in range(last):
                self.copy(1, j, self.own(j)).wait_send()

    def hand_on(self, way, j):
        term = self.own(self.last - j if way == 0 else j)
        self.copy(way, j, term).wait_recv()
        self.inbox[way, j] = term[...] + self.inbox[way, j]
        self.copy(way, j, self.inbox.at[way, j]).start()

    def hop(self, k):
        t, last = self.p.t, self.last

        @pl.when(t == k + 1)
        def _():
            for j in range(last - 1 - k):
                self.hand_on(0, j)

        @pl.when(t == last - 1 - k)
        def _():
            for j in range(last - 1 - k):
                self.hand_on(1, j)

    def total(self, result):
        t, last = self.p.t, self.last
        result[...] = self.own(t)[...].astype(jnp.float32)

        @pl.when(t > 0)
        def _():
            j = last - t
            self.copy(0, j, self.inbox.at[0, 0]).wait_recv()
            result[...] += self.inbox[0, j].astype(jnp.float32)

        @pl.when(t < last)
        def _():
            self.copy(1, t, self.inbox.at[0, 0]).wait_recv()
            result[...] += self.inbox[1, t].astype(jnp.float32)

    def finish(self):
        t, last = self.p.t, self.last
        for j in range(last - 1):

            @pl.when((t > 0) & (t < last - j))
            def _():
                self.copy(0, j, self.inbox.at[0, j]).wait_send()

            @pl.when((t < last) & (t > j))
            def _():
                self.copy(1, j, self.inbox.at[1, j]).wait_send()


def add_rows(into, other, result=None):
    result = into if result is None else result

    def tile(i, carry):
        rows = pl.ds(pl.multiple_of(i * 16, 16), 16)
        result[rows] = into[rows] + other[rows]
        return carry

    lax.fori_loop(0, into.shape[0] // 16, tile, None)


class ReducePlane:
    chips = ((0, 0), (1, 0), (0, 1), (1, 1))

    def __init__(self, place, terms, scratch):
        self.p, self.terms = place, terms
        self.held, self.near, self.along, self.last, self.send, self.recv, self.local = scratch
        self.rows = self.held.shape[1]
        self.half = self.rows // 2

    @staticmethod
    def scratch(rows, width):
        return [
            pltpu.VMEM((4, rows, width), jnp.bfloat16),
            pltpu.VMEM((4, rows, width), jnp.bfloat16),
            pltpu.VMEM((4, rows // 2, width), jnp.bfloat16),
            pltpu.VMEM((2, rows // 2, width), jnp.bfloat16),
            pltpu.SemaphoreType.DMA((10,)),
            pltpu.SemaphoreType.DMA((10,)),
            pltpu.SemaphoreType.DMA((4,)),
        ]

    def block(self, k, other):
        first = self.p.chip(*self.chips[k], other) * self.rows
        return self.terms.at[pl.ds(pl.multiple_of(first, 16), self.rows)]

    def half_of(self, k, part):
        return self.held.at[k, pl.ds(part * self.half, self.half)]

    def load(self, k):
        return pltpu.make_async_copy(self.block(k, 0), self.held.at[k], self.local.at[k])

    def copy(self, i):
        at = self.p.at
        if i < 4:
            src, dst, to = self.block(i, 1), self.near.at[i], at(0, 0, 1)
        elif i < 8:
            src, to = (
                (self.half_of(1, 0), at(1, 0)),
                (self.half_of(3, 0), at(1, 0)),
                (self.half_of(2, 1), at(0, 1)),
                (self.half_of(3, 1), at(0, 1)),
            )[i - 4]
            dst = self.along.at[i - 4]
        else:
            src, to = ((self.half_of(2, 0), at(0, 1)), (self.half_of(1, 1), at(1, 0)))[i - 8]
            dst = self.last.at[i - 8]
        return remote(src, dst, self.send.at[i], self.recv.at[i], to)

    def begin(self):
        for k in (3, 1, 2, 0):
            self.copy(k).start()
            self.load(k).start()

    def cores(self):
        for k in (3, 1, 2, 0):
            self.load(k).wait()
            self.copy(k).wait_recv()
            add_rows(self.held.at[k], self.near.at[k])
            if k == 3:
                self.copy(5).start()
                self.copy(7).start()
            elif k == 1:
                self.copy(4).start()
            elif k == 2:
                self.copy(6).start()

    def turn(self):
        self.copy(5).wait_recv()
        add_rows(self.half_of(2, 0), self.along.at[1])
        self.copy(8).start()
        self.copy(7).wait_recv()
        add_rows(self.half_of(1, 1), self.along.at[3])
        self.copy(9).start()
        self.copy(4).wait_recv()
        add_rows(self.half_of(0, 0), self.along.at[0])
        self.copy(6).wait_recv()
        add_rows(self.half_of(0, 1), self.along.at[2])

    def finish(self, result):
        for part in (0, 1):
            self.copy(8 + part).wait_recv()
            rows = pl.ds(part * self.half, self.half)
            add_rows(self.half_of(0, part), self.last.at[part], result.at[rows])
        for i in range(10):
            self.copy(i).wait_send()


def dma_sems(*dims):
    return pltpu.SemaphoreType.DMA(dims)


def in_vmem():
    return pl.BlockSpec(memory_space=pltpu.VMEM)


def in_any():
    return pl.BlockSpec(memory_space=pl.ANY)


def comm_params(number):
    return pltpu.CompilerParams(
        collective_id=number, has_side_effects=True, vmem_limit_bytes=VMEM_BYTES
    )


def shaped(dims, kind):
    return jax.ShapeDtypeStruct(dims, kind)


def first_gather(n_dp, n_line, mats, rows_in, order):
    count = len(mats)
    parts = 2

    def kernel(*refs):
        srcs, (c, e) = refs[:count], refs[count : count + 2]
        dsts, (c_out, e_out) = refs[count + 2 : 2 * count + 2], refs[2 * count + 2 : 2 * count + 4]
        ps, pr, pl_sem, ls, lr, ll = refs[2 * count + 4 : 2 * count + 10]
        held = refs[2 * count + 10 :]
        place = Place(n_dp, n_line)
        place.meet()
        planes = [
            GatherPlane(place, a, b, ps.at[i], pr.at[i], pl_sem.at[i], held[i])
            for i, (a, b) in enumerate(zip(srcs, dsts))
        ]
        rows = c.shape[0]
        span = rows // parts
        lines = [
            GatherLine(place, c_out, rows, i * span, span, ls.at[i], lr.at[i])
            for i in range(parts)
        ]
        lines.append(
            GatherLine(place, e_out, e.shape[0], 0, e.shape[0], ls.at[parts], lr.at[parts])
        )
        for i in range(parts):
            lines[i].step(0, c.at[pl.ds(i * span, span)])
        lines[parts].step(0, e)
        early, late = planes[: count // 2], planes[count // 2 :]
        for part in early:
            part.begin()
        copies = []
        for i, (src, dst) in enumerate(((c, c_out), (e, e_out))):
            own = dst.at[pl.ds(pl.multiple_of(place.t * src.shape[0], 8), src.shape[0])]
            copies.append(Kept(src, own, held[count + i], ll.at[i]))
            copies[i].begin()
        for line in lines:
            line.step(1)
        for part in late:
            part.begin()
        for part in early:
            part.forward()
        for copy in copies:
            copy.turn()
        for line in lines:
            line.step(2)
        for part in early:
            part.share()
        for part in late:
            part.forward()
        for part in late:
            part.share()
        for part in lines + planes:
            part.finish()
        for copy in copies:
            copy.finish()

    return pl.pallas_call(
        kernel,
        out_shape=tuple(shaped((n_dp * m.shape[0], m.shape[1]), m.dtype) for m in mats)
        + (
            shaped((n_line * rows_in.shape[0], rows_in.shape[1]), rows_in.dtype),
            shaped((n_line * order.shape[0], order.shape[1]), order.dtype),
        ),
        in_specs=[in_any()] * (count + 2),
        out_specs=[in_any()] * (count + 2),
        scratch_shapes=[
            dma_sems(count, 9),
            dma_sems(count, 9),
            dma_sems(count, 2),
            dma_sems(parts + 1, 2, n_line - 1),
            dma_sems(parts + 1, 2, n_line - 1),
            dma_sems(2, 2),
        ]
        + [vmem_like(m) for m in (*mats, rows_in, order)],
        compiler_params=comm_params(1),
        name="first_gather",
    )(*mats, rows_in, order)


CHUNKS = 8
LAST_CHUNKS = 8


def line_scratch(n_line, span, width, chunks):
    hops = n_line - 1
    return [
        pltpu.VMEM((chunks, 2, hops, span, width), jnp.bfloat16),
        dma_sems(chunks, 2, hops),
        dma_sems(chunks, 2, hops),
        dma_sems(chunks, 2, hops),
        dma_sems(chunks, 2, hops),
        pltpu.VMEM((span, width), jnp.float32),
    ]


def sum_rows_and_spread(place, terms, scratch, finish_rows, spread, between):
    inbox, rs, rr, gs, gr, total = scratch
    span = total.shape[0]
    count = inbox.shape[0]
    rows = span * count
    hops = place.n_line - 1
    sums = [
        ReduceLine(place, terms, rows, c * span, span, inbox.at[c], rs.at[c], rr.at[c])
        for c in range(count)
    ]
    gathers = []
    if spread is not None:
        gathers = [
            GatherLine(place, spread, rows, c * span, span, gs.at[c], gr.at[c])
            for c in range(count)
        ]
    sums[0].ends()

    def total_of(c):
        sums[c].total(total)
        finish_rows(c, pl.ds(c * span, span), total)
        if gathers:
            gathers[c].step(0)

    stages = [lambda c, k=k: sums[c].hop(k) for k in range(hops - 1)] + [total_of]
    lags = [LAGS[min(k, len(LAGS) - 1)] for k in range(hops)]
    if gathers:
        stages += [lambda c, k=k: gathers[c].step(k) for k in range(1, hops)]
        lags += [lags[-1] + LAG_STEP * k for k in range(1, hops)]
    for i in range(count + lags[-1]):
        if i < count:
            sums[i].sent()
        if i + 1 < count:
            sums[i + 1].ends()
        for work, lag in zip(stages, lags):
            if 0 <= i - lag < count:
                work(i - lag)
        if i in between:
            between[i]()
    for part in gathers + sums:
        part.finish()


LAGS = (0, 1, 1)
LAG_STEP = 1


def middle_gather(n_dp, n_line, terms, tokens, gain, mats):
    rows, width = tokens.shape
    count = len(mats)

    def kernel(*refs):
        s, tok, gain_ref = refs[:3]
        srcs = refs[3 : 3 + count]
        after, hidden = refs[3 + count : 5 + count]
        dsts = refs[5 + count : 5 + 2 * count]
        ps, pr, pl_sem = refs[5 + 2 * count : 8 + 2 * count]
        held = refs[8 + 2 * count : 8 + 3 * count]
        scratch = refs[8 + 3 * count :]
        place = Place(n_dp, n_line)
        place.meet()
        planes = [
            GatherPlane(place, a, b, ps.at[i], pr.at[i], pl_sem.at[i], held[i])
            for i, (a, b) in enumerate(zip(srcs, dsts))
        ]
        planes[0].begin()

        def norm(c, here, total):
            values = tok[here].astype(jnp.float32) + total[...]
            after[here] = values
            low = rms_scale(values, gain_ref[...]).astype(jnp.bfloat16)
            first = pl.multiple_of(place.t * rows, 16) + c * total.shape[0]
            hidden[pl.ds(pl.multiple_of(first, 16), total.shape[0])] = low

        between = {6: planes[0].forward, 9: planes[0].share}
        sum_rows_and_spread(place, s, scratch, norm, hidden, between)
        for part in planes:
            part.finish()

    return pl.pallas_call(
        kernel,
        out_shape=(
            shaped((rows, width), jnp.float32),
            shaped((n_line * rows, width), jnp.bfloat16),
        )
        + tuple(shaped((n_dp * m.shape[0], m.shape[1]), m.dtype) for m in mats),
        in_specs=[in_vmem()] * 3 + [in_any()] * count,
        out_specs=[in_vmem()] * 2 + [in_any()] * count,
        scratch_shapes=[dma_sems(count, 9), dma_sems(count, 9), dma_sems(count, 2)]
        + [vmem_like(m) for m in mats]
        + line_scratch(n_line, rows // CHUNKS, width, CHUNKS),
        compiler_params=comm_params(2),
        name="middle_gather",
    )(terms, tokens, gain, *mats)


def middle_sums(
    n_dp, n_line, terms, after, gain, grad_in, grad_gate, hidden, grad_up, product, down
):
    rows, width = after.shape
    block = width // n_dp
    wide = grad_up.shape[1]
    spread_rows = n_line * rows

    def kernel(*refs):
        s, after_ref, gain_ref, g_ref, gg_far = refs[:5]
        hid_far, gu_far, pr_far, dw_far = refs[5:9]
        grad_after, gain_sum, spread, result, up_far, feed_far, gate_far = refs[9:16]
        hid, gu, pr, dw, gg, up_out, feed, sems = refs[16:24]
        rest = refs[24:]
        fetch = Fetch(
            [
                (hid_far, hid),
                (gu_far, gu),
                (pr_far, pr),
                (dw_far, dw),
                (feed, feed_far),
                (up_out.at[0], up_far.at[pl.ds(0, width // 2)]),
                (up_out.at[1], up_far.at[pl.ds(width // 2, width // 2)]),
                (gg_far, gg),
                (up_out.at[0], gate_far.at[pl.ds(0, width // 2)]),
                (up_out.at[1], gate_far.at[pl.ds(width // 2, width // 2)]),
            ],
            sems,
        )
        fetch.start(0, 7, 1, 2, 3)
        place = Place(n_dp, n_line)
        place.meet()
        plane = ReducePlane(place, gate_far, rest[:7])
        scratch = rest[7:]
        gain_sum[...] = jnp.zeros_like(gain_sum)

        def norm(c, here, total):
            grad = total[...]
            grad_rows, normed = norm_back(after_ref[here], gain_ref[...], grad)
            gain_sum[...] += jnp.sum(grad * normed, axis=0, keepdims=True)
            both = g_ref[here].astype(jnp.float32) + grad_rows
            grad_after[here] = both
            first = pl.multiple_of(place.t * rows, 16) + c * total.shape[0]
            spread[pl.ds(pl.multiple_of(first, 16), total.shape[0])] = both.astype(jnp.bfloat16)

        def feed_part(i):
            cols = pl.ds(i * (width // 4), width // 4)
            feed[:, cols] = times_trans(pr[...], dw[cols]).astype(jnp.bfloat16)

        def rows_part(right, i):
            cols = pl.ds(i * (width // 4), width // 4)
            here = pl.ds((i % 2) * (width // 4), width // 4)
            up_out[i // 2, here] = trans_times(hid[:, cols], right[...]).astype(jnp.bfloat16)

        def zero():
            fetch.wait(0, 7)
            rows_part(gg, 0)
            rows_part(gg, 1)
            fetch.start(8)

        def one():
            rows_part(gg, 2)
            rows_part(gg, 3)
            fetch.start(9)

        def two():
            fetch.wait(1, 8, 9)
            plane.begin()
            rows_part(gu, 0)

        def three():
            plane.cores()
            rows_part(gu, 1)
            fetch.start(5)

        def four():
            rows_part(gu, 2)

        def five():
            rows_part(gu, 3)
            fetch.start(6)
            fetch.wait(2, 3)

        def six():
            feed_part(0)

        def seven():
            plane.turn()
            feed_part(1)

        def eight():
            feed_part(2)

        def nine():
            feed_part(3)
            fetch.start(4)

        steps = dict(enumerate((zero, one, two, three, four, five, six, seven, eight, nine)))
        sum_rows_and_spread(place, s, scratch, norm, spread, steps)
        plane.finish(result)
        fetch.wait(4, 5, 6)

    low, full = jnp.bfloat16, jnp.float32
    near, far = in_vmem(), in_any()
    return pl.pallas_call(
        kernel,
        out_shape=(
            shaped((rows, width), full),
            shaped((1, width), full),
            shaped((spread_rows, width), low),
            shaped((block, wide), low),
            shaped((width, wide), low),
            shaped((spread_rows, width), low),
            shaped((width, wide), low),
        ),
        in_specs=[near] * 4 + [far] * 5,
        out_specs=[near] * 4 + [far] * 3,
        scratch_shapes=[vmem_like(m) for m in (hidden, grad_up, product, down, grad_gate)]
        + [
            pltpu.VMEM((2, width // 2, wide), low),
            pltpu.VMEM((spread_rows, width), low),
            dma_sems(10),
        ]
        + ReducePlane.scratch(block, wide)
        + line_scratch(n_line, rows // CHUNKS, width, CHUNKS),
        compiler_params=comm_params(3),
        name="middle_sums",
    )(terms, after, gain, grad_in, grad_gate, hidden, grad_up, product, down)


class Exchange:
    def __init__(self, place, axis, src, slots, send, recv, local):
        self.p, self.src, self.slots = place, src, slots
        self.over_dp = axis == "dp"
        self.size = place.n_dp if self.over_dp else place.n_line
        self.me = place.d if self.over_dp else place.t
        self.send, self.recv, self.local = send, recv, local

    def copy(self, i):
        to = lax.rem(self.me + i, self.size)
        device = (to, self.p.t) if self.over_dp else (self.p.d, to)
        return remote(
            self.src, self.slots.at[self.me], self.send.at[i - 1], self.recv.at[i - 1], device
        )

    def mine(self):
        return pltpu.make_async_copy(self.src, self.slots.at[self.me], self.local)

    def begin(self):
        for i in range(1, self.size):
            self.copy(i).start()
        self.mine().start()

    def wait(self):
        self.mine().wait()
        for i in range(1, self.size):
            self.copy(i).wait()

    def finish(self):
        self.wait()
        total = self.slots[0]
        for i in range(1, self.size):
            total = total + self.slots[i]
        return total


def last_sums(n_dp, n_line, terms, tokens, gain, grad_after, small, mats):
    rows, width = tokens.shape
    count = len(mats)
    per = len(ReducePlane.scratch(16, 128))

    def kernel(*refs):
        s, tok, gain_ref, g_ref, small_ref = refs[:5]
        srcs = refs[5 : 5 + count]
        grad_tok, small_out, first_out = refs[5 + count : 8 + count]
        results = refs[8 + count : 8 + 2 * count]
        rest = refs[8 + 2 * count :]
        own_first, row_sum = rest[count * per : count * per + 2]
        slots_a, slots_b, slots_c, slots_d = rest[count * per + 2 : count * per + 6]
        xs, xr, xl = rest[count * per + 6 : count * per + 9]
        scratch = rest[count * per + 9 :]
        place = Place(n_dp, n_line)
        place.meet(True)
        planes = [
            ReducePlane(place, srcs[i], rest[i * per : (i + 1) * per]) for i in range(count)
        ]
        for part in planes:
            part.begin()
        early = Exchange(place, "dp", small_ref, slots_a, xs.at[0], xr.at[0], xl.at[0])
        early.begin()
        own_first[...] = jnp.zeros_like(own_first)

        def norm(c, here, total):
            grad = total[...]
            grad_rows, normed = norm_back(tok[here].astype(jnp.float32), gain_ref[...], grad)
            own_first[...] += jnp.sum(grad * normed, axis=0, keepdims=True)
            grad_tok[here] = g_ref[here] + grad_rows

        def cores():
            for part in planes:
                part.cores()

        def turn():
            for part in planes:
                part.turn()

        sum_rows_and_spread(place, s, scratch, norm, None, {0: cores, 5: turn})
        first = Exchange(place, "dp", own_first, slots_b, xs.at[1], xr.at[1], xl.at[1])
        first.begin()
        small_out[...] = early.finish()
        row_sum[0:1] = small_out[0:1]
        row_sum[1:2] = first.finish()
        both = Exchange(place, "tensor", row_sum, slots_c, xs.at[2], xr.at[2], xl.at[2])
        both.begin()
        for part, result in zip(planes, results):
            part.finish(result)
        first_out[...] = both.finish()

    return pl.pallas_call(
        kernel,
        out_shape=(
            shaped((rows, width), jnp.float32),
            shaped(small.shape, jnp.float32),
            shaped((2, width), jnp.float32),
        )
        + tuple(shaped((m.shape[0] // n_dp, m.shape[1]), jnp.bfloat16) for m in mats),
        in_specs=[in_vmem()] * 5 + [in_any()] * count,
        out_specs=[in_vmem()] * (3 + count),
        scratch_shapes=sum([ReducePlane.scratch(m.shape[0] // n_dp, m.shape[1]) for m in mats], [])
        + [
            pltpu.VMEM((1, width), jnp.float32),
            pltpu.VMEM((2, width), jnp.float32),
            pltpu.VMEM((n_dp,) + small.shape, jnp.float32),
            pltpu.VMEM((n_dp, 1, width), jnp.float32),
            pltpu.VMEM((n_line, 2, width), jnp.float32),
            pltpu.VMEM((1, width), jnp.float32),
            dma_sems(3, n_dp),
            dma_sems(3, n_dp),
            dma_sems(3),
        ]
        + line_scratch(n_line, rows // LAST_CHUNKS, width, LAST_CHUNKS),
        compiler_params=comm_params(4),
        name="last_sums",
    )(terms, tokens, gain, grad_after, small, *mats)


def loop(count, body, unroll=1):
    def step(i, carry):
        body(i)
        return carry

    lax.fori_loop(0, count, step, None, unroll=unroll)


def tile_rows(i, size, ahead=0):
    return pl.ds(pl.multiple_of(i * size + ahead, 8), size)


def moved_up(values, distance, count):
    size = values.shape[0]
    return pltpu.roll(values, (size - distance) % size, 0)[:count]


def take_lanes(ref, here):
    return jnp.concatenate([ref[c, here] for c in range(ref.shape[0])], axis=1)


def put_lanes(ref, here, values):
    for c in range(ref.shape[0]):
        ref[c, here] = values[:, c * LANES : (c + 1) * LANES]


def gelu_parts(values):
    inner = GELU_C * (values + 0.044715 * (values * values * values))
    tanh = jnp.tanh(inner)
    half = 0.5 * (1.0 + tanh)
    slope = half + 0.5 * values * (1.0 - tanh * tanh) * GELU_C * (
        1.0 + 3.0 * 0.044715 * (values * values)
    )
    return values * half, slope


GELU_C = 0.7978845608028654
RIM = 128
LANES = 128
TILE = 16


def one_minus_exp(values, exponential):
    series = jnp.ones_like(values)
    for term in range(9, 1, -1):
        series = 1.0 + values * (1.0 / term) * series
    return jnp.where(values > -0.35, -values * series, 1.0 - exponential)


def rate_and_scale(pre_recur, soft, start):
    sr = jax.nn.sigmoid(pre_recur)
    log_rate = -rate_scale * sr * soft
    decay = jnp.exp(log_rate)
    rate = jnp.where(start, 0.0, decay)
    scale = jnp.where(start, 1.0, jnp.sqrt(one_minus_exp(2.0 * log_rate, decay * decay)))
    return sr, rate, scale


class RimSwap:
    def __init__(self, place, own):
        self.odd = lax.rem(place.t, 2)
        self.partner = (place.d, place.t + 1 - 2 * self.odd)
        self.first = pl.multiple_of(RIM - RIM * self.odd, RIM)
        self.edge = pl.ds(pl.multiple_of((1 - self.odd) * own + self.odd * RIM, RIM), RIM)
        self.over_there = pl.ds(pl.multiple_of(self.odd * (own + RIM), RIM), RIM)
        self.beyond = pl.ds(pl.multiple_of((1 - self.odd) * (own + RIM), RIM), RIM)

    def block(self, index, size):
        return pl.ds(pl.multiple_of(self.first + index * size, RIM), size)


LATE_SHARE = 4


def recur_forward(
    n_dp,
    n_line,
    tok_all,
    cot,
    to_place,
    to_stored,
    x_full,
    y_full,
    out_full,
    gain,
    gates,
    taps,
    soft,
    flags,
):
    rows, width = tok_all.shape
    count, own = taps.shape
    size = gates.shape[0]
    wide = own + 2 * RIM
    blocks = (wide - RIM) // size
    chunk = rows // 8
    cot_rows = cot.shape[0] - cot.shape[0] // LATE_SHARE
    parts = 1

    def kernel(*refs):
        (tok_far, cot_ref, plc, sto, wx_far, wy_far, wo_far, gain_ref, gw, cw, sp, fl) = refs[:12]
        far, cot_all = refs[12:23], refs[23]
        tok, wx, wy, wo = refs[24:28]
        results = refs[28:39]
        hp, xext, y, conv_low, conv, pre_r, pre_i, rate, state, merged_st, terms = results
        (h, xf, local, cum, merged, agg, slots, hs, hr, es, er, el, gs, gr, gl) = refs[39:54]
        in_sems, out_sems, cot_held = refs[54:]
        fetch = Fetch(((tok_far, tok), (wx_far, wx), (wy_far, wy), (wo_far, wo)), in_sems)
        store = Fetch(zip(results, far), out_sems)
        fetch.start(0, 1, 2, 3)
        place = Place(n_dp, n_line)
        place.meet(True)
        swap = RimSwap(place, own)
        own_cot = cot_all.at[pl.ds(pl.multiple_of(place.t * cot_rows, 16), cot_rows)]
        cot_ref = cot_ref.at[pl.ds(0, cot_rows)]
        keep = Kept(cot_ref, own_cot, cot_held, gl)
        keep.begin()
        span = cot_rows // parts
        lines = [
            GatherLine(place, cot_all, cot_rows, c * span, span, gs.at[c], gr.at[c])
            for c in range(parts)
        ]
        for c, line in enumerate(lines):
            line.step(0, cot_ref.at[pl.ds(c * span, span)])

        def norm(i):
            here = tile_rows(i, TILE)
            h[here] = rms_scale(tok[here].astype(jnp.float32), gain_ref[...]).astype(jnp.bfloat16)

        fetch.wait(0)
        loop(rows // TILE, norm)
        fetch.wait(1)

        def project(i):
            here = tile_rows(i, 128)
            hp[here] = plain_dot(plc[here], h[...]).astype(jnp.bfloat16)
            xext[tile_rows(i, 128, 16)] = plain_dot(hp[here], wx[...]).astype(jnp.bfloat16)

        loop(rows // 128, project)
        store.start(0)
        edge = remote(
            xext.at[pl.ds(rows, 16)],
            xext.at[pl.ds(0, 16)],
            hs.at[0],
            hr.at[0],
            (lax.rem(place.d + 1, n_dp), place.t),
        )
        edge.start()
        keep.turn()
        for line in lines:
            line.step(1)

        def project_y(i):
            here = tile_rows(i, 128)
            y[here] = plain_dot(hp[here], wy[...])

        fetch.wait(2)
        loop(rows // 128, project_y)
        store.start(2)
        edge.wait()
        top = xext[pl.ds(0, 16)]
        xext[pl.ds(0, 16)] = jnp.where(place.d > 0, top, jnp.zeros_like(top))
        store.start(1)

        def widen(i):
            xf[tile_rows(i, TILE)] = xext[tile_rows(i, TILE)].astype(jnp.float32)

        loop(rows // TILE + 1, widen)

        def convolve(i):
            here = tile_rows(i, TILE)
            near = xf[pl.ds(pl.multiple_of(i * TILE + 8, 8), TILE + 8)]
            same = fl[tile_rows(i, TILE, 8)]
            total = cw[0:1] * near[8:]
            for k in range(1, count):
                total += cw[k : k + 1] * moved_up(near, 8 - k, TILE) * same[:, k : k + 1]
            conv[here] = total
            conv_low[here, RIM : RIM + own] = total.astype(jnp.bfloat16)

        loop(rows // TILE, convolve)
        store.start(4)
        rim = remote(
            conv_low.at[:, swap.edge],
            conv_low.at[:, swap.over_there],
            hs.at[1],
            hr.at[1],
            swap.partner,
        )
        rim.start()
        for i in range(blocks):
            index = lax.rem(i + swap.odd, blocks)
            cols = swap.block(index, size)
            other = pl.ds(pl.multiple_of(wide + swap.first + index * size, RIM), size)
            if i == blocks - 1:
                rim.wait()
            pre_r[:, cols] = plain_dot(conv_low[:, cols], gw[:, cols])
            pre_i[:, cols] = plain_dot(conv_low[:, cols], gw[:, other])

        store.start(3, 5, 6)

        def drive(i):
            here = tile_rows(i, TILE)
            start = fl[tile_rows(i, TILE, 8)][:, 0:1] > 0.0
            own_cols = pl.ds(RIM, own)
            _, decay, scale = rate_and_scale(pre_r[here, own_cols], sp[...], start)
            put_lanes(rate, here, decay)
            put_lanes(local, here, conv[here] * jax.nn.sigmoid(pre_i[here, own_cols]) * scale)

        loop(rows // TILE, drive)
        store.start(7)
        for line in lines:
            line.step(2)
        groups = own // LANES

        def scan(i, carry):
            here = pl.ds(i, 8, chunk)
            result = []
            for c in range(groups):
                product, total = carry[c]
                r = rate[c, here]
                product = product * r
                total = total * r + local[c, here]
                cum[c, here] = product
                local[c, here] = total
                result.append((product, total))
            return tuple(result)

        blank = (jnp.ones((8, LANES), jnp.float32), jnp.zeros((8, LANES), jnp.float32))
        lax.fori_loop(0, chunk, scan, (blank,) * groups)
        product, total = jnp.ones((1, own), jnp.float32), jnp.zeros((1, own), jnp.float32)
        for j in range(8):
            last = pl.ds(j * chunk + chunk - 1, 1)
            total = take_lanes(local, last) + take_lanes(cum, last) * total
            product = product * take_lanes(cum, last)
        agg[0:1] = product
        agg[1:2] = total
        swap_all = Exchange(place, "dp", agg, slots, es, er, el)
        swap_all.begin()
        swap_all.wait()
        entry = jnp.zeros((1, own), jnp.float32)
        for q in range(n_dp):
            longer = slots[q, 1:2] + slots[q, 0:1] * entry
            entry = jnp.where(q < place.d, longer, entry)
        state[pl.ds(0, 8)] = jnp.broadcast_to(entry, (8, own))
        for j in range(8):

            def settle(i, entry=entry):
                here = tile_rows(i, TILE, j * chunk)
                values = take_lanes(local, here) + take_lanes(cum, here) * entry
                state[tile_rows(i, TILE, j * chunk + 8)] = values
                merged[here] = (values * gelu_parts(y[here])[0]).astype(jnp.bfloat16)

            loop(chunk // TILE, settle)
            last = pl.ds(j * chunk + chunk - 1, 1)
            entry = take_lanes(local, last) + take_lanes(cum, last) * entry
        store.start(8)
        merged_st[...] = plain_dot(sto[...], merged[...]).astype(jnp.bfloat16)

        store.start(9)
        fetch.wait(3)

        def mix(i):
            some = tile_rows(i, 512)
            terms[:, pl.ds(pl.multiple_of(i * 512, 512), 512)] = times_trans(
                merged_st[...], wo[some, :]
            ).astype(jnp.bfloat16)

        loop(width // 512, mix)
        for line in lines:
            line.finish()
        keep.finish()
        store.start(10)
        store.wait(*range(11))

    low, full = jnp.bfloat16, jnp.float32
    results = (
        shaped((rows, width), low),
        shaped((rows + 16, own), low),
        shaped((rows, own), full),
        shaped((rows, wide), low),
        shaped((rows, own), full),
        shaped((rows, wide), full),
        shaped((rows, wide), full),
        shaped((own // LANES, rows, LANES), full),
        shaped((rows + 8, own), full),
        shaped((rows, own), low),
        shaped((rows, width), low),
    )
    near, far = in_vmem(), in_any()
    return pl.pallas_call(
        kernel,
        out_shape=results + (shaped((n_line * cot_rows, width), low),),
        in_specs=[far, far, near, near, far, far, far] + [near] * 5,
        out_specs=[far] * 12,
        scratch_shapes=[vmem_like(m) for m in (tok_all, x_full, y_full, out_full) + results]
        + [
            pltpu.VMEM((rows, width), low),
            pltpu.VMEM((rows + 16, own), full),
            pltpu.VMEM((own // LANES, rows, LANES), full),
            pltpu.VMEM((own // LANES, rows, LANES), full),
            pltpu.VMEM((rows, own), low),
            pltpu.VMEM((2, own), full),
            pltpu.VMEM((n_dp, 2, own), full),
            dma_sems(2),
            dma_sems(2),
            dma_sems(n_dp),
            dma_sems(n_dp),
            pltpu.SemaphoreType.DMA,
            dma_sems(parts, 2, n_line - 1),
            dma_sems(parts, 2, n_line - 1),
            dma_sems(2),
            dma_sems(4),
            dma_sems(11),
            pltpu.VMEM((cot_rows, width), low),
        ],
        compiler_params=comm_params(5),
        name="recur_forward",
    )(
        tok_all,
        cot,
        to_place,
        to_stored,
        x_full,
        y_full,
        out_full,
        gain,
        gates,
        taps,
        soft,
        flags,
    )


class RowProducts:
    def __init__(self, left, right, far, stage, sems):
        self.left, self.right, self.far, self.stage, self.sems = left, right, far, stage, sems
        self.part = stage.shape[1]
        self.count = far.shape[0] // self.part

    def slot(self, i):
        return self.stage.at[i % 2, :, pl.ds(0, self.far.shape[1])]

    def copy(self, i):
        some = pl.ds(i * self.part, self.part)
        return pltpu.make_async_copy(self.slot(i), self.far.at[some], self.sems.at[i])

    def run(self):
        for i in range(self.count):
            if i >= 2:
                self.copy(i - 2).wait()
            some = pl.ds(i * self.part, self.part)
            self.slot(i)[...] = trans_times(self.left[:, some], self.right[...]).astype(
                jnp.bfloat16
            )
            self.copy(i).start()

    def finish(self):
        self.copy(self.count - 2).wait()
        self.copy(self.count - 1).wait()


def recur_backward(
    n_dp,
    n_line,
    mixer_in,
    to_place,
    to_stored,
    x_full,
    y_full,
    out_full,
    gates,
    taps,
    soft,
    slope,
    flags,
    kept,
    weight_terms,
    row_terms,
    hidden_place,
    merged_stored,
):
    rows, width = mixer_in.shape
    count, own = taps.shape
    size = gates.shape[0]
    wide = own + 2 * RIM
    blocks = (wide - RIM) // size
    chunk = rows // 8
    own_rows = rows // n_line
    parts = 4
    span = own_rows // parts

    def kernel(*refs):
        (mix_far, plc, sto, wx_far, wy_far, wo_far, gw, cw, sp, sg, fl) = refs[:11]
        kept_far, weights, feed_far, hp_far, merged_far = refs[11:19], *refs[19:23]
        (gate_grads, tap_grads, decay_grad, terms_far, weight_sum, row_sum) = refs[23:29]
        out_far, xy_far = refs[29:31]
        mix, wy, wo, feed, merged = refs[31:36]
        (xext, y, conv_low, conv, pre_r, pre_i, rate, state) = refs[36:44]
        (gxy, mp, gm, lam, reach, gp_r, gp_i, grad, spread, rim_out, rim_in) = refs[44:55]
        (ret_out, ret_in, tap_sums, decay_sums, ends, agg, slots) = refs[55:62]
        (hs, hr, es, er, el, in_sems, out_sems, inbox, ls, lr, total) = refs[62:73]
        stage, stage_sems = refs[73:75]
        hp, terms, wx = mix, mix, wo
        fetch = Fetch(
            [
                (mix_far, mix),
                (wo_far, wo),
                (kept_far[1], y),
                (kept_far[7], state),
                (kept_far[6], rate),
                (kept_far[4], pre_r),
                (kept_far[5], pre_i),
                (kept_far[3], conv),
                (kept_far[2], conv_low),
                (kept_far[0], xext),
                (wx_far, wx),
                (wy_far, wy),
                (feed_far, feed),
                (merged_far, merged),
                (hp_far, hp),
            ],
            in_sems,
        )
        fetch.start(12, 0, 1, 13)
        store = Fetch(((terms, terms_far),), out_sems)
        out_rows = RowProducts(mix, merged, out_far, stage, stage_sems.at[0])
        xy_rows = RowProducts(hp, gxy, xy_far, stage, stage_sems.at[1])
        place = Place(n_dp, n_line)
        place.meet(True)
        plane = ReducePlane(place, weights, refs[75:])
        plane.begin()
        lines = [
            ReduceLine(place, feed, own_rows, c * span, span, inbox.at[c], ls.at[c], lr.at[c])
            for c in range(parts)
        ]

        def send(c):
            if c > 0:
                lines[c - 1].sent()
            if c < parts:
                lines[c].ends()

        def add_up(c):
            lines[c].total(total)
            row_sum[pl.ds(c * span, span)] = total[...].astype(jnp.bfloat16)

        fetch.wait(12)
        send(0)
        fetch.start(*range(2, 10), 11)
        swap = RimSwap(place, own)
        own_cols = pl.ds(RIM, own)

        def project(i):
            here = tile_rows(i, 128)
            mp[here] = plain_dot(plc[here], mix[...]).astype(jnp.bfloat16)
            gm[here] = plain_dot(mp[here], wo[...])

        fetch.wait(0, 1)
        loop(rows // 128, project)
        fetch.start(10)
        fetch.wait(13)
        out_rows.run()
        fetch.start(14)

        def split(i):
            here = tile_rows(i, TILE)
            branch, slope_y = gelu_parts(y[here])
            grads = gm[here]
            put_lanes(lam, here, grads * branch)
            values = state[tile_rows(i, TILE, 8)]
            gxy[here, own:] = (grads * values * slope_y).astype(jnp.bfloat16)

        fetch.wait(2, 3)
        loop(rows // TILE, split)
        send(1)
        lines[0].hop(0)
        fetch.wait(4)
        groups = own // LANES

        def scan(i, carry):
            here = pl.ds(chunk - 1 - i, 8, chunk)
            result = []
            for c in range(groups):
                product, message = carry[c]
                r = rate[c, here]
                value = lam[c, here] + message
                lam[c, here] = value
                reach[c, here] = product
                result.append((product * r, value * r))
            return tuple(result)

        blank = (jnp.ones((8, LANES), jnp.float32), jnp.zeros((8, LANES), jnp.float32))
        done = lax.fori_loop(0, chunk, scan, (blank,) * groups)
        for c in range(groups):
            lanes = pl.ds(c * LANES, LANES)
            ends[0, :, lanes] = done[c][0]
            ends[1, :, lanes] = done[c][1]
        product, message = jnp.ones((1, own), jnp.float32), jnp.zeros((1, own), jnp.float32)
        for j in reversed(range(8)):
            message = ends[1, j : j + 1] + ends[0, j : j + 1] * message
            product = product * ends[0, j : j + 1]
        agg[0:1] = product
        agg[1:2] = message
        swap_all = Exchange(place, "dp", agg, slots, es, er, el)
        swap_all.begin()
        plane.cores()
        swap_all.wait()
        lines[0].hop(1)
        entry = jnp.zeros((1, own), jnp.float32)
        for q in reversed(range(n_dp)):
            longer = slots[q, 1:2] + slots[q, 0:1] * entry
            entry = jnp.where(q > place.d, longer, entry)
        fetch.wait(5, 6, 7)
        for ref in (tap_sums, decay_sums):
            ref[...] = jnp.zeros_like(ref)
        for ref in (gp_r, gp_i):
            ref[:, 0:RIM] = jnp.zeros((rows, RIM), jnp.bfloat16)
            ref[:, RIM + own :] = jnp.zeros((rows, RIM), jnp.bfloat16)
        grad[pl.ds(0, 8)] = jnp.zeros((8, own), jnp.float32)
        grad[pl.ds(rows + 8, 8)] = jnp.zeros((8, own), jnp.float32)
        for j in reversed(range(8)):

            def back(i, entry=entry):
                here = tile_rows(i, TILE, j * chunk)
                flag = fl[tile_rows(i, TILE, j * chunk + 8)]
                start = flag[:, 0:1] > 0.0
                values = take_lanes(lam, here) + take_lanes(reach, here) * entry
                before = moved_up(
                    state[pl.ds(pl.multiple_of(j * chunk + i * TILE, 8), TILE + 8)], 7, TILE
                )
                sr, decay, scale = rate_and_scale(pre_r[here, own_cols], sp[...], start)
                si = jax.nn.sigmoid(pre_i[here, own_cols])
                block = conv[here]
                driven = values * si
                log_grad = values * before * decay - block * driven * (decay * decay) / scale
                log_grad = jnp.where(start, 0.0, log_grad)
                inner = sr * log_grad
                gp_r[here, own_cols] = (
                    -rate_scale * sp[...] * inner * (1.0 - sr)
                ).astype(jnp.bfloat16)
                gp_i[here, own_cols] = (driven * block * (1.0 - si) * scale).astype(jnp.bfloat16)
                grad[tile_rows(i, TILE, j * chunk + 8)] = driven * scale
                decay_sums[...] += inner[:8] + inner[8:]

            loop(chunk // TILE, back)
            if j == 4:
                send(2)
                lines[1].hop(0)
            entry = ends[1, j : j + 1] + ends[0, j : j + 1] * entry
        lines[1].hop(1)
        add_up(0)
        decay_grad[...] = rate_scale * sg[...] * jnp.sum(decay_sums[...], axis=0, keepdims=True)

        for i in range(blocks):
            index = lax.rem(i + 2 - 2 * swap.odd, blocks)
            cols = swap.block(index, size)
            other = pl.ds(pl.multiple_of(wide + swap.first + index * size, RIM), size)
            spread[:, cols] = times_trans(gp_r[:, cols], gw[:, cols]) + times_trans(
                gp_i[:, cols], gw[:, other]
            )
            if i == 0:
                rim_out[...] = spread[:, swap.beyond].astype(jnp.bfloat16)
                rim = remote(rim_out, rim_in, hs.at[0], hr.at[0], swap.partner)
                rim.start()
        send(3)
        lines[2].hop(0)
        rim.wait()
        shared = pl.ds(pl.multiple_of((1 - swap.odd) * (own - RIM), RIM), RIM)

        def join(i):
            here = tile_rows(i, TILE)
            there = tile_rows(i, TILE, 8)
            grad[there] += spread[here, own_cols]
            grad[there, shared] += rim_in[here].astype(jnp.float32)

        loop(rows // TILE, join)

        near = grad[pl.ds(0, 16)]
        back_rows = jnp.zeros((8, own), jnp.float32)
        for k in range(1, count):
            masked = near * fl[pl.ds(0, 16)][:, k : k + 1]
            back_rows += cw[k : k + 1] * moved_up(masked, k, 8)
        ret_out[...] = back_rows
        ret = remote(
            ret_out,
            ret_in,
            hs.at[1],
            hr.at[1],
            (lax.rem(place.d + n_dp - 1, n_dp), place.t),
        )
        ret.start()
        fetch.wait(8)
        for i in range(blocks):
            cols = swap.block(i, size)
            spread[0:size, cols] = trans_times(conv_low[:, cols], gp_r[:, cols])
            spread[size : 2 * size, cols] = trans_times(conv_low[:, cols], gp_i[:, cols])
        gate_grads[:, 0:own] = spread[0:size, own_cols].astype(jnp.bfloat16)
        gate_grads[:, own:] = spread[size : 2 * size, own_cols].astype(jnp.bfloat16)

        def taps_back(i, added=None):
            here = tile_rows(i, TILE)
            start = pl.ds(pl.multiple_of(i * TILE + 8, 8), TILE + 8)
            after = grad[start]
            flag = fl[start]
            behind = xext[pl.ds(pl.multiple_of(i * TILE, 16), 2 * TILE)].astype(jnp.float32)
            total = cw[0:1] * after[:TILE]
            for k in range(count):
                if k > 0:
                    masked = after * flag[:, k : k + 1]
                    total += cw[k : k + 1] * moved_up(masked, k, TILE)
                    mine = masked[:TILE]
                else:
                    mine = after[:TILE]
                term = mine * moved_up(behind, 16 - k, TILE)
                tap_sums[k] += term[:8] + term[8:]
            if added is not None:
                total = total + jnp.concatenate([jnp.zeros((8, own), jnp.float32), added], axis=0)
            gxy[here, 0:own] = total.astype(jnp.bfloat16)

        fetch.wait(9)
        loop(rows // TILE - 1, taps_back)
        lines[2].hop(1)
        add_up(1)
        ret.wait()
        taps_back(rows // TILE - 1, jnp.where(place.d < n_dp - 1, ret_in[...], 0.0))
        tap_grads[...] = jnp.zeros_like(tap_grads)
        for k in range(count):
            tap_grads[k : k + 1] = jnp.sum(tap_sums[k], axis=0, keepdims=True)

        fetch.wait(14)
        out_rows.finish()
        plane.turn()
        xy_rows.run()
        send(4)
        lines[3].hop(0)

        def restore(i):
            here = tile_rows(i, 128)
            mp[here, 0 : 2 * own] = plain_dot(sto[here], gxy[...]).astype(jnp.bfloat16)

        loop(rows // 128, restore)

        def spread_back(i):
            some = tile_rows(i, 512)
            terms[:, pl.ds(pl.multiple_of(i * 512, 512), 512)] = (
                times_trans(mp[:, 0:own], wx[some]) + times_trans(mp[:, own : 2 * own], wy[some])
            ).astype(jnp.bfloat16)

        fetch.wait(10, 11)
        loop(width // 512, spread_back)
        store.start(0)
        lines[3].hop(1)
        add_up(2)
        plane.finish(weight_sum)
        add_up(3)
        for line in lines:
            line.finish()
        xy_rows.finish()
        store.wait(0)

    low, full = jnp.bfloat16, jnp.float32
    block = weight_terms.shape[0] // n_dp
    near, far = in_vmem(), in_any()
    return pl.pallas_call(
        kernel,
        out_shape=(
            shaped((size, 2 * own), low),
            shaped((8, own), full),
            shaped((1, own), full),
            shaped((rows, width), low),
            shaped((block, weight_terms.shape[1]), low),
            shaped((own_rows, width), low),
            shaped((width, own), low),
            shaped((width, 2 * own), low),
        ),
        in_specs=[far, near, near, far, far, far] + [near] * 5 + [far] * 12,
        out_specs=[near, near, near, far, near, near, far, far],
        scratch_shapes=[
            vmem_like(m) for m in (mixer_in, y_full, out_full, row_terms, merged_stored, *kept)
        ]
        + [
            pltpu.VMEM((rows, 2 * own), low),
            pltpu.VMEM((rows, width), low),
            pltpu.VMEM((rows, own), full),
            pltpu.VMEM((own // LANES, rows, LANES), full),
            pltpu.VMEM((own // LANES, rows, LANES), full),
            pltpu.VMEM((rows, wide), low),
            pltpu.VMEM((rows, wide), low),
            pltpu.VMEM((rows + 16, own), full),
            pltpu.VMEM((rows, wide), full),
            pltpu.VMEM((rows, RIM), low),
            pltpu.VMEM((rows, RIM), low),
            pltpu.VMEM((8, own), full),
            pltpu.VMEM((8, own), full),
            pltpu.VMEM((count, 8, own), full),
            pltpu.VMEM((8, own), full),
            pltpu.VMEM((2, 8, own), full),
            pltpu.VMEM((2, own), full),
            pltpu.VMEM((n_dp, 2, own), full),
            dma_sems(2),
            dma_sems(2),
            dma_sems(n_dp),
            dma_sems(n_dp),
            pltpu.SemaphoreType.DMA,
            dma_sems(15),
            dma_sems(1),
            pltpu.VMEM((parts, 2, n_line - 1, span, width), low),
            dma_sems(parts, 2, n_line - 1),
            dma_sems(parts, 2, n_line - 1),
            pltpu.VMEM((span, width), full),
            pltpu.VMEM((2, width // 5, 2 * own), low),
            dma_sems(2, 5),
        ]
        + ReducePlane.scratch(block, weight_terms.shape[1]),
        compiler_params=comm_params(6),
        name="recur_backward",
    )(
        mixer_in,
        to_place,
        to_stored,
        x_full,
        y_full,
        out_full,
        gates,
        taps,
        soft,
        slope,
        flags,
        *kept,
        weight_terms,
        row_terms,
        hidden_place,
        merged_stored,
    )


def column_parts(width, size=768):
    return [(c, min(size, width - c)) for c in range(0, width, size)]


def feed_forward(n_dp, n_line, hidden, gate, up, down, grads, grad_own):
    rows, width = hidden.shape
    units = gate.shape[1]
    own_rows = grad_own.shape[0]
    ready = grads.shape[0] // n_line
    late = own_rows - ready
    part = width // 4

    def kernel(*refs):
        hid_far, wg_far, wu_far, wd_far, grads_far, own_far = refs[:6]
        product_far, gup_far, back_far, gdown_far, gg_far = refs[6:11]
        hid, wg, wu, wd, grad, slope, branch, product, ggate, gup, stage, back = refs[11:23]
        in_sems, out_sems, stage_sems, ls, lr = refs[23:]
        place = Place(n_dp, n_line)
        pairs = [(hid_far, hid), (wg_far, wg), (wu_far, wu), (wd_far, wd)]
        pairs += [
            (grads_far.at[pl.ds(q * ready, ready)], grad.at[pl.ds(q * own_rows, ready)])
            for q in range(n_line)
        ]
        mine = pl.ds(pl.multiple_of(place.t * own_rows + ready, 16), late)
        pairs.append((own_far.at[pl.ds(ready, late)], grad.at[mine]))
        fetch = Fetch(pairs, in_sems)
        fetch.start(*range(len(pairs)))
        store = Fetch(
            ((product, product_far), (gup, gup_far), (back, back_far), (ggate, gg_far)), out_sems
        )
        place.meet()
        line = GatherLine(place, grad, own_rows, ready, late, ls, lr)
        line.step(0, own_far.at[pl.ds(ready, late)])
        columns = column_parts(units)
        fetch.wait(0, 1)
        for c, size in columns:
            cols = pl.ds(c, size)

            def gates(i, cols=cols):
                here = tile_rows(i, 256)
                branch[here, cols] = plain_dot(hid[here], wg[:, cols])

            loop(rows // 256, gates)
        line.step(1)
        fetch.wait(2)
        for c, size in columns:
            cols = pl.ds(c, size)

            def ups(i, cols=cols):
                here = tile_rows(i, 256)
                value = plain_dot(hid[here], wu[:, cols])
                active, bend = gelu_parts(branch[here, cols])
                product[here, cols] = (active * value).astype(jnp.bfloat16)
                branch[here, cols] = active
                slope[here, cols] = bend * value

            loop(rows // 256, ups)
        store.start(0)
        line.step(2)
        fetch.wait(*range(4, len(pairs)))
        line.finish()

        down_rows = RowProducts(grad, product, gdown_far, stage, stage_sems)
        down_rows.run()
        fetch.wait(3)
        for c, size in columns:
            cols = pl.ds(c, size)

            def backs(i, cols=cols):
                here = tile_rows(i, 256)
                value = plain_dot(grad[here], wd[:, cols])
                ggate[here, cols] = (value * slope[here, cols]).astype(jnp.bfloat16)
                gup[here, cols] = (value * branch[here, cols]).astype(jnp.bfloat16)

            loop(rows // 256, backs)
        store.start(1, 3)
        for i in range(4):
            some = pl.ds(i * part, part)
            back[:, some] = (
                times_trans(ggate[...], wg[some]) + times_trans(gup[...], wu[some])
            ).astype(jnp.bfloat16)
        store.start(2)
        down_rows.finish()
        store.wait(0, 1, 2, 3)

    low, full = jnp.bfloat16, jnp.float32
    return pl.pallas_call(
        kernel,
        out_shape=(
            shaped((rows, units), low),
            shaped((rows, units), low),
            shaped((rows, width), low),
            shaped((width, units), low),
            shaped((rows, units), low),
        ),
        in_specs=[in_any()] * 6,
        out_specs=[in_any()] * 5,
        scratch_shapes=[vmem_like(m) for m in (hidden, gate, up, down)]
        + [
            pltpu.VMEM((n_line * own_rows, width), low),
            pltpu.VMEM((rows, units), full),
            pltpu.VMEM((rows, units), full),
            pltpu.VMEM((rows, units), low),
            pltpu.VMEM((rows, units), low),
            pltpu.VMEM((rows, units), low),
            pltpu.VMEM((2, part, units), low),
            pltpu.VMEM((rows, width), low),
            dma_sems(5 + n_line),
            dma_sems(4),
            dma_sems(4),
            dma_sems(2, n_line - 1),
            dma_sems(2, n_line - 1),
        ],
        compiler_params=comm_params(7),
        name="feed_forward",
    )(hidden, gate, up, down, grads, grad_own)


def matches(mesh):
    return mesh.shape["dp"] == 8 and mesh.shape["tensor"] == 4


def local_blocks(
    tokens,
    norm_gain,
    x_weight,
    y_weight,
    conv_weight,
    recur_gate_weight,
    input_gate_weight,
    decay_param,
    out_weight,
    mlp_gain,
    gate_weight,
    up_weight,
    down_weight,
    seq_lengths,
    token_order,
    cotangent,
):
    n_dp, n_tensor = lax.axis_size("dp"), lax.axis_size("tensor")
    tensor_index = lax.axis_index("tensor")
    dp_index = lax.axis_index("dp")
    tok_rows, width = tokens.shape
    row_count = tok_rows * n_tensor
    own_width = conv_weight.shape[1]
    kernel_taps = conv_weight.shape[0]
    edge_rows = kernel_taps - 1
    dp_width = norm_gain.shape[0]
    gate_rows = recur_gate_weight.shape[0]
    own_start = tensor_index * tok_rows

    gains = jnp.concatenate([norm_gain, mlp_gain])
    spare = gate_rows * 128 - gains.shape[0]
    gains = jnp.pad(gains, (0, spare)).reshape(gate_rows, 128)
    minor = jnp.concatenate([recur_gate_weight, input_gate_weight, gains], axis=1)
    own_order = (token_order - dp_index * row_count).astype(jnp.int32)
    order_rows = jnp.broadcast_to(own_order[None, :], (8, tok_rows))
    x_full, y_full, out_full, minor_full, tok_all, order_full = first_gather(
        n_dp, n_tensor, (x_weight, y_weight, out_weight.T, minor), tokens, order_rows
    )
    late_up, late_down, _ = lax.optimization_barrier((up_weight, down_weight.T, tok_all))
    up_full = lax.all_gather(late_up, "dp", axis=0, tiled=True)
    down_full = lax.all_gather(late_down, "dp", axis=0, tiled=True)
    order_all = order_full.reshape(n_tensor, 8, tok_rows)[:, 0].reshape(row_count)
    both_gates = minor_full[:, : 2 * own_width]
    gain_rows = minor_full[:, 2 * own_width :].reshape(n_dp, -1)
    first_gain = gain_rows[:, :dp_width].reshape(1, width).astype(jnp.float32)
    second_gain = gain_rows[:, dp_width : 2 * dp_width].reshape(1, width).astype(jnp.float32)
    block_size = both_gates.shape[0]
    row_index = jnp.arange(row_count, dtype=jnp.int32)
    hits = row_index[:, None] == order_all[None, :]
    to_place = hits.astype(jnp.bfloat16)
    to_stored = (order_all[:, None] == row_index[None, :]).astype(jnp.bfloat16)
    places = dp_index * row_count + jnp.arange(-8, row_count + 8, dtype=jnp.int32)
    inside = (jnp.arange(row_count + 16) >= 8) & (jnp.arange(row_count + 16) < row_count + 8)
    ends = jnp.cumsum(seq_lengths)
    segment = segment_of(places, ends)
    starts = (places == 0) | (segment != segment_of(places - 1, ends))
    columns = [starts] + [
        segment_of(places - shift, ends) == segment for shift in range(1, kernel_taps)
    ]
    columns += [jnp.zeros_like(starts)] * (8 - len(columns))
    flags = (jnp.stack(columns, axis=1) & inside[:, None]).astype(jnp.float32)
    live_own = (token_order < ends[-1]).astype(jnp.float32)
    grad_in_own = (cotangent.astype(jnp.float32) * live_own[:, None]).astype(jnp.bfloat16)
    soft = jax.nn.softplus(-decay_param).reshape(1, own_width)
    slope = jax.nn.sigmoid(-decay_param).reshape(1, own_width)
    zero_rim = jnp.zeros((block_size, RIM), jnp.bfloat16)
    gates_wide = jnp.concatenate(
        [
            zero_rim,
            both_gates[:, :own_width],
            zero_rim,
            zero_rim,
            both_gates[:, own_width:],
            zero_rim,
        ],
        axis=1,
    )
    hidden_place, *kept, merged_stored, mixer_terms, grad_rows = recur_forward(
        n_dp,
        n_tensor,
        tok_all,
        grad_in_own,
        to_place,
        to_stored,
        x_full,
        y_full,
        out_full,
        first_gain,
        gates_wide,
        conv_weight,
        soft,
        flags,
    )
    after_own, hidden_two, gate_full = middle_gather(
        n_dp, n_tensor, mixer_terms, tokens, second_gain, (gate_weight,)
    )
    product, grad_up_pre, back_terms, grad_down, grad_gate_pre = feed_forward(
        n_dp,
        n_tensor,
        hidden_two,
        gate_full,
        up_full,
        down_full,
        grad_rows,
        grad_in_own,
    )
    down_sum = lax.psum_scatter(grad_down, "dp", scatter_dimension=0, tiled=True)
    grad_after_own, second_part, mixer_in, gate_sum, grad_up, feed_terms, _ = middle_sums(
        n_dp,
        n_tensor,
        back_terms,
        after_own,
        second_gain,
        grad_in_own,
        grad_gate_pre,
        hidden_two,
        grad_up_pre,
        product,
        down_full,
    )
    (
        gate_grads,
        tap_grads,
        decay_grad,
        one_terms,
        up_sum,
        feed_out,
        grad_out_mat,
        grad_xy_mat,
    ) = recur_backward(
        n_dp,
        n_tensor,
        mixer_in,
        to_place,
        to_stored,
        x_full,
        y_full,
        out_full,
        gates_wide,
        conv_weight,
        soft,
        slope,
        flags,
        kept,
        grad_up,
        feed_terms,
        hidden_place,
        merged_stored,
    )
    output = (after_own + feed_out.astype(jnp.float32)) * live_own[:, None]
    output = output.astype(jnp.bfloat16)
    small = jnp.concatenate(
        [
            second_part,
            tap_grads[:kernel_taps].reshape(1, -1),
            jnp.pad(decay_grad, ((0, 0), (0, width - own_width))),
            jnp.zeros((1, width), jnp.float32),
        ],
        axis=0,
    )
    grad_tokens, small_sum, gain_sums, xy_sum, out_sum, gates_sum = last_sums(
        n_dp,
        n_tensor,
        one_terms,
        tokens,
        first_gain,
        grad_after_own,
        small,
        (grad_xy_mat, grad_out_mat, gate_grads),
    )
    xy_sum, gates_sum = xy_sum.astype(jnp.float32), gates_sum.astype(jnp.float32)
    own_gains = lax.dynamic_slice_in_dim(gain_sums, dp_index * dp_width, dp_width, 1)
    return (
        output,
        grad_tokens,
        own_gains[1],
        xy_sum[:, :own_width],
        xy_sum[:, own_width:],
        small_sum[1].reshape(kernel_taps, own_width),
        gates_sum[:, :own_width],
        gates_sum[:, own_width:],
        small_sum[2, :own_width],
        out_sum.astype(jnp.float32).T,
        own_gains[0],
        gate_sum.astype(jnp.float32),
        up_sum.astype(jnp.float32),
        down_sum.astype(jnp.float32).T,
    )


def solution(mesh):
    in_specs = (
        P(("dp", "tensor"), None),
        P("dp"),
        P("dp", "tensor"),
        P("dp", "tensor"),
        P(None, "tensor"),
        P("dp", "tensor"),
        P("dp", "tensor"),
        P("tensor"),
        P("tensor", "dp"),
        P("dp"),
        P("dp", "tensor"),
        P("dp", "tensor"),
        P("tensor", "dp"),
        P(),
        P(("dp", "tensor")),
        P(("dp", "tensor"), None),
    )
    out_specs = (
        P(("dp", "tensor"), None),
        P(("dp", "tensor"), None),
        P("dp"),
        P("dp", "tensor"),
        P("dp", "tensor"),
        P(None, "tensor"),
        P("dp", "tensor"),
        P("dp", "tensor"),
        P("tensor"),
        P("tensor", "dp"),
        P("dp"),
        P("dp", "tensor"),
        P("dp", "tensor"),
        P("tensor", "dp"),
    )
    fits = matches(mesh)
    local = local_blocks if fits else local_general
    return jax.shard_map(local, mesh=mesh, in_specs=in_specs, out_specs=out_specs, check_vma=False)
```

```python
import jax
import jax.numpy as jnp
from jax import lax
from jax.experimental import pallas as pl
from jax.experimental.pallas import tpu as pltpu
from jax.sharding import PartitionSpec as P

epsilon = 1e-06
rate_scale = 8.0


def from_behind(block, axis, distance):
    devices = range(lax.axis_size(axis))
    route = [(i - distance, i) for i in devices if i - distance in devices]
    return lax.ppermute(block, axis, route)


def extended_2(array, sides, width):
    for axis, dim in sides:
        size, length = (lax.axis_size(axis), array.shape[dim])
        up = [(i, (i + 1) % size) for i in range(size - 1)]
        down = [(j, i) for i, j in up]
        last = lax.slice_in_dim(array, length - width, length, axis=dim)
        leading = lax.slice_in_dim(array, 0, width, axis=dim)
        before = lax.ppermute(last, axis, up)
        after = lax.ppermute(leading, axis, down)
        array = jnp.concatenate([before, array, after], axis=dim)
    return array


def entering(value, axis, join, neutral, backward):
    count, mine = (lax.axis_size(axis), lax.axis_index(axis))
    pieces = jax.tree.map(lambda part: lax.all_gather(part, axis), value)
    if backward:
        pieces = jax.tree.map(lambda part: part[::-1], pieces)
        mine = count - 1 - mine
    total = jax.tree.map(
        lambda part, zero: jnp.full_like(part, 0) + jnp.asarray(zero, part.dtype), value, neutral
    )

    def lap(position, total):
        longer = join(total, jax.tree.map(lambda part: part[position], pieces))
        return jax.tree.map(lambda new, old: jnp.where(position < mine, new, old), longer, total)

    return lax.fori_loop(0, count - 1, lap, total)


def rms_scale(values, gain):
    return values * lax.rsqrt(jnp.mean(values * values, axis=-1, keepdims=True) + epsilon) * gain


def norm_back(values, gain, grad):
    inv_root = lax.rsqrt(jnp.mean(values * values, axis=-1, keepdims=True) + epsilon)
    normed = values * inv_root
    upstream = grad * gain
    grad_values = inv_root * (
        upstream - normed * jnp.mean(upstream * normed, axis=-1, keepdims=True)
    )
    return (grad_values, normed)


def segment_of(places, ends):
    return jnp.sum((ends[None, :] <= places[:, None]).astype(jnp.int32), axis=1)


def pair_step(early, later):
    return (early[0] * later[0], later[0] * early[1] + later[1])


def plain_dot(left, right):
    return jnp.dot(left, right, preferred_element_type=jnp.float32)


def times_trans(left, right):
    return lax.dot_general(
        left, right, (((1,), (1,)), ((), ())), preferred_element_type=jnp.float32
    )


def trans_times(left, right):
    return lax.dot_general(
        left, right, (((0,), (0,)), ((), ())), preferred_element_type=jnp.float32
    )


def gelu_tanh(values):
    return jax.nn.gelu(values, approximate=True)


def collect(
    norm_gain,
    mlp_gain,
    x_weight,
    y_weight,
    recur_gate_weight,
    input_gate_weight,
    gate_weight,
    up_weight,
    out_weight,
    down_weight,
):
    return (
        lax.all_gather(norm_gain, "dp", axis=0, tiled=True),
        lax.all_gather(mlp_gain, "dp", axis=0, tiled=True),
        lax.all_gather(x_weight, "dp", axis=0, tiled=True),
        lax.all_gather(y_weight, "dp", axis=0, tiled=True),
        lax.all_gather(recur_gate_weight, "dp", axis=0, tiled=True),
        lax.all_gather(input_gate_weight, "dp", axis=0, tiled=True),
        lax.all_gather(gate_weight, "dp", axis=0, tiled=True),
        lax.all_gather(up_weight, "dp", axis=0, tiled=True),
        lax.all_gather(out_weight, "dp", axis=1, tiled=True),
        lax.all_gather(down_weight, "dp", axis=1, tiled=True),
    )


def row_sums(term_rows, tok_rows):
    return lax.psum_scatter(
        term_rows(jnp.int32(0), lax.axis_size("tensor") * tok_rows).astype(jnp.bfloat16),
        "tensor",
        scatter_dimension=0,
        tiled=True,
    ).astype(jnp.float32)


def spread_rows(values):
    return lax.all_gather(values, "tensor", axis=0, tiled=True)


def local_general(
    tokens,
    norm_gain,
    x_weight,
    y_weight,
    conv_weight,
    recur_gate_weight,
    input_gate_weight,
    decay_param,
    out_weight,
    mlp_gain,
    gate_weight,
    up_weight,
    down_weight,
    seq_lengths,
    token_order,
    cotangent,
):
    n_tensor = lax.axis_size("tensor")
    tensor_index = lax.axis_index("tensor")
    dp_index = lax.axis_index("dp")
    tok_rows = tokens.shape[0]
    row_count = tok_rows * n_tensor
    own_width = conv_weight.shape[1]
    kernel_taps = conv_weight.shape[0]
    edge_rows = kernel_taps - 1
    dp_width = norm_gain.shape[0]
    own_start = tensor_index * tok_rows
    shards = (
        norm_gain,
        mlp_gain,
        x_weight,
        y_weight,
        recur_gate_weight,
        input_gate_weight,
        gate_weight,
        up_weight,
        out_weight,
        down_weight,
    )
    (
        gain_one,
        gain_two,
        x_full,
        y_full,
        recur_full,
        input_full,
        gate_full,
        up_full,
        out_full,
        down_full,
    ) = collect(*shards)
    block_size = recur_full.shape[0]
    first_gain = gain_one.astype(jnp.float32)
    second_gain = gain_two.astype(jnp.float32)
    both_gates = jnp.concatenate([recur_full, input_full], axis=1)
    tok_own = tokens.astype(jnp.float32)
    own_order = token_order - dp_index * row_count
    first_rows = rms_scale(tok_own, first_gain).astype(jnp.bfloat16)
    first_all, cot_all, order_all = (
        lax.all_gather(first_rows, "tensor", axis=0, tiled=True),
        lax.all_gather(cotangent, "tensor", axis=0, tiled=True),
        lax.all_gather(own_order, "tensor", axis=0, tiled=True),
    )
    row_index = jnp.arange(row_count, dtype=jnp.int32)
    inverse = jnp.zeros((row_count,), jnp.int32).at[order_all].set(row_index)
    hidden_place = jnp.take(first_all, inverse, axis=0)
    places = dp_index * row_count + row_index
    ends = jnp.cumsum(seq_lengths)
    segment = segment_of(places, ends)
    starts = (places == 0) | (segment != segment_of(places - 1, ends))
    live = (places < ends[-1]).astype(jnp.float32)
    live_stored = jnp.take(live, order_all, axis=0)
    same = [
        (segment_of(places - shift, ends) == segment).astype(jnp.float32)
        for shift in range(kernel_taps)
    ]
    low_edge = tensor_index * own_width
    own_blocks = (low_edge + jnp.arange(own_width, dtype=jnp.int32)) // block_size
    first_block = low_edge // block_size
    block_count = own_width // block_size + 2

    def block_start(index):
        return (first_block + index) * block_size - low_edge + block_size

    def block_mask(index):
        inside = own_blocks == first_block + index
        return jnp.concatenate([inside, inside])

    def convolve(extended, kernel):
        return sum(
            (
                kernel[shift][None, :]
                * extended[edge_rows - shift : edge_rows - shift + row_count]
                * same[shift][:, None]
                for shift in range(kernel_taps)
            )
        )

    def gates(conv_vals, pre_recur, pre_input, decay_vals):
        log_rate = -rate_scale * jax.nn.sigmoid(pre_recur) * jax.nn.softplus(-decay_vals)
        decay_rate = jnp.where(starts[:, None], 0.0, jnp.exp(log_rate))
        scale_in = jnp.where(starts[:, None], 1.0, jnp.sqrt(-jnp.expm1(2.0 * log_rate)))
        return (decay_rate, conv_vals * jax.nn.sigmoid(pre_input) * scale_in)

    def glu(gate_pre, up_pre):
        return gelu_tanh(gate_pre) * up_pre

    x_branch = plain_dot(hidden_place, x_full).astype(jnp.bfloat16)
    y_before = plain_dot(hidden_place, y_full)
    previous = from_behind(x_branch[row_count - edge_rows :], "dp", 1)
    extended = jnp.concatenate([previous, x_branch], axis=0).astype(jnp.float32)
    conv_out = convolve(extended, conv_weight)
    conv_wide = extended_2(conv_out.astype(jnp.bfloat16), (("tensor", 1),), block_size)
    pre_both = jnp.zeros((row_count, 2 * own_width), jnp.float32)
    for index in range(block_count):
        piece = lax.dynamic_slice_in_dim(conv_wide, block_start(index), block_size, 1)
        pre_both = pre_both + jnp.where(
            block_mask(index)[None, :], plain_dot(piece, both_gates), 0.0
        )
    (decay_rate, driven), gate_pull = jax.vjp(
        gates, conv_out, pre_both[:, :own_width], pre_both[:, own_width:], decay_param
    )
    cum_rate, local_state = lax.associative_scan(pair_step, (decay_rate, driven), axis=0)
    ident = (jnp.ones((own_width,), jnp.float32), jnp.zeros((own_width,), jnp.float32))
    rate_in, state_in = entering((cum_rate[-1], local_state[-1]), "dp", pair_step, ident, False)
    state = local_state + cum_rate * state_in[None, :]
    y_branch = gelu_tanh(y_before)
    merged = (state * y_branch).astype(jnp.bfloat16)
    merged_stored = jnp.take(merged, order_all, axis=0)

    def mixer_rows(begin, number):
        return plain_dot(merged_stored, out_full)

    after_own = tok_own + row_sums(mixer_rows, tok_rows)
    hidden_two = spread_rows(rms_scale(after_own, second_gain).astype(jnp.bfloat16))
    gate_pre = plain_dot(hidden_two, gate_full)
    up_pre = plain_dot(hidden_two, up_full)
    glu_out, glu_pull = jax.vjp(glu, gate_pre, up_pre)
    product = glu_out.astype(jnp.bfloat16)

    def down_rows(begin, number):
        return plain_dot(product, down_full)

    feed_out = row_sums(down_rows, tok_rows)
    live_own = lax.dynamic_slice_in_dim(live_stored, own_start, tok_rows, 0)
    output = ((after_own + feed_out) * live_own[:, None]).astype(jnp.bfloat16)
    grad_out = cot_all.astype(jnp.float32) * live_stored[:, None]
    fresh = lax.optimization_barrier((shards, grad_out))[0]
    (
        gain_one,
        gain_two,
        x_full,
        y_full,
        recur_full,
        input_full,
        gate_full,
        up_full,
        out_full,
        down_full,
    ) = collect(*fresh)
    first_gain = gain_one.astype(jnp.float32)
    second_gain = gain_two.astype(jnp.float32)
    both_gates = jnp.concatenate([recur_full, input_full], axis=1)
    down_in = grad_out.astype(jnp.bfloat16)
    grad_down = trans_times(product, down_in)
    grad_product = times_trans(down_in, down_full)
    grad_gate_pre, grad_up_pre = glu_pull(grad_product)
    grad_gate_pre = grad_gate_pre.astype(jnp.bfloat16)
    grad_up_pre = grad_up_pre.astype(jnp.bfloat16)
    grad_gate = trans_times(hidden_two, grad_gate_pre)
    grad_up = trans_times(hidden_two, grad_up_pre)

    def feed_rows(begin, number):
        return times_trans(grad_gate_pre, gate_full) + times_trans(grad_up_pre, up_full)

    grad_out_own = lax.dynamic_slice_in_dim(grad_out, own_start, tok_rows, 0)
    grad_two_own = row_sums(feed_rows, tok_rows)
    grad_norm_own, normed_two = norm_back(after_own, second_gain, grad_two_own)
    second_part = jnp.sum(grad_two_own * normed_two, axis=0)
    grad_after_own = grad_out_own + grad_norm_own
    mixer_in = spread_rows(grad_after_own.astype(jnp.bfloat16))
    grad_out_mat = trans_times(merged_stored, mixer_in)
    grad_merged = jnp.take(times_trans(mixer_in, out_full), inverse, axis=0)
    grad_state = grad_merged * y_branch
    gelu_pull = jax.vjp(gelu_tanh, y_before)[1]
    grad_y_before = gelu_pull(grad_merged * state)[0].astype(jnp.bfloat16)
    rate_next = jnp.concatenate([decay_rate[1:], jnp.ones((1, own_width), jnp.float32)], axis=0)
    rev_rate, local_lam = lax.associative_scan(
        pair_step, (rate_next, grad_state), reverse=True, axis=0
    )
    head_rate = decay_rate[0] * rev_rate[0]
    head_lam = decay_rate[0] * local_lam[0]
    factor_in, lam_in = entering((head_rate, head_lam), "dp", pair_step, ident, True)
    lam = local_lam + rev_rate * lam_in[None, :]
    state_prev = jnp.concatenate([state_in[None, :], state[:-1]], axis=0)
    grad_conv_local, grad_pre_recur, grad_pre_input, grad_decay_own = gate_pull(
        (lam * state_prev, lam)
    )
    grad_pre = jnp.concatenate([grad_pre_recur, grad_pre_input], axis=1).astype(jnp.bfloat16)
    grad_both = jnp.zeros((block_size, 2 * own_width), jnp.float32)
    grad_wide = jnp.zeros((row_count, own_width + 2 * block_size), jnp.float32)
    for index in range(block_count):
        begin = block_start(index)
        piece = lax.dynamic_slice_in_dim(conv_wide, begin, block_size, 1)
        masked = jnp.where(block_mask(index)[None, :], grad_pre, jnp.zeros((), jnp.bfloat16))
        grad_both = grad_both + trans_times(piece, masked)
        added = lax.dynamic_slice_in_dim(grad_wide, begin, block_size, 1) + times_trans(
            masked, both_gates
        )
        grad_wide = lax.dynamic_update_slice_in_dim(grad_wide, added, begin, 1)
    grad_recur = grad_both[:, :own_width]
    grad_input = grad_both[:, own_width:]
    rims = jnp.concatenate(
        [grad_wide[:, :block_size], grad_wide[:, own_width + block_size :]], axis=1
    )
    arrived = extended_2(rims.astype(jnp.bfloat16), (("tensor", 1),), block_size).astype(rims.dtype)
    from_lower = jnp.pad(arrived[:, :block_size], ((0, 0), (0, own_width - block_size)))
    from_upper = jnp.pad(arrived[:, 3 * block_size :], ((0, 0), (own_width - block_size, 0)))
    grad_conv = (
        grad_conv_local
        + grad_wide[:, block_size : block_size + own_width]
        + from_lower
        + from_upper
    )
    conv_pull = jax.vjp(convolve, extended, conv_weight)[1]
    grad_extended, grad_kernel = conv_pull(grad_conv)
    returned = from_behind(grad_extended[:edge_rows], "dp", -1)
    grad_x_branch = grad_extended[edge_rows:] + jnp.concatenate(
        [jnp.zeros((row_count - edge_rows, own_width), jnp.float32), returned], axis=0
    )
    grad_x_low = grad_x_branch.astype(jnp.bfloat16)
    grad_x_stored = jnp.take(grad_x_low, order_all, axis=0)
    grad_y_stored = jnp.take(grad_y_before, order_all, axis=0)
    grad_x_mat = trans_times(first_all, grad_x_stored)
    grad_y_mat = trans_times(first_all, grad_y_stored)

    def mixer_back_rows(begin, number):
        return times_trans(grad_x_stored, x_full) + times_trans(grad_y_stored, y_full)

    grad_one_own = row_sums(mixer_back_rows, tok_rows)
    grad_norm_one, normed_one = norm_back(tok_own, first_gain, grad_one_own)
    first_part = jnp.sum(grad_one_own * normed_one, axis=0)
    grad_tokens = grad_after_own + grad_norm_one
    chosen = jnp.arange(n_tensor, dtype=jnp.int32) == tensor_index
    kernel_tile = jnp.where(chosen[:, None, None], grad_kernel[None, :, :], 0.0)
    decay_tile = jnp.where(chosen[:, None], grad_decay_own[None, :], 0.0)
    small = lax.psum((first_part, second_part, kernel_tile, decay_tile), ("dp", "tensor"))
    grad_first_gain = lax.dynamic_slice_in_dim(small[0], dp_index * dp_width, dp_width, 0)
    grad_second_gain = lax.dynamic_slice_in_dim(small[1], dp_index * dp_width, dp_width, 0)
    grad_kernel_sum = lax.dynamic_index_in_dim(small[2], tensor_index, 0, keepdims=False)
    grad_decay = lax.dynamic_index_in_dim(small[3], tensor_index, 0, keepdims=False)
    sums = (
        lax.psum_scatter(
            grad_x_mat.astype(jnp.bfloat16), "dp", scatter_dimension=0, tiled=True
        ).astype(jnp.float32),
        lax.psum_scatter(
            grad_y_mat.astype(jnp.bfloat16), "dp", scatter_dimension=0, tiled=True
        ).astype(jnp.float32),
        lax.psum_scatter(
            grad_recur.astype(jnp.bfloat16), "dp", scatter_dimension=0, tiled=True
        ).astype(jnp.float32),
        lax.psum_scatter(
            grad_input.astype(jnp.bfloat16), "dp", scatter_dimension=0, tiled=True
        ).astype(jnp.float32),
        lax.psum_scatter(
            grad_gate.astype(jnp.bfloat16), "dp", scatter_dimension=0, tiled=True
        ).astype(jnp.float32),
        lax.psum_scatter(
            grad_up.astype(jnp.bfloat16), "dp", scatter_dimension=0, tiled=True
        ).astype(jnp.float32),
        lax.psum_scatter(
            grad_out_mat.astype(jnp.bfloat16), "dp", scatter_dimension=1, tiled=True
        ).astype(jnp.float32),
        lax.psum_scatter(
            grad_down.astype(jnp.bfloat16), "dp", scatter_dimension=1, tiled=True
        ).astype(jnp.float32),
    )
    return (
        output,
        grad_tokens,
        grad_first_gain,
        sums[0],
        sums[1],
        grad_kernel_sum,
        sums[2],
        sums[3],
        grad_decay,
        sums[6],
        grad_second_gain,
        sums[4],
        sums[5],
        sums[7],
    )


MESH = pl.DeviceIdType.MESH
VMEM_BYTES = 60 * 2**20


def remote(src, dst, send, recv, device):
    return pltpu.make_async_remote_copy(
        src_ref=src,
        dst_ref=dst,
        send_sem=send,
        recv_sem=recv,
        device_id=device,
        device_id_type=MESH,
    )


class Place:
    def __init__(self, n_dp, n_line):
        self.n_dp, self.n_line = n_dp, n_line
        self.d, self.t = lax.axis_index("dp"), lax.axis_index("tensor")
        self.core = lax.rem(self.d, 2)
        self.x = lax.rem(lax.div(self.d, 2), 2)
        self.y = lax.div(self.d, 4)

    def chip(self, flip_x, flip_y, flip_core=0):
        x = 1 - self.x if flip_x else self.x
        y = 1 - self.y if flip_y else self.y
        core = 1 - self.core if flip_core else self.core
        return y * 4 + x * 2 + core

    def at(self, flip_x=0, flip_y=0, flip_core=0):
        return (self.chip(flip_x, flip_y, flip_core), self.t)

    def up(self):
        return (self.d, lax.rem(self.t + 1, self.n_line))

    def down(self):
        return (self.d, lax.rem(self.t + self.n_line - 1, self.n_line))

    def meet(self, everyone=False):
        barrier = pltpu.get_barrier_semaphore()

        def greet(device):
            pl.semaphore_signal(barrier, inc=1, device_id=device, device_id_type=MESH)

        if everyone:
            for i in range(1, self.n_dp):
                greet((lax.rem(self.d + i, self.n_dp), self.t))
            for i in range(1, self.n_line):
                greet((self.d, lax.rem(self.t + i, self.n_line)))
            pl.semaphore_wait(barrier, self.n_dp + self.n_line - 2)
            return
        for flips in ((1, 0), (0, 1), (0, 0, 1)):
            greet(self.at(*flips))
        below, above = self.t > 0, self.t < self.n_line - 1

        @pl.when(below)
        def _():
            greet(self.down())

        @pl.when(above)
        def _():
            greet(self.up())

        pl.semaphore_wait(barrier, 3 + below.astype(jnp.int32) + above.astype(jnp.int32))


class Fetch:
    def __init__(self, pairs, sems):
        self.copies = [
            pltpu.make_async_copy(src, dst, sems.at[i]) for i, (src, dst) in enumerate(pairs)
        ]

    def start(self, *which):
        for i in which:
            self.copies[i].start()

    def wait(self, *which):
        for i in which:
            self.copies[i].wait()


def vmem_like(array):
    return pltpu.VMEM(array.shape, array.dtype)


class Kept:
    def __init__(self, src, dst, held, sems):
        self.there = pltpu.make_async_copy(src, held, sems.at[0])
        self.back = pltpu.make_async_copy(held, dst, sems.at[1])

    def begin(self):
        self.there.start()

    def turn(self):
        self.there.wait()
        self.back.start()

    def finish(self):
        self.back.wait()


class GatherPlane:
    def __init__(self, place, src, dst, send, recv, local, held):
        self.p, self.src, self.dst = place, src, dst
        self.rows = src.shape[0]
        self.send, self.recv = send, recv
        self.keep = Kept(src, self.block(0, 0), held, local)

    def block(self, fx, fy, fc=0, part=None):
        first = self.p.chip(fx, fy, fc) * self.rows
        size = self.rows
        if part is not None:
            size = self.rows // 2
            first = first + part * size
        return self.dst.at[pl.ds(pl.multiple_of(first, 16), size)]

    def copy(self, i, src, dst, device):
        return remote(src, dst, self.send.at[i], self.recv.at[i], device)

    def outgoing(self, i):
        at, block = self.p.at, self.block
        if i == 0:
            return self.copy(0, self.src, block(0, 0), at(1, 0))
        if i == 1:
            return self.copy(1, self.src, block(0, 0), at(0, 1))
        if i == 2:
            return self.copy(2, self.src, block(0, 0), at(0, 0, 1))
        if i == 3:
            return self.copy(3, block(1, 0, 0, 0), block(1, 0, 0, 0), at(0, 1))
        if i == 4:
            return self.copy(4, block(0, 1, 0, 1), block(0, 1, 0, 1), at(1, 0))
        spot = ((1, 0), (0, 1), (1, 1, 0, 0), (1, 1, 0, 1))[i - 5]
        return self.copy(i, block(*spot), block(*spot), at(0, 0, 1))

    def arrive(self, i):
        spot = (
            (1, 0),
            (0, 1),
            (0, 0, 1),
            (1, 1, 0, 0),
            (1, 1, 0, 1),
            (1, 0, 1),
            (0, 1, 1),
            (1, 1, 1, 0),
            (1, 1, 1, 1),
        )[i]
        here = self.block(*spot)
        self.copy(i, here, here, self.p.at(0, 0, 1)).wait_recv()

    def begin(self):
        for i in (0, 1, 2):
            self.outgoing(i).start()
        self.keep.begin()

    def forward(self):
        self.keep.turn()
        self.arrive(0)
        self.outgoing(3).start()
        self.arrive(1)
        self.outgoing(4).start()
        self.outgoing(5).start()
        self.outgoing(6).start()

    def share(self):
        self.arrive(3)
        self.outgoing(7).start()
        self.arrive(4)
        self.outgoing(8).start()

    def finish(self):
        for i in (2, 5, 6, 7, 8):
            self.arrive(i)
        for i in range(9):
            self.outgoing(i).wait_send()
        self.keep.finish()


class GatherLine:
    def __init__(self, place, dst, rows, begin, span, send, recv):
        self.p, self.dst, self.rows = place, dst, rows
        self.begin, self.span = begin, span
        self.send, self.recv = send, recv
        self.last = place.n_line - 1

    def block(self, owner):
        first = owner * self.rows + self.begin
        return self.dst.at[pl.ds(pl.multiple_of(first, 8), self.span)]

    def copy(self, way, k, owner, source=None):
        to = self.p.up() if way == 0 else self.p.down()
        block = self.block(owner)
        return remote(
            block if source is None else source,
            block,
            self.send.at[way, k],
            self.recv.at[way, k],
            to,
        )

    def step(self, k, source=None):
        t, last = self.p.t, self.last
        if k > 0:
            self.arrive(k - 1)

        @pl.when((t < last) & (t >= k))
        def _():
            self.copy(0, k, t - k, source).start()

        @pl.when((t > 0) & (t + k <= last))
        def _():
            self.copy(1, k, t + k, source).start()

    def arrive(self, k):
        t, last = self.p.t, self.last

        @pl.when(t >= k + 1)
        def _():
            self.copy(0, k, t - 1 - k).wait_recv()

        @pl.when(t + k + 1 <= last)
        def _():
            self.copy(1, k, t + 1 + k).wait_recv()

    def finish(self):
        t, last = self.p.t, self.last
        self.arrive(last - 1)
        for k in range(last):

            @pl.when((t < last) & (t >= k))
            def _():
                self.copy(0, k, t - k).wait_send()

            @pl.when((t > 0) & (t + k <= last))
            def _():
                self.copy(1, k, t + k).wait_send()


class ReduceLine:
    def __init__(self, place, terms, rows, begin, span, inbox, send, recv):
        self.p, self.terms, self.rows = place, terms, rows
        self.begin, self.span = begin, span
        self.inbox = inbox
        self.send, self.recv = send, recv
        self.last = place.n_line - 1

    def own(self, owner):
        first = owner * self.rows + self.begin
        return self.terms.at[pl.ds(pl.multiple_of(first, 16), self.span)]

    def copy(self, way, j, source):
        to = self.p.up() if way == 0 else self.p.down()
        return remote(
            source, self.inbox.at[way, j], self.send.at[way, j], self.recv.at[way, j], to
        )

    def ends(self):
        t, last = self.p.t, self.last

        @pl.when(t == 0)
        def _():
            for j in range(last):
                self.copy(0, j, self.own(last - j)).start()

        @pl.when(t == last)
        def _():
            for j in range(last):
                self.copy(1, j, self.own(j)).start()

    def sent(self):
        t, last = self.p.t, self.last

        @pl.when(t == 0)
        def _():
            for j in range(last):
                self.copy(0, j, self.own(last - j)).wait_send()

        @pl.when(t == last)
        def _():
            for j in range(last):
                self.copy(1, j, self.own(j)).wait_send()

    def hand_on(self, way, j):
        term = self.own(self.last - j if way == 0 else j)
        self.copy(way, j, term).wait_recv()
        self.inbox[way, j] = term[...] + self.inbox[way, j]
        self.copy(way, j, self.inbox.at[way, j]).start()

    def hop(self, k):
        t, last = self.p.t, self.last

        @pl.when(t == k + 1)
        def _():
            for j in range(last - 1 - k):
                self.hand_on(0, j)

        @pl.when(t == last - 1 - k)
        def _():
            for j in range(last - 1 - k):
                self.hand_on(1, j)

    def total(self, result):
        t, last = self.p.t, self.last
        result[...] = self.own(t)[...].astype(jnp.float32)

        @pl.when(t > 0)
        def _():
            j = last - t
            self.copy(0, j, self.inbox.at[0, 0]).wait_recv()
            result[...] += self.inbox[0, j].astype(jnp.float32)

        @pl.when(t < last)
        def _():
            self.copy(1, t, self.inbox.at[0, 0]).wait_recv()
            result[...] += self.inbox[1, t].astype(jnp.float32)

    def finish(self):
        t, last = self.p.t, self.last
        for j in range(last - 1):

            @pl.when((t > 0) & (t < last - j))
            def _():
                self.copy(0, j, self.inbox.at[0, j]).wait_send()

            @pl.when((t < last) & (t > j))
            def _():
                self.copy(1, j, self.inbox.at[1, j]).wait_send()


def add_rows(into, other, result=None):
    result = into if result is None else result

    def tile(i, carry):
        rows = pl.ds(pl.multiple_of(i * 16, 16), 16)
        result[rows] = into[rows] + other[rows]
        return carry

    lax.fori_loop(0, into.shape[0] // 16, tile, None)


class ReducePlane:
    chips = ((0, 0), (1, 0), (0, 1), (1, 1))

    def __init__(self, place, terms, scratch):
        self.p, self.terms = place, terms
        self.held, self.near, self.along, self.last, self.send, self.recv, self.local = scratch
        self.rows = self.held.shape[1]
        self.half = self.rows // 2

    @staticmethod
    def scratch(rows, width):
        return [
            pltpu.VMEM((4, rows, width), jnp.bfloat16),
            pltpu.VMEM((4, rows, width), jnp.bfloat16),
            pltpu.VMEM((4, rows // 2, width), jnp.bfloat16),
            pltpu.VMEM((2, rows // 2, width), jnp.bfloat16),
            pltpu.SemaphoreType.DMA((10,)),
            pltpu.SemaphoreType.DMA((10,)),
            pltpu.SemaphoreType.DMA((4,)),
        ]

    def block(self, k, other):
        first = self.p.chip(*self.chips[k], other) * self.rows
        return self.terms.at[pl.ds(pl.multiple_of(first, 16), self.rows)]

    def half_of(self, k, part):
        return self.held.at[k, pl.ds(part * self.half, self.half)]

    def load(self, k):
        return pltpu.make_async_copy(self.block(k, 0), self.held.at[k], self.local.at[k])

    def copy(self, i):
        at = self.p.at
        if i < 4:
            src, dst, to = self.block(i, 1), self.near.at[i], at(0, 0, 1)
        elif i < 8:
            src, to = (
                (self.half_of(1, 0), at(1, 0)),
                (self.half_of(3, 0), at(1, 0)),
                (self.half_of(2, 1), at(0, 1)),
                (self.half_of(3, 1), at(0, 1)),
            )[i - 4]
            dst = self.along.at[i - 4]
        else:
            src, to = ((self.half_of(2, 0), at(0, 1)), (self.half_of(1, 1), at(1, 0)))[i - 8]
            dst = self.last.at[i - 8]
        return remote(src, dst, self.send.at[i], self.recv.at[i], to)

    def begin(self):
        for k in (3, 1, 2, 0):
            self.copy(k).start()
            self.load(k).start()

    def cores(self):
        for k in (3, 1, 2, 0):
            self.load(k).wait()
            self.copy(k).wait_recv()
            add_rows(self.held.at[k], self.near.at[k])
            if k == 3:
                self.copy(5).start()
                self.copy(7).start()
            elif k == 1:
                self.copy(4).start()
            elif k == 2:
                self.copy(6).start()

    def turn(self):
        self.copy(5).wait_recv()
        add_rows(self.half_of(2, 0), self.along.at[1])
        self.copy(8).start()
        self.copy(7).wait_recv()
        add_rows(self.half_of(1, 1), self.along.at[3])
        self.copy(9).start()
        self.copy(4).wait_recv()
        add_rows(self.half_of(0, 0), self.along.at[0])
        self.copy(6).wait_recv()
        add_rows(self.half_of(0, 1), self.along.at[2])

    def finish(self, result):
        for part in (0, 1):
            self.copy(8 + part).wait_recv()
            rows = pl.ds(part * self.half, self.half)
            add_rows(self.half_of(0, part), self.last.at[part], result.at[rows])
        for i in range(10):
            self.copy(i).wait_send()


def dma_sems(*dims):
    return pltpu.SemaphoreType.DMA(dims)


def in_vmem():
    return pl.BlockSpec(memory_space=pltpu.VMEM)


def in_any():
    return pl.BlockSpec(memory_space=pl.ANY)


def comm_params(number):
    return pltpu.CompilerParams(
        collective_id=number, has_side_effects=True, vmem_limit_bytes=VMEM_BYTES
    )


def shaped(dims, kind):
    return jax.ShapeDtypeStruct(dims, kind)


def first_gather(n_dp, n_line, mats, rows_in, order):
    count = len(mats)
    parts = 2

    def kernel(*refs):
        srcs, (c, e) = refs[:count], refs[count : count + 2]
        dsts, (c_out, e_out) = refs[count + 2 : 2 * count + 2], refs[2 * count + 2 : 2 * count + 4]
        ps, pr, pl_sem, ls, lr, ll = refs[2 * count + 4 : 2 * count + 10]
        held = refs[2 * count + 10 :]
        place = Place(n_dp, n_line)
        place.meet()
        planes = [
            GatherPlane(place, a, b, ps.at[i], pr.at[i], pl_sem.at[i], held[i])
            for i, (a, b) in enumerate(zip(srcs, dsts))
        ]
        rows = c.shape[0]
        span = rows // parts
        lines = [
            GatherLine(place, c_out, rows, i * span, span, ls.at[i], lr.at[i])
            for i in range(parts)
        ]
        lines.append(
            GatherLine(place, e_out, e.shape[0], 0, e.shape[0], ls.at[parts], lr.at[parts])
        )
        for i in range(parts):
            lines[i].step(0, c.at[pl.ds(i * span, span)])
        lines[parts].step(0, e)
        early, late = planes[: count // 2], planes[count // 2 :]
        for part in early:
            part.begin()
        copies = []
        for i, (src, dst) in enumerate(((c, c_out), (e, e_out))):
            own = dst.at[pl.ds(pl.multiple_of(place.t * src.shape[0], 8), src.shape[0])]
            copies.append(Kept(src, own, held[count + i], ll.at[i]))
            copies[i].begin()
        for line in lines:
            line.step(1)
        for part in late:
            part.begin()
        for part in early:
            part.forward()
        for copy in copies:
            copy.turn()
        for line in lines:
            line.step(2)
        for part in early:
            part.share()
        for part in late:
            part.forward()
        for part in late:
            part.share()
        for part in lines + planes:
            part.finish()
        for copy in copies:
            copy.finish()

    return pl.pallas_call(
        kernel,
        out_shape=tuple(shaped((n_dp * m.shape[0], m.shape[1]), m.dtype) for m in mats)
        + (
            shaped((n_line * rows_in.shape[0], rows_in.shape[1]), rows_in.dtype),
            shaped((n_line * order.shape[0], order.shape[1]), order.dtype),
        ),
        in_specs=[in_any()] * (count + 2),
        out_specs=[in_any()] * (count + 2),
        scratch_shapes=[
            dma_sems(count, 9),
            dma_sems(count, 9),
            dma_sems(count, 2),
            dma_sems(parts + 1, 2, n_line - 1),
            dma_sems(parts + 1, 2, n_line - 1),
            dma_sems(2, 2),
        ]
        + [vmem_like(m) for m in (*mats, rows_in, order)],
        compiler_params=comm_params(1),
        name="first_gather",
    )(*mats, rows_in, order)


CHUNKS = 8
LAST_CHUNKS = 8


def line_scratch(n_line, span, width, chunks):
    hops = n_line - 1
    return [
        pltpu.VMEM((chunks, 2, hops, span, width), jnp.bfloat16),
        dma_sems(chunks, 2, hops),
        dma_sems(chunks, 2, hops),
        dma_sems(chunks, 2, hops),
        dma_sems(chunks, 2, hops),
        pltpu.VMEM((span, width), jnp.float32),
    ]


def sum_rows_and_spread(place, terms, scratch, finish_rows, spread, between):
    inbox, rs, rr, gs, gr, total = scratch
    span = total.shape[0]
    count = inbox.shape[0]
    rows = span * count
    hops = place.n_line - 1
    sums = [
        ReduceLine(place, terms, rows, c * span, span, inbox.at[c], rs.at[c], rr.at[c])
        for c in range(count)
    ]
    gathers = []
    if spread is not None:
        gathers = [
            GatherLine(place, spread, rows, c * span, span, gs.at[c], gr.at[c])
            for c in range(count)
        ]
    sums[0].ends()

    def total_of(c):
        sums[c].total(total)
        finish_rows(c, pl.ds(c * span, span), total)
        if gathers:
            gathers[c].step(0)

    stages = [lambda c, k=k: sums[c].hop(k) for k in range(hops - 1)] + [total_of]
    lags = [LAGS[min(k, len(LAGS) - 1)] for k in range(hops)]
    if gathers:
        stages += [lambda c, k=k: gathers[c].step(k) for k in range(1, hops)]
        lags += [lags[-1] + LAG_STEP * k for k in range(1, hops)]
    for i in range(count + lags[-1]):
        if i < count:
            sums[i].sent()
        if i + 1 < count:
            sums[i + 1].ends()
        for work, lag in zip(stages, lags):
            if 0 <= i - lag < count:
                work(i - lag)
        if i in between:
            between[i]()
    for part in gathers + sums:
        part.finish()


LAGS = (0, 1, 1)
LAG_STEP = 1


def middle_gather(n_dp, n_line, terms, tokens, gain, mats):
    rows, width = tokens.shape
    count = len(mats)

    def kernel(*refs):
        s, tok, gain_ref = refs[:3]
        srcs = refs[3 : 3 + count]
        after, hidden = refs[3 + count : 5 + count]
        dsts = refs[5 + count : 5 + 2 * count]
        ps, pr, pl_sem = refs[5 + 2 * count : 8 + 2 * count]
        held = refs[8 + 2 * count : 8 + 3 * count]
        scratch = refs[8 + 3 * count :]
        place = Place(n_dp, n_line)
        place.meet()
        planes = [
            GatherPlane(place, a, b, ps.at[i], pr.at[i], pl_sem.at[i], held[i])
            for i, (a, b) in enumerate(zip(srcs, dsts))
        ]
        planes[0].begin()

        def norm(c, here, total):
            values = tok[here].astype(jnp.float32) + total[...]
            after[here] = values
            low = rms_scale(values, gain_ref[...]).astype(jnp.bfloat16)
            first = pl.multiple_of(place.t * rows, 16) + c * total.shape[0]
            hidden[pl.ds(pl.multiple_of(first, 16), total.shape[0])] = low

        between = {
            2: planes[1].begin,
            6: planes[0].forward,
            8: planes[1].forward,
            9: planes[0].share,
            10: planes[1].share,
        }
        sum_rows_and_spread(place, s, scratch, norm, hidden, between)
        for part in planes:
            part.finish()

    return pl.pallas_call(
        kernel,
        out_shape=(
            shaped((rows, width), jnp.float32),
            shaped((n_line * rows, width), jnp.bfloat16),
        )
        + tuple(shaped((n_dp * m.shape[0], m.shape[1]), m.dtype) for m in mats),
        in_specs=[in_vmem()] * 3 + [in_any()] * count,
        out_specs=[in_vmem()] * 2 + [in_any()] * count,
        scratch_shapes=[dma_sems(count, 9), dma_sems(count, 9), dma_sems(count, 2)]
        + [vmem_like(m) for m in mats]
        + line_scratch(n_line, rows // CHUNKS, width, CHUNKS),
        compiler_params=comm_params(2),
        name="middle_gather",
    )(terms, tokens, gain, *mats)


def middle_sums(
    n_dp, n_line, terms, after, gain, grad_in, mat, hidden, grad_up, product, down, down_rest
):
    rows, width = after.shape
    block = mat.shape[0] // n_dp
    wide = grad_up.shape[1]
    spread_rows = n_line * rows

    def kernel(*refs):
        s, after_ref, gain_ref, g_ref, src = refs[:5]
        hid_far, gu_far, pr_far, dw_far, dw_rest = refs[5:10]
        grad_after, gain_sum, spread, result, up_far, feed_far = refs[10:16]
        hid, gu, pr, dw, up_out, feed, sems = refs[16:23]
        rest = refs[23:]
        cut = dw_far.shape[1]
        fetch = Fetch(
            [
                (hid_far, hid),
                (gu_far, gu),
                (pr_far, pr),
                (dw_far, dw.at[:, pl.ds(0, cut)]),
                (feed, feed_far),
                (up_out.at[0], up_far.at[pl.ds(0, width // 2)]),
                (up_out.at[1], up_far.at[pl.ds(width // 2, width // 2)]),
                (dw_rest, dw.at[:, pl.ds(cut, wide - cut)]),
            ],
            sems,
        )
        fetch.start(0, 1, 2, 3, 7)
        place = Place(n_dp, n_line)
        place.meet()
        plane = ReducePlane(place, src, rest[:7])
        scratch = rest[7:]
        plane.begin()
        gain_sum[...] = jnp.zeros_like(gain_sum)

        def norm(c, here, total):
            grad = total[...]
            grad_rows, normed = norm_back(after_ref[here], gain_ref[...], grad)
            gain_sum[...] += jnp.sum(grad * normed, axis=0, keepdims=True)
            both = g_ref[here].astype(jnp.float32) + grad_rows
            grad_after[here] = both
            first = pl.multiple_of(place.t * rows, 16) + c * total.shape[0]
            spread[pl.ds(pl.multiple_of(first, 16), total.shape[0])] = both.astype(jnp.bfloat16)

        def feed_part(i):
            cols = pl.ds(i * (width // 4), width // 4)
            feed[:, cols] = times_trans(pr[...], dw[cols]).astype(jnp.bfloat16)

        def up_part(i):
            cols = pl.ds(i * (width // 4), width // 4)
            here = pl.ds((i % 2) * (width // 4), width // 4)
            up_out[i // 2, here] = trans_times(hid[:, cols], gu[...]).astype(jnp.bfloat16)

        def early():
            plane.cores()
            fetch.wait(0, 1)

        def two():
            up_part(0)

        def three():
            up_part(1)
            fetch.start(5)

        def four():
            up_part(2)

        def five():
            up_part(3)
            fetch.start(6)
            fetch.wait(2, 3, 7)

        def six():
            feed_part(0)

        def seven():
            plane.turn()
            feed_part(1)

        def eight():
            feed_part(2)

        def nine():
            feed_part(3)
            fetch.start(4)

        steps = {1: early, 2: two, 3: three, 4: four, 5: five, 6: six, 7: seven, 8: eight, 9: nine}
        sum_rows_and_spread(place, s, scratch, norm, spread, steps)
        plane.finish(result)
        fetch.wait(4, 5, 6)

    low, full = jnp.bfloat16, jnp.float32
    near, far = in_vmem(), in_any()
    return pl.pallas_call(
        kernel,
        out_shape=(
            shaped((rows, width), full),
            shaped((1, width), full),
            shaped((spread_rows, width), low),
            shaped((block, mat.shape[1]), low),
            shaped((width, wide), low),
            shaped((spread_rows, width), low),
        ),
        in_specs=[near] * 4 + [far] * 6,
        out_specs=[near] * 4 + [far] * 2,
        scratch_shapes=[vmem_like(m) for m in (hidden, grad_up, product, mat)]
        + [
            pltpu.VMEM((2, width // 2, wide), low),
            pltpu.VMEM((spread_rows, width), low),
            dma_sems(8),
        ]
        + ReducePlane.scratch(block, mat.shape[1])
        + line_scratch(n_line, rows // CHUNKS, width, CHUNKS),
        compiler_params=comm_params(3),
        name="middle_sums",
    )(terms, after, gain, grad_in, mat, hidden, grad_up, product, down, down_rest)


class Exchange:
    def __init__(self, place, axis, src, slots, send, recv, local):
        self.p, self.src, self.slots = place, src, slots
        self.over_dp = axis == "dp"
        self.size = place.n_dp if self.over_dp else place.n_line
        self.me = place.d if self.over_dp else place.t
        self.send, self.recv, self.local = send, recv, local

    def copy(self, i):
        to = lax.rem(self.me + i, self.size)
        device = (to, self.p.t) if self.over_dp else (self.p.d, to)
        return remote(
            self.src, self.slots.at[self.me], self.send.at[i - 1], self.recv.at[i - 1], device
        )

    def mine(self):
        return pltpu.make_async_copy(self.src, self.slots.at[self.me], self.local)

    def begin(self):
        for i in range(1, self.size):
            self.copy(i).start()
        self.mine().start()

    def wait(self):
        self.mine().wait()
        for i in range(1, self.size):
            self.copy(i).wait()

    def finish(self):
        self.wait()
        total = self.slots[0]
        for i in range(1, self.size):
            total = total + self.slots[i]
        return total


def last_sums(n_dp, n_line, terms, tokens, gain, grad_after, small, mats):
    rows, width = tokens.shape
    count = len(mats)
    per = len(ReducePlane.scratch(16, 128))

    def kernel(*refs):
        s, tok, gain_ref, g_ref, small_ref = refs[:5]
        srcs = refs[5 : 5 + count]
        grad_tok, small_out, first_out = refs[5 + count : 8 + count]
        results = refs[8 + count : 8 + 2 * count]
        rest = refs[8 + 2 * count :]
        own_first, row_sum = rest[count * per : count * per + 2]
        slots_a, slots_b, slots_c, slots_d = rest[count * per + 2 : count * per + 6]
        xs, xr, xl = rest[count * per + 6 : count * per + 9]
        scratch = rest[count * per + 9 :]
        place = Place(n_dp, n_line)
        place.meet(True)
        planes = [
            ReducePlane(place, srcs[i], rest[i * per : (i + 1) * per]) for i in range(count)
        ]
        for part in planes:
            part.begin()
        early = Exchange(place, "dp", small_ref, slots_a, xs.at[0], xr.at[0], xl.at[0])
        early.begin()
        own_first[...] = jnp.zeros_like(own_first)

        def norm(c, here, total):
            grad = total[...]
            grad_rows, normed = norm_back(tok[here].astype(jnp.float32), gain_ref[...], grad)
            own_first[...] += jnp.sum(grad * normed, axis=0, keepdims=True)
            grad_tok[here] = g_ref[here] + grad_rows

        def cores():
            for part in planes:
                part.cores()

        def turn():
            for part in planes:
                part.turn()

        sum_rows_and_spread(place, s, scratch, norm, None, {0: cores, 5: turn})
        first = Exchange(place, "dp", own_first, slots_b, xs.at[1], xr.at[1], xl.at[1])
        first.begin()
        small_out[...] = early.finish()
        row_sum[0:1] = small_out[0:1]
        row_sum[1:2] = first.finish()
        both = Exchange(place, "tensor", row_sum, slots_c, xs.at[2], xr.at[2], xl.at[2])
        both.begin()
        for part, result in zip(planes, results):
            part.finish(result)
        first_out[...] = both.finish()

    return pl.pallas_call(
        kernel,
        out_shape=(
            shaped((rows, width), jnp.float32),
            shaped(small.shape, jnp.float32),
            shaped((2, width), jnp.float32),
        )
        + tuple(shaped((m.shape[0] // n_dp, m.shape[1]), jnp.bfloat16) for m in mats),
        in_specs=[in_vmem()] * 5 + [in_any()] * count,
        out_specs=[in_vmem()] * (3 + count),
        scratch_shapes=sum([ReducePlane.scratch(m.shape[0] // n_dp, m.shape[1]) for m in mats], [])
        + [
            pltpu.VMEM((1, width), jnp.float32),
            pltpu.VMEM((2, width), jnp.float32),
            pltpu.VMEM((n_dp,) + small.shape, jnp.float32),
            pltpu.VMEM((n_dp, 1, width), jnp.float32),
            pltpu.VMEM((n_line, 2, width), jnp.float32),
            pltpu.VMEM((1, width), jnp.float32),
            dma_sems(3, n_dp),
            dma_sems(3, n_dp),
            dma_sems(3),
        ]
        + line_scratch(n_line, rows // LAST_CHUNKS, width, LAST_CHUNKS),
        compiler_params=comm_params(4),
        name="last_sums",
    )(terms, tokens, gain, grad_after, small, *mats)


def loop(count, body, unroll=1):
    def step(i, carry):
        body(i)
        return carry

    lax.fori_loop(0, count, step, None, unroll=unroll)


def tile_rows(i, size, ahead=0):
    return pl.ds(pl.multiple_of(i * size + ahead, 8), size)


def moved_up(values, distance, count):
    size = values.shape[0]
    return pltpu.roll(values, (size - distance) % size, 0)[:count]


def take_lanes(ref, here):
    return jnp.concatenate([ref[c, here] for c in range(ref.shape[0])], axis=1)


def put_lanes(ref, here, values):
    for c in range(ref.shape[0]):
        ref[c, here] = values[:, c * LANES : (c + 1) * LANES]


def gelu_parts(values):
    inner = GELU_C * (values + 0.044715 * (values * values * values))
    tanh = jnp.tanh(inner)
    half = 0.5 * (1.0 + tanh)
    slope = half + 0.5 * values * (1.0 - tanh * tanh) * GELU_C * (
        1.0 + 3.0 * 0.044715 * (values * values)
    )
    return values * half, slope


GELU_C = 0.7978845608028654
RIM = 128
LANES = 128
TILE = 16


def one_minus_exp(values, exponential):
    series = jnp.ones_like(values)
    for term in range(9, 1, -1):
        series = 1.0 + values * (1.0 / term) * series
    return jnp.where(values > -0.35, -values * series, 1.0 - exponential)


def rate_and_scale(pre_recur, soft, start):
    sr = jax.nn.sigmoid(pre_recur)
    log_rate = -rate_scale * sr * soft
    decay = jnp.exp(log_rate)
    rate = jnp.where(start, 0.0, decay)
    scale = jnp.where(start, 1.0, jnp.sqrt(one_minus_exp(2.0 * log_rate, decay * decay)))
    return sr, rate, scale


class RimSwap:
    def __init__(self, place, own):
        self.odd = lax.rem(place.t, 2)
        self.partner = (place.d, place.t + 1 - 2 * self.odd)
        self.first = pl.multiple_of(RIM - RIM * self.odd, RIM)
        self.edge = pl.ds(pl.multiple_of((1 - self.odd) * own + self.odd * RIM, RIM), RIM)
        self.over_there = pl.ds(pl.multiple_of(self.odd * (own + RIM), RIM), RIM)
        self.beyond = pl.ds(pl.multiple_of((1 - self.odd) * (own + RIM), RIM), RIM)

    def block(self, index, size):
        return pl.ds(pl.multiple_of(self.first + index * size, RIM), size)


LATE_SHARE = 4


def recur_forward(
    n_dp,
    n_line,
    tok_all,
    cot,
    to_place,
    to_stored,
    x_full,
    y_full,
    out_full,
    gain,
    gates,
    taps,
    soft,
    flags,
):
    rows, width = tok_all.shape
    count, own = taps.shape
    size = gates.shape[0]
    wide = own + 2 * RIM
    blocks = (wide - RIM) // size
    chunk = rows // 8
    cot_rows = cot.shape[0] - cot.shape[0] // LATE_SHARE
    parts = 1

    def kernel(*refs):
        (tok_far, cot_ref, plc, sto, wx_far, wy_far, wo_far, gain_ref, gates_in, cw, sp, fl) = refs[:12]
        far, gw, cot_all = refs[12:23], refs[23], refs[24]
        tok, wx, wy, wo = refs[25:29]
        results = refs[29:40]
        hp, xext, y, conv_low, conv, pre_r, pre_i, rate, state, merged_st, terms = results
        (h, xf, local, cum, merged, agg, slots, hs, hr, es, er, el, gs, gr, gl) = refs[40:55]
        in_sems, out_sems, cot_held = refs[55:]
        fetch = Fetch(((tok_far, tok), (wx_far, wx), (wy_far, wy), (wo_far, wo)), in_sems)
        store = Fetch(zip(results, far), out_sems)
        fetch.start(0, 1, 2, 3)
        place = Place(n_dp, n_line)
        place.meet(True)
        swap = RimSwap(place, own)
        for side in range(2):
            first = side * wide
            gw[:, first : first + RIM] = jnp.zeros((size, RIM), jnp.bfloat16)
            gw[:, first + RIM : first + RIM + own] = gates_in[:, side * own : (side + 1) * own]
            gw[:, first + RIM + own : first + wide] = jnp.zeros((size, RIM), jnp.bfloat16)
        own_cot = cot_all.at[pl.ds(pl.multiple_of(place.t * cot_rows, 16), cot_rows)]
        cot_ref = cot_ref.at[pl.ds(0, cot_rows)]
        keep = Kept(cot_ref, own_cot, cot_held, gl)
        keep.begin()
        span = cot_rows // parts
        lines = [
            GatherLine(place, cot_all, cot_rows, c * span, span, gs.at[c], gr.at[c])
            for c in range(parts)
        ]
        for c, line in enumerate(lines):
            line.step(0, cot_ref.at[pl.ds(c * span, span)])

        def norm(i):
            here = tile_rows(i, TILE)
            h[here] = rms_scale(tok[here].astype(jnp.float32), gain_ref[...]).astype(jnp.bfloat16)

        fetch.wait(0)
        loop(rows // TILE, norm)
        fetch.wait(1)

        def project(i):
            here = tile_rows(i, 128)
            hp[here] = plain_dot(plc[here], h[...]).astype(jnp.bfloat16)
            xext[tile_rows(i, 128, 16)] = plain_dot(hp[here], wx[...]).astype(jnp.bfloat16)

        loop(rows // 128, project)
        store.start(0)
        edge = remote(
            xext.at[pl.ds(rows, 16)],
            xext.at[pl.ds(0, 16)],
            hs.at[0],
            hr.at[0],
            (lax.rem(place.d + 1, n_dp), place.t),
        )
        edge.start()
        keep.turn()
        for line in lines:
            line.step(1)

        def project_y(i):
            here = tile_rows(i, 128)
            y[here] = plain_dot(hp[here], wy[...])

        fetch.wait(2)
        loop(rows // 128, project_y)
        store.start(2)
        edge.wait()
        top = xext[pl.ds(0, 16)]
        xext[pl.ds(0, 16)] = jnp.where(place.d > 0, top, jnp.zeros_like(top))
        store.start(1)

        def widen(i):
            xf[tile_rows(i, TILE)] = xext[tile_rows(i, TILE)].astype(jnp.float32)

        loop(rows // TILE + 1, widen)

        def convolve(i):
            here = tile_rows(i, TILE)
            near = xf[pl.ds(pl.multiple_of(i * TILE + 8, 8), TILE + 8)]
            same = fl[tile_rows(i, TILE, 8)]
            total = cw[0:1] * near[8:]
            for k in range(1, count):
                total += cw[k : k + 1] * moved_up(near, 8 - k, TILE) * same[:, k : k + 1]
            conv[here] = total
            conv_low[here, RIM : RIM + own] = total.astype(jnp.bfloat16)

        loop(rows // TILE, convolve)
        store.start(4)
        rim = remote(
            conv_low.at[:, swap.edge],
            conv_low.at[:, swap.over_there],
            hs.at[1],
            hr.at[1],
            swap.partner,
        )
        rim.start()
        for i in range(blocks):
            index = lax.rem(i + swap.odd, blocks)
            cols = swap.block(index, size)
            other = pl.ds(pl.multiple_of(wide + swap.first + index * size, RIM), size)
            if i == blocks - 1:
                rim.wait()
            pre_r[:, cols] = plain_dot(conv_low[:, cols], gw[:, cols])
            pre_i[:, cols] = plain_dot(conv_low[:, cols], gw[:, other])

        store.start(3, 5, 6)

        def drive(i):
            here = tile_rows(i, TILE)
            start = fl[tile_rows(i, TILE, 8)][:, 0:1] > 0.0
            own_cols = pl.ds(RIM, own)
            _, decay, scale = rate_and_scale(pre_r[here, own_cols], sp[...], start)
            put_lanes(rate, here, decay)
            put_lanes(local, here, conv[here] * jax.nn.sigmoid(pre_i[here, own_cols]) * scale)

        loop(rows // TILE, drive)
        store.start(7)
        for line in lines:
            line.step(2)
        groups = own // LANES

        def scan(i, carry):
            here = pl.ds(i, 8, chunk)
            result = []
            for c in range(groups):
                product, total = carry[c]
                r = rate[c, here]
                product = product * r
                total = total * r + local[c, here]
                cum[c, here] = product
                local[c, here] = total
                result.append((product, total))
            return tuple(result)

        blank = (jnp.ones((8, LANES), jnp.float32), jnp.zeros((8, LANES), jnp.float32))
        lax.fori_loop(0, chunk, scan, (blank,) * groups)
        product, total = jnp.ones((1, own), jnp.float32), jnp.zeros((1, own), jnp.float32)
        for j in range(8):
            last = pl.ds(j * chunk + chunk - 1, 1)
            total = take_lanes(local, last) + take_lanes(cum, last) * total
            product = product * take_lanes(cum, last)
        agg[0:1] = product
        agg[1:2] = total
        swap_all = Exchange(place, "dp", agg, slots, es, er, el)
        swap_all.begin()
        swap_all.wait()
        entry = jnp.zeros((1, own), jnp.float32)
        for q in range(n_dp):
            longer = slots[q, 1:2] + slots[q, 0:1] * entry
            entry = jnp.where(q < place.d, longer, entry)
        state[pl.ds(0, 8)] = jnp.broadcast_to(entry, (8, own))
        for j in range(8):

            def settle(i, entry=entry):
                here = tile_rows(i, TILE, j * chunk)
                values = take_lanes(local, here) + take_lanes(cum, here) * entry
                state[tile_rows(i, TILE, j * chunk + 8)] = values
                merged[here] = (values * gelu_parts(y[here])[0]).astype(jnp.bfloat16)

            loop(chunk // TILE, settle)
            last = pl.ds(j * chunk + chunk - 1, 1)
            entry = take_lanes(local, last) + take_lanes(cum, last) * entry
        store.start(8)
        merged_st[...] = plain_dot(sto[...], merged[...]).astype(jnp.bfloat16)

        store.start(9)
        fetch.wait(3)

        def mix(i):
            some = tile_rows(i, 512)
            terms[:, pl.ds(pl.multiple_of(i * 512, 512), 512)] = times_trans(
                merged_st[...], wo[some, :]
            ).astype(jnp.bfloat16)

        loop(width // 512, mix)
        for line in lines:
            line.finish()
        keep.finish()
        store.start(10)
        store.wait(*range(11))

    low, full = jnp.bfloat16, jnp.float32
    results = (
        shaped((rows, width), low),
        shaped((rows + 16, own), low),
        shaped((rows, own), full),
        shaped((rows, wide), low),
        shaped((rows, own), full),
        shaped((rows, wide), full),
        shaped((rows, wide), full),
        shaped((own // LANES, rows, LANES), full),
        shaped((rows + 8, own), full),
        shaped((rows, own), low),
        shaped((rows, width), low),
    )
    near, far = in_vmem(), in_any()
    return pl.pallas_call(
        kernel,
        out_shape=results
        + (shaped((size, 2 * wide), low), shaped((n_line * cot_rows, width), low)),
        in_specs=[far, far, near, near, far, far, far] + [near] * 5,
        out_specs=[far] * 11 + [near, far],
        scratch_shapes=[vmem_like(m) for m in (tok_all, x_full, y_full, out_full) + results]
        + [
            pltpu.VMEM((rows, width), low),
            pltpu.VMEM((rows + 16, own), full),
            pltpu.VMEM((own // LANES, rows, LANES), full),
            pltpu.VMEM((own // LANES, rows, LANES), full),
            pltpu.VMEM((rows, own), low),
            pltpu.VMEM((2, own), full),
            pltpu.VMEM((n_dp, 2, own), full),
            dma_sems(2),
            dma_sems(2),
            dma_sems(n_dp),
            dma_sems(n_dp),
            pltpu.SemaphoreType.DMA,
            dma_sems(parts, 2, n_line - 1),
            dma_sems(parts, 2, n_line - 1),
            dma_sems(2),
            dma_sems(4),
            dma_sems(11),
            pltpu.VMEM((cot_rows, width), low),
        ],
        compiler_params=comm_params(5),
        name="recur_forward",
    )(
        tok_all,
        cot,
        to_place,
        to_stored,
        x_full,
        y_full,
        out_full,
        gain,
        gates,
        taps,
        soft,
        flags,
    )


class RowProducts:
    def __init__(self, left, right, far, stage, sems):
        self.left, self.right, self.far, self.stage, self.sems = left, right, far, stage, sems
        self.part = stage.shape[1]
        self.count = far.shape[0] // self.part

    def slot(self, i):
        return self.stage.at[i % 2, :, pl.ds(0, self.far.shape[1])]

    def copy(self, i):
        some = pl.ds(i * self.part, self.part)
        return pltpu.make_async_copy(self.slot(i), self.far.at[some], self.sems.at[i])

    def run(self):
        for i in range(self.count):
            if i >= 2:
                self.copy(i - 2).wait()
            some = pl.ds(i * self.part, self.part)
            self.slot(i)[...] = trans_times(self.left[:, some], self.right[...]).astype(
                jnp.bfloat16
            )
            self.copy(i).start()

    def finish(self):
        self.copy(self.count - 2).wait()
        self.copy(self.count - 1).wait()


def recur_backward(
    n_dp,
    n_line,
    mixer_in,
    to_place,
    to_stored,
    x_full,
    y_full,
    out_full,
    gates,
    taps,
    soft,
    slope,
    flags,
    kept,
    weight_terms,
    row_terms,
    hidden_place,
    merged_stored,
):
    rows, width = mixer_in.shape
    count, own = taps.shape
    size = gates.shape[0]
    wide = own + 2 * RIM
    blocks = (wide - RIM) // size
    chunk = rows // 8
    own_rows = rows // n_line
    parts = 4
    span = own_rows // parts

    def kernel(*refs):
        (mix_far, plc, sto, wx_far, wy_far, wo_far, gw, cw, sp, sg, fl) = refs[:11]
        kept_far, weights, feed_far, hp_far, merged_far = refs[11:19], *refs[19:23]
        (gate_grads, tap_grads, decay_grad, terms_far, weight_sum, row_sum) = refs[23:29]
        out_far, xy_far = refs[29:31]
        mix, wy, wo, feed, merged = refs[31:36]
        (xext, y, conv_low, conv, pre_r, pre_i, rate, state) = refs[36:44]
        (gxy, mp, gm, lam, reach, gp_r, gp_i, grad, spread, rim_out, rim_in) = refs[44:55]
        (ret_out, ret_in, tap_sums, decay_sums, ends, agg, slots) = refs[55:62]
        (hs, hr, es, er, el, in_sems, out_sems, inbox, ls, lr, total) = refs[62:73]
        stage, stage_sems = refs[73:75]
        hp, terms, wx = mix, mix, wo
        fetch = Fetch(
            [
                (mix_far, mix),
                (wo_far, wo),
                (kept_far[1], y),
                (kept_far[7], state),
                (kept_far[6], rate),
                (kept_far[4], pre_r),
                (kept_far[5], pre_i),
                (kept_far[3], conv),
                (kept_far[2], conv_low),
                (kept_far[0], xext),
                (wx_far, wx),
                (wy_far, wy),
                (feed_far, feed),
                (merged_far, merged),
                (hp_far, hp),
            ],
            in_sems,
        )
        fetch.start(12, 0, 1, 13)
        store = Fetch(((terms, terms_far),), out_sems)
        out_rows = RowProducts(mix, merged, out_far, stage, stage_sems.at[0])
        xy_rows = RowProducts(hp, gxy, xy_far, stage, stage_sems.at[1])
        place = Place(n_dp, n_line)
        place.meet(True)
        plane = ReducePlane(place, weights, refs[75:])
        plane.begin()
        lines = [
            ReduceLine(place, feed, own_rows, c * span, span, inbox.at[c], ls.at[c], lr.at[c])
            for c in range(parts)
        ]

        def send(c):
            if c > 0:
                lines[c - 1].sent()
            if c < parts:
                lines[c].ends()

        def add_up(c):
            lines[c].total(total)
            row_sum[pl.ds(c * span, span)] = total[...].astype(jnp.bfloat16)

        fetch.wait(12)
        send(0)
        fetch.start(*range(2, 10), 11)
        swap = RimSwap(place, own)
        own_cols = pl.ds(RIM, own)

        def project(i):
            here = tile_rows(i, 128)
            mp[here] = plain_dot(plc[here], mix[...]).astype(jnp.bfloat16)
            gm[here] = plain_dot(mp[here], wo[...])

        fetch.wait(0, 1)
        loop(rows // 128, project)
        fetch.start(10)
        fetch.wait(13)
        out_rows.run()
        fetch.start(14)

        def split(i):
            here = tile_rows(i, TILE)
            branch, slope_y = gelu_parts(y[here])
            grads = gm[here]
            put_lanes(lam, here, grads * branch)
            values = state[tile_rows(i, TILE, 8)]
            gxy[here, own:] = (grads * values * slope_y).astype(jnp.bfloat16)

        fetch.wait(2, 3)
        loop(rows // TILE, split)
        send(1)
        lines[0].hop(0)
        fetch.wait(4)
        groups = own // LANES

        def scan(i, carry):
            here = pl.ds(chunk - 1 - i, 8, chunk)
            result = []
            for c in range(groups):
                product, message = carry[c]
                r = rate[c, here]
                value = lam[c, here] + message
                lam[c, here] = value
                reach[c, here] = product
                result.append((product * r, value * r))
            return tuple(result)

        blank = (jnp.ones((8, LANES), jnp.float32), jnp.zeros((8, LANES), jnp.float32))
        done = lax.fori_loop(0, chunk, scan, (blank,) * groups)
        for c in range(groups):
            lanes = pl.ds(c * LANES, LANES)
            ends[0, :, lanes] = done[c][0]
            ends[1, :, lanes] = done[c][1]
        product, message = jnp.ones((1, own), jnp.float32), jnp.zeros((1, own), jnp.float32)
        for j in reversed(range(8)):
            message = ends[1, j : j + 1] + ends[0, j : j + 1] * message
            product = product * ends[0, j : j + 1]
        agg[0:1] = product
        agg[1:2] = message
        swap_all = Exchange(place, "dp", agg, slots, es, er, el)
        swap_all.begin()
        plane.cores()
        swap_all.wait()
        lines[0].hop(1)
        entry = jnp.zeros((1, own), jnp.float32)
        for q in reversed(range(n_dp)):
            longer = slots[q, 1:2] + slots[q, 0:1] * entry
            entry = jnp.where(q > place.d, longer, entry)
        fetch.wait(5, 6, 7)
        for ref in (tap_sums, decay_sums):
            ref[...] = jnp.zeros_like(ref)
        for ref in (gp_r, gp_i):
            ref[:, 0:RIM] = jnp.zeros((rows, RIM), jnp.bfloat16)
            ref[:, RIM + own :] = jnp.zeros((rows, RIM), jnp.bfloat16)
        grad[pl.ds(0, 8)] = jnp.zeros((8, own), jnp.float32)
        grad[pl.ds(rows + 8, 8)] = jnp.zeros((8, own), jnp.float32)
        for j in reversed(range(8)):

            def back(i, entry=entry):
                here = tile_rows(i, TILE, j * chunk)
                flag = fl[tile_rows(i, TILE, j * chunk + 8)]
                start = flag[:, 0:1] > 0.0
                values = take_lanes(lam, here) + take_lanes(reach, here) * entry
                before = moved_up(
                    state[pl.ds(pl.multiple_of(j * chunk + i * TILE, 8), TILE + 8)], 7, TILE
                )
                sr, decay, scale = rate_and_scale(pre_r[here, own_cols], sp[...], start)
                si = jax.nn.sigmoid(pre_i[here, own_cols])
                block = conv[here]
                driven = values * si
                log_grad = values * before * decay - block * driven * (decay * decay) / scale
                log_grad = jnp.where(start, 0.0, log_grad)
                inner = sr * log_grad
                gp_r[here, own_cols] = (
                    -rate_scale * sp[...] * inner * (1.0 - sr)
                ).astype(jnp.bfloat16)
                gp_i[here, own_cols] = (driven * block * (1.0 - si) * scale).astype(jnp.bfloat16)
                grad[tile_rows(i, TILE, j * chunk + 8)] = driven * scale
                decay_sums[...] += inner[:8] + inner[8:]

            loop(chunk // TILE, back)
            if j == 4:
                send(2)
                lines[1].hop(0)
            entry = ends[1, j : j + 1] + ends[0, j : j + 1] * entry
        lines[1].hop(1)
        add_up(0)
        decay_grad[...] = rate_scale * sg[...] * jnp.sum(decay_sums[...], axis=0, keepdims=True)

        for i in range(blocks):
            index = lax.rem(i + 2 - 2 * swap.odd, blocks)
            cols = swap.block(index, size)
            other = pl.ds(pl.multiple_of(wide + swap.first + index * size, RIM), size)
            spread[:, cols] = times_trans(gp_r[:, cols], gw[:, cols]) + times_trans(
                gp_i[:, cols], gw[:, other]
            )
            if i == 0:
                rim_out[...] = spread[:, swap.beyond].astype(jnp.bfloat16)
                rim = remote(rim_out, rim_in, hs.at[0], hr.at[0], swap.partner)
                rim.start()
        send(3)
        lines[2].hop(0)
        rim.wait()
        shared = pl.ds(pl.multiple_of((1 - swap.odd) * (own - RIM), RIM), RIM)

        def join(i):
            here = tile_rows(i, TILE)
            there = tile_rows(i, TILE, 8)
            grad[there] += spread[here, own_cols]
            grad[there, shared] += rim_in[here].astype(jnp.float32)

        loop(rows // TILE, join)

        near = grad[pl.ds(0, 16)]
        back_rows = jnp.zeros((8, own), jnp.float32)
        for k in range(1, count):
            masked = near * fl[pl.ds(0, 16)][:, k : k + 1]
            back_rows += cw[k : k + 1] * moved_up(masked, k, 8)
        ret_out[...] = back_rows
        ret = remote(
            ret_out,
            ret_in,
            hs.at[1],
            hr.at[1],
            (lax.rem(place.d + n_dp - 1, n_dp), place.t),
        )
        ret.start()
        fetch.wait(8)
        for i in range(blocks):
            cols = swap.block(i, size)
            spread[0:size, cols] = trans_times(conv_low[:, cols], gp_r[:, cols])
            spread[size : 2 * size, cols] = trans_times(conv_low[:, cols], gp_i[:, cols])
        gate_grads[:, 0:own] = spread[0:size, own_cols].astype(jnp.bfloat16)
        gate_grads[:, own:] = spread[size : 2 * size, own_cols].astype(jnp.bfloat16)

        def taps_back(i, added=None):
            here = tile_rows(i, TILE)
            start = pl.ds(pl.multiple_of(i * TILE + 8, 8), TILE + 8)
            after = grad[start]
            flag = fl[start]
            behind = xext[pl.ds(pl.multiple_of(i * TILE, 16), 2 * TILE)].astype(jnp.float32)
            total = cw[0:1] * after[:TILE]
            for k in range(count):
                if k > 0:
                    masked = after * flag[:, k : k + 1]
                    total += cw[k : k + 1] * moved_up(masked, k, TILE)
                    mine = masked[:TILE]
                else:
                    mine = after[:TILE]
                term = mine * moved_up(behind, 16 - k, TILE)
                tap_sums[k] += term[:8] + term[8:]
            if added is not None:
                total = total + jnp.concatenate([jnp.zeros((8, own), jnp.float32), added], axis=0)
            gxy[here, 0:own] = total.astype(jnp.bfloat16)

        fetch.wait(9)
        loop(rows // TILE - 1, taps_back)
        lines[2].hop(1)
        add_up(1)
        ret.wait()
        taps_back(rows // TILE - 1, jnp.where(place.d < n_dp - 1, ret_in[...], 0.0))
        tap_grads[...] = jnp.zeros_like(tap_grads)
        for k in range(count):
            tap_grads[k : k + 1] = jnp.sum(tap_sums[k], axis=0, keepdims=True)

        fetch.wait(14)
        out_rows.finish()
        plane.turn()
        xy_rows.run()
        send(4)
        lines[3].hop(0)

        def restore(i):
            here = tile_rows(i, 128)
            mp[here, 0 : 2 * own] = plain_dot(sto[here], gxy[...]).astype(jnp.bfloat16)

        loop(rows // 128, restore)

        def spread_back(i):
            some = tile_rows(i, 512)
            terms[:, pl.ds(pl.multiple_of(i * 512, 512), 512)] = (
                times_trans(mp[:, 0:own], wx[some]) + times_trans(mp[:, own : 2 * own], wy[some])
            ).astype(jnp.bfloat16)

        fetch.wait(10, 11)
        loop(width // 512, spread_back)
        store.start(0)
        lines[3].hop(1)
        add_up(2)
        plane.finish(weight_sum)
        add_up(3)
        for line in lines:
            line.finish()
        xy_rows.finish()
        store.wait(0)

    low, full = jnp.bfloat16, jnp.float32
    block = weight_terms.shape[0] // n_dp
    near, far = in_vmem(), in_any()
    return pl.pallas_call(
        kernel,
        out_shape=(
            shaped((size, 2 * own), low),
            shaped((8, own), full),
            shaped((1, own), full),
            shaped((rows, width), low),
            shaped((block, weight_terms.shape[1]), low),
            shaped((own_rows, width), low),
            shaped((width, own), low),
            shaped((width, 2 * own), low),
        ),
        in_specs=[far, near, near, far, far, far] + [near] * 5 + [far] * 12,
        out_specs=[near, near, near, far, near, near, far, far],
        scratch_shapes=[
            vmem_like(m) for m in (mixer_in, y_full, out_full, row_terms, merged_stored, *kept)
        ]
        + [
            pltpu.VMEM((rows, 2 * own), low),
            pltpu.VMEM((rows, width), low),
            pltpu.VMEM((rows, own), full),
            pltpu.VMEM((own // LANES, rows, LANES), full),
            pltpu.VMEM((own // LANES, rows, LANES), full),
            pltpu.VMEM((rows, wide), low),
            pltpu.VMEM((rows, wide), low),
            pltpu.VMEM((rows + 16, own), full),
            pltpu.VMEM((rows, wide), full),
            pltpu.VMEM((rows, RIM), low),
            pltpu.VMEM((rows, RIM), low),
            pltpu.VMEM((8, own), full),
            pltpu.VMEM((8, own), full),
            pltpu.VMEM((count, 8, own), full),
            pltpu.VMEM((8, own), full),
            pltpu.VMEM((2, 8, own), full),
            pltpu.VMEM((2, own), full),
            pltpu.VMEM((n_dp, 2, own), full),
            dma_sems(2),
            dma_sems(2),
            dma_sems(n_dp),
            dma_sems(n_dp),
            pltpu.SemaphoreType.DMA,
            dma_sems(15),
            dma_sems(1),
            pltpu.VMEM((parts, 2, n_line - 1, span, width), low),
            dma_sems(parts, 2, n_line - 1),
            dma_sems(parts, 2, n_line - 1),
            pltpu.VMEM((span, width), full),
            pltpu.VMEM((2, width // 5, 2 * own), low),
            dma_sems(2, 5),
        ]
        + ReducePlane.scratch(block, weight_terms.shape[1]),
        compiler_params=comm_params(6),
        name="recur_backward",
    )(
        mixer_in,
        to_place,
        to_stored,
        x_full,
        y_full,
        out_full,
        gates,
        taps,
        soft,
        slope,
        flags,
        *kept,
        weight_terms,
        row_terms,
        hidden_place,
        merged_stored,
    )


def column_parts(width, size=768):
    return [(c, min(size, width - c)) for c in range(0, width, size)]


def feed_forward(n_dp, n_line, hidden, gate, up, down, down_rest, grads, grad_own):
    rows, width = hidden.shape
    units = gate.shape[1]
    own_rows = grad_own.shape[0]
    ready = grads.shape[0] // n_line
    late = own_rows - ready
    part = width // 4

    def kernel(*refs):
        hid_far, wg_far, wu_far, wd_far, wd_rest, grads_far, own_far = refs[:7]
        product_far, gup_far, back_far, gdown_far, ggate_far = refs[7:12]
        hid, wg, wu, wd, grad, slope, branch, product, ggate, gup, stage, back = refs[12:24]
        in_sems, out_sems, stage_sems, ls, lr = refs[24:]
        place = Place(n_dp, n_line)
        cut = wd_far.shape[1]
        pairs = [
            (hid_far, hid),
            (wg_far, wg),
            (wu_far, wu),
            (wd_far, wd.at[:, pl.ds(0, cut)]),
            (wd_rest, wd.at[:, pl.ds(cut, units - cut)]),
        ]
        pairs += [
            (grads_far.at[pl.ds(q * ready, ready)], grad.at[pl.ds(q * own_rows, ready)])
            for q in range(n_line)
        ]
        mine = pl.ds(pl.multiple_of(place.t * own_rows + ready, 16), late)
        pairs.append((own_far.at[pl.ds(ready, late)], grad.at[mine]))
        fetch = Fetch(pairs, in_sems)
        fetch.start(*range(len(pairs)))
        store = Fetch(((product, product_far), (gup, gup_far), (back, back_far)), out_sems)
        place.meet()
        line = GatherLine(place, grad, own_rows, ready, late, ls, lr)
        line.step(0, own_far.at[pl.ds(ready, late)])
        columns = column_parts(units)
        fetch.wait(0, 1)
        for c, size in columns:
            cols = pl.ds(c, size)

            def gates(i, cols=cols):
                here = tile_rows(i, 256)
                branch[here, cols] = plain_dot(hid[here], wg[:, cols])

            loop(rows // 256, gates)
        line.step(1)
        fetch.wait(2)
        for c, size in columns:
            cols = pl.ds(c, size)

            def ups(i, cols=cols):
                here = tile_rows(i, 256)
                value = plain_dot(hid[here], wu[:, cols])
                active, bend = gelu_parts(branch[here, cols])
                product[here, cols] = (active * value).astype(jnp.bfloat16)
                branch[here, cols] = active
                slope[here, cols] = bend * value

            loop(rows // 256, ups)
        store.start(0)
        line.step(2)
        fetch.wait(*range(5, len(pairs)))
        line.finish()

        down_rows = RowProducts(grad, product, gdown_far, stage, stage_sems.at[0])
        down_rows.run()
        fetch.wait(3, 4)
        for c, size in columns:
            cols = pl.ds(c, size)

            def backs(i, cols=cols):
                here = tile_rows(i, 256)
                value = plain_dot(grad[here], wd[:, cols])
                ggate[here, cols] = (value * slope[here, cols]).astype(jnp.bfloat16)
                gup[here, cols] = (value * branch[here, cols]).astype(jnp.bfloat16)

            loop(rows // 256, backs)
        store.start(1)
        for i in range(4):
            some = pl.ds(i * part, part)
            back[:, some] = (
                times_trans(ggate[...], wg[some]) + times_trans(gup[...], wu[some])
            ).astype(jnp.bfloat16)
        store.start(2)
        down_rows.finish()
        gate_rows = RowProducts(hid, ggate, ggate_far, stage, stage_sems.at[1])
        gate_rows.run()
        gate_rows.finish()
        store.wait(0, 1, 2)

    low, full = jnp.bfloat16, jnp.float32
    return pl.pallas_call(
        kernel,
        out_shape=(
            shaped((rows, units), low),
            shaped((rows, units), low),
            shaped((rows, width), low),
            shaped((width, units), low),
            shaped((width, units), low),
        ),
        in_specs=[in_any()] * 7,
        out_specs=[in_any()] * 5,
        scratch_shapes=[vmem_like(m) for m in (hidden, gate, up, gate)]
        + [
            pltpu.VMEM((n_line * own_rows, width), low),
            pltpu.VMEM((rows, units), full),
            pltpu.VMEM((rows, units), full),
            pltpu.VMEM((rows, units), low),
            pltpu.VMEM((rows, units), low),
            pltpu.VMEM((rows, units), low),
            pltpu.VMEM((2, part, units), low),
            pltpu.VMEM((rows, width), low),
            dma_sems(6 + n_line),
            dma_sems(3),
            dma_sems(2, 4),
            dma_sems(2, n_line - 1),
            dma_sems(2, n_line - 1),
        ],
        compiler_params=comm_params(7),
        name="feed_forward",
    )(hidden, gate, up, down, down_rest, grads, grad_own)


def matches(mesh):
    return mesh.shape["dp"] == 8 and mesh.shape["tensor"] == 4


def local_blocks(
    tokens,
    norm_gain,
    x_weight,
    y_weight,
    conv_weight,
    recur_gate_weight,
    input_gate_weight,
    decay_param,
    out_weight,
    mlp_gain,
    gate_weight,
    up_weight,
    down_weight,
    seq_lengths,
    token_order,
    cotangent,
):
    n_dp, n_tensor = lax.axis_size("dp"), lax.axis_size("tensor")
    tensor_index = lax.axis_index("tensor")
    dp_index = lax.axis_index("dp")
    tok_rows, width = tokens.shape
    row_count = tok_rows * n_tensor
    own_width = conv_weight.shape[1]
    kernel_taps = conv_weight.shape[0]
    edge_rows = kernel_taps - 1
    dp_width = norm_gain.shape[0]
    gate_rows = recur_gate_weight.shape[0]
    own_start = tensor_index * tok_rows

    gains = jnp.concatenate([norm_gain, mlp_gain])
    spare = gate_rows * 128 - gains.shape[0]
    gains = jnp.pad(gains, (0, spare)).reshape(gate_rows, 128)
    minor = jnp.concatenate([recur_gate_weight, input_gate_weight, gains], axis=1)
    own_order = (token_order - dp_index * row_count).astype(jnp.int32)
    order_rows = jnp.broadcast_to(own_order[None, :], (8, tok_rows))
    x_full, y_full, out_full, minor_full, tok_all, order_full = first_gather(
        n_dp, n_tensor, (x_weight, y_weight, out_weight.T, minor), tokens, order_rows
    )
    down_rows = down_weight.T
    cut = 2 * down_rows.shape[1] // 3
    late_up, late_down, _ = lax.optimization_barrier((up_weight, down_rows[:, :cut], tok_all))
    up_full = lax.all_gather(late_up, "dp", axis=0, tiled=True)
    down_full = lax.all_gather(late_down, "dp", axis=0, tiled=True)
    order_all = order_full.reshape(n_tensor, 8, tok_rows)[:, 0].reshape(row_count)
    gain_rows = minor_full[:, 2 * own_width :].reshape(n_dp, -1)
    first_gain = gain_rows[:, :dp_width].reshape(1, width).astype(jnp.float32)
    second_gain = gain_rows[:, dp_width : 2 * dp_width].reshape(1, width).astype(jnp.float32)
    row_index = jnp.arange(row_count, dtype=jnp.int32)
    hits = row_index[:, None] == order_all[None, :]
    to_place = hits.astype(jnp.bfloat16)
    to_stored = (order_all[:, None] == row_index[None, :]).astype(jnp.bfloat16)
    places = dp_index * row_count + jnp.arange(-8, row_count + 8, dtype=jnp.int32)
    inside = (jnp.arange(row_count + 16) >= 8) & (jnp.arange(row_count + 16) < row_count + 8)
    ends = jnp.cumsum(seq_lengths)
    segment = segment_of(places, ends)
    starts = (places == 0) | (segment != segment_of(places - 1, ends))
    columns = [starts] + [
        segment_of(places - shift, ends) == segment for shift in range(1, kernel_taps)
    ]
    columns += [jnp.zeros_like(starts)] * (8 - len(columns))
    flags = (jnp.stack(columns, axis=1) & inside[:, None]).astype(jnp.float32)
    live_own = (token_order < ends[-1]).astype(jnp.float32)
    grad_in_own = (cotangent.astype(jnp.float32) * live_own[:, None]).astype(jnp.bfloat16)
    soft = jax.nn.softplus(-decay_param).reshape(1, own_width)
    slope = jax.nn.sigmoid(-decay_param).reshape(1, own_width)
    hidden_place, *kept, merged_stored, mixer_terms, gates_wide, grad_rows = recur_forward(
        n_dp,
        n_tensor,
        tok_all,
        grad_in_own,
        to_place,
        to_stored,
        x_full,
        y_full,
        out_full,
        first_gain,
        minor_full,
        conv_weight,
        soft,
        flags,
    )
    after_own, hidden_two, gate_full, down_rest = middle_gather(
        n_dp, n_tensor, mixer_terms, tokens, second_gain, (gate_weight, down_rows[:, cut:])
    )
    product, grad_up_pre, back_terms, grad_down, grad_gate = feed_forward(
        n_dp,
        n_tensor,
        hidden_two,
        gate_full,
        up_full,
        down_full,
        down_rest,
        grad_rows,
        grad_in_own,
    )
    down_sum = lax.psum_scatter(grad_down, "dp", scatter_dimension=0, tiled=True)
    grad_after_own, second_part, mixer_in, gate_sum, grad_up, feed_terms = middle_sums(
        n_dp,
        n_tensor,
        back_terms,
        after_own,
        second_gain,
        grad_in_own,
        grad_gate,
        hidden_two,
        grad_up_pre,
        product,
        down_full,
        down_rest,
    )
    (
        gate_grads,
        tap_grads,
        decay_grad,
        one_terms,
        up_sum,
        feed_out,
        grad_out_mat,
        grad_xy_mat,
    ) = recur_backward(
        n_dp,
        n_tensor,
        mixer_in,
        to_place,
        to_stored,
        x_full,
        y_full,
        out_full,
        gates_wide,
        conv_weight,
        soft,
        slope,
        flags,
        kept,
        grad_up,
        feed_terms,
        hidden_place,
        merged_stored,
    )
    output = (after_own + feed_out.astype(jnp.float32)) * live_own[:, None]
    output = output.astype(jnp.bfloat16)
    small = jnp.concatenate(
        [
            second_part,
            tap_grads[:kernel_taps].reshape(1, -1),
            jnp.pad(decay_grad, ((0, 0), (0, width - own_width))),
            jnp.zeros((1, width), jnp.float32),
        ],
        axis=0,
    )
    grad_tokens, small_sum, gain_sums, xy_sum, out_sum, gates_sum = last_sums(
        n_dp,
        n_tensor,
        one_terms,
        tokens,
        first_gain,
        grad_after_own,
        small,
        (grad_xy_mat, grad_out_mat, gate_grads),
    )
    xy_sum, gates_sum = xy_sum.astype(jnp.float32), gates_sum.astype(jnp.float32)
    own_gains = lax.dynamic_slice_in_dim(gain_sums, dp_index * dp_width, dp_width, 1)
    return (
        output,
        grad_tokens,
        own_gains[1],
        xy_sum[:, :own_width],
        xy_sum[:, own_width:],
        small_sum[1].reshape(kernel_taps, own_width),
        gates_sum[:, :own_width],
        gates_sum[:, own_width:],
        small_sum[2, :own_width],
        out_sum.astype(jnp.float32).T,
        own_gains[0],
        gate_sum.astype(jnp.float32),
        up_sum.astype(jnp.float32),
        down_sum.astype(jnp.float32).T,
    )


def solution(mesh):
    in_specs = (
        P(("dp", "tensor"), None),
        P("dp"),
        P("dp", "tensor"),
        P("dp", "tensor"),
        P(None, "tensor"),
        P("dp", "tensor"),
        P("dp", "tensor"),
        P("tensor"),
        P("tensor", "dp"),
        P("dp"),
        P("dp", "tensor"),
        P("dp", "tensor"),
        P("tensor", "dp"),
        P(),
        P(("dp", "tensor")),
        P(("dp", "tensor"), None),
    )
    out_specs = (
        P(("dp", "tensor"), None),
        P(("dp", "tensor"), None),
        P("dp"),
        P("dp", "tensor"),
        P("dp", "tensor"),
        P(None, "tensor"),
        P("dp", "tensor"),
        P("dp", "tensor"),
        P("tensor"),
        P("tensor", "dp"),
        P("dp"),
        P("dp", "tensor"),
        P("dp", "tensor"),
        P("tensor", "dp"),
    )
    fits = matches(mesh)
    local = local_blocks if fits else local_general
    return jax.shard_map(local, mesh=mesh, in_specs=in_specs, out_specs=out_specs, check_vma=False)
```

```python
import jax
import jax.numpy as jnp
from jax import lax
from jax.experimental import pallas as pl
from jax.experimental.pallas import tpu as pltpu
from jax.sharding import PartitionSpec as P

epsilon = 1e-06
rate_scale = 8.0


def from_behind(block, axis, distance):
    devices = range(lax.axis_size(axis))
    route = [(i - distance, i) for i in devices if i - distance in devices]
    return lax.ppermute(block, axis, route)


def extended_2(array, sides, width):
    for axis, dim in sides:
        size, length = (lax.axis_size(axis), array.shape[dim])
        up = [(i, (i + 1) % size) for i in range(size - 1)]
        down = [(j, i) for i, j in up]
        last = lax.slice_in_dim(array, length - width, length, axis=dim)
        leading = lax.slice_in_dim(array, 0, width, axis=dim)
        before = lax.ppermute(last, axis, up)
        after = lax.ppermute(leading, axis, down)
        array = jnp.concatenate([before, array, after], axis=dim)
    return array


def entering(value, axis, join, neutral, backward):
    count, mine = (lax.axis_size(axis), lax.axis_index(axis))
    pieces = jax.tree.map(lambda part: lax.all_gather(part, axis), value)
    if backward:
        pieces = jax.tree.map(lambda part: part[::-1], pieces)
        mine = count - 1 - mine
    total = jax.tree.map(
        lambda part, zero: jnp.full_like(part, 0) + jnp.asarray(zero, part.dtype), value, neutral
    )

    def lap(position, total):
        longer = join(total, jax.tree.map(lambda part: part[position], pieces))
        return jax.tree.map(lambda new, old: jnp.where(position < mine, new, old), longer, total)

    return lax.fori_loop(0, count - 1, lap, total)


def rms_scale(values, gain):
    return values * lax.rsqrt(jnp.mean(values * values, axis=-1, keepdims=True) + epsilon) * gain


def norm_back(values, gain, grad):
    inv_root = lax.rsqrt(jnp.mean(values * values, axis=-1, keepdims=True) + epsilon)
    normed = values * inv_root
    upstream = grad * gain
    grad_values = inv_root * (
        upstream - normed * jnp.mean(upstream * normed, axis=-1, keepdims=True)
    )
    return (grad_values, normed)


def segment_of(places, ends):
    return jnp.sum((ends[None, :] <= places[:, None]).astype(jnp.int32), axis=1)


def pair_step(early, later):
    return (early[0] * later[0], later[0] * early[1] + later[1])


def plain_dot(left, right):
    return jnp.dot(left, right, preferred_element_type=jnp.float32)


def times_trans(left, right):
    return lax.dot_general(
        left, right, (((1,), (1,)), ((), ())), preferred_element_type=jnp.float32
    )


def trans_times(left, right):
    return lax.dot_general(
        left, right, (((0,), (0,)), ((), ())), preferred_element_type=jnp.float32
    )


def gelu_tanh(values):
    return jax.nn.gelu(values, approximate=True)


def collect(
    norm_gain,
    mlp_gain,
    x_weight,
    y_weight,
    recur_gate_weight,
    input_gate_weight,
    gate_weight,
    up_weight,
    out_weight,
    down_weight,
):
    return (
        lax.all_gather(norm_gain, "dp", axis=0, tiled=True),
        lax.all_gather(mlp_gain, "dp", axis=0, tiled=True),
        lax.all_gather(x_weight, "dp", axis=0, tiled=True),
        lax.all_gather(y_weight, "dp", axis=0, tiled=True),
        lax.all_gather(recur_gate_weight, "dp", axis=0, tiled=True),
        lax.all_gather(input_gate_weight, "dp", axis=0, tiled=True),
        lax.all_gather(gate_weight, "dp", axis=0, tiled=True),
        lax.all_gather(up_weight, "dp", axis=0, tiled=True),
        lax.all_gather(out_weight, "dp", axis=1, tiled=True),
        lax.all_gather(down_weight, "dp", axis=1, tiled=True),
    )


def row_sums(term_rows, tok_rows):
    return lax.psum_scatter(
        term_rows(jnp.int32(0), lax.axis_size("tensor") * tok_rows).astype(jnp.bfloat16),
        "tensor",
        scatter_dimension=0,
        tiled=True,
    ).astype(jnp.float32)


def spread_rows(values):
    return lax.all_gather(values, "tensor", axis=0, tiled=True)


def local_general(
    tokens,
    norm_gain,
    x_weight,
    y_weight,
    conv_weight,
    recur_gate_weight,
    input_gate_weight,
    decay_param,
    out_weight,
    mlp_gain,
    gate_weight,
    up_weight,
    down_weight,
    seq_lengths,
    token_order,
    cotangent,
):
    n_tensor = lax.axis_size("tensor")
    tensor_index = lax.axis_index("tensor")
    dp_index = lax.axis_index("dp")
    tok_rows = tokens.shape[0]
    row_count = tok_rows * n_tensor
    own_width = conv_weight.shape[1]
    kernel_taps = conv_weight.shape[0]
    edge_rows = kernel_taps - 1
    dp_width = norm_gain.shape[0]
    own_start = tensor_index * tok_rows
    shards = (
        norm_gain,
        mlp_gain,
        x_weight,
        y_weight,
        recur_gate_weight,
        input_gate_weight,
        gate_weight,
        up_weight,
        out_weight,
        down_weight,
    )
    (
        gain_one,
        gain_two,
        x_full,
        y_full,
        recur_full,
        input_full,
        gate_full,
        up_full,
        out_full,
        down_full,
    ) = collect(*shards)
    block_size = recur_full.shape[0]
    first_gain = gain_one.astype(jnp.float32)
    second_gain = gain_two.astype(jnp.float32)
    both_gates = jnp.concatenate([recur_full, input_full], axis=1)
    tok_own = tokens.astype(jnp.float32)
    own_order = token_order - dp_index * row_count
    first_rows = rms_scale(tok_own, first_gain).astype(jnp.bfloat16)
    first_all, cot_all, order_all = (
        lax.all_gather(first_rows, "tensor", axis=0, tiled=True),
        lax.all_gather(cotangent, "tensor", axis=0, tiled=True),
        lax.all_gather(own_order, "tensor", axis=0, tiled=True),
    )
    row_index = jnp.arange(row_count, dtype=jnp.int32)
    inverse = jnp.zeros((row_count,), jnp.int32).at[order_all].set(row_index)
    hidden_place = jnp.take(first_all, inverse, axis=0)
    places = dp_index * row_count + row_index
    ends = jnp.cumsum(seq_lengths)
    segment = segment_of(places, ends)
    starts = (places == 0) | (segment != segment_of(places - 1, ends))
    live = (places < ends[-1]).astype(jnp.float32)
    live_stored = jnp.take(live, order_all, axis=0)
    same = [
        (segment_of(places - shift, ends) == segment).astype(jnp.float32)
        for shift in range(kernel_taps)
    ]
    low_edge = tensor_index * own_width
    own_blocks = (low_edge + jnp.arange(own_width, dtype=jnp.int32)) // block_size
    first_block = low_edge // block_size
    block_count = own_width // block_size + 2

    def block_start(index):
        return (first_block + index) * block_size - low_edge + block_size

    def block_mask(index):
        inside = own_blocks == first_block + index
        return jnp.concatenate([inside, inside])

    def convolve(extended, kernel):
        return sum(
            (
                kernel[shift][None, :]
                * extended[edge_rows - shift : edge_rows - shift + row_count]
                * same[shift][:, None]
                for shift in range(kernel_taps)
            )
        )

    def gates(conv_vals, pre_recur, pre_input, decay_vals):
        log_rate = -rate_scale * jax.nn.sigmoid(pre_recur) * jax.nn.softplus(-decay_vals)
        decay_rate = jnp.where(starts[:, None], 0.0, jnp.exp(log_rate))
        scale_in = jnp.where(starts[:, None], 1.0, jnp.sqrt(-jnp.expm1(2.0 * log_rate)))
        return (decay_rate, conv_vals * jax.nn.sigmoid(pre_input) * scale_in)

    def glu(gate_pre, up_pre):
        return gelu_tanh(gate_pre) * up_pre

    x_branch = plain_dot(hidden_place, x_full).astype(jnp.bfloat16)
    y_before = plain_dot(hidden_place, y_full)
    previous = from_behind(x_branch[row_count - edge_rows :], "dp", 1)
    extended = jnp.concatenate([previous, x_branch], axis=0).astype(jnp.float32)
    conv_out = convolve(extended, conv_weight)
    conv_wide = extended_2(conv_out.astype(jnp.bfloat16), (("tensor", 1),), block_size)
    pre_both = jnp.zeros((row_count, 2 * own_width), jnp.float32)
    for index in range(block_count):
        piece = lax.dynamic_slice_in_dim(conv_wide, block_start(index), block_size, 1)
        pre_both = pre_both + jnp.where(
            block_mask(index)[None, :], plain_dot(piece, both_gates), 0.0
        )
    (decay_rate, driven), gate_pull = jax.vjp(
        gates, conv_out, pre_both[:, :own_width], pre_both[:, own_width:], decay_param
    )
    cum_rate, local_state = lax.associative_scan(pair_step, (decay_rate, driven), axis=0)
    ident = (jnp.ones((own_width,), jnp.float32), jnp.zeros((own_width,), jnp.float32))
    rate_in, state_in = entering((cum_rate[-1], local_state[-1]), "dp", pair_step, ident, False)
    state = local_state + cum_rate * state_in[None, :]
    y_branch = gelu_tanh(y_before)
    merged = (state * y_branch).astype(jnp.bfloat16)
    merged_stored = jnp.take(merged, order_all, axis=0)

    def mixer_rows(begin, number):
        return plain_dot(merged_stored, out_full)

    after_own = tok_own + row_sums(mixer_rows, tok_rows)
    hidden_two = spread_rows(rms_scale(after_own, second_gain).astype(jnp.bfloat16))
    gate_pre = plain_dot(hidden_two, gate_full)
    up_pre = plain_dot(hidden_two, up_full)
    glu_out, glu_pull = jax.vjp(glu, gate_pre, up_pre)
    product = glu_out.astype(jnp.bfloat16)

    def down_rows(begin, number):
        return plain_dot(product, down_full)

    feed_out = row_sums(down_rows, tok_rows)
    live_own = lax.dynamic_slice_in_dim(live_stored, own_start, tok_rows, 0)
    output = ((after_own + feed_out) * live_own[:, None]).astype(jnp.bfloat16)
    grad_out = cot_all.astype(jnp.float32) * live_stored[:, None]
    fresh = lax.optimization_barrier((shards, grad_out))[0]
    (
        gain_one,
        gain_two,
        x_full,
        y_full,
        recur_full,
        input_full,
        gate_full,
        up_full,
        out_full,
        down_full,
    ) = collect(*fresh)
    first_gain = gain_one.astype(jnp.float32)
    second_gain = gain_two.astype(jnp.float32)
    both_gates = jnp.concatenate([recur_full, input_full], axis=1)
    down_in = grad_out.astype(jnp.bfloat16)
    grad_down = trans_times(product, down_in)
    grad_product = times_trans(down_in, down_full)
    grad_gate_pre, grad_up_pre = glu_pull(grad_product)
    grad_gate_pre = grad_gate_pre.astype(jnp.bfloat16)
    grad_up_pre = grad_up_pre.astype(jnp.bfloat16)
    grad_gate = trans_times(hidden_two, grad_gate_pre)
    grad_up = trans_times(hidden_two, grad_up_pre)

    def feed_rows(begin, number):
        return times_trans(grad_gate_pre, gate_full) + times_trans(grad_up_pre, up_full)

    grad_out_own = lax.dynamic_slice_in_dim(grad_out, own_start, tok_rows, 0)
    grad_two_own = row_sums(feed_rows, tok_rows)
    grad_norm_own, normed_two = norm_back(after_own, second_gain, grad_two_own)
    second_part = jnp.sum(grad_two_own * normed_two, axis=0)
    grad_after_own = grad_out_own + grad_norm_own
    mixer_in = spread_rows(grad_after_own.astype(jnp.bfloat16))
    grad_out_mat = trans_times(merged_stored, mixer_in)
    grad_merged = jnp.take(times_trans(mixer_in, out_full), inverse, axis=0)
    grad_state = grad_merged * y_branch
    gelu_pull = jax.vjp(gelu_tanh, y_before)[1]
    grad_y_before = gelu_pull(grad_merged * state)[0].astype(jnp.bfloat16)
    rate_next = jnp.concatenate([decay_rate[1:], jnp.ones((1, own_width), jnp.float32)], axis=0)
    rev_rate, local_lam = lax.associative_scan(
        pair_step, (rate_next, grad_state), reverse=True, axis=0
    )
    head_rate = decay_rate[0] * rev_rate[0]
    head_lam = decay_rate[0] * local_lam[0]
    factor_in, lam_in = entering((head_rate, head_lam), "dp", pair_step, ident, True)
    lam = local_lam + rev_rate * lam_in[None, :]
    state_prev = jnp.concatenate([state_in[None, :], state[:-1]], axis=0)
    grad_conv_local, grad_pre_recur, grad_pre_input, grad_decay_own = gate_pull(
        (lam * state_prev, lam)
    )
    grad_pre = jnp.concatenate([grad_pre_recur, grad_pre_input], axis=1).astype(jnp.bfloat16)
    grad_both = jnp.zeros((block_size, 2 * own_width), jnp.float32)
    grad_wide = jnp.zeros((row_count, own_width + 2 * block_size), jnp.float32)
    for index in range(block_count):
        begin = block_start(index)
        piece = lax.dynamic_slice_in_dim(conv_wide, begin, block_size, 1)
        masked = jnp.where(block_mask(index)[None, :], grad_pre, jnp.zeros((), jnp.bfloat16))
        grad_both = grad_both + trans_times(piece, masked)
        added = lax.dynamic_slice_in_dim(grad_wide, begin, block_size, 1) + times_trans(
            masked, both_gates
        )
        grad_wide = lax.dynamic_update_slice_in_dim(grad_wide, added, begin, 1)
    grad_recur = grad_both[:, :own_width]
    grad_input = grad_both[:, own_width:]
    rims = jnp.concatenate(
        [grad_wide[:, :block_size], grad_wide[:, own_width + block_size :]], axis=1
    )
    arrived = extended_2(rims.astype(jnp.bfloat16), (("tensor", 1),), block_size).astype(rims.dtype)
    from_lower = jnp.pad(arrived[:, :block_size], ((0, 0), (0, own_width - block_size)))
    from_upper = jnp.pad(arrived[:, 3 * block_size :], ((0, 0), (own_width - block_size, 0)))
    grad_conv = (
        grad_conv_local
        + grad_wide[:, block_size : block_size + own_width]
        + from_lower
        + from_upper
    )
    conv_pull = jax.vjp(convolve, extended, conv_weight)[1]
    grad_extended, grad_kernel = conv_pull(grad_conv)
    returned = from_behind(grad_extended[:edge_rows], "dp", -1)
    grad_x_branch = grad_extended[edge_rows:] + jnp.concatenate(
        [jnp.zeros((row_count - edge_rows, own_width), jnp.float32), returned], axis=0
    )
    grad_x_low = grad_x_branch.astype(jnp.bfloat16)
    grad_x_stored = jnp.take(grad_x_low, order_all, axis=0)
    grad_y_stored = jnp.take(grad_y_before, order_all, axis=0)
    grad_x_mat = trans_times(first_all, grad_x_stored)
    grad_y_mat = trans_times(first_all, grad_y_stored)

    def mixer_back_rows(begin, number):
        return times_trans(grad_x_stored, x_full) + times_trans(grad_y_stored, y_full)

    grad_one_own = row_sums(mixer_back_rows, tok_rows)
    grad_norm_one, normed_one = norm_back(tok_own, first_gain, grad_one_own)
    first_part = jnp.sum(grad_one_own * normed_one, axis=0)
    grad_tokens = grad_after_own + grad_norm_one
    chosen = jnp.arange(n_tensor, dtype=jnp.int32) == tensor_index
    kernel_tile = jnp.where(chosen[:, None, None], grad_kernel[None, :, :], 0.0)
    decay_tile = jnp.where(chosen[:, None], grad_decay_own[None, :], 0.0)
    small = lax.psum((first_part, second_part, kernel_tile, decay_tile), ("dp", "tensor"))
    grad_first_gain = lax.dynamic_slice_in_dim(small[0], dp_index * dp_width, dp_width, 0)
    grad_second_gain = lax.dynamic_slice_in_dim(small[1], dp_index * dp_width, dp_width, 0)
    grad_kernel_sum = lax.dynamic_index_in_dim(small[2], tensor_index, 0, keepdims=False)
    grad_decay = lax.dynamic_index_in_dim(small[3], tensor_index, 0, keepdims=False)
    sums = (
        lax.psum_scatter(
            grad_x_mat.astype(jnp.bfloat16), "dp", scatter_dimension=0, tiled=True
        ).astype(jnp.float32),
        lax.psum_scatter(
            grad_y_mat.astype(jnp.bfloat16), "dp", scatter_dimension=0, tiled=True
        ).astype(jnp.float32),
        lax.psum_scatter(
            grad_recur.astype(jnp.bfloat16), "dp", scatter_dimension=0, tiled=True
        ).astype(jnp.float32),
        lax.psum_scatter(
            grad_input.astype(jnp.bfloat16), "dp", scatter_dimension=0, tiled=True
        ).astype(jnp.float32),
        lax.psum_scatter(
            grad_gate.astype(jnp.bfloat16), "dp", scatter_dimension=0, tiled=True
        ).astype(jnp.float32),
        lax.psum_scatter(
            grad_up.astype(jnp.bfloat16), "dp", scatter_dimension=0, tiled=True
        ).astype(jnp.float32),
        lax.psum_scatter(
            grad_out_mat.astype(jnp.bfloat16), "dp", scatter_dimension=1, tiled=True
        ).astype(jnp.float32),
        lax.psum_scatter(
            grad_down.astype(jnp.bfloat16), "dp", scatter_dimension=1, tiled=True
        ).astype(jnp.float32),
    )
    return (
        output,
        grad_tokens,
        grad_first_gain,
        sums[0],
        sums[1],
        grad_kernel_sum,
        sums[2],
        sums[3],
        grad_decay,
        sums[6],
        grad_second_gain,
        sums[4],
        sums[5],
        sums[7],
    )


MESH = pl.DeviceIdType.MESH
VMEM_BYTES = 60 * 2**20


def remote(src, dst, send, recv, device):
    return pltpu.make_async_remote_copy(
        src_ref=src,
        dst_ref=dst,
        send_sem=send,
        recv_sem=recv,
        device_id=device,
        device_id_type=MESH,
    )


class Place:
    def __init__(self, n_dp, n_line):
        self.n_dp, self.n_line = n_dp, n_line
        self.d, self.t = lax.axis_index("dp"), lax.axis_index("tensor")
        self.core = lax.rem(self.d, 2)
        self.x = lax.rem(lax.div(self.d, 2), 2)
        self.y = lax.div(self.d, 4)

    def chip(self, flip_x, flip_y, flip_core=0):
        x = 1 - self.x if flip_x else self.x
        y = 1 - self.y if flip_y else self.y
        core = 1 - self.core if flip_core else self.core
        return y * 4 + x * 2 + core

    def at(self, flip_x=0, flip_y=0, flip_core=0):
        return (self.chip(flip_x, flip_y, flip_core), self.t)

    def up(self):
        return (self.d, lax.rem(self.t + 1, self.n_line))

    def down(self):
        return (self.d, lax.rem(self.t + self.n_line - 1, self.n_line))

    def meet(self, everyone=False):
        barrier = pltpu.get_barrier_semaphore()

        def greet(device):
            pl.semaphore_signal(barrier, inc=1, device_id=device, device_id_type=MESH)

        if everyone:
            for i in range(1, self.n_dp):
                greet((lax.rem(self.d + i, self.n_dp), self.t))
            for i in range(1, self.n_line):
                greet((self.d, lax.rem(self.t + i, self.n_line)))
            pl.semaphore_wait(barrier, self.n_dp + self.n_line - 2)
            return
        for flips in ((1, 0), (0, 1), (0, 0, 1)):
            greet(self.at(*flips))
        below, above = self.t > 0, self.t < self.n_line - 1

        @pl.when(below)
        def _():
            greet(self.down())

        @pl.when(above)
        def _():
            greet(self.up())

        pl.semaphore_wait(barrier, 3 + below.astype(jnp.int32) + above.astype(jnp.int32))


class Fetch:
    def __init__(self, pairs, sems):
        self.copies = [
            pltpu.make_async_copy(src, dst, sems.at[i]) for i, (src, dst) in enumerate(pairs)
        ]

    def start(self, *which):
        for i in which:
            self.copies[i].start()

    def wait(self, *which):
        for i in which:
            self.copies[i].wait()


def vmem_like(array):
    return pltpu.VMEM(array.shape, array.dtype)


class Kept:
    def __init__(self, src, dst, held, sems):
        self.there = pltpu.make_async_copy(src, held, sems.at[0])
        self.back = pltpu.make_async_copy(held, dst, sems.at[1])

    def begin(self):
        self.there.start()

    def turn(self):
        self.there.wait()
        self.back.start()

    def finish(self):
        self.back.wait()


class GatherPlane:
    def __init__(self, place, src, dst, send, recv, local, held):
        self.p, self.src, self.dst = place, src, dst
        self.rows = src.shape[0]
        self.send, self.recv = send, recv
        self.keep = Kept(src, self.block(0, 0), held, local)

    def block(self, fx, fy, fc=0, part=None):
        first = self.p.chip(fx, fy, fc) * self.rows
        size = self.rows
        if part is not None:
            size = self.rows // 2
            first = first + part * size
        return self.dst.at[pl.ds(pl.multiple_of(first, 16), size)]

    def copy(self, i, src, dst, device):
        return remote(src, dst, self.send.at[i], self.recv.at[i], device)

    def outgoing(self, i):
        at, block = self.p.at, self.block
        if i == 0:
            return self.copy(0, self.src, block(0, 0), at(1, 0))
        if i == 1:
            return self.copy(1, self.src, block(0, 0), at(0, 1))
        if i == 2:
            return self.copy(2, self.src, block(0, 0), at(0, 0, 1))
        if i == 3:
            return self.copy(3, block(1, 0, 0, 0), block(1, 0, 0, 0), at(0, 1))
        if i == 4:
            return self.copy(4, block(0, 1, 0, 1), block(0, 1, 0, 1), at(1, 0))
        spot = ((1, 0), (0, 1), (1, 1, 0, 0), (1, 1, 0, 1))[i - 5]
        return self.copy(i, block(*spot), block(*spot), at(0, 0, 1))

    def arrive(self, i):
        spot = (
            (1, 0),
            (0, 1),
            (0, 0, 1),
            (1, 1, 0, 0),
            (1, 1, 0, 1),
            (1, 0, 1),
            (0, 1, 1),
            (1, 1, 1, 0),
            (1, 1, 1, 1),
        )[i]
        here = self.block(*spot)
        self.copy(i, here, here, self.p.at(0, 0, 1)).wait_recv()

    def begin(self):
        for i in (0, 1, 2):
            self.outgoing(i).start()
        self.keep.begin()

    def forward(self):
        self.keep.turn()
        self.arrive(0)
        self.outgoing(3).start()
        self.arrive(1)
        self.outgoing(4).start()
        self.outgoing(5).start()
        self.outgoing(6).start()

    def share(self):
        self.arrive(3)
        self.outgoing(7).start()
        self.arrive(4)
        self.outgoing(8).start()

    def finish(self):
        for i in (2, 5, 6, 7, 8):
            self.arrive(i)
        for i in range(9):
            self.outgoing(i).wait_send()
        self.keep.finish()


class GatherLine:
    def __init__(self, place, dst, rows, begin, span, send, recv):
        self.p, self.dst, self.rows = place, dst, rows
        self.begin, self.span = begin, span
        self.send, self.recv = send, recv
        self.last = place.n_line - 1

    def block(self, owner):
        first = owner * self.rows + self.begin
        return self.dst.at[pl.ds(pl.multiple_of(first, 8), self.span)]

    def copy(self, way, k, owner, source=None):
        to = self.p.up() if way == 0 else self.p.down()
        block = self.block(owner)
        return remote(
            block if source is None else source,
            block,
            self.send.at[way, k],
            self.recv.at[way, k],
            to,
        )

    def step(self, k, source=None):
        t, last = self.p.t, self.last
        if k > 0:
            self.arrive(k - 1)

        @pl.when((t < last) & (t >= k))
        def _():
            self.copy(0, k, t - k, source).start()

        @pl.when((t > 0) & (t + k <= last))
        def _():
            self.copy(1, k, t + k, source).start()

    def arrive(self, k):
        t, last = self.p.t, self.last

        @pl.when(t >= k + 1)
        def _():
            self.copy(0, k, t - 1 - k).wait_recv()

        @pl.when(t + k + 1 <= last)
        def _():
            self.copy(1, k, t + 1 + k).wait_recv()

    def finish(self):
        t, last = self.p.t, self.last
        self.arrive(last - 1)
        for k in range(last):

            @pl.when((t < last) & (t >= k))
            def _():
                self.copy(0, k, t - k).wait_send()

            @pl.when((t > 0) & (t + k <= last))
            def _():
                self.copy(1, k, t + k).wait_send()


class ReduceLine:
    def __init__(self, place, terms, rows, begin, span, inbox, send, recv):
        self.p, self.terms, self.rows = place, terms, rows
        self.begin, self.span = begin, span
        self.inbox = inbox
        self.send, self.recv = send, recv
        self.last = place.n_line - 1

    def own(self, owner):
        first = owner * self.rows + self.begin
        return self.terms.at[pl.ds(pl.multiple_of(first, 16), self.span)]

    def copy(self, way, j, source):
        to = self.p.up() if way == 0 else self.p.down()
        return remote(
            source, self.inbox.at[way, j], self.send.at[way, j], self.recv.at[way, j], to
        )

    def ends(self):
        t, last = self.p.t, self.last

        @pl.when(t == 0)
        def _():
            for j in range(last):
                self.copy(0, j, self.own(last - j)).start()

        @pl.when(t == last)
        def _():
            for j in range(last):
                self.copy(1, j, self.own(j)).start()

    def sent(self):
        t, last = self.p.t, self.last

        @pl.when(t == 0)
        def _():
            for j in range(last):
                self.copy(0, j, self.own(last - j)).wait_send()

        @pl.when(t == last)
        def _():
            for j in range(last):
                self.copy(1, j, self.own(j)).wait_send()

    def hand_on(self, way, j):
        term = self.own(self.last - j if way == 0 else j)
        self.copy(way, j, term).wait_recv()
        self.inbox[way, j] = term[...] + self.inbox[way, j]
        self.copy(way, j, self.inbox.at[way, j]).start()

    def hop(self, k):
        t, last = self.p.t, self.last

        @pl.when(t == k + 1)
        def _():
            for j in range(last - 1 - k):
                self.hand_on(0, j)

        @pl.when(t == last - 1 - k)
        def _():
            for j in range(last - 1 - k):
                self.hand_on(1, j)

    def total(self, result):
        t, last = self.p.t, self.last
        result[...] = self.own(t)[...].astype(jnp.float32)

        @pl.when(t > 0)
        def _():
            j = last - t
            self.copy(0, j, self.inbox.at[0, 0]).wait_recv()
            result[...] += self.inbox[0, j].astype(jnp.float32)

        @pl.when(t < last)
        def _():
            self.copy(1, t, self.inbox.at[0, 0]).wait_recv()
            result[...] += self.inbox[1, t].astype(jnp.float32)

    def finish(self):
        t, last = self.p.t, self.last
        for j in range(last - 1):

            @pl.when((t > 0) & (t < last - j))
            def _():
                self.copy(0, j, self.inbox.at[0, j]).wait_send()

            @pl.when((t < last) & (t > j))
            def _():
                self.copy(1, j, self.inbox.at[1, j]).wait_send()


def add_rows(into, other, result=None):
    result = into if result is None else result

    def tile(i, carry):
        rows = pl.ds(pl.multiple_of(i * 16, 16), 16)
        result[rows] = into[rows] + other[rows]
        return carry

    lax.fori_loop(0, into.shape[0] // 16, tile, None)


class ReducePlane:
    chips = ((0, 0), (1, 0), (0, 1), (1, 1))

    def __init__(self, place, terms, scratch):
        self.p, self.terms = place, terms
        self.held, self.near, self.along, self.last, self.send, self.recv, self.local = scratch
        self.rows = self.held.shape[1]
        self.half = self.rows // 2

    @staticmethod
    def scratch(rows, width):
        return [
            pltpu.VMEM((4, rows, width), jnp.bfloat16),
            pltpu.VMEM((4, rows, width), jnp.bfloat16),
            pltpu.VMEM((4, rows // 2, width), jnp.bfloat16),
            pltpu.VMEM((2, rows // 2, width), jnp.bfloat16),
            pltpu.SemaphoreType.DMA((10,)),
            pltpu.SemaphoreType.DMA((10,)),
            pltpu.SemaphoreType.DMA((4,)),
        ]

    def block(self, k, other):
        first = self.p.chip(*self.chips[k], other) * self.rows
        return self.terms.at[pl.ds(pl.multiple_of(first, 16), self.rows)]

    def half_of(self, k, part):
        return self.held.at[k, pl.ds(part * self.half, self.half)]

    def load(self, k):
        return pltpu.make_async_copy(self.block(k, 0), self.held.at[k], self.local.at[k])

    def copy(self, i):
        at = self.p.at
        if i < 4:
            src, dst, to = self.block(i, 1), self.near.at[i], at(0, 0, 1)
        elif i < 8:
            src, to = (
                (self.half_of(1, 0), at(1, 0)),
                (self.half_of(3, 0), at(1, 0)),
                (self.half_of(2, 1), at(0, 1)),
                (self.half_of(3, 1), at(0, 1)),
            )[i - 4]
            dst = self.along.at[i - 4]
        else:
            src, to = ((self.half_of(2, 0), at(0, 1)), (self.half_of(1, 1), at(1, 0)))[i - 8]
            dst = self.last.at[i - 8]
        return remote(src, dst, self.send.at[i], self.recv.at[i], to)

    def begin(self):
        for k in (3, 1, 2, 0):
            self.copy(k).start()
            self.load(k).start()

    def cores(self):
        for k in (3, 1, 2, 0):
            self.load(k).wait()
            self.copy(k).wait_recv()
            add_rows(self.held.at[k], self.near.at[k])
            if k == 3:
                self.copy(5).start()
                self.copy(7).start()
            elif k == 1:
                self.copy(4).start()
            elif k == 2:
                self.copy(6).start()

    def turn(self):
        self.copy(5).wait_recv()
        add_rows(self.half_of(2, 0), self.along.at[1])
        self.copy(8).start()
        self.copy(7).wait_recv()
        add_rows(self.half_of(1, 1), self.along.at[3])
        self.copy(9).start()
        self.copy(4).wait_recv()
        add_rows(self.half_of(0, 0), self.along.at[0])
        self.copy(6).wait_recv()
        add_rows(self.half_of(0, 1), self.along.at[2])

    def finish(self, result):
        for part in (0, 1):
            self.copy(8 + part).wait_recv()
            rows = pl.ds(part * self.half, self.half)
            add_rows(self.half_of(0, part), self.last.at[part], result.at[rows])
        for i in range(10):
            self.copy(i).wait_send()


def dma_sems(*dims):
    return pltpu.SemaphoreType.DMA(dims)


def in_vmem():
    return pl.BlockSpec(memory_space=pltpu.VMEM)


def in_any():
    return pl.BlockSpec(memory_space=pl.ANY)


def comm_params(number):
    return pltpu.CompilerParams(
        collective_id=number, has_side_effects=True, vmem_limit_bytes=VMEM_BYTES
    )


def shaped(dims, kind):
    return jax.ShapeDtypeStruct(dims, kind)


def first_gather(n_dp, n_line, mats, rows_in, order):
    count = len(mats)
    parts = 2

    def kernel(*refs):
        srcs, (c, e) = refs[:count], refs[count : count + 2]
        dsts, (c_out, e_out) = refs[count + 2 : 2 * count + 2], refs[2 * count + 2 : 2 * count + 4]
        ps, pr, pl_sem, ls, lr, ll = refs[2 * count + 4 : 2 * count + 10]
        held = refs[2 * count + 10 :]
        place = Place(n_dp, n_line)
        place.meet()
        planes = [
            GatherPlane(place, a, b, ps.at[i], pr.at[i], pl_sem.at[i], held[i])
            for i, (a, b) in enumerate(zip(srcs, dsts))
        ]
        rows = c.shape[0]
        span = rows // parts
        lines = [
            GatherLine(place, c_out, rows, i * span, span, ls.at[i], lr.at[i])
            for i in range(parts)
        ]
        lines.append(
            GatherLine(place, e_out, e.shape[0], 0, e.shape[0], ls.at[parts], lr.at[parts])
        )
        for i in range(parts):
            lines[i].step(0, c.at[pl.ds(i * span, span)])
        lines[parts].step(0, e)
        early, late = planes[: count // 2], planes[count // 2 :]
        for part in early:
            part.begin()
        copies = []
        for i, (src, dst) in enumerate(((c, c_out), (e, e_out))):
            own = dst.at[pl.ds(pl.multiple_of(place.t * src.shape[0], 8), src.shape[0])]
            copies.append(Kept(src, own, held[count + i], ll.at[i]))
            copies[i].begin()
        for line in lines:
            line.step(1)
        for part in late:
            part.begin()
        for part in early:
            part.forward()
        for copy in copies:
            copy.turn()
        for line in lines:
            line.step(2)
        for part in early:
            part.share()
        for part in late:
            part.forward()
        for part in late:
            part.share()
        for part in lines + planes:
            part.finish()
        for copy in copies:
            copy.finish()

    return pl.pallas_call(
        kernel,
        out_shape=tuple(shaped((n_dp * m.shape[0], m.shape[1]), m.dtype) for m in mats)
        + (
            shaped((n_line * rows_in.shape[0], rows_in.shape[1]), rows_in.dtype),
            shaped((n_line * order.shape[0], order.shape[1]), order.dtype),
        ),
        in_specs=[in_any()] * (count + 2),
        out_specs=[in_any()] * (count + 2),
        scratch_shapes=[
            dma_sems(count, 9),
            dma_sems(count, 9),
            dma_sems(count, 2),
            dma_sems(parts + 1, 2, n_line - 1),
            dma_sems(parts + 1, 2, n_line - 1),
            dma_sems(2, 2),
        ]
        + [vmem_like(m) for m in (*mats, rows_in, order)],
        compiler_params=comm_params(1),
        name="first_gather",
    )(*mats, rows_in, order)


CHUNKS = 8
LAST_CHUNKS = 8


def line_scratch(n_line, span, width, chunks):
    hops = n_line - 1
    return [
        pltpu.VMEM((chunks, 2, hops, span, width), jnp.bfloat16),
        dma_sems(chunks, 2, hops),
        dma_sems(chunks, 2, hops),
        dma_sems(chunks, 2, hops),
        dma_sems(chunks, 2, hops),
        pltpu.VMEM((span, width), jnp.float32),
    ]


def sum_rows_and_spread(place, terms, scratch, finish_rows, spread, between):
    inbox, rs, rr, gs, gr, total = scratch
    span = total.shape[0]
    count = inbox.shape[0]
    rows = span * count
    hops = place.n_line - 1
    sums = [
        ReduceLine(place, terms, rows, c * span, span, inbox.at[c], rs.at[c], rr.at[c])
        for c in range(count)
    ]
    gathers = []
    if spread is not None:
        gathers = [
            GatherLine(place, spread, rows, c * span, span, gs.at[c], gr.at[c])
            for c in range(count)
        ]
    sums[0].ends()

    def total_of(c):
        sums[c].total(total)
        finish_rows(c, pl.ds(c * span, span), total)
        if gathers:
            gathers[c].step(0)

    stages = [lambda c, k=k: sums[c].hop(k) for k in range(hops - 1)] + [total_of]
    lags = [LAGS[min(k, len(LAGS) - 1)] for k in range(hops)]
    if gathers:
        stages += [lambda c, k=k: gathers[c].step(k) for k in range(1, hops)]
        lags += [lags[-1] + LAG_STEP * k for k in range(1, hops)]
    for i in range(count + lags[-1]):
        if i < count:
            sums[i].sent()
        if i + 1 < count:
            sums[i + 1].ends()
        for work, lag in zip(stages, lags):
            if 0 <= i - lag < count:
                work(i - lag)
        if i in between:
            between[i]()
    for part in gathers + sums:
        part.finish()


LAGS = (0, 1, 1)
LAG_STEP = 1


def middle_gather(n_dp, n_line, terms, tokens, gain, mats):
    rows, width = tokens.shape
    count = len(mats)

    def kernel(*refs):
        s, tok, gain_ref = refs[:3]
        srcs = refs[3 : 3 + count]
        after, hidden = refs[3 + count : 5 + count]
        dsts = refs[5 + count : 5 + 2 * count]
        ps, pr, pl_sem = refs[5 + 2 * count : 8 + 2 * count]
        held = refs[8 + 2 * count : 8 + 3 * count]
        scratch = refs[8 + 3 * count :]
        place = Place(n_dp, n_line)
        place.meet()
        planes = [
            GatherPlane(place, a, b, ps.at[i], pr.at[i], pl_sem.at[i], held[i])
            for i, (a, b) in enumerate(zip(srcs, dsts))
        ]
        planes[0].begin()

        def norm(c, here, total):
            values = tok[here].astype(jnp.float32) + total[...]
            after[here] = values
            low = rms_scale(values, gain_ref[...]).astype(jnp.bfloat16)
            first = pl.multiple_of(place.t * rows, 16) + c * total.shape[0]
            hidden[pl.ds(pl.multiple_of(first, 16), total.shape[0])] = low

        between = {6: planes[0].forward, 9: planes[0].share}
        sum_rows_and_spread(place, s, scratch, norm, hidden, between)
        for part in planes:
            part.finish()

    return pl.pallas_call(
        kernel,
        out_shape=(
            shaped((rows, width), jnp.float32),
            shaped((n_line * rows, width), jnp.bfloat16),
        )
        + tuple(shaped((n_dp * m.shape[0], m.shape[1]), m.dtype) for m in mats),
        in_specs=[in_vmem()] * 3 + [in_any()] * count,
        out_specs=[in_vmem()] * 2 + [in_any()] * count,
        scratch_shapes=[dma_sems(count, 9), dma_sems(count, 9), dma_sems(count, 2)]
        + [vmem_like(m) for m in mats]
        + line_scratch(n_line, rows // CHUNKS, width, CHUNKS),
        compiler_params=comm_params(2),
        name="middle_gather",
    )(terms, tokens, gain, *mats)


def middle_sums(n_dp, n_line, terms, after, gain, grad_in, mat, hidden, grad_up, product, down):
    rows, width = after.shape
    block = mat.shape[0] // n_dp
    wide = grad_up.shape[1]
    spread_rows = n_line * rows

    def kernel(*refs):
        s, after_ref, gain_ref, g_ref, src = refs[:5]
        hid_far, gu_far, pr_far, dw_far = refs[5:9]
        grad_after, gain_sum, spread, result, up_far, feed_far = refs[9:15]
        hid, gu, pr, dw, up_out, feed, sems = refs[15:22]
        rest = refs[22:]
        fetch = Fetch(
            [
                (hid_far, hid),
                (gu_far, gu),
                (pr_far, pr),
                (dw_far, dw),
                (feed, feed_far),
                (up_out.at[0], up_far.at[pl.ds(0, width // 2)]),
                (up_out.at[1], up_far.at[pl.ds(width // 2, width // 2)]),
            ],
            sems,
        )
        fetch.start(0, 1, 2, 3)
        place = Place(n_dp, n_line)
        place.meet()
        plane = ReducePlane(place, src, rest[:7])
        scratch = rest[7:]
        plane.begin()
        gain_sum[...] = jnp.zeros_like(gain_sum)

        def norm(c, here, total):
            grad = total[...]
            grad_rows, normed = norm_back(after_ref[here], gain_ref[...], grad)
            gain_sum[...] += jnp.sum(grad * normed, axis=0, keepdims=True)
            both = g_ref[here].astype(jnp.float32) + grad_rows
            grad_after[here] = both
            first = pl.multiple_of(place.t * rows, 16) + c * total.shape[0]
            spread[pl.ds(pl.multiple_of(first, 16), total.shape[0])] = both.astype(jnp.bfloat16)

        def feed_part(i):
            cols = pl.ds(i * (width // 4), width // 4)
            feed[:, cols] = times_trans(pr[...], dw[cols]).astype(jnp.bfloat16)

        def up_part(i):
            cols = pl.ds(i * (width // 4), width // 4)
            here = pl.ds((i % 2) * (width // 4), width // 4)
            up_out[i // 2, here] = trans_times(hid[:, cols], gu[...]).astype(jnp.bfloat16)

        def early():
            plane.cores()
            fetch.wait(0, 1)

        def two():
            up_part(0)

        def three():
            up_part(1)
            fetch.start(5)

        def four():
            up_part(2)

        def five():
            up_part(3)
            fetch.start(6)
            fetch.wait(2, 3)

        def six():
            feed_part(0)

        def seven():
            plane.turn()
            feed_part(1)

        def eight():
            feed_part(2)

        def nine():
            feed_part(3)
            fetch.start(4)

        steps = {1: early, 2: two, 3: three, 4: four, 5: five, 6: six, 7: seven, 8: eight, 9: nine}
        sum_rows_and_spread(place, s, scratch, norm, spread, steps)
        plane.finish(result)
        fetch.wait(4, 5, 6)

    low, full = jnp.bfloat16, jnp.float32
    near, far = in_vmem(), in_any()
    return pl.pallas_call(
        kernel,
        out_shape=(
            shaped((rows, width), full),
            shaped((1, width), full),
            shaped((spread_rows, width), low),
            shaped((block, mat.shape[1]), low),
            shaped((width, wide), low),
            shaped((spread_rows, width), low),
        ),
        in_specs=[near] * 4 + [far] * 5,
        out_specs=[near] * 4 + [far] * 2,
        scratch_shapes=[vmem_like(m) for m in (hidden, grad_up, product, down)]
        + [
            pltpu.VMEM((2, width // 2, wide), low),
            pltpu.VMEM((spread_rows, width), low),
            dma_sems(7),
        ]
        + ReducePlane.scratch(block, mat.shape[1])
        + line_scratch(n_line, rows // CHUNKS, width, CHUNKS),
        compiler_params=comm_params(3),
        name="middle_sums",
    )(terms, after, gain, grad_in, mat, hidden, grad_up, product, down)


class Exchange:
    def __init__(self, place, axis, src, slots, send, recv, local):
        self.p, self.src, self.slots = place, src, slots
        self.over_dp = axis == "dp"
        self.size = place.n_dp if self.over_dp else place.n_line
        self.me = place.d if self.over_dp else place.t
        self.send, self.recv, self.local = send, recv, local

    def copy(self, i):
        to = lax.rem(self.me + i, self.size)
        device = (to, self.p.t) if self.over_dp else (self.p.d, to)
        return remote(
            self.src, self.slots.at[self.me], self.send.at[i - 1], self.recv.at[i - 1], device
        )

    def mine(self):
        return pltpu.make_async_copy(self.src, self.slots.at[self.me], self.local)

    def begin(self):
        for i in range(1, self.size):
            self.copy(i).start()
        self.mine().start()

    def wait(self):
        self.mine().wait()
        for i in range(1, self.size):
            self.copy(i).wait()

    def finish(self):
        self.wait()
        total = self.slots[0]
        for i in range(1, self.size):
            total = total + self.slots[i]
        return total


def last_sums(n_dp, n_line, terms, tokens, gain, grad_after, second, small, mats):
    rows, width = tokens.shape
    count = len(mats)
    per = len(ReducePlane.scratch(16, 128))

    def kernel(*refs):
        s, tok, gain_ref, g_ref, second_ref, small_ref = refs[:6]
        srcs = refs[6 : 6 + count]
        grad_tok, small_out, first_out = refs[6 + count : 9 + count]
        results = refs[9 + count : 9 + 2 * count]
        rest = refs[9 + 2 * count :]
        own_first, row_sum = rest[count * per : count * per + 2]
        slots_a, slots_b, slots_c, slots_d = rest[count * per + 2 : count * per + 6]
        xs, xr, xl = rest[count * per + 6 : count * per + 9]
        scratch = rest[count * per + 9 :]
        place = Place(n_dp, n_line)
        place.meet(True)
        planes = [
            ReducePlane(place, srcs[i], rest[i * per : (i + 1) * per]) for i in range(count)
        ]
        for part in planes:
            part.begin()
        early = Exchange(place, "dp", small_ref, slots_a, xs.at[0], xr.at[0], xl.at[0])
        early.begin()
        gain = Exchange(place, "dp", second_ref, slots_d, xs.at[3], xr.at[3], xl.at[3])
        gain.begin()
        own_first[...] = jnp.zeros_like(own_first)

        def norm(c, here, total):
            grad = total[...]
            grad_rows, normed = norm_back(tok[here].astype(jnp.float32), gain_ref[...], grad)
            own_first[...] += jnp.sum(grad * normed, axis=0, keepdims=True)
            grad_tok[here] = g_ref[here] + grad_rows

        def cores():
            for part in planes:
                part.cores()

        def turn():
            for part in planes:
                part.turn()

        sum_rows_and_spread(place, s, scratch, norm, None, {0: cores, 5: turn})
        first = Exchange(place, "dp", own_first, slots_b, xs.at[1], xr.at[1], xl.at[1])
        first.begin()
        small_out[...] = early.finish()
        row_sum[0:1] = gain.finish()
        row_sum[1:2] = first.finish()
        both = Exchange(place, "tensor", row_sum, slots_c, xs.at[2], xr.at[2], xl.at[2])
        both.begin()
        for part, result in zip(planes, results):
            part.finish(result)
        first_out[...] = both.finish()

    return pl.pallas_call(
        kernel,
        out_shape=(
            shaped((rows, width), jnp.float32),
            shaped(small.shape, jnp.float32),
            shaped((2, width), jnp.float32),
        )
        + tuple(shaped((m.shape[0] // n_dp, m.shape[1]), jnp.bfloat16) for m in mats),
        in_specs=[in_vmem()] * 6 + [in_any()] * count,
        out_specs=[in_vmem()] * (3 + count),
        scratch_shapes=sum([ReducePlane.scratch(m.shape[0] // n_dp, m.shape[1]) for m in mats], [])
        + [
            pltpu.VMEM((1, width), jnp.float32),
            pltpu.VMEM((2, width), jnp.float32),
            pltpu.VMEM((n_dp,) + small.shape, jnp.float32),
            pltpu.VMEM((n_dp, 1, width), jnp.float32),
            pltpu.VMEM((n_line, 2, width), jnp.float32),
            pltpu.VMEM((n_dp, 1, width), jnp.float32),
            dma_sems(4, n_dp),
            dma_sems(4, n_dp),
            dma_sems(4),
        ]
        + line_scratch(n_line, rows // LAST_CHUNKS, width, LAST_CHUNKS),
        compiler_params=comm_params(4),
        name="last_sums",
    )(terms, tokens, gain, grad_after, second, small, *mats)


def loop(count, body, unroll=1):
    def step(i, carry):
        body(i)
        return carry

    lax.fori_loop(0, count, step, None, unroll=unroll)


def tile_rows(i, size, ahead=0):
    return pl.ds(pl.multiple_of(i * size + ahead, 8), size)


def moved_up(values, distance, count):
    size = values.shape[0]
    return pltpu.roll(values, (size - distance) % size, 0)[:count]


def take_lanes(ref, here):
    return jnp.concatenate([ref[c, here] for c in range(ref.shape[0])], axis=1)


def put_lanes(ref, here, values):
    for c in range(ref.shape[0]):
        ref[c, here] = values[:, c * LANES : (c + 1) * LANES]


def gelu_parts(values):
    inner = GELU_C * (values + 0.044715 * (values * values * values))
    tanh = jnp.tanh(inner)
    half = 0.5 * (1.0 + tanh)
    slope = half + 0.5 * values * (1.0 - tanh * tanh) * GELU_C * (
        1.0 + 3.0 * 0.044715 * (values * values)
    )
    return values * half, slope


GELU_C = 0.7978845608028654
RIM = 128
LANES = 128
TILE = 16


def one_minus_exp(values, exponential):
    series = jnp.ones_like(values)
    for term in range(9, 1, -1):
        series = 1.0 + values * (1.0 / term) * series
    return jnp.where(values > -0.35, -values * series, 1.0 - exponential)


def rate_and_scale(pre_recur, soft, start):
    sr = jax.nn.sigmoid(pre_recur)
    log_rate = -rate_scale * sr * soft
    decay = jnp.exp(log_rate)
    rate = jnp.where(start, 0.0, decay)
    scale = jnp.where(start, 1.0, jnp.sqrt(one_minus_exp(2.0 * log_rate, decay * decay)))
    return sr, rate, scale


class RimSwap:
    def __init__(self, place, own):
        self.odd = lax.rem(place.t, 2)
        self.partner = (place.d, place.t + 1 - 2 * self.odd)
        self.first = pl.multiple_of(RIM - RIM * self.odd, RIM)
        self.edge = pl.ds(pl.multiple_of((1 - self.odd) * own + self.odd * RIM, RIM), RIM)
        self.over_there = pl.ds(pl.multiple_of(self.odd * (own + RIM), RIM), RIM)
        self.beyond = pl.ds(pl.multiple_of((1 - self.odd) * (own + RIM), RIM), RIM)

    def block(self, index, size):
        return pl.ds(pl.multiple_of(self.first + index * size, RIM), size)


LATE_SHARE = 4


def recur_forward(
    n_dp,
    n_line,
    tok_all,
    cot,
    to_place,
    to_stored,
    x_full,
    y_full,
    out_full,
    gain,
    gates,
    taps,
    soft,
    flags,
):
    rows, width = tok_all.shape
    count, own = taps.shape
    size = gates.shape[0]
    wide = own + 2 * RIM
    blocks = (wide - RIM) // size
    chunk = rows // 8
    cot_rows = cot.shape[0] - cot.shape[0] // LATE_SHARE
    parts = 1

    def kernel(*refs):
        (tok_far, cot_ref, plc, sto, wx_far, wy_far, wo_far, gain_ref, gates_in, cw, sp, fl) = refs[:12]
        far, gw, cot_all = refs[12:23], refs[23], refs[24]
        tok, wx, wy, wo = refs[25:29]
        results = refs[29:40]
        hp, xext, y, conv_low, conv, pre_r, pre_i, rate, state, merged_st, terms = results
        (h, xf, local, cum, merged, agg, slots, hs, hr, es, er, el, gs, gr, gl) = refs[40:55]
        in_sems, out_sems, cot_held = refs[55:]
        fetch = Fetch(((tok_far, tok), (wx_far, wx), (wy_far, wy), (wo_far, wo)), in_sems)
        store = Fetch(zip(results, far), out_sems)
        fetch.start(0, 1, 2, 3)
        place = Place(n_dp, n_line)
        place.meet(True)
        swap = RimSwap(place, own)
        for side in range(2):
            first = side * wide
            gw[:, first : first + RIM] = jnp.zeros((size, RIM), jnp.bfloat16)
            gw[:, first + RIM : first + RIM + own] = gates_in[:, side * own : (side + 1) * own]
            gw[:, first + RIM + own : first + wide] = jnp.zeros((size, RIM), jnp.bfloat16)
        own_cot = cot_all.at[pl.ds(pl.multiple_of(place.t * cot_rows, 16), cot_rows)]
        cot_ref = cot_ref.at[pl.ds(0, cot_rows)]
        keep = Kept(cot_ref, own_cot, cot_held, gl)
        keep.begin()
        span = cot_rows // parts
        lines = [
            GatherLine(place, cot_all, cot_rows, c * span, span, gs.at[c], gr.at[c])
            for c in range(parts)
        ]
        for c, line in enumerate(lines):
            line.step(0, cot_ref.at[pl.ds(c * span, span)])

        def norm(i):
            here = tile_rows(i, TILE)
            h[here] = rms_scale(tok[here].astype(jnp.float32), gain_ref[...]).astype(jnp.bfloat16)

        fetch.wait(0)
        loop(rows // TILE, norm)
        fetch.wait(1)

        def project(i):
            here = tile_rows(i, 128)
            hp[here] = plain_dot(plc[here], h[...]).astype(jnp.bfloat16)
            xext[tile_rows(i, 128, 16)] = plain_dot(hp[here], wx[...]).astype(jnp.bfloat16)

        loop(rows // 128, project)
        store.start(0)
        edge = remote(
            xext.at[pl.ds(rows, 16)],
            xext.at[pl.ds(0, 16)],
            hs.at[0],
            hr.at[0],
            (lax.rem(place.d + 1, n_dp), place.t),
        )
        edge.start()
        keep.turn()
        for line in lines:
            line.step(1)

        def project_y(i):
            here = tile_rows(i, 128)
            y[here] = plain_dot(hp[here], wy[...])

        fetch.wait(2)
        loop(rows // 128, project_y)
        store.start(2)
        edge.wait()
        top = xext[pl.ds(0, 16)]
        xext[pl.ds(0, 16)] = jnp.where(place.d > 0, top, jnp.zeros_like(top))
        store.start(1)

        def widen(i):
            xf[tile_rows(i, TILE)] = xext[tile_rows(i, TILE)].astype(jnp.float32)

        loop(rows // TILE + 1, widen)

        def convolve(i):
            here = tile_rows(i, TILE)
            near = xf[pl.ds(pl.multiple_of(i * TILE + 8, 8), TILE + 8)]
            same = fl[tile_rows(i, TILE, 8)]
            total = cw[0:1] * near[8:]
            for k in range(1, count):
                total += cw[k : k + 1] * moved_up(near, 8 - k, TILE) * same[:, k : k + 1]
            conv[here] = total
            conv_low[here, RIM : RIM + own] = total.astype(jnp.bfloat16)

        loop(rows // TILE, convolve)
        store.start(4)
        rim = remote(
            conv_low.at[:, swap.edge],
            conv_low.at[:, swap.over_there],
            hs.at[1],
            hr.at[1],
            swap.partner,
        )
        rim.start()
        for i in range(blocks):
            index = lax.rem(i + swap.odd, blocks)
            cols = swap.block(index, size)
            other = pl.ds(pl.multiple_of(wide + swap.first + index * size, RIM), size)
            if i == blocks - 1:
                rim.wait()
            pre_r[:, cols] = plain_dot(conv_low[:, cols], gw[:, cols])
            pre_i[:, cols] = plain_dot(conv_low[:, cols], gw[:, other])

        store.start(3, 5, 6)

        def drive(i):
            here = tile_rows(i, TILE)
            start = fl[tile_rows(i, TILE, 8)][:, 0:1] > 0.0
            own_cols = pl.ds(RIM, own)
            _, decay, scale = rate_and_scale(pre_r[here, own_cols], sp[...], start)
            put_lanes(rate, here, decay)
            put_lanes(local, here, conv[here] * jax.nn.sigmoid(pre_i[here, own_cols]) * scale)

        loop(rows // TILE, drive)
        store.start(7)
        for line in lines:
            line.step(2)
        groups = own // LANES

        def scan(i, carry):
            here = pl.ds(i, 8, chunk)
            result = []
            for c in range(groups):
                product, total = carry[c]
                r = rate[c, here]
                product = product * r
                total = total * r + local[c, here]
                cum[c, here] = product
                local[c, here] = total
                result.append((product, total))
            return tuple(result)

        blank = (jnp.ones((8, LANES), jnp.float32), jnp.zeros((8, LANES), jnp.float32))
        lax.fori_loop(0, chunk, scan, (blank,) * groups)
        product, total = jnp.ones((1, own), jnp.float32), jnp.zeros((1, own), jnp.float32)
        for j in range(8):
            last = pl.ds(j * chunk + chunk - 1, 1)
            total = take_lanes(local, last) + take_lanes(cum, last) * total
            product = product * take_lanes(cum, last)
        agg[0:1] = product
        agg[1:2] = total
        swap_all = Exchange(place, "dp", agg, slots, es, er, el)
        swap_all.begin()
        swap_all.wait()
        entry = jnp.zeros((1, own), jnp.float32)
        for q in range(n_dp):
            longer = slots[q, 1:2] + slots[q, 0:1] * entry
            entry = jnp.where(q < place.d, longer, entry)
        state[pl.ds(0, 8)] = jnp.broadcast_to(entry, (8, own))
        for j in range(8):

            def settle(i, entry=entry):
                here = tile_rows(i, TILE, j * chunk)
                values = take_lanes(local, here) + take_lanes(cum, here) * entry
                state[tile_rows(i, TILE, j * chunk + 8)] = values
                merged[here] = (values * gelu_parts(y[here])[0]).astype(jnp.bfloat16)

            loop(chunk // TILE, settle)
            last = pl.ds(j * chunk + chunk - 1, 1)
            entry = take_lanes(local, last) + take_lanes(cum, last) * entry
        store.start(8)
        merged_st[...] = plain_dot(sto[...], merged[...]).astype(jnp.bfloat16)

        store.start(9)
        fetch.wait(3)

        def mix(i):
            some = tile_rows(i, 512)
            terms[:, pl.ds(pl.multiple_of(i * 512, 512), 512)] = times_trans(
                merged_st[...], wo[some, :]
            ).astype(jnp.bfloat16)

        loop(width // 512, mix)
        for line in lines:
            line.finish()
        keep.finish()
        store.start(10)
        store.wait(*range(11))

    low, full = jnp.bfloat16, jnp.float32
    results = (
        shaped((rows, width), low),
        shaped((rows + 16, own), low),
        shaped((rows, own), full),
        shaped((rows, wide), low),
        shaped((rows, own), full),
        shaped((rows, wide), full),
        shaped((rows, wide), full),
        shaped((own // LANES, rows, LANES), full),
        shaped((rows + 8, own), full),
        shaped((rows, own), low),
        shaped((rows, width), low),
    )
    near, far = in_vmem(), in_any()
    return pl.pallas_call(
        kernel,
        out_shape=results
        + (shaped((size, 2 * wide), low), shaped((n_line * cot_rows, width), low)),
        in_specs=[far, far, near, near, far, far, far] + [near] * 5,
        out_specs=[far] * 11 + [near, far],
        scratch_shapes=[vmem_like(m) for m in (tok_all, x_full, y_full, out_full) + results]
        + [
            pltpu.VMEM((rows, width), low),
            pltpu.VMEM((rows + 16, own), full),
            pltpu.VMEM((own // LANES, rows, LANES), full),
            pltpu.VMEM((own // LANES, rows, LANES), full),
            pltpu.VMEM((rows, own), low),
            pltpu.VMEM((2, own), full),
            pltpu.VMEM((n_dp, 2, own), full),
            dma_sems(2),
            dma_sems(2),
            dma_sems(n_dp),
            dma_sems(n_dp),
            pltpu.SemaphoreType.DMA,
            dma_sems(parts, 2, n_line - 1),
            dma_sems(parts, 2, n_line - 1),
            dma_sems(2),
            dma_sems(4),
            dma_sems(11),
            pltpu.VMEM((cot_rows, width), low),
        ],
        compiler_params=comm_params(5),
        name="recur_forward",
    )(
        tok_all,
        cot,
        to_place,
        to_stored,
        x_full,
        y_full,
        out_full,
        gain,
        gates,
        taps,
        soft,
        flags,
    )


class RowProducts:
    def __init__(self, left, right, far, stage, sems):
        self.left, self.right, self.far, self.stage, self.sems = left, right, far, stage, sems
        self.part = stage.shape[1]
        self.count = far.shape[0] // self.part

    def slot(self, i):
        return self.stage.at[i % 2, :, pl.ds(0, self.far.shape[1])]

    def copy(self, i):
        some = pl.ds(i * self.part, self.part)
        return pltpu.make_async_copy(self.slot(i), self.far.at[some], self.sems.at[i])

    def run(self):
        for i in range(self.count):
            if i >= 2:
                self.copy(i - 2).wait()
            some = pl.ds(i * self.part, self.part)
            self.slot(i)[...] = trans_times(self.left[:, some], self.right[...]).astype(
                jnp.bfloat16
            )
            self.copy(i).start()

    def finish(self):
        self.copy(self.count - 2).wait()
        self.copy(self.count - 1).wait()


def recur_backward(
    n_dp,
    n_line,
    mixer_in,
    to_place,
    to_stored,
    x_full,
    y_full,
    out_full,
    gates,
    taps,
    soft,
    slope,
    flags,
    kept,
    weight_terms,
    row_terms,
    hidden_place,
    merged_stored,
):
    rows, width = mixer_in.shape
    count, own = taps.shape
    size = gates.shape[0]
    wide = own + 2 * RIM
    blocks = (wide - RIM) // size
    chunk = rows // 8
    own_rows = rows // n_line
    parts = 4
    span = own_rows // parts

    def kernel(*refs):
        (mix_far, plc, sto, wx_far, wy_far, wo_far, gw, cw, sp, sg, fl) = refs[:11]
        kept_far, weights, feed_far, hp_far, merged_far = refs[11:19], *refs[19:23]
        (gate_grads, tap_grads, terms_far, weight_sum, row_sum) = refs[23:28]
        out_far, xy_far = refs[28:30]
        mix, wy, wo, feed, merged = refs[30:35]
        (xext, y, conv_low, conv, pre_r, pre_i, rate, state) = refs[35:43]
        (gxy, mp, gm, lam, reach, gp_r, gp_i, grad, spread, rim_out, rim_in) = refs[43:54]
        (ret_out, ret_in, tap_sums, decay_sums, ends, agg, slots) = refs[54:61]
        (hs, hr, es, er, el, in_sems, out_sems, inbox, ls, lr, total) = refs[61:72]
        stage, stage_sems = refs[72:74]
        hp, terms, wx = mix, mix, wo
        fetch = Fetch(
            [
                (mix_far, mix),
                (wo_far, wo),
                (kept_far[1], y),
                (kept_far[7], state),
                (kept_far[6], rate),
                (kept_far[4], pre_r),
                (kept_far[5], pre_i),
                (kept_far[3], conv),
                (kept_far[2], conv_low),
                (kept_far[0], xext),
                (wx_far, wx),
                (wy_far, wy),
                (feed_far, feed),
                (merged_far, merged),
                (hp_far, hp),
            ],
            in_sems,
        )
        fetch.start(12, 0, 1, 13)
        store = Fetch(((terms, terms_far),), out_sems)
        out_rows = RowProducts(mix, merged, out_far, stage, stage_sems.at[0])
        xy_rows = RowProducts(hp, gxy, xy_far, stage, stage_sems.at[1])
        place = Place(n_dp, n_line)
        place.meet(True)
        plane = ReducePlane(place, weights, refs[74:])
        plane.begin()
        lines = [
            ReduceLine(place, feed, own_rows, c * span, span, inbox.at[c], ls.at[c], lr.at[c])
            for c in range(parts)
        ]

        def send(c):
            if c > 0:
                lines[c - 1].sent()
            if c < parts:
                lines[c].ends()

        def add_up(c):
            lines[c].total(total)
            row_sum[pl.ds(c * span, span)] = total[...].astype(jnp.bfloat16)

        fetch.wait(12)
        send(0)
        fetch.start(*range(2, 10), 11)
        swap = RimSwap(place, own)
        own_cols = pl.ds(RIM, own)

        def project(i):
            here = tile_rows(i, 128)
            mp[here] = plain_dot(plc[here], mix[...]).astype(jnp.bfloat16)
            gm[here] = plain_dot(mp[here], wo[...])

        fetch.wait(0, 1)
        loop(rows // 128, project)
        fetch.start(10)
        fetch.wait(13)
        out_rows.run()
        fetch.start(14)

        def split(i):
            here = tile_rows(i, TILE)
            branch, slope_y = gelu_parts(y[here])
            grads = gm[here]
            put_lanes(lam, here, grads * branch)
            values = state[tile_rows(i, TILE, 8)]
            gxy[here, own:] = (grads * values * slope_y).astype(jnp.bfloat16)

        fetch.wait(2, 3)
        loop(rows // TILE, split)
        send(1)
        lines[0].hop(0)
        fetch.wait(4)
        groups = own // LANES

        def scan(i, carry):
            here = pl.ds(chunk - 1 - i, 8, chunk)
            result = []
            for c in range(groups):
                product, message = carry[c]
                r = rate[c, here]
                value = lam[c, here] + message
                lam[c, here] = value
                reach[c, here] = product
                result.append((product * r, value * r))
            return tuple(result)

        blank = (jnp.ones((8, LANES), jnp.float32), jnp.zeros((8, LANES), jnp.float32))
        done = lax.fori_loop(0, chunk, scan, (blank,) * groups)
        for c in range(groups):
            lanes = pl.ds(c * LANES, LANES)
            ends[0, :, lanes] = done[c][0]
            ends[1, :, lanes] = done[c][1]
        product, message = jnp.ones((1, own), jnp.float32), jnp.zeros((1, own), jnp.float32)
        for j in reversed(range(8)):
            message = ends[1, j : j + 1] + ends[0, j : j + 1] * message
            product = product * ends[0, j : j + 1]
        agg[0:1] = product
        agg[1:2] = message
        swap_all = Exchange(place, "dp", agg, slots, es, er, el)
        swap_all.begin()
        plane.cores()
        swap_all.wait()
        lines[0].hop(1)
        entry = jnp.zeros((1, own), jnp.float32)
        for q in reversed(range(n_dp)):
            longer = slots[q, 1:2] + slots[q, 0:1] * entry
            entry = jnp.where(q > place.d, longer, entry)
        fetch.wait(5, 6, 7)
        for ref in (tap_sums, decay_sums):
            ref[...] = jnp.zeros_like(ref)
        for ref in (gp_r, gp_i):
            ref[:, 0:RIM] = jnp.zeros((rows, RIM), jnp.bfloat16)
            ref[:, RIM + own :] = jnp.zeros((rows, RIM), jnp.bfloat16)
        grad[pl.ds(0, 8)] = jnp.zeros((8, own), jnp.float32)
        grad[pl.ds(rows + 8, 8)] = jnp.zeros((8, own), jnp.float32)
        for j in reversed(range(8)):

            def back(i, entry=entry):
                here = tile_rows(i, TILE, j * chunk)
                flag = fl[tile_rows(i, TILE, j * chunk + 8)]
                start = flag[:, 0:1] > 0.0
                values = take_lanes(lam, here) + take_lanes(reach, here) * entry
                before = moved_up(
                    state[pl.ds(pl.multiple_of(j * chunk + i * TILE, 8), TILE + 8)], 7, TILE
                )
                sr, decay, scale = rate_and_scale(pre_r[here, own_cols], sp[...], start)
                si = jax.nn.sigmoid(pre_i[here, own_cols])
                block = conv[here]
                driven = values * si
                log_grad = values * before * decay - block * driven * (decay * decay) / scale
                log_grad = jnp.where(start, 0.0, log_grad)
                inner = sr * log_grad
                gp_r[here, own_cols] = (
                    -rate_scale * sp[...] * inner * (1.0 - sr)
                ).astype(jnp.bfloat16)
                gp_i[here, own_cols] = (driven * block * (1.0 - si) * scale).astype(jnp.bfloat16)
                grad[tile_rows(i, TILE, j * chunk + 8)] = driven * scale
                decay_sums[...] += inner[:8] + inner[8:]

            loop(chunk // TILE, back)
            if j == 4:
                send(2)
                lines[1].hop(0)
            entry = ends[1, j : j + 1] + ends[0, j : j + 1] * entry
        lines[1].hop(1)
        add_up(0)

        for i in range(blocks):
            index = lax.rem(i + 2 - 2 * swap.odd, blocks)
            cols = swap.block(index, size)
            other = pl.ds(pl.multiple_of(wide + swap.first + index * size, RIM), size)
            spread[:, cols] = times_trans(gp_r[:, cols], gw[:, cols]) + times_trans(
                gp_i[:, cols], gw[:, other]
            )
            if i == 0:
                rim_out[...] = spread[:, swap.beyond].astype(jnp.bfloat16)
                rim = remote(rim_out, rim_in, hs.at[0], hr.at[0], swap.partner)
                rim.start()
        send(3)
        lines[2].hop(0)
        rim.wait()
        shared = pl.ds(pl.multiple_of((1 - swap.odd) * (own - RIM), RIM), RIM)

        def join(i):
            here = tile_rows(i, TILE)
            there = tile_rows(i, TILE, 8)
            grad[there] += spread[here, own_cols]
            grad[there, shared] += rim_in[here].astype(jnp.float32)

        loop(rows // TILE, join)

        near = grad[pl.ds(0, 16)]
        back_rows = jnp.zeros((8, own), jnp.float32)
        for k in range(1, count):
            masked = near * fl[pl.ds(0, 16)][:, k : k + 1]
            back_rows += cw[k : k + 1] * moved_up(masked, k, 8)
        ret_out[...] = back_rows
        ret = remote(
            ret_out,
            ret_in,
            hs.at[1],
            hr.at[1],
            (lax.rem(place.d + n_dp - 1, n_dp), place.t),
        )
        ret.start()
        fetch.wait(8)
        for i in range(blocks):
            cols = swap.block(i, size)
            spread[0:size, cols] = trans_times(conv_low[:, cols], gp_r[:, cols])
            spread[size : 2 * size, cols] = trans_times(conv_low[:, cols], gp_i[:, cols])
        gate_grads[:, 0:own] = spread[0:size, own_cols].astype(jnp.bfloat16)
        gate_grads[:, own:] = spread[size : 2 * size, own_cols].astype(jnp.bfloat16)

        def taps_back(i, added=None):
            here = tile_rows(i, TILE)
            start = pl.ds(pl.multiple_of(i * TILE + 8, 8), TILE + 8)
            after = grad[start]
            flag = fl[start]
            behind = xext[pl.ds(pl.multiple_of(i * TILE, 16), 2 * TILE)].astype(jnp.float32)
            total = cw[0:1] * after[:TILE]
            for k in range(count):
                if k > 0:
                    masked = after * flag[:, k : k + 1]
                    total += cw[k : k + 1] * moved_up(masked, k, TILE)
                    mine = masked[:TILE]
                else:
                    mine = after[:TILE]
                term = mine * moved_up(behind, 16 - k, TILE)
                tap_sums[k] += term[:8] + term[8:]
            if added is not None:
                total = total + jnp.concatenate([jnp.zeros((8, own), jnp.float32), added], axis=0)
            gxy[here, 0:own] = total.astype(jnp.bfloat16)

        fetch.wait(9)
        loop(rows // TILE - 1, taps_back)
        lines[2].hop(1)
        add_up(1)
        ret.wait()
        taps_back(rows // TILE - 1, jnp.where(place.d < n_dp - 1, ret_in[...], 0.0))
        tap_grads[...] = jnp.zeros_like(tap_grads)
        for k in range(count):
            tap_grads[k : k + 1] = jnp.sum(tap_sums[k], axis=0, keepdims=True)
        tap_grads[count : count + 1] = (
            rate_scale * sg[...] * jnp.sum(decay_sums[...], axis=0, keepdims=True)
        )

        fetch.wait(14)
        out_rows.finish()
        plane.turn()
        xy_rows.run()
        send(4)
        lines[3].hop(0)

        def restore(i):
            here = tile_rows(i, 128)
            mp[here, 0 : 2 * own] = plain_dot(sto[here], gxy[...]).astype(jnp.bfloat16)

        loop(rows // 128, restore)

        def spread_back(i):
            some = tile_rows(i, 512)
            terms[:, pl.ds(pl.multiple_of(i * 512, 512), 512)] = (
                times_trans(mp[:, 0:own], wx[some]) + times_trans(mp[:, own : 2 * own], wy[some])
            ).astype(jnp.bfloat16)

        fetch.wait(10, 11)
        loop(width // 512, spread_back)
        store.start(0)
        lines[3].hop(1)
        add_up(2)
        plane.finish(weight_sum)
        add_up(3)
        for line in lines:
            line.finish()
        xy_rows.finish()
        store.wait(0)

    low, full = jnp.bfloat16, jnp.float32
    block = weight_terms.shape[0] // n_dp
    near, far = in_vmem(), in_any()
    return pl.pallas_call(
        kernel,
        out_shape=(
            shaped((size, 2 * own), low),
            shaped((8, own), full),
            shaped((rows, width), low),
            shaped((block, weight_terms.shape[1]), low),
            shaped((own_rows, width), low),
            shaped((width, own), low),
            shaped((width, 2 * own), low),
        ),
        in_specs=[far, near, near, far, far, far] + [near] * 5 + [far] * 12,
        out_specs=[near, near, far, near, near, far, far],
        scratch_shapes=[
            vmem_like(m) for m in (mixer_in, y_full, out_full, row_terms, merged_stored, *kept)
        ]
        + [
            pltpu.VMEM((rows, 2 * own), low),
            pltpu.VMEM((rows, width), low),
            pltpu.VMEM((rows, own), full),
            pltpu.VMEM((own // LANES, rows, LANES), full),
            pltpu.VMEM((own // LANES, rows, LANES), full),
            pltpu.VMEM((rows, wide), low),
            pltpu.VMEM((rows, wide), low),
            pltpu.VMEM((rows + 16, own), full),
            pltpu.VMEM((rows, wide), full),
            pltpu.VMEM((rows, RIM), low),
            pltpu.VMEM((rows, RIM), low),
            pltpu.VMEM((8, own), full),
            pltpu.VMEM((8, own), full),
            pltpu.VMEM((count, 8, own), full),
            pltpu.VMEM((8, own), full),
            pltpu.VMEM((2, 8, own), full),
            pltpu.VMEM((2, own), full),
            pltpu.VMEM((n_dp, 2, own), full),
            dma_sems(2),
            dma_sems(2),
            dma_sems(n_dp),
            dma_sems(n_dp),
            pltpu.SemaphoreType.DMA,
            dma_sems(15),
            dma_sems(1),
            pltpu.VMEM((parts, 2, n_line - 1, span, width), low),
            dma_sems(parts, 2, n_line - 1),
            dma_sems(parts, 2, n_line - 1),
            pltpu.VMEM((span, width), full),
            pltpu.VMEM((2, width // 5, 2 * own), low),
            dma_sems(2, 5),
        ]
        + ReducePlane.scratch(block, weight_terms.shape[1]),
        compiler_params=comm_params(6),
        name="recur_backward",
    )(
        mixer_in,
        to_place,
        to_stored,
        x_full,
        y_full,
        out_full,
        gates,
        taps,
        soft,
        slope,
        flags,
        *kept,
        weight_terms,
        row_terms,
        hidden_place,
        merged_stored,
    )


def column_parts(width, size=768):
    return [(c, min(size, width - c)) for c in range(0, width, size)]


def feed_forward(n_dp, n_line, hidden, gate, up, down, grads, grad_own):
    rows, width = hidden.shape
    units = gate.shape[1]
    own_rows = grad_own.shape[0]
    ready = grads.shape[0] // n_line
    late = own_rows - ready
    part = width // 4

    def kernel(*refs):
        hid_far, wg_far, wu_far, wd_far, grads_far, own_far = refs[:6]
        product_far, gup_far, back_far, gdown_far, ggate_far = refs[6:11]
        hid, wg, wu, wd, grad, slope, branch, product, ggate, gup, stage, back = refs[11:23]
        in_sems, out_sems, stage_sems, ls, lr = refs[23:]
        place = Place(n_dp, n_line)
        pairs = [(hid_far, hid), (wg_far, wg), (wu_far, wu), (wd_far, wd)]
        pairs += [
            (grads_far.at[pl.ds(q * ready, ready)], grad.at[pl.ds(q * own_rows, ready)])
            for q in range(n_line)
        ]
        mine = pl.ds(pl.multiple_of(place.t * own_rows + ready, 16), late)
        pairs.append((own_far.at[pl.ds(ready, late)], grad.at[mine]))
        fetch = Fetch(pairs, in_sems)
        fetch.start(*range(len(pairs)))
        store = Fetch(((product, product_far), (gup, gup_far), (back, back_far)), out_sems)
        place.meet()
        line = GatherLine(place, grad, own_rows, ready, late, ls, lr)
        line.step(0, own_far.at[pl.ds(ready, late)])
        columns = column_parts(units)
        fetch.wait(0, 1)
        for c, size in columns:
            cols = pl.ds(c, size)

            def gates(i, cols=cols):
                here = tile_rows(i, 256)
                branch[here, cols] = plain_dot(hid[here], wg[:, cols])

            loop(rows // 256, gates)
        line.step(1)
        fetch.wait(2)
        for c, size in columns:
            cols = pl.ds(c, size)

            def ups(i, cols=cols):
                here = tile_rows(i, 256)
                value = plain_dot(hid[here], wu[:, cols])
                active, bend = gelu_parts(branch[here, cols])
                product[here, cols] = (active * value).astype(jnp.bfloat16)
                branch[here, cols] = active
                slope[here, cols] = bend * value

            loop(rows // 256, ups)
        store.start(0)
        line.step(2)
        fetch.wait(*range(4, len(pairs)))
        line.finish()

        down_rows = RowProducts(grad, product, gdown_far, stage, stage_sems.at[0])
        down_rows.run()
        fetch.wait(3)
        for c, size in columns:
            cols = pl.ds(c, size)

            def backs(i, cols=cols):
                here = tile_rows(i, 256)
                value = plain_dot(grad[here], wd[:, cols])
                ggate[here, cols] = (value * slope[here, cols]).astype(jnp.bfloat16)
                gup[here, cols] = (value * branch[here, cols]).astype(jnp.bfloat16)

            loop(rows // 256, backs)
        store.start(1)
        for i in range(4):
            some = pl.ds(i * part, part)
            back[:, some] = (
                times_trans(ggate[...], wg[some]) + times_trans(gup[...], wu[some])
            ).astype(jnp.bfloat16)
        store.start(2)
        down_rows.finish()
        gate_rows = RowProducts(hid, ggate, ggate_far, stage, stage_sems.at[1])
        gate_rows.run()
        gate_rows.finish()
        store.wait(0, 1, 2)

    low, full = jnp.bfloat16, jnp.float32
    return pl.pallas_call(
        kernel,
        out_shape=(
            shaped((rows, units), low),
            shaped((rows, units), low),
            shaped((rows, width), low),
            shaped((width, units), low),
            shaped((width, units), low),
        ),
        in_specs=[in_any()] * 6,
        out_specs=[in_any()] * 5,
        scratch_shapes=[vmem_like(m) for m in (hidden, gate, up, down)]
        + [
            pltpu.VMEM((n_line * own_rows, width), low),
            pltpu.VMEM((rows, units), full),
            pltpu.VMEM((rows, units), full),
            pltpu.VMEM((rows, units), low),
            pltpu.VMEM((rows, units), low),
            pltpu.VMEM((rows, units), low),
            pltpu.VMEM((2, part, units), low),
            pltpu.VMEM((rows, width), low),
            dma_sems(5 + n_line),
            dma_sems(3),
            dma_sems(2, 4),
            dma_sems(2, n_line - 1),
            dma_sems(2, n_line - 1),
        ],
        compiler_params=comm_params(7),
        name="feed_forward",
    )(hidden, gate, up, down, grads, grad_own)


def matches(mesh):
    return mesh.shape["dp"] == 8 and mesh.shape["tensor"] == 4


def local_blocks(
    tokens,
    norm_gain,
    x_weight,
    y_weight,
    conv_weight,
    recur_gate_weight,
    input_gate_weight,
    decay_param,
    out_weight,
    mlp_gain,
    gate_weight,
    up_weight,
    down_weight,
    seq_lengths,
    token_order,
    cotangent,
):
    n_dp, n_tensor = lax.axis_size("dp"), lax.axis_size("tensor")
    tensor_index = lax.axis_index("tensor")
    dp_index = lax.axis_index("dp")
    tok_rows, width = tokens.shape
    row_count = tok_rows * n_tensor
    own_width = conv_weight.shape[1]
    kernel_taps = conv_weight.shape[0]
    edge_rows = kernel_taps - 1
    dp_width = norm_gain.shape[0]
    gate_rows = recur_gate_weight.shape[0]
    own_start = tensor_index * tok_rows

    gains = jnp.concatenate([norm_gain, mlp_gain])
    spare = gate_rows * 128 - gains.shape[0]
    gains = jnp.pad(gains, (0, spare)).reshape(gate_rows, 128)
    minor = jnp.concatenate([recur_gate_weight, input_gate_weight, gains], axis=1)
    own_order = (token_order - dp_index * row_count).astype(jnp.int32)
    order_rows = jnp.broadcast_to(own_order[None, :], (8, tok_rows))
    x_full, y_full, out_full, minor_full, tok_all, order_full = first_gather(
        n_dp, n_tensor, (x_weight, y_weight, out_weight.T, minor), tokens, order_rows
    )
    late_up, late_down, _ = lax.optimization_barrier((up_weight, down_weight.T, tok_all))
    up_full = lax.all_gather(late_up, "dp", axis=0, tiled=True)
    down_full = lax.all_gather(late_down, "dp", axis=0, tiled=True)
    order_all = order_full.reshape(n_tensor, 8, tok_rows)[:, 0].reshape(row_count)
    gain_rows = minor_full[:, 2 * own_width :].reshape(n_dp, -1)
    first_gain = gain_rows[:, :dp_width].reshape(1, width).astype(jnp.float32)
    second_gain = gain_rows[:, dp_width : 2 * dp_width].reshape(1, width).astype(jnp.float32)
    row_index = jnp.arange(row_count, dtype=jnp.int32)
    hits = row_index[:, None] == order_all[None, :]
    to_place = hits.astype(jnp.bfloat16)
    to_stored = (order_all[:, None] == row_index[None, :]).astype(jnp.bfloat16)
    places = dp_index * row_count + jnp.arange(-8, row_count + 8, dtype=jnp.int32)
    inside = (jnp.arange(row_count + 16) >= 8) & (jnp.arange(row_count + 16) < row_count + 8)
    ends = jnp.cumsum(seq_lengths)
    segment = segment_of(places, ends)
    starts = (places == 0) | (segment != segment_of(places - 1, ends))
    columns = [starts] + [
        segment_of(places - shift, ends) == segment for shift in range(1, kernel_taps)
    ]
    columns += [jnp.zeros_like(starts)] * (8 - len(columns))
    flags = (jnp.stack(columns, axis=1) & inside[:, None]).astype(jnp.float32)
    live_own = (token_order < ends[-1]).astype(jnp.float32)
    grad_in_own = (cotangent.astype(jnp.float32) * live_own[:, None]).astype(jnp.bfloat16)
    soft = jax.nn.softplus(-decay_param).reshape(1, own_width)
    slope = jax.nn.sigmoid(-decay_param).reshape(1, own_width)
    hidden_place, *kept, merged_stored, mixer_terms, gates_wide, grad_rows = recur_forward(
        n_dp,
        n_tensor,
        tok_all,
        grad_in_own,
        to_place,
        to_stored,
        x_full,
        y_full,
        out_full,
        first_gain,
        minor_full,
        conv_weight,
        soft,
        flags,
    )
    after_own, hidden_two, gate_full = middle_gather(
        n_dp, n_tensor, mixer_terms, tokens, second_gain, (gate_weight,)
    )
    product, grad_up_pre, back_terms, grad_down, grad_gate = feed_forward(
        n_dp,
        n_tensor,
        hidden_two,
        gate_full,
        up_full,
        down_full,
        grad_rows,
        grad_in_own,
    )
    down_sum = lax.psum_scatter(grad_down, "dp", scatter_dimension=0, tiled=True)
    grad_after_own, second_part, mixer_in, gate_sum, grad_up, feed_terms = middle_sums(
        n_dp,
        n_tensor,
        back_terms,
        after_own,
        second_gain,
        grad_in_own,
        grad_gate,
        hidden_two,
        grad_up_pre,
        product,
        down_full,
    )
    (
        gate_grads,
        tap_grads,
        one_terms,
        up_sum,
        feed_out,
        grad_out_mat,
        grad_xy_mat,
    ) = recur_backward(
        n_dp,
        n_tensor,
        mixer_in,
        to_place,
        to_stored,
        x_full,
        y_full,
        out_full,
        gates_wide,
        conv_weight,
        soft,
        slope,
        flags,
        kept,
        grad_up,
        feed_terms,
        hidden_place,
        merged_stored,
    )
    output = (after_own + feed_out.astype(jnp.float32)) * live_own[:, None]
    output = output.astype(jnp.bfloat16)
    grad_tokens, small_sum, gain_sums, xy_sum, out_sum, gates_sum = last_sums(
        n_dp,
        n_tensor,
        one_terms,
        tokens,
        first_gain,
        grad_after_own,
        second_part,
        tap_grads,
        (grad_xy_mat, grad_out_mat, gate_grads),
    )
    xy_sum, gates_sum = xy_sum.astype(jnp.float32), gates_sum.astype(jnp.float32)
    own_gains = lax.dynamic_slice_in_dim(gain_sums, dp_index * dp_width, dp_width, 1)
    return (
        output,
        grad_tokens,
        own_gains[1],
        xy_sum[:, :own_width],
        xy_sum[:, own_width:],
        small_sum[:kernel_taps],
        gates_sum[:, :own_width],
        gates_sum[:, own_width:],
        small_sum[kernel_taps],
        out_sum.astype(jnp.float32).T,
        own_gains[0],
        gate_sum.astype(jnp.float32),
        up_sum.astype(jnp.float32),
        down_sum.astype(jnp.float32).T,
    )


def solution(mesh):
    in_specs = (
        P(("dp", "tensor"), None),
        P("dp"),
        P("dp", "tensor"),
        P("dp", "tensor"),
        P(None, "tensor"),
        P("dp", "tensor"),
        P("dp", "tensor"),
        P("tensor"),
        P("tensor", "dp"),
        P("dp"),
        P("dp", "tensor"),
        P("dp", "tensor"),
        P("tensor", "dp"),
        P(),
        P(("dp", "tensor")),
        P(("dp", "tensor"), None),
    )
    out_specs = (
        P(("dp", "tensor"), None),
        P(("dp", "tensor"), None),
        P("dp"),
        P("dp", "tensor"),
        P("dp", "tensor"),
        P(None, "tensor"),
        P("dp", "tensor"),
        P("dp", "tensor"),
        P("tensor"),
        P("tensor", "dp"),
        P("dp"),
        P("dp", "tensor"),
        P("dp", "tensor"),
        P("tensor", "dp"),
    )
    fits = matches(mesh)
    local = local_blocks if fits else local_general
    return jax.shard_map(local, mesh=mesh, in_specs=in_specs, out_specs=out_specs, check_vma=False)
```

```python
import jax
import jax.numpy as jnp
from jax import lax
from jax.experimental import pallas as pl
from jax.experimental.pallas import tpu as pltpu
from jax.sharding import PartitionSpec as P

epsilon = 1e-06
rate_scale = 8.0


def from_behind(block, axis, distance):
    devices = range(lax.axis_size(axis))
    route = [(i - distance, i) for i in devices if i - distance in devices]
    return lax.ppermute(block, axis, route)


def extended_2(array, sides, width):
    for axis, dim in sides:
        size, length = (lax.axis_size(axis), array.shape[dim])
        up = [(i, (i + 1) % size) for i in range(size - 1)]
        down = [(j, i) for i, j in up]
        last = lax.slice_in_dim(array, length - width, length, axis=dim)
        leading = lax.slice_in_dim(array, 0, width, axis=dim)
        before = lax.ppermute(last, axis, up)
        after = lax.ppermute(leading, axis, down)
        array = jnp.concatenate([before, array, after], axis=dim)
    return array


def entering(value, axis, join, neutral, backward):
    count, mine = (lax.axis_size(axis), lax.axis_index(axis))
    pieces = jax.tree.map(lambda part: lax.all_gather(part, axis), value)
    if backward:
        pieces = jax.tree.map(lambda part: part[::-1], pieces)
        mine = count - 1 - mine
    total = jax.tree.map(
        lambda part, zero: jnp.full_like(part, 0) + jnp.asarray(zero, part.dtype), value, neutral
    )

    def lap(position, total):
        longer = join(total, jax.tree.map(lambda part: part[position], pieces))
        return jax.tree.map(lambda new, old: jnp.where(position < mine, new, old), longer, total)

    return lax.fori_loop(0, count - 1, lap, total)


def rms_scale(values, gain):
    return values * lax.rsqrt(jnp.mean(values * values, axis=-1, keepdims=True) + epsilon) * gain


def norm_back(values, gain, grad):
    inv_root = lax.rsqrt(jnp.mean(values * values, axis=-1, keepdims=True) + epsilon)
    normed = values * inv_root
    upstream = grad * gain
    grad_values = inv_root * (
        upstream - normed * jnp.mean(upstream * normed, axis=-1, keepdims=True)
    )
    return (grad_values, normed)


def segment_of(places, ends):
    return jnp.sum((ends[None, :] <= places[:, None]).astype(jnp.int32), axis=1)


def pair_step(early, later):
    return (early[0] * later[0], later[0] * early[1] + later[1])


def plain_dot(left, right):
    return jnp.dot(left, right, preferred_element_type=jnp.float32)


def times_trans(left, right):
    return lax.dot_general(
        left, right, (((1,), (1,)), ((), ())), preferred_element_type=jnp.float32
    )


def trans_times(left, right):
    return lax.dot_general(
        left, right, (((0,), (0,)), ((), ())), preferred_element_type=jnp.float32
    )


def gelu_tanh(values):
    return jax.nn.gelu(values, approximate=True)


def collect(
    norm_gain,
    mlp_gain,
    x_weight,
    y_weight,
    recur_gate_weight,
    input_gate_weight,
    gate_weight,
    up_weight,
    out_weight,
    down_weight,
):
    return (
        lax.all_gather(norm_gain, "dp", axis=0, tiled=True),
        lax.all_gather(mlp_gain, "dp", axis=0, tiled=True),
        lax.all_gather(x_weight, "dp", axis=0, tiled=True),
        lax.all_gather(y_weight, "dp", axis=0, tiled=True),
        lax.all_gather(recur_gate_weight, "dp", axis=0, tiled=True),
        lax.all_gather(input_gate_weight, "dp", axis=0, tiled=True),
        lax.all_gather(gate_weight, "dp", axis=0, tiled=True),
        lax.all_gather(up_weight, "dp", axis=0, tiled=True),
        lax.all_gather(out_weight, "dp", axis=1, tiled=True),
        lax.all_gather(down_weight, "dp", axis=1, tiled=True),
    )


def row_sums(term_rows, tok_rows):
    return lax.psum_scatter(
        term_rows(jnp.int32(0), lax.axis_size("tensor") * tok_rows).astype(jnp.bfloat16),
        "tensor",
        scatter_dimension=0,
        tiled=True,
    ).astype(jnp.float32)


def spread_rows(values):
    return lax.all_gather(values, "tensor", axis=0, tiled=True)


def local_general(
    tokens,
    norm_gain,
    x_weight,
    y_weight,
    conv_weight,
    recur_gate_weight,
    input_gate_weight,
    decay_param,
    out_weight,
    mlp_gain,
    gate_weight,
    up_weight,
    down_weight,
    seq_lengths,
    token_order,
    cotangent,
):
    n_tensor = lax.axis_size("tensor")
    tensor_index = lax.axis_index("tensor")
    dp_index = lax.axis_index("dp")
    tok_rows = tokens.shape[0]
    row_count = tok_rows * n_tensor
    own_width = conv_weight.shape[1]
    kernel_taps = conv_weight.shape[0]
    edge_rows = kernel_taps - 1
    dp_width = norm_gain.shape[0]
    own_start = tensor_index * tok_rows
    shards = (
        norm_gain,
        mlp_gain,
        x_weight,
        y_weight,
        recur_gate_weight,
        input_gate_weight,
        gate_weight,
        up_weight,
        out_weight,
        down_weight,
    )
    (
        gain_one,
        gain_two,
        x_full,
        y_full,
        recur_full,
        input_full,
        gate_full,
        up_full,
        out_full,
        down_full,
    ) = collect(*shards)
    block_size = recur_full.shape[0]
    first_gain = gain_one.astype(jnp.float32)
    second_gain = gain_two.astype(jnp.float32)
    both_gates = jnp.concatenate([recur_full, input_full], axis=1)
    tok_own = tokens.astype(jnp.float32)
    own_order = token_order - dp_index * row_count
    first_rows = rms_scale(tok_own, first_gain).astype(jnp.bfloat16)
    first_all, cot_all, order_all = (
        lax.all_gather(first_rows, "tensor", axis=0, tiled=True),
        lax.all_gather(cotangent, "tensor", axis=0, tiled=True),
        lax.all_gather(own_order, "tensor", axis=0, tiled=True),
    )
    row_index = jnp.arange(row_count, dtype=jnp.int32)
    inverse = jnp.zeros((row_count,), jnp.int32).at[order_all].set(row_index)
    hidden_place = jnp.take(first_all, inverse, axis=0)
    places = dp_index * row_count + row_index
    ends = jnp.cumsum(seq_lengths)
    segment = segment_of(places, ends)
    starts = (places == 0) | (segment != segment_of(places - 1, ends))
    live = (places < ends[-1]).astype(jnp.float32)
    live_stored = jnp.take(live, order_all, axis=0)
    same = [
        (segment_of(places - shift, ends) == segment).astype(jnp.float32)
        for shift in range(kernel_taps)
    ]
    low_edge = tensor_index * own_width
    own_blocks = (low_edge + jnp.arange(own_width, dtype=jnp.int32)) // block_size
    first_block = low_edge // block_size
    block_count = own_width // block_size + 2

    def block_start(index):
        return (first_block + index) * block_size - low_edge + block_size

    def block_mask(index):
        inside = own_blocks == first_block + index
        return jnp.concatenate([inside, inside])

    def convolve(extended, kernel):
        return sum(
            (
                kernel[shift][None, :]
                * extended[edge_rows - shift : edge_rows - shift + row_count]
                * same[shift][:, None]
                for shift in range(kernel_taps)
            )
        )

    def gates(conv_vals, pre_recur, pre_input, decay_vals):
        log_rate = -rate_scale * jax.nn.sigmoid(pre_recur) * jax.nn.softplus(-decay_vals)
        decay_rate = jnp.where(starts[:, None], 0.0, jnp.exp(log_rate))
        scale_in = jnp.where(starts[:, None], 1.0, jnp.sqrt(-jnp.expm1(2.0 * log_rate)))
        return (decay_rate, conv_vals * jax.nn.sigmoid(pre_input) * scale_in)

    def glu(gate_pre, up_pre):
        return gelu_tanh(gate_pre) * up_pre

    x_branch = plain_dot(hidden_place, x_full).astype(jnp.bfloat16)
    y_before = plain_dot(hidden_place, y_full)
    previous = from_behind(x_branch[row_count - edge_rows :], "dp", 1)
    extended = jnp.concatenate([previous, x_branch], axis=0).astype(jnp.float32)
    conv_out = convolve(extended, conv_weight)
    conv_wide = extended_2(conv_out.astype(jnp.bfloat16), (("tensor", 1),), block_size)
    pre_both = jnp.zeros((row_count, 2 * own_width), jnp.float32)
    for index in range(block_count):
        piece = lax.dynamic_slice_in_dim(conv_wide, block_start(index), block_size, 1)
        pre_both = pre_both + jnp.where(
            block_mask(index)[None, :], plain_dot(piece, both_gates), 0.0
        )
    (decay_rate, driven), gate_pull = jax.vjp(
        gates, conv_out, pre_both[:, :own_width], pre_both[:, own_width:], decay_param
    )
    cum_rate, local_state = lax.associative_scan(pair_step, (decay_rate, driven), axis=0)
    ident = (jnp.ones((own_width,), jnp.float32), jnp.zeros((own_width,), jnp.float32))
    rate_in, state_in = entering((cum_rate[-1], local_state[-1]), "dp", pair_step, ident, False)
    state = local_state + cum_rate * state_in[None, :]
    y_branch = gelu_tanh(y_before)
    merged = (state * y_branch).astype(jnp.bfloat16)
    merged_stored = jnp.take(merged, order_all, axis=0)

    def mixer_rows(begin, number):
        return plain_dot(merged_stored, out_full)

    after_own = tok_own + row_sums(mixer_rows, tok_rows)
    hidden_two = spread_rows(rms_scale(after_own, second_gain).astype(jnp.bfloat16))
    gate_pre = plain_dot(hidden_two, gate_full)
    up_pre = plain_dot(hidden_two, up_full)
    glu_out, glu_pull = jax.vjp(glu, gate_pre, up_pre)
    product = glu_out.astype(jnp.bfloat16)

    def down_rows(begin, number):
        return plain_dot(product, down_full)

    feed_out = row_sums(down_rows, tok_rows)
    live_own = lax.dynamic_slice_in_dim(live_stored, own_start, tok_rows, 0)
    output = ((after_own + feed_out) * live_own[:, None]).astype(jnp.bfloat16)
    grad_out = cot_all.astype(jnp.float32) * live_stored[:, None]
    fresh = lax.optimization_barrier((shards, grad_out))[0]
    (
        gain_one,
        gain_two,
        x_full,
        y_full,
        recur_full,
        input_full,
        gate_full,
        up_full,
        out_full,
        down_full,
    ) = collect(*fresh)
    first_gain = gain_one.astype(jnp.float32)
    second_gain = gain_two.astype(jnp.float32)
    both_gates = jnp.concatenate([recur_full, input_full], axis=1)
    down_in = grad_out.astype(jnp.bfloat16)
    grad_down = trans_times(product, down_in)
    grad_product = times_trans(down_in, down_full)
    grad_gate_pre, grad_up_pre = glu_pull(grad_product)
    grad_gate_pre = grad_gate_pre.astype(jnp.bfloat16)
    grad_up_pre = grad_up_pre.astype(jnp.bfloat16)
    grad_gate = trans_times(hidden_two, grad_gate_pre)
    grad_up = trans_times(hidden_two, grad_up_pre)

    def feed_rows(begin, number):
        return times_trans(grad_gate_pre, gate_full) + times_trans(grad_up_pre, up_full)

    grad_out_own = lax.dynamic_slice_in_dim(grad_out, own_start, tok_rows, 0)
    grad_two_own = row_sums(feed_rows, tok_rows)
    grad_norm_own, normed_two = norm_back(after_own, second_gain, grad_two_own)
    second_part = jnp.sum(grad_two_own * normed_two, axis=0)
    grad_after_own = grad_out_own + grad_norm_own
    mixer_in = spread_rows(grad_after_own.astype(jnp.bfloat16))
    grad_out_mat = trans_times(merged_stored, mixer_in)
    grad_merged = jnp.take(times_trans(mixer_in, out_full), inverse, axis=0)
    grad_state = grad_merged * y_branch
    gelu_pull = jax.vjp(gelu_tanh, y_before)[1]
    grad_y_before = gelu_pull(grad_merged * state)[0].astype(jnp.bfloat16)
    rate_next = jnp.concatenate([decay_rate[1:], jnp.ones((1, own_width), jnp.float32)], axis=0)
    rev_rate, local_lam = lax.associative_scan(
        pair_step, (rate_next, grad_state), reverse=True, axis=0
    )
    head_rate = decay_rate[0] * rev_rate[0]
    head_lam = decay_rate[0] * local_lam[0]
    factor_in, lam_in = entering((head_rate, head_lam), "dp", pair_step, ident, True)
    lam = local_lam + rev_rate * lam_in[None, :]
    state_prev = jnp.concatenate([state_in[None, :], state[:-1]], axis=0)
    grad_conv_local, grad_pre_recur, grad_pre_input, grad_decay_own = gate_pull(
        (lam * state_prev, lam)
    )
    grad_pre = jnp.concatenate([grad_pre_recur, grad_pre_input], axis=1).astype(jnp.bfloat16)
    grad_both = jnp.zeros((block_size, 2 * own_width), jnp.float32)
    grad_wide = jnp.zeros((row_count, own_width + 2 * block_size), jnp.float32)
    for index in range(block_count):
        begin = block_start(index)
        piece = lax.dynamic_slice_in_dim(conv_wide, begin, block_size, 1)
        masked = jnp.where(block_mask(index)[None, :], grad_pre, jnp.zeros((), jnp.bfloat16))
        grad_both = grad_both + trans_times(piece, masked)
        added = lax.dynamic_slice_in_dim(grad_wide, begin, block_size, 1) + times_trans(
            masked, both_gates
        )
        grad_wide = lax.dynamic_update_slice_in_dim(grad_wide, added, begin, 1)
    grad_recur = grad_both[:, :own_width]
    grad_input = grad_both[:, own_width:]
    rims = jnp.concatenate(
        [grad_wide[:, :block_size], grad_wide[:, own_width + block_size :]], axis=1
    )
    arrived = extended_2(rims.astype(jnp.bfloat16), (("tensor", 1),), block_size).astype(rims.dtype)
    from_lower = jnp.pad(arrived[:, :block_size], ((0, 0), (0, own_width - block_size)))
    from_upper = jnp.pad(arrived[:, 3 * block_size :], ((0, 0), (own_width - block_size, 0)))
    grad_conv = (
        grad_conv_local
        + grad_wide[:, block_size : block_size + own_width]
        + from_lower
        + from_upper
    )
    conv_pull = jax.vjp(convolve, extended, conv_weight)[1]
    grad_extended, grad_kernel = conv_pull(grad_conv)
    returned = from_behind(grad_extended[:edge_rows], "dp", -1)
    grad_x_branch = grad_extended[edge_rows:] + jnp.concatenate(
        [jnp.zeros((row_count - edge_rows, own_width), jnp.float32), returned], axis=0
    )
    grad_x_low = grad_x_branch.astype(jnp.bfloat16)
    grad_x_stored = jnp.take(grad_x_low, order_all, axis=0)
    grad_y_stored = jnp.take(grad_y_before, order_all, axis=0)
    grad_x_mat = trans_times(first_all, grad_x_stored)
    grad_y_mat = trans_times(first_all, grad_y_stored)

    def mixer_back_rows(begin, number):
        return times_trans(grad_x_stored, x_full) + times_trans(grad_y_stored, y_full)

    grad_one_own = row_sums(mixer_back_rows, tok_rows)
    grad_norm_one, normed_one = norm_back(tok_own, first_gain, grad_one_own)
    first_part = jnp.sum(grad_one_own * normed_one, axis=0)
    grad_tokens = grad_after_own + grad_norm_one
    chosen = jnp.arange(n_tensor, dtype=jnp.int32) == tensor_index
    kernel_tile = jnp.where(chosen[:, None, None], grad_kernel[None, :, :], 0.0)
    decay_tile = jnp.where(chosen[:, None], grad_decay_own[None, :], 0.0)
    small = lax.psum((first_part, second_part, kernel_tile, decay_tile), ("dp", "tensor"))
    grad_first_gain = lax.dynamic_slice_in_dim(small[0], dp_index * dp_width, dp_width, 0)
    grad_second_gain = lax.dynamic_slice_in_dim(small[1], dp_index * dp_width, dp_width, 0)
    grad_kernel_sum = lax.dynamic_index_in_dim(small[2], tensor_index, 0, keepdims=False)
    grad_decay = lax.dynamic_index_in_dim(small[3], tensor_index, 0, keepdims=False)
    sums = (
        lax.psum_scatter(
            grad_x_mat.astype(jnp.bfloat16), "dp", scatter_dimension=0, tiled=True
        ).astype(jnp.float32),
        lax.psum_scatter(
            grad_y_mat.astype(jnp.bfloat16), "dp", scatter_dimension=0, tiled=True
        ).astype(jnp.float32),
        lax.psum_scatter(
            grad_recur.astype(jnp.bfloat16), "dp", scatter_dimension=0, tiled=True
        ).astype(jnp.float32),
        lax.psum_scatter(
            grad_input.astype(jnp.bfloat16), "dp", scatter_dimension=0, tiled=True
        ).astype(jnp.float32),
        lax.psum_scatter(
            grad_gate.astype(jnp.bfloat16), "dp", scatter_dimension=0, tiled=True
        ).astype(jnp.float32),
        lax.psum_scatter(
            grad_up.astype(jnp.bfloat16), "dp", scatter_dimension=0, tiled=True
        ).astype(jnp.float32),
        lax.psum_scatter(
            grad_out_mat.astype(jnp.bfloat16), "dp", scatter_dimension=1, tiled=True
        ).astype(jnp.float32),
        lax.psum_scatter(
            grad_down.astype(jnp.bfloat16), "dp", scatter_dimension=1, tiled=True
        ).astype(jnp.float32),
    )
    return (
        output,
        grad_tokens,
        grad_first_gain,
        sums[0],
        sums[1],
        grad_kernel_sum,
        sums[2],
        sums[3],
        grad_decay,
        sums[6],
        grad_second_gain,
        sums[4],
        sums[5],
        sums[7],
    )


MESH = pl.DeviceIdType.MESH
VMEM_BYTES = 60 * 2**20


def remote(src, dst, send, recv, device):
    return pltpu.make_async_remote_copy(
        src_ref=src,
        dst_ref=dst,
        send_sem=send,
        recv_sem=recv,
        device_id=device,
        device_id_type=MESH,
    )


class Place:
    def __init__(self, n_dp, n_line):
        self.n_dp, self.n_line = n_dp, n_line
        self.d, self.t = lax.axis_index("dp"), lax.axis_index("tensor")
        self.core = lax.rem(self.d, 2)
        self.x = lax.rem(lax.div(self.d, 2), 2)
        self.y = lax.div(self.d, 4)

    def chip(self, flip_x, flip_y, flip_core=0):
        x = 1 - self.x if flip_x else self.x
        y = 1 - self.y if flip_y else self.y
        core = 1 - self.core if flip_core else self.core
        return y * 4 + x * 2 + core

    def at(self, flip_x=0, flip_y=0, flip_core=0):
        return (self.chip(flip_x, flip_y, flip_core), self.t)

    def up(self):
        return (self.d, lax.rem(self.t + 1, self.n_line))

    def down(self):
        return (self.d, lax.rem(self.t + self.n_line - 1, self.n_line))

    def meet(self, everyone=False):
        barrier = pltpu.get_barrier_semaphore()

        def greet(device):
            pl.semaphore_signal(barrier, inc=1, device_id=device, device_id_type=MESH)

        if everyone:
            for i in range(1, self.n_dp):
                greet((lax.rem(self.d + i, self.n_dp), self.t))
            for i in range(1, self.n_line):
                greet((self.d, lax.rem(self.t + i, self.n_line)))
            pl.semaphore_wait(barrier, self.n_dp + self.n_line - 2)
            return
        for flips in ((1, 0), (0, 1), (0, 0, 1)):
            greet(self.at(*flips))
        below, above = self.t > 0, self.t < self.n_line - 1

        @pl.when(below)
        def _():
            greet(self.down())

        @pl.when(above)
        def _():
            greet(self.up())

        pl.semaphore_wait(barrier, 3 + below.astype(jnp.int32) + above.astype(jnp.int32))


class Fetch:
    def __init__(self, pairs, sems):
        self.copies = [
            pltpu.make_async_copy(src, dst, sems.at[i]) for i, (src, dst) in enumerate(pairs)
        ]

    def start(self, *which):
        for i in which:
            self.copies[i].start()

    def wait(self, *which):
        for i in which:
            self.copies[i].wait()


def vmem_like(array):
    return pltpu.VMEM(array.shape, array.dtype)


class Kept:
    def __init__(self, src, dst, held, sems):
        self.there = pltpu.make_async_copy(src, held, sems.at[0])
        self.back = pltpu.make_async_copy(held, dst, sems.at[1])

    def begin(self):
        self.there.start()

    def turn(self):
        self.there.wait()
        self.back.start()

    def finish(self):
        self.back.wait()


class GatherPlane:
    def __init__(self, place, src, dst, send, recv, local, held):
        self.p, self.src, self.dst = place, src, dst
        self.rows = src.shape[0]
        self.send, self.recv = send, recv
        self.keep = Kept(src, self.block(0, 0), held, local)

    def block(self, fx, fy, fc=0, part=None):
        first = self.p.chip(fx, fy, fc) * self.rows
        size = self.rows
        if part is not None:
            size = self.rows // 2
            first = first + part * size
        return self.dst.at[pl.ds(pl.multiple_of(first, 16), size)]

    def copy(self, i, src, dst, device):
        return remote(src, dst, self.send.at[i], self.recv.at[i], device)

    def outgoing(self, i):
        at, block = self.p.at, self.block
        if i == 0:
            return self.copy(0, self.src, block(0, 0), at(1, 0))
        if i == 1:
            return self.copy(1, self.src, block(0, 0), at(0, 1))
        if i == 2:
            return self.copy(2, self.src, block(0, 0), at(0, 0, 1))
        if i == 3:
            return self.copy(3, block(1, 0, 0, 0), block(1, 0, 0, 0), at(0, 1))
        if i == 4:
            return self.copy(4, block(0, 1, 0, 1), block(0, 1, 0, 1), at(1, 0))
        spot = ((1, 0), (0, 1), (1, 1, 0, 0), (1, 1, 0, 1))[i - 5]
        return self.copy(i, block(*spot), block(*spot), at(0, 0, 1))

    def arrive(self, i):
        spot = (
            (1, 0),
            (0, 1),
            (0, 0, 1),
            (1, 1, 0, 0),
            (1, 1, 0, 1),
            (1, 0, 1),
            (0, 1, 1),
            (1, 1, 1, 0),
            (1, 1, 1, 1),
        )[i]
        here = self.block(*spot)
        self.copy(i, here, here, self.p.at(0, 0, 1)).wait_recv()

    def begin(self):
        for i in (0, 1, 2):
            self.outgoing(i).start()
        self.keep.begin()

    def forward(self):
        self.keep.turn()
        self.arrive(0)
        self.outgoing(3).start()
        self.arrive(1)
        self.outgoing(4).start()
        self.outgoing(5).start()
        self.outgoing(6).start()

    def share(self):
        self.arrive(3)
        self.outgoing(7).start()
        self.arrive(4)
        self.outgoing(8).start()

    def finish(self):
        for i in (2, 5, 6, 7, 8):
            self.arrive(i)
        for i in range(9):
            self.outgoing(i).wait_send()
        self.keep.finish()


class GatherLine:
    def __init__(self, place, dst, rows, begin, span, send, recv):
        self.p, self.dst, self.rows = place, dst, rows
        self.begin, self.span = begin, span
        self.send, self.recv = send, recv
        self.last = place.n_line - 1

    def block(self, owner):
        first = owner * self.rows + self.begin
        return self.dst.at[pl.ds(pl.multiple_of(first, 8), self.span)]

    def copy(self, way, k, owner, source=None):
        to = self.p.up() if way == 0 else self.p.down()
        block = self.block(owner)
        return remote(
            block if source is None else source,
            block,
            self.send.at[way, k],
            self.recv.at[way, k],
            to,
        )

    def step(self, k, source=None):
        t, last = self.p.t, self.last
        if k > 0:
            self.arrive(k - 1)

        @pl.when((t < last) & (t >= k))
        def _():
            self.copy(0, k, t - k, source).start()

        @pl.when((t > 0) & (t + k <= last))
        def _():
            self.copy(1, k, t + k, source).start()

    def arrive(self, k):
        t, last = self.p.t, self.last

        @pl.when(t >= k + 1)
        def _():
            self.copy(0, k, t - 1 - k).wait_recv()

        @pl.when(t + k + 1 <= last)
        def _():
            self.copy(1, k, t + 1 + k).wait_recv()

    def finish(self):
        t, last = self.p.t, self.last
        self.arrive(last - 1)
        for k in range(last):

            @pl.when((t < last) & (t >= k))
            def _():
                self.copy(0, k, t - k).wait_send()

            @pl.when((t > 0) & (t + k <= last))
            def _():
                self.copy(1, k, t + k).wait_send()


class ReduceLine:
    def __init__(self, place, terms, rows, begin, span, inbox, send, recv):
        self.p, self.terms, self.rows = place, terms, rows
        self.begin, self.span = begin, span
        self.inbox = inbox
        self.send, self.recv = send, recv
        self.last = place.n_line - 1

    def own(self, owner):
        first = owner * self.rows + self.begin
        return self.terms.at[pl.ds(pl.multiple_of(first, 16), self.span)]

    def copy(self, way, j, source):
        to = self.p.up() if way == 0 else self.p.down()
        return remote(
            source, self.inbox.at[way, j], self.send.at[way, j], self.recv.at[way, j], to
        )

    def ends(self):
        t, last = self.p.t, self.last

        @pl.when(t == 0)
        def _():
            for j in range(last):
                self.copy(0, j, self.own(last - j)).start()

        @pl.when(t == last)
        def _():
            for j in range(last):
                self.copy(1, j, self.own(j)).start()

    def sent(self):
        t, last = self.p.t, self.last

        @pl.when(t == 0)
        def _():
            for j in range(last):
                self.copy(0, j, self.own(last - j)).wait_send()

        @pl.when(t == last)
        def _():
            for j in range(last):
                self.copy(1, j, self.own(j)).wait_send()

    def hand_on(self, way, j):
        term = self.own(self.last - j if way == 0 else j)
        self.copy(way, j, term).wait_recv()
        self.inbox[way, j] = term[...] + self.inbox[way, j]
        self.copy(way, j, self.inbox.at[way, j]).start()

    def hop(self, k):
        t, last = self.p.t, self.last

        @pl.when(t == k + 1)
        def _():
            for j in range(last - 1 - k):
                self.hand_on(0, j)

        @pl.when(t == last - 1 - k)
        def _():
            for j in range(last - 1 - k):
                self.hand_on(1, j)

    def total(self, result):
        t, last = self.p.t, self.last
        result[...] = self.own(t)[...].astype(jnp.float32)

        @pl.when(t > 0)
        def _():
            j = last - t
            self.copy(0, j, self.inbox.at[0, 0]).wait_recv()
            result[...] += self.inbox[0, j].astype(jnp.float32)

        @pl.when(t < last)
        def _():
            self.copy(1, t, self.inbox.at[0, 0]).wait_recv()
            result[...] += self.inbox[1, t].astype(jnp.float32)

    def finish(self):
        t, last = self.p.t, self.last
        for j in range(last - 1):

            @pl.when((t > 0) & (t < last - j))
            def _():
                self.copy(0, j, self.inbox.at[0, j]).wait_send()

            @pl.when((t < last) & (t > j))
            def _():
                self.copy(1, j, self.inbox.at[1, j]).wait_send()


def add_rows(into, other, result=None):
    result = into if result is None else result

    def tile(i, carry):
        rows = pl.ds(pl.multiple_of(i * 16, 16), 16)
        result[rows] = into[rows] + other[rows]
        return carry

    lax.fori_loop(0, into.shape[0] // 16, tile, None)


class ReducePlane:
    chips = ((0, 0), (1, 0), (0, 1), (1, 1))

    def __init__(self, place, terms, scratch):
        self.p, self.terms = place, terms
        self.held, self.near, self.along, self.last, self.send, self.recv, self.local = scratch
        self.rows = self.held.shape[1]
        self.half = self.rows // 2

    @staticmethod
    def scratch(rows, width):
        return [
            pltpu.VMEM((4, rows, width), jnp.bfloat16),
            pltpu.VMEM((4, rows, width), jnp.bfloat16),
            pltpu.VMEM((4, rows // 2, width), jnp.bfloat16),
            pltpu.VMEM((2, rows // 2, width), jnp.bfloat16),
            pltpu.SemaphoreType.DMA((10,)),
            pltpu.SemaphoreType.DMA((10,)),
            pltpu.SemaphoreType.DMA((4,)),
        ]

    def block(self, k, other):
        first = self.p.chip(*self.chips[k], other) * self.rows
        return self.terms.at[pl.ds(pl.multiple_of(first, 16), self.rows)]

    def half_of(self, k, part):
        return self.held.at[k, pl.ds(part * self.half, self.half)]

    def load(self, k):
        return pltpu.make_async_copy(self.block(k, 0), self.held.at[k], self.local.at[k])

    def copy(self, i):
        at = self.p.at
        if i < 4:
            src, dst, to = self.block(i, 1), self.near.at[i], at(0, 0, 1)
        elif i < 8:
            src, to = (
                (self.half_of(1, 0), at(1, 0)),
                (self.half_of(3, 0), at(1, 0)),
                (self.half_of(2, 1), at(0, 1)),
                (self.half_of(3, 1), at(0, 1)),
            )[i - 4]
            dst = self.along.at[i - 4]
        else:
            src, to = ((self.half_of(2, 0), at(0, 1)), (self.half_of(1, 1), at(1, 0)))[i - 8]
            dst = self.last.at[i - 8]
        return remote(src, dst, self.send.at[i], self.recv.at[i], to)

    def begin(self, which=(3, 1, 2, 0)):
        for k in which:
            self.copy(k).start()
            self.load(k).start()

    def cores(self, which=(3, 1, 2, 0)):
        for k in which:
            self.load(k).wait()
            self.copy(k).wait_recv()
            add_rows(self.held.at[k], self.near.at[k])
            if k == 3:
                self.copy(5).start()
                self.copy(7).start()
            elif k == 1:
                self.copy(4).start()
            elif k == 2:
                self.copy(6).start()

    def turn(self):
        self.copy(5).wait_recv()
        add_rows(self.half_of(2, 0), self.along.at[1])
        self.copy(8).start()
        self.copy(7).wait_recv()
        add_rows(self.half_of(1, 1), self.along.at[3])
        self.copy(9).start()
        self.copy(4).wait_recv()
        add_rows(self.half_of(0, 0), self.along.at[0])
        self.copy(6).wait_recv()
        add_rows(self.half_of(0, 1), self.along.at[2])

    def finish(self, result):
        for part in (0, 1):
            self.copy(8 + part).wait_recv()
            rows = pl.ds(part * self.half, self.half)
            add_rows(self.half_of(0, part), self.last.at[part], result.at[rows])
        for i in range(10):
            self.copy(i).wait_send()


def dma_sems(*dims):
    return pltpu.SemaphoreType.DMA(dims)


def in_vmem():
    return pl.BlockSpec(memory_space=pltpu.VMEM)


def in_any():
    return pl.BlockSpec(memory_space=pl.ANY)


def comm_params(number):
    return pltpu.CompilerParams(
        collective_id=number, has_side_effects=True, vmem_limit_bytes=VMEM_BYTES
    )


def shaped(dims, kind):
    return jax.ShapeDtypeStruct(dims, kind)


def first_gather(n_dp, n_line, mats, rows_in, order):
    count = len(mats)
    parts = 2

    def kernel(*refs):
        srcs, (c, e) = refs[:count], refs[count : count + 2]
        dsts, (c_out, e_out) = refs[count + 2 : 2 * count + 2], refs[2 * count + 2 : 2 * count + 4]
        ps, pr, pl_sem, ls, lr, ll = refs[2 * count + 4 : 2 * count + 10]
        held = refs[2 * count + 10 :]
        place = Place(n_dp, n_line)
        place.meet()
        planes = [
            GatherPlane(place, a, b, ps.at[i], pr.at[i], pl_sem.at[i], held[i])
            for i, (a, b) in enumerate(zip(srcs, dsts))
        ]
        rows = c.shape[0]
        span = rows // parts
        lines = [
            GatherLine(place, c_out, rows, i * span, span, ls.at[i], lr.at[i])
            for i in range(parts)
        ]
        lines.append(
            GatherLine(place, e_out, e.shape[0], 0, e.shape[0], ls.at[parts], lr.at[parts])
        )
        for i in range(parts):
            lines[i].step(0, c.at[pl.ds(i * span, span)])
        lines[parts].step(0, e)
        early, late = planes[: count // 2], planes[count // 2 :]
        for part in early:
            part.begin()
        copies = []
        for i, (src, dst) in enumerate(((c, c_out), (e, e_out))):
            own = dst.at[pl.ds(pl.multiple_of(place.t * src.shape[0], 8), src.shape[0])]
            copies.append(Kept(src, own, held[count + i], ll.at[i]))
            copies[i].begin()
        for line in lines:
            line.step(1)
        for part in late:
            part.begin()
        for part in early:
            part.forward()
        for copy in copies:
            copy.turn()
        for line in lines:
            line.step(2)
        for part in early:
            part.share()
        for part in late:
            part.forward()
        for part in late:
            part.share()
        for part in lines + planes:
            part.finish()
        for copy in copies:
            copy.finish()

    return pl.pallas_call(
        kernel,
        out_shape=tuple(shaped((n_dp * m.shape[0], m.shape[1]), m.dtype) for m in mats)
        + (
            shaped((n_line * rows_in.shape[0], rows_in.shape[1]), rows_in.dtype),
            shaped((n_line * order.shape[0], order.shape[1]), order.dtype),
        ),
        in_specs=[in_any()] * (count + 2),
        out_specs=[in_any()] * (count + 2),
        scratch_shapes=[
            dma_sems(count, 9),
            dma_sems(count, 9),
            dma_sems(count, 2),
            dma_sems(parts + 1, 2, n_line - 1),
            dma_sems(parts + 1, 2, n_line - 1),
            dma_sems(2, 2),
        ]
        + [vmem_like(m) for m in (*mats, rows_in, order)],
        compiler_params=comm_params(1),
        name="first_gather",
    )(*mats, rows_in, order)


CHUNKS = 8
LAST_CHUNKS = 8


def line_scratch(n_line, span, width, chunks):
    hops = n_line - 1
    return [
        pltpu.VMEM((chunks, 2, hops, span, width), jnp.bfloat16),
        dma_sems(chunks, 2, hops),
        dma_sems(chunks, 2, hops),
        dma_sems(chunks, 2, hops),
        dma_sems(chunks, 2, hops),
        pltpu.VMEM((span, width), jnp.float32),
    ]


def sum_rows_and_spread(place, terms, scratch, finish_rows, spread, between):
    inbox, rs, rr, gs, gr, total = scratch
    span = total.shape[0]
    count = inbox.shape[0]
    rows = span * count
    hops = place.n_line - 1
    sums = [
        ReduceLine(place, terms, rows, c * span, span, inbox.at[c], rs.at[c], rr.at[c])
        for c in range(count)
    ]
    gathers = []
    if spread is not None:
        gathers = [
            GatherLine(place, spread, rows, c * span, span, gs.at[c], gr.at[c])
            for c in range(count)
        ]
    sums[0].ends()

    def total_of(c):
        sums[c].total(total)
        finish_rows(c, pl.ds(c * span, span), total)
        if gathers:
            gathers[c].step(0)

    stages = [lambda c, k=k: sums[c].hop(k) for k in range(hops - 1)] + [total_of]
    lags = [LAGS[min(k, len(LAGS) - 1)] for k in range(hops)]
    if gathers:
        stages += [lambda c, k=k: gathers[c].step(k) for k in range(1, hops)]
        lags += [lags[-1] + LAG_STEP * k for k in range(1, hops)]
    for i in range(count + lags[-1]):
        if i < count:
            sums[i].sent()
        if i + 1 < count:
            sums[i + 1].ends()
        for work, lag in zip(stages, lags):
            if 0 <= i - lag < count:
                work(i - lag)
        if i in between:
            between[i]()
    for part in gathers + sums:
        part.finish()


LAGS = (0, 1, 1)
LAG_STEP = 1


def middle_gather(n_dp, n_line, terms, tokens, gain, mats):
    rows, width = tokens.shape
    count = len(mats)

    def kernel(*refs):
        s, tok, gain_ref = refs[:3]
        srcs = refs[3 : 3 + count]
        after, hidden = refs[3 + count : 5 + count]
        dsts = refs[5 + count : 5 + 2 * count]
        ps, pr, pl_sem = refs[5 + 2 * count : 8 + 2 * count]
        held = refs[8 + 2 * count : 8 + 3 * count]
        scratch = refs[8 + 3 * count :]
        place = Place(n_dp, n_line)
        place.meet()
        planes = [
            GatherPlane(place, a, b, ps.at[i], pr.at[i], pl_sem.at[i], held[i])
            for i, (a, b) in enumerate(zip(srcs, dsts))
        ]
        planes[0].begin()

        def norm(c, here, total):
            values = tok[here].astype(jnp.float32) + total[...]
            after[here] = values
            low = rms_scale(values, gain_ref[...]).astype(jnp.bfloat16)
            first = pl.multiple_of(place.t * rows, 16) + c * total.shape[0]
            hidden[pl.ds(pl.multiple_of(first, 16), total.shape[0])] = low

        between = {6: planes[0].forward, 9: planes[0].share}
        sum_rows_and_spread(place, s, scratch, norm, hidden, between)
        for part in planes:
            part.finish()

    return pl.pallas_call(
        kernel,
        out_shape=(
            shaped((rows, width), jnp.float32),
            shaped((n_line * rows, width), jnp.bfloat16),
        )
        + tuple(shaped((n_dp * m.shape[0], m.shape[1]), m.dtype) for m in mats),
        in_specs=[in_vmem()] * 3 + [in_any()] * count,
        out_specs=[in_vmem()] * 2 + [in_any()] * count,
        scratch_shapes=[dma_sems(count, 9), dma_sems(count, 9), dma_sems(count, 2)]
        + [vmem_like(m) for m in mats]
        + line_scratch(n_line, rows // CHUNKS, width, CHUNKS),
        compiler_params=comm_params(2),
        name="middle_gather",
    )(terms, tokens, gain, *mats)


def middle_sums(n_dp, n_line, terms, after, gain, grad_in, mat, hidden, grad_up, product, down):
    rows, width = after.shape
    block = mat.shape[0] // n_dp
    wide = grad_up.shape[1]
    spread_rows = n_line * rows

    def kernel(*refs):
        s, after_ref, gain_ref, g_ref, src = refs[:5]
        hid_far, gu_far, pr_far, dw_far = refs[5:9]
        grad_after, gain_sum, spread, result, up_far, feed_far = refs[9:15]
        hid, gu, pr, dw, up_out, feed, sems = refs[15:22]
        rest = refs[22:]
        fetch = Fetch(
            [
                (hid_far, hid),
                (gu_far, gu),
                (pr_far, pr),
                (dw_far, dw),
                (feed, feed_far),
                (up_out.at[0], up_far.at[pl.ds(0, width // 2)]),
                (up_out.at[1], up_far.at[pl.ds(width // 2, width // 2)]),
            ],
            sems,
        )
        fetch.start(0, 1, 2, 3)
        place = Place(n_dp, n_line)
        place.meet()
        plane = ReducePlane(place, src, rest[:7])
        scratch = rest[7:]
        plane.begin()
        gain_sum[...] = jnp.zeros_like(gain_sum)

        def norm(c, here, total):
            grad = total[...]
            grad_rows, normed = norm_back(after_ref[here], gain_ref[...], grad)
            gain_sum[...] += jnp.sum(grad * normed, axis=0, keepdims=True)
            both = g_ref[here].astype(jnp.float32) + grad_rows
            grad_after[here] = both
            first = pl.multiple_of(place.t * rows, 16) + c * total.shape[0]
            spread[pl.ds(pl.multiple_of(first, 16), total.shape[0])] = both.astype(jnp.bfloat16)

        def feed_part(i):
            cols = pl.ds(i * (width // 4), width // 4)
            feed[:, cols] = times_trans(pr[...], dw[cols]).astype(jnp.bfloat16)

        def up_part(i):
            cols = pl.ds(i * (width // 4), width // 4)
            here = pl.ds((i % 2) * (width // 4), width // 4)
            up_out[i // 2, here] = trans_times(hid[:, cols], gu[...]).astype(jnp.bfloat16)

        def early():
            plane.cores()
            fetch.wait(0, 1)

        def two():
            up_part(0)

        def three():
            up_part(1)
            fetch.start(5)

        def four():
            up_part(2)

        def five():
            up_part(3)
            fetch.start(6)
            fetch.wait(2, 3)

        def six():
            feed_part(0)

        def seven():
            plane.turn()
            feed_part(1)

        def eight():
            feed_part(2)

        def nine():
            feed_part(3)
            fetch.start(4)

        steps = {1: early, 2: two, 3: three, 4: four, 5: five, 6: six, 7: seven, 8: eight, 9: nine}
        sum_rows_and_spread(place, s, scratch, norm, spread, steps)
        plane.finish(result)
        fetch.wait(4, 5, 6)

    low, full = jnp.bfloat16, jnp.float32
    near, far = in_vmem(), in_any()
    return pl.pallas_call(
        kernel,
        out_shape=(
            shaped((rows, width), full),
            shaped((1, width), full),
            shaped((spread_rows, width), low),
            shaped((block, mat.shape[1]), low),
            shaped((width, wide), low),
            shaped((spread_rows, width), low),
        ),
        in_specs=[near] * 4 + [far] * 5,
        out_specs=[near] * 4 + [far] * 2,
        scratch_shapes=[vmem_like(m) for m in (hidden, grad_up, product, down)]
        + [
            pltpu.VMEM((2, width // 2, wide), low),
            pltpu.VMEM((spread_rows, width), low),
            dma_sems(7),
        ]
        + ReducePlane.scratch(block, mat.shape[1])
        + line_scratch(n_line, rows // CHUNKS, width, CHUNKS),
        compiler_params=comm_params(3),
        name="middle_sums",
    )(terms, after, gain, grad_in, mat, hidden, grad_up, product, down)


class Exchange:
    def __init__(self, place, axis, src, slots, send, recv, local):
        self.p, self.src, self.slots = place, src, slots
        self.over_dp = axis == "dp"
        self.size = place.n_dp if self.over_dp else place.n_line
        self.me = place.d if self.over_dp else place.t
        self.send, self.recv, self.local = send, recv, local

    def copy(self, i):
        to = lax.rem(self.me + i, self.size)
        device = (to, self.p.t) if self.over_dp else (self.p.d, to)
        return remote(
            self.src, self.slots.at[self.me], self.send.at[i - 1], self.recv.at[i - 1], device
        )

    def mine(self):
        return pltpu.make_async_copy(self.src, self.slots.at[self.me], self.local)

    def begin(self):
        for i in range(1, self.size):
            self.copy(i).start()
        self.mine().start()

    def wait(self):
        self.mine().wait()
        for i in range(1, self.size):
            self.copy(i).wait()

    def finish(self):
        self.wait()
        total = self.slots[0]
        for i in range(1, self.size):
            total = total + self.slots[i]
        return total


def last_sums(n_dp, n_line, terms, tokens, gain, grad_after, second, small, mats):
    rows, width = tokens.shape
    count = len(mats)
    per = len(ReducePlane.scratch(16, 128))

    def kernel(*refs):
        s, tok, gain_ref, g_ref, second_ref, small_ref = refs[:6]
        srcs = refs[6 : 6 + count]
        grad_tok, small_out, first_out = refs[6 + count : 9 + count]
        results = refs[9 + count : 9 + 2 * count]
        rest = refs[9 + 2 * count :]
        own_first, row_sum = rest[count * per : count * per + 2]
        slots_a, slots_b, slots_c, slots_d = rest[count * per + 2 : count * per + 6]
        xs, xr, xl = rest[count * per + 6 : count * per + 9]
        scratch = rest[count * per + 9 :]
        place = Place(n_dp, n_line)
        place.meet(True)
        planes = [
            ReducePlane(place, srcs[i], rest[i * per : (i + 1) * per]) for i in range(count)
        ]
        for part in planes:
            part.begin()
        early = Exchange(place, "dp", small_ref, slots_a, xs.at[0], xr.at[0], xl.at[0])
        early.begin()
        gain = Exchange(place, "dp", second_ref, slots_d, xs.at[3], xr.at[3], xl.at[3])
        gain.begin()
        own_first[...] = jnp.zeros_like(own_first)

        def norm(c, here, total):
            grad = total[...]
            grad_rows, normed = norm_back(tok[here].astype(jnp.float32), gain_ref[...], grad)
            own_first[...] += jnp.sum(grad * normed, axis=0, keepdims=True)
            grad_tok[here] = g_ref[here] + grad_rows

        def cores():
            for part in planes:
                part.cores()

        def turn():
            for part in planes:
                part.turn()

        sum_rows_and_spread(place, s, scratch, norm, None, {0: cores, 5: turn})
        first = Exchange(place, "dp", own_first, slots_b, xs.at[1], xr.at[1], xl.at[1])
        first.begin()
        small_out[...] = early.finish()
        row_sum[0:1] = gain.finish()
        row_sum[1:2] = first.finish()
        both = Exchange(place, "tensor", row_sum, slots_c, xs.at[2], xr.at[2], xl.at[2])
        both.begin()
        for part, result in zip(planes, results):
            part.finish(result)
        first_out[...] = both.finish()

    return pl.pallas_call(
        kernel,
        out_shape=(
            shaped((rows, width), jnp.float32),
            shaped(small.shape, jnp.float32),
            shaped((2, width), jnp.float32),
        )
        + tuple(shaped((m.shape[0] // n_dp, m.shape[1]), jnp.bfloat16) for m in mats),
        in_specs=[in_vmem()] * 6 + [in_any()] * count,
        out_specs=[in_vmem()] * (3 + count),
        scratch_shapes=sum([ReducePlane.scratch(m.shape[0] // n_dp, m.shape[1]) for m in mats], [])
        + [
            pltpu.VMEM((1, width), jnp.float32),
            pltpu.VMEM((2, width), jnp.float32),
            pltpu.VMEM((n_dp,) + small.shape, jnp.float32),
            pltpu.VMEM((n_dp, 1, width), jnp.float32),
            pltpu.VMEM((n_line, 2, width), jnp.float32),
            pltpu.VMEM((n_dp, 1, width), jnp.float32),
            dma_sems(4, n_dp),
            dma_sems(4, n_dp),
            dma_sems(4),
        ]
        + line_scratch(n_line, rows // LAST_CHUNKS, width, LAST_CHUNKS),
        compiler_params=comm_params(4),
        name="last_sums",
    )(terms, tokens, gain, grad_after, second, small, *mats)


def loop(count, body, unroll=1):
    def step(i, carry):
        body(i)
        return carry

    lax.fori_loop(0, count, step, None, unroll=unroll)


def tile_rows(i, size, ahead=0):
    return pl.ds(pl.multiple_of(i * size + ahead, 8), size)


def moved_up(values, distance, count):
    size = values.shape[0]
    return pltpu.roll(values, (size - distance) % size, 0)[:count]


def take_lanes(ref, here):
    return jnp.concatenate([ref[c, here] for c in range(ref.shape[0])], axis=1)


def put_lanes(ref, here, values):
    for c in range(ref.shape[0]):
        ref[c, here] = values[:, c * LANES : (c + 1) * LANES]


def gelu_parts(values):
    inner = GELU_C * (values + 0.044715 * (values * values * values))
    tanh = jnp.tanh(inner)
    half = 0.5 * (1.0 + tanh)
    slope = half + 0.5 * values * (1.0 - tanh * tanh) * GELU_C * (
        1.0 + 3.0 * 0.044715 * (values * values)
    )
    return values * half, slope


GELU_C = 0.7978845608028654
RIM = 128
LANES = 128
TILE = 16


def one_minus_exp(values, exponential):
    series = jnp.ones_like(values)
    for term in range(9, 1, -1):
        series = 1.0 + values * (1.0 / term) * series
    return jnp.where(values > -0.35, -values * series, 1.0 - exponential)


def rate_and_scale(pre_recur, soft, start):
    sr = jax.nn.sigmoid(pre_recur)
    log_rate = -rate_scale * sr * soft
    decay = jnp.exp(log_rate)
    rate = jnp.where(start, 0.0, decay)
    scale = jnp.where(start, 1.0, jnp.sqrt(one_minus_exp(2.0 * log_rate, decay * decay)))
    return sr, rate, scale


class RimSwap:
    def __init__(self, place, own):
        self.odd = lax.rem(place.t, 2)
        self.partner = (place.d, place.t + 1 - 2 * self.odd)
        self.first = pl.multiple_of(RIM - RIM * self.odd, RIM)
        self.edge = pl.ds(pl.multiple_of((1 - self.odd) * own + self.odd * RIM, RIM), RIM)
        self.over_there = pl.ds(pl.multiple_of(self.odd * (own + RIM), RIM), RIM)
        self.beyond = pl.ds(pl.multiple_of((1 - self.odd) * (own + RIM), RIM), RIM)

    def block(self, index, size):
        return pl.ds(pl.multiple_of(self.first + index * size, RIM), size)


LATE_SHARE = 4


def recur_forward(
    n_dp,
    n_line,
    tok_all,
    cot,
    to_place,
    to_stored,
    x_full,
    y_full,
    out_full,
    gain,
    gates,
    taps,
    soft,
    flags,
):
    rows, width = tok_all.shape
    count, own = taps.shape
    size = gates.shape[0]
    wide = own + 2 * RIM
    blocks = (wide - RIM) // size
    chunk = rows // 8
    cot_rows = cot.shape[0] - cot.shape[0] // LATE_SHARE
    parts = 1

    def kernel(*refs):
        (tok_far, cot_ref, plc, sto, wx_far, wy_far, wo_far, gain_ref, gates_in, cw, sp, fl) = refs[:12]
        far, gw, cot_all = refs[12:23], refs[23], refs[24]
        tok, wx, wy, wo = refs[25:29]
        results = refs[29:40]
        hp, xext, y, conv_low, conv, pre_r, pre_i, rate, state, merged_st, terms = results
        (h, xf, local, cum, merged, agg, slots, hs, hr, es, er, el, gs, gr, gl) = refs[40:55]
        in_sems, out_sems, cot_held = refs[55:]
        fetch = Fetch(((tok_far, tok), (wx_far, wx), (wy_far, wy), (wo_far, wo)), in_sems)
        store = Fetch(zip(results, far), out_sems)
        fetch.start(0, 1, 2, 3)
        place = Place(n_dp, n_line)
        place.meet(True)
        swap = RimSwap(place, own)
        for side in range(2):
            first = side * wide
            gw[:, first : first + RIM] = jnp.zeros((size, RIM), jnp.bfloat16)
            gw[:, first + RIM : first + RIM + own] = gates_in[:, side * own : (side + 1) * own]
            gw[:, first + RIM + own : first + wide] = jnp.zeros((size, RIM), jnp.bfloat16)
        own_cot = cot_all.at[pl.ds(pl.multiple_of(place.t * cot_rows, 16), cot_rows)]
        cot_ref = cot_ref.at[pl.ds(0, cot_rows)]
        keep = Kept(cot_ref, own_cot, cot_held, gl)
        keep.begin()
        span = cot_rows // parts
        lines = [
            GatherLine(place, cot_all, cot_rows, c * span, span, gs.at[c], gr.at[c])
            for c in range(parts)
        ]
        for c, line in enumerate(lines):
            line.step(0, cot_ref.at[pl.ds(c * span, span)])

        def norm(i):
            here = tile_rows(i, TILE)
            h[here] = rms_scale(tok[here].astype(jnp.float32), gain_ref[...]).astype(jnp.bfloat16)

        fetch.wait(0)
        loop(rows // TILE, norm)
        fetch.wait(1)

        def project(i):
            here = tile_rows(i, 128)
            hp[here] = plain_dot(plc[here], h[...]).astype(jnp.bfloat16)
            xext[tile_rows(i, 128, 16)] = plain_dot(hp[here], wx[...]).astype(jnp.bfloat16)

        loop(rows // 128, project)
        store.start(0)
        edge = remote(
            xext.at[pl.ds(rows, 16)],
            xext.at[pl.ds(0, 16)],
            hs.at[0],
            hr.at[0],
            (lax.rem(place.d + 1, n_dp), place.t),
        )
        edge.start()
        keep.turn()
        for line in lines:
            line.step(1)

        def project_y(i):
            here = tile_rows(i, 128)
            y[here] = plain_dot(hp[here], wy[...])

        fetch.wait(2)
        loop(rows // 128, project_y)
        store.start(2)
        edge.wait()
        top = xext[pl.ds(0, 16)]
        xext[pl.ds(0, 16)] = jnp.where(place.d > 0, top, jnp.zeros_like(top))
        store.start(1)

        def widen(i):
            xf[tile_rows(i, TILE)] = xext[tile_rows(i, TILE)].astype(jnp.float32)

        loop(rows // TILE + 1, widen)

        def convolve(i):
            here = tile_rows(i, TILE)
            near = xf[pl.ds(pl.multiple_of(i * TILE + 8, 8), TILE + 8)]
            same = fl[tile_rows(i, TILE, 8)]
            total = cw[0:1] * near[8:]
            for k in range(1, count):
                total += cw[k : k + 1] * moved_up(near, 8 - k, TILE) * same[:, k : k + 1]
            conv[here] = total
            conv_low[here, RIM : RIM + own] = total.astype(jnp.bfloat16)

        loop(rows // TILE, convolve)
        store.start(4)
        rim = remote(
            conv_low.at[:, swap.edge],
            conv_low.at[:, swap.over_there],
            hs.at[1],
            hr.at[1],
            swap.partner,
        )
        rim.start()
        for i in range(blocks):
            index = lax.rem(i + swap.odd, blocks)
            cols = swap.block(index, size)
            other = pl.ds(pl.multiple_of(wide + swap.first + index * size, RIM), size)
            if i == blocks - 1:
                rim.wait()
            pre_r[:, cols] = plain_dot(conv_low[:, cols], gw[:, cols])
            pre_i[:, cols] = plain_dot(conv_low[:, cols], gw[:, other])

        store.start(3, 5, 6)

        def drive(i):
            here = tile_rows(i, TILE)
            start = fl[tile_rows(i, TILE, 8)][:, 0:1] > 0.0
            own_cols = pl.ds(RIM, own)
            _, decay, scale = rate_and_scale(pre_r[here, own_cols], sp[...], start)
            put_lanes(rate, here, decay)
            put_lanes(local, here, conv[here] * jax.nn.sigmoid(pre_i[here, own_cols]) * scale)

        loop(rows // TILE, drive)
        store.start(7)
        for line in lines:
            line.step(2)
        groups = own // LANES

        def scan(i, carry):
            here = pl.ds(i, 8, chunk)
            result = []
            for c in range(groups):
                product, total = carry[c]
                r = rate[c, here]
                product = product * r
                total = total * r + local[c, here]
                cum[c, here] = product
                local[c, here] = total
                result.append((product, total))
            return tuple(result)

        blank = (jnp.ones((8, LANES), jnp.float32), jnp.zeros((8, LANES), jnp.float32))
        lax.fori_loop(0, chunk, scan, (blank,) * groups)
        product, total = jnp.ones((1, own), jnp.float32), jnp.zeros((1, own), jnp.float32)
        for j in range(8):
            last = pl.ds(j * chunk + chunk - 1, 1)
            total = take_lanes(local, last) + take_lanes(cum, last) * total
            product = product * take_lanes(cum, last)
        agg[0:1] = product
        agg[1:2] = total
        swap_all = Exchange(place, "dp", agg, slots, es, er, el)
        swap_all.begin()
        swap_all.wait()
        entry = jnp.zeros((1, own), jnp.float32)
        for q in range(n_dp):
            longer = slots[q, 1:2] + slots[q, 0:1] * entry
            entry = jnp.where(q < place.d, longer, entry)
        state[pl.ds(0, 8)] = jnp.broadcast_to(entry, (8, own))
        for j in range(8):

            def settle(i, entry=entry):
                here = tile_rows(i, TILE, j * chunk)
                values = take_lanes(local, here) + take_lanes(cum, here) * entry
                state[tile_rows(i, TILE, j * chunk + 8)] = values
                merged[here] = (values * gelu_parts(y[here])[0]).astype(jnp.bfloat16)

            loop(chunk // TILE, settle)
            last = pl.ds(j * chunk + chunk - 1, 1)
            entry = take_lanes(local, last) + take_lanes(cum, last) * entry
        store.start(8)
        merged_st[...] = plain_dot(sto[...], merged[...]).astype(jnp.bfloat16)

        store.start(9)
        fetch.wait(3)

        def mix(i):
            some = tile_rows(i, 512)
            terms[:, pl.ds(pl.multiple_of(i * 512, 512), 512)] = times_trans(
                merged_st[...], wo[some, :]
            ).astype(jnp.bfloat16)

        loop(width // 512, mix)
        for line in lines:
            line.finish()
        keep.finish()
        store.start(10)
        store.wait(*range(11))

    low, full = jnp.bfloat16, jnp.float32
    results = (
        shaped((rows, width), low),
        shaped((rows + 16, own), low),
        shaped((rows, own), full),
        shaped((rows, wide), low),
        shaped((rows, own), full),
        shaped((rows, wide), full),
        shaped((rows, wide), full),
        shaped((own // LANES, rows, LANES), full),
        shaped((rows + 8, own), full),
        shaped((rows, own), low),
        shaped((rows, width), low),
    )
    near, far = in_vmem(), in_any()
    return pl.pallas_call(
        kernel,
        out_shape=results
        + (shaped((size, 2 * wide), low), shaped((n_line * cot_rows, width), low)),
        in_specs=[far, far, near, near, far, far, far] + [near] * 5,
        out_specs=[far] * 11 + [near, far],
        scratch_shapes=[vmem_like(m) for m in (tok_all, x_full, y_full, out_full) + results]
        + [
            pltpu.VMEM((rows, width), low),
            pltpu.VMEM((rows + 16, own), full),
            pltpu.VMEM((own // LANES, rows, LANES), full),
            pltpu.VMEM((own // LANES, rows, LANES), full),
            pltpu.VMEM((rows, own), low),
            pltpu.VMEM((2, own), full),
            pltpu.VMEM((n_dp, 2, own), full),
            dma_sems(2),
            dma_sems(2),
            dma_sems(n_dp),
            dma_sems(n_dp),
            pltpu.SemaphoreType.DMA,
            dma_sems(parts, 2, n_line - 1),
            dma_sems(parts, 2, n_line - 1),
            dma_sems(2),
            dma_sems(4),
            dma_sems(11),
            pltpu.VMEM((cot_rows, width), low),
        ],
        compiler_params=comm_params(5),
        name="recur_forward",
    )(
        tok_all,
        cot,
        to_place,
        to_stored,
        x_full,
        y_full,
        out_full,
        gain,
        gates,
        taps,
        soft,
        flags,
    )


class RowProducts:
    def __init__(self, left, right, far, stage, sems):
        self.left, self.right, self.far, self.stage, self.sems = left, right, far, stage, sems
        self.part = stage.shape[1]
        self.count = far.shape[0] // self.part

    def slot(self, i):
        return self.stage.at[i % 2, :, pl.ds(0, self.far.shape[1])]

    def copy(self, i):
        some = pl.ds(i * self.part, self.part)
        return pltpu.make_async_copy(self.slot(i), self.far.at[some], self.sems.at[i])

    def run(self):
        for i in range(self.count):
            if i >= 2:
                self.copy(i - 2).wait()
            some = pl.ds(i * self.part, self.part)
            self.slot(i)[...] = trans_times(self.left[:, some], self.right[...]).astype(
                jnp.bfloat16
            )
            self.copy(i).start()

    def finish(self):
        self.copy(self.count - 2).wait()
        self.copy(self.count - 1).wait()


def recur_backward(
    n_dp,
    n_line,
    mixer_in,
    to_place,
    to_stored,
    x_full,
    y_full,
    out_full,
    gates,
    taps,
    soft,
    slope,
    flags,
    kept,
    weight_terms,
    row_terms,
    hidden_place,
    merged_stored,
):
    rows, width = mixer_in.shape
    count, own = taps.shape
    size = gates.shape[0]
    wide = own + 2 * RIM
    blocks = (wide - RIM) // size
    chunk = rows // 8
    own_rows = rows // n_line
    parts = 4
    span = own_rows // parts

    def kernel(*refs):
        (mix_far, plc, sto, wx_far, wy_far, wo_far, gw, cw, sp, sg, fl) = refs[:11]
        kept_far, weights, feed_far, hp_far, merged_far = refs[11:19], *refs[19:23]
        (gate_grads, tap_grads, terms_far, weight_sum, row_sum) = refs[23:28]
        out_far, xy_far = refs[28:30]
        mix, wy, wo, feed, merged = refs[30:35]
        (xext, y, conv_low, conv, pre_r, pre_i, rate, state) = refs[35:43]
        (gxy, mp, gm, lam, reach, gp_r, gp_i, grad, spread, rim_out, rim_in) = refs[43:54]
        (ret_out, ret_in, tap_sums, decay_sums, ends, agg, slots) = refs[54:61]
        (hs, hr, es, er, el, in_sems, out_sems, inbox, ls, lr, total) = refs[61:72]
        stage, stage_sems = refs[72:74]
        hp, terms, wx = mix, mix, wo
        fetch = Fetch(
            [
                (mix_far, mix),
                (wo_far, wo),
                (kept_far[1], y),
                (kept_far[7], state),
                (kept_far[6], rate),
                (kept_far[4], pre_r),
                (kept_far[5], pre_i),
                (kept_far[3], conv),
                (kept_far[2], conv_low),
                (kept_far[0], xext),
                (wx_far, wx),
                (wy_far, wy),
                (feed_far, feed),
                (merged_far, merged),
                (hp_far, hp),
            ],
            in_sems,
        )
        fetch.start(12, 0, 1, 13)
        store = Fetch(((terms, terms_far),), out_sems)
        out_rows = RowProducts(mix, merged, out_far, stage, stage_sems.at[0])
        xy_rows = RowProducts(hp, gxy, xy_far, stage, stage_sems.at[1])
        place = Place(n_dp, n_line)
        place.meet(True)
        plane = ReducePlane(place, weights, refs[74:])
        plane.begin((3,))
        lines = [
            ReduceLine(place, feed, own_rows, c * span, span, inbox.at[c], ls.at[c], lr.at[c])
            for c in range(parts)
        ]

        def send(c):
            if c > 0:
                lines[c - 1].sent()
            if c < parts:
                lines[c].ends()

        def add_up(c):
            lines[c].total(total)
            row_sum[pl.ds(c * span, span)] = total[...].astype(jnp.bfloat16)

        fetch.wait(12)
        send(0)
        fetch.start(*range(2, 10), 11)
        swap = RimSwap(place, own)
        own_cols = pl.ds(RIM, own)

        def project(i):
            here = tile_rows(i, 128)
            mp[here] = plain_dot(plc[here], mix[...]).astype(jnp.bfloat16)
            gm[here] = plain_dot(mp[here], wo[...])

        fetch.wait(0, 1)
        plane.cores((3,))
        plane.begin((1, 2, 0))
        loop(rows // 128, project)
        fetch.start(10)
        fetch.wait(13)
        out_rows.run()
        fetch.start(14)

        def split(i):
            here = tile_rows(i, TILE)
            branch, slope_y = gelu_parts(y[here])
            grads = gm[here]
            put_lanes(lam, here, grads * branch)
            values = state[tile_rows(i, TILE, 8)]
            gxy[here, own:] = (grads * values * slope_y).astype(jnp.bfloat16)

        fetch.wait(2, 3)
        loop(rows // TILE, split)
        send(1)
        lines[0].hop(0)
        fetch.wait(4)
        groups = own // LANES

        def scan(i, carry):
            here = pl.ds(chunk - 1 - i, 8, chunk)
            result = []
            for c in range(groups):
                product, message = carry[c]
                r = rate[c, here]
                value = lam[c, here] + message
                lam[c, here] = value
                reach[c, here] = product
                result.append((product * r, value * r))
            return tuple(result)

        blank = (jnp.ones((8, LANES), jnp.float32), jnp.zeros((8, LANES), jnp.float32))
        done = lax.fori_loop(0, chunk, scan, (blank,) * groups)
        for c in range(groups):
            lanes = pl.ds(c * LANES, LANES)
            ends[0, :, lanes] = done[c][0]
            ends[1, :, lanes] = done[c][1]
        product, message = jnp.ones((1, own), jnp.float32), jnp.zeros((1, own), jnp.float32)
        for j in reversed(range(8)):
            message = ends[1, j : j + 1] + ends[0, j : j + 1] * message
            product = product * ends[0, j : j + 1]
        agg[0:1] = product
        agg[1:2] = message
        swap_all = Exchange(place, "dp", agg, slots, es, er, el)
        swap_all.begin()
        plane.cores((1, 2, 0))
        swap_all.wait()
        lines[0].hop(1)
        entry = jnp.zeros((1, own), jnp.float32)
        for q in reversed(range(n_dp)):
            longer = slots[q, 1:2] + slots[q, 0:1] * entry
            entry = jnp.where(q > place.d, longer, entry)
        fetch.wait(5, 6, 7)
        for ref in (tap_sums, decay_sums):
            ref[...] = jnp.zeros_like(ref)
        for ref in (gp_r, gp_i):
            ref[:, 0:RIM] = jnp.zeros((rows, RIM), jnp.bfloat16)
            ref[:, RIM + own :] = jnp.zeros((rows, RIM), jnp.bfloat16)
        grad[pl.ds(0, 8)] = jnp.zeros((8, own), jnp.float32)
        grad[pl.ds(rows + 8, 8)] = jnp.zeros((8, own), jnp.float32)
        for j in reversed(range(8)):

            def back(i, entry=entry):
                here = tile_rows(i, TILE, j * chunk)
                flag = fl[tile_rows(i, TILE, j * chunk + 8)]
                start = flag[:, 0:1] > 0.0
                values = take_lanes(lam, here) + take_lanes(reach, here) * entry
                before = moved_up(
                    state[pl.ds(pl.multiple_of(j * chunk + i * TILE, 8), TILE + 8)], 7, TILE
                )
                sr, decay, scale = rate_and_scale(pre_r[here, own_cols], sp[...], start)
                si = jax.nn.sigmoid(pre_i[here, own_cols])
                block = conv[here]
                driven = values * si
                log_grad = values * before * decay - block * driven * (decay * decay) / scale
                log_grad = jnp.where(start, 0.0, log_grad)
                inner = sr * log_grad
                gp_r[here, own_cols] = (
                    -rate_scale * sp[...] * inner * (1.0 - sr)
                ).astype(jnp.bfloat16)
                gp_i[here, own_cols] = (driven * block * (1.0 - si) * scale).astype(jnp.bfloat16)
                grad[tile_rows(i, TILE, j * chunk + 8)] = driven * scale
                decay_sums[...] += inner[:8] + inner[8:]

            loop(chunk // TILE, back)
            if j == 4:
                send(2)
                lines[1].hop(0)
            entry = ends[1, j : j + 1] + ends[0, j : j + 1] * entry
        lines[1].hop(1)
        add_up(0)

        for i in range(blocks):
            index = lax.rem(i + 2 - 2 * swap.odd, blocks)
            cols = swap.block(index, size)
            other = pl.ds(pl.multiple_of(wide + swap.first + index * size, RIM), size)
            spread[:, cols] = times_trans(gp_r[:, cols], gw[:, cols]) + times_trans(
                gp_i[:, cols], gw[:, other]
            )
            if i == 0:
                rim_out[...] = spread[:, swap.beyond].astype(jnp.bfloat16)
                rim = remote(rim_out, rim_in, hs.at[0], hr.at[0], swap.partner)
                rim.start()
        send(3)
        lines[2].hop(0)
        rim.wait()
        shared = pl.ds(pl.multiple_of((1 - swap.odd) * (own - RIM), RIM), RIM)

        def join(i):
            here = tile_rows(i, TILE)
            there = tile_rows(i, TILE, 8)
            grad[there] += spread[here, own_cols]
            grad[there, shared] += rim_in[here].astype(jnp.float32)

        loop(rows // TILE, join)

        near = grad[pl.ds(0, 16)]
        back_rows = jnp.zeros((8, own), jnp.float32)
        for k in range(1, count):
            masked = near * fl[pl.ds(0, 16)][:, k : k + 1]
            back_rows += cw[k : k + 1] * moved_up(masked, k, 8)
        ret_out[...] = back_rows
        ret = remote(
            ret_out,
            ret_in,
            hs.at[1],
            hr.at[1],
            (lax.rem(place.d + n_dp - 1, n_dp), place.t),
        )
        ret.start()
        plane.turn()
        fetch.wait(8)
        for i in range(blocks):
            cols = swap.block(i, size)
            spread[0:size, cols] = trans_times(conv_low[:, cols], gp_r[:, cols])
            spread[size : 2 * size, cols] = trans_times(conv_low[:, cols], gp_i[:, cols])
        gate_grads[:, 0:own] = spread[0:size, own_cols].astype(jnp.bfloat16)
        gate_grads[:, own:] = spread[size : 2 * size, own_cols].astype(jnp.bfloat16)

        def taps_back(i, added=None):
            here = tile_rows(i, TILE)
            start = pl.ds(pl.multiple_of(i * TILE + 8, 8), TILE + 8)
            after = grad[start]
            flag = fl[start]
            behind = xext[pl.ds(pl.multiple_of(i * TILE, 16), 2 * TILE)].astype(jnp.float32)
            total = cw[0:1] * after[:TILE]
            for k in range(count):
                if k > 0:
                    masked = after * flag[:, k : k + 1]
                    total += cw[k : k + 1] * moved_up(masked, k, TILE)
                    mine = masked[:TILE]
                else:
                    mine = after[:TILE]
                term = mine * moved_up(behind, 16 - k, TILE)
                tap_sums[k] += term[:8] + term[8:]
            if added is not None:
                total = total + jnp.concatenate([jnp.zeros((8, own), jnp.float32), added], axis=0)
            gxy[here, 0:own] = total.astype(jnp.bfloat16)

        fetch.wait(9)
        loop(rows // TILE - 1, taps_back)
        lines[2].hop(1)
        add_up(1)
        ret.wait()
        taps_back(rows // TILE - 1, jnp.where(place.d < n_dp - 1, ret_in[...], 0.0))
        tap_grads[...] = jnp.zeros_like(tap_grads)
        for k in range(count):
            tap_grads[k : k + 1] = jnp.sum(tap_sums[k], axis=0, keepdims=True)
        tap_grads[count : count + 1] = (
            rate_scale * sg[...] * jnp.sum(decay_sums[...], axis=0, keepdims=True)
        )

        fetch.wait(14)
        out_rows.finish()
        xy_rows.run()
        send(4)
        lines[3].hop(0)

        def restore(i):
            here = tile_rows(i, 128)
            mp[here, 0 : 2 * own] = plain_dot(sto[here], gxy[...]).astype(jnp.bfloat16)

        loop(rows // 128, restore)

        def spread_back(i):
            some = tile_rows(i, 512)
            terms[:, pl.ds(pl.multiple_of(i * 512, 512), 512)] = (
                times_trans(mp[:, 0:own], wx[some]) + times_trans(mp[:, own : 2 * own], wy[some])
            ).astype(jnp.bfloat16)

        fetch.wait(10, 11)
        loop(width // 512, spread_back)
        store.start(0)
        lines[3].hop(1)
        add_up(2)
        plane.finish(weight_sum)
        add_up(3)
        for line in lines:
            line.finish()
        xy_rows.finish()
        store.wait(0)

    low, full = jnp.bfloat16, jnp.float32
    block = weight_terms.shape[0] // n_dp
    near, far = in_vmem(), in_any()
    return pl.pallas_call(
        kernel,
        out_shape=(
            shaped((size, 2 * own), low),
            shaped((8, own), full),
            shaped((rows, width), low),
            shaped((block, weight_terms.shape[1]), low),
            shaped((own_rows, width), low),
            shaped((width, own), low),
            shaped((width, 2 * own), low),
        ),
        in_specs=[far, near, near, far, far, far] + [near] * 5 + [far] * 12,
        out_specs=[near, near, far, near, near, far, far],
        scratch_shapes=[
            vmem_like(m) for m in (mixer_in, y_full, out_full, row_terms, merged_stored, *kept)
        ]
        + [
            pltpu.VMEM((rows, 2 * own), low),
            pltpu.VMEM((rows, width), low),
            pltpu.VMEM((rows, own), full),
            pltpu.VMEM((own // LANES, rows, LANES), full),
            pltpu.VMEM((own // LANES, rows, LANES), full),
            pltpu.VMEM((rows, wide), low),
            pltpu.VMEM((rows, wide), low),
            pltpu.VMEM((rows + 16, own), full),
            pltpu.VMEM((rows, wide), full),
            pltpu.VMEM((rows, RIM), low),
            pltpu.VMEM((rows, RIM), low),
            pltpu.VMEM((8, own), full),
            pltpu.VMEM((8, own), full),
            pltpu.VMEM((count, 8, own), full),
            pltpu.VMEM((8, own), full),
            pltpu.VMEM((2, 8, own), full),
            pltpu.VMEM((2, own), full),
            pltpu.VMEM((n_dp, 2, own), full),
            dma_sems(2),
            dma_sems(2),
            dma_sems(n_dp),
            dma_sems(n_dp),
            pltpu.SemaphoreType.DMA,
            dma_sems(15),
            dma_sems(1),
            pltpu.VMEM((parts, 2, n_line - 1, span, width), low),
            dma_sems(parts, 2, n_line - 1),
            dma_sems(parts, 2, n_line - 1),
            pltpu.VMEM((span, width), full),
            pltpu.VMEM((2, width // 5, 2 * own), low),
            dma_sems(2, 5),
        ]
        + ReducePlane.scratch(block, weight_terms.shape[1]),
        compiler_params=comm_params(6),
        name="recur_backward",
    )(
        mixer_in,
        to_place,
        to_stored,
        x_full,
        y_full,
        out_full,
        gates,
        taps,
        soft,
        slope,
        flags,
        *kept,
        weight_terms,
        row_terms,
        hidden_place,
        merged_stored,
    )


def column_parts(width, size=768):
    return [(c, min(size, width - c)) for c in range(0, width, size)]


def feed_forward(n_dp, n_line, hidden, gate, up, down, grads, grad_own):
    rows, width = hidden.shape
    units = gate.shape[1]
    own_rows = grad_own.shape[0]
    ready = grads.shape[0] // n_line
    late = own_rows - ready
    part = width // 4

    def kernel(*refs):
        hid_far, wg_far, wu_far, wd_far, grads_far, own_far = refs[:6]
        product_far, gup_far, back_far, gdown_far, ggate_far = refs[6:11]
        hid, wg, wu, wd, grad, slope, branch, product, ggate, gup, stage, back = refs[11:23]
        in_sems, out_sems, stage_sems, ls, lr = refs[23:]
        place = Place(n_dp, n_line)
        pairs = [(hid_far, hid), (wg_far, wg), (wu_far, wu), (wd_far, wd)]
        pairs += [
            (grads_far.at[pl.ds(q * ready, ready)], grad.at[pl.ds(q * own_rows, ready)])
            for q in range(n_line)
        ]
        mine = pl.ds(pl.multiple_of(place.t * own_rows + ready, 16), late)
        pairs.append((own_far.at[pl.ds(ready, late)], grad.at[mine]))
        fetch = Fetch(pairs, in_sems)
        fetch.start(*range(len(pairs)))
        store = Fetch(((product, product_far), (gup, gup_far), (back, back_far)), out_sems)
        place.meet()
        line = GatherLine(place, grad, own_rows, ready, late, ls, lr)
        line.step(0, own_far.at[pl.ds(ready, late)])
        columns = column_parts(units)
        fetch.wait(0, 1)
        for c, size in columns:
            cols = pl.ds(c, size)

            def gates(i, cols=cols):
                here = tile_rows(i, 256)
                branch[here, cols] = plain_dot(hid[here], wg[:, cols])

            loop(rows // 256, gates)
        line.step(1)
        fetch.wait(2)
        for c, size in columns:
            cols = pl.ds(c, size)

            def ups(i, cols=cols):
                here = tile_rows(i, 256)
                value = plain_dot(hid[here], wu[:, cols])
                active, bend = gelu_parts(branch[here, cols])
                product[here, cols] = (active * value).astype(jnp.bfloat16)
                branch[here, cols] = active
                slope[here, cols] = bend * value

            loop(rows // 256, ups)
        store.start(0)
        line.step(2)
        fetch.wait(*range(4, len(pairs)))
        line.finish()

        down_rows = RowProducts(grad, product, gdown_far, stage, stage_sems.at[0])
        down_rows.run()
        fetch.wait(3)
        for c, size in columns:
            cols = pl.ds(c, size)

            def backs(i, cols=cols):
                here = tile_rows(i, 256)
                value = plain_dot(grad[here], wd[:, cols])
                ggate[here, cols] = (value * slope[here, cols]).astype(jnp.bfloat16)
                gup[here, cols] = (value * branch[here, cols]).astype(jnp.bfloat16)

            loop(rows // 256, backs)
        store.start(1)
        for i in range(4):
            some = pl.ds(i * part, part)
            back[:, some] = (
                times_trans(ggate[...], wg[some]) + times_trans(gup[...], wu[some])
            ).astype(jnp.bfloat16)
        store.start(2)
        down_rows.finish()
        gate_rows = RowProducts(hid, ggate, ggate_far, stage, stage_sems.at[1])
        gate_rows.run()
        gate_rows.finish()
        store.wait(0, 1, 2)

    low, full = jnp.bfloat16, jnp.float32
    return pl.pallas_call(
        kernel,
        out_shape=(
            shaped((rows, units), low),
            shaped((rows, units), low),
            shaped((rows, width), low),
            shaped((width, units), low),
            shaped((width, units), low),
        ),
        in_specs=[in_any()] * 6,
        out_specs=[in_any()] * 5,
        scratch_shapes=[vmem_like(m) for m in (hidden, gate, up, down)]
        + [
            pltpu.VMEM((n_line * own_rows, width), low),
            pltpu.VMEM((rows, units), full),
            pltpu.VMEM((rows, units), full),
            pltpu.VMEM((rows, units), low),
            pltpu.VMEM((rows, units), low),
            pltpu.VMEM((rows, units), low),
            pltpu.VMEM((2, part, units), low),
            pltpu.VMEM((rows, width), low),
            dma_sems(5 + n_line),
            dma_sems(3),
            dma_sems(2, 4),
            dma_sems(2, n_line - 1),
            dma_sems(2, n_line - 1),
        ],
        compiler_params=comm_params(7),
        name="feed_forward",
    )(hidden, gate, up, down, grads, grad_own)


def matches(mesh):
    return mesh.shape["dp"] == 8 and mesh.shape["tensor"] == 4


def local_blocks(
    tokens,
    norm_gain,
    x_weight,
    y_weight,
    conv_weight,
    recur_gate_weight,
    input_gate_weight,
    decay_param,
    out_weight,
    mlp_gain,
    gate_weight,
    up_weight,
    down_weight,
    seq_lengths,
    token_order,
    cotangent,
):
    n_dp, n_tensor = lax.axis_size("dp"), lax.axis_size("tensor")
    tensor_index = lax.axis_index("tensor")
    dp_index = lax.axis_index("dp")
    tok_rows, width = tokens.shape
    row_count = tok_rows * n_tensor
    own_width = conv_weight.shape[1]
    kernel_taps = conv_weight.shape[0]
    edge_rows = kernel_taps - 1
    dp_width = norm_gain.shape[0]
    gate_rows = recur_gate_weight.shape[0]
    own_start = tensor_index * tok_rows

    gains = jnp.concatenate([norm_gain, mlp_gain])
    spare = gate_rows * 128 - gains.shape[0]
    gains = jnp.pad(gains, (0, spare)).reshape(gate_rows, 128)
    minor = jnp.concatenate([recur_gate_weight, input_gate_weight, gains], axis=1)
    own_order = (token_order - dp_index * row_count).astype(jnp.int32)
    order_rows = jnp.broadcast_to(own_order[None, :], (8, tok_rows))
    x_full, y_full, out_full, minor_full, tok_all, order_full = first_gather(
        n_dp, n_tensor, (x_weight, y_weight, out_weight.T, minor), tokens, order_rows
    )
    late_down, _ = lax.optimization_barrier((down_weight.T, tok_all))
    up_full = lax.all_gather(up_weight, "dp", axis=0, tiled=True)
    down_full = lax.all_gather(late_down, "dp", axis=0, tiled=True)
    order_all = order_full.reshape(n_tensor, 8, tok_rows)[:, 0].reshape(row_count)
    gain_rows = minor_full[:, 2 * own_width :].reshape(n_dp, -1)
    first_gain = gain_rows[:, :dp_width].reshape(1, width).astype(jnp.float32)
    second_gain = gain_rows[:, dp_width : 2 * dp_width].reshape(1, width).astype(jnp.float32)
    row_index = jnp.arange(row_count, dtype=jnp.int32)
    hits = row_index[:, None] == order_all[None, :]
    to_place = hits.astype(jnp.bfloat16)
    to_stored = (order_all[:, None] == row_index[None, :]).astype(jnp.bfloat16)
    places = dp_index * row_count + jnp.arange(-8, row_count + 8, dtype=jnp.int32)
    inside = (jnp.arange(row_count + 16) >= 8) & (jnp.arange(row_count + 16) < row_count + 8)
    ends = jnp.cumsum(seq_lengths)
    segment = segment_of(places, ends)
    starts = (places == 0) | (segment != segment_of(places - 1, ends))
    columns = [starts] + [
        segment_of(places - shift, ends) == segment for shift in range(1, kernel_taps)
    ]
    columns += [jnp.zeros_like(starts)] * (8 - len(columns))
    flags = (jnp.stack(columns, axis=1) & inside[:, None]).astype(jnp.float32)
    live_own = (token_order < ends[-1]).astype(jnp.float32)
    grad_in_own = (cotangent.astype(jnp.float32) * live_own[:, None]).astype(jnp.bfloat16)
    soft = jax.nn.softplus(-decay_param).reshape(1, own_width)
    slope = jax.nn.sigmoid(-decay_param).reshape(1, own_width)
    hidden_place, *kept, merged_stored, mixer_terms, gates_wide, grad_rows = recur_forward(
        n_dp,
        n_tensor,
        tok_all,
        grad_in_own,
        to_place,
        to_stored,
        x_full,
        y_full,
        out_full,
        first_gain,
        minor_full,
        conv_weight,
        soft,
        flags,
    )
    after_own, hidden_two, gate_full = middle_gather(
        n_dp, n_tensor, mixer_terms, tokens, second_gain, (gate_weight,)
    )
    product, grad_up_pre, back_terms, grad_down, grad_gate = feed_forward(
        n_dp,
        n_tensor,
        hidden_two,
        gate_full,
        up_full,
        down_full,
        grad_rows,
        grad_in_own,
    )
    down_sum = lax.psum_scatter(grad_down, "dp", scatter_dimension=0, tiled=True)
    grad_after_own, second_part, mixer_in, gate_sum, grad_up, feed_terms = middle_sums(
        n_dp,
        n_tensor,
        back_terms,
        after_own,
        second_gain,
        grad_in_own,
        grad_gate,
        hidden_two,
        grad_up_pre,
        product,
        down_full,
    )
    (
        gate_grads,
        tap_grads,
        one_terms,
        up_sum,
        feed_out,
        grad_out_mat,
        grad_xy_mat,
    ) = recur_backward(
        n_dp,
        n_tensor,
        mixer_in,
        to_place,
        to_stored,
        x_full,
        y_full,
        out_full,
        gates_wide,
        conv_weight,
        soft,
        slope,
        flags,
        kept,
        grad_up,
        feed_terms,
        hidden_place,
        merged_stored,
    )
    output = (after_own + feed_out.astype(jnp.float32)) * live_own[:, None]
    output = output.astype(jnp.bfloat16)
    grad_tokens, small_sum, gain_sums, xy_sum, out_sum, gates_sum = last_sums(
        n_dp,
        n_tensor,
        one_terms,
        tokens,
        first_gain,
        grad_after_own,
        second_part,
        tap_grads,
        (grad_xy_mat, grad_out_mat, gate_grads),
    )
    xy_sum, gates_sum = xy_sum.astype(jnp.float32), gates_sum.astype(jnp.float32)
    own_gains = lax.dynamic_slice_in_dim(gain_sums, dp_index * dp_width, dp_width, 1)
    return (
        output,
        grad_tokens,
        own_gains[1],
        xy_sum[:, :own_width],
        xy_sum[:, own_width:],
        small_sum[:kernel_taps],
        gates_sum[:, :own_width],
        gates_sum[:, own_width:],
        small_sum[kernel_taps],
        out_sum.astype(jnp.float32).T,
        own_gains[0],
        gate_sum.astype(jnp.float32),
        up_sum.astype(jnp.float32),
        down_sum.astype(jnp.float32).T,
    )


def solution(mesh):
    in_specs = (
        P(("dp", "tensor"), None),
        P("dp"),
        P("dp", "tensor"),
        P("dp", "tensor"),
        P(None, "tensor"),
        P("dp", "tensor"),
        P("dp", "tensor"),
        P("tensor"),
        P("tensor", "dp"),
        P("dp"),
        P("dp", "tensor"),
        P("dp", "tensor"),
        P("tensor", "dp"),
        P(),
        P(("dp", "tensor")),
        P(("dp", "tensor"), None),
    )
    out_specs = (
        P(("dp", "tensor"), None),
        P(("dp", "tensor"), None),
        P("dp"),
        P("dp", "tensor"),
        P("dp", "tensor"),
        P(None, "tensor"),
        P("dp", "tensor"),
        P("dp", "tensor"),
        P("tensor"),
        P("tensor", "dp"),
        P("dp"),
        P("dp", "tensor"),
        P("dp", "tensor"),
        P("tensor", "dp"),
    )
    fits = matches(mesh)
    local = local_blocks if fits else local_general
    return jax.shard_map(local, mesh=mesh, in_specs=in_specs, out_specs=out_specs, check_vma=False)
```

```python
import jax
import jax.numpy as jnp
from jax import lax
from jax.experimental import pallas as pl
from jax.experimental.pallas import tpu as pltpu
from jax.sharding import PartitionSpec as P

epsilon = 1e-06
rate_scale = 8.0


def from_behind(block, axis, distance):
    devices = range(lax.axis_size(axis))
    route = [(i - distance, i) for i in devices if i - distance in devices]
    return lax.ppermute(block, axis, route)


def extended_2(array, sides, width):
    for axis, dim in sides:
        size, length = (lax.axis_size(axis), array.shape[dim])
        up = [(i, (i + 1) % size) for i in range(size - 1)]
        down = [(j, i) for i, j in up]
        last = lax.slice_in_dim(array, length - width, length, axis=dim)
        leading = lax.slice_in_dim(array, 0, width, axis=dim)
        before = lax.ppermute(last, axis, up)
        after = lax.ppermute(leading, axis, down)
        array = jnp.concatenate([before, array, after], axis=dim)
    return array


def entering(value, axis, join, neutral, backward):
    count, mine = (lax.axis_size(axis), lax.axis_index(axis))
    pieces = jax.tree.map(lambda part: lax.all_gather(part, axis), value)
    if backward:
        pieces = jax.tree.map(lambda part: part[::-1], pieces)
        mine = count - 1 - mine
    total = jax.tree.map(
        lambda part, zero: jnp.full_like(part, 0) + jnp.asarray(zero, part.dtype), value, neutral
    )

    def lap(position, total):
        longer = join(total, jax.tree.map(lambda part: part[position], pieces))
        return jax.tree.map(lambda new, old: jnp.where(position < mine, new, old), longer, total)

    return lax.fori_loop(0, count - 1, lap, total)


def rms_scale(values, gain):
    return values * lax.rsqrt(jnp.mean(values * values, axis=-1, keepdims=True) + epsilon) * gain


def norm_back(values, gain, grad):
    inv_root = lax.rsqrt(jnp.mean(values * values, axis=-1, keepdims=True) + epsilon)
    normed = values * inv_root
    upstream = grad * gain
    grad_values = inv_root * (
        upstream - normed * jnp.mean(upstream * normed, axis=-1, keepdims=True)
    )
    return (grad_values, normed)


def segment_of(places, ends):
    return jnp.sum((ends[None, :] <= places[:, None]).astype(jnp.int32), axis=1)


def pair_step(early, later):
    return (early[0] * later[0], later[0] * early[1] + later[1])


def plain_dot(left, right):
    return jnp.dot(left, right, preferred_element_type=jnp.float32)


def times_trans(left, right):
    return lax.dot_general(
        left, right, (((1,), (1,)), ((), ())), preferred_element_type=jnp.float32
    )


def trans_times(left, right):
    return lax.dot_general(
        left, right, (((0,), (0,)), ((), ())), preferred_element_type=jnp.float32
    )


def gelu_tanh(values):
    return jax.nn.gelu(values, approximate=True)


def collect(
    norm_gain,
    mlp_gain,
    x_weight,
    y_weight,
    recur_gate_weight,
    input_gate_weight,
    gate_weight,
    up_weight,
    out_weight,
    down_weight,
):
    return (
        lax.all_gather(norm_gain, "dp", axis=0, tiled=True),
        lax.all_gather(mlp_gain, "dp", axis=0, tiled=True),
        lax.all_gather(x_weight, "dp", axis=0, tiled=True),
        lax.all_gather(y_weight, "dp", axis=0, tiled=True),
        lax.all_gather(recur_gate_weight, "dp", axis=0, tiled=True),
        lax.all_gather(input_gate_weight, "dp", axis=0, tiled=True),
        lax.all_gather(gate_weight, "dp", axis=0, tiled=True),
        lax.all_gather(up_weight, "dp", axis=0, tiled=True),
        lax.all_gather(out_weight, "dp", axis=1, tiled=True),
        lax.all_gather(down_weight, "dp", axis=1, tiled=True),
    )


def row_sums(term_rows, tok_rows):
    return lax.psum_scatter(
        term_rows(jnp.int32(0), lax.axis_size("tensor") * tok_rows).astype(jnp.bfloat16),
        "tensor",
        scatter_dimension=0,
        tiled=True,
    ).astype(jnp.float32)


def spread_rows(values):
    return lax.all_gather(values, "tensor", axis=0, tiled=True)


def local_general(
    tokens,
    norm_gain,
    x_weight,
    y_weight,
    conv_weight,
    recur_gate_weight,
    input_gate_weight,
    decay_param,
    out_weight,
    mlp_gain,
    gate_weight,
    up_weight,
    down_weight,
    seq_lengths,
    token_order,
    cotangent,
):
    n_tensor = lax.axis_size("tensor")
    tensor_index = lax.axis_index("tensor")
    dp_index = lax.axis_index("dp")
    tok_rows = tokens.shape[0]
    row_count = tok_rows * n_tensor
    own_width = conv_weight.shape[1]
    kernel_taps = conv_weight.shape[0]
    edge_rows = kernel_taps - 1
    dp_width = norm_gain.shape[0]
    own_start = tensor_index * tok_rows
    shards = (
        norm_gain,
        mlp_gain,
        x_weight,
        y_weight,
        recur_gate_weight,
        input_gate_weight,
        gate_weight,
        up_weight,
        out_weight,
        down_weight,
    )
    (
        gain_one,
        gain_two,
        x_full,
        y_full,
        recur_full,
        input_full,
        gate_full,
        up_full,
        out_full,
        down_full,
    ) = collect(*shards)
    block_size = recur_full.shape[0]
    first_gain = gain_one.astype(jnp.float32)
    second_gain = gain_two.astype(jnp.float32)
    both_gates = jnp.concatenate([recur_full, input_full], axis=1)
    tok_own = tokens.astype(jnp.float32)
    own_order = token_order - dp_index * row_count
    first_rows = rms_scale(tok_own, first_gain).astype(jnp.bfloat16)
    first_all, cot_all, order_all = (
        lax.all_gather(first_rows, "tensor", axis=0, tiled=True),
        lax.all_gather(cotangent, "tensor", axis=0, tiled=True),
        lax.all_gather(own_order, "tensor", axis=0, tiled=True),
    )
    row_index = jnp.arange(row_count, dtype=jnp.int32)
    inverse = jnp.zeros((row_count,), jnp.int32).at[order_all].set(row_index)
    hidden_place = jnp.take(first_all, inverse, axis=0)
    places = dp_index * row_count + row_index
    ends = jnp.cumsum(seq_lengths)
    segment = segment_of(places, ends)
    starts = (places == 0) | (segment != segment_of(places - 1, ends))
    live = (places < ends[-1]).astype(jnp.float32)
    live_stored = jnp.take(live, order_all, axis=0)
    same = [
        (segment_of(places - shift, ends) == segment).astype(jnp.float32)
        for shift in range(kernel_taps)
    ]
    low_edge = tensor_index * own_width
    own_blocks = (low_edge + jnp.arange(own_width, dtype=jnp.int32)) // block_size
    first_block = low_edge // block_size
    block_count = own_width // block_size + 2

    def block_start(index):
        return (first_block + index) * block_size - low_edge + block_size

    def block_mask(index):
        inside = own_blocks == first_block + index
        return jnp.concatenate([inside, inside])

    def convolve(extended, kernel):
        return sum(
            (
                kernel[shift][None, :]
                * extended[edge_rows - shift : edge_rows - shift + row_count]
                * same[shift][:, None]
                for shift in range(kernel_taps)
            )
        )

    def gates(conv_vals, pre_recur, pre_input, decay_vals):
        log_rate = -rate_scale * jax.nn.sigmoid(pre_recur) * jax.nn.softplus(-decay_vals)
        decay_rate = jnp.where(starts[:, None], 0.0, jnp.exp(log_rate))
        scale_in = jnp.where(starts[:, None], 1.0, jnp.sqrt(-jnp.expm1(2.0 * log_rate)))
        return (decay_rate, conv_vals * jax.nn.sigmoid(pre_input) * scale_in)

    def glu(gate_pre, up_pre):
        return gelu_tanh(gate_pre) * up_pre

    x_branch = plain_dot(hidden_place, x_full).astype(jnp.bfloat16)
    y_before = plain_dot(hidden_place, y_full)
    previous = from_behind(x_branch[row_count - edge_rows :], "dp", 1)
    extended = jnp.concatenate([previous, x_branch], axis=0).astype(jnp.float32)
    conv_out = convolve(extended, conv_weight)
    conv_wide = extended_2(conv_out.astype(jnp.bfloat16), (("tensor", 1),), block_size)
    pre_both = jnp.zeros((row_count, 2 * own_width), jnp.float32)
    for index in range(block_count):
        piece = lax.dynamic_slice_in_dim(conv_wide, block_start(index), block_size, 1)
        pre_both = pre_both + jnp.where(
            block_mask(index)[None, :], plain_dot(piece, both_gates), 0.0
        )
    (decay_rate, driven), gate_pull = jax.vjp(
        gates, conv_out, pre_both[:, :own_width], pre_both[:, own_width:], decay_param
    )
    cum_rate, local_state = lax.associative_scan(pair_step, (decay_rate, driven), axis=0)
    ident = (jnp.ones((own_width,), jnp.float32), jnp.zeros((own_width,), jnp.float32))
    rate_in, state_in = entering((cum_rate[-1], local_state[-1]), "dp", pair_step, ident, False)
    state = local_state + cum_rate * state_in[None, :]
    y_branch = gelu_tanh(y_before)
    merged = (state * y_branch).astype(jnp.bfloat16)
    merged_stored = jnp.take(merged, order_all, axis=0)

    def mixer_rows(begin, number):
        return plain_dot(merged_stored, out_full)

    after_own = tok_own + row_sums(mixer_rows, tok_rows)
    hidden_two = spread_rows(rms_scale(after_own, second_gain).astype(jnp.bfloat16))
    gate_pre = plain_dot(hidden_two, gate_full)
    up_pre = plain_dot(hidden_two, up_full)
    glu_out, glu_pull = jax.vjp(glu, gate_pre, up_pre)
    product = glu_out.astype(jnp.bfloat16)

    def down_rows(begin, number):
        return plain_dot(product, down_full)

    feed_out = row_sums(down_rows, tok_rows)
    live_own = lax.dynamic_slice_in_dim(live_stored, own_start, tok_rows, 0)
    output = ((after_own + feed_out) * live_own[:, None]).astype(jnp.bfloat16)
    grad_out = cot_all.astype(jnp.float32) * live_stored[:, None]
    fresh = lax.optimization_barrier((shards, grad_out))[0]
    (
        gain_one,
        gain_two,
        x_full,
        y_full,
        recur_full,
        input_full,
        gate_full,
        up_full,
        out_full,
        down_full,
    ) = collect(*fresh)
    first_gain = gain_one.astype(jnp.float32)
    second_gain = gain_two.astype(jnp.float32)
    both_gates = jnp.concatenate([recur_full, input_full], axis=1)
    down_in = grad_out.astype(jnp.bfloat16)
    grad_down = trans_times(product, down_in)
    grad_product = times_trans(down_in, down_full)
    grad_gate_pre, grad_up_pre = glu_pull(grad_product)
    grad_gate_pre = grad_gate_pre.astype(jnp.bfloat16)
    grad_up_pre = grad_up_pre.astype(jnp.bfloat16)
    grad_gate = trans_times(hidden_two, grad_gate_pre)
    grad_up = trans_times(hidden_two, grad_up_pre)

    def feed_rows(begin, number):
        return times_trans(grad_gate_pre, gate_full) + times_trans(grad_up_pre, up_full)

    grad_out_own = lax.dynamic_slice_in_dim(grad_out, own_start, tok_rows, 0)
    grad_two_own = row_sums(feed_rows, tok_rows)
    grad_norm_own, normed_two = norm_back(after_own, second_gain, grad_two_own)
    second_part = jnp.sum(grad_two_own * normed_two, axis=0)
    grad_after_own = grad_out_own + grad_norm_own
    mixer_in = spread_rows(grad_after_own.astype(jnp.bfloat16))
    grad_out_mat = trans_times(merged_stored, mixer_in)
    grad_merged = jnp.take(times_trans(mixer_in, out_full), inverse, axis=0)
    grad_state = grad_merged * y_branch
    gelu_pull = jax.vjp(gelu_tanh, y_before)[1]
    grad_y_before = gelu_pull(grad_merged * state)[0].astype(jnp.bfloat16)
    rate_next = jnp.concatenate([decay_rate[1:], jnp.ones((1, own_width), jnp.float32)], axis=0)
    rev_rate, local_lam = lax.associative_scan(
        pair_step, (rate_next, grad_state), reverse=True, axis=0
    )
    head_rate = decay_rate[0] * rev_rate[0]
    head_lam = decay_rate[0] * local_lam[0]
    factor_in, lam_in = entering((head_rate, head_lam), "dp", pair_step, ident, True)
    lam = local_lam + rev_rate * lam_in[None, :]
    state_prev = jnp.concatenate([state_in[None, :], state[:-1]], axis=0)
    grad_conv_local, grad_pre_recur, grad_pre_input, grad_decay_own = gate_pull(
        (lam * state_prev, lam)
    )
    grad_pre = jnp.concatenate([grad_pre_recur, grad_pre_input], axis=1).astype(jnp.bfloat16)
    grad_both = jnp.zeros((block_size, 2 * own_width), jnp.float32)
    grad_wide = jnp.zeros((row_count, own_width + 2 * block_size), jnp.float32)
    for index in range(block_count):
        begin = block_start(index)
        piece = lax.dynamic_slice_in_dim(conv_wide, begin, block_size, 1)
        masked = jnp.where(block_mask(index)[None, :], grad_pre, jnp.zeros((), jnp.bfloat16))
        grad_both = grad_both + trans_times(piece, masked)
        added = lax.dynamic_slice_in_dim(grad_wide, begin, block_size, 1) + times_trans(
            masked, both_gates
        )
        grad_wide = lax.dynamic_update_slice_in_dim(grad_wide, added, begin, 1)
    grad_recur = grad_both[:, :own_width]
    grad_input = grad_both[:, own_width:]
    rims = jnp.concatenate(
        [grad_wide[:, :block_size], grad_wide[:, own_width + block_size :]], axis=1
    )
    arrived = extended_2(rims.astype(jnp.bfloat16), (("tensor", 1),), block_size).astype(rims.dtype)
    from_lower = jnp.pad(arrived[:, :block_size], ((0, 0), (0, own_width - block_size)))
    from_upper = jnp.pad(arrived[:, 3 * block_size :], ((0, 0), (own_width - block_size, 0)))
    grad_conv = (
        grad_conv_local
        + grad_wide[:, block_size : block_size + own_width]
        + from_lower
        + from_upper
    )
    conv_pull = jax.vjp(convolve, extended, conv_weight)[1]
    grad_extended, grad_kernel = conv_pull(grad_conv)
    returned = from_behind(grad_extended[:edge_rows], "dp", -1)
    grad_x_branch = grad_extended[edge_rows:] + jnp.concatenate(
        [jnp.zeros((row_count - edge_rows, own_width), jnp.float32), returned], axis=0
    )
    grad_x_low = grad_x_branch.astype(jnp.bfloat16)
    grad_x_stored = jnp.take(grad_x_low, order_all, axis=0)
    grad_y_stored = jnp.take(grad_y_before, order_all, axis=0)
    grad_x_mat = trans_times(first_all, grad_x_stored)
    grad_y_mat = trans_times(first_all, grad_y_stored)

    def mixer_back_rows(begin, number):
        return times_trans(grad_x_stored, x_full) + times_trans(grad_y_stored, y_full)

    grad_one_own = row_sums(mixer_back_rows, tok_rows)
    grad_norm_one, normed_one = norm_back(tok_own, first_gain, grad_one_own)
    first_part = jnp.sum(grad_one_own * normed_one, axis=0)
    grad_tokens = grad_after_own + grad_norm_one
    chosen = jnp.arange(n_tensor, dtype=jnp.int32) == tensor_index
    kernel_tile = jnp.where(chosen[:, None, None], grad_kernel[None, :, :], 0.0)
    decay_tile = jnp.where(chosen[:, None], grad_decay_own[None, :], 0.0)
    small = lax.psum((first_part, second_part, kernel_tile, decay_tile), ("dp", "tensor"))
    grad_first_gain = lax.dynamic_slice_in_dim(small[0], dp_index * dp_width, dp_width, 0)
    grad_second_gain = lax.dynamic_slice_in_dim(small[1], dp_index * dp_width, dp_width, 0)
    grad_kernel_sum = lax.dynamic_index_in_dim(small[2], tensor_index, 0, keepdims=False)
    grad_decay = lax.dynamic_index_in_dim(small[3], tensor_index, 0, keepdims=False)
    sums = (
        lax.psum_scatter(
            grad_x_mat.astype(jnp.bfloat16), "dp", scatter_dimension=0, tiled=True
        ).astype(jnp.float32),
        lax.psum_scatter(
            grad_y_mat.astype(jnp.bfloat16), "dp", scatter_dimension=0, tiled=True
        ).astype(jnp.float32),
        lax.psum_scatter(
            grad_recur.astype(jnp.bfloat16), "dp", scatter_dimension=0, tiled=True
        ).astype(jnp.float32),
        lax.psum_scatter(
            grad_input.astype(jnp.bfloat16), "dp", scatter_dimension=0, tiled=True
        ).astype(jnp.float32),
        lax.psum_scatter(
            grad_gate.astype(jnp.bfloat16), "dp", scatter_dimension=0, tiled=True
        ).astype(jnp.float32),
        lax.psum_scatter(
            grad_up.astype(jnp.bfloat16), "dp", scatter_dimension=0, tiled=True
        ).astype(jnp.float32),
        lax.psum_scatter(
            grad_out_mat.astype(jnp.bfloat16), "dp", scatter_dimension=1, tiled=True
        ).astype(jnp.float32),
        lax.psum_scatter(
            grad_down.astype(jnp.bfloat16), "dp", scatter_dimension=1, tiled=True
        ).astype(jnp.float32),
    )
    return (
        output,
        grad_tokens,
        grad_first_gain,
        sums[0],
        sums[1],
        grad_kernel_sum,
        sums[2],
        sums[3],
        grad_decay,
        sums[6],
        grad_second_gain,
        sums[4],
        sums[5],
        sums[7],
    )


MESH = pl.DeviceIdType.MESH
VMEM_BYTES = 60 * 2**20


def remote(src, dst, send, recv, device):
    return pltpu.make_async_remote_copy(
        src_ref=src,
        dst_ref=dst,
        send_sem=send,
        recv_sem=recv,
        device_id=device,
        device_id_type=MESH,
    )


class Place:
    def __init__(self, n_dp, n_line):
        self.n_dp, self.n_line = n_dp, n_line
        self.d, self.t = lax.axis_index("dp"), lax.axis_index("tensor")
        self.core = lax.rem(self.d, 2)
        self.x = lax.rem(lax.div(self.d, 2), 2)
        self.y = lax.div(self.d, 4)

    def chip(self, flip_x, flip_y, flip_core=0):
        x = 1 - self.x if flip_x else self.x
        y = 1 - self.y if flip_y else self.y
        core = 1 - self.core if flip_core else self.core
        return y * 4 + x * 2 + core

    def at(self, flip_x=0, flip_y=0, flip_core=0):
        return (self.chip(flip_x, flip_y, flip_core), self.t)

    def up(self):
        return (self.d, lax.rem(self.t + 1, self.n_line))

    def down(self):
        return (self.d, lax.rem(self.t + self.n_line - 1, self.n_line))

    def meet(self, everyone=False):
        barrier = pltpu.get_barrier_semaphore()

        def greet(device):
            pl.semaphore_signal(barrier, inc=1, device_id=device, device_id_type=MESH)

        if everyone:
            for i in range(1, self.n_dp):
                greet((lax.rem(self.d + i, self.n_dp), self.t))
            for i in range(1, self.n_line):
                greet((self.d, lax.rem(self.t + i, self.n_line)))
            pl.semaphore_wait(barrier, self.n_dp + self.n_line - 2)
            return
        for flips in ((1, 0), (0, 1), (0, 0, 1)):
            greet(self.at(*flips))
        below, above = self.t > 0, self.t < self.n_line - 1

        @pl.when(below)
        def _():
            greet(self.down())

        @pl.when(above)
        def _():
            greet(self.up())

        pl.semaphore_wait(barrier, 3 + below.astype(jnp.int32) + above.astype(jnp.int32))


class Fetch:
    def __init__(self, pairs, sems):
        self.copies = [
            pltpu.make_async_copy(src, dst, sems.at[i]) for i, (src, dst) in enumerate(pairs)
        ]

    def start(self, *which):
        for i in which:
            self.copies[i].start()

    def wait(self, *which):
        for i in which:
            self.copies[i].wait()


def vmem_like(array):
    return pltpu.VMEM(array.shape, array.dtype)


class Kept:
    def __init__(self, src, dst, held, sems):
        self.there = pltpu.make_async_copy(src, held, sems.at[0])
        self.back = pltpu.make_async_copy(held, dst, sems.at[1])

    def begin(self):
        self.there.start()

    def turn(self):
        self.there.wait()
        self.back.start()

    def finish(self):
        self.back.wait()


class GatherPlane:
    def __init__(self, place, src, dst, send, recv, local, held):
        self.p, self.src, self.dst = place, src, dst
        self.rows = src.shape[0]
        self.send, self.recv = send, recv
        self.keep = Kept(src, self.block(0, 0), held, local)

    def block(self, fx, fy, fc=0, part=None):
        first = self.p.chip(fx, fy, fc) * self.rows
        size = self.rows
        if part is not None:
            size = self.rows // 2
            first = first + part * size
        return self.dst.at[pl.ds(pl.multiple_of(first, 16), size)]

    def copy(self, i, src, dst, device):
        return remote(src, dst, self.send.at[i], self.recv.at[i], device)

    def outgoing(self, i):
        at, block = self.p.at, self.block
        if i == 0:
            return self.copy(0, self.src, block(0, 0), at(1, 0))
        if i == 1:
            return self.copy(1, self.src, block(0, 0), at(0, 1))
        if i == 2:
            return self.copy(2, self.src, block(0, 0), at(0, 0, 1))
        if i == 3:
            return self.copy(3, block(1, 0, 0, 0), block(1, 0, 0, 0), at(0, 1))
        if i == 4:
            return self.copy(4, block(0, 1, 0, 1), block(0, 1, 0, 1), at(1, 0))
        spot = ((1, 0), (0, 1), (1, 1, 0, 0), (1, 1, 0, 1))[i - 5]
        return self.copy(i, block(*spot), block(*spot), at(0, 0, 1))

    def arrive(self, i):
        spot = (
            (1, 0),
            (0, 1),
            (0, 0, 1),
            (1, 1, 0, 0),
            (1, 1, 0, 1),
            (1, 0, 1),
            (0, 1, 1),
            (1, 1, 1, 0),
            (1, 1, 1, 1),
        )[i]
        here = self.block(*spot)
        self.copy(i, here, here, self.p.at(0, 0, 1)).wait_recv()

    def begin(self):
        for i in (0, 1, 2):
            self.outgoing(i).start()
        self.keep.begin()

    def forward(self):
        self.keep.turn()
        self.arrive(0)
        self.outgoing(3).start()
        self.arrive(1)
        self.outgoing(4).start()
        self.outgoing(5).start()
        self.outgoing(6).start()

    def share(self):
        self.arrive(3)
        self.outgoing(7).start()
        self.arrive(4)
        self.outgoing(8).start()

    def finish(self):
        for i in (2, 5, 6, 7, 8):
            self.arrive(i)
        for i in range(9):
            self.outgoing(i).wait_send()
        self.keep.finish()


class GatherLine:
    def __init__(self, place, dst, rows, begin, span, send, recv):
        self.p, self.dst, self.rows = place, dst, rows
        self.begin, self.span = begin, span
        self.send, self.recv = send, recv
        self.last = place.n_line - 1

    def block(self, owner):
        first = owner * self.rows + self.begin
        return self.dst.at[pl.ds(pl.multiple_of(first, 8), self.span)]

    def copy(self, way, k, owner, source=None):
        to = self.p.up() if way == 0 else self.p.down()
        block = self.block(owner)
        return remote(
            block if source is None else source,
            block,
            self.send.at[way, k],
            self.recv.at[way, k],
            to,
        )

    def step(self, k, source=None):
        t, last = self.p.t, self.last
        if k > 0:
            self.arrive(k - 1)

        @pl.when((t < last) & (t >= k))
        def _():
            self.copy(0, k, t - k, source).start()

        @pl.when((t > 0) & (t + k <= last))
        def _():
            self.copy(1, k, t + k, source).start()

    def arrive(self, k):
        t, last = self.p.t, self.last

        @pl.when(t >= k + 1)
        def _():
            self.copy(0, k, t - 1 - k).wait_recv()

        @pl.when(t + k + 1 <= last)
        def _():
            self.copy(1, k, t + 1 + k).wait_recv()

    def finish(self):
        t, last = self.p.t, self.last
        self.arrive(last - 1)
        for k in range(last):

            @pl.when((t < last) & (t >= k))
            def _():
                self.copy(0, k, t - k).wait_send()

            @pl.when((t > 0) & (t + k <= last))
            def _():
                self.copy(1, k, t + k).wait_send()


class ReduceLine:
    def __init__(self, place, terms, rows, begin, span, inbox, send, recv):
        self.p, self.terms, self.rows = place, terms, rows
        self.begin, self.span = begin, span
        self.inbox = inbox
        self.send, self.recv = send, recv
        self.last = place.n_line - 1

    def own(self, owner):
        first = owner * self.rows + self.begin
        return self.terms.at[pl.ds(pl.multiple_of(first, 16), self.span)]

    def copy(self, way, j, source):
        to = self.p.up() if way == 0 else self.p.down()
        return remote(
            source, self.inbox.at[way, j], self.send.at[way, j], self.recv.at[way, j], to
        )

    def ends(self):
        t, last = self.p.t, self.last

        @pl.when(t == 0)
        def _():
            for j in range(last):
                self.copy(0, j, self.own(last - j)).start()

        @pl.when(t == last)
        def _():
            for j in range(last):
                self.copy(1, j, self.own(j)).start()

    def sent(self):
        t, last = self.p.t, self.last

        @pl.when(t == 0)
        def _():
            for j in range(last):
                self.copy(0, j, self.own(last - j)).wait_send()

        @pl.when(t == last)
        def _():
            for j in range(last):
                self.copy(1, j, self.own(j)).wait_send()

    def hand_on(self, way, j):
        term = self.own(self.last - j if way == 0 else j)
        self.copy(way, j, term).wait_recv()
        self.inbox[way, j] = term[...] + self.inbox[way, j]
        self.copy(way, j, self.inbox.at[way, j]).start()

    def hop(self, k):
        t, last = self.p.t, self.last

        @pl.when(t == k + 1)
        def _():
            for j in range(last - 1 - k):
                self.hand_on(0, j)

        @pl.when(t == last - 1 - k)
        def _():
            for j in range(last - 1 - k):
                self.hand_on(1, j)

    def total(self, result):
        t, last = self.p.t, self.last
        result[...] = self.own(t)[...].astype(jnp.float32)

        @pl.when(t > 0)
        def _():
            j = last - t
            self.copy(0, j, self.inbox.at[0, 0]).wait_recv()
            result[...] += self.inbox[0, j].astype(jnp.float32)

        @pl.when(t < last)
        def _():
            self.copy(1, t, self.inbox.at[0, 0]).wait_recv()
            result[...] += self.inbox[1, t].astype(jnp.float32)

    def finish(self):
        t, last = self.p.t, self.last
        for j in range(last - 1):

            @pl.when((t > 0) & (t < last - j))
            def _():
                self.copy(0, j, self.inbox.at[0, j]).wait_send()

            @pl.when((t < last) & (t > j))
            def _():
                self.copy(1, j, self.inbox.at[1, j]).wait_send()


def add_rows(into, other, result=None):
    result = into if result is None else result

    def tile(i, carry):
        rows = pl.ds(pl.multiple_of(i * 16, 16), 16)
        result[rows] = into[rows] + other[rows]
        return carry

    lax.fori_loop(0, into.shape[0] // 16, tile, None)


class ReducePlane:
    chips = ((0, 0), (1, 0), (0, 1), (1, 1))

    def __init__(self, place, terms, scratch):
        self.p, self.terms = place, terms
        self.held, self.near, self.along, self.last, self.send, self.recv, self.local = scratch
        self.rows = self.held.shape[1]
        self.half = self.rows // 2

    @staticmethod
    def scratch(rows, width):
        return [
            pltpu.VMEM((4, rows, width), jnp.bfloat16),
            pltpu.VMEM((4, rows, width), jnp.bfloat16),
            pltpu.VMEM((4, rows // 2, width), jnp.bfloat16),
            pltpu.VMEM((2, rows // 2, width), jnp.bfloat16),
            pltpu.SemaphoreType.DMA((10,)),
            pltpu.SemaphoreType.DMA((10,)),
            pltpu.SemaphoreType.DMA((4,)),
        ]

    def block(self, k, other):
        first = self.p.chip(*self.chips[k], other) * self.rows
        return self.terms.at[pl.ds(pl.multiple_of(first, 16), self.rows)]

    def half_of(self, k, part):
        return self.held.at[k, pl.ds(part * self.half, self.half)]

    def load(self, k):
        return pltpu.make_async_copy(self.block(k, 0), self.held.at[k], self.local.at[k])

    def copy(self, i):
        at = self.p.at
        if i < 4:
            src, dst, to = self.block(i, 1), self.near.at[i], at(0, 0, 1)
        elif i < 8:
            src, to = (
                (self.half_of(1, 0), at(1, 0)),
                (self.half_of(3, 0), at(1, 0)),
                (self.half_of(2, 1), at(0, 1)),
                (self.half_of(3, 1), at(0, 1)),
            )[i - 4]
            dst = self.along.at[i - 4]
        else:
            src, to = ((self.half_of(2, 0), at(0, 1)), (self.half_of(1, 1), at(1, 0)))[i - 8]
            dst = self.last.at[i - 8]
        return remote(src, dst, self.send.at[i], self.recv.at[i], to)

    def begin(self):
        for k in (3, 1, 2, 0):
            self.copy(k).start()
            self.load(k).start()

    def cores(self):
        for k in (3, 1, 2, 0):
            self.load(k).wait()
            self.copy(k).wait_recv()
            add_rows(self.held.at[k], self.near.at[k])
            if k == 3:
                self.copy(5).start()
                self.copy(7).start()
            elif k == 1:
                self.copy(4).start()
            elif k == 2:
                self.copy(6).start()

    def turn(self):
        self.copy(5).wait_recv()
        add_rows(self.half_of(2, 0), self.along.at[1])
        self.copy(8).start()
        self.copy(7).wait_recv()
        add_rows(self.half_of(1, 1), self.along.at[3])
        self.copy(9).start()
        self.copy(4).wait_recv()
        add_rows(self.half_of(0, 0), self.along.at[0])
        self.copy(6).wait_recv()
        add_rows(self.half_of(0, 1), self.along.at[2])

    def finish(self, result):
        for part in (0, 1):
            self.copy(8 + part).wait_recv()
            rows = pl.ds(part * self.half, self.half)
            add_rows(self.half_of(0, part), self.last.at[part], result.at[rows])
        for i in range(10):
            self.copy(i).wait_send()


def dma_sems(*dims):
    return pltpu.SemaphoreType.DMA(dims)


def in_vmem():
    return pl.BlockSpec(memory_space=pltpu.VMEM)


def in_any():
    return pl.BlockSpec(memory_space=pl.ANY)


def comm_params(number):
    return pltpu.CompilerParams(
        collective_id=number, has_side_effects=True, vmem_limit_bytes=VMEM_BYTES
    )


def shaped(dims, kind):
    return jax.ShapeDtypeStruct(dims, kind)


def first_gather(n_dp, n_line, mats, rows_in, order):
    count = len(mats)
    parts = 2

    def kernel(*refs):
        srcs, (c, e) = refs[:count], refs[count : count + 2]
        dsts, (c_out, e_out) = refs[count + 2 : 2 * count + 2], refs[2 * count + 2 : 2 * count + 4]
        ps, pr, pl_sem, ls, lr, ll = refs[2 * count + 4 : 2 * count + 10]
        held = refs[2 * count + 10 :]
        place = Place(n_dp, n_line)
        place.meet()
        planes = [
            GatherPlane(place, a, b, ps.at[i], pr.at[i], pl_sem.at[i], held[i])
            for i, (a, b) in enumerate(zip(srcs, dsts))
        ]
        rows = c.shape[0]
        span = rows // parts
        lines = [
            GatherLine(place, c_out, rows, i * span, span, ls.at[i], lr.at[i])
            for i in range(parts)
        ]
        lines.append(
            GatherLine(place, e_out, e.shape[0], 0, e.shape[0], ls.at[parts], lr.at[parts])
        )
        for i in range(parts):
            lines[i].step(0, c.at[pl.ds(i * span, span)])
        lines[parts].step(0, e)
        early, late = planes[: count // 2], planes[count // 2 :]
        for part in early:
            part.begin()
        copies = []
        for i, (src, dst) in enumerate(((c, c_out), (e, e_out))):
            own = dst.at[pl.ds(pl.multiple_of(place.t * src.shape[0], 8), src.shape[0])]
            copies.append(Kept(src, own, held[count + i], ll.at[i]))
            copies[i].begin()
        for line in lines:
            line.step(1)
        for part in late:
            part.begin()
        for part in early:
            part.forward()
        for copy in copies:
            copy.turn()
        for line in lines:
            line.step(2)
        for part in early:
            part.share()
        for part in late:
            part.forward()
        for part in late:
            part.share()
        for part in lines + planes:
            part.finish()
        for copy in copies:
            copy.finish()

    return pl.pallas_call(
        kernel,
        out_shape=tuple(shaped((n_dp * m.shape[0], m.shape[1]), m.dtype) for m in mats)
        + (
            shaped((n_line * rows_in.shape[0], rows_in.shape[1]), rows_in.dtype),
            shaped((n_line * order.shape[0], order.shape[1]), order.dtype),
        ),
        in_specs=[in_any()] * (count + 2),
        out_specs=[in_any()] * (count + 2),
        scratch_shapes=[
            dma_sems(count, 9),
            dma_sems(count, 9),
            dma_sems(count, 2),
            dma_sems(parts + 1, 2, n_line - 1),
            dma_sems(parts + 1, 2, n_line - 1),
            dma_sems(2, 2),
        ]
        + [vmem_like(m) for m in (*mats, rows_in, order)],
        compiler_params=comm_params(1),
        name="first_gather",
    )(*mats, rows_in, order)


CHUNKS = 8
LAST_CHUNKS = 8


def line_scratch(n_line, span, width, chunks):
    hops = n_line - 1
    return [
        pltpu.VMEM((chunks, 2, hops, span, width), jnp.bfloat16),
        dma_sems(chunks, 2, hops),
        dma_sems(chunks, 2, hops),
        dma_sems(chunks, 2, hops),
        dma_sems(chunks, 2, hops),
        pltpu.VMEM((span, width), jnp.float32),
    ]


def sum_rows_and_spread(place, terms, scratch, finish_rows, spread, between):
    inbox, rs, rr, gs, gr, total = scratch
    span = total.shape[0]
    count = inbox.shape[0]
    rows = span * count
    hops = place.n_line - 1
    sums = [
        ReduceLine(place, terms, rows, c * span, span, inbox.at[c], rs.at[c], rr.at[c])
        for c in range(count)
    ]
    gathers = []
    if spread is not None:
        gathers = [
            GatherLine(place, spread, rows, c * span, span, gs.at[c], gr.at[c])
            for c in range(count)
        ]
    sums[0].ends()

    def total_of(c):
        sums[c].total(total)
        finish_rows(c, pl.ds(c * span, span), total)
        if gathers:
            gathers[c].step(0)

    stages = [lambda c, k=k: sums[c].hop(k) for k in range(hops - 1)] + [total_of]
    lags = [LAGS[min(k, len(LAGS) - 1)] for k in range(hops)]
    if gathers:
        stages += [lambda c, k=k: gathers[c].step(k) for k in range(1, hops)]
        lags += [lags[-1] + LAG_STEP * k for k in range(1, hops)]
    for i in range(count + lags[-1]):
        if i < count:
            sums[i].sent()
        if i + 1 < count:
            sums[i + 1].ends()
        for work, lag in zip(stages, lags):
            if 0 <= i - lag < count:
                work(i - lag)
        if i in between:
            between[i]()
    for part in gathers + sums:
        part.finish()


LAGS = (0, 1, 1)
LAG_STEP = 1


def middle_gather(n_dp, n_line, terms, tokens, gain, mats):
    rows, width = tokens.shape
    count = len(mats)

    def kernel(*refs):
        s, tok, gain_ref = refs[:3]
        srcs = refs[3 : 3 + count]
        after, hidden = refs[3 + count : 5 + count]
        dsts = refs[5 + count : 5 + 2 * count]
        ps, pr, pl_sem = refs[5 + 2 * count : 8 + 2 * count]
        held = refs[8 + 2 * count : 8 + 3 * count]
        scratch = refs[8 + 3 * count :]
        place = Place(n_dp, n_line)
        place.meet()
        planes = [
            GatherPlane(place, a, b, ps.at[i], pr.at[i], pl_sem.at[i], held[i])
            for i, (a, b) in enumerate(zip(srcs, dsts))
        ]
        planes[0].begin()

        def norm(c, here, total):
            values = tok[here].astype(jnp.float32) + total[...]
            after[here] = values
            low = rms_scale(values, gain_ref[...]).astype(jnp.bfloat16)
            first = pl.multiple_of(place.t * rows, 16) + c * total.shape[0]
            hidden[pl.ds(pl.multiple_of(first, 16), total.shape[0])] = low

        between = {7: planes[0].forward, 10: planes[0].share}
        sum_rows_and_spread(place, s, scratch, norm, hidden, between)
        for part in planes:
            part.finish()

    return pl.pallas_call(
        kernel,
        out_shape=(
            shaped((rows, width), jnp.float32),
            shaped((n_line * rows, width), jnp.bfloat16),
        )
        + tuple(shaped((n_dp * m.shape[0], m.shape[1]), m.dtype) for m in mats),
        in_specs=[in_vmem()] * 3 + [in_any()] * count,
        out_specs=[in_vmem()] * 2 + [in_any()] * count,
        scratch_shapes=[dma_sems(count, 9), dma_sems(count, 9), dma_sems(count, 2)]
        + [vmem_like(m) for m in mats]
        + line_scratch(n_line, rows // CHUNKS, width, CHUNKS),
        compiler_params=comm_params(2),
        name="middle_gather",
    )(terms, tokens, gain, *mats)


def middle_sums(n_dp, n_line, terms, after, gain, grad_in, mat, hidden, grad_up, product, down):
    rows, width = after.shape
    block = mat.shape[0] // n_dp
    wide = grad_up.shape[1]
    spread_rows = n_line * rows

    def kernel(*refs):
        s, after_ref, gain_ref, g_ref, src = refs[:5]
        hid_far, gu_far, pr_far, dw_far = refs[5:9]
        grad_after, gain_sum, spread, result, up_far, feed_far = refs[9:15]
        hid, gu, pr, dw, up_out, feed, sems = refs[15:22]
        rest = refs[22:]
        fetch = Fetch(
            [
                (hid_far, hid),
                (gu_far, gu),
                (pr_far, pr),
                (dw_far, dw),
                (feed, feed_far),
                (up_out.at[0], up_far.at[pl.ds(0, width // 2)]),
                (up_out.at[1], up_far.at[pl.ds(width // 2, width // 2)]),
            ],
            sems,
        )
        place = Place(n_dp, n_line)
        place.meet()
        plane = ReducePlane(place, src, rest[:7])
        scratch = rest[7:]
        plane.begin()
        fetch.start(0, 1, 2, 3)
        gain_sum[...] = jnp.zeros_like(gain_sum)

        def norm(c, here, total):
            grad = total[...]
            grad_rows, normed = norm_back(after_ref[here], gain_ref[...], grad)
            gain_sum[...] += jnp.sum(grad * normed, axis=0, keepdims=True)
            both = g_ref[here].astype(jnp.float32) + grad_rows
            grad_after[here] = both
            first = pl.multiple_of(place.t * rows, 16) + c * total.shape[0]
            spread[pl.ds(pl.multiple_of(first, 16), total.shape[0])] = both.astype(jnp.bfloat16)

        def feed_part(i):
            cols = pl.ds(i * (width // 4), width // 4)
            feed[:, cols] = times_trans(pr[...], dw[cols]).astype(jnp.bfloat16)

        def up_part(i):
            cols = pl.ds(i * (width // 4), width // 4)
            here = pl.ds((i % 2) * (width // 4), width // 4)
            up_out[i // 2, here] = trans_times(hid[:, cols], gu[...]).astype(jnp.bfloat16)

        def early():
            fetch.wait(0, 1)

        def two():
            up_part(0)

        def three():
            up_part(1)
            fetch.start(5)

        def four():
            up_part(2)

        def five():
            up_part(3)
            fetch.start(6)
            fetch.wait(2, 3)

        def six():
            feed_part(0)

        def seven():
            plane.turn()
            feed_part(1)

        def eight():
            feed_part(2)

        def nine():
            feed_part(3)
            fetch.start(4)

        steps = {0: plane.cores, 1: early, 2: two, 3: three, 4: four, 5: five, 6: six, 7: seven, 8: eight, 9: nine}
        sum_rows_and_spread(place, s, scratch, norm, spread, steps)
        plane.finish(result)
        fetch.wait(4, 5, 6)

    low, full = jnp.bfloat16, jnp.float32
    near, far = in_vmem(), in_any()
    return pl.pallas_call(
        kernel,
        out_shape=(
            shaped((rows, width), full),
            shaped((1, width), full),
            shaped((spread_rows, width), low),
            shaped((block, mat.shape[1]), low),
            shaped((width, wide), low),
            shaped((spread_rows, width), low),
        ),
        in_specs=[near] * 4 + [far] * 5,
        out_specs=[near] * 4 + [far] * 2,
        scratch_shapes=[vmem_like(m) for m in (hidden, grad_up, product, down)]
        + [
            pltpu.VMEM((2, width // 2, wide), low),
            pltpu.VMEM((spread_rows, width), low),
            dma_sems(7),
        ]
        + ReducePlane.scratch(block, mat.shape[1])
        + line_scratch(n_line, rows // CHUNKS, width, CHUNKS),
        compiler_params=comm_params(3),
        name="middle_sums",
    )(terms, after, gain, grad_in, mat, hidden, grad_up, product, down)


class Exchange:
    def __init__(self, place, axis, src, slots, send, recv, local):
        self.p, self.src, self.slots = place, src, slots
        self.over_dp = axis == "dp"
        self.size = place.n_dp if self.over_dp else place.n_line
        self.me = place.d if self.over_dp else place.t
        self.send, self.recv, self.local = send, recv, local

    def copy(self, i):
        to = lax.rem(self.me + i, self.size)
        device = (to, self.p.t) if self.over_dp else (self.p.d, to)
        return remote(
            self.src, self.slots.at[self.me], self.send.at[i - 1], self.recv.at[i - 1], device
        )

    def mine(self):
        return pltpu.make_async_copy(self.src, self.slots.at[self.me], self.local)

    def begin(self):
        for i in range(1, self.size):
            self.copy(i).start()
        self.mine().start()

    def wait(self):
        self.mine().wait()
        for i in range(1, self.size):
            self.copy(i).wait()

    def finish(self):
        self.wait()
        total = self.slots[0]
        for i in range(1, self.size):
            total = total + self.slots[i]
        return total


def last_sums(n_dp, n_line, terms, tokens, gain, grad_after, second, small, mats):
    rows, width = tokens.shape
    count = len(mats)
    per = len(ReducePlane.scratch(16, 128))

    def kernel(*refs):
        s, tok, gain_ref, g_ref, second_ref, small_ref = refs[:6]
        srcs = refs[6 : 6 + count]
        grad_tok, small_out, first_out = refs[6 + count : 9 + count]
        results = refs[9 + count : 9 + 2 * count]
        rest = refs[9 + 2 * count :]
        own_first, row_sum = rest[count * per : count * per + 2]
        slots_a, slots_b, slots_c, slots_d = rest[count * per + 2 : count * per + 6]
        xs, xr, xl = rest[count * per + 6 : count * per + 9]
        scratch = rest[count * per + 9 :]
        place = Place(n_dp, n_line)
        place.meet(True)
        planes = [
            ReducePlane(place, srcs[i], rest[i * per : (i + 1) * per]) for i in range(count)
        ]
        for part in planes:
            part.begin()
        early = Exchange(place, "dp", small_ref, slots_a, xs.at[0], xr.at[0], xl.at[0])
        early.begin()
        gain = Exchange(place, "dp", second_ref, slots_d, xs.at[3], xr.at[3], xl.at[3])
        gain.begin()
        own_first[...] = jnp.zeros_like(own_first)

        def norm(c, here, total):
            grad = total[...]
            grad_rows, normed = norm_back(tok[here].astype(jnp.float32), gain_ref[...], grad)
            own_first[...] += jnp.sum(grad * normed, axis=0, keepdims=True)
            grad_tok[here] = g_ref[here] + grad_rows

        def cores():
            for part in planes:
                part.cores()

        def turn():
            for part in planes:
                part.turn()

        sum_rows_and_spread(place, s, scratch, norm, None, {0: cores, 5: turn})
        first = Exchange(place, "dp", own_first, slots_b, xs.at[1], xr.at[1], xl.at[1])
        first.begin()
        small_out[...] = early.finish()
        row_sum[0:1] = gain.finish()
        row_sum[1:2] = first.finish()
        both = Exchange(place, "tensor", row_sum, slots_c, xs.at[2], xr.at[2], xl.at[2])
        both.begin()
        for part, result in zip(planes, results):
            part.finish(result)
        first_out[...] = both.finish()

    return pl.pallas_call(
        kernel,
        out_shape=(
            shaped((rows, width), jnp.float32),
            shaped(small.shape, jnp.float32),
            shaped((2, width), jnp.float32),
        )
        + tuple(shaped((m.shape[0] // n_dp, m.shape[1]), jnp.bfloat16) for m in mats),
        in_specs=[in_vmem()] * 6 + [in_any()] * count,
        out_specs=[in_vmem()] * (3 + count),
        scratch_shapes=sum([ReducePlane.scratch(m.shape[0] // n_dp, m.shape[1]) for m in mats], [])
        + [
            pltpu.VMEM((1, width), jnp.float32),
            pltpu.VMEM((2, width), jnp.float32),
            pltpu.VMEM((n_dp,) + small.shape, jnp.float32),
            pltpu.VMEM((n_dp, 1, width), jnp.float32),
            pltpu.VMEM((n_line, 2, width), jnp.float32),
            pltpu.VMEM((n_dp, 1, width), jnp.float32),
            dma_sems(4, n_dp),
            dma_sems(4, n_dp),
            dma_sems(4),
        ]
        + line_scratch(n_line, rows // LAST_CHUNKS, width, LAST_CHUNKS),
        compiler_params=comm_params(4),
        name="last_sums",
    )(terms, tokens, gain, grad_after, second, small, *mats)


def loop(count, body, unroll=1):
    def step(i, carry):
        body(i)
        return carry

    lax.fori_loop(0, count, step, None, unroll=unroll)


def tile_rows(i, size, ahead=0):
    return pl.ds(pl.multiple_of(i * size + ahead, 8), size)


def moved_up(values, distance, count):
    size = values.shape[0]
    return pltpu.roll(values, (size - distance) % size, 0)[:count]


def take_lanes(ref, here):
    return jnp.concatenate([ref[c, here] for c in range(ref.shape[0])], axis=1)


def put_lanes(ref, here, values):
    for c in range(ref.shape[0]):
        ref[c, here] = values[:, c * LANES : (c + 1) * LANES]


def gelu_parts(values):
    inner = GELU_C * (values + 0.044715 * (values * values * values))
    tanh = jnp.tanh(inner)
    half = 0.5 * (1.0 + tanh)
    slope = half + 0.5 * values * (1.0 - tanh * tanh) * GELU_C * (
        1.0 + 3.0 * 0.044715 * (values * values)
    )
    return values * half, slope


GELU_C = 0.7978845608028654
RIM = 128
LANES = 128
TILE = 16


def one_minus_exp(values, exponential):
    series = jnp.ones_like(values)
    for term in range(9, 1, -1):
        series = 1.0 + values * (1.0 / term) * series
    return jnp.where(values > -0.35, -values * series, 1.0 - exponential)


def rate_and_scale(pre_recur, soft, start):
    sr = jax.nn.sigmoid(pre_recur)
    log_rate = -rate_scale * sr * soft
    decay = jnp.exp(log_rate)
    rate = jnp.where(start, 0.0, decay)
    scale = jnp.where(start, 1.0, jnp.sqrt(one_minus_exp(2.0 * log_rate, decay * decay)))
    return sr, rate, scale


class RimSwap:
    def __init__(self, place, own):
        self.odd = lax.rem(place.t, 2)
        self.partner = (place.d, place.t + 1 - 2 * self.odd)
        self.first = pl.multiple_of(RIM - RIM * self.odd, RIM)
        self.edge = pl.ds(pl.multiple_of((1 - self.odd) * own + self.odd * RIM, RIM), RIM)
        self.over_there = pl.ds(pl.multiple_of(self.odd * (own + RIM), RIM), RIM)
        self.beyond = pl.ds(pl.multiple_of((1 - self.odd) * (own + RIM), RIM), RIM)

    def block(self, index, size):
        return pl.ds(pl.multiple_of(self.first + index * size, RIM), size)


LATE_SHARE = 4


def recur_forward(
    n_dp,
    n_line,
    tok_all,
    cot,
    to_place,
    to_stored,
    x_full,
    y_full,
    out_full,
    gain,
    gates,
    taps,
    soft,
    flags,
):
    rows, width = tok_all.shape
    count, own = taps.shape
    size = gates.shape[0]
    wide = own + 2 * RIM
    blocks = (wide - RIM) // size
    chunk = rows // 8
    cot_rows = cot.shape[0] - cot.shape[0] // LATE_SHARE
    parts = 1

    def kernel(*refs):
        (tok_far, cot_ref, plc, sto, wx_far, wy_far, wo_far, gain_ref, gates_in, cw, sp, fl) = refs[:12]
        far, gw, cot_all = refs[12:23], refs[23], refs[24]
        tok, wx, wy, wo = refs[25:29]
        results = refs[29:40]
        hp, xext, y, conv_low, conv, pre_r, pre_i, rate, state, merged_st, terms = results
        (h, xf, local, cum, merged, agg, slots, hs, hr, es, er, el, gs, gr, gl) = refs[40:55]
        in_sems, out_sems, cot_held = refs[55:]
        fetch = Fetch(((tok_far, tok), (wx_far, wx), (wy_far, wy), (wo_far, wo)), in_sems)
        store = Fetch(zip(results, far), out_sems)
        fetch.start(0, 1)
        place = Place(n_dp, n_line)
        place.meet(True)
        swap = RimSwap(place, own)
        for side in range(2):
            first = side * wide
            gw[:, first : first + RIM] = jnp.zeros((size, RIM), jnp.bfloat16)
            gw[:, first + RIM : first + RIM + own] = gates_in[:, side * own : (side + 1) * own]
            gw[:, first + RIM + own : first + wide] = jnp.zeros((size, RIM), jnp.bfloat16)
        own_cot = cot_all.at[pl.ds(pl.multiple_of(place.t * cot_rows, 16), cot_rows)]
        cot_ref = cot_ref.at[pl.ds(0, cot_rows)]
        keep = Kept(cot_ref, own_cot, cot_held, gl)
        keep.begin()
        span = cot_rows // parts
        lines = [
            GatherLine(place, cot_all, cot_rows, c * span, span, gs.at[c], gr.at[c])
            for c in range(parts)
        ]
        for c, line in enumerate(lines):
            line.step(0, cot_ref.at[pl.ds(c * span, span)])
        fetch.start(2, 3)

        def norm(i):
            here = tile_rows(i, TILE)
            h[here] = rms_scale(tok[here].astype(jnp.float32), gain_ref[...]).astype(jnp.bfloat16)

        fetch.wait(0)
        loop(rows // TILE, norm)
        fetch.wait(1)

        def project(i):
            here = tile_rows(i, 128)
            hp[here] = plain_dot(plc[here], h[...]).astype(jnp.bfloat16)
            xext[tile_rows(i, 128, 16)] = plain_dot(hp[here], wx[...]).astype(jnp.bfloat16)

        loop(rows // 128, project)
        store.start(0)
        edge = remote(
            xext.at[pl.ds(rows, 16)],
            xext.at[pl.ds(0, 16)],
            hs.at[0],
            hr.at[0],
            (lax.rem(place.d + 1, n_dp), place.t),
        )
        edge.start()
        keep.turn()
        for line in lines:
            line.step(1)

        def project_y(i):
            here = tile_rows(i, 128)
            y[here] = plain_dot(hp[here], wy[...])

        fetch.wait(2)
        loop(rows // 128, project_y)
        store.start(2)
        edge.wait()
        top = xext[pl.ds(0, 16)]
        xext[pl.ds(0, 16)] = jnp.where(place.d > 0, top, jnp.zeros_like(top))
        store.start(1)

        def widen(i):
            xf[tile_rows(i, TILE)] = xext[tile_rows(i, TILE)].astype(jnp.float32)

        loop(rows // TILE + 1, widen)

        def convolve(i):
            here = tile_rows(i, TILE)
            near = xf[pl.ds(pl.multiple_of(i * TILE + 8, 8), TILE + 8)]
            same = fl[tile_rows(i, TILE, 8)]
            total = cw[0:1] * near[8:]
            for k in range(1, count):
                total += cw[k : k + 1] * moved_up(near, 8 - k, TILE) * same[:, k : k + 1]
            conv[here] = total
            conv_low[here, RIM : RIM + own] = total.astype(jnp.bfloat16)

        loop(rows // TILE, convolve)
        store.start(4)
        rim = remote(
            conv_low.at[:, swap.edge],
            conv_low.at[:, swap.over_there],
            hs.at[1],
            hr.at[1],
            swap.partner,
        )
        rim.start()
        for i in range(blocks):
            index = lax.rem(i + swap.odd, blocks)
            cols = swap.block(index, size)
            other = pl.ds(pl.multiple_of(wide + swap.first + index * size, RIM), size)
            if i == blocks - 1:
                rim.wait()
            pre_r[:, cols] = plain_dot(conv_low[:, cols], gw[:, cols])
            pre_i[:, cols] = plain_dot(conv_low[:, cols], gw[:, other])

        store.start(3, 5, 6)

        def drive(i):
            here = tile_rows(i, TILE)
            start = fl[tile_rows(i, TILE, 8)][:, 0:1] > 0.0
            own_cols = pl.ds(RIM, own)
            _, decay, scale = rate_and_scale(pre_r[here, own_cols], sp[...], start)
            put_lanes(rate, here, decay)
            put_lanes(local, here, conv[here] * jax.nn.sigmoid(pre_i[here, own_cols]) * scale)

        loop(rows // TILE, drive)
        store.start(7)
        for line in lines:
            line.step(2)
        groups = own // LANES

        def scan(i, carry):
            here = pl.ds(i, 8, chunk)
            result = []
            for c in range(groups):
                product, total = carry[c]
                r = rate[c, here]
                product = product * r
                total = total * r + local[c, here]
                cum[c, here] = product
                local[c, here] = total
                result.append((product, total))
            return tuple(result)

        blank = (jnp.ones((8, LANES), jnp.float32), jnp.zeros((8, LANES), jnp.float32))
        lax.fori_loop(0, chunk, scan, (blank,) * groups)
        product, total = jnp.ones((1, own), jnp.float32), jnp.zeros((1, own), jnp.float32)
        for j in range(8):
            last = pl.ds(j * chunk + chunk - 1, 1)
            total = take_lanes(local, last) + take_lanes(cum, last) * total
            product = product * take_lanes(cum, last)
        agg[0:1] = product
        agg[1:2] = total
        swap_all = Exchange(place, "dp", agg, slots, es, er, el)
        swap_all.begin()
        swap_all.wait()
        entry = jnp.zeros((1, own), jnp.float32)
        for q in range(n_dp):
            longer = slots[q, 1:2] + slots[q, 0:1] * entry
            entry = jnp.where(q < place.d, longer, entry)
        state[pl.ds(0, 8)] = jnp.broadcast_to(entry, (8, own))
        for j in range(8):

            def settle(i, entry=entry):
                here = tile_rows(i, TILE, j * chunk)
                values = take_lanes(local, here) + take_lanes(cum, here) * entry
                state[tile_rows(i, TILE, j * chunk + 8)] = values
                merged[here] = (values * gelu_parts(y[here])[0]).astype(jnp.bfloat16)

            loop(chunk // TILE, settle)
            last = pl.ds(j * chunk + chunk - 1, 1)
            entry = take_lanes(local, last) + take_lanes(cum, last) * entry
        store.start(8)
        merged_st[...] = plain_dot(sto[...], merged[...]).astype(jnp.bfloat16)

        store.start(9)
        fetch.wait(3)

        def mix(i):
            some = tile_rows(i, 512)
            terms[:, pl.ds(pl.multiple_of(i * 512, 512), 512)] = times_trans(
                merged_st[...], wo[some, :]
            ).astype(jnp.bfloat16)

        loop(width // 512, mix)
        for line in lines:
            line.finish()
        keep.finish()
        store.start(10)
        store.wait(*range(11))

    low, full = jnp.bfloat16, jnp.float32
    results = (
        shaped((rows, width), low),
        shaped((rows + 16, own), low),
        shaped((rows, own), full),
        shaped((rows, wide), low),
        shaped((rows, own), full),
        shaped((rows, wide), full),
        shaped((rows, wide), full),
        shaped((own // LANES, rows, LANES), full),
        shaped((rows + 8, own), full),
        shaped((rows, own), low),
        shaped((rows, width), low),
    )
    near, far = in_vmem(), in_any()
    return pl.pallas_call(
        kernel,
        out_shape=results
        + (shaped((size, 2 * wide), low), shaped((n_line * cot_rows, width), low)),
        in_specs=[far, far, near, near, far, far, far] + [near] * 5,
        out_specs=[far] * 11 + [near, far],
        scratch_shapes=[vmem_like(m) for m in (tok_all, x_full, y_full, out_full) + results]
        + [
            pltpu.VMEM((rows, width), low),
            pltpu.VMEM((rows + 16, own), full),
            pltpu.VMEM((own // LANES, rows, LANES), full),
            pltpu.VMEM((own // LANES, rows, LANES), full),
            pltpu.VMEM((rows, own), low),
            pltpu.VMEM((2, own), full),
            pltpu.VMEM((n_dp, 2, own), full),
            dma_sems(2),
            dma_sems(2),
            dma_sems(n_dp),
            dma_sems(n_dp),
            pltpu.SemaphoreType.DMA,
            dma_sems(parts, 2, n_line - 1),
            dma_sems(parts, 2, n_line - 1),
            dma_sems(2),
            dma_sems(4),
            dma_sems(11),
            pltpu.VMEM((cot_rows, width), low),
        ],
        compiler_params=comm_params(5),
        name="recur_forward",
    )(
        tok_all,
        cot,
        to_place,
        to_stored,
        x_full,
        y_full,
        out_full,
        gain,
        gates,
        taps,
        soft,
        flags,
    )


class RowProducts:
    def __init__(self, left, right, far, stage, sems):
        self.left, self.right, self.far, self.stage, self.sems = left, right, far, stage, sems
        self.part = stage.shape[1]
        self.count = far.shape[0] // self.part

    def slot(self, i):
        return self.stage.at[i % 2, :, pl.ds(0, self.far.shape[1])]

    def copy(self, i):
        some = pl.ds(i * self.part, self.part)
        return pltpu.make_async_copy(self.slot(i), self.far.at[some], self.sems.at[i])

    def run(self):
        for i in range(self.count):
            if i >= 2:
                self.copy(i - 2).wait()
            some = pl.ds(i * self.part, self.part)
            self.slot(i)[...] = trans_times(self.left[:, some], self.right[...]).astype(
                jnp.bfloat16
            )
            self.copy(i).start()

    def finish(self):
        self.copy(self.count - 2).wait()
        self.copy(self.count - 1).wait()


def recur_backward(
    n_dp,
    n_line,
    mixer_in,
    to_place,
    to_stored,
    x_full,
    y_full,
    out_full,
    gates,
    taps,
    soft,
    slope,
    flags,
    kept,
    weight_terms,
    row_terms,
    hidden_place,
    merged_stored,
):
    rows, width = mixer_in.shape
    count, own = taps.shape
    size = gates.shape[0]
    wide = own + 2 * RIM
    blocks = (wide - RIM) // size
    chunk = rows // 8
    own_rows = rows // n_line
    parts = 4
    span = own_rows // parts

    def kernel(*refs):
        (mix_far, plc, sto, wx_far, wy_far, wo_far, gw, cw, sp, sg, fl) = refs[:11]
        kept_far, weights, feed_far, hp_far, merged_far = refs[11:19], *refs[19:23]
        (gate_grads, tap_grads, terms_far, weight_sum, row_sum) = refs[23:28]
        out_far, xy_far = refs[28:30]
        mix, wy, wo, feed, merged = refs[30:35]
        (xext, y, conv_low, conv, pre_r, pre_i, rate, state) = refs[35:43]
        (gxy, mp, gm, lam, reach, gp_r, gp_i, grad, spread, rim_out, rim_in) = refs[43:54]
        (ret_out, ret_in, tap_sums, decay_sums, ends, agg, slots) = refs[54:61]
        (hs, hr, es, er, el, in_sems, out_sems, inbox, ls, lr, total) = refs[61:72]
        stage, stage_sems = refs[72:74]
        hp, terms, wx = mix, mix, wo
        fetch = Fetch(
            [
                (mix_far, mix),
                (wo_far, wo),
                (kept_far[1], y),
                (kept_far[7], state),
                (kept_far[6], rate),
                (kept_far[4], pre_r),
                (kept_far[5], pre_i),
                (kept_far[3], conv),
                (kept_far[2], conv_low),
                (kept_far[0], xext),
                (wx_far, wx),
                (wy_far, wy),
                (feed_far, feed),
                (merged_far, merged),
                (hp_far, hp),
            ],
            in_sems,
        )
        fetch.start(12, 0, 1, 13)
        store = Fetch(((terms, terms_far),), out_sems)
        out_rows = RowProducts(mix, merged, out_far, stage, stage_sems.at[0])
        xy_rows = RowProducts(hp, gxy, xy_far, stage, stage_sems.at[1])
        place = Place(n_dp, n_line)
        place.meet(True)
        plane = ReducePlane(place, weights, refs[74:])
        plane.begin()
        lines = [
            ReduceLine(place, feed, own_rows, c * span, span, inbox.at[c], ls.at[c], lr.at[c])
            for c in range(parts)
        ]

        def send(c):
            if c > 0:
                lines[c - 1].sent()
            if c < parts:
                lines[c].ends()

        def add_up(c):
            lines[c].total(total)
            row_sum[pl.ds(c * span, span)] = total[...].astype(jnp.bfloat16)

        fetch.wait(12)
        send(0)
        fetch.start(*range(2, 10), 11)
        swap = RimSwap(place, own)
        own_cols = pl.ds(RIM, own)

        def project(i):
            here = tile_rows(i, 128)
            mp[here] = plain_dot(plc[here], mix[...]).astype(jnp.bfloat16)
            gm[here] = plain_dot(mp[here], wo[...])

        fetch.wait(0, 1)
        loop(rows // 128, project)
        fetch.start(10)
        fetch.wait(13)
        out_rows.run()
        fetch.start(14)

        def split(i):
            here = tile_rows(i, TILE)
            branch, slope_y = gelu_parts(y[here])
            grads = gm[here]
            put_lanes(lam, here, grads * branch)
            values = state[tile_rows(i, TILE, 8)]
            gxy[here, own:] = (grads * values * slope_y).astype(jnp.bfloat16)

        fetch.wait(2, 3)
        loop(rows // TILE, split)
        send(1)
        lines[0].hop(0)
        fetch.wait(4)
        groups = own // LANES

        def scan(i, carry):
            here = pl.ds(chunk - 1 - i, 8, chunk)
            result = []
            for c in range(groups):
                product, message = carry[c]
                r = rate[c, here]
                value = lam[c, here] + message
                lam[c, here] = value
                reach[c, here] = product
                result.append((product * r, value * r))
            return tuple(result)

        blank = (jnp.ones((8, LANES), jnp.float32), jnp.zeros((8, LANES), jnp.float32))
        done = lax.fori_loop(0, chunk, scan, (blank,) * groups)
        for c in range(groups):
            lanes = pl.ds(c * LANES, LANES)
            ends[0, :, lanes] = done[c][0]
            ends[1, :, lanes] = done[c][1]
        product, message = jnp.ones((1, own), jnp.float32), jnp.zeros((1, own), jnp.float32)
        for j in reversed(range(8)):
            message = ends[1, j : j + 1] + ends[0, j : j + 1] * message
            product = product * ends[0, j : j + 1]
        agg[0:1] = product
        agg[1:2] = message
        swap_all = Exchange(place, "dp", agg, slots, es, er, el)
        swap_all.begin()
        plane.cores()
        swap_all.wait()
        lines[0].hop(1)
        entry = jnp.zeros((1, own), jnp.float32)
        for q in reversed(range(n_dp)):
            longer = slots[q, 1:2] + slots[q, 0:1] * entry
            entry = jnp.where(q > place.d, longer, entry)
        fetch.wait(5, 6, 7)
        for ref in (tap_sums, decay_sums):
            ref[...] = jnp.zeros_like(ref)
        for ref in (gp_r, gp_i):
            ref[:, 0:RIM] = jnp.zeros((rows, RIM), jnp.bfloat16)
            ref[:, RIM + own :] = jnp.zeros((rows, RIM), jnp.bfloat16)
        grad[pl.ds(0, 8)] = jnp.zeros((8, own), jnp.float32)
        grad[pl.ds(rows + 8, 8)] = jnp.zeros((8, own), jnp.float32)
        for j in reversed(range(8)):

            def back(i, entry=entry):
                here = tile_rows(i, TILE, j * chunk)
                flag = fl[tile_rows(i, TILE, j * chunk + 8)]
                start = flag[:, 0:1] > 0.0
                values = take_lanes(lam, here) + take_lanes(reach, here) * entry
                before = moved_up(
                    state[pl.ds(pl.multiple_of(j * chunk + i * TILE, 8), TILE + 8)], 7, TILE
                )
                sr, decay, scale = rate_and_scale(pre_r[here, own_cols], sp[...], start)
                si = jax.nn.sigmoid(pre_i[here, own_cols])
                block = conv[here]
                driven = values * si
                log_grad = values * before * decay - block * driven * (decay * decay) / scale
                log_grad = jnp.where(start, 0.0, log_grad)
                inner = sr * log_grad
                gp_r[here, own_cols] = (
                    -rate_scale * sp[...] * inner * (1.0 - sr)
                ).astype(jnp.bfloat16)
                gp_i[here, own_cols] = (driven * block * (1.0 - si) * scale).astype(jnp.bfloat16)
                grad[tile_rows(i, TILE, j * chunk + 8)] = driven * scale
                decay_sums[...] += inner[:8] + inner[8:]

            loop(chunk // TILE, back)
            if j == 4:
                send(2)
                lines[1].hop(0)
            entry = ends[1, j : j + 1] + ends[0, j : j + 1] * entry
        lines[1].hop(1)
        add_up(0)

        for i in range(blocks):
            index = lax.rem(i + 2 - 2 * swap.odd, blocks)
            cols = swap.block(index, size)
            other = pl.ds(pl.multiple_of(wide + swap.first + index * size, RIM), size)
            spread[:, cols] = times_trans(gp_r[:, cols], gw[:, cols]) + times_trans(
                gp_i[:, cols], gw[:, other]
            )
            if i == 0:
                rim_out[...] = spread[:, swap.beyond].astype(jnp.bfloat16)
                rim = remote(rim_out, rim_in, hs.at[0], hr.at[0], swap.partner)
                rim.start()
        send(3)
        lines[2].hop(0)
        rim.wait()
        shared = pl.ds(pl.multiple_of((1 - swap.odd) * (own - RIM), RIM), RIM)

        def join(i):
            here = tile_rows(i, TILE)
            there = tile_rows(i, TILE, 8)
            grad[there] += spread[here, own_cols]
            grad[there, shared] += rim_in[here].astype(jnp.float32)

        loop(rows // TILE, join)

        near = grad[pl.ds(0, 16)]
        back_rows = jnp.zeros((8, own), jnp.float32)
        for k in range(1, count):
            masked = near * fl[pl.ds(0, 16)][:, k : k + 1]
            back_rows += cw[k : k + 1] * moved_up(masked, k, 8)
        ret_out[...] = back_rows
        ret = remote(
            ret_out,
            ret_in,
            hs.at[1],
            hr.at[1],
            (lax.rem(place.d + n_dp - 1, n_dp), place.t),
        )
        ret.start()
        fetch.wait(8)
        for i in range(blocks):
            cols = swap.block(i, size)
            spread[0:size, cols] = trans_times(conv_low[:, cols], gp_r[:, cols])
            spread[size : 2 * size, cols] = trans_times(conv_low[:, cols], gp_i[:, cols])
        gate_grads[:, 0:own] = spread[0:size, own_cols].astype(jnp.bfloat16)
        gate_grads[:, own:] = spread[size : 2 * size, own_cols].astype(jnp.bfloat16)

        def taps_back(i, added=None):
            here = tile_rows(i, TILE)
            start = pl.ds(pl.multiple_of(i * TILE + 8, 8), TILE + 8)
            after = grad[start]
            flag = fl[start]
            behind = xext[pl.ds(pl.multiple_of(i * TILE, 16), 2 * TILE)].astype(jnp.float32)
            total = cw[0:1] * after[:TILE]
            for k in range(count):
                if k > 0:
                    masked = after * flag[:, k : k + 1]
                    total += cw[k : k + 1] * moved_up(masked, k, TILE)
                    mine = masked[:TILE]
                else:
                    mine = after[:TILE]
                term = mine * moved_up(behind, 16 - k, TILE)
                tap_sums[k] += term[:8] + term[8:]
            if added is not None:
                total = total + jnp.concatenate([jnp.zeros((8, own), jnp.float32), added], axis=0)
            gxy[here, 0:own] = total.astype(jnp.bfloat16)

        fetch.wait(9)
        loop(rows // TILE - 1, taps_back)
        lines[2].hop(1)
        add_up(1)
        ret.wait()
        taps_back(rows // TILE - 1, jnp.where(place.d < n_dp - 1, ret_in[...], 0.0))
        tap_grads[...] = jnp.zeros_like(tap_grads)
        for k in range(count):
            tap_grads[k : k + 1] = jnp.sum(tap_sums[k], axis=0, keepdims=True)
        tap_grads[count : count + 1] = (
            rate_scale * sg[...] * jnp.sum(decay_sums[...], axis=0, keepdims=True)
        )

        fetch.wait(14)
        out_rows.finish()
        plane.turn()
        xy_rows.run()
        send(4)
        lines[3].hop(0)

        def restore(i):
            here = tile_rows(i, 128)
            mp[here, 0 : 2 * own] = plain_dot(sto[here], gxy[...]).astype(jnp.bfloat16)

        loop(rows // 128, restore)

        def spread_back(i):
            some = tile_rows(i, 512)
            terms[:, pl.ds(pl.multiple_of(i * 512, 512), 512)] = (
                times_trans(mp[:, 0:own], wx[some]) + times_trans(mp[:, own : 2 * own], wy[some])
            ).astype(jnp.bfloat16)

        fetch.wait(10, 11)
        loop(width // 512, spread_back)
        store.start(0)
        lines[3].hop(1)
        add_up(2)
        plane.finish(weight_sum)
        add_up(3)
        for line in lines:
            line.finish()
        xy_rows.finish()
        store.wait(0)

    low, full = jnp.bfloat16, jnp.float32
    block = weight_terms.shape[0] // n_dp
    near, far = in_vmem(), in_any()
    return pl.pallas_call(
        kernel,
        out_shape=(
            shaped((size, 2 * own), low),
            shaped((8, own), full),
            shaped((rows, width), low),
            shaped((block, weight_terms.shape[1]), low),
            shaped((own_rows, width), low),
            shaped((width, own), low),
            shaped((width, 2 * own), low),
        ),
        in_specs=[far, near, near, far, far, far] + [near] * 5 + [far] * 12,
        out_specs=[near, near, far, near, near, far, far],
        scratch_shapes=[
            vmem_like(m) for m in (mixer_in, y_full, out_full, row_terms, merged_stored, *kept)
        ]
        + [
            pltpu.VMEM((rows, 2 * own), low),
            pltpu.VMEM((rows, width), low),
            pltpu.VMEM((rows, own), full),
            pltpu.VMEM((own // LANES, rows, LANES), full),
            pltpu.VMEM((own // LANES, rows, LANES), full),
            pltpu.VMEM((rows, wide), low),
            pltpu.VMEM((rows, wide), low),
            pltpu.VMEM((rows + 16, own), full),
            pltpu.VMEM((rows, wide), full),
            pltpu.VMEM((rows, RIM), low),
            pltpu.VMEM((rows, RIM), low),
            pltpu.VMEM((8, own), full),
            pltpu.VMEM((8, own), full),
            pltpu.VMEM((count, 8, own), full),
            pltpu.VMEM((8, own), full),
            pltpu.VMEM((2, 8, own), full),
            pltpu.VMEM((2, own), full),
            pltpu.VMEM((n_dp, 2, own), full),
            dma_sems(2),
            dma_sems(2),
            dma_sems(n_dp),
            dma_sems(n_dp),
            pltpu.SemaphoreType.DMA,
            dma_sems(15),
            dma_sems(1),
            pltpu.VMEM((parts, 2, n_line - 1, span, width), low),
            dma_sems(parts, 2, n_line - 1),
            dma_sems(parts, 2, n_line - 1),
            pltpu.VMEM((span, width), full),
            pltpu.VMEM((2, width // 5, 2 * own), low),
            dma_sems(2, 5),
        ]
        + ReducePlane.scratch(block, weight_terms.shape[1]),
        compiler_params=comm_params(6),
        name="recur_backward",
    )(
        mixer_in,
        to_place,
        to_stored,
        x_full,
        y_full,
        out_full,
        gates,
        taps,
        soft,
        slope,
        flags,
        *kept,
        weight_terms,
        row_terms,
        hidden_place,
        merged_stored,
    )


def column_parts(width, size=768):
    return [(c, min(size, width - c)) for c in range(0, width, size)]


def feed_forward(n_dp, n_line, hidden, gate, up, down, grads, grad_own):
    rows, width = hidden.shape
    units = gate.shape[1]
    own_rows = grad_own.shape[0]
    ready = grads.shape[0] // n_line
    late = own_rows - ready
    part = width // 4

    def kernel(*refs):
        hid_far, wg_far, wu_far, wd_far, grads_far, own_far = refs[:6]
        product_far, gup_far, back_far, gdown_far, ggate_far = refs[6:11]
        hid, wg, wu, wd, grad, slope, branch, product, ggate, gup, stage, back = refs[11:23]
        in_sems, out_sems, stage_sems, ls, lr = refs[23:]
        place = Place(n_dp, n_line)
        pairs = [(hid_far, hid), (wg_far, wg), (wu_far, wu), (wd_far, wd)]
        pairs += [
            (grads_far.at[pl.ds(q * ready, ready)], grad.at[pl.ds(q * own_rows, ready)])
            for q in range(n_line)
        ]
        mine = pl.ds(pl.multiple_of(place.t * own_rows + ready, 16), late)
        pairs.append((own_far.at[pl.ds(ready, late)], grad.at[mine]))
        fetch = Fetch(pairs, in_sems)
        fetch.start(*range(len(pairs)))
        store = Fetch(((product, product_far), (gup, gup_far), (back, back_far)), out_sems)
        place.meet()
        line = GatherLine(place, grad, own_rows, ready, late, ls, lr)
        line.step(0, own_far.at[pl.ds(ready, late)])
        columns = column_parts(units)
        fetch.wait(0, 1)
        for c, size in columns:
            cols = pl.ds(c, size)

            def gates(i, cols=cols):
                here = tile_rows(i, 256)
                branch[here, cols] = plain_dot(hid[here], wg[:, cols])

            loop(rows // 256, gates)
        line.step(1)
        fetch.wait(2)
        for c, size in columns:
            cols = pl.ds(c, size)

            def ups(i, cols=cols):
                here = tile_rows(i, 256)
                value = plain_dot(hid[here], wu[:, cols])
                active, bend = gelu_parts(branch[here, cols])
                product[here, cols] = (active * value).astype(jnp.bfloat16)
                branch[here, cols] = active
                slope[here, cols] = bend * value

            loop(rows // 256, ups)
        store.start(0)
        line.step(2)
        fetch.wait(*range(4, len(pairs)))
        line.finish()

        down_rows = RowProducts(grad, product, gdown_far, stage, stage_sems.at[0])
        down_rows.run()
        fetch.wait(3)
        for c, size in columns:
            cols = pl.ds(c, size)

            def backs(i, cols=cols):
                here = tile_rows(i, 256)
                value = plain_dot(grad[here], wd[:, cols])
                ggate[here, cols] = (value * slope[here, cols]).astype(jnp.bfloat16)
                gup[here, cols] = (value * branch[here, cols]).astype(jnp.bfloat16)

            loop(rows // 256, backs)
        store.start(1)
        for i in range(4):
            some = pl.ds(i * part, part)
            back[:, some] = (
                times_trans(ggate[...], wg[some]) + times_trans(gup[...], wu[some])
            ).astype(jnp.bfloat16)
        store.start(2)
        down_rows.finish()
        gate_rows = RowProducts(hid, ggate, ggate_far, stage, stage_sems.at[1])
        gate_rows.run()
        gate_rows.finish()
        store.wait(0, 1, 2)

    low, full = jnp.bfloat16, jnp.float32
    return pl.pallas_call(
        kernel,
        out_shape=(
            shaped((rows, units), low),
            shaped((rows, units), low),
            shaped((rows, width), low),
            shaped((width, units), low),
            shaped((width, units), low),
        ),
        in_specs=[in_any()] * 6,
        out_specs=[in_any()] * 5,
        scratch_shapes=[vmem_like(m) for m in (hidden, gate, up, down)]
        + [
            pltpu.VMEM((n_line * own_rows, width), low),
            pltpu.VMEM((rows, units), full),
            pltpu.VMEM((rows, units), full),
            pltpu.VMEM((rows, units), low),
            pltpu.VMEM((rows, units), low),
            pltpu.VMEM((rows, units), low),
            pltpu.VMEM((2, part, units), low),
            pltpu.VMEM((rows, width), low),
            dma_sems(5 + n_line),
            dma_sems(3),
            dma_sems(2, 4),
            dma_sems(2, n_line - 1),
            dma_sems(2, n_line - 1),
        ],
        compiler_params=comm_params(7),
        name="feed_forward",
    )(hidden, gate, up, down, grads, grad_own)


def matches(mesh):
    return mesh.shape["dp"] == 8 and mesh.shape["tensor"] == 4


def local_blocks(
    tokens,
    norm_gain,
    x_weight,
    y_weight,
    conv_weight,
    recur_gate_weight,
    input_gate_weight,
    decay_param,
    out_weight,
    mlp_gain,
    gate_weight,
    up_weight,
    down_weight,
    seq_lengths,
    token_order,
    cotangent,
):
    n_dp, n_tensor = lax.axis_size("dp"), lax.axis_size("tensor")
    tensor_index = lax.axis_index("tensor")
    dp_index = lax.axis_index("dp")
    tok_rows, width = tokens.shape
    row_count = tok_rows * n_tensor
    own_width = conv_weight.shape[1]
    kernel_taps = conv_weight.shape[0]
    edge_rows = kernel_taps - 1
    dp_width = norm_gain.shape[0]
    gate_rows = recur_gate_weight.shape[0]
    own_start = tensor_index * tok_rows

    gains = jnp.concatenate([norm_gain, mlp_gain])
    spare = gate_rows * 128 - gains.shape[0]
    gains = jnp.pad(gains, (0, spare)).reshape(gate_rows, 128)
    minor = jnp.concatenate([recur_gate_weight, input_gate_weight, gains], axis=1)
    own_order = (token_order - dp_index * row_count).astype(jnp.int32)
    order_rows = jnp.broadcast_to(own_order[None, :], (8, tok_rows))
    x_full, y_full, out_full, minor_full, tok_all, order_full = first_gather(
        n_dp, n_tensor, (x_weight, y_weight, out_weight.T, minor), tokens, order_rows
    )
    late_up, late_down, _ = lax.optimization_barrier((up_weight, down_weight.T, tok_all))
    up_full = lax.all_gather(late_up, "dp", axis=0, tiled=True)
    down_full = lax.all_gather(late_down, "dp", axis=0, tiled=True)
    order_all = order_full.reshape(n_tensor, 8, tok_rows)[:, 0].reshape(row_count)
    gain_rows = minor_full[:, 2 * own_width :].reshape(n_dp, -1)
    first_gain = gain_rows[:, :dp_width].reshape(1, width).astype(jnp.float32)
    second_gain = gain_rows[:, dp_width : 2 * dp_width].reshape(1, width).astype(jnp.float32)
    row_index = jnp.arange(row_count, dtype=jnp.int32)
    hits = row_index[:, None] == order_all[None, :]
    to_place = hits.astype(jnp.bfloat16)
    to_stored = (order_all[:, None] == row_index[None, :]).astype(jnp.bfloat16)
    places = dp_index * row_count + jnp.arange(-8, row_count + 8, dtype=jnp.int32)
    inside = (jnp.arange(row_count + 16) >= 8) & (jnp.arange(row_count + 16) < row_count + 8)
    ends = jnp.cumsum(seq_lengths)
    segment = segment_of(places, ends)
    starts = (places == 0) | (segment != segment_of(places - 1, ends))
    columns = [starts] + [
        segment_of(places - shift, ends) == segment for shift in range(1, kernel_taps)
    ]
    columns += [jnp.zeros_like(starts)] * (8 - len(columns))
    flags = (jnp.stack(columns, axis=1) & inside[:, None]).astype(jnp.float32)
    live_own = (token_order < ends[-1]).astype(jnp.float32)
    grad_in_own = (cotangent.astype(jnp.float32) * live_own[:, None]).astype(jnp.bfloat16)
    soft = jax.nn.softplus(-decay_param).reshape(1, own_width)
    slope = jax.nn.sigmoid(-decay_param).reshape(1, own_width)
    hidden_place, *kept, merged_stored, mixer_terms, gates_wide, grad_rows = recur_forward(
        n_dp,
        n_tensor,
        tok_all,
        grad_in_own,
        to_place,
        to_stored,
        x_full,
        y_full,
        out_full,
        first_gain,
        minor_full,
        conv_weight,
        soft,
        flags,
    )
    after_own, hidden_two, gate_full = middle_gather(
        n_dp, n_tensor, mixer_terms, tokens, second_gain, (gate_weight,)
    )
    product, grad_up_pre, back_terms, grad_down, grad_gate = feed_forward(
        n_dp,
        n_tensor,
        hidden_two,
        gate_full,
        up_full,
        down_full,
        grad_rows,
        grad_in_own,
    )
    down_sum = lax.psum_scatter(grad_down, "dp", scatter_dimension=0, tiled=True)
    grad_after_own, second_part, mixer_in, gate_sum, grad_up, feed_terms = middle_sums(
        n_dp,
        n_tensor,
        back_terms,
        after_own,
        second_gain,
        grad_in_own,
        grad_gate,
        hidden_two,
        grad_up_pre,
        product,
        down_full,
    )
    (
        gate_grads,
        tap_grads,
        one_terms,
        up_sum,
        feed_out,
        grad_out_mat,
        grad_xy_mat,
    ) = recur_backward(
        n_dp,
        n_tensor,
        mixer_in,
        to_place,
        to_stored,
        x_full,
        y_full,
        out_full,
        gates_wide,
        conv_weight,
        soft,
        slope,
        flags,
        kept,
        grad_up,
        feed_terms,
        hidden_place,
        merged_stored,
    )
    output = (after_own + feed_out.astype(jnp.float32)) * live_own[:, None]
    output = output.astype(jnp.bfloat16)
    grad_tokens, small_sum, gain_sums, xy_sum, out_sum, gates_sum = last_sums(
        n_dp,
        n_tensor,
        one_terms,
        tokens,
        first_gain,
        grad_after_own,
        second_part,
        tap_grads,
        (grad_xy_mat, grad_out_mat, gate_grads),
    )
    xy_sum, gates_sum = xy_sum.astype(jnp.float32), gates_sum.astype(jnp.float32)
    own_gains = lax.dynamic_slice_in_dim(gain_sums, dp_index * dp_width, dp_width, 1)
    return (
        output,
        grad_tokens,
        own_gains[1],
        xy_sum[:, :own_width],
        xy_sum[:, own_width:],
        small_sum[:kernel_taps],
        gates_sum[:, :own_width],
        gates_sum[:, own_width:],
        small_sum[kernel_taps],
        out_sum.astype(jnp.float32).T,
        own_gains[0],
        gate_sum.astype(jnp.float32),
        up_sum.astype(jnp.float32),
        down_sum.astype(jnp.float32).T,
    )


def solution(mesh):
    in_specs = (
        P(("dp", "tensor"), None),
        P("dp"),
        P("dp", "tensor"),
        P("dp", "tensor"),
        P(None, "tensor"),
        P("dp", "tensor"),
        P("dp", "tensor"),
        P("tensor"),
        P("tensor", "dp"),
        P("dp"),
        P("dp", "tensor"),
        P("dp", "tensor"),
        P("tensor", "dp"),
        P(),
        P(("dp", "tensor")),
        P(("dp", "tensor"), None),
    )
    out_specs = (
        P(("dp", "tensor"), None),
        P(("dp", "tensor"), None),
        P("dp"),
        P("dp", "tensor"),
        P("dp", "tensor"),
        P(None, "tensor"),
        P("dp", "tensor"),
        P("dp", "tensor"),
        P("tensor"),
        P("tensor", "dp"),
        P("dp"),
        P("dp", "tensor"),
        P("dp", "tensor"),
        P("tensor", "dp"),
    )
    fits = matches(mesh)
    local = local_blocks if fits else local_general
    return jax.shard_map(local, mesh=mesh, in_specs=in_specs, out_specs=out_specs, check_vma=False)
```

```python
import jax
import jax.numpy as jnp
from jax import lax
from jax.experimental import pallas as pl
from jax.experimental.pallas import tpu as pltpu
from jax.sharding import PartitionSpec as P

epsilon = 1e-06
rate_scale = 8.0


def from_behind(block, axis, distance):
    devices = range(lax.axis_size(axis))
    route = [(i - distance, i) for i in devices if i - distance in devices]
    return lax.ppermute(block, axis, route)


def extended_2(array, sides, width):
    for axis, dim in sides:
        size, length = (lax.axis_size(axis), array.shape[dim])
        up = [(i, (i + 1) % size) for i in range(size - 1)]
        down = [(j, i) for i, j in up]
        last = lax.slice_in_dim(array, length - width, length, axis=dim)
        leading = lax.slice_in_dim(array, 0, width, axis=dim)
        before = lax.ppermute(last, axis, up)
        after = lax.ppermute(leading, axis, down)
        array = jnp.concatenate([before, array, after], axis=dim)
    return array


def entering(value, axis, join, neutral, backward):
    count, mine = (lax.axis_size(axis), lax.axis_index(axis))
    pieces = jax.tree.map(lambda part: lax.all_gather(part, axis), value)
    if backward:
        pieces = jax.tree.map(lambda part: part[::-1], pieces)
        mine = count - 1 - mine
    total = jax.tree.map(
        lambda part, zero: jnp.full_like(part, 0) + jnp.asarray(zero, part.dtype), value, neutral
    )

    def lap(position, total):
        longer = join(total, jax.tree.map(lambda part: part[position], pieces))
        return jax.tree.map(lambda new, old: jnp.where(position < mine, new, old), longer, total)

    return lax.fori_loop(0, count - 1, lap, total)


def rms_scale(values, gain):
    return values * lax.rsqrt(jnp.mean(values * values, axis=-1, keepdims=True) + epsilon) * gain


def norm_back(values, gain, grad):
    inv_root = lax.rsqrt(jnp.mean(values * values, axis=-1, keepdims=True) + epsilon)
    normed = values * inv_root
    upstream = grad * gain
    grad_values = inv_root * (
        upstream - normed * jnp.mean(upstream * normed, axis=-1, keepdims=True)
    )
    return (grad_values, normed)


def segment_of(places, ends):
    return jnp.sum((ends[None, :] <= places[:, None]).astype(jnp.int32), axis=1)


def pair_step(early, later):
    return (early[0] * later[0], later[0] * early[1] + later[1])


def plain_dot(left, right):
    return jnp.dot(left, right, preferred_element_type=jnp.float32)


def times_trans(left, right):
    return lax.dot_general(
        left, right, (((1,), (1,)), ((), ())), preferred_element_type=jnp.float32
    )


def trans_times(left, right):
    return lax.dot_general(
        left, right, (((0,), (0,)), ((), ())), preferred_element_type=jnp.float32
    )


def gelu_tanh(values):
    return jax.nn.gelu(values, approximate=True)


def collect(
    norm_gain,
    mlp_gain,
    x_weight,
    y_weight,
    recur_gate_weight,
    input_gate_weight,
    gate_weight,
    up_weight,
    out_weight,
    down_weight,
):
    return (
        lax.all_gather(norm_gain, "dp", axis=0, tiled=True),
        lax.all_gather(mlp_gain, "dp", axis=0, tiled=True),
        lax.all_gather(x_weight, "dp", axis=0, tiled=True),
        lax.all_gather(y_weight, "dp", axis=0, tiled=True),
        lax.all_gather(recur_gate_weight, "dp", axis=0, tiled=True),
        lax.all_gather(input_gate_weight, "dp", axis=0, tiled=True),
        lax.all_gather(gate_weight, "dp", axis=0, tiled=True),
        lax.all_gather(up_weight, "dp", axis=0, tiled=True),
        lax.all_gather(out_weight, "dp", axis=1, tiled=True),
        lax.all_gather(down_weight, "dp", axis=1, tiled=True),
    )


def row_sums(term_rows, tok_rows):
    return lax.psum_scatter(
        term_rows(jnp.int32(0), lax.axis_size("tensor") * tok_rows).astype(jnp.bfloat16),
        "tensor",
        scatter_dimension=0,
        tiled=True,
    ).astype(jnp.float32)


def spread_rows(values):
    return lax.all_gather(values, "tensor", axis=0, tiled=True)


def local_general(
    tokens,
    norm_gain,
    x_weight,
    y_weight,
    conv_weight,
    recur_gate_weight,
    input_gate_weight,
    decay_param,
    out_weight,
    mlp_gain,
    gate_weight,
    up_weight,
    down_weight,
    seq_lengths,
    token_order,
    cotangent,
):
    n_tensor = lax.axis_size("tensor")
    tensor_index = lax.axis_index("tensor")
    dp_index = lax.axis_index("dp")
    tok_rows = tokens.shape[0]
    row_count = tok_rows * n_tensor
    own_width = conv_weight.shape[1]
    kernel_taps = conv_weight.shape[0]
    edge_rows = kernel_taps - 1
    dp_width = norm_gain.shape[0]
    own_start = tensor_index * tok_rows
    shards = (
        norm_gain,
        mlp_gain,
        x_weight,
        y_weight,
        recur_gate_weight,
        input_gate_weight,
        gate_weight,
        up_weight,
        out_weight,
        down_weight,
    )
    (
        gain_one,
        gain_two,
        x_full,
        y_full,
        recur_full,
        input_full,
        gate_full,
        up_full,
        out_full,
        down_full,
    ) = collect(*shards)
    block_size = recur_full.shape[0]
    first_gain = gain_one.astype(jnp.float32)
    second_gain = gain_two.astype(jnp.float32)
    both_gates = jnp.concatenate([recur_full, input_full], axis=1)
    tok_own = tokens.astype(jnp.float32)
    own_order = token_order - dp_index * row_count
    first_rows = rms_scale(tok_own, first_gain).astype(jnp.bfloat16)
    first_all, cot_all, order_all = (
        lax.all_gather(first_rows, "tensor", axis=0, tiled=True),
        lax.all_gather(cotangent, "tensor", axis=0, tiled=True),
        lax.all_gather(own_order, "tensor", axis=0, tiled=True),
    )
    row_index = jnp.arange(row_count, dtype=jnp.int32)
    inverse = jnp.zeros((row_count,), jnp.int32).at[order_all].set(row_index)
    hidden_place = jnp.take(first_all, inverse, axis=0)
    places = dp_index * row_count + row_index
    ends = jnp.cumsum(seq_lengths)
    segment = segment_of(places, ends)
    starts = (places == 0) | (segment != segment_of(places - 1, ends))
    live = (places < ends[-1]).astype(jnp.float32)
    live_stored = jnp.take(live, order_all, axis=0)
    same = [
        (segment_of(places - shift, ends) == segment).astype(jnp.float32)
        for shift in range(kernel_taps)
    ]
    low_edge = tensor_index * own_width
    own_blocks = (low_edge + jnp.arange(own_width, dtype=jnp.int32)) // block_size
    first_block = low_edge // block_size
    block_count = own_width // block_size + 2

    def block_start(index):
        return (first_block + index) * block_size - low_edge + block_size

    def block_mask(index):
        inside = own_blocks == first_block + index
        return jnp.concatenate([inside, inside])

    def convolve(extended, kernel):
        return sum(
            (
                kernel[shift][None, :]
                * extended[edge_rows - shift : edge_rows - shift + row_count]
                * same[shift][:, None]
                for shift in range(kernel_taps)
            )
        )

    def gates(conv_vals, pre_recur, pre_input, decay_vals):
        log_rate = -rate_scale * jax.nn.sigmoid(pre_recur) * jax.nn.softplus(-decay_vals)
        decay_rate = jnp.where(starts[:, None], 0.0, jnp.exp(log_rate))
        scale_in = jnp.where(starts[:, None], 1.0, jnp.sqrt(-jnp.expm1(2.0 * log_rate)))
        return (decay_rate, conv_vals * jax.nn.sigmoid(pre_input) * scale_in)

    def glu(gate_pre, up_pre):
        return gelu_tanh(gate_pre) * up_pre

    x_branch = plain_dot(hidden_place, x_full).astype(jnp.bfloat16)
    y_before = plain_dot(hidden_place, y_full)
    previous = from_behind(x_branch[row_count - edge_rows :], "dp", 1)
    extended = jnp.concatenate([previous, x_branch], axis=0).astype(jnp.float32)
    conv_out = convolve(extended, conv_weight)
    conv_wide = extended_2(conv_out.astype(jnp.bfloat16), (("tensor", 1),), block_size)
    pre_both = jnp.zeros((row_count, 2 * own_width), jnp.float32)
    for index in range(block_count):
        piece = lax.dynamic_slice_in_dim(conv_wide, block_start(index), block_size, 1)
        pre_both = pre_both + jnp.where(
            block_mask(index)[None, :], plain_dot(piece, both_gates), 0.0
        )
    (decay_rate, driven), gate_pull = jax.vjp(
        gates, conv_out, pre_both[:, :own_width], pre_both[:, own_width:], decay_param
    )
    cum_rate, local_state = lax.associative_scan(pair_step, (decay_rate, driven), axis=0)
    ident = (jnp.ones((own_width,), jnp.float32), jnp.zeros((own_width,), jnp.float32))
    rate_in, state_in = entering((cum_rate[-1], local_state[-1]), "dp", pair_step, ident, False)
    state = local_state + cum_rate * state_in[None, :]
    y_branch = gelu_tanh(y_before)
    merged = (state * y_branch).astype(jnp.bfloat16)
    merged_stored = jnp.take(merged, order_all, axis=0)

    def mixer_rows(begin, number):
        return plain_dot(merged_stored, out_full)

    after_own = tok_own + row_sums(mixer_rows, tok_rows)
    hidden_two = spread_rows(rms_scale(after_own, second_gain).astype(jnp.bfloat16))
    gate_pre = plain_dot(hidden_two, gate_full)
    up_pre = plain_dot(hidden_two, up_full)
    glu_out, glu_pull = jax.vjp(glu, gate_pre, up_pre)
    product = glu_out.astype(jnp.bfloat16)

    def down_rows(begin, number):
        return plain_dot(product, down_full)

    feed_out = row_sums(down_rows, tok_rows)
    live_own = lax.dynamic_slice_in_dim(live_stored, own_start, tok_rows, 0)
    output = ((after_own + feed_out) * live_own[:, None]).astype(jnp.bfloat16)
    grad_out = cot_all.astype(jnp.float32) * live_stored[:, None]
    fresh = lax.optimization_barrier((shards, grad_out))[0]
    (
        gain_one,
        gain_two,
        x_full,
        y_full,
        recur_full,
        input_full,
        gate_full,
        up_full,
        out_full,
        down_full,
    ) = collect(*fresh)
    first_gain = gain_one.astype(jnp.float32)
    second_gain = gain_two.astype(jnp.float32)
    both_gates = jnp.concatenate([recur_full, input_full], axis=1)
    down_in = grad_out.astype(jnp.bfloat16)
    grad_down = trans_times(product, down_in)
    grad_product = times_trans(down_in, down_full)
    grad_gate_pre, grad_up_pre = glu_pull(grad_product)
    grad_gate_pre = grad_gate_pre.astype(jnp.bfloat16)
    grad_up_pre = grad_up_pre.astype(jnp.bfloat16)
    grad_gate = trans_times(hidden_two, grad_gate_pre)
    grad_up = trans_times(hidden_two, grad_up_pre)

    def feed_rows(begin, number):
        return times_trans(grad_gate_pre, gate_full) + times_trans(grad_up_pre, up_full)

    grad_out_own = lax.dynamic_slice_in_dim(grad_out, own_start, tok_rows, 0)
    grad_two_own = row_sums(feed_rows, tok_rows)
    grad_norm_own, normed_two = norm_back(after_own, second_gain, grad_two_own)
    second_part = jnp.sum(grad_two_own * normed_two, axis=0)
    grad_after_own = grad_out_own + grad_norm_own
    mixer_in = spread_rows(grad_after_own.astype(jnp.bfloat16))
    grad_out_mat = trans_times(merged_stored, mixer_in)
    grad_merged = jnp.take(times_trans(mixer_in, out_full), inverse, axis=0)
    grad_state = grad_merged * y_branch
    gelu_pull = jax.vjp(gelu_tanh, y_before)[1]
    grad_y_before = gelu_pull(grad_merged * state)[0].astype(jnp.bfloat16)
    rate_next = jnp.concatenate([decay_rate[1:], jnp.ones((1, own_width), jnp.float32)], axis=0)
    rev_rate, local_lam = lax.associative_scan(
        pair_step, (rate_next, grad_state), reverse=True, axis=0
    )
    head_rate = decay_rate[0] * rev_rate[0]
    head_lam = decay_rate[0] * local_lam[0]
    factor_in, lam_in = entering((head_rate, head_lam), "dp", pair_step, ident, True)
    lam = local_lam + rev_rate * lam_in[None, :]
    state_prev = jnp.concatenate([state_in[None, :], state[:-1]], axis=0)
    grad_conv_local, grad_pre_recur, grad_pre_input, grad_decay_own = gate_pull(
        (lam * state_prev, lam)
    )
    grad_pre = jnp.concatenate([grad_pre_recur, grad_pre_input], axis=1).astype(jnp.bfloat16)
    grad_both = jnp.zeros((block_size, 2 * own_width), jnp.float32)
    grad_wide = jnp.zeros((row_count, own_width + 2 * block_size), jnp.float32)
    for index in range(block_count):
        begin = block_start(index)
        piece = lax.dynamic_slice_in_dim(conv_wide, begin, block_size, 1)
        masked = jnp.where(block_mask(index)[None, :], grad_pre, jnp.zeros((), jnp.bfloat16))
        grad_both = grad_both + trans_times(piece, masked)
        added = lax.dynamic_slice_in_dim(grad_wide, begin, block_size, 1) + times_trans(
            masked, both_gates
        )
        grad_wide = lax.dynamic_update_slice_in_dim(grad_wide, added, begin, 1)
    grad_recur = grad_both[:, :own_width]
    grad_input = grad_both[:, own_width:]
    rims = jnp.concatenate(
        [grad_wide[:, :block_size], grad_wide[:, own_width + block_size :]], axis=1
    )
    arrived = extended_2(rims.astype(jnp.bfloat16), (("tensor", 1),), block_size).astype(rims.dtype)
    from_lower = jnp.pad(arrived[:, :block_size], ((0, 0), (0, own_width - block_size)))
    from_upper = jnp.pad(arrived[:, 3 * block_size :], ((0, 0), (own_width - block_size, 0)))
    grad_conv = (
        grad_conv_local
        + grad_wide[:, block_size : block_size + own_width]
        + from_lower
        + from_upper
    )
    conv_pull = jax.vjp(convolve, extended, conv_weight)[1]
    grad_extended, grad_kernel = conv_pull(grad_conv)
    returned = from_behind(grad_extended[:edge_rows], "dp", -1)
    grad_x_branch = grad_extended[edge_rows:] + jnp.concatenate(
        [jnp.zeros((row_count - edge_rows, own_width), jnp.float32), returned], axis=0
    )
    grad_x_low = grad_x_branch.astype(jnp.bfloat16)
    grad_x_stored = jnp.take(grad_x_low, order_all, axis=0)
    grad_y_stored = jnp.take(grad_y_before, order_all, axis=0)
    grad_x_mat = trans_times(first_all, grad_x_stored)
    grad_y_mat = trans_times(first_all, grad_y_stored)

    def mixer_back_rows(begin, number):
        return times_trans(grad_x_stored, x_full) + times_trans(grad_y_stored, y_full)

    grad_one_own = row_sums(mixer_back_rows, tok_rows)
    grad_norm_one, normed_one = norm_back(tok_own, first_gain, grad_one_own)
    first_part = jnp.sum(grad_one_own * normed_one, axis=0)
    grad_tokens = grad_after_own + grad_norm_one
    chosen = jnp.arange(n_tensor, dtype=jnp.int32) == tensor_index
    kernel_tile = jnp.where(chosen[:, None, None], grad_kernel[None, :, :], 0.0)
    decay_tile = jnp.where(chosen[:, None], grad_decay_own[None, :], 0.0)
    small = lax.psum((first_part, second_part, kernel_tile, decay_tile), ("dp", "tensor"))
    grad_first_gain = lax.dynamic_slice_in_dim(small[0], dp_index * dp_width, dp_width, 0)
    grad_second_gain = lax.dynamic_slice_in_dim(small[1], dp_index * dp_width, dp_width, 0)
    grad_kernel_sum = lax.dynamic_index_in_dim(small[2], tensor_index, 0, keepdims=False)
    grad_decay = lax.dynamic_index_in_dim(small[3], tensor_index, 0, keepdims=False)
    sums = (
        lax.psum_scatter(
            grad_x_mat.astype(jnp.bfloat16), "dp", scatter_dimension=0, tiled=True
        ).astype(jnp.float32),
        lax.psum_scatter(
            grad_y_mat.astype(jnp.bfloat16), "dp", scatter_dimension=0, tiled=True
        ).astype(jnp.float32),
        lax.psum_scatter(
            grad_recur.astype(jnp.bfloat16), "dp", scatter_dimension=0, tiled=True
        ).astype(jnp.float32),
        lax.psum_scatter(
            grad_input.astype(jnp.bfloat16), "dp", scatter_dimension=0, tiled=True
        ).astype(jnp.float32),
        lax.psum_scatter(
            grad_gate.astype(jnp.bfloat16), "dp", scatter_dimension=0, tiled=True
        ).astype(jnp.float32),
        lax.psum_scatter(
            grad_up.astype(jnp.bfloat16), "dp", scatter_dimension=0, tiled=True
        ).astype(jnp.float32),
        lax.psum_scatter(
            grad_out_mat.astype(jnp.bfloat16), "dp", scatter_dimension=1, tiled=True
        ).astype(jnp.float32),
        lax.psum_scatter(
            grad_down.astype(jnp.bfloat16), "dp", scatter_dimension=1, tiled=True
        ).astype(jnp.float32),
    )
    return (
        output,
        grad_tokens,
        grad_first_gain,
        sums[0],
        sums[1],
        grad_kernel_sum,
        sums[2],
        sums[3],
        grad_decay,
        sums[6],
        grad_second_gain,
        sums[4],
        sums[5],
        sums[7],
    )


MESH = pl.DeviceIdType.MESH
VMEM_BYTES = 60 * 2**20


def remote(src, dst, send, recv, device):
    return pltpu.make_async_remote_copy(
        src_ref=src,
        dst_ref=dst,
        send_sem=send,
        recv_sem=recv,
        device_id=device,
        device_id_type=MESH,
    )


class Place:
    def __init__(self, n_dp, n_line):
        self.n_dp, self.n_line = n_dp, n_line
        self.d, self.t = lax.axis_index("dp"), lax.axis_index("tensor")
        self.core = lax.rem(self.d, 2)
        self.x = lax.rem(lax.div(self.d, 2), 2)
        self.y = lax.div(self.d, 4)

    def chip(self, flip_x, flip_y, flip_core=0):
        x = 1 - self.x if flip_x else self.x
        y = 1 - self.y if flip_y else self.y
        core = 1 - self.core if flip_core else self.core
        return y * 4 + x * 2 + core

    def at(self, flip_x=0, flip_y=0, flip_core=0):
        return (self.chip(flip_x, flip_y, flip_core), self.t)

    def up(self):
        return (self.d, lax.rem(self.t + 1, self.n_line))

    def down(self):
        return (self.d, lax.rem(self.t + self.n_line - 1, self.n_line))

    def meet(self, everyone=False):
        barrier = pltpu.get_barrier_semaphore()

        def greet(device):
            pl.semaphore_signal(barrier, inc=1, device_id=device, device_id_type=MESH)

        if everyone:
            for i in range(1, self.n_dp):
                greet((lax.rem(self.d + i, self.n_dp), self.t))
            for i in range(1, self.n_line):
                greet((self.d, lax.rem(self.t + i, self.n_line)))
            pl.semaphore_wait(barrier, self.n_dp + self.n_line - 2)
            return
        for flips in ((1, 0), (0, 1), (0, 0, 1)):
            greet(self.at(*flips))
        below, above = self.t > 0, self.t < self.n_line - 1

        @pl.when(below)
        def _():
            greet(self.down())

        @pl.when(above)
        def _():
            greet(self.up())

        pl.semaphore_wait(barrier, 3 + below.astype(jnp.int32) + above.astype(jnp.int32))


class Fetch:
    def __init__(self, pairs, sems):
        self.copies = [
            pltpu.make_async_copy(src, dst, sems.at[i]) for i, (src, dst) in enumerate(pairs)
        ]

    def start(self, *which):
        for i in which:
            self.copies[i].start()

    def wait(self, *which):
        for i in which:
            self.copies[i].wait()


def vmem_like(array):
    return pltpu.VMEM(array.shape, array.dtype)


class Kept:
    def __init__(self, src, dst, held, sems):
        self.there = pltpu.make_async_copy(src, held, sems.at[0])
        self.back = pltpu.make_async_copy(held, dst, sems.at[1])

    def begin(self):
        self.there.start()

    def turn(self):
        self.there.wait()
        self.back.start()

    def finish(self):
        self.back.wait()


class GatherPlane:
    def __init__(self, place, src, dst, send, recv, local, held):
        self.p, self.src, self.dst = place, src, dst
        self.rows = src.shape[0]
        self.send, self.recv = send, recv
        self.keep = Kept(src, self.block(0, 0), held, local)

    def block(self, fx, fy, fc=0, part=None):
        first = self.p.chip(fx, fy, fc) * self.rows
        size = self.rows
        if part is not None:
            size = self.rows // 2
            first = first + part * size
        return self.dst.at[pl.ds(pl.multiple_of(first, 16), size)]

    def copy(self, i, src, dst, device):
        return remote(src, dst, self.send.at[i], self.recv.at[i], device)

    def outgoing(self, i):
        at, block = self.p.at, self.block
        if i == 0:
            return self.copy(0, self.src, block(0, 0), at(1, 0))
        if i == 1:
            return self.copy(1, self.src, block(0, 0), at(0, 1))
        if i == 2:
            return self.copy(2, self.src, block(0, 0), at(0, 0, 1))
        if i == 3:
            return self.copy(3, block(1, 0, 0, 0), block(1, 0, 0, 0), at(0, 1))
        if i == 4:
            return self.copy(4, block(0, 1, 0, 1), block(0, 1, 0, 1), at(1, 0))
        spot = ((1, 0), (0, 1), (1, 1, 0, 0), (1, 1, 0, 1))[i - 5]
        return self.copy(i, block(*spot), block(*spot), at(0, 0, 1))

    def arrive(self, i):
        spot = (
            (1, 0),
            (0, 1),
            (0, 0, 1),
            (1, 1, 0, 0),
            (1, 1, 0, 1),
            (1, 0, 1),
            (0, 1, 1),
            (1, 1, 1, 0),
            (1, 1, 1, 1),
        )[i]
        here = self.block(*spot)
        self.copy(i, here, here, self.p.at(0, 0, 1)).wait_recv()

    def begin(self):
        for i in (0, 1, 2):
            self.outgoing(i).start()
        self.keep.begin()

    def forward(self):
        self.keep.turn()
        self.arrive(0)
        self.outgoing(3).start()
        self.arrive(1)
        self.outgoing(4).start()
        self.outgoing(5).start()
        self.outgoing(6).start()

    def share(self):
        self.arrive(3)
        self.outgoing(7).start()
        self.arrive(4)
        self.outgoing(8).start()

    def finish(self):
        for i in (2, 5, 6, 7, 8):
            self.arrive(i)
        for i in range(9):
            self.outgoing(i).wait_send()
        self.keep.finish()


class GatherLine:
    def __init__(self, place, dst, rows, begin, span, send, recv):
        self.p, self.dst, self.rows = place, dst, rows
        self.begin, self.span = begin, span
        self.send, self.recv = send, recv
        self.last = place.n_line - 1

    def block(self, owner):
        first = owner * self.rows + self.begin
        return self.dst.at[pl.ds(pl.multiple_of(first, 8), self.span)]

    def copy(self, way, k, owner, source=None):
        to = self.p.up() if way == 0 else self.p.down()
        block = self.block(owner)
        return remote(
            block if source is None else source,
            block,
            self.send.at[way, k],
            self.recv.at[way, k],
            to,
        )

    def step(self, k, source=None):
        t, last = self.p.t, self.last
        if k > 0:
            self.arrive(k - 1)

        @pl.when((t < last) & (t >= k))
        def _():
            self.copy(0, k, t - k, source).start()

        @pl.when((t > 0) & (t + k <= last))
        def _():
            self.copy(1, k, t + k, source).start()

    def arrive(self, k):
        t, last = self.p.t, self.last

        @pl.when(t >= k + 1)
        def _():
            self.copy(0, k, t - 1 - k).wait_recv()

        @pl.when(t + k + 1 <= last)
        def _():
            self.copy(1, k, t + 1 + k).wait_recv()

    def finish(self):
        t, last = self.p.t, self.last
        self.arrive(last - 1)
        for k in range(last):

            @pl.when((t < last) & (t >= k))
            def _():
                self.copy(0, k, t - k).wait_send()

            @pl.when((t > 0) & (t + k <= last))
            def _():
                self.copy(1, k, t + k).wait_send()


class ReduceLine:
    def __init__(self, place, terms, rows, begin, span, inbox, send, recv):
        self.p, self.terms, self.rows = place, terms, rows
        self.begin, self.span = begin, span
        self.inbox = inbox
        self.send, self.recv = send, recv
        self.last = place.n_line - 1

    def own(self, owner):
        first = owner * self.rows + self.begin
        return self.terms.at[pl.ds(pl.multiple_of(first, 16), self.span)]

    def copy(self, way, j, source):
        to = self.p.up() if way == 0 else self.p.down()
        return remote(
            source, self.inbox.at[way, j], self.send.at[way, j], self.recv.at[way, j], to
        )

    def ends(self):
        t, last = self.p.t, self.last

        @pl.when(t == 0)
        def _():
            for j in range(last):
                self.copy(0, j, self.own(last - j)).start()

        @pl.when(t == last)
        def _():
            for j in range(last):
                self.copy(1, j, self.own(j)).start()

    def sent(self):
        t, last = self.p.t, self.last

        @pl.when(t == 0)
        def _():
            for j in range(last):
                self.copy(0, j, self.own(last - j)).wait_send()

        @pl.when(t == last)
        def _():
            for j in range(last):
                self.copy(1, j, self.own(j)).wait_send()

    def hand_on(self, way, j):
        term = self.own(self.last - j if way == 0 else j)
        self.copy(way, j, term).wait_recv()
        self.inbox[way, j] = term[...] + self.inbox[way, j]
        self.copy(way, j, self.inbox.at[way, j]).start()

    def hop(self, k):
        t, last = self.p.t, self.last

        @pl.when(t == k + 1)
        def _():
            for j in range(last - 1 - k):
                self.hand_on(0, j)

        @pl.when(t == last - 1 - k)
        def _():
            for j in range(last - 1 - k):
                self.hand_on(1, j)

    def total(self, result):
        t, last = self.p.t, self.last
        result[...] = self.own(t)[...].astype(jnp.float32)

        @pl.when(t > 0)
        def _():
            j = last - t
            self.copy(0, j, self.inbox.at[0, 0]).wait_recv()
            result[...] += self.inbox[0, j].astype(jnp.float32)

        @pl.when(t < last)
        def _():
            self.copy(1, t, self.inbox.at[0, 0]).wait_recv()
            result[...] += self.inbox[1, t].astype(jnp.float32)

    def finish(self):
        t, last = self.p.t, self.last
        for j in range(last - 1):

            @pl.when((t > 0) & (t < last - j))
            def _():
                self.copy(0, j, self.inbox.at[0, j]).wait_send()

            @pl.when((t < last) & (t > j))
            def _():
                self.copy(1, j, self.inbox.at[1, j]).wait_send()


def add_rows(into, other, result=None):
    result = into if result is None else result

    def tile(i, carry):
        rows = pl.ds(pl.multiple_of(i * 16, 16), 16)
        result[rows] = into[rows] + other[rows]
        return carry

    lax.fori_loop(0, into.shape[0] // 16, tile, None)


class ReducePlane:
    chips = ((0, 0), (1, 0), (0, 1), (1, 1))

    def __init__(self, place, terms, scratch):
        self.p, self.terms = place, terms
        self.held, self.near, self.along, self.last, self.send, self.recv, self.local = scratch
        self.rows = self.held.shape[1]
        self.half = self.rows // 2

    @staticmethod
    def scratch(rows, width):
        return [
            pltpu.VMEM((4, rows, width), jnp.bfloat16),
            pltpu.VMEM((4, rows, width), jnp.bfloat16),
            pltpu.VMEM((4, rows // 2, width), jnp.bfloat16),
            pltpu.VMEM((2, rows // 2, width), jnp.bfloat16),
            pltpu.SemaphoreType.DMA((10,)),
            pltpu.SemaphoreType.DMA((10,)),
            pltpu.SemaphoreType.DMA((4,)),
        ]

    def block(self, k, other):
        first = self.p.chip(*self.chips[k], other) * self.rows
        return self.terms.at[pl.ds(pl.multiple_of(first, 16), self.rows)]

    def half_of(self, k, part):
        return self.held.at[k, pl.ds(part * self.half, self.half)]

    def load(self, k):
        return pltpu.make_async_copy(self.block(k, 0), self.held.at[k], self.local.at[k])

    def copy(self, i):
        at = self.p.at
        if i < 4:
            src, dst, to = self.block(i, 1), self.near.at[i], at(0, 0, 1)
        elif i < 8:
            src, to = (
                (self.half_of(1, 0), at(1, 0)),
                (self.half_of(3, 0), at(1, 0)),
                (self.half_of(2, 1), at(0, 1)),
                (self.half_of(3, 1), at(0, 1)),
            )[i - 4]
            dst = self.along.at[i - 4]
        else:
            src, to = ((self.half_of(2, 0), at(0, 1)), (self.half_of(1, 1), at(1, 0)))[i - 8]
            dst = self.last.at[i - 8]
        return remote(src, dst, self.send.at[i], self.recv.at[i], to)

    def begin(self):
        for k in (3, 1, 2, 0):
            self.copy(k).start()
            self.load(k).start()

    def cores(self):
        for k in (3, 1, 2, 0):
            self.load(k).wait()
            self.copy(k).wait_recv()
            add_rows(self.held.at[k], self.near.at[k])
            if k == 3:
                self.copy(5).start()
                self.copy(7).start()
            elif k == 1:
                self.copy(4).start()
            elif k == 2:
                self.copy(6).start()

    def turn(self):
        self.copy(5).wait_recv()
        add_rows(self.half_of(2, 0), self.along.at[1])
        self.copy(8).start()
        self.copy(7).wait_recv()
        add_rows(self.half_of(1, 1), self.along.at[3])
        self.copy(9).start()
        self.copy(4).wait_recv()
        add_rows(self.half_of(0, 0), self.along.at[0])
        self.copy(6).wait_recv()
        add_rows(self.half_of(0, 1), self.along.at[2])

    def finish(self, result):
        for part in (0, 1):
            self.copy(8 + part).wait_recv()
            rows = pl.ds(part * self.half, self.half)
            add_rows(self.half_of(0, part), self.last.at[part], result.at[rows])
        for i in range(10):
            self.copy(i).wait_send()


def dma_sems(*dims):
    return pltpu.SemaphoreType.DMA(dims)


def in_vmem():
    return pl.BlockSpec(memory_space=pltpu.VMEM)


def in_any():
    return pl.BlockSpec(memory_space=pl.ANY)


def comm_params(number):
    return pltpu.CompilerParams(
        collective_id=number, has_side_effects=True, vmem_limit_bytes=VMEM_BYTES
    )


def shaped(dims, kind):
    return jax.ShapeDtypeStruct(dims, kind)


def first_gather(n_dp, n_line, mats, rows_in, order):
    count = len(mats)
    parts = 2

    def kernel(*refs):
        srcs, (c, e) = refs[:count], refs[count : count + 2]
        dsts, (c_out, e_out) = refs[count + 2 : 2 * count + 2], refs[2 * count + 2 : 2 * count + 4]
        ps, pr, pl_sem, ls, lr, ll = refs[2 * count + 4 : 2 * count + 10]
        held = refs[2 * count + 10 :]
        place = Place(n_dp, n_line)
        place.meet()
        planes = [
            GatherPlane(place, a, b, ps.at[i], pr.at[i], pl_sem.at[i], held[i])
            for i, (a, b) in enumerate(zip(srcs, dsts))
        ]
        rows = c.shape[0]
        span = rows // parts
        lines = [
            GatherLine(place, c_out, rows, i * span, span, ls.at[i], lr.at[i])
            for i in range(parts)
        ]
        lines.append(
            GatherLine(place, e_out, e.shape[0], 0, e.shape[0], ls.at[parts], lr.at[parts])
        )
        for i in range(parts):
            lines[i].step(0, c.at[pl.ds(i * span, span)])
        lines[parts].step(0, e)
        early, late = planes[: count // 2], planes[count // 2 :]
        for part in early:
            part.begin()
        copies = []
        for i, (src, dst) in enumerate(((c, c_out), (e, e_out))):
            own = dst.at[pl.ds(pl.multiple_of(place.t * src.shape[0], 8), src.shape[0])]
            copies.append(Kept(src, own, held[count + i], ll.at[i]))
            copies[i].begin()
        for line in lines:
            line.step(1)
        for part in late:
            part.begin()
        for part in early:
            part.forward()
        for copy in copies:
            copy.turn()
        for line in lines:
            line.step(2)
        for part in early:
            part.share()
        for part in late:
            part.forward()
        for part in late:
            part.share()
        for part in lines + planes:
            part.finish()
        for copy in copies:
            copy.finish()

    return pl.pallas_call(
        kernel,
        out_shape=tuple(shaped((n_dp * m.shape[0], m.shape[1]), m.dtype) for m in mats)
        + (
            shaped((n_line * rows_in.shape[0], rows_in.shape[1]), rows_in.dtype),
            shaped((n_line * order.shape[0], order.shape[1]), order.dtype),
        ),
        in_specs=[in_any()] * (count + 2),
        out_specs=[in_any()] * (count + 2),
        scratch_shapes=[
            dma_sems(count, 9),
            dma_sems(count, 9),
            dma_sems(count, 2),
            dma_sems(parts + 1, 2, n_line - 1),
            dma_sems(parts + 1, 2, n_line - 1),
            dma_sems(2, 2),
        ]
        + [vmem_like(m) for m in (*mats, rows_in, order)],
        compiler_params=comm_params(1),
        name="first_gather",
    )(*mats, rows_in, order)


CHUNKS = 8
LAST_CHUNKS = 8


def line_scratch(n_line, span, width, chunks):
    hops = n_line - 1
    return [
        pltpu.VMEM((chunks, 2, hops, span, width), jnp.bfloat16),
        dma_sems(chunks, 2, hops),
        dma_sems(chunks, 2, hops),
        dma_sems(chunks, 2, hops),
        dma_sems(chunks, 2, hops),
        pltpu.VMEM((span, width), jnp.float32),
    ]


def sum_rows_and_spread(place, terms, scratch, finish_rows, spread, between):
    inbox, rs, rr, gs, gr, total = scratch
    span = total.shape[0]
    count = inbox.shape[0]
    rows = span * count
    hops = place.n_line - 1
    sums = [
        ReduceLine(place, terms, rows, c * span, span, inbox.at[c], rs.at[c], rr.at[c])
        for c in range(count)
    ]
    gathers = []
    if spread is not None:
        gathers = [
            GatherLine(place, spread, rows, c * span, span, gs.at[c], gr.at[c])
            for c in range(count)
        ]
    sums[0].ends()

    def total_of(c):
        sums[c].total(total)
        finish_rows(c, pl.ds(c * span, span), total)
        if gathers:
            gathers[c].step(0)

    stages = [lambda c, k=k: sums[c].hop(k) for k in range(hops - 1)] + [total_of]
    lags = [LAGS[min(k, len(LAGS) - 1)] for k in range(hops)]
    if gathers:
        stages += [lambda c, k=k: gathers[c].step(k) for k in range(1, hops)]
        lags += [lags[-1] + LAG_STEP * k for k in range(1, hops)]
    for i in range(count + lags[-1]):
        if i < count:
            sums[i].sent()
        if i + 1 < count:
            sums[i + 1].ends()
        for work, lag in zip(stages, lags):
            if 0 <= i - lag < count:
                work(i - lag)
        if i in between:
            between[i]()
    for part in gathers + sums:
        part.finish()


LAGS = (0, 1, 1)
LAG_STEP = 1


def middle_gather(n_dp, n_line, terms, tokens, gain, mats):
    rows, width = tokens.shape
    count = len(mats)

    def kernel(*refs):
        s, tok, gain_ref = refs[:3]
        srcs = refs[3 : 3 + count]
        after, hidden = refs[3 + count : 5 + count]
        dsts = refs[5 + count : 5 + 2 * count]
        ps, pr, pl_sem = refs[5 + 2 * count : 8 + 2 * count]
        held = refs[8 + 2 * count : 8 + 3 * count]
        scratch = refs[8 + 3 * count :]
        place = Place(n_dp, n_line)
        place.meet()
        planes = [
            GatherPlane(place, a, b, ps.at[i], pr.at[i], pl_sem.at[i], held[i])
            for i, (a, b) in enumerate(zip(srcs, dsts))
        ]
        planes[0].begin()

        def norm(c, here, total):
            values = tok[here].astype(jnp.float32) + total[...]
            after[here] = values
            low = rms_scale(values, gain_ref[...]).astype(jnp.bfloat16)
            first = pl.multiple_of(place.t * rows, 16) + c * total.shape[0]
            hidden[pl.ds(pl.multiple_of(first, 16), total.shape[0])] = low

        between = {5: planes[0].forward, 8: planes[0].share}
        sum_rows_and_spread(place, s, scratch, norm, hidden, between)
        for part in planes:
            part.finish()

    return pl.pallas_call(
        kernel,
        out_shape=(
            shaped((rows, width), jnp.float32),
            shaped((n_line * rows, width), jnp.bfloat16),
        )
        + tuple(shaped((n_dp * m.shape[0], m.shape[1]), m.dtype) for m in mats),
        in_specs=[in_vmem()] * 3 + [in_any()] * count,
        out_specs=[in_vmem()] * 2 + [in_any()] * count,
        scratch_shapes=[dma_sems(count, 9), dma_sems(count, 9), dma_sems(count, 2)]
        + [vmem_like(m) for m in mats]
        + line_scratch(n_line, rows // CHUNKS, width, CHUNKS),
        compiler_params=comm_params(2),
        name="middle_gather",
    )(terms, tokens, gain, *mats)


def middle_sums(n_dp, n_line, terms, after, gain, grad_in, mat, hidden, grad_up, product, down):
    rows, width = after.shape
    block = mat.shape[0] // n_dp
    wide = grad_up.shape[1]
    spread_rows = n_line * rows

    def kernel(*refs):
        s, after_ref, gain_ref, g_ref, src = refs[:5]
        hid_far, gu_far, pr_far, dw_far = refs[5:9]
        grad_after, gain_sum, spread, result, up_far, feed_far = refs[9:15]
        hid, gu, pr, dw, up_out, feed, sems = refs[15:22]
        rest = refs[22:]
        fetch = Fetch(
            [
                (hid_far, hid),
                (gu_far, gu),
                (pr_far, pr),
                (dw_far, dw),
                (feed, feed_far),
                (up_out.at[0], up_far.at[pl.ds(0, width // 2)]),
                (up_out.at[1], up_far.at[pl.ds(width // 2, width // 2)]),
            ],
            sems,
        )
        fetch.start(0, 1, 2, 3)
        place = Place(n_dp, n_line)
        place.meet()
        plane = ReducePlane(place, src, rest[:7])
        scratch = rest[7:]
        plane.begin()
        gain_sum[...] = jnp.zeros_like(gain_sum)

        def norm(c, here, total):
            grad = total[...]
            grad_rows, normed = norm_back(after_ref[here], gain_ref[...], grad)
            gain_sum[...] += jnp.sum(grad * normed, axis=0, keepdims=True)
            both = g_ref[here].astype(jnp.float32) + grad_rows
            grad_after[here] = both
            first = pl.multiple_of(place.t * rows, 16) + c * total.shape[0]
            spread[pl.ds(pl.multiple_of(first, 16), total.shape[0])] = both.astype(jnp.bfloat16)

        def feed_part(i):
            cols = pl.ds(i * (width // 4), width // 4)
            feed[:, cols] = times_trans(pr[...], dw[cols]).astype(jnp.bfloat16)

        def up_part(i):
            cols = pl.ds(i * (width // 4), width // 4)
            here = pl.ds((i % 2) * (width // 4), width // 4)
            up_out[i // 2, here] = trans_times(hid[:, cols], gu[...]).astype(jnp.bfloat16)

        def early():
            plane.cores()
            fetch.wait(0, 1)

        def two():
            up_part(0)

        def three():
            up_part(1)
            fetch.start(5)

        def four():
            up_part(2)

        def five():
            up_part(3)
            fetch.start(6)
            fetch.wait(2, 3)

        def six():
            plane.turn()
            feed_part(0)

        def seven():
            feed_part(1)

        def eight():
            feed_part(2)

        def nine():
            feed_part(3)
            fetch.start(4)

        steps = {1: early, 2: two, 3: three, 4: four, 5: five, 6: six, 7: seven, 8: eight, 9: nine}
        sum_rows_and_spread(place, s, scratch, norm, spread, steps)
        plane.finish(result)
        fetch.wait(4, 5, 6)

    low, full = jnp.bfloat16, jnp.float32
    near, far = in_vmem(), in_any()
    return pl.pallas_call(
        kernel,
        out_shape=(
            shaped((rows, width), full),
            shaped((1, width), full),
            shaped((spread_rows, width), low),
            shaped((block, mat.shape[1]), low),
            shaped((width, wide), low),
            shaped((spread_rows, width), low),
        ),
        in_specs=[near] * 4 + [far] * 5,
        out_specs=[near] * 4 + [far] * 2,
        scratch_shapes=[vmem_like(m) for m in (hidden, grad_up, product, down)]
        + [
            pltpu.VMEM((2, width // 2, wide), low),
            pltpu.VMEM((spread_rows, width), low),
            dma_sems(7),
        ]
        + ReducePlane.scratch(block, mat.shape[1])
        + line_scratch(n_line, rows // CHUNKS, width, CHUNKS),
        compiler_params=comm_params(3),
        name="middle_sums",
    )(terms, after, gain, grad_in, mat, hidden, grad_up, product, down)


class Exchange:
    def __init__(self, place, axis, src, slots, send, recv, local):
        self.p, self.src, self.slots = place, src, slots
        self.over_dp = axis == "dp"
        self.size = place.n_dp if self.over_dp else place.n_line
        self.me = place.d if self.over_dp else place.t
        self.send, self.recv, self.local = send, recv, local

    def copy(self, i):
        to = lax.rem(self.me + i, self.size)
        device = (to, self.p.t) if self.over_dp else (self.p.d, to)
        return remote(
            self.src, self.slots.at[self.me], self.send.at[i - 1], self.recv.at[i - 1], device
        )

    def mine(self):
        return pltpu.make_async_copy(self.src, self.slots.at[self.me], self.local)

    def begin(self):
        for i in range(1, self.size):
            self.copy(i).start()
        self.mine().start()

    def wait(self):
        self.mine().wait()
        for i in range(1, self.size):
            self.copy(i).wait()

    def finish(self):
        self.wait()
        total = self.slots[0]
        for i in range(1, self.size):
            total = total + self.slots[i]
        return total


def last_sums(n_dp, n_line, terms, tokens, gain, grad_after, second, small, mats):
    rows, width = tokens.shape
    count = len(mats)
    per = len(ReducePlane.scratch(16, 128))

    def kernel(*refs):
        s, tok, gain_ref, g_ref, second_ref, small_ref = refs[:6]
        srcs = refs[6 : 6 + count]
        grad_tok, small_out, first_out = refs[6 + count : 9 + count]
        results = refs[9 + count : 9 + 2 * count]
        rest = refs[9 + 2 * count :]
        own_first, row_sum = rest[count * per : count * per + 2]
        slots_a, slots_b, slots_c, slots_d = rest[count * per + 2 : count * per + 6]
        xs, xr, xl = rest[count * per + 6 : count * per + 9]
        scratch = rest[count * per + 9 :]
        place = Place(n_dp, n_line)
        place.meet(True)
        planes = [
            ReducePlane(place, srcs[i], rest[i * per : (i + 1) * per]) for i in range(count)
        ]
        for part in planes:
            part.begin()
        early = Exchange(place, "dp", small_ref, slots_a, xs.at[0], xr.at[0], xl.at[0])
        early.begin()
        gain = Exchange(place, "dp", second_ref, slots_d, xs.at[3], xr.at[3], xl.at[3])
        gain.begin()
        own_first[...] = jnp.zeros_like(own_first)

        def norm(c, here, total):
            grad = total[...]
            grad_rows, normed = norm_back(tok[here].astype(jnp.float32), gain_ref[...], grad)
            own_first[...] += jnp.sum(grad * normed, axis=0, keepdims=True)
            grad_tok[here] = g_ref[here] + grad_rows

        def cores():
            for part in planes:
                part.cores()

        def turn():
            for part in planes:
                part.turn()

        sum_rows_and_spread(place, s, scratch, norm, None, {0: cores, 5: turn})
        first = Exchange(place, "dp", own_first, slots_b, xs.at[1], xr.at[1], xl.at[1])
        first.begin()
        small_out[...] = early.finish()
        row_sum[0:1] = gain.finish()
        row_sum[1:2] = first.finish()
        both = Exchange(place, "tensor", row_sum, slots_c, xs.at[2], xr.at[2], xl.at[2])
        both.begin()
        for part, result in zip(planes, results):
            part.finish(result)
        first_out[...] = both.finish()

    return pl.pallas_call(
        kernel,
        out_shape=(
            shaped((rows, width), jnp.float32),
            shaped(small.shape, jnp.float32),
            shaped((2, width), jnp.float32),
        )
        + tuple(shaped((m.shape[0] // n_dp, m.shape[1]), jnp.bfloat16) for m in mats),
        in_specs=[in_vmem()] * 6 + [in_any()] * count,
        out_specs=[in_vmem()] * (3 + count),
        scratch_shapes=sum([ReducePlane.scratch(m.shape[0] // n_dp, m.shape[1]) for m in mats], [])
        + [
            pltpu.VMEM((1, width), jnp.float32),
            pltpu.VMEM((2, width), jnp.float32),
            pltpu.VMEM((n_dp,) + small.shape, jnp.float32),
            pltpu.VMEM((n_dp, 1, width), jnp.float32),
            pltpu.VMEM((n_line, 2, width), jnp.float32),
            pltpu.VMEM((n_dp, 1, width), jnp.float32),
            dma_sems(4, n_dp),
            dma_sems(4, n_dp),
            dma_sems(4),
        ]
        + line_scratch(n_line, rows // LAST_CHUNKS, width, LAST_CHUNKS),
        compiler_params=comm_params(4),
        name="last_sums",
    )(terms, tokens, gain, grad_after, second, small, *mats)


def loop(count, body, unroll=1):
    def step(i, carry):
        body(i)
        return carry

    lax.fori_loop(0, count, step, None, unroll=unroll)


def tile_rows(i, size, ahead=0):
    return pl.ds(pl.multiple_of(i * size + ahead, 8), size)


def moved_up(values, distance, count):
    size = values.shape[0]
    return pltpu.roll(values, (size - distance) % size, 0)[:count]


def take_lanes(ref, here):
    return jnp.concatenate([ref[c, here] for c in range(ref.shape[0])], axis=1)


def put_lanes(ref, here, values):
    for c in range(ref.shape[0]):
        ref[c, here] = values[:, c * LANES : (c + 1) * LANES]


def gelu_parts(values):
    inner = GELU_C * (values + 0.044715 * (values * values * values))
    tanh = jnp.tanh(inner)
    half = 0.5 * (1.0 + tanh)
    slope = half + 0.5 * values * (1.0 - tanh * tanh) * GELU_C * (
        1.0 + 3.0 * 0.044715 * (values * values)
    )
    return values * half, slope


GELU_C = 0.7978845608028654
RIM = 128
LANES = 128
TILE = 16


def one_minus_exp(values, exponential):
    series = jnp.ones_like(values)
    for term in range(9, 1, -1):
        series = 1.0 + values * (1.0 / term) * series
    return jnp.where(values > -0.35, -values * series, 1.0 - exponential)


def rate_and_scale(pre_recur, soft, start):
    sr = jax.nn.sigmoid(pre_recur)
    log_rate = -rate_scale * sr * soft
    decay = jnp.exp(log_rate)
    rate = jnp.where(start, 0.0, decay)
    scale = jnp.where(start, 1.0, jnp.sqrt(one_minus_exp(2.0 * log_rate, decay * decay)))
    return sr, rate, scale


class RimSwap:
    def __init__(self, place, own):
        self.odd = lax.rem(place.t, 2)
        self.partner = (place.d, place.t + 1 - 2 * self.odd)
        self.first = pl.multiple_of(RIM - RIM * self.odd, RIM)
        self.edge = pl.ds(pl.multiple_of((1 - self.odd) * own + self.odd * RIM, RIM), RIM)
        self.over_there = pl.ds(pl.multiple_of(self.odd * (own + RIM), RIM), RIM)
        self.beyond = pl.ds(pl.multiple_of((1 - self.odd) * (own + RIM), RIM), RIM)

    def block(self, index, size):
        return pl.ds(pl.multiple_of(self.first + index * size, RIM), size)


LATE_SHARE = 4


def recur_forward(
    n_dp,
    n_line,
    tok_all,
    cot,
    to_place,
    to_stored,
    x_full,
    y_full,
    out_full,
    gain,
    gates,
    taps,
    soft,
    flags,
):
    rows, width = tok_all.shape
    count, own = taps.shape
    size = gates.shape[0]
    wide = own + 2 * RIM
    blocks = (wide - RIM) // size
    chunk = rows // 8
    cot_rows = cot.shape[0] - cot.shape[0] // LATE_SHARE
    parts = 1

    def kernel(*refs):
        (tok_far, cot_ref, plc, sto, wx_far, wy_far, wo_far, gain_ref, gates_in, cw, sp, fl) = refs[:12]
        far, gw, cot_all = refs[12:23], refs[23], refs[24]
        tok, wx, wy, wo = refs[25:29]
        results = refs[29:40]
        hp, xext, y, conv_low, conv, pre_r, pre_i, rate, state, merged_st, terms = results
        (h, xf, local, cum, merged, agg, slots, hs, hr, es, er, el, gs, gr, gl) = refs[40:55]
        in_sems, out_sems, cot_held = refs[55:]
        fetch = Fetch(((tok_far, tok), (wx_far, wx), (wy_far, wy), (wo_far, wo)), in_sems)
        store = Fetch(zip(results, far), out_sems)
        fetch.start(0, 1, 2, 3)
        place = Place(n_dp, n_line)
        place.meet(True)
        swap = RimSwap(place, own)
        for side in range(2):
            first = side * wide
            gw[:, first : first + RIM] = jnp.zeros((size, RIM), jnp.bfloat16)
            gw[:, first + RIM : first + RIM + own] = gates_in[:, side * own : (side + 1) * own]
            gw[:, first + RIM + own : first + wide] = jnp.zeros((size, RIM), jnp.bfloat16)
        own_cot = cot_all.at[pl.ds(pl.multiple_of(place.t * cot_rows, 16), cot_rows)]
        cot_ref = cot_ref.at[pl.ds(0, cot_rows)]
        keep = Kept(cot_ref, own_cot, cot_held, gl)
        keep.begin()
        span = cot_rows // parts
        lines = [
            GatherLine(place, cot_all, cot_rows, c * span, span, gs.at[c], gr.at[c])
            for c in range(parts)
        ]
        for c, line in enumerate(lines):
            line.step(0, cot_ref.at[pl.ds(c * span, span)])

        def norm(i):
            here = tile_rows(i, TILE)
            h[here] = rms_scale(tok[here].astype(jnp.float32), gain_ref[...]).astype(jnp.bfloat16)

        fetch.wait(0)
        loop(rows // TILE, norm)
        fetch.wait(1)

        def project(i):
            here = tile_rows(i, 128)
            hp[here] = plain_dot(plc[here], h[...]).astype(jnp.bfloat16)
            xext[tile_rows(i, 128, 16)] = plain_dot(hp[here], wx[...]).astype(jnp.bfloat16)

        loop(rows // 128, project)
        store.start(0)
        edge = remote(
            xext.at[pl.ds(rows, 16)],
            xext.at[pl.ds(0, 16)],
            hs.at[0],
            hr.at[0],
            (lax.rem(place.d + 1, n_dp), place.t),
        )
        edge.start()
        keep.turn()
        for line in lines:
            line.step(1)

        def project_y(i):
            here = tile_rows(i, 128)
            y[here] = plain_dot(hp[here], wy[...])

        fetch.wait(2)
        loop(rows // 128, project_y)
        store.start(2)
        edge.wait()
        top = xext[pl.ds(0, 16)]
        xext[pl.ds(0, 16)] = jnp.where(place.d > 0, top, jnp.zeros_like(top))
        store.start(1)

        def widen(i):
            xf[tile_rows(i, TILE)] = xext[tile_rows(i, TILE)].astype(jnp.float32)

        loop(rows // TILE + 1, widen)

        def convolve(i):
            here = tile_rows(i, TILE)
            near = xf[pl.ds(pl.multiple_of(i * TILE + 8, 8), TILE + 8)]
            same = fl[tile_rows(i, TILE, 8)]
            total = cw[0:1] * near[8:]
            for k in range(1, count):
                total += cw[k : k + 1] * moved_up(near, 8 - k, TILE) * same[:, k : k + 1]
            conv[here] = total
            conv_low[here, RIM : RIM + own] = total.astype(jnp.bfloat16)

        loop(rows // TILE, convolve)
        store.start(4)
        rim = remote(
            conv_low.at[:, swap.edge],
            conv_low.at[:, swap.over_there],
            hs.at[1],
            hr.at[1],
            swap.partner,
        )
        rim.start()
        for i in range(blocks):
            index = lax.rem(i + swap.odd, blocks)
            cols = swap.block(index, size)
            other = pl.ds(pl.multiple_of(wide + swap.first + index * size, RIM), size)
            if i == blocks - 1:
                rim.wait()
            pre_r[:, cols] = plain_dot(conv_low[:, cols], gw[:, cols])
            pre_i[:, cols] = plain_dot(conv_low[:, cols], gw[:, other])

        store.start(3, 5, 6)

        def drive(i):
            here = tile_rows(i, TILE)
            start = fl[tile_rows(i, TILE, 8)][:, 0:1] > 0.0
            own_cols = pl.ds(RIM, own)
            _, decay, scale = rate_and_scale(pre_r[here, own_cols], sp[...], start)
            put_lanes(rate, here, decay)
            put_lanes(local, here, conv[here] * jax.nn.sigmoid(pre_i[here, own_cols]) * scale)

        loop(rows // TILE, drive)
        store.start(7)
        for line in lines:
            line.step(2)
        groups = own // LANES

        def scan(i, carry):
            here = pl.ds(i, 8, chunk)
            result = []
            for c in range(groups):
                product, total = carry[c]
                r = rate[c, here]
                product = product * r
                total = total * r + local[c, here]
                cum[c, here] = product
                local[c, here] = total
                result.append((product, total))
            return tuple(result)

        blank = (jnp.ones((8, LANES), jnp.float32), jnp.zeros((8, LANES), jnp.float32))
        lax.fori_loop(0, chunk, scan, (blank,) * groups)
        product, total = jnp.ones((1, own), jnp.float32), jnp.zeros((1, own), jnp.float32)
        for j in range(8):
            last = pl.ds(j * chunk + chunk - 1, 1)
            total = take_lanes(local, last) + take_lanes(cum, last) * total
            product = product * take_lanes(cum, last)
        agg[0:1] = product
        agg[1:2] = total
        swap_all = Exchange(place, "dp", agg, slots, es, er, el)
        swap_all.begin()
        swap_all.wait()
        entry = jnp.zeros((1, own), jnp.float32)
        for q in range(n_dp):
            longer = slots[q, 1:2] + slots[q, 0:1] * entry
            entry = jnp.where(q < place.d, longer, entry)
        state[pl.ds(0, 8)] = jnp.broadcast_to(entry, (8, own))
        for j in range(8):

            def settle(i, entry=entry):
                here = tile_rows(i, TILE, j * chunk)
                values = take_lanes(local, here) + take_lanes(cum, here) * entry
                state[tile_rows(i, TILE, j * chunk + 8)] = values
                merged[here] = (values * gelu_parts(y[here])[0]).astype(jnp.bfloat16)

            loop(chunk // TILE, settle)
            last = pl.ds(j * chunk + chunk - 1, 1)
            entry = take_lanes(local, last) + take_lanes(cum, last) * entry
        store.start(8)
        merged_st[...] = plain_dot(sto[...], merged[...]).astype(jnp.bfloat16)

        store.start(9)
        fetch.wait(3)

        def mix(i):
            some = tile_rows(i, 512)
            terms[:, pl.ds(pl.multiple_of(i * 512, 512), 512)] = times_trans(
                merged_st[...], wo[some, :]
            ).astype(jnp.bfloat16)

        loop(width // 512, mix)
        for line in lines:
            line.finish()
        keep.finish()
        store.start(10)
        store.wait(*range(11))

    low, full = jnp.bfloat16, jnp.float32
    results = (
        shaped((rows, width), low),
        shaped((rows + 16, own), low),
        shaped((rows, own), full),
        shaped((rows, wide), low),
        shaped((rows, own), full),
        shaped((rows, wide), full),
        shaped((rows, wide), full),
        shaped((own // LANES, rows, LANES), full),
        shaped((rows + 8, own), full),
        shaped((rows, own), low),
        shaped((rows, width), low),
    )
    near, far = in_vmem(), in_any()
    return pl.pallas_call(
        kernel,
        out_shape=results
        + (shaped((size, 2 * wide), low), shaped((n_line * cot_rows, width), low)),
        in_specs=[far, far, near, near, far, far, far] + [near] * 5,
        out_specs=[far] * 11 + [near, far],
        scratch_shapes=[vmem_like(m) for m in (tok_all, x_full, y_full, out_full) + results]
        + [
            pltpu.VMEM((rows, width), low),
            pltpu.VMEM((rows + 16, own), full),
            pltpu.VMEM((own // LANES, rows, LANES), full),
            pltpu.VMEM((own // LANES, rows, LANES), full),
            pltpu.VMEM((rows, own), low),
            pltpu.VMEM((2, own), full),
            pltpu.VMEM((n_dp, 2, own), full),
            dma_sems(2),
            dma_sems(2),
            dma_sems(n_dp),
            dma_sems(n_dp),
            pltpu.SemaphoreType.DMA,
            dma_sems(parts, 2, n_line - 1),
            dma_sems(parts, 2, n_line - 1),
            dma_sems(2),
            dma_sems(4),
            dma_sems(11),
            pltpu.VMEM((cot_rows, width), low),
        ],
        compiler_params=comm_params(5),
        name="recur_forward",
    )(
        tok_all,
        cot,
        to_place,
        to_stored,
        x_full,
        y_full,
        out_full,
        gain,
        gates,
        taps,
        soft,
        flags,
    )


class RowProducts:
    def __init__(self, left, right, far, stage, sems):
        self.left, self.right, self.far, self.stage, self.sems = left, right, far, stage, sems
        self.part = stage.shape[1]
        self.count = far.shape[0] // self.part

    def slot(self, i):
        return self.stage.at[i % 2, :, pl.ds(0, self.far.shape[1])]

    def copy(self, i):
        some = pl.ds(i * self.part, self.part)
        return pltpu.make_async_copy(self.slot(i), self.far.at[some], self.sems.at[i])

    def run(self):
        for i in range(self.count):
            if i >= 2:
                self.copy(i - 2).wait()
            some = pl.ds(i * self.part, self.part)
            self.slot(i)[...] = trans_times(self.left[:, some], self.right[...]).astype(
                jnp.bfloat16
            )
            self.copy(i).start()

    def finish(self):
        self.copy(self.count - 2).wait()
        self.copy(self.count - 1).wait()


def recur_backward(
    n_dp,
    n_line,
    mixer_in,
    to_place,
    to_stored,
    x_full,
    y_full,
    out_full,
    gates,
    taps,
    soft,
    slope,
    flags,
    kept,
    weight_terms,
    row_terms,
    hidden_place,
    merged_stored,
):
    rows, width = mixer_in.shape
    count, own = taps.shape
    size = gates.shape[0]
    wide = own + 2 * RIM
    blocks = (wide - RIM) // size
    chunk = rows // 8
    own_rows = rows // n_line
    parts = 4
    span = own_rows // parts

    def kernel(*refs):
        (mix_far, plc, sto, wx_far, wy_far, wo_far, gw, cw, sp, sg, fl) = refs[:11]
        kept_far, weights, feed_far, hp_far, merged_far = refs[11:19], *refs[19:23]
        (gate_grads, tap_grads, terms_far, weight_sum, row_sum) = refs[23:28]
        out_far, xy_far = refs[28:30]
        mix, wy, wo, feed, merged = refs[30:35]
        (xext, y, conv_low, conv, pre_r, pre_i, rate, state) = refs[35:43]
        (gxy, mp, gm, lam, reach, gp_r, gp_i, grad, spread, rim_out, rim_in) = refs[43:54]
        (ret_out, ret_in, tap_sums, decay_sums, ends, agg, slots) = refs[54:61]
        (hs, hr, es, er, el, in_sems, out_sems, inbox, ls, lr, total) = refs[61:72]
        stage, stage_sems = refs[72:74]
        hp, terms, wx = mix, mix, wo
        fetch = Fetch(
            [
                (mix_far, mix),
                (wo_far, wo),
                (kept_far[1], y),
                (kept_far[7], state),
                (kept_far[6], rate),
                (kept_far[4], pre_r),
                (kept_far[5], pre_i),
                (kept_far[3], conv),
                (kept_far[2], conv_low),
                (kept_far[0], xext),
                (wx_far, wx),
                (wy_far, wy),
                (feed_far, feed),
                (merged_far, merged),
                (hp_far, hp),
            ],
            in_sems,
        )
        fetch.start(12, 0, 1, 13)
        store = Fetch(((terms, terms_far),), out_sems)
        out_rows = RowProducts(mix, merged, out_far, stage, stage_sems.at[0])
        xy_rows = RowProducts(hp, gxy, xy_far, stage, stage_sems.at[1])
        place = Place(n_dp, n_line)
        place.meet(True)
        plane = ReducePlane(place, weights, refs[74:])
        plane.begin()
        lines = [
            ReduceLine(place, feed, own_rows, c * span, span, inbox.at[c], ls.at[c], lr.at[c])
            for c in range(parts)
        ]

        def send(c):
            if c > 0:
                lines[c - 1].sent()
            if c < parts:
                lines[c].ends()

        def add_up(c):
            lines[c].total(total)
            row_sum[pl.ds(c * span, span)] = total[...].astype(jnp.bfloat16)

        fetch.wait(12)
        send(0)
        fetch.start(*range(2, 10), 11)
        swap = RimSwap(place, own)
        own_cols = pl.ds(RIM, own)

        def project(i):
            here = tile_rows(i, 128)
            mp[here] = plain_dot(plc[here], mix[...]).astype(jnp.bfloat16)
            gm[here] = plain_dot(mp[here], wo[...])

        fetch.wait(0, 1)
        loop(rows // 128, project)
        fetch.start(10)
        fetch.wait(13)
        out_rows.run()
        fetch.start(14)

        def split(i):
            here = tile_rows(i, TILE)
            branch, slope_y = gelu_parts(y[here])
            grads = gm[here]
            put_lanes(lam, here, grads * branch)
            values = state[tile_rows(i, TILE, 8)]
            gxy[here, own:] = (grads * values * slope_y).astype(jnp.bfloat16)

        fetch.wait(2, 3)
        loop(rows // TILE, split)
        send(1)
        lines[0].hop(0)
        fetch.wait(4)
        groups = own // LANES

        def scan(i, carry):
            here = pl.ds(chunk - 1 - i, 8, chunk)
            result = []
            for c in range(groups):
                product, message = carry[c]
                r = rate[c, here]
                value = lam[c, here] + message
                lam[c, here] = value
                reach[c, here] = product
                result.append((product * r, value * r))
            return tuple(result)

        blank = (jnp.ones((8, LANES), jnp.float32), jnp.zeros((8, LANES), jnp.float32))
        done = lax.fori_loop(0, chunk, scan, (blank,) * groups)
        for c in range(groups):
            lanes = pl.ds(c * LANES, LANES)
            ends[0, :, lanes] = done[c][0]
            ends[1, :, lanes] = done[c][1]
        product, message = jnp.ones((1, own), jnp.float32), jnp.zeros((1, own), jnp.float32)
        for j in reversed(range(8)):
            message = ends[1, j : j + 1] + ends[0, j : j + 1] * message
            product = product * ends[0, j : j + 1]
        agg[0:1] = product
        agg[1:2] = message
        swap_all = Exchange(place, "dp", agg, slots, es, er, el)
        swap_all.begin()
        plane.cores()
        swap_all.wait()
        lines[0].hop(1)
        entry = jnp.zeros((1, own), jnp.float32)
        for q in reversed(range(n_dp)):
            longer = slots[q, 1:2] + slots[q, 0:1] * entry
            entry = jnp.where(q > place.d, longer, entry)
        fetch.wait(5, 6, 7)
        for ref in (tap_sums, decay_sums):
            ref[...] = jnp.zeros_like(ref)
        for ref in (gp_r, gp_i):
            ref[:, 0:RIM] = jnp.zeros((rows, RIM), jnp.bfloat16)
            ref[:, RIM + own :] = jnp.zeros((rows, RIM), jnp.bfloat16)
        grad[pl.ds(0, 8)] = jnp.zeros((8, own), jnp.float32)
        grad[pl.ds(rows + 8, 8)] = jnp.zeros((8, own), jnp.float32)
        for j in reversed(range(8)):

            def back(i, entry=entry):
                here = tile_rows(i, TILE, j * chunk)
                flag = fl[tile_rows(i, TILE, j * chunk + 8)]
                start = flag[:, 0:1] > 0.0
                values = take_lanes(lam, here) + take_lanes(reach, here) * entry
                before = moved_up(
                    state[pl.ds(pl.multiple_of(j * chunk + i * TILE, 8), TILE + 8)], 7, TILE
                )
                sr, decay, scale = rate_and_scale(pre_r[here, own_cols], sp[...], start)
                si = jax.nn.sigmoid(pre_i[here, own_cols])
                block = conv[here]
                driven = values * si
                log_grad = values * before * decay - block * driven * (decay * decay) / scale
                log_grad = jnp.where(start, 0.0, log_grad)
                inner = sr * log_grad
                gp_r[here, own_cols] = (
                    -rate_scale * sp[...] * inner * (1.0 - sr)
                ).astype(jnp.bfloat16)
                gp_i[here, own_cols] = (driven * block * (1.0 - si) * scale).astype(jnp.bfloat16)
                grad[tile_rows(i, TILE, j * chunk + 8)] = driven * scale
                decay_sums[...] += inner[:8] + inner[8:]

            loop(chunk // TILE, back)
            if j == 4:
                send(2)
                lines[1].hop(0)
            entry = ends[1, j : j + 1] + ends[0, j : j + 1] * entry
        lines[1].hop(1)
        add_up(0)

        for i in range(blocks):
            index = lax.rem(i + 2 - 2 * swap.odd, blocks)
            cols = swap.block(index, size)
            other = pl.ds(pl.multiple_of(wide + swap.first + index * size, RIM), size)
            spread[:, cols] = times_trans(gp_r[:, cols], gw[:, cols]) + times_trans(
                gp_i[:, cols], gw[:, other]
            )
            if i == 0:
                rim_out[...] = spread[:, swap.beyond].astype(jnp.bfloat16)
                rim = remote(rim_out, rim_in, hs.at[0], hr.at[0], swap.partner)
                rim.start()
        send(3)
        lines[2].hop(0)
        rim.wait()
        shared = pl.ds(pl.multiple_of((1 - swap.odd) * (own - RIM), RIM), RIM)

        def join(i):
            here = tile_rows(i, TILE)
            there = tile_rows(i, TILE, 8)
            grad[there] += spread[here, own_cols]
            grad[there, shared] += rim_in[here].astype(jnp.float32)

        loop(rows // TILE, join)

        near = grad[pl.ds(0, 16)]
        back_rows = jnp.zeros((8, own), jnp.float32)
        for k in range(1, count):
            masked = near * fl[pl.ds(0, 16)][:, k : k + 1]
            back_rows += cw[k : k + 1] * moved_up(masked, k, 8)
        ret_out[...] = back_rows
        ret = remote(
            ret_out,
            ret_in,
            hs.at[1],
            hr.at[1],
            (lax.rem(place.d + n_dp - 1, n_dp), place.t),
        )
        ret.start()
        fetch.wait(8)
        for i in range(blocks):
            cols = swap.block(i, size)
            spread[0:size, cols] = trans_times(conv_low[:, cols], gp_r[:, cols])
            spread[size : 2 * size, cols] = trans_times(conv_low[:, cols], gp_i[:, cols])
        gate_grads[:, 0:own] = spread[0:size, own_cols].astype(jnp.bfloat16)
        gate_grads[:, own:] = spread[size : 2 * size, own_cols].astype(jnp.bfloat16)

        def taps_back(i, added=None):
            here = tile_rows(i, TILE)
            start = pl.ds(pl.multiple_of(i * TILE + 8, 8), TILE + 8)
            after = grad[start]
            flag = fl[start]
            behind = xext[pl.ds(pl.multiple_of(i * TILE, 16), 2 * TILE)].astype(jnp.float32)
            total = cw[0:1] * after[:TILE]
            for k in range(count):
                if k > 0:
                    masked = after * flag[:, k : k + 1]
                    total += cw[k : k + 1] * moved_up(masked, k, TILE)
                    mine = masked[:TILE]
                else:
                    mine = after[:TILE]
                term = mine * moved_up(behind, 16 - k, TILE)
                tap_sums[k] += term[:8] + term[8:]
            if added is not None:
                total = total + jnp.concatenate([jnp.zeros((8, own), jnp.float32), added], axis=0)
            gxy[here, 0:own] = total.astype(jnp.bfloat16)

        fetch.wait(9)
        loop(rows // TILE - 1, taps_back)
        lines[2].hop(1)
        add_up(1)
        ret.wait()
        taps_back(rows // TILE - 1, jnp.where(place.d < n_dp - 1, ret_in[...], 0.0))
        tap_grads[...] = jnp.zeros_like(tap_grads)
        for k in range(count):
            tap_grads[k : k + 1] = jnp.sum(tap_sums[k], axis=0, keepdims=True)
        tap_grads[count : count + 1] = (
            rate_scale * sg[...] * jnp.sum(decay_sums[...], axis=0, keepdims=True)
        )

        fetch.wait(14)
        out_rows.finish()
        plane.turn()
        xy_rows.run()
        send(4)
        lines[3].hop(0)

        def restore(i):
            here = tile_rows(i, 128)
            mp[here, 0 : 2 * own] = plain_dot(sto[here], gxy[...]).astype(jnp.bfloat16)

        loop(rows // 128, restore)

        def spread_back(i):
            some = tile_rows(i, 512)
            terms[:, pl.ds(pl.multiple_of(i * 512, 512), 512)] = (
                times_trans(mp[:, 0:own], wx[some]) + times_trans(mp[:, own : 2 * own], wy[some])
            ).astype(jnp.bfloat16)

        fetch.wait(10, 11)
        loop(width // 512, spread_back)
        store.start(0)
        lines[3].hop(1)
        add_up(2)
        plane.finish(weight_sum)
        add_up(3)
        for line in lines:
            line.finish()
        xy_rows.finish()
        store.wait(0)

    low, full = jnp.bfloat16, jnp.float32
    block = weight_terms.shape[0] // n_dp
    near, far = in_vmem(), in_any()
    return pl.pallas_call(
        kernel,
        out_shape=(
            shaped((size, 2 * own), low),
            shaped((8, own), full),
            shaped((rows, width), low),
            shaped((block, weight_terms.shape[1]), low),
            shaped((own_rows, width), low),
            shaped((width, own), low),
            shaped((width, 2 * own), low),
        ),
        in_specs=[far, near, near, far, far, far] + [near] * 5 + [far] * 12,
        out_specs=[near, near, far, near, near, far, far],
        scratch_shapes=[
            vmem_like(m) for m in (mixer_in, y_full, out_full, row_terms, merged_stored, *kept)
        ]
        + [
            pltpu.VMEM((rows, 2 * own), low),
            pltpu.VMEM((rows, width), low),
            pltpu.VMEM((rows, own), full),
            pltpu.VMEM((own // LANES, rows, LANES), full),
            pltpu.VMEM((own // LANES, rows, LANES), full),
            pltpu.VMEM((rows, wide), low),
            pltpu.VMEM((rows, wide), low),
            pltpu.VMEM((rows + 16, own), full),
            pltpu.VMEM((rows, wide), full),
            pltpu.VMEM((rows, RIM), low),
            pltpu.VMEM((rows, RIM), low),
            pltpu.VMEM((8, own), full),
            pltpu.VMEM((8, own), full),
            pltpu.VMEM((count, 8, own), full),
            pltpu.VMEM((8, own), full),
            pltpu.VMEM((2, 8, own), full),
            pltpu.VMEM((2, own), full),
            pltpu.VMEM((n_dp, 2, own), full),
            dma_sems(2),
            dma_sems(2),
            dma_sems(n_dp),
            dma_sems(n_dp),
            pltpu.SemaphoreType.DMA,
            dma_sems(15),
            dma_sems(1),
            pltpu.VMEM((parts, 2, n_line - 1, span, width), low),
            dma_sems(parts, 2, n_line - 1),
            dma_sems(parts, 2, n_line - 1),
            pltpu.VMEM((span, width), full),
            pltpu.VMEM((2, width // 5, 2 * own), low),
            dma_sems(2, 5),
        ]
        + ReducePlane.scratch(block, weight_terms.shape[1]),
        compiler_params=comm_params(6),
        name="recur_backward",
    )(
        mixer_in,
        to_place,
        to_stored,
        x_full,
        y_full,
        out_full,
        gates,
        taps,
        soft,
        slope,
        flags,
        *kept,
        weight_terms,
        row_terms,
        hidden_place,
        merged_stored,
    )


def column_parts(width, size=768):
    return [(c, min(size, width - c)) for c in range(0, width, size)]


def feed_forward(n_dp, n_line, hidden, gate, up, down, grads, grad_own):
    rows, width = hidden.shape
    units = gate.shape[1]
    own_rows = grad_own.shape[0]
    ready = grads.shape[0] // n_line
    late = own_rows - ready
    part = width // 4

    def kernel(*refs):
        hid_far, wg_far, wu_far, wd_far, grads_far, own_far = refs[:6]
        product_far, gup_far, back_far, gdown_far, ggate_far = refs[6:11]
        hid, wg, wu, wd, grad, slope, branch, product, ggate, gup, stage, back = refs[11:23]
        in_sems, out_sems, stage_sems, ls, lr = refs[23:]
        place = Place(n_dp, n_line)
        pairs = [(hid_far, hid), (wg_far, wg), (wu_far, wu), (wd_far, wd)]
        pairs += [
            (grads_far.at[pl.ds(q * ready, ready)], grad.at[pl.ds(q * own_rows, ready)])
            for q in range(n_line)
        ]
        mine = pl.ds(pl.multiple_of(place.t * own_rows + ready, 16), late)
        pairs.append((own_far.at[pl.ds(ready, late)], grad.at[mine]))
        fetch = Fetch(pairs, in_sems)
        fetch.start(*range(len(pairs)))
        store = Fetch(((product, product_far), (gup, gup_far), (back, back_far)), out_sems)
        place.meet()
        line = GatherLine(place, grad, own_rows, ready, late, ls, lr)
        line.step(0, own_far.at[pl.ds(ready, late)])
        columns = column_parts(units)
        fetch.wait(0, 1)
        for c, size in columns:
            cols = pl.ds(c, size)

            def gates(i, cols=cols):
                here = tile_rows(i, 256)
                branch[here, cols] = plain_dot(hid[here], wg[:, cols])

            loop(rows // 256, gates)
        line.step(1)
        fetch.wait(2)
        for c, size in columns:
            cols = pl.ds(c, size)

            def ups(i, cols=cols):
                here = tile_rows(i, 256)
                value = plain_dot(hid[here], wu[:, cols])
                active, bend = gelu_parts(branch[here, cols])
                product[here, cols] = (active * value).astype(jnp.bfloat16)
                branch[here, cols] = active
                slope[here, cols] = bend * value

            loop(rows // 256, ups)
        store.start(0)
        line.step(2)
        fetch.wait(*range(4, len(pairs)))
        line.finish()

        down_rows = RowProducts(grad, product, gdown_far, stage, stage_sems.at[0])
        down_rows.run()
        fetch.wait(3)
        for c, size in columns:
            cols = pl.ds(c, size)

            def backs(i, cols=cols):
                here = tile_rows(i, 256)
                value = plain_dot(grad[here], wd[:, cols])
                ggate[here, cols] = (value * slope[here, cols]).astype(jnp.bfloat16)
                gup[here, cols] = (value * branch[here, cols]).astype(jnp.bfloat16)

            loop(rows // 256, backs)
        store.start(1)
        for i in range(4):
            some = pl.ds(i * part, part)
            back[:, some] = (
                times_trans(ggate[...], wg[some]) + times_trans(gup[...], wu[some])
            ).astype(jnp.bfloat16)
        store.start(2)
        down_rows.finish()
        gate_rows = RowProducts(hid, ggate, ggate_far, stage, stage_sems.at[1])
        gate_rows.run()
        gate_rows.finish()
        store.wait(0, 1, 2)

    low, full = jnp.bfloat16, jnp.float32
    return pl.pallas_call(
        kernel,
        out_shape=(
            shaped((rows, units), low),
            shaped((rows, units), low),
            shaped((rows, width), low),
            shaped((width, units), low),
            shaped((width, units), low),
        ),
        in_specs=[in_any()] * 6,
        out_specs=[in_any()] * 5,
        scratch_shapes=[vmem_like(m) for m in (hidden, gate, up, down)]
        + [
            pltpu.VMEM((n_line * own_rows, width), low),
            pltpu.VMEM((rows, units), full),
            pltpu.VMEM((rows, units), full),
            pltpu.VMEM((rows, units), low),
            pltpu.VMEM((rows, units), low),
            pltpu.VMEM((rows, units), low),
            pltpu.VMEM((2, part, units), low),
            pltpu.VMEM((rows, width), low),
            dma_sems(5 + n_line),
            dma_sems(3),
            dma_sems(2, 4),
            dma_sems(2, n_line - 1),
            dma_sems(2, n_line - 1),
        ],
        compiler_params=comm_params(7),
        name="feed_forward",
    )(hidden, gate, up, down, grads, grad_own)


def matches(mesh):
    return mesh.shape["dp"] == 8 and mesh.shape["tensor"] == 4


def local_blocks(
    tokens,
    norm_gain,
    x_weight,
    y_weight,
    conv_weight,
    recur_gate_weight,
    input_gate_weight,
    decay_param,
    out_weight,
    mlp_gain,
    gate_weight,
    up_weight,
    down_weight,
    seq_lengths,
    token_order,
    cotangent,
):
    n_dp, n_tensor = lax.axis_size("dp"), lax.axis_size("tensor")
    tensor_index = lax.axis_index("tensor")
    dp_index = lax.axis_index("dp")
    tok_rows, width = tokens.shape
    row_count = tok_rows * n_tensor
    own_width = conv_weight.shape[1]
    kernel_taps = conv_weight.shape[0]
    edge_rows = kernel_taps - 1
    dp_width = norm_gain.shape[0]
    gate_rows = recur_gate_weight.shape[0]
    own_start = tensor_index * tok_rows

    gains = jnp.concatenate([norm_gain, mlp_gain])
    spare = gate_rows * 128 - gains.shape[0]
    gains = jnp.pad(gains, (0, spare)).reshape(gate_rows, 128)
    minor = jnp.concatenate([recur_gate_weight, input_gate_weight, gains], axis=1)
    own_order = (token_order - dp_index * row_count).astype(jnp.int32)
    order_rows = jnp.broadcast_to(own_order[None, :], (8, tok_rows))
    x_full, y_full, out_full, minor_full, tok_all, order_full = first_gather(
        n_dp, n_tensor, (x_weight, y_weight, out_weight.T, minor), tokens, order_rows
    )
    late_up, late_down, _ = lax.optimization_barrier((up_weight, down_weight.T, tok_all))
    up_full = lax.all_gather(late_up, "dp", axis=0, tiled=True)
    down_full = lax.all_gather(late_down, "dp", axis=0, tiled=True)
    order_all = order_full.reshape(n_tensor, 8, tok_rows)[:, 0].reshape(row_count)
    gain_rows = minor_full[:, 2 * own_width :].reshape(n_dp, -1)
    first_gain = gain_rows[:, :dp_width].reshape(1, width).astype(jnp.float32)
    second_gain = gain_rows[:, dp_width : 2 * dp_width].reshape(1, width).astype(jnp.float32)
    row_index = jnp.arange(row_count, dtype=jnp.int32)
    hits = row_index[:, None] == order_all[None, :]
    to_place = hits.astype(jnp.bfloat16)
    to_stored = (order_all[:, None] == row_index[None, :]).astype(jnp.bfloat16)
    places = dp_index * row_count + jnp.arange(-8, row_count + 8, dtype=jnp.int32)
    inside = (jnp.arange(row_count + 16) >= 8) & (jnp.arange(row_count + 16) < row_count + 8)
    ends = jnp.cumsum(seq_lengths)
    segment = segment_of(places, ends)
    starts = (places == 0) | (segment != segment_of(places - 1, ends))
    columns = [starts] + [
        segment_of(places - shift, ends) == segment for shift in range(1, kernel_taps)
    ]
    columns += [jnp.zeros_like(starts)] * (8 - len(columns))
    flags = (jnp.stack(columns, axis=1) & inside[:, None]).astype(jnp.float32)
    live_own = (token_order < ends[-1]).astype(jnp.float32)
    grad_in_own = (cotangent.astype(jnp.float32) * live_own[:, None]).astype(jnp.bfloat16)
    soft = jax.nn.softplus(-decay_param).reshape(1, own_width)
    slope = jax.nn.sigmoid(-decay_param).reshape(1, own_width)
    hidden_place, *kept, merged_stored, mixer_terms, gates_wide, grad_rows = recur_forward(
        n_dp,
        n_tensor,
        tok_all,
        grad_in_own,
        to_place,
        to_stored,
        x_full,
        y_full,
        out_full,
        first_gain,
        minor_full,
        conv_weight,
        soft,
        flags,
    )
    after_own, hidden_two, gate_full = middle_gather(
        n_dp, n_tensor, mixer_terms, tokens, second_gain, (gate_weight,)
    )
    product, grad_up_pre, back_terms, grad_down, grad_gate = feed_forward(
        n_dp,
        n_tensor,
        hidden_two,
        gate_full,
        up_full,
        down_full,
        grad_rows,
        grad_in_own,
    )
    down_sum = lax.psum_scatter(grad_down, "dp", scatter_dimension=0, tiled=True)
    grad_after_own, second_part, mixer_in, gate_sum, grad_up, feed_terms = middle_sums(
        n_dp,
        n_tensor,
        back_terms,
        after_own,
        second_gain,
        grad_in_own,
        grad_gate,
        hidden_two,
        grad_up_pre,
        product,
        down_full,
    )
    (
        gate_grads,
        tap_grads,
        one_terms,
        up_sum,
        feed_out,
        grad_out_mat,
        grad_xy_mat,
    ) = recur_backward(
        n_dp,
        n_tensor,
        mixer_in,
        to_place,
        to_stored,
        x_full,
        y_full,
        out_full,
        gates_wide,
        conv_weight,
        soft,
        slope,
        flags,
        kept,
        grad_up,
        feed_terms,
        hidden_place,
        merged_stored,
    )
    output = (after_own + feed_out.astype(jnp.float32)) * live_own[:, None]
    output = output.astype(jnp.bfloat16)
    grad_tokens, small_sum, gain_sums, xy_sum, out_sum, gates_sum = last_sums(
        n_dp,
        n_tensor,
        one_terms,
        tokens,
        first_gain,
        grad_after_own,
        second_part,
        tap_grads,
        (grad_xy_mat, grad_out_mat, gate_grads),
    )
    xy_sum, gates_sum = xy_sum.astype(jnp.float32), gates_sum.astype(jnp.float32)
    own_gains = lax.dynamic_slice_in_dim(gain_sums, dp_index * dp_width, dp_width, 1)
    return (
        output,
        grad_tokens,
        own_gains[1],
        xy_sum[:, :own_width],
        xy_sum[:, own_width:],
        small_sum[:kernel_taps],
        gates_sum[:, :own_width],
        gates_sum[:, own_width:],
        small_sum[kernel_taps],
        out_sum.astype(jnp.float32).T,
        own_gains[0],
        gate_sum.astype(jnp.float32),
        up_sum.astype(jnp.float32),
        down_sum.astype(jnp.float32).T,
    )


def solution(mesh):
    in_specs = (
        P(("dp", "tensor"), None),
        P("dp"),
        P("dp", "tensor"),
        P("dp", "tensor"),
        P(None, "tensor"),
        P("dp", "tensor"),
        P("dp", "tensor"),
        P("tensor"),
        P("tensor", "dp"),
        P("dp"),
        P("dp", "tensor"),
        P("dp", "tensor"),
        P("tensor", "dp"),
        P(),
        P(("dp", "tensor")),
        P(("dp", "tensor"), None),
    )
    out_specs = (
        P(("dp", "tensor"), None),
        P(("dp", "tensor"), None),
        P("dp"),
        P("dp", "tensor"),
        P("dp", "tensor"),
        P(None, "tensor"),
        P("dp", "tensor"),
        P("dp", "tensor"),
        P("tensor"),
        P("tensor", "dp"),
        P("dp"),
        P("dp", "tensor"),
        P("dp", "tensor"),
        P("tensor", "dp"),
    )
    fits = matches(mesh)
    local = local_blocks if fits else local_general
    return jax.shard_map(local, mesh=mesh, in_specs=in_specs, out_specs=out_specs, check_vma=False)
```

```python
import jax
import jax.numpy as jnp
from jax import lax
from jax.experimental import pallas as pl
from jax.experimental.pallas import tpu as pltpu
from jax.sharding import PartitionSpec as P

epsilon = 1e-06
rate_scale = 8.0


def from_behind(block, axis, distance):
    devices = range(lax.axis_size(axis))
    route = [(i - distance, i) for i in devices if i - distance in devices]
    return lax.ppermute(block, axis, route)


def extended_2(array, sides, width):
    for axis, dim in sides:
        size, length = (lax.axis_size(axis), array.shape[dim])
        up = [(i, (i + 1) % size) for i in range(size - 1)]
        down = [(j, i) for i, j in up]
        last = lax.slice_in_dim(array, length - width, length, axis=dim)
        leading = lax.slice_in_dim(array, 0, width, axis=dim)
        before = lax.ppermute(last, axis, up)
        after = lax.ppermute(leading, axis, down)
        array = jnp.concatenate([before, array, after], axis=dim)
    return array


def entering(value, axis, join, neutral, backward):
    count, mine = (lax.axis_size(axis), lax.axis_index(axis))
    pieces = jax.tree.map(lambda part: lax.all_gather(part, axis), value)
    if backward:
        pieces = jax.tree.map(lambda part: part[::-1], pieces)
        mine = count - 1 - mine
    total = jax.tree.map(
        lambda part, zero: jnp.full_like(part, 0) + jnp.asarray(zero, part.dtype), value, neutral
    )

    def lap(position, total):
        longer = join(total, jax.tree.map(lambda part: part[position], pieces))
        return jax.tree.map(lambda new, old: jnp.where(position < mine, new, old), longer, total)

    return lax.fori_loop(0, count - 1, lap, total)


def rms_scale(values, gain):
    return values * lax.rsqrt(jnp.mean(values * values, axis=-1, keepdims=True) + epsilon) * gain


def norm_back(values, gain, grad):
    inv_root = lax.rsqrt(jnp.mean(values * values, axis=-1, keepdims=True) + epsilon)
    normed = values * inv_root
    upstream = grad * gain
    grad_values = inv_root * (
        upstream - normed * jnp.mean(upstream * normed, axis=-1, keepdims=True)
    )
    return (grad_values, normed)


def segment_of(places, ends):
    return jnp.sum((ends[None, :] <= places[:, None]).astype(jnp.int32), axis=1)


def pair_step(early, later):
    return (early[0] * later[0], later[0] * early[1] + later[1])


def plain_dot(left, right):
    return jnp.dot(left, right, preferred_element_type=jnp.float32)


def times_trans(left, right):
    return lax.dot_general(
        left, right, (((1,), (1,)), ((), ())), preferred_element_type=jnp.float32
    )


def trans_times(left, right):
    return lax.dot_general(
        left, right, (((0,), (0,)), ((), ())), preferred_element_type=jnp.float32
    )


def gelu_tanh(values):
    return jax.nn.gelu(values, approximate=True)


def collect(
    norm_gain,
    mlp_gain,
    x_weight,
    y_weight,
    recur_gate_weight,
    input_gate_weight,
    gate_weight,
    up_weight,
    out_weight,
    down_weight,
):
    return (
        lax.all_gather(norm_gain, "dp", axis=0, tiled=True),
        lax.all_gather(mlp_gain, "dp", axis=0, tiled=True),
        lax.all_gather(x_weight, "dp", axis=0, tiled=True),
        lax.all_gather(y_weight, "dp", axis=0, tiled=True),
        lax.all_gather(recur_gate_weight, "dp", axis=0, tiled=True),
        lax.all_gather(input_gate_weight, "dp", axis=0, tiled=True),
        lax.all_gather(gate_weight, "dp", axis=0, tiled=True),
        lax.all_gather(up_weight, "dp", axis=0, tiled=True),
        lax.all_gather(out_weight, "dp", axis=1, tiled=True),
        lax.all_gather(down_weight, "dp", axis=1, tiled=True),
    )


def row_sums(term_rows, tok_rows):
    return lax.psum_scatter(
        term_rows(jnp.int32(0), lax.axis_size("tensor") * tok_rows).astype(jnp.bfloat16),
        "tensor",
        scatter_dimension=0,
        tiled=True,
    ).astype(jnp.float32)


def spread_rows(values):
    return lax.all_gather(values, "tensor", axis=0, tiled=True)


def local_general(
    tokens,
    norm_gain,
    x_weight,
    y_weight,
    conv_weight,
    recur_gate_weight,
    input_gate_weight,
    decay_param,
    out_weight,
    mlp_gain,
    gate_weight,
    up_weight,
    down_weight,
    seq_lengths,
    token_order,
    cotangent,
):
    n_tensor = lax.axis_size("tensor")
    tensor_index = lax.axis_index("tensor")
    dp_index = lax.axis_index("dp")
    tok_rows = tokens.shape[0]
    row_count = tok_rows * n_tensor
    own_width = conv_weight.shape[1]
    kernel_taps = conv_weight.shape[0]
    edge_rows = kernel_taps - 1
    dp_width = norm_gain.shape[0]
    own_start = tensor_index * tok_rows
    shards = (
        norm_gain,
        mlp_gain,
        x_weight,
        y_weight,
        recur_gate_weight,
        input_gate_weight,
        gate_weight,
        up_weight,
        out_weight,
        down_weight,
    )
    (
        gain_one,
        gain_two,
        x_full,
        y_full,
        recur_full,
        input_full,
        gate_full,
        up_full,
        out_full,
        down_full,
    ) = collect(*shards)
    block_size = recur_full.shape[0]
    first_gain = gain_one.astype(jnp.float32)
    second_gain = gain_two.astype(jnp.float32)
    both_gates = jnp.concatenate([recur_full, input_full], axis=1)
    tok_own = tokens.astype(jnp.float32)
    own_order = token_order - dp_index * row_count
    first_rows = rms_scale(tok_own, first_gain).astype(jnp.bfloat16)
    first_all, cot_all, order_all = (
        lax.all_gather(first_rows, "tensor", axis=0, tiled=True),
        lax.all_gather(cotangent, "tensor", axis=0, tiled=True),
        lax.all_gather(own_order, "tensor", axis=0, tiled=True),
    )
    row_index = jnp.arange(row_count, dtype=jnp.int32)
    inverse = jnp.zeros((row_count,), jnp.int32).at[order_all].set(row_index)
    hidden_place = jnp.take(first_all, inverse, axis=0)
    places = dp_index * row_count + row_index
    ends = jnp.cumsum(seq_lengths)
    segment = segment_of(places, ends)
    starts = (places == 0) | (segment != segment_of(places - 1, ends))
    live = (places < ends[-1]).astype(jnp.float32)
    live_stored = jnp.take(live, order_all, axis=0)
    same = [
        (segment_of(places - shift, ends) == segment).astype(jnp.float32)
        for shift in range(kernel_taps)
    ]
    low_edge = tensor_index * own_width
    own_blocks = (low_edge + jnp.arange(own_width, dtype=jnp.int32)) // block_size
    first_block = low_edge // block_size
    block_count = own_width // block_size + 2

    def block_start(index):
        return (first_block + index) * block_size - low_edge + block_size

    def block_mask(index):
        inside = own_blocks == first_block + index
        return jnp.concatenate([inside, inside])

    def convolve(extended, kernel):
        return sum(
            (
                kernel[shift][None, :]
                * extended[edge_rows - shift : edge_rows - shift + row_count]
                * same[shift][:, None]
                for shift in range(kernel_taps)
            )
        )

    def gates(conv_vals, pre_recur, pre_input, decay_vals):
        log_rate = -rate_scale * jax.nn.sigmoid(pre_recur) * jax.nn.softplus(-decay_vals)
        decay_rate = jnp.where(starts[:, None], 0.0, jnp.exp(log_rate))
        scale_in = jnp.where(starts[:, None], 1.0, jnp.sqrt(-jnp.expm1(2.0 * log_rate)))
        return (decay_rate, conv_vals * jax.nn.sigmoid(pre_input) * scale_in)

    def glu(gate_pre, up_pre):
        return gelu_tanh(gate_pre) * up_pre

    x_branch = plain_dot(hidden_place, x_full).astype(jnp.bfloat16)
    y_before = plain_dot(hidden_place, y_full)
    previous = from_behind(x_branch[row_count - edge_rows :], "dp", 1)
    extended = jnp.concatenate([previous, x_branch], axis=0).astype(jnp.float32)
    conv_out = convolve(extended, conv_weight)
    conv_wide = extended_2(conv_out.astype(jnp.bfloat16), (("tensor", 1),), block_size)
    pre_both = jnp.zeros((row_count, 2 * own_width), jnp.float32)
    for index in range(block_count):
        piece = lax.dynamic_slice_in_dim(conv_wide, block_start(index), block_size, 1)
        pre_both = pre_both + jnp.where(
            block_mask(index)[None, :], plain_dot(piece, both_gates), 0.0
        )
    (decay_rate, driven), gate_pull = jax.vjp(
        gates, conv_out, pre_both[:, :own_width], pre_both[:, own_width:], decay_param
    )
    cum_rate, local_state = lax.associative_scan(pair_step, (decay_rate, driven), axis=0)
    ident = (jnp.ones((own_width,), jnp.float32), jnp.zeros((own_width,), jnp.float32))
    rate_in, state_in = entering((cum_rate[-1], local_state[-1]), "dp", pair_step, ident, False)
    state = local_state + cum_rate * state_in[None, :]
    y_branch = gelu_tanh(y_before)
    merged = (state * y_branch).astype(jnp.bfloat16)
    merged_stored = jnp.take(merged, order_all, axis=0)

    def mixer_rows(begin, number):
        return plain_dot(merged_stored, out_full)

    after_own = tok_own + row_sums(mixer_rows, tok_rows)
    hidden_two = spread_rows(rms_scale(after_own, second_gain).astype(jnp.bfloat16))
    gate_pre = plain_dot(hidden_two, gate_full)
    up_pre = plain_dot(hidden_two, up_full)
    glu_out, glu_pull = jax.vjp(glu, gate_pre, up_pre)
    product = glu_out.astype(jnp.bfloat16)

    def down_rows(begin, number):
        return plain_dot(product, down_full)

    feed_out = row_sums(down_rows, tok_rows)
    live_own = lax.dynamic_slice_in_dim(live_stored, own_start, tok_rows, 0)
    output = ((after_own + feed_out) * live_own[:, None]).astype(jnp.bfloat16)
    grad_out = cot_all.astype(jnp.float32) * live_stored[:, None]
    fresh = lax.optimization_barrier((shards, grad_out))[0]
    (
        gain_one,
        gain_two,
        x_full,
        y_full,
        recur_full,
        input_full,
        gate_full,
        up_full,
        out_full,
        down_full,
    ) = collect(*fresh)
    first_gain = gain_one.astype(jnp.float32)
    second_gain = gain_two.astype(jnp.float32)
    both_gates = jnp.concatenate([recur_full, input_full], axis=1)
    down_in = grad_out.astype(jnp.bfloat16)
    grad_down = trans_times(product, down_in)
    grad_product = times_trans(down_in, down_full)
    grad_gate_pre, grad_up_pre = glu_pull(grad_product)
    grad_gate_pre = grad_gate_pre.astype(jnp.bfloat16)
    grad_up_pre = grad_up_pre.astype(jnp.bfloat16)
    grad_gate = trans_times(hidden_two, grad_gate_pre)
    grad_up = trans_times(hidden_two, grad_up_pre)

    def feed_rows(begin, number):
        return times_trans(grad_gate_pre, gate_full) + times_trans(grad_up_pre, up_full)

    grad_out_own = lax.dynamic_slice_in_dim(grad_out, own_start, tok_rows, 0)
    grad_two_own = row_sums(feed_rows, tok_rows)
    grad_norm_own, normed_two = norm_back(after_own, second_gain, grad_two_own)
    second_part = jnp.sum(grad_two_own * normed_two, axis=0)
    grad_after_own = grad_out_own + grad_norm_own
    mixer_in = spread_rows(grad_after_own.astype(jnp.bfloat16))
    grad_out_mat = trans_times(merged_stored, mixer_in)
    grad_merged = jnp.take(times_trans(mixer_in, out_full), inverse, axis=0)
    grad_state = grad_merged * y_branch
    gelu_pull = jax.vjp(gelu_tanh, y_before)[1]
    grad_y_before = gelu_pull(grad_merged * state)[0].astype(jnp.bfloat16)
    rate_next = jnp.concatenate([decay_rate[1:], jnp.ones((1, own_width), jnp.float32)], axis=0)
    rev_rate, local_lam = lax.associative_scan(
        pair_step, (rate_next, grad_state), reverse=True, axis=0
    )
    head_rate = decay_rate[0] * rev_rate[0]
    head_lam = decay_rate[0] * local_lam[0]
    factor_in, lam_in = entering((head_rate, head_lam), "dp", pair_step, ident, True)
    lam = local_lam + rev_rate * lam_in[None, :]
    state_prev = jnp.concatenate([state_in[None, :], state[:-1]], axis=0)
    grad_conv_local, grad_pre_recur, grad_pre_input, grad_decay_own = gate_pull(
        (lam * state_prev, lam)
    )
    grad_pre = jnp.concatenate([grad_pre_recur, grad_pre_input], axis=1).astype(jnp.bfloat16)
    grad_both = jnp.zeros((block_size, 2 * own_width), jnp.float32)
    grad_wide = jnp.zeros((row_count, own_width + 2 * block_size), jnp.float32)
    for index in range(block_count):
        begin = block_start(index)
        piece = lax.dynamic_slice_in_dim(conv_wide, begin, block_size, 1)
        masked = jnp.where(block_mask(index)[None, :], grad_pre, jnp.zeros((), jnp.bfloat16))
        grad_both = grad_both + trans_times(piece, masked)
        added = lax.dynamic_slice_in_dim(grad_wide, begin, block_size, 1) + times_trans(
            masked, both_gates
        )
        grad_wide = lax.dynamic_update_slice_in_dim(grad_wide, added, begin, 1)
    grad_recur = grad_both[:, :own_width]
    grad_input = grad_both[:, own_width:]
    rims = jnp.concatenate(
        [grad_wide[:, :block_size], grad_wide[:, own_width + block_size :]], axis=1
    )
    arrived = extended_2(rims.astype(jnp.bfloat16), (("tensor", 1),), block_size).astype(rims.dtype)
    from_lower = jnp.pad(arrived[:, :block_size], ((0, 0), (0, own_width - block_size)))
    from_upper = jnp.pad(arrived[:, 3 * block_size :], ((0, 0), (own_width - block_size, 0)))
    grad_conv = (
        grad_conv_local
        + grad_wide[:, block_size : block_size + own_width]
        + from_lower
        + from_upper
    )
    conv_pull = jax.vjp(convolve, extended, conv_weight)[1]
    grad_extended, grad_kernel = conv_pull(grad_conv)
    returned = from_behind(grad_extended[:edge_rows], "dp", -1)
    grad_x_branch = grad_extended[edge_rows:] + jnp.concatenate(
        [jnp.zeros((row_count - edge_rows, own_width), jnp.float32), returned], axis=0
    )
    grad_x_low = grad_x_branch.astype(jnp.bfloat16)
    grad_x_stored = jnp.take(grad_x_low, order_all, axis=0)
    grad_y_stored = jnp.take(grad_y_before, order_all, axis=0)
    grad_x_mat = trans_times(first_all, grad_x_stored)
    grad_y_mat = trans_times(first_all, grad_y_stored)

    def mixer_back_rows(begin, number):
        return times_trans(grad_x_stored, x_full) + times_trans(grad_y_stored, y_full)

    grad_one_own = row_sums(mixer_back_rows, tok_rows)
    grad_norm_one, normed_one = norm_back(tok_own, first_gain, grad_one_own)
    first_part = jnp.sum(grad_one_own * normed_one, axis=0)
    grad_tokens = grad_after_own + grad_norm_one
    chosen = jnp.arange(n_tensor, dtype=jnp.int32) == tensor_index
    kernel_tile = jnp.where(chosen[:, None, None], grad_kernel[None, :, :], 0.0)
    decay_tile = jnp.where(chosen[:, None], grad_decay_own[None, :], 0.0)
    small = lax.psum((first_part, second_part, kernel_tile, decay_tile), ("dp", "tensor"))
    grad_first_gain = lax.dynamic_slice_in_dim(small[0], dp_index * dp_width, dp_width, 0)
    grad_second_gain = lax.dynamic_slice_in_dim(small[1], dp_index * dp_width, dp_width, 0)
    grad_kernel_sum = lax.dynamic_index_in_dim(small[2], tensor_index, 0, keepdims=False)
    grad_decay = lax.dynamic_index_in_dim(small[3], tensor_index, 0, keepdims=False)
    sums = (
        lax.psum_scatter(
            grad_x_mat.astype(jnp.bfloat16), "dp", scatter_dimension=0, tiled=True
        ).astype(jnp.float32),
        lax.psum_scatter(
            grad_y_mat.astype(jnp.bfloat16), "dp", scatter_dimension=0, tiled=True
        ).astype(jnp.float32),
        lax.psum_scatter(
            grad_recur.astype(jnp.bfloat16), "dp", scatter_dimension=0, tiled=True
        ).astype(jnp.float32),
        lax.psum_scatter(
            grad_input.astype(jnp.bfloat16), "dp", scatter_dimension=0, tiled=True
        ).astype(jnp.float32),
        lax.psum_scatter(
            grad_gate.astype(jnp.bfloat16), "dp", scatter_dimension=0, tiled=True
        ).astype(jnp.float32),
        lax.psum_scatter(
            grad_up.astype(jnp.bfloat16), "dp", scatter_dimension=0, tiled=True
        ).astype(jnp.float32),
        lax.psum_scatter(
            grad_out_mat.astype(jnp.bfloat16), "dp", scatter_dimension=1, tiled=True
        ).astype(jnp.float32),
        lax.psum_scatter(
            grad_down.astype(jnp.bfloat16), "dp", scatter_dimension=1, tiled=True
        ).astype(jnp.float32),
    )
    return (
        output,
        grad_tokens,
        grad_first_gain,
        sums[0],
        sums[1],
        grad_kernel_sum,
        sums[2],
        sums[3],
        grad_decay,
        sums[6],
        grad_second_gain,
        sums[4],
        sums[5],
        sums[7],
    )


MESH = pl.DeviceIdType.MESH
VMEM_BYTES = 60 * 2**20


def remote(src, dst, send, recv, device):
    return pltpu.make_async_remote_copy(
        src_ref=src,
        dst_ref=dst,
        send_sem=send,
        recv_sem=recv,
        device_id=device,
        device_id_type=MESH,
    )


class Place:
    def __init__(self, n_dp, n_line):
        self.n_dp, self.n_line = n_dp, n_line
        self.d, self.t = lax.axis_index("dp"), lax.axis_index("tensor")
        self.core = lax.rem(self.d, 2)
        self.x = lax.rem(lax.div(self.d, 2), 2)
        self.y = lax.div(self.d, 4)

    def chip(self, flip_x, flip_y, flip_core=0):
        x = 1 - self.x if flip_x else self.x
        y = 1 - self.y if flip_y else self.y
        core = 1 - self.core if flip_core else self.core
        return y * 4 + x * 2 + core

    def at(self, flip_x=0, flip_y=0, flip_core=0):
        return (self.chip(flip_x, flip_y, flip_core), self.t)

    def up(self):
        return (self.d, lax.rem(self.t + 1, self.n_line))

    def down(self):
        return (self.d, lax.rem(self.t + self.n_line - 1, self.n_line))

    def meet(self, everyone=False):
        barrier = pltpu.get_barrier_semaphore()

        def greet(device):
            pl.semaphore_signal(barrier, inc=1, device_id=device, device_id_type=MESH)

        if everyone:
            for i in range(1, self.n_dp):
                greet((lax.rem(self.d + i, self.n_dp), self.t))
            for i in range(1, self.n_line):
                greet((self.d, lax.rem(self.t + i, self.n_line)))
            pl.semaphore_wait(barrier, self.n_dp + self.n_line - 2)
            return
        for flips in ((1, 0), (0, 1), (0, 0, 1)):
            greet(self.at(*flips))
        below, above = self.t > 0, self.t < self.n_line - 1

        @pl.when(below)
        def _():
            greet(self.down())

        @pl.when(above)
        def _():
            greet(self.up())

        pl.semaphore_wait(barrier, 3 + below.astype(jnp.int32) + above.astype(jnp.int32))


class Fetch:
    def __init__(self, pairs, sems):
        self.copies = [
            pltpu.make_async_copy(src, dst, sems.at[i]) for i, (src, dst) in enumerate(pairs)
        ]

    def start(self, *which):
        for i in which:
            self.copies[i].start()

    def wait(self, *which):
        for i in which:
            self.copies[i].wait()


def vmem_like(array):
    return pltpu.VMEM(array.shape, array.dtype)


class Kept:
    def __init__(self, src, dst, held, sems):
        self.there = pltpu.make_async_copy(src, held, sems.at[0])
        self.back = pltpu.make_async_copy(held, dst, sems.at[1])

    def begin(self):
        self.there.start()

    def turn(self):
        self.there.wait()
        self.back.start()

    def finish(self):
        self.back.wait()


class GatherPlane:
    def __init__(self, place, src, dst, send, recv, local, held):
        self.p, self.src, self.dst = place, src, dst
        self.rows = src.shape[0]
        self.send, self.recv = send, recv
        self.keep = Kept(src, self.block(0, 0), held, local)

    def block(self, fx, fy, fc=0, part=None):
        first = self.p.chip(fx, fy, fc) * self.rows
        size = self.rows
        if part is not None:
            size = self.rows // 2
            first = first + part * size
        return self.dst.at[pl.ds(pl.multiple_of(first, 16), size)]

    def copy(self, i, src, dst, device):
        return remote(src, dst, self.send.at[i], self.recv.at[i], device)

    def outgoing(self, i):
        at, block = self.p.at, self.block
        if i == 0:
            return self.copy(0, self.src, block(0, 0), at(1, 0))
        if i == 1:
            return self.copy(1, self.src, block(0, 0), at(0, 1))
        if i == 2:
            return self.copy(2, self.src, block(0, 0), at(0, 0, 1))
        if i == 3:
            return self.copy(3, block(1, 0, 0, 0), block(1, 0, 0, 0), at(0, 1))
        if i == 4:
            return self.copy(4, block(0, 1, 0, 1), block(0, 1, 0, 1), at(1, 0))
        spot = ((1, 0), (0, 1), (1, 1, 0, 0), (1, 1, 0, 1))[i - 5]
        return self.copy(i, block(*spot), block(*spot), at(0, 0, 1))

    def arrive(self, i):
        spot = (
            (1, 0),
            (0, 1),
            (0, 0, 1),
            (1, 1, 0, 0),
            (1, 1, 0, 1),
            (1, 0, 1),
            (0, 1, 1),
            (1, 1, 1, 0),
            (1, 1, 1, 1),
        )[i]
        here = self.block(*spot)
        self.copy(i, here, here, self.p.at(0, 0, 1)).wait_recv()

    def begin(self):
        for i in (0, 1, 2):
            self.outgoing(i).start()
        self.keep.begin()

    def forward(self):
        self.keep.turn()
        self.arrive(0)
        self.outgoing(3).start()
        self.arrive(1)
        self.outgoing(4).start()
        self.outgoing(5).start()
        self.outgoing(6).start()

    def share(self):
        self.arrive(3)
        self.outgoing(7).start()
        self.arrive(4)
        self.outgoing(8).start()

    def finish(self):
        for i in (2, 5, 6, 7, 8):
            self.arrive(i)
        for i in range(9):
            self.outgoing(i).wait_send()
        self.keep.finish()


class GatherLine:
    def __init__(self, place, dst, rows, begin, span, send, recv):
        self.p, self.dst, self.rows = place, dst, rows
        self.begin, self.span = begin, span
        self.send, self.recv = send, recv
        self.last = place.n_line - 1

    def block(self, owner):
        first = owner * self.rows + self.begin
        return self.dst.at[pl.ds(pl.multiple_of(first, 8), self.span)]

    def copy(self, way, k, owner, source=None):
        to = self.p.up() if way == 0 else self.p.down()
        block = self.block(owner)
        return remote(
            block if source is None else source,
            block,
            self.send.at[way, k],
            self.recv.at[way, k],
            to,
        )

    def step(self, k, source=None):
        t, last = self.p.t, self.last
        if k > 0:
            self.arrive(k - 1)

        @pl.when((t < last) & (t >= k))
        def _():
            self.copy(0, k, t - k, source).start()

        @pl.when((t > 0) & (t + k <= last))
        def _():
            self.copy(1, k, t + k, source).start()

    def arrive(self, k):
        t, last = self.p.t, self.last

        @pl.when(t >= k + 1)
        def _():
            self.copy(0, k, t - 1 - k).wait_recv()

        @pl.when(t + k + 1 <= last)
        def _():
            self.copy(1, k, t + 1 + k).wait_recv()

    def finish(self):
        t, last = self.p.t, self.last
        self.arrive(last - 1)
        for k in range(last):

            @pl.when((t < last) & (t >= k))
            def _():
                self.copy(0, k, t - k).wait_send()

            @pl.when((t > 0) & (t + k <= last))
            def _():
                self.copy(1, k, t + k).wait_send()


class ReduceLine:
    def __init__(self, place, terms, rows, begin, span, inbox, send, recv):
        self.p, self.terms, self.rows = place, terms, rows
        self.begin, self.span = begin, span
        self.inbox = inbox
        self.send, self.recv = send, recv
        self.last = place.n_line - 1

    def own(self, owner):
        first = owner * self.rows + self.begin
        return self.terms.at[pl.ds(pl.multiple_of(first, 16), self.span)]

    def copy(self, way, j, source):
        to = self.p.up() if way == 0 else self.p.down()
        return remote(
            source, self.inbox.at[way, j], self.send.at[way, j], self.recv.at[way, j], to
        )

    def ends(self):
        t, last = self.p.t, self.last

        @pl.when(t == 0)
        def _():
            for j in range(last):
                self.copy(0, j, self.own(last - j)).start()

        @pl.when(t == last)
        def _():
            for j in range(last):
                self.copy(1, j, self.own(j)).start()

    def sent(self):
        t, last = self.p.t, self.last

        @pl.when(t == 0)
        def _():
            for j in range(last):
                self.copy(0, j, self.own(last - j)).wait_send()

        @pl.when(t == last)
        def _():
            for j in range(last):
                self.copy(1, j, self.own(j)).wait_send()

    def hand_on(self, way, j):
        term = self.own(self.last - j if way == 0 else j)
        self.copy(way, j, term).wait_recv()
        self.inbox[way, j] = term[...] + self.inbox[way, j]
        self.copy(way, j, self.inbox.at[way, j]).start()

    def hop(self, k):
        t, last = self.p.t, self.last

        @pl.when(t == k + 1)
        def _():
            for j in range(last - 1 - k):
                self.hand_on(0, j)

        @pl.when(t == last - 1 - k)
        def _():
            for j in range(last - 1 - k):
                self.hand_on(1, j)

    def total(self, result):
        t, last = self.p.t, self.last
        result[...] = self.own(t)[...].astype(jnp.float32)

        @pl.when(t > 0)
        def _():
            j = last - t
            self.copy(0, j, self.inbox.at[0, 0]).wait_recv()
            result[...] += self.inbox[0, j].astype(jnp.float32)

        @pl.when(t < last)
        def _():
            self.copy(1, t, self.inbox.at[0, 0]).wait_recv()
            result[...] += self.inbox[1, t].astype(jnp.float32)

    def finish(self):
        t, last = self.p.t, self.last
        for j in range(last - 1):

            @pl.when((t > 0) & (t < last - j))
            def _():
                self.copy(0, j, self.inbox.at[0, j]).wait_send()

            @pl.when((t < last) & (t > j))
            def _():
                self.copy(1, j, self.inbox.at[1, j]).wait_send()


def add_rows(into, other, result=None):
    result = into if result is None else result

    def tile(i, carry):
        rows = pl.ds(pl.multiple_of(i * 16, 16), 16)
        result[rows] = into[rows] + other[rows]
        return carry

    lax.fori_loop(0, into.shape[0] // 16, tile, None)


class ReducePlane:
    chips = ((0, 0), (1, 0), (0, 1), (1, 1))

    def __init__(self, place, terms, scratch):
        self.p, self.terms = place, terms
        self.held, self.near, self.along, self.last, self.send, self.recv, self.local = scratch
        self.rows = self.held.shape[1]
        self.half = self.rows // 2

    @staticmethod
    def scratch(rows, width):
        return [
            pltpu.VMEM((4, rows, width), jnp.bfloat16),
            pltpu.VMEM((4, rows, width), jnp.bfloat16),
            pltpu.VMEM((4, rows // 2, width), jnp.bfloat16),
            pltpu.VMEM((2, rows // 2, width), jnp.bfloat16),
            pltpu.SemaphoreType.DMA((10,)),
            pltpu.SemaphoreType.DMA((10,)),
            pltpu.SemaphoreType.DMA((4,)),
        ]

    def block(self, k, other):
        first = self.p.chip(*self.chips[k], other) * self.rows
        return self.terms.at[pl.ds(pl.multiple_of(first, 16), self.rows)]

    def half_of(self, k, part):
        return self.held.at[k, pl.ds(part * self.half, self.half)]

    def load(self, k):
        return pltpu.make_async_copy(self.block(k, 0), self.held.at[k], self.local.at[k])

    def copy(self, i):
        at = self.p.at
        if i < 4:
            src, dst, to = self.block(i, 1), self.near.at[i], at(0, 0, 1)
        elif i < 8:
            src, to = (
                (self.half_of(1, 0), at(1, 0)),
                (self.half_of(3, 0), at(1, 0)),
                (self.half_of(2, 1), at(0, 1)),
                (self.half_of(3, 1), at(0, 1)),
            )[i - 4]
            dst = self.along.at[i - 4]
        else:
            src, to = ((self.half_of(2, 0), at(0, 1)), (self.half_of(1, 1), at(1, 0)))[i - 8]
            dst = self.last.at[i - 8]
        return remote(src, dst, self.send.at[i], self.recv.at[i], to)

    def begin(self):
        for k in (3, 1, 2, 0):
            self.copy(k).start()
            self.load(k).start()

    def cores(self):
        for k in (3, 1, 2, 0):
            self.load(k).wait()
            self.copy(k).wait_recv()
            add_rows(self.held.at[k], self.near.at[k])
            if k == 3:
                self.copy(5).start()
                self.copy(7).start()
            elif k == 1:
                self.copy(4).start()
            elif k == 2:
                self.copy(6).start()

    def turn(self):
        self.copy(5).wait_recv()
        add_rows(self.half_of(2, 0), self.along.at[1])
        self.copy(8).start()
        self.copy(7).wait_recv()
        add_rows(self.half_of(1, 1), self.along.at[3])
        self.copy(9).start()
        self.copy(4).wait_recv()
        add_rows(self.half_of(0, 0), self.along.at[0])
        self.copy(6).wait_recv()
        add_rows(self.half_of(0, 1), self.along.at[2])

    def finish(self, result):
        for part in (0, 1):
            self.copy(8 + part).wait_recv()
            rows = pl.ds(part * self.half, self.half)
            add_rows(self.half_of(0, part), self.last.at[part], result.at[rows])
        for i in range(10):
            self.copy(i).wait_send()


def dma_sems(*dims):
    return pltpu.SemaphoreType.DMA(dims)


def in_vmem():
    return pl.BlockSpec(memory_space=pltpu.VMEM)


def in_any():
    return pl.BlockSpec(memory_space=pl.ANY)


def comm_params(number):
    return pltpu.CompilerParams(
        collective_id=number, has_side_effects=True, vmem_limit_bytes=VMEM_BYTES
    )


def shaped(dims, kind):
    return jax.ShapeDtypeStruct(dims, kind)


def first_gather(n_dp, n_line, mats, rows_in, order):
    count = len(mats)
    parts = 2

    def kernel(*refs):
        srcs, (c, e) = refs[:count], refs[count : count + 2]
        dsts, (c_out, e_out) = refs[count + 2 : 2 * count + 2], refs[2 * count + 2 : 2 * count + 4]
        ps, pr, pl_sem, ls, lr, ll = refs[2 * count + 4 : 2 * count + 10]
        held = refs[2 * count + 10 :]
        place = Place(n_dp, n_line)
        place.meet()
        planes = [
            GatherPlane(place, a, b, ps.at[i], pr.at[i], pl_sem.at[i], held[i])
            for i, (a, b) in enumerate(zip(srcs, dsts))
        ]
        rows = c.shape[0]
        span = rows // parts
        lines = [
            GatherLine(place, c_out, rows, i * span, span, ls.at[i], lr.at[i])
            for i in range(parts)
        ]
        lines.append(
            GatherLine(place, e_out, e.shape[0], 0, e.shape[0], ls.at[parts], lr.at[parts])
        )
        for i in range(parts):
            lines[i].step(0, c.at[pl.ds(i * span, span)])
        lines[parts].step(0, e)
        early, late = planes[: count // 2], planes[count // 2 :]
        for part in early:
            part.begin()
        copies = []
        for i, (src, dst) in enumerate(((c, c_out), (e, e_out))):
            own = dst.at[pl.ds(pl.multiple_of(place.t * src.shape[0], 8), src.shape[0])]
            copies.append(Kept(src, own, held[count + i], ll.at[i]))
            copies[i].begin()
        for line in lines:
            line.step(1)
        for part in late:
            part.begin()
        for part in early:
            part.forward()
        for copy in copies:
            copy.turn()
        for line in lines:
            line.step(2)
        for part in early:
            part.share()
        for part in late:
            part.forward()
        for part in late:
            part.share()
        for part in lines + planes:
            part.finish()
        for copy in copies:
            copy.finish()

    return pl.pallas_call(
        kernel,
        out_shape=tuple(shaped((n_dp * m.shape[0], m.shape[1]), m.dtype) for m in mats)
        + (
            shaped((n_line * rows_in.shape[0], rows_in.shape[1]), rows_in.dtype),
            shaped((n_line * order.shape[0], order.shape[1]), order.dtype),
        ),
        in_specs=[in_any()] * (count + 2),
        out_specs=[in_any()] * (count + 2),
        scratch_shapes=[
            dma_sems(count, 9),
            dma_sems(count, 9),
            dma_sems(count, 2),
            dma_sems(parts + 1, 2, n_line - 1),
            dma_sems(parts + 1, 2, n_line - 1),
            dma_sems(2, 2),
        ]
        + [vmem_like(m) for m in (*mats, rows_in, order)],
        compiler_params=comm_params(1),
        name="first_gather",
    )(*mats, rows_in, order)


CHUNKS = 8
LAST_CHUNKS = 8


def line_scratch(n_line, span, width, chunks):
    hops = n_line - 1
    return [
        pltpu.VMEM((chunks, 2, hops, span, width), jnp.bfloat16),
        dma_sems(chunks, 2, hops),
        dma_sems(chunks, 2, hops),
        dma_sems(chunks, 2, hops),
        dma_sems(chunks, 2, hops),
        pltpu.VMEM((span, width), jnp.float32),
    ]


def sum_rows_and_spread(place, terms, scratch, finish_rows, spread, between):
    inbox, rs, rr, gs, gr, total = scratch
    span = total.shape[0]
    count = inbox.shape[0]
    rows = span * count
    hops = place.n_line - 1
    sums = [
        ReduceLine(place, terms, rows, c * span, span, inbox.at[c], rs.at[c], rr.at[c])
        for c in range(count)
    ]
    gathers = []
    if spread is not None:
        gathers = [
            GatherLine(place, spread, rows, c * span, span, gs.at[c], gr.at[c])
            for c in range(count)
        ]
    sums[0].ends()

    def total_of(c):
        sums[c].total(total)
        finish_rows(c, pl.ds(c * span, span), total)
        if gathers:
            gathers[c].step(0)

    stages = [lambda c, k=k: sums[c].hop(k) for k in range(hops - 1)] + [total_of]
    lags = [LAGS[min(k, len(LAGS) - 1)] for k in range(hops)]
    if gathers:
        stages += [lambda c, k=k: gathers[c].step(k) for k in range(1, hops)]
        lags += [lags[-1] + LAG_STEP * k for k in range(1, hops)]
    for i in range(count + lags[-1]):
        if i < count:
            sums[i].sent()
        if i + 1 < count:
            sums[i + 1].ends()
        for work, lag in zip(stages, lags):
            if 0 <= i - lag < count:
                work(i - lag)
        if i in between:
            between[i]()
    for part in gathers + sums:
        part.finish()


LAGS = (0, 1, 1)
LAG_STEP = 1


def middle_gather(n_dp, n_line, terms, tokens, gain, mats):
    rows, width = tokens.shape
    count = len(mats)

    def kernel(*refs):
        s, tok, gain_ref = refs[:3]
        srcs = refs[3 : 3 + count]
        after, hidden = refs[3 + count : 5 + count]
        dsts = refs[5 + count : 5 + 2 * count]
        ps, pr, pl_sem = refs[5 + 2 * count : 8 + 2 * count]
        held = refs[8 + 2 * count : 8 + 3 * count]
        scratch = refs[8 + 3 * count :]
        place = Place(n_dp, n_line)
        place.meet()
        planes = [
            GatherPlane(place, a, b, ps.at[i], pr.at[i], pl_sem.at[i], held[i])
            for i, (a, b) in enumerate(zip(srcs, dsts))
        ]
        planes[0].begin()

        def norm(c, here, total):
            values = tok[here].astype(jnp.float32) + total[...]
            after[here] = values
            low = rms_scale(values, gain_ref[...]).astype(jnp.bfloat16)
            first = pl.multiple_of(place.t * rows, 16) + c * total.shape[0]
            hidden[pl.ds(pl.multiple_of(first, 16), total.shape[0])] = low

        between = {5: planes[0].forward, 8: planes[0].share}
        sum_rows_and_spread(place, s, scratch, norm, hidden, between)
        for part in planes:
            part.finish()

    return pl.pallas_call(
        kernel,
        out_shape=(
            shaped((rows, width), jnp.float32),
            shaped((n_line * rows, width), jnp.bfloat16),
        )
        + tuple(shaped((n_dp * m.shape[0], m.shape[1]), m.dtype) for m in mats),
        in_specs=[in_vmem()] * 3 + [in_any()] * count,
        out_specs=[in_vmem()] * 2 + [in_any()] * count,
        scratch_shapes=[dma_sems(count, 9), dma_sems(count, 9), dma_sems(count, 2)]
        + [vmem_like(m) for m in mats]
        + line_scratch(n_line, rows // CHUNKS, width, CHUNKS),
        compiler_params=comm_params(2),
        name="middle_gather",
    )(terms, tokens, gain, *mats)


def middle_sums(n_dp, n_line, terms, after, gain, grad_in, mat, hidden, grad_up, product, down):
    rows, width = after.shape
    block = mat.shape[0] // n_dp
    wide = grad_up.shape[1]
    spread_rows = n_line * rows

    def kernel(*refs):
        s, after_ref, gain_ref, g_ref, src = refs[:5]
        hid_far, gu_far, pr_far, dw_far = refs[5:9]
        grad_after, gain_sum, spread, result, up_far, feed_far = refs[9:15]
        hid, gu, pr, dw, up_out, feed, sems = refs[15:22]
        rest = refs[22:]
        fetch = Fetch(
            [
                (hid_far, hid),
                (gu_far, gu),
                (pr_far, pr),
                (dw_far, dw),
                (feed, feed_far),
                (up_out.at[0], up_far.at[pl.ds(0, width // 2)]),
                (up_out.at[1], up_far.at[pl.ds(width // 2, width // 2)]),
            ],
            sems,
        )
        fetch.start(0, 1, 2, 3)
        place = Place(n_dp, n_line)
        place.meet()
        plane = ReducePlane(place, src, rest[:7])
        scratch = rest[7:]
        plane.begin()
        gain_sum[...] = jnp.zeros_like(gain_sum)

        def norm(c, here, total):
            grad = total[...]
            grad_rows, normed = norm_back(after_ref[here], gain_ref[...], grad)
            gain_sum[...] += jnp.sum(grad * normed, axis=0, keepdims=True)
            both = g_ref[here].astype(jnp.float32) + grad_rows
            grad_after[here] = both
            first = pl.multiple_of(place.t * rows, 16) + c * total.shape[0]
            spread[pl.ds(pl.multiple_of(first, 16), total.shape[0])] = both.astype(jnp.bfloat16)

        def feed_part(i):
            cols = pl.ds(i * (width // 4), width // 4)
            feed[:, cols] = times_trans(pr[...], dw[cols]).astype(jnp.bfloat16)

        def up_part(i):
            cols = pl.ds(i * (width // 4), width // 4)
            here = pl.ds((i % 2) * (width // 4), width // 4)
            up_out[i // 2, here] = trans_times(hid[:, cols], gu[...]).astype(jnp.bfloat16)

        def early():
            plane.cores()
            fetch.wait(0, 1)

        def two():
            up_part(0)

        def three():
            up_part(1)
            fetch.start(5)

        def four():
            up_part(2)

        def five():
            plane.turn()
            up_part(3)
            fetch.start(6)
            fetch.wait(2, 3)

        def six():
            feed_part(0)

        def seven():
            feed_part(1)

        def eight():
            feed_part(2)

        def nine():
            feed_part(3)
            fetch.start(4)

        steps = {1: early, 2: two, 3: three, 4: four, 5: five, 6: six, 7: seven, 8: eight, 9: nine}
        sum_rows_and_spread(place, s, scratch, norm, spread, steps)
        plane.finish(result)
        fetch.wait(4, 5, 6)

    low, full = jnp.bfloat16, jnp.float32
    near, far = in_vmem(), in_any()
    return pl.pallas_call(
        kernel,
        out_shape=(
            shaped((rows, width), full),
            shaped((1, width), full),
            shaped((spread_rows, width), low),
            shaped((block, mat.shape[1]), low),
            shaped((width, wide), low),
            shaped((spread_rows, width), low),
        ),
        in_specs=[near] * 4 + [far] * 5,
        out_specs=[near] * 4 + [far] * 2,
        scratch_shapes=[vmem_like(m) for m in (hidden, grad_up, product, down)]
        + [
            pltpu.VMEM((2, width // 2, wide), low),
            pltpu.VMEM((spread_rows, width), low),
            dma_sems(7),
        ]
        + ReducePlane.scratch(block, mat.shape[1])
        + line_scratch(n_line, rows // CHUNKS, width, CHUNKS),
        compiler_params=comm_params(3),
        name="middle_sums",
    )(terms, after, gain, grad_in, mat, hidden, grad_up, product, down)


class Exchange:
    def __init__(self, place, axis, src, slots, send, recv, local):
        self.p, self.src, self.slots = place, src, slots
        self.over_dp = axis == "dp"
        self.size = place.n_dp if self.over_dp else place.n_line
        self.me = place.d if self.over_dp else place.t
        self.send, self.recv, self.local = send, recv, local

    def copy(self, i):
        to = lax.rem(self.me + i, self.size)
        device = (to, self.p.t) if self.over_dp else (self.p.d, to)
        return remote(
            self.src, self.slots.at[self.me], self.send.at[i - 1], self.recv.at[i - 1], device
        )

    def mine(self):
        return pltpu.make_async_copy(self.src, self.slots.at[self.me], self.local)

    def begin(self):
        for i in range(1, self.size):
            self.copy(i).start()
        self.mine().start()

    def wait(self):
        self.mine().wait()
        for i in range(1, self.size):
            self.copy(i).wait()

    def finish(self):
        self.wait()
        total = self.slots[0]
        for i in range(1, self.size):
            total = total + self.slots[i]
        return total


def last_sums(n_dp, n_line, terms, tokens, gain, grad_after, second, small, mats):
    rows, width = tokens.shape
    count = len(mats)
    per = len(ReducePlane.scratch(16, 128))

    def kernel(*refs):
        s, tok, gain_ref, g_ref, second_ref, small_ref = refs[:6]
        srcs = refs[6 : 6 + count]
        grad_tok, small_out, first_out = refs[6 + count : 9 + count]
        results = refs[9 + count : 9 + 2 * count]
        rest = refs[9 + 2 * count :]
        own_first, row_sum = rest[count * per : count * per + 2]
        slots_a, slots_b, slots_c, slots_d = rest[count * per + 2 : count * per + 6]
        xs, xr, xl = rest[count * per + 6 : count * per + 9]
        scratch = rest[count * per + 9 :]
        place = Place(n_dp, n_line)
        place.meet(True)
        planes = [
            ReducePlane(place, srcs[i], rest[i * per : (i + 1) * per]) for i in range(count)
        ]
        for part in planes:
            part.begin()
        early = Exchange(place, "dp", small_ref, slots_a, xs.at[0], xr.at[0], xl.at[0])
        early.begin()
        gain = Exchange(place, "dp", second_ref, slots_d, xs.at[3], xr.at[3], xl.at[3])
        gain.begin()
        own_first[...] = jnp.zeros_like(own_first)

        def norm(c, here, total):
            grad = total[...]
            grad_rows, normed = norm_back(tok[here].astype(jnp.float32), gain_ref[...], grad)
            own_first[...] += jnp.sum(grad * normed, axis=0, keepdims=True)
            grad_tok[here] = g_ref[here] + grad_rows

        def cores():
            for part in planes:
                part.cores()

        def turn():
            for part in planes:
                part.turn()

        sum_rows_and_spread(place, s, scratch, norm, None, {0: cores, 4: turn})
        first = Exchange(place, "dp", own_first, slots_b, xs.at[1], xr.at[1], xl.at[1])
        first.begin()
        small_out[...] = early.finish()
        row_sum[0:1] = gain.finish()
        row_sum[1:2] = first.finish()
        both = Exchange(place, "tensor", row_sum, slots_c, xs.at[2], xr.at[2], xl.at[2])
        both.begin()
        for part, result in zip(planes, results):
            part.finish(result)
        first_out[...] = both.finish()

    return pl.pallas_call(
        kernel,
        out_shape=(
            shaped((rows, width), jnp.float32),
            shaped(small.shape, jnp.float32),
            shaped((2, width), jnp.float32),
        )
        + tuple(shaped((m.shape[0] // n_dp, m.shape[1]), jnp.bfloat16) for m in mats),
        in_specs=[in_vmem()] * 6 + [in_any()] * count,
        out_specs=[in_vmem()] * (3 + count),
        scratch_shapes=sum([ReducePlane.scratch(m.shape[0] // n_dp, m.shape[1]) for m in mats], [])
        + [
            pltpu.VMEM((1, width), jnp.float32),
            pltpu.VMEM((2, width), jnp.float32),
            pltpu.VMEM((n_dp,) + small.shape, jnp.float32),
            pltpu.VMEM((n_dp, 1, width), jnp.float32),
            pltpu.VMEM((n_line, 2, width), jnp.float32),
            pltpu.VMEM((n_dp, 1, width), jnp.float32),
            dma_sems(4, n_dp),
            dma_sems(4, n_dp),
            dma_sems(4),
        ]
        + line_scratch(n_line, rows // LAST_CHUNKS, width, LAST_CHUNKS),
        compiler_params=comm_params(4),
        name="last_sums",
    )(terms, tokens, gain, grad_after, second, small, *mats)


def loop(count, body, unroll=1):
    def step(i, carry):
        body(i)
        return carry

    lax.fori_loop(0, count, step, None, unroll=unroll)


def tile_rows(i, size, ahead=0):
    return pl.ds(pl.multiple_of(i * size + ahead, 8), size)


def moved_up(values, distance, count):
    size = values.shape[0]
    return pltpu.roll(values, (size - distance) % size, 0)[:count]


def take_lanes(ref, here):
    return jnp.concatenate([ref[c, here] for c in range(ref.shape[0])], axis=1)


def put_lanes(ref, here, values):
    for c in range(ref.shape[0]):
        ref[c, here] = values[:, c * LANES : (c + 1) * LANES]


def gelu_parts(values):
    inner = GELU_C * (values + 0.044715 * (values * values * values))
    tanh = jnp.tanh(inner)
    half = 0.5 * (1.0 + tanh)
    slope = half + 0.5 * values * (1.0 - tanh * tanh) * GELU_C * (
        1.0 + 3.0 * 0.044715 * (values * values)
    )
    return values * half, slope


GELU_C = 0.7978845608028654
RIM = 128
LANES = 128
TILE = 16


def one_minus_exp(values, exponential):
    series = jnp.ones_like(values)
    for term in range(9, 1, -1):
        series = 1.0 + values * (1.0 / term) * series
    return jnp.where(values > -0.35, -values * series, 1.0 - exponential)


def rate_and_scale(pre_recur, soft, start):
    sr = jax.nn.sigmoid(pre_recur)
    log_rate = -rate_scale * sr * soft
    decay = jnp.exp(log_rate)
    rate = jnp.where(start, 0.0, decay)
    scale = jnp.where(start, 1.0, jnp.sqrt(one_minus_exp(2.0 * log_rate, decay * decay)))
    return sr, rate, scale


class RimSwap:
    def __init__(self, place, own):
        self.odd = lax.rem(place.t, 2)
        self.partner = (place.d, place.t + 1 - 2 * self.odd)
        self.first = pl.multiple_of(RIM - RIM * self.odd, RIM)
        self.edge = pl.ds(pl.multiple_of((1 - self.odd) * own + self.odd * RIM, RIM), RIM)
        self.over_there = pl.ds(pl.multiple_of(self.odd * (own + RIM), RIM), RIM)
        self.beyond = pl.ds(pl.multiple_of((1 - self.odd) * (own + RIM), RIM), RIM)

    def block(self, index, size):
        return pl.ds(pl.multiple_of(self.first + index * size, RIM), size)


LATE_SHARE = 4


def recur_forward(
    n_dp,
    n_line,
    tok_all,
    cot,
    to_place,
    to_stored,
    x_full,
    y_full,
    out_full,
    gain,
    gates,
    taps,
    soft,
    flags,
):
    rows, width = tok_all.shape
    count, own = taps.shape
    size = gates.shape[0]
    wide = own + 2 * RIM
    blocks = (wide - RIM) // size
    chunk = rows // 8
    cot_rows = cot.shape[0] - cot.shape[0] // LATE_SHARE
    parts = 1

    def kernel(*refs):
        (tok_far, cot_ref, plc, sto, wx_far, wy_far, wo_far, gain_ref, gates_in, cw, sp, fl) = refs[:12]
        far, gw, cot_all = refs[12:23], refs[23], refs[24]
        tok, wx, wy, wo = refs[25:29]
        results = refs[29:40]
        hp, xext, y, conv_low, conv, pre_r, pre_i, rate, state, merged_st, terms = results
        (h, xf, local, cum, merged, agg, slots, hs, hr, es, er, el, gs, gr, gl) = refs[40:55]
        in_sems, out_sems, cot_held = refs[55:]
        fetch = Fetch(((tok_far, tok), (wx_far, wx), (wy_far, wy), (wo_far, wo)), in_sems)
        store = Fetch(zip(results, far), out_sems)
        fetch.start(0, 1, 2, 3)
        place = Place(n_dp, n_line)
        place.meet(True)
        swap = RimSwap(place, own)
        for side in range(2):
            first = side * wide
            gw[:, first : first + RIM] = jnp.zeros((size, RIM), jnp.bfloat16)
            gw[:, first + RIM : first + RIM + own] = gates_in[:, side * own : (side + 1) * own]
            gw[:, first + RIM + own : first + wide] = jnp.zeros((size, RIM), jnp.bfloat16)
        own_cot = cot_all.at[pl.ds(pl.multiple_of(place.t * cot_rows, 16), cot_rows)]
        cot_ref = cot_ref.at[pl.ds(0, cot_rows)]
        keep = Kept(cot_ref, own_cot, cot_held, gl)
        keep.begin()
        span = cot_rows // parts
        lines = [
            GatherLine(place, cot_all, cot_rows, c * span, span, gs.at[c], gr.at[c])
            for c in range(parts)
        ]
        for c, line in enumerate(lines):
            line.step(0, cot_ref.at[pl.ds(c * span, span)])

        def norm(i):
            here = tile_rows(i, TILE)
            h[here] = rms_scale(tok[here].astype(jnp.float32), gain_ref[...]).astype(jnp.bfloat16)

        fetch.wait(0)
        loop(rows // TILE, norm)
        fetch.wait(1)

        def project(i):
            here = tile_rows(i, 128)
            hp[here] = plain_dot(plc[here], h[...]).astype(jnp.bfloat16)
            xext[tile_rows(i, 128, 16)] = plain_dot(hp[here], wx[...]).astype(jnp.bfloat16)

        loop(rows // 128, project)
        store.start(0)
        edge = remote(
            xext.at[pl.ds(rows, 16)],
            xext.at[pl.ds(0, 16)],
            hs.at[0],
            hr.at[0],
            (lax.rem(place.d + 1, n_dp), place.t),
        )
        edge.start()
        keep.turn()
        for line in lines:
            line.step(1)

        def project_y(i):
            here = tile_rows(i, 128)
            y[here] = plain_dot(hp[here], wy[...])

        fetch.wait(2)
        loop(rows // 128, project_y)
        store.start(2)
        edge.wait()
        top = xext[pl.ds(0, 16)]
        xext[pl.ds(0, 16)] = jnp.where(place.d > 0, top, jnp.zeros_like(top))
        store.start(1)

        def widen(i):
            xf[tile_rows(i, TILE)] = xext[tile_rows(i, TILE)].astype(jnp.float32)

        loop(rows // TILE + 1, widen)

        def convolve(i):
            here = tile_rows(i, TILE)
            near = xf[pl.ds(pl.multiple_of(i * TILE + 8, 8), TILE + 8)]
            same = fl[tile_rows(i, TILE, 8)]
            total = cw[0:1] * near[8:]
            for k in range(1, count):
                total += cw[k : k + 1] * moved_up(near, 8 - k, TILE) * same[:, k : k + 1]
            conv[here] = total
            conv_low[here, RIM : RIM + own] = total.astype(jnp.bfloat16)

        loop(rows // TILE, convolve)
        store.start(4)
        rim = remote(
            conv_low.at[:, swap.edge],
            conv_low.at[:, swap.over_there],
            hs.at[1],
            hr.at[1],
            swap.partner,
        )
        rim.start()
        for i in range(blocks):
            index = lax.rem(i + swap.odd, blocks)
            cols = swap.block(index, size)
            other = pl.ds(pl.multiple_of(wide + swap.first + index * size, RIM), size)
            if i == blocks - 1:
                rim.wait()
            pre_r[:, cols] = plain_dot(conv_low[:, cols], gw[:, cols])
            pre_i[:, cols] = plain_dot(conv_low[:, cols], gw[:, other])

        store.start(3, 5, 6)

        def drive(i):
            here = tile_rows(i, TILE)
            start = fl[tile_rows(i, TILE, 8)][:, 0:1] > 0.0
            own_cols = pl.ds(RIM, own)
            _, decay, scale = rate_and_scale(pre_r[here, own_cols], sp[...], start)
            put_lanes(rate, here, decay)
            put_lanes(local, here, conv[here] * jax.nn.sigmoid(pre_i[here, own_cols]) * scale)

        loop(rows // TILE, drive)
        store.start(7)
        for line in lines:
            line.step(2)
        groups = own // LANES

        def scan(i, carry):
            here = pl.ds(i, 8, chunk)
            result = []
            for c in range(groups):
                product, total = carry[c]
                r = rate[c, here]
                product = product * r
                total = total * r + local[c, here]
                cum[c, here] = product
                local[c, here] = total
                result.append((product, total))
            return tuple(result)

        blank = (jnp.ones((8, LANES), jnp.float32), jnp.zeros((8, LANES), jnp.float32))
        lax.fori_loop(0, chunk, scan, (blank,) * groups)
        product, total = jnp.ones((1, own), jnp.float32), jnp.zeros((1, own), jnp.float32)
        for j in range(8):
            last = pl.ds(j * chunk + chunk - 1, 1)
            total = take_lanes(local, last) + take_lanes(cum, last) * total
            product = product * take_lanes(cum, last)
        agg[0:1] = product
        agg[1:2] = total
        swap_all = Exchange(place, "dp", agg, slots, es, er, el)
        swap_all.begin()
        swap_all.wait()
        entry = jnp.zeros((1, own), jnp.float32)
        for q in range(n_dp):
            longer = slots[q, 1:2] + slots[q, 0:1] * entry
            entry = jnp.where(q < place.d, longer, entry)
        state[pl.ds(0, 8)] = jnp.broadcast_to(entry, (8, own))
        for j in range(8):

            def settle(i, entry=entry):
                here = tile_rows(i, TILE, j * chunk)
                values = take_lanes(local, here) + take_lanes(cum, here) * entry
                state[tile_rows(i, TILE, j * chunk + 8)] = values
                merged[here] = (values * gelu_parts(y[here])[0]).astype(jnp.bfloat16)

            loop(chunk // TILE, settle)
            last = pl.ds(j * chunk + chunk - 1, 1)
            entry = take_lanes(local, last) + take_lanes(cum, last) * entry
        store.start(8)
        merged_st[...] = plain_dot(sto[...], merged[...]).astype(jnp.bfloat16)

        store.start(9)
        fetch.wait(3)

        def mix(i):
            some = tile_rows(i, 512)
            terms[:, pl.ds(pl.multiple_of(i * 512, 512), 512)] = times_trans(
                merged_st[...], wo[some, :]
            ).astype(jnp.bfloat16)

        loop(width // 512, mix)
        for line in lines:
            line.finish()
        keep.finish()
        store.start(10)
        store.wait(*range(11))

    low, full = jnp.bfloat16, jnp.float32
    results = (
        shaped((rows, width), low),
        shaped((rows + 16, own), low),
        shaped((rows, own), full),
        shaped((rows, wide), low),
        shaped((rows, own), full),
        shaped((rows, wide), full),
        shaped((rows, wide), full),
        shaped((own // LANES, rows, LANES), full),
        shaped((rows + 8, own), full),
        shaped((rows, own), low),
        shaped((rows, width), low),
    )
    near, far = in_vmem(), in_any()
    return pl.pallas_call(
        kernel,
        out_shape=results
        + (shaped((size, 2 * wide), low), shaped((n_line * cot_rows, width), low)),
        in_specs=[far, far, near, near, far, far, far] + [near] * 5,
        out_specs=[far] * 11 + [near, far],
        scratch_shapes=[vmem_like(m) for m in (tok_all, x_full, y_full, out_full) + results]
        + [
            pltpu.VMEM((rows, width), low),
            pltpu.VMEM((rows + 16, own), full),
            pltpu.VMEM((own // LANES, rows, LANES), full),
            pltpu.VMEM((own // LANES, rows, LANES), full),
            pltpu.VMEM((rows, own), low),
            pltpu.VMEM((2, own), full),
            pltpu.VMEM((n_dp, 2, own), full),
            dma_sems(2),
            dma_sems(2),
            dma_sems(n_dp),
            dma_sems(n_dp),
            pltpu.SemaphoreType.DMA,
            dma_sems(parts, 2, n_line - 1),
            dma_sems(parts, 2, n_line - 1),
            dma_sems(2),
            dma_sems(4),
            dma_sems(11),
            pltpu.VMEM((cot_rows, width), low),
        ],
        compiler_params=comm_params(5),
        name="recur_forward",
    )(
        tok_all,
        cot,
        to_place,
        to_stored,
        x_full,
        y_full,
        out_full,
        gain,
        gates,
        taps,
        soft,
        flags,
    )


class RowProducts:
    def __init__(self, left, right, far, stage, sems):
        self.left, self.right, self.far, self.stage, self.sems = left, right, far, stage, sems
        self.part = stage.shape[1]
        self.count = far.shape[0] // self.part

    def slot(self, i):
        return self.stage.at[i % 2, :, pl.ds(0, self.far.shape[1])]

    def copy(self, i):
        some = pl.ds(i * self.part, self.part)
        return pltpu.make_async_copy(self.slot(i), self.far.at[some], self.sems.at[i])

    def run(self):
        for i in range(self.count):
            if i >= 2:
                self.copy(i - 2).wait()
            some = pl.ds(i * self.part, self.part)
            self.slot(i)[...] = trans_times(self.left[:, some], self.right[...]).astype(
                jnp.bfloat16
            )
            self.copy(i).start()

    def finish(self):
        self.copy(self.count - 2).wait()
        self.copy(self.count - 1).wait()


def recur_backward(
    n_dp,
    n_line,
    mixer_in,
    to_place,
    to_stored,
    x_full,
    y_full,
    out_full,
    gates,
    taps,
    soft,
    slope,
    flags,
    kept,
    weight_terms,
    row_terms,
    hidden_place,
    merged_stored,
):
    rows, width = mixer_in.shape
    count, own = taps.shape
    size = gates.shape[0]
    wide = own + 2 * RIM
    blocks = (wide - RIM) // size
    chunk = rows // 8
    own_rows = rows // n_line
    parts = 4
    span = own_rows // parts

    def kernel(*refs):
        (mix_far, plc, sto, wx_far, wy_far, wo_far, gw, cw, sp, sg, fl) = refs[:11]
        kept_far, weights, feed_far, hp_far, merged_far = refs[11:19], *refs[19:23]
        (gate_grads, tap_grads, terms_far, weight_sum, row_sum) = refs[23:28]
        out_far, xy_far = refs[28:30]
        mix, wy, wo, feed, merged = refs[30:35]
        (xext, y, conv_low, conv, pre_r, pre_i, rate, state) = refs[35:43]
        (gxy, mp, gm, lam, reach, gp_r, gp_i, grad, spread, rim_out, rim_in) = refs[43:54]
        (ret_out, ret_in, tap_sums, decay_sums, ends, agg, slots) = refs[54:61]
        (hs, hr, es, er, el, in_sems, out_sems, inbox, ls, lr, total) = refs[61:72]
        stage, stage_sems = refs[72:74]
        hp, terms, wx = mix, mix, wo
        fetch = Fetch(
            [
                (mix_far, mix),
                (wo_far, wo),
                (kept_far[1], y),
                (kept_far[7], state),
                (kept_far[6], rate),
                (kept_far[4], pre_r),
                (kept_far[5], pre_i),
                (kept_far[3], conv),
                (kept_far[2], conv_low),
                (kept_far[0], xext),
                (wx_far, wx),
                (wy_far, wy),
                (feed_far, feed),
                (merged_far, merged),
                (hp_far, hp),
            ],
            in_sems,
        )
        fetch.start(12, 0, 1, 13)
        store = Fetch(((terms, terms_far),), out_sems)
        out_rows = RowProducts(mix, merged, out_far, stage, stage_sems.at[0])
        xy_rows = RowProducts(hp, gxy, xy_far, stage, stage_sems.at[1])
        place = Place(n_dp, n_line)
        place.meet(True)
        plane = ReducePlane(place, weights, refs[74:])
        plane.begin()
        lines = [
            ReduceLine(place, feed, own_rows, c * span, span, inbox.at[c], ls.at[c], lr.at[c])
            for c in range(parts)
        ]

        def send(c):
            if c > 0:
                lines[c - 1].sent()
            if c < parts:
                lines[c].ends()

        def add_up(c):
            lines[c].total(total)
            row_sum[pl.ds(c * span, span)] = total[...].astype(jnp.bfloat16)

        fetch.wait(12)
        send(0)
        fetch.start(*range(2, 10), 11)
        swap = RimSwap(place, own)
        own_cols = pl.ds(RIM, own)

        def project(i):
            here = tile_rows(i, 128)
            mp[here] = plain_dot(plc[here], mix[...]).astype(jnp.bfloat16)
            gm[here] = plain_dot(mp[here], wo[...])

        fetch.wait(0, 1)
        loop(rows // 128, project)
        fetch.start(10)
        fetch.wait(13)
        out_rows.run()
        fetch.start(14)

        def split(i):
            here = tile_rows(i, TILE)
            branch, slope_y = gelu_parts(y[here])
            grads = gm[here]
            put_lanes(lam, here, grads * branch)
            values = state[tile_rows(i, TILE, 8)]
            gxy[here, own:] = (grads * values * slope_y).astype(jnp.bfloat16)

        fetch.wait(2, 3)
        loop(rows // TILE, split)
        send(1)
        lines[0].hop(0)
        fetch.wait(4)
        groups = own // LANES

        def scan(i, carry):
            here = pl.ds(chunk - 1 - i, 8, chunk)
            result = []
            for c in range(groups):
                product, message = carry[c]
                r = rate[c, here]
                value = lam[c, here] + message
                lam[c, here] = value
                reach[c, here] = product
                result.append((product * r, value * r))
            return tuple(result)

        blank = (jnp.ones((8, LANES), jnp.float32), jnp.zeros((8, LANES), jnp.float32))
        done = lax.fori_loop(0, chunk, scan, (blank,) * groups)
        for c in range(groups):
            lanes = pl.ds(c * LANES, LANES)
            ends[0, :, lanes] = done[c][0]
            ends[1, :, lanes] = done[c][1]
        product, message = jnp.ones((1, own), jnp.float32), jnp.zeros((1, own), jnp.float32)
        for j in reversed(range(8)):
            message = ends[1, j : j + 1] + ends[0, j : j + 1] * message
            product = product * ends[0, j : j + 1]
        agg[0:1] = product
        agg[1:2] = message
        swap_all = Exchange(place, "dp", agg, slots, es, er, el)
        swap_all.begin()
        plane.cores()
        swap_all.wait()
        lines[0].hop(1)
        entry = jnp.zeros((1, own), jnp.float32)
        for q in reversed(range(n_dp)):
            longer = slots[q, 1:2] + slots[q, 0:1] * entry
            entry = jnp.where(q > place.d, longer, entry)
        fetch.wait(5, 6, 7)
        for ref in (tap_sums, decay_sums):
            ref[...] = jnp.zeros_like(ref)
        for ref in (gp_r, gp_i):
            ref[:, 0:RIM] = jnp.zeros((rows, RIM), jnp.bfloat16)
            ref[:, RIM + own :] = jnp.zeros((rows, RIM), jnp.bfloat16)
        grad[pl.ds(0, 8)] = jnp.zeros((8, own), jnp.float32)
        grad[pl.ds(rows + 8, 8)] = jnp.zeros((8, own), jnp.float32)
        for j in reversed(range(8)):

            def back(i, entry=entry):
                here = tile_rows(i, TILE, j * chunk)
                flag = fl[tile_rows(i, TILE, j * chunk + 8)]
                start = flag[:, 0:1] > 0.0
                values = take_lanes(lam, here) + take_lanes(reach, here) * entry
                before = moved_up(
                    state[pl.ds(pl.multiple_of(j * chunk + i * TILE, 8), TILE + 8)], 7, TILE
                )
                sr, decay, scale = rate_and_scale(pre_r[here, own_cols], sp[...], start)
                si = jax.nn.sigmoid(pre_i[here, own_cols])
                block = conv[here]
                driven = values * si
                log_grad = values * before * decay - block * driven * (decay * decay) / scale
                log_grad = jnp.where(start, 0.0, log_grad)
                inner = sr * log_grad
                gp_r[here, own_cols] = (
                    -rate_scale * sp[...] * inner * (1.0 - sr)
                ).astype(jnp.bfloat16)
                gp_i[here, own_cols] = (driven * block * (1.0 - si) * scale).astype(jnp.bfloat16)
                grad[tile_rows(i, TILE, j * chunk + 8)] = driven * scale
                decay_sums[...] += inner[:8] + inner[8:]

            loop(chunk // TILE, back)
            if j == 4:
                send(2)
                lines[1].hop(0)
            entry = ends[1, j : j + 1] + ends[0, j : j + 1] * entry
        lines[1].hop(1)
        add_up(0)

        for i in range(blocks):
            index = lax.rem(i + 2 - 2 * swap.odd, blocks)
            cols = swap.block(index, size)
            other = pl.ds(pl.multiple_of(wide + swap.first + index * size, RIM), size)
            spread[:, cols] = times_trans(gp_r[:, cols], gw[:, cols]) + times_trans(
                gp_i[:, cols], gw[:, other]
            )
            if i == 0:
                rim_out[...] = spread[:, swap.beyond].astype(jnp.bfloat16)
                rim = remote(rim_out, rim_in, hs.at[0], hr.at[0], swap.partner)
                rim.start()
        send(3)
        lines[2].hop(0)
        rim.wait()
        shared = pl.ds(pl.multiple_of((1 - swap.odd) * (own - RIM), RIM), RIM)

        def join(i):
            here = tile_rows(i, TILE)
            there = tile_rows(i, TILE, 8)
            grad[there] += spread[here, own_cols]
            grad[there, shared] += rim_in[here].astype(jnp.float32)

        loop(rows // TILE, join)

        near = grad[pl.ds(0, 16)]
        back_rows = jnp.zeros((8, own), jnp.float32)
        for k in range(1, count):
            masked = near * fl[pl.ds(0, 16)][:, k : k + 1]
            back_rows += cw[k : k + 1] * moved_up(masked, k, 8)
        ret_out[...] = back_rows
        ret = remote(
            ret_out,
            ret_in,
            hs.at[1],
            hr.at[1],
            (lax.rem(place.d + n_dp - 1, n_dp), place.t),
        )
        ret.start()
        fetch.wait(8)
        for i in range(blocks):
            cols = swap.block(i, size)
            spread[0:size, cols] = trans_times(conv_low[:, cols], gp_r[:, cols])
            spread[size : 2 * size, cols] = trans_times(conv_low[:, cols], gp_i[:, cols])
        gate_grads[:, 0:own] = spread[0:size, own_cols].astype(jnp.bfloat16)
        gate_grads[:, own:] = spread[size : 2 * size, own_cols].astype(jnp.bfloat16)

        def taps_back(i, added=None):
            here = tile_rows(i, TILE)
            start = pl.ds(pl.multiple_of(i * TILE + 8, 8), TILE + 8)
            after = grad[start]
            flag = fl[start]
            behind = xext[pl.ds(pl.multiple_of(i * TILE, 16), 2 * TILE)].astype(jnp.float32)
            total = cw[0:1] * after[:TILE]
            for k in range(count):
                if k > 0:
                    masked = after * flag[:, k : k + 1]
                    total += cw[k : k + 1] * moved_up(masked, k, TILE)
                    mine = masked[:TILE]
                else:
                    mine = after[:TILE]
                term = mine * moved_up(behind, 16 - k, TILE)
                tap_sums[k] += term[:8] + term[8:]
            if added is not None:
                total = total + jnp.concatenate([jnp.zeros((8, own), jnp.float32), added], axis=0)
            gxy[here, 0:own] = total.astype(jnp.bfloat16)

        fetch.wait(9)
        loop(rows // TILE - 1, taps_back)
        lines[2].hop(1)
        add_up(1)
        ret.wait()
        taps_back(rows // TILE - 1, jnp.where(place.d < n_dp - 1, ret_in[...], 0.0))
        tap_grads[...] = jnp.zeros_like(tap_grads)
        for k in range(count):
            tap_grads[k : k + 1] = jnp.sum(tap_sums[k], axis=0, keepdims=True)
        tap_grads[count : count + 1] = (
            rate_scale * sg[...] * jnp.sum(decay_sums[...], axis=0, keepdims=True)
        )

        fetch.wait(14)
        out_rows.finish()
        plane.turn()
        xy_rows.run()
        send(4)
        lines[3].hop(0)

        def restore(i):
            here = tile_rows(i, 128)
            mp[here, 0 : 2 * own] = plain_dot(sto[here], gxy[...]).astype(jnp.bfloat16)

        loop(rows // 128, restore)

        def spread_back(i):
            some = tile_rows(i, 512)
            terms[:, pl.ds(pl.multiple_of(i * 512, 512), 512)] = (
                times_trans(mp[:, 0:own], wx[some]) + times_trans(mp[:, own : 2 * own], wy[some])
            ).astype(jnp.bfloat16)

        fetch.wait(10, 11)
        loop(width // 512, spread_back)
        store.start(0)
        lines[3].hop(1)
        add_up(2)
        plane.finish(weight_sum)
        add_up(3)
        for line in lines:
            line.finish()
        xy_rows.finish()
        store.wait(0)

    low, full = jnp.bfloat16, jnp.float32
    block = weight_terms.shape[0] // n_dp
    near, far = in_vmem(), in_any()
    return pl.pallas_call(
        kernel,
        out_shape=(
            shaped((size, 2 * own), low),
            shaped((8, own), full),
            shaped((rows, width), low),
            shaped((block, weight_terms.shape[1]), low),
            shaped((own_rows, width), low),
            shaped((width, own), low),
            shaped((width, 2 * own), low),
        ),
        in_specs=[far, near, near, far, far, far] + [near] * 5 + [far] * 12,
        out_specs=[near, near, far, near, near, far, far],
        scratch_shapes=[
            vmem_like(m) for m in (mixer_in, y_full, out_full, row_terms, merged_stored, *kept)
        ]
        + [
            pltpu.VMEM((rows, 2 * own), low),
            pltpu.VMEM((rows, width), low),
            pltpu.VMEM((rows, own), full),
            pltpu.VMEM((own // LANES, rows, LANES), full),
            pltpu.VMEM((own // LANES, rows, LANES), full),
            pltpu.VMEM((rows, wide), low),
            pltpu.VMEM((rows, wide), low),
            pltpu.VMEM((rows + 16, own), full),
            pltpu.VMEM((rows, wide), full),
            pltpu.VMEM((rows, RIM), low),
            pltpu.VMEM((rows, RIM), low),
            pltpu.VMEM((8, own), full),
            pltpu.VMEM((8, own), full),
            pltpu.VMEM((count, 8, own), full),
            pltpu.VMEM((8, own), full),
            pltpu.VMEM((2, 8, own), full),
            pltpu.VMEM((2, own), full),
            pltpu.VMEM((n_dp, 2, own), full),
            dma_sems(2),
            dma_sems(2),
            dma_sems(n_dp),
            dma_sems(n_dp),
            pltpu.SemaphoreType.DMA,
            dma_sems(15),
            dma_sems(1),
            pltpu.VMEM((parts, 2, n_line - 1, span, width), low),
            dma_sems(parts, 2, n_line - 1),
            dma_sems(parts, 2, n_line - 1),
            pltpu.VMEM((span, width), full),
            pltpu.VMEM((2, width // 5, 2 * own), low),
            dma_sems(2, 5),
        ]
        + ReducePlane.scratch(block, weight_terms.shape[1]),
        compiler_params=comm_params(6),
        name="recur_backward",
    )(
        mixer_in,
        to_place,
        to_stored,
        x_full,
        y_full,
        out_full,
        gates,
        taps,
        soft,
        slope,
        flags,
        *kept,
        weight_terms,
        row_terms,
        hidden_place,
        merged_stored,
    )


def column_parts(width, size=768):
    return [(c, min(size, width - c)) for c in range(0, width, size)]


def feed_forward(n_dp, n_line, hidden, gate, up, down, grads, grad_own):
    rows, width = hidden.shape
    units = gate.shape[1]
    own_rows = grad_own.shape[0]
    ready = grads.shape[0] // n_line
    late = own_rows - ready
    part = width // 4

    def kernel(*refs):
        hid_far, wg_far, wu_far, wd_far, grads_far, own_far = refs[:6]
        product_far, gup_far, back_far, gdown_far, ggate_far = refs[6:11]
        hid, wg, wu, wd, grad, slope, branch, product, ggate, gup, stage, back = refs[11:23]
        in_sems, out_sems, stage_sems, ls, lr = refs[23:]
        place = Place(n_dp, n_line)
        pairs = [(hid_far, hid), (wg_far, wg), (wu_far, wu), (wd_far, wd)]
        pairs += [
            (grads_far.at[pl.ds(q * ready, ready)], grad.at[pl.ds(q * own_rows, ready)])
            for q in range(n_line)
        ]
        mine = pl.ds(pl.multiple_of(place.t * own_rows + ready, 16), late)
        pairs.append((own_far.at[pl.ds(ready, late)], grad.at[mine]))
        fetch = Fetch(pairs, in_sems)
        fetch.start(*range(len(pairs)))
        store = Fetch(((product, product_far), (gup, gup_far), (back, back_far)), out_sems)
        place.meet()
        line = GatherLine(place, grad, own_rows, ready, late, ls, lr)
        line.step(0, own_far.at[pl.ds(ready, late)])
        columns = column_parts(units)
        fetch.wait(0, 1)
        for c, size in columns:
            cols = pl.ds(c, size)

            def gates(i, cols=cols):
                here = tile_rows(i, 256)
                branch[here, cols] = plain_dot(hid[here], wg[:, cols])

            loop(rows // 256, gates)
        line.step(1)
        fetch.wait(2)
        for c, size in columns:
            cols = pl.ds(c, size)

            def ups(i, cols=cols):
                here = tile_rows(i, 256)
                value = plain_dot(hid[here], wu[:, cols])
                active, bend = gelu_parts(branch[here, cols])
                product[here, cols] = (active * value).astype(jnp.bfloat16)
                branch[here, cols] = active
                slope[here, cols] = bend * value

            loop(rows // 256, ups)
        store.start(0)
        line.step(2)
        fetch.wait(*range(4, len(pairs)))
        line.finish()

        down_rows = RowProducts(grad, product, gdown_far, stage, stage_sems.at[0])
        down_rows.run()
        fetch.wait(3)
        for c, size in columns:
            cols = pl.ds(c, size)

            def backs(i, cols=cols):
                here = tile_rows(i, 256)
                value = plain_dot(grad[here], wd[:, cols])
                ggate[here, cols] = (value * slope[here, cols]).astype(jnp.bfloat16)
                gup[here, cols] = (value * branch[here, cols]).astype(jnp.bfloat16)

            loop(rows // 256, backs)
        store.start(1)
        for i in range(4):
            some = pl.ds(i * part, part)
            back[:, some] = (
                times_trans(ggate[...], wg[some]) + times_trans(gup[...], wu[some])
            ).astype(jnp.bfloat16)
        store.start(2)
        down_rows.finish()
        gate_rows = RowProducts(hid, ggate, ggate_far, stage, stage_sems.at[1])
        gate_rows.run()
        gate_rows.finish()
        store.wait(0, 1, 2)

    low, full = jnp.bfloat16, jnp.float32
    return pl.pallas_call(
        kernel,
        out_shape=(
            shaped((rows, units), low),
            shaped((rows, units), low),
            shaped((rows, width), low),
            shaped((width, units), low),
            shaped((width, units), low),
        ),
        in_specs=[in_any()] * 6,
        out_specs=[in_any()] * 5,
        scratch_shapes=[vmem_like(m) for m in (hidden, gate, up, down)]
        + [
            pltpu.VMEM((n_line * own_rows, width), low),
            pltpu.VMEM((rows, units), full),
            pltpu.VMEM((rows, units), full),
            pltpu.VMEM((rows, units), low),
            pltpu.VMEM((rows, units), low),
            pltpu.VMEM((rows, units), low),
            pltpu.VMEM((2, part, units), low),
            pltpu.VMEM((rows, width), low),
            dma_sems(5 + n_line),
            dma_sems(3),
            dma_sems(2, 4),
            dma_sems(2, n_line - 1),
            dma_sems(2, n_line - 1),
        ],
        compiler_params=comm_params(7),
        name="feed_forward",
    )(hidden, gate, up, down, grads, grad_own)


def matches(mesh):
    return mesh.shape["dp"] == 8 and mesh.shape["tensor"] == 4


def local_blocks(
    tokens,
    norm_gain,
    x_weight,
    y_weight,
    conv_weight,
    recur_gate_weight,
    input_gate_weight,
    decay_param,
    out_weight,
    mlp_gain,
    gate_weight,
    up_weight,
    down_weight,
    seq_lengths,
    token_order,
    cotangent,
):
    n_dp, n_tensor = lax.axis_size("dp"), lax.axis_size("tensor")
    tensor_index = lax.axis_index("tensor")
    dp_index = lax.axis_index("dp")
    tok_rows, width = tokens.shape
    row_count = tok_rows * n_tensor
    own_width = conv_weight.shape[1]
    kernel_taps = conv_weight.shape[0]
    edge_rows = kernel_taps - 1
    dp_width = norm_gain.shape[0]
    gate_rows = recur_gate_weight.shape[0]
    own_start = tensor_index * tok_rows

    gains = jnp.concatenate([norm_gain, mlp_gain])
    spare = gate_rows * 128 - gains.shape[0]
    gains = jnp.pad(gains, (0, spare)).reshape(gate_rows, 128)
    minor = jnp.concatenate([recur_gate_weight, input_gate_weight, gains], axis=1)
    own_order = (token_order - dp_index * row_count).astype(jnp.int32)
    order_rows = jnp.broadcast_to(own_order[None, :], (8, tok_rows))
    x_full, y_full, out_full, minor_full, tok_all, order_full = first_gather(
        n_dp, n_tensor, (x_weight, y_weight, out_weight.T, minor), tokens, order_rows
    )
    late_up, late_down, _ = lax.optimization_barrier((up_weight, down_weight.T, tok_all))
    up_full = lax.all_gather(late_up, "dp", axis=0, tiled=True)
    down_full = lax.all_gather(late_down, "dp", axis=0, tiled=True)
    order_all = order_full.reshape(n_tensor, 8, tok_rows)[:, 0].reshape(row_count)
    gain_rows = minor_full[:, 2 * own_width :].reshape(n_dp, -1)
    first_gain = gain_rows[:, :dp_width].reshape(1, width).astype(jnp.float32)
    second_gain = gain_rows[:, dp_width : 2 * dp_width].reshape(1, width).astype(jnp.float32)
    row_index = jnp.arange(row_count, dtype=jnp.int32)
    hits = row_index[:, None] == order_all[None, :]
    to_place = hits.astype(jnp.bfloat16)
    to_stored = (order_all[:, None] == row_index[None, :]).astype(jnp.bfloat16)
    places = dp_index * row_count + jnp.arange(-8, row_count + 8, dtype=jnp.int32)
    inside = (jnp.arange(row_count + 16) >= 8) & (jnp.arange(row_count + 16) < row_count + 8)
    ends = jnp.cumsum(seq_lengths)
    segment = segment_of(places, ends)
    starts = (places == 0) | (segment != segment_of(places - 1, ends))
    columns = [starts] + [
        segment_of(places - shift, ends) == segment for shift in range(1, kernel_taps)
    ]
    columns += [jnp.zeros_like(starts)] * (8 - len(columns))
    flags = (jnp.stack(columns, axis=1) & inside[:, None]).astype(jnp.float32)
    live_own = (token_order < ends[-1]).astype(jnp.float32)
    grad_in_own = (cotangent.astype(jnp.float32) * live_own[:, None]).astype(jnp.bfloat16)
    soft = jax.nn.softplus(-decay_param).reshape(1, own_width)
    slope = jax.nn.sigmoid(-decay_param).reshape(1, own_width)
    hidden_place, *kept, merged_stored, mixer_terms, gates_wide, grad_rows = recur_forward(
        n_dp,
        n_tensor,
        tok_all,
        grad_in_own,
        to_place,
        to_stored,
        x_full,
        y_full,
        out_full,
        first_gain,
        minor_full,
        conv_weight,
        soft,
        flags,
    )
    after_own, hidden_two, gate_full = middle_gather(
        n_dp, n_tensor, mixer_terms, tokens, second_gain, (gate_weight,)
    )
    product, grad_up_pre, back_terms, grad_down, grad_gate = feed_forward(
        n_dp,
        n_tensor,
        hidden_two,
        gate_full,
        up_full,
        down_full,
        grad_rows,
        grad_in_own,
    )
    down_sum = lax.psum_scatter(grad_down, "dp", scatter_dimension=0, tiled=True)
    grad_after_own, second_part, mixer_in, gate_sum, grad_up, feed_terms = middle_sums(
        n_dp,
        n_tensor,
        back_terms,
        after_own,
        second_gain,
        grad_in_own,
        grad_gate,
        hidden_two,
        grad_up_pre,
        product,
        down_full,
    )
    (
        gate_grads,
        tap_grads,
        one_terms,
        up_sum,
        feed_out,
        grad_out_mat,
        grad_xy_mat,
    ) = recur_backward(
        n_dp,
        n_tensor,
        mixer_in,
        to_place,
        to_stored,
        x_full,
        y_full,
        out_full,
        gates_wide,
        conv_weight,
        soft,
        slope,
        flags,
        kept,
        grad_up,
        feed_terms,
        hidden_place,
        merged_stored,
    )
    output = (after_own + feed_out.astype(jnp.float32)) * live_own[:, None]
    output = output.astype(jnp.bfloat16)
    grad_tokens, small_sum, gain_sums, xy_sum, out_sum, gates_sum = last_sums(
        n_dp,
        n_tensor,
        one_terms,
        tokens,
        first_gain,
        grad_after_own,
        second_part,
        tap_grads,
        (grad_xy_mat, grad_out_mat, gate_grads),
    )
    xy_sum, gates_sum = xy_sum.astype(jnp.float32), gates_sum.astype(jnp.float32)
    own_gains = lax.dynamic_slice_in_dim(gain_sums, dp_index * dp_width, dp_width, 1)
    return (
        output,
        grad_tokens,
        own_gains[1],
        xy_sum[:, :own_width],
        xy_sum[:, own_width:],
        small_sum[:kernel_taps],
        gates_sum[:, :own_width],
        gates_sum[:, own_width:],
        small_sum[kernel_taps],
        out_sum.astype(jnp.float32).T,
        own_gains[0],
        gate_sum.astype(jnp.float32),
        up_sum.astype(jnp.float32),
        down_sum.astype(jnp.float32).T,
    )


def solution(mesh):
    in_specs = (
        P(("dp", "tensor"), None),
        P("dp"),
        P("dp", "tensor"),
        P("dp", "tensor"),
        P(None, "tensor"),
        P("dp", "tensor"),
        P("dp", "tensor"),
        P("tensor"),
        P("tensor", "dp"),
        P("dp"),
        P("dp", "tensor"),
        P("dp", "tensor"),
        P("tensor", "dp"),
        P(),
        P(("dp", "tensor")),
        P(("dp", "tensor"), None),
    )
    out_specs = (
        P(("dp", "tensor"), None),
        P(("dp", "tensor"), None),
        P("dp"),
        P("dp", "tensor"),
        P("dp", "tensor"),
        P(None, "tensor"),
        P("dp", "tensor"),
        P("dp", "tensor"),
        P("tensor"),
        P("tensor", "dp"),
        P("dp"),
        P("dp", "tensor"),
        P("dp", "tensor"),
        P("tensor", "dp"),
    )
    fits = matches(mesh)
    local = local_blocks if fits else local_general
    return jax.shard_map(local, mesh=mesh, in_specs=in_specs, out_specs=out_specs, check_vma=False)
```

```python
import jax
import jax.numpy as jnp
from jax import lax
from jax.experimental import pallas as pl
from jax.experimental.pallas import tpu as pltpu
from jax.sharding import PartitionSpec as P

epsilon = 1e-06
rate_scale = 8.0


def from_behind(block, axis, distance):
    devices = range(lax.axis_size(axis))
    route = [(i - distance, i) for i in devices if i - distance in devices]
    return lax.ppermute(block, axis, route)


def extended_2(array, sides, width):
    for axis, dim in sides:
        size, length = (lax.axis_size(axis), array.shape[dim])
        up = [(i, (i + 1) % size) for i in range(size - 1)]
        down = [(j, i) for i, j in up]
        last = lax.slice_in_dim(array, length - width, length, axis=dim)
        leading = lax.slice_in_dim(array, 0, width, axis=dim)
        before = lax.ppermute(last, axis, up)
        after = lax.ppermute(leading, axis, down)
        array = jnp.concatenate([before, array, after], axis=dim)
    return array


def entering(value, axis, join, neutral, backward):
    count, mine = (lax.axis_size(axis), lax.axis_index(axis))
    pieces = jax.tree.map(lambda part: lax.all_gather(part, axis), value)
    if backward:
        pieces = jax.tree.map(lambda part: part[::-1], pieces)
        mine = count - 1 - mine
    total = jax.tree.map(
        lambda part, zero: jnp.full_like(part, 0) + jnp.asarray(zero, part.dtype), value, neutral
    )

    def lap(position, total):
        longer = join(total, jax.tree.map(lambda part: part[position], pieces))
        return jax.tree.map(lambda new, old: jnp.where(position < mine, new, old), longer, total)

    return lax.fori_loop(0, count - 1, lap, total)


def rms_scale(values, gain):
    return values * lax.rsqrt(jnp.mean(values * values, axis=-1, keepdims=True) + epsilon) * gain


def norm_back(values, gain, grad):
    inv_root = lax.rsqrt(jnp.mean(values * values, axis=-1, keepdims=True) + epsilon)
    normed = values * inv_root
    upstream = grad * gain
    grad_values = inv_root * (
        upstream - normed * jnp.mean(upstream * normed, axis=-1, keepdims=True)
    )
    return (grad_values, normed)


def segment_of(places, ends):
    return jnp.sum((ends[None, :] <= places[:, None]).astype(jnp.int32), axis=1)


def pair_step(early, later):
    return (early[0] * later[0], later[0] * early[1] + later[1])


def plain_dot(left, right):
    return jnp.dot(left, right, preferred_element_type=jnp.float32)


def times_trans(left, right):
    return lax.dot_general(
        left, right, (((1,), (1,)), ((), ())), preferred_element_type=jnp.float32
    )


def trans_times(left, right):
    return lax.dot_general(
        left, right, (((0,), (0,)), ((), ())), preferred_element_type=jnp.float32
    )


def gelu_tanh(values):
    return jax.nn.gelu(values, approximate=True)


def collect(
    norm_gain,
    mlp_gain,
    x_weight,
    y_weight,
    recur_gate_weight,
    input_gate_weight,
    gate_weight,
    up_weight,
    out_weight,
    down_weight,
):
    return (
        lax.all_gather(norm_gain, "dp", axis=0, tiled=True),
        lax.all_gather(mlp_gain, "dp", axis=0, tiled=True),
        lax.all_gather(x_weight, "dp", axis=0, tiled=True),
        lax.all_gather(y_weight, "dp", axis=0, tiled=True),
        lax.all_gather(recur_gate_weight, "dp", axis=0, tiled=True),
        lax.all_gather(input_gate_weight, "dp", axis=0, tiled=True),
        lax.all_gather(gate_weight, "dp", axis=0, tiled=True),
        lax.all_gather(up_weight, "dp", axis=0, tiled=True),
        lax.all_gather(out_weight, "dp", axis=1, tiled=True),
        lax.all_gather(down_weight, "dp", axis=1, tiled=True),
    )


def row_sums(term_rows, tok_rows):
    return lax.psum_scatter(
        term_rows(jnp.int32(0), lax.axis_size("tensor") * tok_rows).astype(jnp.bfloat16),
        "tensor",
        scatter_dimension=0,
        tiled=True,
    ).astype(jnp.float32)


def spread_rows(values):
    return lax.all_gather(values, "tensor", axis=0, tiled=True)


def local_general(
    tokens,
    norm_gain,
    x_weight,
    y_weight,
    conv_weight,
    recur_gate_weight,
    input_gate_weight,
    decay_param,
    out_weight,
    mlp_gain,
    gate_weight,
    up_weight,
    down_weight,
    seq_lengths,
    token_order,
    cotangent,
):
    n_tensor = lax.axis_size("tensor")
    tensor_index = lax.axis_index("tensor")
    dp_index = lax.axis_index("dp")
    tok_rows = tokens.shape[0]
    row_count = tok_rows * n_tensor
    own_width = conv_weight.shape[1]
    kernel_taps = conv_weight.shape[0]
    edge_rows = kernel_taps - 1
    dp_width = norm_gain.shape[0]
    own_start = tensor_index * tok_rows
    shards = (
        norm_gain,
        mlp_gain,
        x_weight,
        y_weight,
        recur_gate_weight,
        input_gate_weight,
        gate_weight,
        up_weight,
        out_weight,
        down_weight,
    )
    (
        gain_one,
        gain_two,
        x_full,
        y_full,
        recur_full,
        input_full,
        gate_full,
        up_full,
        out_full,
        down_full,
    ) = collect(*shards)
    block_size = recur_full.shape[0]
    first_gain = gain_one.astype(jnp.float32)
    second_gain = gain_two.astype(jnp.float32)
    both_gates = jnp.concatenate([recur_full, input_full], axis=1)
    tok_own = tokens.astype(jnp.float32)
    own_order = token_order - dp_index * row_count
    first_rows = rms_scale(tok_own, first_gain).astype(jnp.bfloat16)
    first_all, cot_all, order_all = (
        lax.all_gather(first_rows, "tensor", axis=0, tiled=True),
        lax.all_gather(cotangent, "tensor", axis=0, tiled=True),
        lax.all_gather(own_order, "tensor", axis=0, tiled=True),
    )
    row_index = jnp.arange(row_count, dtype=jnp.int32)
    inverse = jnp.zeros((row_count,), jnp.int32).at[order_all].set(row_index)
    hidden_place = jnp.take(first_all, inverse, axis=0)
    places = dp_index * row_count + row_index
    ends = jnp.cumsum(seq_lengths)
    segment = segment_of(places, ends)
    starts = (places == 0) | (segment != segment_of(places - 1, ends))
    live = (places < ends[-1]).astype(jnp.float32)
    live_stored = jnp.take(live, order_all, axis=0)
    same = [
        (segment_of(places - shift, ends) == segment).astype(jnp.float32)
        for shift in range(kernel_taps)
    ]
    low_edge = tensor_index * own_width
    own_blocks = (low_edge + jnp.arange(own_width, dtype=jnp.int32)) // block_size
    first_block = low_edge // block_size
    block_count = own_width // block_size + 2

    def block_start(index):
        return (first_block + index) * block_size - low_edge + block_size

    def block_mask(index):
        inside = own_blocks == first_block + index
        return jnp.concatenate([inside, inside])

    def convolve(extended, kernel):
        return sum(
            (
                kernel[shift][None, :]
                * extended[edge_rows - shift : edge_rows - shift + row_count]
                * same[shift][:, None]
                for shift in range(kernel_taps)
            )
        )

    def gates(conv_vals, pre_recur, pre_input, decay_vals):
        log_rate = -rate_scale * jax.nn.sigmoid(pre_recur) * jax.nn.softplus(-decay_vals)
        decay_rate = jnp.where(starts[:, None], 0.0, jnp.exp(log_rate))
        scale_in = jnp.where(starts[:, None], 1.0, jnp.sqrt(-jnp.expm1(2.0 * log_rate)))
        return (decay_rate, conv_vals * jax.nn.sigmoid(pre_input) * scale_in)

    def glu(gate_pre, up_pre):
        return gelu_tanh(gate_pre) * up_pre

    x_branch = plain_dot(hidden_place, x_full).astype(jnp.bfloat16)
    y_before = plain_dot(hidden_place, y_full)
    previous = from_behind(x_branch[row_count - edge_rows :], "dp", 1)
    extended = jnp.concatenate([previous, x_branch], axis=0).astype(jnp.float32)
    conv_out = convolve(extended, conv_weight)
    conv_wide = extended_2(conv_out.astype(jnp.bfloat16), (("tensor", 1),), block_size)
    pre_both = jnp.zeros((row_count, 2 * own_width), jnp.float32)
    for index in range(block_count):
        piece = lax.dynamic_slice_in_dim(conv_wide, block_start(index), block_size, 1)
        pre_both = pre_both + jnp.where(
            block_mask(index)[None, :], plain_dot(piece, both_gates), 0.0
        )
    (decay_rate, driven), gate_pull = jax.vjp(
        gates, conv_out, pre_both[:, :own_width], pre_both[:, own_width:], decay_param
    )
    cum_rate, local_state = lax.associative_scan(pair_step, (decay_rate, driven), axis=0)
    ident = (jnp.ones((own_width,), jnp.float32), jnp.zeros((own_width,), jnp.float32))
    rate_in, state_in = entering((cum_rate[-1], local_state[-1]), "dp", pair_step, ident, False)
    state = local_state + cum_rate * state_in[None, :]
    y_branch = gelu_tanh(y_before)
    merged = (state * y_branch).astype(jnp.bfloat16)
    merged_stored = jnp.take(merged, order_all, axis=0)

    def mixer_rows(begin, number):
        return plain_dot(merged_stored, out_full)

    after_own = tok_own + row_sums(mixer_rows, tok_rows)
    hidden_two = spread_rows(rms_scale(after_own, second_gain).astype(jnp.bfloat16))
    gate_pre = plain_dot(hidden_two, gate_full)
    up_pre = plain_dot(hidden_two, up_full)
    glu_out, glu_pull = jax.vjp(glu, gate_pre, up_pre)
    product = glu_out.astype(jnp.bfloat16)

    def down_rows(begin, number):
        return plain_dot(product, down_full)

    feed_out = row_sums(down_rows, tok_rows)
    live_own = lax.dynamic_slice_in_dim(live_stored, own_start, tok_rows, 0)
    output = ((after_own + feed_out) * live_own[:, None]).astype(jnp.bfloat16)
    grad_out = cot_all.astype(jnp.float32) * live_stored[:, None]
    fresh = lax.optimization_barrier((shards, grad_out))[0]
    (
        gain_one,
        gain_two,
        x_full,
        y_full,
        recur_full,
        input_full,
        gate_full,
        up_full,
        out_full,
        down_full,
    ) = collect(*fresh)
    first_gain = gain_one.astype(jnp.float32)
    second_gain = gain_two.astype(jnp.float32)
    both_gates = jnp.concatenate([recur_full, input_full], axis=1)
    down_in = grad_out.astype(jnp.bfloat16)
    grad_down = trans_times(product, down_in)
    grad_product = times_trans(down_in, down_full)
    grad_gate_pre, grad_up_pre = glu_pull(grad_product)
    grad_gate_pre = grad_gate_pre.astype(jnp.bfloat16)
    grad_up_pre = grad_up_pre.astype(jnp.bfloat16)
    grad_gate = trans_times(hidden_two, grad_gate_pre)
    grad_up = trans_times(hidden_two, grad_up_pre)

    def feed_rows(begin, number):
        return times_trans(grad_gate_pre, gate_full) + times_trans(grad_up_pre, up_full)

    grad_out_own = lax.dynamic_slice_in_dim(grad_out, own_start, tok_rows, 0)
    grad_two_own = row_sums(feed_rows, tok_rows)
    grad_norm_own, normed_two = norm_back(after_own, second_gain, grad_two_own)
    second_part = jnp.sum(grad_two_own * normed_two, axis=0)
    grad_after_own = grad_out_own + grad_norm_own
    mixer_in = spread_rows(grad_after_own.astype(jnp.bfloat16))
    grad_out_mat = trans_times(merged_stored, mixer_in)
    grad_merged = jnp.take(times_trans(mixer_in, out_full), inverse, axis=0)
    grad_state = grad_merged * y_branch
    gelu_pull = jax.vjp(gelu_tanh, y_before)[1]
    grad_y_before = gelu_pull(grad_merged * state)[0].astype(jnp.bfloat16)
    rate_next = jnp.concatenate([decay_rate[1:], jnp.ones((1, own_width), jnp.float32)], axis=0)
    rev_rate, local_lam = lax.associative_scan(
        pair_step, (rate_next, grad_state), reverse=True, axis=0
    )
    head_rate = decay_rate[0] * rev_rate[0]
    head_lam = decay_rate[0] * local_lam[0]
    factor_in, lam_in = entering((head_rate, head_lam), "dp", pair_step, ident, True)
    lam = local_lam + rev_rate * lam_in[None, :]
    state_prev = jnp.concatenate([state_in[None, :], state[:-1]], axis=0)
    grad_conv_local, grad_pre_recur, grad_pre_input, grad_decay_own = gate_pull(
        (lam * state_prev, lam)
    )
    grad_pre = jnp.concatenate([grad_pre_recur, grad_pre_input], axis=1).astype(jnp.bfloat16)
    grad_both = jnp.zeros((block_size, 2 * own_width), jnp.float32)
    grad_wide = jnp.zeros((row_count, own_width + 2 * block_size), jnp.float32)
    for index in range(block_count):
        begin = block_start(index)
        piece = lax.dynamic_slice_in_dim(conv_wide, begin, block_size, 1)
        masked = jnp.where(block_mask(index)[None, :], grad_pre, jnp.zeros((), jnp.bfloat16))
        grad_both = grad_both + trans_times(piece, masked)
        added = lax.dynamic_slice_in_dim(grad_wide, begin, block_size, 1) + times_trans(
            masked, both_gates
        )
        grad_wide = lax.dynamic_update_slice_in_dim(grad_wide, added, begin, 1)
    grad_recur = grad_both[:, :own_width]
    grad_input = grad_both[:, own_width:]
    rims = jnp.concatenate(
        [grad_wide[:, :block_size], grad_wide[:, own_width + block_size :]], axis=1
    )
    arrived = extended_2(rims.astype(jnp.bfloat16), (("tensor", 1),), block_size).astype(rims.dtype)
    from_lower = jnp.pad(arrived[:, :block_size], ((0, 0), (0, own_width - block_size)))
    from_upper = jnp.pad(arrived[:, 3 * block_size :], ((0, 0), (own_width - block_size, 0)))
    grad_conv = (
        grad_conv_local
        + grad_wide[:, block_size : block_size + own_width]
        + from_lower
        + from_upper
    )
    conv_pull = jax.vjp(convolve, extended, conv_weight)[1]
    grad_extended, grad_kernel = conv_pull(grad_conv)
    returned = from_behind(grad_extended[:edge_rows], "dp", -1)
    grad_x_branch = grad_extended[edge_rows:] + jnp.concatenate(
        [jnp.zeros((row_count - edge_rows, own_width), jnp.float32), returned], axis=0
    )
    grad_x_low = grad_x_branch.astype(jnp.bfloat16)
    grad_x_stored = jnp.take(grad_x_low, order_all, axis=0)
    grad_y_stored = jnp.take(grad_y_before, order_all, axis=0)
    grad_x_mat = trans_times(first_all, grad_x_stored)
    grad_y_mat = trans_times(first_all, grad_y_stored)

    def mixer_back_rows(begin, number):
        return times_trans(grad_x_stored, x_full) + times_trans(grad_y_stored, y_full)

    grad_one_own = row_sums(mixer_back_rows, tok_rows)
    grad_norm_one, normed_one = norm_back(tok_own, first_gain, grad_one_own)
    first_part = jnp.sum(grad_one_own * normed_one, axis=0)
    grad_tokens = grad_after_own + grad_norm_one
    chosen = jnp.arange(n_tensor, dtype=jnp.int32) == tensor_index
    kernel_tile = jnp.where(chosen[:, None, None], grad_kernel[None, :, :], 0.0)
    decay_tile = jnp.where(chosen[:, None], grad_decay_own[None, :], 0.0)
    small = lax.psum((first_part, second_part, kernel_tile, decay_tile), ("dp", "tensor"))
    grad_first_gain = lax.dynamic_slice_in_dim(small[0], dp_index * dp_width, dp_width, 0)
    grad_second_gain = lax.dynamic_slice_in_dim(small[1], dp_index * dp_width, dp_width, 0)
    grad_kernel_sum = lax.dynamic_index_in_dim(small[2], tensor_index, 0, keepdims=False)
    grad_decay = lax.dynamic_index_in_dim(small[3], tensor_index, 0, keepdims=False)
    sums = (
        lax.psum_scatter(
            grad_x_mat.astype(jnp.bfloat16), "dp", scatter_dimension=0, tiled=True
        ).astype(jnp.float32),
        lax.psum_scatter(
            grad_y_mat.astype(jnp.bfloat16), "dp", scatter_dimension=0, tiled=True
        ).astype(jnp.float32),
        lax.psum_scatter(
            grad_recur.astype(jnp.bfloat16), "dp", scatter_dimension=0, tiled=True
        ).astype(jnp.float32),
        lax.psum_scatter(
            grad_input.astype(jnp.bfloat16), "dp", scatter_dimension=0, tiled=True
        ).astype(jnp.float32),
        lax.psum_scatter(
            grad_gate.astype(jnp.bfloat16), "dp", scatter_dimension=0, tiled=True
        ).astype(jnp.float32),
        lax.psum_scatter(
            grad_up.astype(jnp.bfloat16), "dp", scatter_dimension=0, tiled=True
        ).astype(jnp.float32),
        lax.psum_scatter(
            grad_out_mat.astype(jnp.bfloat16), "dp", scatter_dimension=1, tiled=True
        ).astype(jnp.float32),
        lax.psum_scatter(
            grad_down.astype(jnp.bfloat16), "dp", scatter_dimension=1, tiled=True
        ).astype(jnp.float32),
    )
    return (
        output,
        grad_tokens,
        grad_first_gain,
        sums[0],
        sums[1],
        grad_kernel_sum,
        sums[2],
        sums[3],
        grad_decay,
        sums[6],
        grad_second_gain,
        sums[4],
        sums[5],
        sums[7],
    )


MESH = pl.DeviceIdType.MESH
VMEM_BYTES = 60 * 2**20


def remote(src, dst, send, recv, device):
    return pltpu.make_async_remote_copy(
        src_ref=src,
        dst_ref=dst,
        send_sem=send,
        recv_sem=recv,
        device_id=device,
        device_id_type=MESH,
    )


class Place:
    def __init__(self, n_dp, n_line):
        self.n_dp, self.n_line = n_dp, n_line
        self.d, self.t = lax.axis_index("dp"), lax.axis_index("tensor")
        self.core = lax.rem(self.d, 2)
        self.x = lax.rem(lax.div(self.d, 2), 2)
        self.y = lax.div(self.d, 4)

    def chip(self, flip_x, flip_y, flip_core=0):
        x = 1 - self.x if flip_x else self.x
        y = 1 - self.y if flip_y else self.y
        core = 1 - self.core if flip_core else self.core
        return y * 4 + x * 2 + core

    def at(self, flip_x=0, flip_y=0, flip_core=0):
        return (self.chip(flip_x, flip_y, flip_core), self.t)

    def up(self):
        return (self.d, lax.rem(self.t + 1, self.n_line))

    def down(self):
        return (self.d, lax.rem(self.t + self.n_line - 1, self.n_line))

    def meet(self, everyone=False):
        barrier = pltpu.get_barrier_semaphore()

        def greet(device):
            pl.semaphore_signal(barrier, inc=1, device_id=device, device_id_type=MESH)

        if everyone:
            for i in range(1, self.n_dp):
                greet((lax.rem(self.d + i, self.n_dp), self.t))
            for i in range(1, self.n_line):
                greet((self.d, lax.rem(self.t + i, self.n_line)))
            pl.semaphore_wait(barrier, self.n_dp + self.n_line - 2)
            return
        for flips in ((1, 0), (0, 1), (0, 0, 1)):
            greet(self.at(*flips))
        below, above = self.t > 0, self.t < self.n_line - 1

        @pl.when(below)
        def _():
            greet(self.down())

        @pl.when(above)
        def _():
            greet(self.up())

        pl.semaphore_wait(barrier, 3 + below.astype(jnp.int32) + above.astype(jnp.int32))


class Fetch:
    def __init__(self, pairs, sems):
        self.copies = [
            pltpu.make_async_copy(src, dst, sems.at[i]) for i, (src, dst) in enumerate(pairs)
        ]

    def start(self, *which):
        for i in which:
            self.copies[i].start()

    def wait(self, *which):
        for i in which:
            self.copies[i].wait()


def vmem_like(array):
    return pltpu.VMEM(array.shape, array.dtype)


class Kept:
    def __init__(self, src, dst, held, sems):
        self.there = pltpu.make_async_copy(src, held, sems.at[0])
        self.back = pltpu.make_async_copy(held, dst, sems.at[1])

    def begin(self):
        self.there.start()

    def turn(self):
        self.there.wait()
        self.back.start()

    def finish(self):
        self.back.wait()


class GatherPlane:
    def __init__(self, place, src, dst, send, recv, local, held):
        self.p, self.src, self.dst = place, src, dst
        self.rows = src.shape[0]
        self.send, self.recv = send, recv
        self.keep = Kept(src, self.block(0, 0), held, local)

    def block(self, fx, fy, fc=0, part=None):
        first = self.p.chip(fx, fy, fc) * self.rows
        size = self.rows
        if part is not None:
            size = self.rows // 2
            first = first + part * size
        return self.dst.at[pl.ds(pl.multiple_of(first, 16), size)]

    def copy(self, i, src, dst, device):
        return remote(src, dst, self.send.at[i], self.recv.at[i], device)

    def outgoing(self, i):
        at, block = self.p.at, self.block
        if i == 0:
            return self.copy(0, self.src, block(0, 0), at(1, 0))
        if i == 1:
            return self.copy(1, self.src, block(0, 0), at(0, 1))
        if i == 2:
            return self.copy(2, self.src, block(0, 0), at(0, 0, 1))
        if i == 3:
            return self.copy(3, block(1, 0, 0, 0), block(1, 0, 0, 0), at(0, 1))
        if i == 4:
            return self.copy(4, block(0, 1, 0, 1), block(0, 1, 0, 1), at(1, 0))
        spot = ((1, 0), (0, 1), (1, 1, 0, 0), (1, 1, 0, 1))[i - 5]
        return self.copy(i, block(*spot), block(*spot), at(0, 0, 1))

    def arrive(self, i):
        spot = (
            (1, 0),
            (0, 1),
            (0, 0, 1),
            (1, 1, 0, 0),
            (1, 1, 0, 1),
            (1, 0, 1),
            (0, 1, 1),
            (1, 1, 1, 0),
            (1, 1, 1, 1),
        )[i]
        here = self.block(*spot)
        self.copy(i, here, here, self.p.at(0, 0, 1)).wait_recv()

    def begin(self):
        for i in (0, 1, 2):
            self.outgoing(i).start()
        self.keep.begin()

    def forward(self):
        self.keep.turn()
        self.arrive(0)
        self.outgoing(3).start()
        self.arrive(1)
        self.outgoing(4).start()
        self.outgoing(5).start()
        self.outgoing(6).start()

    def share(self):
        self.arrive(3)
        self.outgoing(7).start()
        self.arrive(4)
        self.outgoing(8).start()

    def finish(self):
        for i in (2, 5, 6, 7, 8):
            self.arrive(i)
        for i in range(9):
            self.outgoing(i).wait_send()
        self.keep.finish()


class GatherLine:
    def __init__(self, place, dst, rows, begin, span, send, recv):
        self.p, self.dst, self.rows = place, dst, rows
        self.begin, self.span = begin, span
        self.send, self.recv = send, recv
        self.last = place.n_line - 1

    def block(self, owner):
        first = owner * self.rows + self.begin
        return self.dst.at[pl.ds(pl.multiple_of(first, 8), self.span)]

    def copy(self, way, k, owner, source=None):
        to = self.p.up() if way == 0 else self.p.down()
        block = self.block(owner)
        return remote(
            block if source is None else source,
            block,
            self.send.at[way, k],
            self.recv.at[way, k],
            to,
        )

    def step(self, k, source=None):
        t, last = self.p.t, self.last
        if k > 0:
            self.arrive(k - 1)

        @pl.when((t < last) & (t >= k))
        def _():
            self.copy(0, k, t - k, source).start()

        @pl.when((t > 0) & (t + k <= last))
        def _():
            self.copy(1, k, t + k, source).start()

    def arrive(self, k):
        t, last = self.p.t, self.last

        @pl.when(t >= k + 1)
        def _():
            self.copy(0, k, t - 1 - k).wait_recv()

        @pl.when(t + k + 1 <= last)
        def _():
            self.copy(1, k, t + 1 + k).wait_recv()

    def finish(self):
        t, last = self.p.t, self.last
        self.arrive(last - 1)
        for k in range(last):

            @pl.when((t < last) & (t >= k))
            def _():
                self.copy(0, k, t - k).wait_send()

            @pl.when((t > 0) & (t + k <= last))
            def _():
                self.copy(1, k, t + k).wait_send()


class ReduceLine:
    def __init__(self, place, terms, rows, begin, span, inbox, send, recv):
        self.p, self.terms, self.rows = place, terms, rows
        self.begin, self.span = begin, span
        self.inbox = inbox
        self.send, self.recv = send, recv
        self.last = place.n_line - 1

    def own(self, owner):
        first = owner * self.rows + self.begin
        return self.terms.at[pl.ds(pl.multiple_of(first, 16), self.span)]

    def copy(self, way, j, source):
        to = self.p.up() if way == 0 else self.p.down()
        return remote(
            source, self.inbox.at[way, j], self.send.at[way, j], self.recv.at[way, j], to
        )

    def ends(self):
        t, last = self.p.t, self.last

        @pl.when(t == 0)
        def _():
            for j in range(last):
                self.copy(0, j, self.own(last - j)).start()

        @pl.when(t == last)
        def _():
            for j in range(last):
                self.copy(1, j, self.own(j)).start()

    def sent(self):
        t, last = self.p.t, self.last

        @pl.when(t == 0)
        def _():
            for j in range(last):
                self.copy(0, j, self.own(last - j)).wait_send()

        @pl.when(t == last)
        def _():
            for j in range(last):
                self.copy(1, j, self.own(j)).wait_send()

    def hand_on(self, way, j):
        term = self.own(self.last - j if way == 0 else j)
        self.copy(way, j, term).wait_recv()
        self.inbox[way, j] = term[...] + self.inbox[way, j]
        self.copy(way, j, self.inbox.at[way, j]).start()

    def hop(self, k):
        t, last = self.p.t, self.last

        @pl.when(t == k + 1)
        def _():
            for j in range(last - 1 - k):
                self.hand_on(0, j)

        @pl.when(t == last - 1 - k)
        def _():
            for j in range(last - 1 - k):
                self.hand_on(1, j)

    def total(self, result):
        t, last = self.p.t, self.last
        result[...] = self.own(t)[...].astype(jnp.float32)

        @pl.when(t > 0)
        def _():
            j = last - t
            self.copy(0, j, self.inbox.at[0, 0]).wait_recv()
            result[...] += self.inbox[0, j].astype(jnp.float32)

        @pl.when(t < last)
        def _():
            self.copy(1, t, self.inbox.at[0, 0]).wait_recv()
            result[...] += self.inbox[1, t].astype(jnp.float32)

    def finish(self):
        t, last = self.p.t, self.last
        for j in range(last - 1):

            @pl.when((t > 0) & (t < last - j))
            def _():
                self.copy(0, j, self.inbox.at[0, j]).wait_send()

            @pl.when((t < last) & (t > j))
            def _():
                self.copy(1, j, self.inbox.at[1, j]).wait_send()


def add_rows(into, other, result=None):
    result = into if result is None else result

    def tile(i, carry):
        rows = pl.ds(pl.multiple_of(i * 16, 16), 16)
        result[rows] = into[rows] + other[rows]
        return carry

    lax.fori_loop(0, into.shape[0] // 16, tile, None)


class ReducePlane:
    chips = ((0, 0), (1, 0), (0, 1), (1, 1))

    def __init__(self, place, terms, scratch):
        self.p, self.terms = place, terms
        self.held, self.near, self.along, self.last, self.send, self.recv, self.local = scratch
        self.rows = self.held.shape[1]
        self.half = self.rows // 2

    @staticmethod
    def scratch(rows, width):
        return [
            pltpu.VMEM((4, rows, width), jnp.bfloat16),
            pltpu.VMEM((4, rows, width), jnp.bfloat16),
            pltpu.VMEM((4, rows // 2, width), jnp.bfloat16),
            pltpu.VMEM((2, rows // 2, width), jnp.bfloat16),
            pltpu.SemaphoreType.DMA((10,)),
            pltpu.SemaphoreType.DMA((10,)),
            pltpu.SemaphoreType.DMA((4,)),
        ]

    def block(self, k, other):
        first = self.p.chip(*self.chips[k], other) * self.rows
        return self.terms.at[pl.ds(pl.multiple_of(first, 16), self.rows)]

    def half_of(self, k, part):
        return self.held.at[k, pl.ds(part * self.half, self.half)]

    def load(self, k):
        return pltpu.make_async_copy(self.block(k, 0), self.held.at[k], self.local.at[k])

    def copy(self, i):
        at = self.p.at
        if i < 4:
            src, dst, to = self.block(i, 1), self.near.at[i], at(0, 0, 1)
        elif i < 8:
            src, to = (
                (self.half_of(1, 0), at(1, 0)),
                (self.half_of(3, 0), at(1, 0)),
                (self.half_of(2, 1), at(0, 1)),
                (self.half_of(3, 1), at(0, 1)),
            )[i - 4]
            dst = self.along.at[i - 4]
        else:
            src, to = ((self.half_of(2, 0), at(0, 1)), (self.half_of(1, 1), at(1, 0)))[i - 8]
            dst = self.last.at[i - 8]
        return remote(src, dst, self.send.at[i], self.recv.at[i], to)

    def begin(self):
        for k in (3, 1, 2, 0):
            self.copy(k).start()
            self.load(k).start()

    def cores(self):
        for k in (3, 1, 2, 0):
            self.load(k).wait()
            self.copy(k).wait_recv()
            add_rows(self.held.at[k], self.near.at[k])
            if k == 3:
                self.copy(5).start()
                self.copy(7).start()
            elif k == 1:
                self.copy(4).start()
            elif k == 2:
                self.copy(6).start()

    def turn(self):
        self.copy(5).wait_recv()
        add_rows(self.half_of(2, 0), self.along.at[1])
        self.copy(8).start()
        self.copy(7).wait_recv()
        add_rows(self.half_of(1, 1), self.along.at[3])
        self.copy(9).start()
        self.copy(4).wait_recv()
        add_rows(self.half_of(0, 0), self.along.at[0])
        self.copy(6).wait_recv()
        add_rows(self.half_of(0, 1), self.along.at[2])

    def finish(self, result):
        for part in (0, 1):
            self.copy(8 + part).wait_recv()
            rows = pl.ds(part * self.half, self.half)
            add_rows(self.half_of(0, part), self.last.at[part], result.at[rows])
        for i in range(10):
            self.copy(i).wait_send()


def dma_sems(*dims):
    return pltpu.SemaphoreType.DMA(dims)


def in_vmem():
    return pl.BlockSpec(memory_space=pltpu.VMEM)


def in_any():
    return pl.BlockSpec(memory_space=pl.ANY)


def comm_params(number):
    return pltpu.CompilerParams(
        collective_id=number, has_side_effects=True, vmem_limit_bytes=VMEM_BYTES
    )


def shaped(dims, kind):
    return jax.ShapeDtypeStruct(dims, kind)


def first_gather(n_dp, n_line, mats, rows_in, order):
    count = len(mats)
    parts = 2

    def kernel(*refs):
        srcs, (c, e) = refs[:count], refs[count : count + 2]
        dsts, (c_out, e_out) = refs[count + 2 : 2 * count + 2], refs[2 * count + 2 : 2 * count + 4]
        ps, pr, pl_sem, ls, lr, ll = refs[2 * count + 4 : 2 * count + 10]
        held = refs[2 * count + 10 :]
        place = Place(n_dp, n_line)
        place.meet()
        planes = [
            GatherPlane(place, a, b, ps.at[i], pr.at[i], pl_sem.at[i], held[i])
            for i, (a, b) in enumerate(zip(srcs, dsts))
        ]
        rows = c.shape[0]
        span = rows // parts
        lines = [
            GatherLine(place, c_out, rows, i * span, span, ls.at[i], lr.at[i])
            for i in range(parts)
        ]
        lines.append(
            GatherLine(place, e_out, e.shape[0], 0, e.shape[0], ls.at[parts], lr.at[parts])
        )
        for i in range(parts):
            lines[i].step(0, c.at[pl.ds(i * span, span)])
        lines[parts].step(0, e)
        early, late = planes[: count // 2], planes[count // 2 :]
        for part in early:
            part.begin()
        copies = []
        for i, (src, dst) in enumerate(((c, c_out), (e, e_out))):
            own = dst.at[pl.ds(pl.multiple_of(place.t * src.shape[0], 8), src.shape[0])]
            copies.append(Kept(src, own, held[count + i], ll.at[i]))
            copies[i].begin()
        for line in lines:
            line.step(1)
        for part in late:
            part.begin()
        for part in early:
            part.forward()
        for copy in copies:
            copy.turn()
        for line in lines:
            line.step(2)
        for part in early:
            part.share()
        for part in late:
            part.forward()
        for part in late:
            part.share()
        for part in lines + planes:
            part.finish()
        for copy in copies:
            copy.finish()

    return pl.pallas_call(
        kernel,
        out_shape=tuple(shaped((n_dp * m.shape[0], m.shape[1]), m.dtype) for m in mats)
        + (
            shaped((n_line * rows_in.shape[0], rows_in.shape[1]), rows_in.dtype),
            shaped((n_line * order.shape[0], order.shape[1]), order.dtype),
        ),
        in_specs=[in_any()] * (count + 2),
        out_specs=[in_any()] * (count + 2),
        scratch_shapes=[
            dma_sems(count, 9),
            dma_sems(count, 9),
            dma_sems(count, 2),
            dma_sems(parts + 1, 2, n_line - 1),
            dma_sems(parts + 1, 2, n_line - 1),
            dma_sems(2, 2),
        ]
        + [vmem_like(m) for m in (*mats, rows_in, order)],
        compiler_params=comm_params(1),
        name="first_gather",
    )(*mats, rows_in, order)


CHUNKS = 8
LAST_CHUNKS = 8


def line_scratch(n_line, span, width, chunks):
    hops = n_line - 1
    return [
        pltpu.VMEM((chunks, 2, hops, span, width), jnp.bfloat16),
        dma_sems(chunks, 2, hops),
        dma_sems(chunks, 2, hops),
        dma_sems(chunks, 2, hops),
        dma_sems(chunks, 2, hops),
        pltpu.VMEM((span, width), jnp.float32),
    ]


def sum_rows_and_spread(place, terms, scratch, finish_rows, spread, between):
    inbox, rs, rr, gs, gr, total = scratch
    span = total.shape[0]
    count = inbox.shape[0]
    rows = span * count
    hops = place.n_line - 1
    sums = [
        ReduceLine(place, terms, rows, c * span, span, inbox.at[c], rs.at[c], rr.at[c])
        for c in range(count)
    ]
    gathers = []
    if spread is not None:
        gathers = [
            GatherLine(place, spread, rows, c * span, span, gs.at[c], gr.at[c])
            for c in range(count)
        ]
    sums[0].ends()

    def total_of(c):
        sums[c].total(total)
        finish_rows(c, pl.ds(c * span, span), total)
        if gathers:
            gathers[c].step(0)

    stages = [lambda c, k=k: sums[c].hop(k) for k in range(hops - 1)] + [total_of]
    lags = [LAGS[min(k, len(LAGS) - 1)] for k in range(hops)]
    if gathers:
        stages += [lambda c, k=k: gathers[c].step(k) for k in range(1, hops)]
        lags += [lags[-1] + LAG_STEP * k for k in range(1, hops)]
    for i in range(count + lags[-1]):
        if i < count:
            sums[i].sent()
        if i + 1 < count:
            sums[i + 1].ends()
        for work, lag in zip(stages, lags):
            if 0 <= i - lag < count:
                work(i - lag)
        if i in between:
            between[i]()
    for part in gathers + sums:
        part.finish()


LAGS = (0, 1, 1)
LAG_STEP = 1


def middle_gather(n_dp, n_line, terms, tokens, gain, mats):
    rows, width = tokens.shape
    count = len(mats)

    def kernel(*refs):
        s, tok, gain_ref = refs[:3]
        srcs = refs[3 : 3 + count]
        after, hidden = refs[3 + count : 5 + count]
        dsts = refs[5 + count : 5 + 2 * count]
        ps, pr, pl_sem = refs[5 + 2 * count : 8 + 2 * count]
        held = refs[8 + 2 * count : 8 + 3 * count]
        scratch = refs[8 + 3 * count :]
        place = Place(n_dp, n_line)
        place.meet()
        planes = [
            GatherPlane(place, a, b, ps.at[i], pr.at[i], pl_sem.at[i], held[i])
            for i, (a, b) in enumerate(zip(srcs, dsts))
        ]
        planes[0].begin()

        def norm(c, here, total):
            values = tok[here].astype(jnp.float32) + total[...]
            after[here] = values
            low = rms_scale(values, gain_ref[...]).astype(jnp.bfloat16)
            first = pl.multiple_of(place.t * rows, 16) + c * total.shape[0]
            hidden[pl.ds(pl.multiple_of(first, 16), total.shape[0])] = low

        between = {5: planes[0].forward, 8: planes[0].share}
        sum_rows_and_spread(place, s, scratch, norm, hidden, between)
        for part in planes:
            part.finish()

    return pl.pallas_call(
        kernel,
        out_shape=(
            shaped((rows, width), jnp.float32),
            shaped((n_line * rows, width), jnp.bfloat16),
        )
        + tuple(shaped((n_dp * m.shape[0], m.shape[1]), m.dtype) for m in mats),
        in_specs=[in_vmem()] * 3 + [in_any()] * count,
        out_specs=[in_vmem()] * 2 + [in_any()] * count,
        scratch_shapes=[dma_sems(count, 9), dma_sems(count, 9), dma_sems(count, 2)]
        + [vmem_like(m) for m in mats]
        + line_scratch(n_line, rows // CHUNKS, width, CHUNKS),
        compiler_params=comm_params(2),
        name="middle_gather",
    )(terms, tokens, gain, *mats)


def middle_sums(n_dp, n_line, terms, after, gain, grad_in, mat, hidden, grad_up, product, down):
    rows, width = after.shape
    block = mat.shape[0] // n_dp
    wide = grad_up.shape[1]
    spread_rows = n_line * rows

    def kernel(*refs):
        s, after_ref, gain_ref, g_ref, src = refs[:5]
        hid_far, gu_far, pr_far, dw_far = refs[5:9]
        grad_after, gain_sum, spread, result, up_far, feed_far = refs[9:15]
        hid, gu, pr, dw, up_out, feed, sems = refs[15:22]
        rest = refs[22:]
        fetch = Fetch(
            [
                (hid_far, hid),
                (gu_far, gu),
                (pr_far, pr),
                (dw_far, dw),
                (feed, feed_far),
                (up_out.at[0], up_far.at[pl.ds(0, width // 2)]),
                (up_out.at[1], up_far.at[pl.ds(width // 2, width // 2)]),
            ],
            sems,
        )
        fetch.start(0, 1, 2, 3)
        place = Place(n_dp, n_line)
        place.meet()
        plane = ReducePlane(place, src, rest[:7])
        scratch = rest[7:]
        plane.begin()
        gain_sum[...] = jnp.zeros_like(gain_sum)

        def norm(c, here, total):
            grad = total[...]
            grad_rows, normed = norm_back(after_ref[here], gain_ref[...], grad)
            gain_sum[...] += jnp.sum(grad * normed, axis=0, keepdims=True)
            both = g_ref[here].astype(jnp.float32) + grad_rows
            grad_after[here] = both
            first = pl.multiple_of(place.t * rows, 16) + c * total.shape[0]
            spread[pl.ds(pl.multiple_of(first, 16), total.shape[0])] = both.astype(jnp.bfloat16)

        def feed_part(i):
            cols = pl.ds(i * (width // 4), width // 4)
            feed[:, cols] = times_trans(pr[...], dw[cols]).astype(jnp.bfloat16)

        def up_part(i):
            cols = pl.ds(i * (width // 4), width // 4)
            here = pl.ds((i % 2) * (width // 4), width // 4)
            up_out[i // 2, here] = trans_times(hid[:, cols], gu[...]).astype(jnp.bfloat16)

        def early():
            plane.cores()
            fetch.wait(0, 1)

        def two():
            up_part(0)

        def three():
            up_part(1)
            fetch.start(5)

        def four():
            up_part(2)

        def five():
            up_part(3)
            fetch.start(6)
            fetch.wait(2, 3)

        def six():
            plane.turn()
            feed_part(0)

        def seven():
            feed_part(1)

        def eight():
            feed_part(2)

        def nine():
            feed_part(3)
            fetch.start(4)

        steps = {1: early, 2: two, 3: three, 4: four, 5: five, 6: six, 7: seven, 8: eight, 9: nine}
        sum_rows_and_spread(place, s, scratch, norm, spread, steps)
        plane.finish(result)
        fetch.wait(4, 5, 6)

    low, full = jnp.bfloat16, jnp.float32
    near, far = in_vmem(), in_any()
    return pl.pallas_call(
        kernel,
        out_shape=(
            shaped((rows, width), full),
            shaped((1, width), full),
            shaped((spread_rows, width), low),
            shaped((block, mat.shape[1]), low),
            shaped((width, wide), low),
            shaped((spread_rows, width), low),
        ),
        in_specs=[near] * 4 + [far] * 5,
        out_specs=[near] * 4 + [far] * 2,
        scratch_shapes=[vmem_like(m) for m in (hidden, grad_up, product, down)]
        + [
            pltpu.VMEM((2, width // 2, wide), low),
            pltpu.VMEM((spread_rows, width), low),
            dma_sems(7),
        ]
        + ReducePlane.scratch(block, mat.shape[1])
        + line_scratch(n_line, rows // CHUNKS, width, CHUNKS),
        compiler_params=comm_params(3),
        name="middle_sums",
    )(terms, after, gain, grad_in, mat, hidden, grad_up, product, down)


class Exchange:
    def __init__(self, place, axis, src, slots, send, recv, local):
        self.p, self.src, self.slots = place, src, slots
        self.over_dp = axis == "dp"
        self.size = place.n_dp if self.over_dp else place.n_line
        self.me = place.d if self.over_dp else place.t
        self.send, self.recv, self.local = send, recv, local

    def copy(self, i):
        to = lax.rem(self.me + i, self.size)
        device = (to, self.p.t) if self.over_dp else (self.p.d, to)
        return remote(
            self.src, self.slots.at[self.me], self.send.at[i - 1], self.recv.at[i - 1], device
        )

    def mine(self):
        return pltpu.make_async_copy(self.src, self.slots.at[self.me], self.local)

    def begin(self):
        for i in range(1, self.size):
            self.copy(i).start()
        self.mine().start()

    def wait(self):
        self.mine().wait()
        for i in range(1, self.size):
            self.copy(i).wait()

    def finish(self):
        self.wait()
        total = self.slots[0]
        for i in range(1, self.size):
            total = total + self.slots[i]
        return total


def last_sums(n_dp, n_line, terms, tokens, gain, grad_after, second, small, mats):
    rows, width = tokens.shape
    count = len(mats)
    per = len(ReducePlane.scratch(16, 128))

    def kernel(*refs):
        s, tok, gain_ref, g_ref, second_ref, small_ref = refs[:6]
        srcs = refs[6 : 6 + count]
        grad_tok, small_out, first_out = refs[6 + count : 9 + count]
        results = refs[9 + count : 9 + 2 * count]
        rest = refs[9 + 2 * count :]
        own_first, row_sum = rest[count * per : count * per + 2]
        slots_a, slots_b, slots_c, slots_d = rest[count * per + 2 : count * per + 6]
        xs, xr, xl = rest[count * per + 6 : count * per + 9]
        scratch = rest[count * per + 9 :]
        place = Place(n_dp, n_line)
        place.meet(True)
        planes = [
            ReducePlane(place, srcs[i], rest[i * per : (i + 1) * per]) for i in range(count)
        ]
        for part in planes:
            part.begin()
        early = Exchange(place, "dp", small_ref, slots_a, xs.at[0], xr.at[0], xl.at[0])
        early.begin()
        gain = Exchange(place, "dp", second_ref, slots_d, xs.at[3], xr.at[3], xl.at[3])
        gain.begin()
        own_first[...] = jnp.zeros_like(own_first)

        def norm(c, here, total):
            grad = total[...]
            grad_rows, normed = norm_back(tok[here].astype(jnp.float32), gain_ref[...], grad)
            own_first[...] += jnp.sum(grad * normed, axis=0, keepdims=True)
            grad_tok[here] = g_ref[here] + grad_rows

        def cores():
            for part in planes:
                part.cores()

        def turn():
            for part in planes:
                part.turn()

        sum_rows_and_spread(place, s, scratch, norm, None, {0: cores, 5: turn})
        first = Exchange(place, "dp", own_first, slots_b, xs.at[1], xr.at[1], xl.at[1])
        first.begin()
        small_out[...] = early.finish()
        row_sum[0:1] = gain.finish()
        row_sum[1:2] = first.finish()
        both = Exchange(place, "tensor", row_sum, slots_c, xs.at[2], xr.at[2], xl.at[2])
        both.begin()
        for part, result in zip(planes, results):
            part.finish(result)
        first_out[...] = both.finish()

    return pl.pallas_call(
        kernel,
        out_shape=(
            shaped((rows, width), jnp.float32),
            shaped(small.shape, jnp.float32),
            shaped((2, width), jnp.float32),
        )
        + tuple(shaped((m.shape[0] // n_dp, m.shape[1]), jnp.bfloat16) for m in mats),
        in_specs=[in_vmem()] * 6 + [in_any()] * count,
        out_specs=[in_vmem()] * (3 + count),
        scratch_shapes=sum([ReducePlane.scratch(m.shape[0] // n_dp, m.shape[1]) for m in mats], [])
        + [
            pltpu.VMEM((1, width), jnp.float32),
            pltpu.VMEM((2, width), jnp.float32),
            pltpu.VMEM((n_dp,) + small.shape, jnp.float32),
            pltpu.VMEM((n_dp, 1, width), jnp.float32),
            pltpu.VMEM((n_line, 2, width), jnp.float32),
            pltpu.VMEM((n_dp, 1, width), jnp.float32),
            dma_sems(4, n_dp),
            dma_sems(4, n_dp),
            dma_sems(4),
        ]
        + line_scratch(n_line, rows // LAST_CHUNKS, width, LAST_CHUNKS),
        compiler_params=comm_params(4),
        name="last_sums",
    )(terms, tokens, gain, grad_after, second, small, *mats)


def loop(count, body, unroll=1):
    def step(i, carry):
        body(i)
        return carry

    lax.fori_loop(0, count, step, None, unroll=unroll)


def tile_rows(i, size, ahead=0):
    return pl.ds(pl.multiple_of(i * size + ahead, 8), size)


def moved_up(values, distance, count):
    size = values.shape[0]
    return pltpu.roll(values, (size - distance) % size, 0)[:count]


def take_lanes(ref, here):
    return jnp.concatenate([ref[c, here] for c in range(ref.shape[0])], axis=1)


def put_lanes(ref, here, values):
    for c in range(ref.shape[0]):
        ref[c, here] = values[:, c * LANES : (c + 1) * LANES]


def gelu_parts(values):
    inner = GELU_C * (values + 0.044715 * (values * values * values))
    tanh = jnp.tanh(inner)
    half = 0.5 * (1.0 + tanh)
    slope = half + 0.5 * values * (1.0 - tanh * tanh) * GELU_C * (
        1.0 + 3.0 * 0.044715 * (values * values)
    )
    return values * half, slope


GELU_C = 0.7978845608028654
RIM = 128
LANES = 128
TILE = 16


def one_minus_exp(values, exponential):
    series = jnp.ones_like(values)
    for term in range(9, 1, -1):
        series = 1.0 + values * (1.0 / term) * series
    return jnp.where(values > -0.35, -values * series, 1.0 - exponential)


def rate_and_scale(pre_recur, soft, start):
    sr = jax.nn.sigmoid(pre_recur)
    log_rate = -rate_scale * sr * soft
    decay = jnp.exp(log_rate)
    rate = jnp.where(start, 0.0, decay)
    scale = jnp.where(start, 1.0, jnp.sqrt(one_minus_exp(2.0 * log_rate, decay * decay)))
    return sr, rate, scale


class RimSwap:
    def __init__(self, place, own):
        self.odd = lax.rem(place.t, 2)
        self.partner = (place.d, place.t + 1 - 2 * self.odd)
        self.first = pl.multiple_of(RIM - RIM * self.odd, RIM)
        self.edge = pl.ds(pl.multiple_of((1 - self.odd) * own + self.odd * RIM, RIM), RIM)
        self.over_there = pl.ds(pl.multiple_of(self.odd * (own + RIM), RIM), RIM)
        self.beyond = pl.ds(pl.multiple_of((1 - self.odd) * (own + RIM), RIM), RIM)

    def block(self, index, size):
        return pl.ds(pl.multiple_of(self.first + index * size, RIM), size)


LATE_SHARE = 8


def recur_forward(
    n_dp,
    n_line,
    tok_all,
    cot,
    to_place,
    to_stored,
    x_full,
    y_full,
    out_full,
    gain,
    gates,
    taps,
    soft,
    flags,
):
    rows, width = tok_all.shape
    count, own = taps.shape
    size = gates.shape[0]
    wide = own + 2 * RIM
    blocks = (wide - RIM) // size
    chunk = rows // 8
    cot_rows = cot.shape[0] - cot.shape[0] // LATE_SHARE
    parts = 1

    def kernel(*refs):
        (tok_far, cot_ref, plc, sto, wx_far, wy_far, wo_far, gain_ref, gates_in, cw, sp, fl) = refs[:12]
        far, gw, cot_all = refs[12:23], refs[23], refs[24]
        tok, wx, wy, wo = refs[25:29]
        results = refs[29:40]
        hp, xext, y, conv_low, conv, pre_r, pre_i, rate, state, merged_st, terms = results
        (h, xf, local, cum, merged, agg, slots, hs, hr, es, er, el, gs, gr, gl) = refs[40:55]
        in_sems, out_sems, cot_held = refs[55:]
        fetch = Fetch(((tok_far, tok), (wx_far, wx), (wy_far, wy), (wo_far, wo)), in_sems)
        store = Fetch(zip(results, far), out_sems)
        fetch.start(0, 1, 2, 3)
        place = Place(n_dp, n_line)
        place.meet(True)
        swap = RimSwap(place, own)
        for side in range(2):
            first = side * wide
            gw[:, first : first + RIM] = jnp.zeros((size, RIM), jnp.bfloat16)
            gw[:, first + RIM : first + RIM + own] = gates_in[:, side * own : (side + 1) * own]
            gw[:, first + RIM + own : first + wide] = jnp.zeros((size, RIM), jnp.bfloat16)
        own_cot = cot_all.at[pl.ds(pl.multiple_of(place.t * cot_rows, 16), cot_rows)]
        cot_ref = cot_ref.at[pl.ds(0, cot_rows)]
        keep = Kept(cot_ref, own_cot, cot_held, gl)
        keep.begin()
        span = cot_rows // parts
        lines = [
            GatherLine(place, cot_all, cot_rows, c * span, span, gs.at[c], gr.at[c])
            for c in range(parts)
        ]
        for c, line in enumerate(lines):
            line.step(0, cot_ref.at[pl.ds(c * span, span)])

        def norm(i):
            here = tile_rows(i, TILE)
            h[here] = rms_scale(tok[here].astype(jnp.float32), gain_ref[...]).astype(jnp.bfloat16)

        fetch.wait(0)
        loop(rows // TILE, norm)
        fetch.wait(1)

        def project(i):
            here = tile_rows(i, 128)
            hp[here] = plain_dot(plc[here], h[...]).astype(jnp.bfloat16)
            xext[tile_rows(i, 128, 16)] = plain_dot(hp[here], wx[...]).astype(jnp.bfloat16)

        loop(rows // 128, project)
        store.start(0)
        edge = remote(
            xext.at[pl.ds(rows, 16)],
            xext.at[pl.ds(0, 16)],
            hs.at[0],
            hr.at[0],
            (lax.rem(place.d + 1, n_dp), place.t),
        )
        edge.start()
        keep.turn()
        for line in lines:
            line.step(1)

        def project_y(i):
            here = tile_rows(i, 128)
            y[here] = plain_dot(hp[here], wy[...])

        fetch.wait(2)
        loop(rows // 128, project_y)
        store.start(2)
        edge.wait()
        top = xext[pl.ds(0, 16)]
        xext[pl.ds(0, 16)] = jnp.where(place.d > 0, top, jnp.zeros_like(top))
        store.start(1)

        def widen(i):
            xf[tile_rows(i, TILE)] = xext[tile_rows(i, TILE)].astype(jnp.float32)

        loop(rows // TILE + 1, widen)

        def convolve(i):
            here = tile_rows(i, TILE)
            near = xf[pl.ds(pl.multiple_of(i * TILE + 8, 8), TILE + 8)]
            same = fl[tile_rows(i, TILE, 8)]
            total = cw[0:1] * near[8:]
            for k in range(1, count):
                total += cw[k : k + 1] * moved_up(near, 8 - k, TILE) * same[:, k : k + 1]
            conv[here] = total
            conv_low[here, RIM : RIM + own] = total.astype(jnp.bfloat16)

        loop(rows // TILE, convolve)
        store.start(4)
        rim = remote(
            conv_low.at[:, swap.edge],
            conv_low.at[:, swap.over_there],
            hs.at[1],
            hr.at[1],
            swap.partner,
        )
        rim.start()
        for i in range(blocks):
            index = lax.rem(i + swap.odd, blocks)
            cols = swap.block(index, size)
            other = pl.ds(pl.multiple_of(wide + swap.first + index * size, RIM), size)
            if i == blocks - 1:
                rim.wait()
            pre_r[:, cols] = plain_dot(conv_low[:, cols], gw[:, cols])
            pre_i[:, cols] = plain_dot(conv_low[:, cols], gw[:, other])

        store.start(3, 5, 6)

        def drive(i):
            here = tile_rows(i, TILE)
            start = fl[tile_rows(i, TILE, 8)][:, 0:1] > 0.0
            own_cols = pl.ds(RIM, own)
            _, decay, scale = rate_and_scale(pre_r[here, own_cols], sp[...], start)
            put_lanes(rate, here, decay)
            put_lanes(local, here, conv[here] * jax.nn.sigmoid(pre_i[here, own_cols]) * scale)

        loop(rows // TILE, drive)
        store.start(7)
        for line in lines:
            line.step(2)
        groups = own // LANES

        def scan(i, carry):
            here = pl.ds(i, 8, chunk)
            result = []
            for c in range(groups):
                product, total = carry[c]
                r = rate[c, here]
                product = product * r
                total = total * r + local[c, here]
                cum[c, here] = product
                local[c, here] = total
                result.append((product, total))
            return tuple(result)

        blank = (jnp.ones((8, LANES), jnp.float32), jnp.zeros((8, LANES), jnp.float32))
        lax.fori_loop(0, chunk, scan, (blank,) * groups)
        product, total = jnp.ones((1, own), jnp.float32), jnp.zeros((1, own), jnp.float32)
        for j in range(8):
            last = pl.ds(j * chunk + chunk - 1, 1)
            total = take_lanes(local, last) + take_lanes(cum, last) * total
            product = product * take_lanes(cum, last)
        agg[0:1] = product
        agg[1:2] = total
        swap_all = Exchange(place, "dp", agg, slots, es, er, el)
        swap_all.begin()
        swap_all.wait()
        entry = jnp.zeros((1, own), jnp.float32)
        for q in range(n_dp):
            longer = slots[q, 1:2] + slots[q, 0:1] * entry
            entry = jnp.where(q < place.d, longer, entry)
        state[pl.ds(0, 8)] = jnp.broadcast_to(entry, (8, own))
        for j in range(8):

            def settle(i, entry=entry):
                here = tile_rows(i, TILE, j * chunk)
                values = take_lanes(local, here) + take_lanes(cum, here) * entry
                state[tile_rows(i, TILE, j * chunk + 8)] = values
                merged[here] = (values * gelu_parts(y[here])[0]).astype(jnp.bfloat16)

            loop(chunk // TILE, settle)
            last = pl.ds(j * chunk + chunk - 1, 1)
            entry = take_lanes(local, last) + take_lanes(cum, last) * entry
        store.start(8)
        merged_st[...] = plain_dot(sto[...], merged[...]).astype(jnp.bfloat16)

        store.start(9)
        fetch.wait(3)

        def mix(i):
            some = tile_rows(i, 512)
            terms[:, pl.ds(pl.multiple_of(i * 512, 512), 512)] = times_trans(
                merged_st[...], wo[some, :]
            ).astype(jnp.bfloat16)

        loop(width // 512, mix)
        for line in lines:
            line.finish()
        keep.finish()
        store.start(10)
        store.wait(*range(11))

    low, full = jnp.bfloat16, jnp.float32
    results = (
        shaped((rows, width), low),
        shaped((rows + 16, own), low),
        shaped((rows, own), full),
        shaped((rows, wide), low),
        shaped((rows, own), full),
        shaped((rows, wide), full),
        shaped((rows, wide), full),
        shaped((own // LANES, rows, LANES), full),
        shaped((rows + 8, own), full),
        shaped((rows, own), low),
        shaped((rows, width), low),
    )
    near, far = in_vmem(), in_any()
    return pl.pallas_call(
        kernel,
        out_shape=results
        + (shaped((size, 2 * wide), low), shaped((n_line * cot_rows, width), low)),
        in_specs=[far, far, near, near, far, far, far] + [near] * 5,
        out_specs=[far] * 11 + [near, far],
        scratch_shapes=[vmem_like(m) for m in (tok_all, x_full, y_full, out_full) + results]
        + [
            pltpu.VMEM((rows, width), low),
            pltpu.VMEM((rows + 16, own), full),
            pltpu.VMEM((own // LANES, rows, LANES), full),
            pltpu.VMEM((own // LANES, rows, LANES), full),
            pltpu.VMEM((rows, own), low),
            pltpu.VMEM((2, own), full),
            pltpu.VMEM((n_dp, 2, own), full),
            dma_sems(2),
            dma_sems(2),
            dma_sems(n_dp),
            dma_sems(n_dp),
            pltpu.SemaphoreType.DMA,
            dma_sems(parts, 2, n_line - 1),
            dma_sems(parts, 2, n_line - 1),
            dma_sems(2),
            dma_sems(4),
            dma_sems(11),
            pltpu.VMEM((cot_rows, width), low),
        ],
        compiler_params=comm_params(5),
        name="recur_forward",
    )(
        tok_all,
        cot,
        to_place,
        to_stored,
        x_full,
        y_full,
        out_full,
        gain,
        gates,
        taps,
        soft,
        flags,
    )


class RowProducts:
    def __init__(self, left, right, far, stage, sems):
        self.left, self.right, self.far, self.stage, self.sems = left, right, far, stage, sems
        self.part = stage.shape[1]
        self.count = far.shape[0] // self.part

    def slot(self, i):
        return self.stage.at[i % 2, :, pl.ds(0, self.far.shape[1])]

    def copy(self, i):
        some = pl.ds(i * self.part, self.part)
        return pltpu.make_async_copy(self.slot(i), self.far.at[some], self.sems.at[i])

    def run(self):
        for i in range(self.count):
            if i >= 2:
                self.copy(i - 2).wait()
            some = pl.ds(i * self.part, self.part)
            self.slot(i)[...] = trans_times(self.left[:, some], self.right[...]).astype(
                jnp.bfloat16
            )
            self.copy(i).start()

    def finish(self):
        self.copy(self.count - 2).wait()
        self.copy(self.count - 1).wait()


def recur_backward(
    n_dp,
    n_line,
    mixer_in,
    to_place,
    to_stored,
    x_full,
    y_full,
    out_full,
    gates,
    taps,
    soft,
    slope,
    flags,
    kept,
    weight_terms,
    row_terms,
    hidden_place,
    merged_stored,
):
    rows, width = mixer_in.shape
    count, own = taps.shape
    size = gates.shape[0]
    wide = own + 2 * RIM
    blocks = (wide - RIM) // size
    chunk = rows // 8
    own_rows = rows // n_line
    parts = 4
    span = own_rows // parts

    def kernel(*refs):
        (mix_far, plc, sto, wx_far, wy_far, wo_far, gw, cw, sp, sg, fl) = refs[:11]
        kept_far, weights, feed_far, hp_far, merged_far = refs[11:19], *refs[19:23]
        (gate_grads, tap_grads, terms_far, weight_sum, row_sum) = refs[23:28]
        out_far, xy_far = refs[28:30]
        mix, wy, wo, feed, merged = refs[30:35]
        (xext, y, conv_low, conv, pre_r, pre_i, rate, state) = refs[35:43]
        (gxy, mp, gm, lam, reach, gp_r, gp_i, grad, spread, rim_out, rim_in) = refs[43:54]
        (ret_out, ret_in, tap_sums, decay_sums, ends, agg, slots) = refs[54:61]
        (hs, hr, es, er, el, in_sems, out_sems, inbox, ls, lr, total) = refs[61:72]
        stage, stage_sems = refs[72:74]
        hp, terms, wx = mix, mix, wo
        fetch = Fetch(
            [
                (mix_far, mix),
                (wo_far, wo),
                (kept_far[1], y),
                (kept_far[7], state),
                (kept_far[6], rate),
                (kept_far[4], pre_r),
                (kept_far[5], pre_i),
                (kept_far[3], conv),
                (kept_far[2], conv_low),
                (kept_far[0], xext),
                (wx_far, wx),
                (wy_far, wy),
                (feed_far, feed),
                (merged_far, merged),
                (hp_far, hp),
            ],
            in_sems,
        )
        fetch.start(12, 0, 1, 13)
        store = Fetch(((terms, terms_far),), out_sems)
        out_rows = RowProducts(mix, merged, out_far, stage, stage_sems.at[0])
        xy_rows = RowProducts(hp, gxy, xy_far, stage, stage_sems.at[1])
        place = Place(n_dp, n_line)
        place.meet(True)
        plane = ReducePlane(place, weights, refs[74:])
        plane.begin()
        lines = [
            ReduceLine(place, feed, own_rows, c * span, span, inbox.at[c], ls.at[c], lr.at[c])
            for c in range(parts)
        ]

        def send(c):
            if c > 0:
                lines[c - 1].sent()
            if c < parts:
                lines[c].ends()

        def add_up(c):
            lines[c].total(total)
            row_sum[pl.ds(c * span, span)] = total[...].astype(jnp.bfloat16)

        fetch.wait(12)
        send(0)
        fetch.start(*range(2, 10), 11)
        swap = RimSwap(place, own)
        own_cols = pl.ds(RIM, own)

        def project(i):
            here = tile_rows(i, 128)
            mp[here] = plain_dot(plc[here], mix[...]).astype(jnp.bfloat16)
            gm[here] = plain_dot(mp[here], wo[...])

        fetch.wait(0, 1)
        loop(rows // 128, project)
        fetch.start(10)
        fetch.wait(13)
        out_rows.run()
        fetch.start(14)

        def split(i):
            here = tile_rows(i, TILE)
            branch, slope_y = gelu_parts(y[here])
            grads = gm[here]
            put_lanes(lam, here, grads * branch)
            values = state[tile_rows(i, TILE, 8)]
            gxy[here, own:] = (grads * values * slope_y).astype(jnp.bfloat16)

        fetch.wait(2, 3)
        loop(rows // TILE, split)
        send(1)
        lines[0].hop(0)
        fetch.wait(4)
        groups = own // LANES

        def scan(i, carry):
            here = pl.ds(chunk - 1 - i, 8, chunk)
            result = []
            for c in range(groups):
                product, message = carry[c]
                r = rate[c, here]
                value = lam[c, here] + message
                lam[c, here] = value
                reach[c, here] = product
                result.append((product * r, value * r))
            return tuple(result)

        blank = (jnp.ones((8, LANES), jnp.float32), jnp.zeros((8, LANES), jnp.float32))
        done = lax.fori_loop(0, chunk, scan, (blank,) * groups)
        for c in range(groups):
            lanes = pl.ds(c * LANES, LANES)
            ends[0, :, lanes] = done[c][0]
            ends[1, :, lanes] = done[c][1]
        product, message = jnp.ones((1, own), jnp.float32), jnp.zeros((1, own), jnp.float32)
        for j in reversed(range(8)):
            message = ends[1, j : j + 1] + ends[0, j : j + 1] * message
            product = product * ends[0, j : j + 1]
        agg[0:1] = product
        agg[1:2] = message
        swap_all = Exchange(place, "dp", agg, slots, es, er, el)
        swap_all.begin()
        plane.cores()
        swap_all.wait()
        lines[0].hop(1)
        entry = jnp.zeros((1, own), jnp.float32)
        for q in reversed(range(n_dp)):
            longer = slots[q, 1:2] + slots[q, 0:1] * entry
            entry = jnp.where(q > place.d, longer, entry)
        fetch.wait(5, 6, 7)
        for ref in (tap_sums, decay_sums):
            ref[...] = jnp.zeros_like(ref)
        for ref in (gp_r, gp_i):
            ref[:, 0:RIM] = jnp.zeros((rows, RIM), jnp.bfloat16)
            ref[:, RIM + own :] = jnp.zeros((rows, RIM), jnp.bfloat16)
        grad[pl.ds(0, 8)] = jnp.zeros((8, own), jnp.float32)
        grad[pl.ds(rows + 8, 8)] = jnp.zeros((8, own), jnp.float32)
        for j in reversed(range(8)):

            def back(i, entry=entry):
                here = tile_rows(i, TILE, j * chunk)
                flag = fl[tile_rows(i, TILE, j * chunk + 8)]
                start = flag[:, 0:1] > 0.0
                values = take_lanes(lam, here) + take_lanes(reach, here) * entry
                before = moved_up(
                    state[pl.ds(pl.multiple_of(j * chunk + i * TILE, 8), TILE + 8)], 7, TILE
                )
                sr, decay, scale = rate_and_scale(pre_r[here, own_cols], sp[...], start)
                si = jax.nn.sigmoid(pre_i[here, own_cols])
                block = conv[here]
                driven = values * si
                log_grad = values * before * decay - block * driven * (decay * decay) / scale
                log_grad = jnp.where(start, 0.0, log_grad)
                inner = sr * log_grad
                gp_r[here, own_cols] = (
                    -rate_scale * sp[...] * inner * (1.0 - sr)
                ).astype(jnp.bfloat16)
                gp_i[here, own_cols] = (driven * block * (1.0 - si) * scale).astype(jnp.bfloat16)
                grad[tile_rows(i, TILE, j * chunk + 8)] = driven * scale
                decay_sums[...] += inner[:8] + inner[8:]

            loop(chunk // TILE, back)
            if j == 4:
                send(2)
                lines[1].hop(0)
            entry = ends[1, j : j + 1] + ends[0, j : j + 1] * entry
        lines[1].hop(1)
        add_up(0)

        for i in range(blocks):
            index = lax.rem(i + 2 - 2 * swap.odd, blocks)
            cols = swap.block(index, size)
            other = pl.ds(pl.multiple_of(wide + swap.first + index * size, RIM), size)
            spread[:, cols] = times_trans(gp_r[:, cols], gw[:, cols]) + times_trans(
                gp_i[:, cols], gw[:, other]
            )
            if i == 0:
                rim_out[...] = spread[:, swap.beyond].astype(jnp.bfloat16)
                rim = remote(rim_out, rim_in, hs.at[0], hr.at[0], swap.partner)
                rim.start()
        send(3)
        lines[2].hop(0)
        rim.wait()
        shared = pl.ds(pl.multiple_of((1 - swap.odd) * (own - RIM), RIM), RIM)

        def join(i):
            here = tile_rows(i, TILE)
            there = tile_rows(i, TILE, 8)
            grad[there] += spread[here, own_cols]
            grad[there, shared] += rim_in[here].astype(jnp.float32)

        loop(rows // TILE, join)

        near = grad[pl.ds(0, 16)]
        back_rows = jnp.zeros((8, own), jnp.float32)
        for k in range(1, count):
            masked = near * fl[pl.ds(0, 16)][:, k : k + 1]
            back_rows += cw[k : k + 1] * moved_up(masked, k, 8)
        ret_out[...] = back_rows
        ret = remote(
            ret_out,
            ret_in,
            hs.at[1],
            hr.at[1],
            (lax.rem(place.d + n_dp - 1, n_dp), place.t),
        )
        ret.start()
        fetch.wait(8)
        for i in range(blocks):
            cols = swap.block(i, size)
            spread[0:size, cols] = trans_times(conv_low[:, cols], gp_r[:, cols])
            spread[size : 2 * size, cols] = trans_times(conv_low[:, cols], gp_i[:, cols])
        gate_grads[:, 0:own] = spread[0:size, own_cols].astype(jnp.bfloat16)
        gate_grads[:, own:] = spread[size : 2 * size, own_cols].astype(jnp.bfloat16)

        def taps_back(i, added=None):
            here = tile_rows(i, TILE)
            start = pl.ds(pl.multiple_of(i * TILE + 8, 8), TILE + 8)
            after = grad[start]
            flag = fl[start]
            behind = xext[pl.ds(pl.multiple_of(i * TILE, 16), 2 * TILE)].astype(jnp.float32)
            total = cw[0:1] * after[:TILE]
            for k in range(count):
                if k > 0:
                    masked = after * flag[:, k : k + 1]
                    total += cw[k : k + 1] * moved_up(masked, k, TILE)
                    mine = masked[:TILE]
                else:
                    mine = after[:TILE]
                term = mine * moved_up(behind, 16 - k, TILE)
                tap_sums[k] += term[:8] + term[8:]
            if added is not None:
                total = total + jnp.concatenate([jnp.zeros((8, own), jnp.float32), added], axis=0)
            gxy[here, 0:own] = total.astype(jnp.bfloat16)

        fetch.wait(9)
        loop(rows // TILE - 1, taps_back)
        lines[2].hop(1)
        add_up(1)
        ret.wait()
        taps_back(rows // TILE - 1, jnp.where(place.d < n_dp - 1, ret_in[...], 0.0))
        tap_grads[...] = jnp.zeros_like(tap_grads)
        for k in range(count):
            tap_grads[k : k + 1] = jnp.sum(tap_sums[k], axis=0, keepdims=True)
        tap_grads[count : count + 1] = (
            rate_scale * sg[...] * jnp.sum(decay_sums[...], axis=0, keepdims=True)
        )

        fetch.wait(14)
        out_rows.finish()
        plane.turn()
        xy_rows.run()
        send(4)
        lines[3].hop(0)

        def restore(i):
            here = tile_rows(i, 128)
            mp[here, 0 : 2 * own] = plain_dot(sto[here], gxy[...]).astype(jnp.bfloat16)

        loop(rows // 128, restore)

        def spread_back(i):
            some = tile_rows(i, 512)
            terms[:, pl.ds(pl.multiple_of(i * 512, 512), 512)] = (
                times_trans(mp[:, 0:own], wx[some]) + times_trans(mp[:, own : 2 * own], wy[some])
            ).astype(jnp.bfloat16)

        fetch.wait(10, 11)
        loop(width // 512, spread_back)
        store.start(0)
        lines[3].hop(1)
        add_up(2)
        plane.finish(weight_sum)
        add_up(3)
        for line in lines:
            line.finish()
        xy_rows.finish()
        store.wait(0)

    low, full = jnp.bfloat16, jnp.float32
    block = weight_terms.shape[0] // n_dp
    near, far = in_vmem(), in_any()
    return pl.pallas_call(
        kernel,
        out_shape=(
            shaped((size, 2 * own), low),
            shaped((8, own), full),
            shaped((rows, width), low),
            shaped((block, weight_terms.shape[1]), low),
            shaped((own_rows, width), low),
            shaped((width, own), low),
            shaped((width, 2 * own), low),
        ),
        in_specs=[far, near, near, far, far, far] + [near] * 5 + [far] * 12,
        out_specs=[near, near, far, near, near, far, far],
        scratch_shapes=[
            vmem_like(m) for m in (mixer_in, y_full, out_full, row_terms, merged_stored, *kept)
        ]
        + [
            pltpu.VMEM((rows, 2 * own), low),
            pltpu.VMEM((rows, width), low),
            pltpu.VMEM((rows, own), full),
            pltpu.VMEM((own // LANES, rows, LANES), full),
            pltpu.VMEM((own // LANES, rows, LANES), full),
            pltpu.VMEM((rows, wide), low),
            pltpu.VMEM((rows, wide), low),
            pltpu.VMEM((rows + 16, own), full),
            pltpu.VMEM((rows, wide), full),
            pltpu.VMEM((rows, RIM), low),
            pltpu.VMEM((rows, RIM), low),
            pltpu.VMEM((8, own), full),
            pltpu.VMEM((8, own), full),
            pltpu.VMEM((count, 8, own), full),
            pltpu.VMEM((8, own), full),
            pltpu.VMEM((2, 8, own), full),
            pltpu.VMEM((2, own), full),
            pltpu.VMEM((n_dp, 2, own), full),
            dma_sems(2),
            dma_sems(2),
            dma_sems(n_dp),
            dma_sems(n_dp),
            pltpu.SemaphoreType.DMA,
            dma_sems(15),
            dma_sems(1),
            pltpu.VMEM((parts, 2, n_line - 1, span, width), low),
            dma_sems(parts, 2, n_line - 1),
            dma_sems(parts, 2, n_line - 1),
            pltpu.VMEM((span, width), full),
            pltpu.VMEM((2, width // 5, 2 * own), low),
            dma_sems(2, 5),
        ]
        + ReducePlane.scratch(block, weight_terms.shape[1]),
        compiler_params=comm_params(6),
        name="recur_backward",
    )(
        mixer_in,
        to_place,
        to_stored,
        x_full,
        y_full,
        out_full,
        gates,
        taps,
        soft,
        slope,
        flags,
        *kept,
        weight_terms,
        row_terms,
        hidden_place,
        merged_stored,
    )


def column_parts(width, size=768):
    return [(c, min(size, width - c)) for c in range(0, width, size)]


def feed_forward(n_dp, n_line, hidden, gate, up, down, grads, grad_own):
    rows, width = hidden.shape
    units = gate.shape[1]
    own_rows = grad_own.shape[0]
    ready = grads.shape[0] // n_line
    late = own_rows - ready
    part = width // 4

    def kernel(*refs):
        hid_far, wg_far, wu_far, wd_far, grads_far, own_far = refs[:6]
        product_far, gup_far, back_far, gdown_far, ggate_far = refs[6:11]
        hid, wg, wu, wd, grad, slope, branch, product, ggate, gup, stage, back = refs[11:23]
        in_sems, out_sems, stage_sems, ls, lr = refs[23:]
        place = Place(n_dp, n_line)
        pairs = [(hid_far, hid), (wg_far, wg), (wu_far, wu), (wd_far, wd)]
        pairs += [
            (grads_far.at[pl.ds(q * ready, ready)], grad.at[pl.ds(q * own_rows, ready)])
            for q in range(n_line)
        ]
        mine = pl.ds(pl.multiple_of(place.t * own_rows + ready, 16), late)
        pairs.append((own_far.at[pl.ds(ready, late)], grad.at[mine]))
        fetch = Fetch(pairs, in_sems)
        fetch.start(*range(len(pairs)))
        store = Fetch(((product, product_far), (gup, gup_far), (back, back_far)), out_sems)
        place.meet()
        line = GatherLine(place, grad, own_rows, ready, late, ls, lr)
        line.step(0, own_far.at[pl.ds(ready, late)])
        columns = column_parts(units)
        fetch.wait(0, 1)
        for c, size in columns:
            cols = pl.ds(c, size)

            def gates(i, cols=cols):
                here = tile_rows(i, 256)
                branch[here, cols] = plain_dot(hid[here], wg[:, cols])

            loop(rows // 256, gates)
        line.step(1)
        fetch.wait(2)
        for c, size in columns:
            cols = pl.ds(c, size)

            def ups(i, cols=cols):
                here = tile_rows(i, 256)
                value = plain_dot(hid[here], wu[:, cols])
                active, bend = gelu_parts(branch[here, cols])
                product[here, cols] = (active * value).astype(jnp.bfloat16)
                branch[here, cols] = active
                slope[here, cols] = bend * value

            loop(rows // 256, ups)
        store.start(0)
        line.step(2)
        fetch.wait(*range(4, len(pairs)))
        line.finish()

        down_rows = RowProducts(grad, product, gdown_far, stage, stage_sems.at[0])
        down_rows.run()
        fetch.wait(3)
        for c, size in columns:
            cols = pl.ds(c, size)

            def backs(i, cols=cols):
                here = tile_rows(i, 256)
                value = plain_dot(grad[here], wd[:, cols])
                ggate[here, cols] = (value * slope[here, cols]).astype(jnp.bfloat16)
                gup[here, cols] = (value * branch[here, cols]).astype(jnp.bfloat16)

            loop(rows // 256, backs)
        store.start(1)
        for i in range(4):
            some = pl.ds(i * part, part)
            back[:, some] = (
                times_trans(ggate[...], wg[some]) + times_trans(gup[...], wu[some])
            ).astype(jnp.bfloat16)
        store.start(2)
        down_rows.finish()
        gate_rows = RowProducts(hid, ggate, ggate_far, stage, stage_sems.at[1])
        gate_rows.run()
        gate_rows.finish()
        store.wait(0, 1, 2)

    low, full = jnp.bfloat16, jnp.float32
    return pl.pallas_call(
        kernel,
        out_shape=(
            shaped((rows, units), low),
            shaped((rows, units), low),
            shaped((rows, width), low),
            shaped((width, units), low),
            shaped((width, units), low),
        ),
        in_specs=[in_any()] * 6,
        out_specs=[in_any()] * 5,
        scratch_shapes=[vmem_like(m) for m in (hidden, gate, up, down)]
        + [
            pltpu.VMEM((n_line * own_rows, width), low),
            pltpu.VMEM((rows, units), full),
            pltpu.VMEM((rows, units), full),
            pltpu.VMEM((rows, units), low),
            pltpu.VMEM((rows, units), low),
            pltpu.VMEM((rows, units), low),
            pltpu.VMEM((2, part, units), low),
            pltpu.VMEM((rows, width), low),
            dma_sems(5 + n_line),
            dma_sems(3),
            dma_sems(2, 4),
            dma_sems(2, n_line - 1),
            dma_sems(2, n_line - 1),
        ],
        compiler_params=comm_params(7),
        name="feed_forward",
    )(hidden, gate, up, down, grads, grad_own)


def matches(mesh):
    return mesh.shape["dp"] == 8 and mesh.shape["tensor"] == 4


def local_blocks(
    tokens,
    norm_gain,
    x_weight,
    y_weight,
    conv_weight,
    recur_gate_weight,
    input_gate_weight,
    decay_param,
    out_weight,
    mlp_gain,
    gate_weight,
    up_weight,
    down_weight,
    seq_lengths,
    token_order,
    cotangent,
):
    n_dp, n_tensor = lax.axis_size("dp"), lax.axis_size("tensor")
    tensor_index = lax.axis_index("tensor")
    dp_index = lax.axis_index("dp")
    tok_rows, width = tokens.shape
    row_count = tok_rows * n_tensor
    own_width = conv_weight.shape[1]
    kernel_taps = conv_weight.shape[0]
    edge_rows = kernel_taps - 1
    dp_width = norm_gain.shape[0]
    gate_rows = recur_gate_weight.shape[0]
    own_start = tensor_index * tok_rows

    gains = jnp.concatenate([norm_gain, mlp_gain])
    spare = gate_rows * 128 - gains.shape[0]
    gains = jnp.pad(gains, (0, spare)).reshape(gate_rows, 128)
    minor = jnp.concatenate([recur_gate_weight, input_gate_weight, gains], axis=1)
    own_order = (token_order - dp_index * row_count).astype(jnp.int32)
    order_rows = jnp.broadcast_to(own_order[None, :], (8, tok_rows))
    x_full, y_full, out_full, minor_full, tok_all, order_full = first_gather(
        n_dp, n_tensor, (x_weight, y_weight, out_weight.T, minor), tokens, order_rows
    )
    late_up, late_down, _ = lax.optimization_barrier((up_weight, down_weight.T, tok_all))
    up_full = lax.all_gather(late_up, "dp", axis=0, tiled=True)
    down_full = lax.all_gather(late_down, "dp", axis=0, tiled=True)
    order_all = order_full.reshape(n_tensor, 8, tok_rows)[:, 0].reshape(row_count)
    gain_rows = minor_full[:, 2 * own_width :].reshape(n_dp, -1)
    first_gain = gain_rows[:, :dp_width].reshape(1, width).astype(jnp.float32)
    second_gain = gain_rows[:, dp_width : 2 * dp_width].reshape(1, width).astype(jnp.float32)
    row_index = jnp.arange(row_count, dtype=jnp.int32)
    hits = row_index[:, None] == order_all[None, :]
    to_place = hits.astype(jnp.bfloat16)
    to_stored = (order_all[:, None] == row_index[None, :]).astype(jnp.bfloat16)
    places = dp_index * row_count + jnp.arange(-8, row_count + 8, dtype=jnp.int32)
    inside = (jnp.arange(row_count + 16) >= 8) & (jnp.arange(row_count + 16) < row_count + 8)
    ends = jnp.cumsum(seq_lengths)
    segment = segment_of(places, ends)
    starts = (places == 0) | (segment != segment_of(places - 1, ends))
    columns = [starts] + [
        segment_of(places - shift, ends) == segment for shift in range(1, kernel_taps)
    ]
    columns += [jnp.zeros_like(starts)] * (8 - len(columns))
    flags = (jnp.stack(columns, axis=1) & inside[:, None]).astype(jnp.float32)
    live_own = (token_order < ends[-1]).astype(jnp.float32)
    grad_in_own = (cotangent.astype(jnp.float32) * live_own[:, None]).astype(jnp.bfloat16)
    soft = jax.nn.softplus(-decay_param).reshape(1, own_width)
    slope = jax.nn.sigmoid(-decay_param).reshape(1, own_width)
    hidden_place, *kept, merged_stored, mixer_terms, gates_wide, grad_rows = recur_forward(
        n_dp,
        n_tensor,
        tok_all,
        grad_in_own,
        to_place,
        to_stored,
        x_full,
        y_full,
        out_full,
        first_gain,
        minor_full,
        conv_weight,
        soft,
        flags,
    )
    after_own, hidden_two, gate_full = middle_gather(
        n_dp, n_tensor, mixer_terms, tokens, second_gain, (gate_weight,)
    )
    product, grad_up_pre, back_terms, grad_down, grad_gate = feed_forward(
        n_dp,
        n_tensor,
        hidden_two,
        gate_full,
        up_full,
        down_full,
        grad_rows,
        grad_in_own,
    )
    down_sum = lax.psum_scatter(grad_down, "dp", scatter_dimension=0, tiled=True)
    grad_after_own, second_part, mixer_in, gate_sum, grad_up, feed_terms = middle_sums(
        n_dp,
        n_tensor,
        back_terms,
        after_own,
        second_gain,
        grad_in_own,
        grad_gate,
        hidden_two,
        grad_up_pre,
        product,
        down_full,
    )
    (
        gate_grads,
        tap_grads,
        one_terms,
        up_sum,
        feed_out,
        grad_out_mat,
        grad_xy_mat,
    ) = recur_backward(
        n_dp,
        n_tensor,
        mixer_in,
        to_place,
        to_stored,
        x_full,
        y_full,
        out_full,
        gates_wide,
        conv_weight,
        soft,
        slope,
        flags,
        kept,
        grad_up,
        feed_terms,
        hidden_place,
        merged_stored,
    )
    output = (after_own + feed_out.astype(jnp.float32)) * live_own[:, None]
    output = output.astype(jnp.bfloat16)
    grad_tokens, small_sum, gain_sums, xy_sum, out_sum, gates_sum = last_sums(
        n_dp,
        n_tensor,
        one_terms,
        tokens,
        first_gain,
        grad_after_own,
        second_part,
        tap_grads,
        (grad_xy_mat, grad_out_mat, gate_grads),
    )
    xy_sum, gates_sum = xy_sum.astype(jnp.float32), gates_sum.astype(jnp.float32)
    own_gains = lax.dynamic_slice_in_dim(gain_sums, dp_index * dp_width, dp_width, 1)
    return (
        output,
        grad_tokens,
        own_gains[1],
        xy_sum[:, :own_width],
        xy_sum[:, own_width:],
        small_sum[:kernel_taps],
        gates_sum[:, :own_width],
        gates_sum[:, own_width:],
        small_sum[kernel_taps],
        out_sum.astype(jnp.float32).T,
        own_gains[0],
        gate_sum.astype(jnp.float32),
        up_sum.astype(jnp.float32),
        down_sum.astype(jnp.float32).T,
    )


def solution(mesh):
    in_specs = (
        P(("dp", "tensor"), None),
        P("dp"),
        P("dp", "tensor"),
        P("dp", "tensor"),
        P(None, "tensor"),
        P("dp", "tensor"),
        P("dp", "tensor"),
        P("tensor"),
        P("tensor", "dp"),
        P("dp"),
        P("dp", "tensor"),
        P("dp", "tensor"),
        P("tensor", "dp"),
        P(),
        P(("dp", "tensor")),
        P(("dp", "tensor"), None),
    )
    out_specs = (
        P(("dp", "tensor"), None),
        P(("dp", "tensor"), None),
        P("dp"),
        P("dp", "tensor"),
        P("dp", "tensor"),
        P(None, "tensor"),
        P("dp", "tensor"),
        P("dp", "tensor"),
        P("tensor"),
        P("tensor", "dp"),
        P("dp"),
        P("dp", "tensor"),
        P("dp", "tensor"),
        P("tensor", "dp"),
    )
    fits = matches(mesh)
    local = local_blocks if fits else local_general
    return jax.shard_map(local, mesh=mesh, in_specs=in_specs, out_specs=out_specs, check_vma=False)
```
